32 devices in a mesh: gx: 8 (over z, x), gy: 4 (over y, core).
Axes of the slice: x: 2, y: 2, z: 4, core: 2. Of those that a mesh axis runs over, the one named last changes fastest.
Arguments:
- fields: float32 [4, 16, 8, 8, 8, 128], P(None, 'gx', None, 'gy'), may hold values from -6 to 6
- viscosity: float32 [16, 8, 8, 8, 128], P('gx', None, 'gy'), may hold values from 0.002 to 0.02
- inv_density: float32 [16, 8, 16], P('gx', 'gy'), may hold values from 0.5 to 2
- elem_group: int32 [16, 8, 16], P('gx', 'gy'), may hold values from 0 to 3
- coarse_inverse: float32 [128, 128], P(('gx', 'gy')), as said below
Outputs:
- fields_new: float32 [4, 16, 8, 8, 8, 128], P(None, 'gx', None, 'gy')
- pressure: float32 [16, 8, 8, 8, 128], P('gx', None, 'gy')
The draws below stay inside these ranges and needn't reach their ends.
Inputs may be any that keep to these rules, and one draw needn't show every extreme that they name: `elem_group`: the coarse unknown of an element among the 4 of its own device. `coarse_inverse`: symmetric and positive definite.
All inputs are finite; a program needn't handle non-finite values.
Results may differ from the reference program's by a relative error of at most 0.0015.
Values sent between devices are 32-bit elements; how exact they have to be, the bound alone decides.
No kernel may reach another device: no remote copies, remote signals or barrier semaphores. Data moves between devices by JAX's collectives and lax.ppermute only.
A program may use at most 64 MiB of HBM per device.

```python
import math
import jax
import jax.numpy as jnp
import numpy as np
from jax import lax

ORDER = 7
EX = 2
EY = 2
EZ = 16
ITERS = 2
CHEB = 2
NCD = 4
NXE = 16
NYE = 8
NC = 128
N_GX = 8
N_GY = 4


def draw_coarse_inverse(key, part):
    folded = jax.random.fold_in(key, 17)
    key_place, key_first, key_second, key_diag = jax.random.split(folded, 4)
    device = jnp.arange(NC, dtype=jnp.int32) // NCD
    half_x = max(N_GX // 2, 1)
    device_x = (device // N_GY % half_x).astype(jnp.float32)
    device_y = (device % N_GY).astype(jnp.float32)
    placed = jax.random.uniform(key_place, (NC, 2), jnp.float32, 0.0, 1.0)
    spot_x = device_x + placed[:, 0]
    spot_y = device_y + placed[:, 1]
    gap_x = spot_x[:, None] - spot_x[None, :]
    gap_y = spot_y[:, None] - spot_y[None, :]
    distance = jnp.sqrt(gap_x * gap_x + gap_y * gap_y)
    second = jnp.clip(jax.random.normal(key_second, (NC,), jnp.float32), -3.0, 3.0)
    reach = 3.0
    first = jnp.clip(jax.random.normal(key_first, (NC,), jnp.float32), -3.0, 3.0)
    diagonal = jax.random.uniform(key_diag, (NC,), jnp.float32, 1.0, 2.0)
    kernel = jnp.exp(-distance / reach)
    coupling = 0.2 * kernel * (first[:, None] * first[None, :] + second[:, None] * second[None, :])
    matrix = coupling + jnp.diag(diagonal)
    return (matrix / (1.0 * EX * EY * EZ)).astype(jnp.float32)


def plant(values, own_key, least, top_value):
    longest = values.shape.index(max(values.shape))
    spots = []
    for shift in (0, 1):
        where = [jax.random.randint(jax.random.fold_in(own_key, axis), (), 0, length) for axis, length in enumerate(values.shape)]
        where[longest] = (where[longest] + shift) % values.shape[longest]
        spots.append(tuple(where))
    return values.at[spots[0]].set(least).at[spots[1]].set(top_value)


def levels(rng, dims, shards, least, top_value):
    def one(position, parts):
        draws = jax.random.uniform(jax.random.fold_in(jax.random.fold_in(rng, 6), position), (parts,), jnp.float32, least / len(shards), top_value / len(shards))
        return jnp.repeat(jnp.exp(draws), dims[position] // parts).reshape((-1,) + (1,) * (len(dims) - position - 1))

    level = one(*shards[0])
    for cut in shards[1:]:
        level = level * one(*cut)
    return level


def normal_values(own_key, dims, width, bound, cuts=(), held_as=jnp.bfloat16):
    gain = levels(own_key, dims, cuts, -0.22, 0.18) if cuts else 1.0
    entries = jax.random.normal(own_key, dims, jnp.float32) * width * gain
    return jnp.minimum(jnp.maximum(entries, -bound), bound).astype(held_as)


def setup_inputs(seed: int = 0) -> dict:
    streams_of = jax.random.split(jax.random.key(seed), 6)
    return {
        "fields": normal_values(streams_of[0], (4, NXE, ORDER + 1, NYE, ORDER + 1, EZ * (ORDER + 1)), 1.0, 6.0, ((1, 8), (3, 4)), jnp.float32),
        "viscosity": jnp.clip(jnp.exp(math.log(0.02) - 2.30258502 * jax.random.uniform(streams_of[1], (NXE, ORDER + 1, NYE, ORDER + 1, EZ * (ORDER + 1)), jnp.float32) ** levels(streams_of[1], (NXE, ORDER + 1, NYE, ORDER + 1, EZ * (ORDER + 1)), ((0, 8), (2, 4)), -0.2, 0.2)), 0.002, 0.02),
        "inv_density": jnp.clip(jnp.exp(math.log(2.0) - 1.3862944 * jax.random.uniform(streams_of[2], (NXE, NYE, EZ), jnp.float32) ** levels(streams_of[2], (NXE, NYE, EZ), ((0, 8), (1, 4)), -0.2, 0.2)), 0.5, 2.0),
        "elem_group": plant(jax.random.randint(streams_of[3], (NXE, NYE, EZ), 0, NCD), jax.random.fold_in(streams_of[3], 1), 0, NCD - 1).astype(jnp.int32),
        "coarse_inverse": draw_coarse_inverse(jax.random.fold_in(streams_of[5], 71), 0),
    }


dt_step = 0.01
sigma_p = 4.0
prandtl = 0.7
cheb_ratio = 0.1


def tables():
    points = np.array([-1.0, -0.8717401485096066, -0.5917001814331423, -0.2092992179024789,
                       0.2092992179024789, 0.5917001814331423, 0.8717401485096066, 1.0])
    weights = np.array([1.0 / 28.0, 0.2107042271435061, 0.3411226924835044, 0.4124587946587038,
                        0.4124587946587038, 0.3411226924835044, 0.2107042271435061, 1.0 / 28.0])
    identity = np.eye(8)
    differ = points[:, None] - points[None, :] + identity
    barycentric = 1.0 / np.prod(differ, axis=1)
    offdiag = (barycentric[None, :] / barycentric[:, None]) / differ * (1.0 - identity)
    derivative = offdiag - identity * np.sum(offdiag, axis=1)[:, None]
    mass_one = identity * weights[None, :]
    stiff_one = derivative.T @ mass_one @ derivative
    stiff_three = (np.kron(np.kron(stiff_one, mass_one), mass_one)
                   + np.kron(np.kron(mass_one, stiff_one), mass_one)
                   + np.kron(np.kron(mass_one, mass_one), stiff_one))
    three_diag = np.sum(stiff_three * np.eye(512), axis=1)
    spectral_bound = float(np.max(np.sum(np.abs(stiff_three), axis=1) / three_diag))
    return derivative, weights, np.sum(stiff_one * identity, axis=1), spectral_bound


def join_pairs(field, elem_axis):
    node_axis = elem_axis + 1
    top_node = field.shape[node_axis] - 1
    last_face = lax.index_in_dim(field, top_node, node_axis, keepdims=False)
    first_face = lax.index_in_dim(field, 0, node_axis, keepdims=False)
    elem_count = field.shape[elem_axis]
    summed = (lax.slice_in_dim(last_face, 0, elem_count - 1, axis=elem_axis)
              + lax.slice_in_dim(first_face, 1, elem_count, axis=elem_axis))
    new_last = jnp.concatenate([summed, lax.slice_in_dim(last_face, elem_count - 1, elem_count, axis=elem_axis)], elem_axis)
    new_first = jnp.concatenate([lax.slice_in_dim(first_face, 0, 1, axis=elem_axis), summed], elem_axis)
    middle = lax.slice_in_dim(field, 1, top_node, axis=node_axis)
    return jnp.concatenate([jnp.expand_dims(new_first, node_axis), middle, jnp.expand_dims(new_last, node_axis)], node_axis)


def reference(fields, viscosity, inv_density, elem_group, coarse_inverse):
    precision = lax.Precision.HIGHEST
    derivative_np, weights_np, stiff_np, spectral_bound = tables()
    derivative = jnp.asarray(derivative_np, jnp.float32)
    weights_line = jnp.asarray(weights_np, jnp.float32)
    stiff_line = jnp.asarray(stiff_np, jnp.float32)
    line_nodes = ORDER + 1
    elems_x = fields.shape[1]
    elems_y = fields.shape[3]
    length = fields.shape[5]
    elems_z = length // line_nodes

    def split_z(field):
        return field.reshape(field.shape[:-1] + (elems_z, line_nodes))

    def merge_z(field):
        return field.reshape(field.shape[:-2] + (length,))

    def gradient(field):
        along_x = jnp.einsum('ia,cxaybl->cxiybl', derivative, field, precision=precision)
        along_y = jnp.einsum('jb,cxaybl->cxayjl', derivative, field, precision=precision)
        along_z = merge_z(jnp.einsum('kq,cxaybzq->cxaybzk', derivative, split_z(field), precision=precision))
        return along_x, along_y, along_z

    def adjoint(first_part, second_part, third_part):
        result = jnp.einsum('ai,cxaybl->cxiybl', derivative, first_part, precision=precision)
        result = result + jnp.einsum('bj,cxaybl->cxayjl', derivative, second_part, precision=precision)
        return result + merge_z(jnp.einsum('qk,cxaybzq->cxaybzk', derivative, split_z(third_part), precision=precision))

    def assemble(field):
        field = join_pairs(field, 1)
        field = join_pairs(field, 3)
        return merge_z(join_pairs(split_z(field), 5))

    def on_x(values):
        return values[None, :, None, None, None]

    def on_y(values):
        return values[None, None, None, :, None]

    weights_z = jnp.tile(weights_line, elems_z)
    stiff_z = jnp.tile(stiff_line, elems_z)
    weight = on_x(weights_line) * on_y(weights_line) * weights_z
    diag_stiff = (on_x(stiff_line) * on_y(weights_line) * weights_z
                  + on_x(weights_line) * on_y(stiff_line) * weights_z
                  + on_x(weights_line) * on_y(weights_line) * stiff_z)
    kappa = jnp.repeat(inv_density, line_nodes, axis=2)[:, None, :, None, :]
    unit = jnp.ones((1, elems_x, line_nodes, elems_y, line_nodes, length), jnp.float32)
    multiplicity = assemble(unit)[0]
    mass_sum = assemble(unit * weight)[0]
    pdiag = assemble((kappa * diag_stiff + sigma_p * weight)[None])[0]
    start = assemble(fields * weight) / mass_sum
    velocity = start[:3]
    factors = [1.0, 1.0, 1.0, 1.0 / prandtl]
    updated = []
    for channel in range(4):
        field = start[channel:channel + 1]
        along_x, along_y, along_z = gradient(field)
        advect = velocity[0] * along_x + velocity[1] * along_y + velocity[2] * along_z
        scaled = factors[channel] * viscosity * weight
        rhs = -weight * advect - adjoint(scaled * along_x, scaled * along_y, scaled * along_z)
        updated.append(field + dt_step * assemble(rhs) / mass_sum)
    fields_new = jnp.concatenate(updated, 0)

    div_x = jnp.einsum('ia,xaybl->xiybl', derivative, fields_new[0], precision=precision)
    div_y = jnp.einsum('jb,xaybl->xayjl', derivative, fields_new[1], precision=precision)
    div_z = merge_z(jnp.einsum('kq,xaybzq->xaybzk', derivative, split_z(fields_new[2]), precision=precision))
    rhs_p = assemble((-weight * (div_x + div_y + div_z))[None])[0]

    inv_mult = 1.0 / multiplicity
    inv_diag = 1.0 / pdiag
    kappa_weight = kappa * weight

    def apply_op(field):
        along_x, along_y, along_z = gradient(field[None])
        local = adjoint(kappa_weight * along_x, kappa_weight * along_y, kappa_weight * along_z)[0] + sigma_p * weight * field
        return assemble(local[None])[0]

    def inner_product(first_field, second_field):
        return jnp.sum(first_field * second_field * inv_mult)

    device_x = jnp.arange(elems_x, dtype=jnp.int32) // EX
    device_y = jnp.arange(elems_y, dtype=jnp.int32) // EY
    coarse_ids = NCD * (device_x[:, None, None] * N_GY + device_y[None, :, None]) + elem_group

    def restrict(resid):
        elem_sums = split_z(resid * inv_mult).sum(axis=(1, 3, 5))
        return jax.ops.segment_sum(elem_sums.reshape(-1), coarse_ids.reshape(-1), num_segments=NC)

    def prolong(values):
        elem_values = values[coarse_ids]
        local = jnp.repeat(elem_values, line_nodes, axis=2)[:, None, :, None, :] * inv_mult
        return assemble(local[None])[0]

    upper = spectral_bound
    lower = cheb_ratio * upper
    cheb_theta = 0.5 * (upper + lower)
    cheb_delta = 0.5 * (upper - lower)

    def precondition(resid):
        update = resid * inv_diag / cheb_theta
        smoothed = update
        cheb_rho = cheb_delta / cheb_theta
        for step in range(CHEB - 1):
            defect = resid - apply_op(smoothed)
            rho_next = 1.0 / (2.0 * cheb_theta / cheb_delta - cheb_rho)
            update = rho_next * cheb_rho * update + (2.0 * rho_next / cheb_delta) * defect * inv_diag
            smoothed = smoothed + update
            cheb_rho = rho_next
        coarse_values = jnp.dot(coarse_inverse, restrict(resid), precision=precision)
        return smoothed + prolong(coarse_values)

    pressure = jnp.zeros_like(rhs_p)
    resid = rhs_p
    precond_r = precondition(resid)
    rz_value = inner_product(resid, precond_r)
    direction = precond_r
    for iteration in range(ITERS):
        image = apply_op(direction)
        step_size = rz_value / inner_product(direction, image)
        pressure = pressure + step_size * direction
        if iteration + 1 < ITERS:
            resid = resid - step_size * image
            precond_r = precondition(resid)
            rz_next = inner_product(resid, precond_r)
            direction = precond_r + (rz_next / rz_value) * direction
            rz_value = rz_next
    return fields_new, pressure
```

```python
import jax
import jax.numpy as jnp
import numpy as np
from jax import lax
from jax.sharding import PartitionSpec as P

ORDER = 7
ITERS = 2
NCD = 4


dt_step = 0.01
sigma_p = 4.0
prandtl = 0.7
cheb_ratio = 0.1


def swap_faces(first_face, last_face, axis):
    count = lax.axis_size(axis)
    even = lax.axis_index(axis) % 2 == 0
    first_pairs = [(i, i ^ 1) for i in range(count) if i ^ 1 < count]
    second_pairs = [(i, ((i + 1) ^ 1) - 1) for i in range(1, count) if ((i + 1) ^ 1) - 1 < count]
    got_first = lax.ppermute(jnp.where(even, last_face, first_face), axis, first_pairs)
    got_second = lax.ppermute(jnp.where(even, first_face, last_face), axis, second_pairs)
    return jnp.where(even, got_second, got_first), jnp.where(even, got_first, got_second)


def with_halo(cells, sides, width):
    for axis, dim in sides:
        head = lax.slice_in_dim(cells, 0, width, axis=dim)
        tail = lax.slice_in_dim(cells, cells.shape[dim] - width, cells.shape[dim], axis=dim)
        before, after = swap_faces(head, tail, axis)
        cells = jnp.concatenate([before, cells, after], axis=dim)
    return cells


def tables():
    points = np.array(
        [
            -1.0,
            -0.8717401485096066,
            -0.5917001814331423,
            -0.2092992179024789,
            0.2092992179024789,
            0.5917001814331423,
            0.8717401485096066,
            1.0,
        ]
    )
    weights = np.array(
        [
            1.0 / 28.0,
            0.2107042271435061,
            0.3411226924835044,
            0.4124587946587038,
            0.4124587946587038,
            0.3411226924835044,
            0.2107042271435061,
            1.0 / 28.0,
        ]
    )
    identity = np.eye(8)
    differ = points[:, None] - points[None, :] + identity
    barycentric = 1.0 / np.prod(differ, axis=1)
    offdiag = barycentric[None, :] / barycentric[:, None] / differ * (1.0 - identity)
    derivative = offdiag - identity * np.sum(offdiag, axis=1)[:, None]
    mass_one = identity * weights[None, :]
    stiff_one = derivative.T @ mass_one @ derivative
    stiff_three = (
        np.kron(np.kron(stiff_one, mass_one), mass_one)
        + np.kron(np.kron(mass_one, stiff_one), mass_one)
        + np.kron(np.kron(mass_one, mass_one), stiff_one)
    )
    three_diag = np.sum(stiff_three * np.eye(512), axis=1)
    spectral_bound = float(np.max(np.sum(np.abs(stiff_three), axis=1) / three_diag))
    return (derivative, weights, np.sum(stiff_one * identity, axis=1), spectral_bound)


def join_pairs(field, elem_axis):
    node_axis = elem_axis + 1
    top_node = field.shape[node_axis] - 1
    last_face = lax.index_in_dim(field, top_node, node_axis, keepdims=False)
    first_face = lax.index_in_dim(field, 0, node_axis, keepdims=False)
    elem_count = field.shape[elem_axis]
    summed = lax.slice_in_dim(last_face, 0, elem_count - 1, axis=elem_axis) + lax.slice_in_dim(
        first_face, 1, elem_count, axis=elem_axis
    )
    new_last = jnp.concatenate(
        [summed, lax.slice_in_dim(last_face, elem_count - 1, elem_count, axis=elem_axis)], elem_axis
    )
    new_first = jnp.concatenate(
        [lax.slice_in_dim(first_face, 0, 1, axis=elem_axis), summed], elem_axis
    )
    middle = lax.slice_in_dim(field, 1, top_node, axis=node_axis)
    return jnp.concatenate(
        [jnp.expand_dims(new_first, node_axis), middle, jnp.expand_dims(new_last, node_axis)],
        node_axis,
    )


def add_edges(grid, extra_first, extra_last, edge_dim):
    extent = grid.shape[edge_dim]
    return jnp.concatenate(
        [
            lax.slice_in_dim(grid, 0, 1, axis=edge_dim) + extra_first,
            lax.slice_in_dim(grid, 1, extent - 1, axis=edge_dim),
            lax.slice_in_dim(grid, extent - 1, extent, axis=edge_dim) + extra_last,
        ],
        edge_dim,
    )


def per_device(fields, viscosity, inv_density, elem_group, coarse_inverse):
    precision = lax.Precision.HIGHEST
    derivative_np, weights_np, stiff_np, spectral_bound = tables()
    line_nodes = ORDER + 1
    elems_x = fields.shape[1]
    elems_y = fields.shape[3]
    length = fields.shape[5]
    elems_z = length // line_nodes
    rows_x = elems_x * line_nodes
    rows_y = elems_y * line_nodes
    derivative = jnp.asarray(derivative_np, jnp.float32)
    weights_line = jnp.asarray(weights_np, jnp.float32)
    stiff_line = jnp.asarray(stiff_np, jnp.float32)
    band_np = np.kron(np.eye(elems_z), derivative_np)
    band_matrix = jnp.asarray(band_np, jnp.float32)
    band_trans = jnp.asarray(band_np.T, jnp.float32)
    pair_np = np.eye(length)
    joints = np.arange(elems_z - 1) * line_nodes + ORDER
    pair_np[joints, joints + 1] = 1.0
    pair_np[joints + 1, joints] = 1.0
    pair_table = jnp.asarray(pair_np, jnp.float32)
    block_np = np.kron(np.eye(elems_z), np.ones((line_nodes, 1)))
    block_table = jnp.asarray(block_np, jnp.float32)
    block_trans = jnp.asarray(block_np.T, jnp.float32)

    def gradient(field):
        along_x = jnp.einsum("ia,cxaybl->cxiybl", derivative, field, precision=precision)
        along_y = jnp.einsum("jb,cxaybl->cxayjl", derivative, field, precision=precision)
        along_z = jnp.matmul(field, band_trans, precision=precision)
        return (along_x, along_y, along_z)

    def adjoint(first_part, second_part, third_part):
        result = jnp.einsum("ai,cxaybl->cxiybl", derivative, first_part, precision=precision)
        result = result + jnp.einsum(
            "bj,cxaybl->cxayjl", derivative, second_part, precision=precision
        )
        return result + jnp.matmul(third_part, band_matrix, precision=precision)

    def assemble(field):
        channels = field.shape[0]
        field = join_pairs(field, 1)
        grid = field.reshape(channels, rows_x, rows_y, length)
        border = with_halo(grid, (("gx", 1),), 1)
        grid = add_edges(grid, border[:, 0:1], border[:, -1:], 1)
        field = join_pairs(
            grid.reshape(channels, elems_x, line_nodes, elems_y, line_nodes, length), 3
        )
        grid = field.reshape(channels, rows_x, rows_y, length)
        border = with_halo(grid, (("gy", 2),), 1)
        grid = add_edges(grid, border[:, :, 0:1], border[:, :, -1:], 2)
        field = grid.reshape(channels, elems_x, line_nodes, elems_y, line_nodes, length)
        return jnp.matmul(field, pair_table, precision=precision)

    def on_x(values):
        return values[None, :, None, None, None]

    def on_y(values):
        return values[None, None, None, :, None]

    weights_z = jnp.tile(weights_line, elems_z)
    stiff_z = jnp.tile(stiff_line, elems_z)
    weight = on_x(weights_line) * on_y(weights_line) * weights_z
    diag_stiff = (
        on_x(stiff_line) * on_y(weights_line) * weights_z
        + on_x(weights_line) * on_y(stiff_line) * weights_z
        + on_x(weights_line) * on_y(weights_line) * stiff_z
    )
    kappa = jnp.dot(inv_density, block_trans, precision=precision)[:, None, :, None, :]
    unit = jnp.ones((1, elems_x, line_nodes, elems_y, line_nodes, length), jnp.float32)
    stacked = jnp.concatenate(
        [unit, unit * weight, (kappa * diag_stiff + sigma_p * weight)[None], fields * weight], 0
    )
    summed = assemble(stacked)
    multiplicity = summed[0]
    mass_sum = summed[1]
    pdiag = summed[2]
    start = summed[3:] / mass_sum
    along_x, along_y, along_z = gradient(start)
    advect = start[0] * along_x + start[1] * along_y + start[2] * along_z
    factors = jnp.asarray([1.0, 1.0, 1.0, 1.0 / prandtl], jnp.float32)[
        :, None, None, None, None, None
    ]
    scaled = factors * viscosity * weight
    rhs = -weight * advect - adjoint(scaled * along_x, scaled * along_y, scaled * along_z)
    fields_new = start + dt_step * assemble(rhs) / mass_sum
    div_x = jnp.einsum("ia,xaybl->xiybl", derivative, fields_new[0], precision=precision)
    div_y = jnp.einsum("jb,xaybl->xayjl", derivative, fields_new[1], precision=precision)
    div_z = jnp.matmul(fields_new[2], band_trans, precision=precision)
    rhs_p = assemble((-weight * (div_x + div_y + div_z))[None])[0]
    inv_mult = 1.0 / multiplicity
    inv_diag = 1.0 / pdiag
    kappa_weight = kappa * weight
    one_hot = (elem_group[..., None] == jnp.arange(NCD, dtype=jnp.int32)).astype(jnp.float32)

    def op_local(field):
        grad_x, grad_y, grad_z = gradient(field[None])
        return (
            adjoint(kappa_weight * grad_x, kappa_weight * grad_y, kappa_weight * grad_z)[0]
            + sigma_p * weight * field
        )

    def restrict(resid):
        node_sums = (resid * inv_mult).sum(axis=(1, 3))
        elem_sums = jnp.dot(node_sums, block_table, precision=precision)
        return jnp.einsum("xyz,xyzk->k", elem_sums, one_hot, precision=precision)

    def spread_out(values):
        count = lax.axis_size("gx") * lax.axis_size("gy")
        copies = jnp.broadcast_to(values[None], (count,) + values.shape)
        return lax.all_to_all(copies, ("gx", "gy"), 0, 0, tiled=True)

    def gather_rest(resid):
        return spread_out(restrict(resid)).reshape(-1)

    def total(value):
        return jnp.sum(spread_out(value[None]))

    lower = cheb_ratio * spectral_bound
    cheb_theta = 0.5 * (spectral_bound + lower)
    cheb_delta = 0.5 * (spectral_bound - lower)

    def precondition(resid, restricted_all):
        coarse_values = jnp.dot(coarse_inverse, restricted_all, precision=precision)
        elem_values = jnp.einsum("xyzk,k->xyz", one_hot, coarse_values, precision=precision)
        spread = jnp.dot(elem_values, block_trans, precision=precision)[:, None, :, None, :]
        coarse_local = spread * inv_mult
        update = resid * inv_diag / cheb_theta
        smoothed = update
        cheb_rho = cheb_delta / cheb_theta
        local = op_local(smoothed)
        both = assemble(jnp.stack([local, coarse_local], 0))
        applied = both[0]
        coarse_term = both[1]
        defect = resid - applied
        rho_next = 1.0 / (2.0 * cheb_theta / cheb_delta - cheb_rho)
        update = rho_next * cheb_rho * update + 2.0 * rho_next / cheb_delta * defect * inv_diag
        smoothed = smoothed + update
        return smoothed + coarse_term

    pressure = jnp.zeros_like(rhs_p)
    resid = rhs_p
    restricted_all = gather_rest(resid)
    precond_r = precondition(resid, restricted_all)
    rz_value = total(jnp.sum(resid * precond_r * inv_mult))
    direction = precond_r
    for iteration in range(ITERS):
        last_turn = iteration + 1 == ITERS
        image = assemble(op_local(direction)[None])[0]
        partial_sum = jnp.sum(direction * image * inv_mult)
        curvature = total(partial_sum)
        step_size = rz_value / curvature
        pressure = pressure + step_size * direction
        if not last_turn:
            resid = resid - step_size * image
            restricted_all = gather_rest(resid)
            precond_r = precondition(resid, restricted_all)
            rz_next = total(jnp.sum(resid * precond_r * inv_mult))
            direction = precond_r + rz_next / rz_value * direction
            rz_value = rz_next
    return (fields_new, pressure)


def solution(mesh):
    placed = (
        P(None, "gx", None, "gy", None, None),
        P("gx", None, "gy", None, None),
        P("gx", "gy", None),
        P("gx", "gy", None),
        P(("gx", "gy"), None),
    )
    return jax.shard_map(
        per_device,
        mesh=mesh,
        in_specs=placed,
        out_specs=(P(None, "gx", None, "gy", None, None), P("gx", None, "gy", None, None)),
        check_vma=False,
    )
```

```python
import functools

import jax
import jax.numpy as jnp
import numpy as np
from jax import lax
from jax.experimental import pallas as pl
from jax.experimental.pallas import tpu as pltpu
from jax.sharding import PartitionSpec as P

NCD = 4
NODES = 8
LANES = 128
TILE = (8, 128)
BOTH = ("gx", "gy")

dt_step = 0.01
sigma_p = 4.0
prandtl = 0.7
cheb_ratio = 0.1


def tables():
    points = np.array(
        [
            -1.0,
            -0.8717401485096066,
            -0.5917001814331423,
            -0.2092992179024789,
            0.2092992179024789,
            0.5917001814331423,
            0.8717401485096066,
            1.0,
        ]
    )
    weights = np.array(
        [
            1.0 / 28.0,
            0.2107042271435061,
            0.3411226924835044,
            0.4124587946587038,
            0.4124587946587038,
            0.3411226924835044,
            0.2107042271435061,
            1.0 / 28.0,
        ]
    )
    identity = np.eye(8)
    differ = points[:, None] - points[None, :] + identity
    barycentric = 1.0 / np.prod(differ, axis=1)
    offdiag = barycentric[None, :] / barycentric[:, None] / differ * (1.0 - identity)
    derivative = offdiag - identity * np.sum(offdiag, axis=1)[:, None]
    mass_one = identity * weights[None, :]
    stiff_one = derivative.T @ mass_one @ derivative
    stiff_three = (
        np.kron(np.kron(stiff_one, mass_one), mass_one)
        + np.kron(np.kron(mass_one, stiff_one), mass_one)
        + np.kron(np.kron(mass_one, mass_one), stiff_one)
    )
    three_diag = np.sum(stiff_three * np.eye(512), axis=1)
    spectral_bound = float(np.max(np.sum(np.abs(stiff_three), axis=1) / three_diag))
    return (derivative, weights, stiff_one, spectral_bound)


DERIV, WEIGHTS, STIFF, BOUND = tables()
SCALED = STIFF / WEIGHTS[:, None]
LINE = np.diag(STIFF) / WEIGHTS
THETA = 0.5 * (BOUND + cheb_ratio * BOUND)
DELTA = 0.5 * (BOUND - cheb_ratio * BOUND)
RHO = DELTA / THETA
RHO_NEXT = 1.0 / (2.0 * THETA / DELTA - RHO)


def constant_tables(elems_z):
    def turned(matrix):
        rows = np.arange(8)
        return [np.repeat(matrix[rows, (rows - s) % 8][:, None], LANES, 1) for s in range(8)]

    wz = np.tile(WEIGHTS, elems_z)
    kz = np.tile(LINE, elems_z)
    tiles = turned(DERIV) + turned(DERIV.T) + turned(SCALED)
    tiles += [WEIGHTS[:, None] * wz[None, :], LINE[:, None] + kz[None, :]]
    eye = np.eye(elems_z)
    mats = [np.kron(eye, DERIV.T), np.kron(eye, DERIV), np.kron(eye, SCALED.T)]
    spread = np.kron(eye, np.ones((1, 8)))
    return (
        np.stack(tiles).astype(np.float32),
        np.stack(mats).astype(np.float32),
        spread.astype(np.float32),
    )


T_D, T_DT, T_K, T_W, T_LINE = 0, 8, 16, 24, 25


class Place:
    def __init__(self):
        self.ix = lax.axis_index("gx")
        self.iy = lax.axis_index("gy")
        self.nx = lax.axis_size("gx")
        self.ny = lax.axis_size("gy")
        self.even_x = self.ix % 2 == 0
        self.even_y = self.iy % 2 == 0
        self.row = lax.broadcasted_iota(jnp.int32, TILE, 0)
        self.lane = lax.broadcasted_iota(jnp.int32, TILE, 1)
        self.low_z = (self.lane % 8 == 0) & (self.lane > 0)
        self.high_z = (self.lane % 8 == 7) & (self.lane < LANES - 1)
        self.prev_x = self.ix > 0
        self.next_x = self.ix < self.nx - 1
        self.prev_y = self.iy > 0
        self.next_y = self.iy < self.ny - 1

    def mult_tile(self, ey):
        along_z = 1.0 + jnp.where(self.low_z | self.high_z, 1.0, 0.0)
        low = 1.0 if ey == 1 else jnp.where(self.prev_y, 1.0, 0.0)
        high = 1.0 if ey == 0 else jnp.where(self.next_y, 1.0, 0.0)
        along_y = 1.0 + jnp.where(self.row == 0, low, jnp.where(self.row == 7, high, 0.0))
        return along_y * along_z

    def inv_x(self, ex, a):
        if a == 0:
            return 0.5 if ex == 1 else jnp.where(self.prev_x, 0.5, 1.0)
        if a == 7:
            return 0.5 if ex == 0 else jnp.where(self.next_x, 0.5, 1.0)
        return 1.0

    def join_z(self, t):
        up = pltpu.roll(t, LANES - 1, 1)
        down = pltpu.roll(t, 1, 1)
        return t + jnp.where(self.high_z, up, jnp.where(self.low_z, down, 0.0))

    def to_low(self, below):
        return jnp.where(self.row == 0, pltpu.roll(below, 1, 0), 0.0)

    def to_high(self, above):
        return jnp.where(self.row == 7, pltpu.roll(above, 7, 0), 0.0)

    def join_y(self, below, above):
        return below + self.to_high(above), above + self.to_low(below)

    def before_x(self, first, second):
        return jnp.where(self.even_x, second, first)

    def after_x(self, first, second):
        return jnp.where(self.even_x, first, second)

    def before_y(self, first, second):
        return jnp.where(self.even_y, second, first)

    def after_y(self, first, second):
        return jnp.where(self.even_y, first, second)


def along_x(matrix, tiles):
    out = []
    for i in range(8):
        acc = None
        for a in range(8):
            term = float(matrix[i, a]) * tiles[a]
            acc = term if acc is None else acc + term
        out.append(acc)
    return out


def along_y(ctab, base, tile):
    acc = ctab[base] * tile
    for s in range(1, 8):
        acc = acc + ctab[base + s] * pltpu.roll(tile, s, 0)
    return acc


def along_z(rows, matrix):
    return jnp.dot(
        rows, matrix, precision=lax.Precision.HIGHEST, preferred_element_type=jnp.float32
    )


def total(tile):
    return jnp.sum(jnp.sum(tile, axis=0, keepdims=True), axis=1, keepdims=True)


def store_y_faces(place, field, first_out, second_out, lead, at):
    for ex in range(2):
        for a in range(8):
            low = field[lead + (ex, a, 0, pl.ds(0, 1), slice(None))]
            high = field[lead + (ex, a, 1, pl.ds(7, 1), slice(None))]
            row = at + ex * 8 + a
            first_out[pl.ds(row, 1), :] = place.after_y(high, low)
            second_out[pl.ds(row, 1), :] = place.after_y(low, high)


def join_own(place, tiles):
    for ex in range(2):
        for a in range(8):
            tiles[ex][a] = list(place.join_y(*tiles[ex][a]))
    for ey in range(2):
        both = tiles[0][7][ey] + tiles[1][0][ey]
        tiles[0][7][ey] = both
        tiles[1][0][ey] = both


def mass_kernel(pack_rows, fields, kappa, group, coarse, ctab, spread, out, xf, pack, first, second):
    place = Place()
    spread_v = spread[...]
    pack[...] = jnp.zeros(pack.shape, jnp.float32)
    pack[pl.ds(0, 4), :] = along_z(kappa[...], spread_v)
    pack[pl.ds(4, 4), :] = along_z(group[...].astype(jnp.float32), spread_v)
    pack[pl.ds(8, coarse.shape[0]), :] = coarse[...]
    first[pl.ds(64, pack_rows), :] = pack[...]
    second[pl.ds(64, pack_rows), :] = pack[...]
    weight = ctab[T_W]

    def channel(ch, carry):
        tiles = [
            [
                [
                    place.join_z(fields[ch, ex, a, ey] * (float(WEIGHTS[a]) * weight))
                    for ey in range(2)
                ]
                for a in range(8)
            ]
            for ex in range(2)
        ]
        join_own(place, tiles)
        for ex in range(2):
            for a in range(8):
                for ey in range(2):
                    out[ch, ex, a, ey] = tiles[ex][a][ey]
        for ey in range(2):
            xf[0, ch, ey] = tiles[0][0][ey]
            xf[1, ch, ey] = tiles[1][7][ey]
        store_y_faces(place, out, first, second, (ch,), ch * 16)
        return carry

    lax.fori_loop(0, 4, channel, 0)


def turn_faces_kernel(pack_rows, xf, *refs):
    place = Place()
    if pack_rows:
        pack, y_first, y_second, first, second = refs
    else:
        y_first, y_second, first, second = refs
    for ch in range(4):
        sides = []
        for side in range(2):
            row = pl.ds(ch * 16 + 15 * side, 1)
            got_a, got_b = y_first[row, :], y_second[row, :]
            low = xf[side, ch, 0] + jnp.where(place.row == 0, place.before_y(got_a, got_b), 0.0)
            high = xf[side, ch, 1] + jnp.where(place.row == 7, place.after_y(got_a, got_b), 0.0)
            sides.append((low, high))
        for ey in range(2):
            rows = pl.ds(ch * 16 + ey * 8, 8)
            first[rows, :] = place.after_x(sides[1][ey], sides[0][ey])
            second[rows, :] = place.after_x(sides[0][ey], sides[1][ey])
    if pack_rows:
        came = pl.ds(64, pack_rows)
        parts = (
            place.before_y(y_first[came, :], y_second[came, :]),
            pack[...],
            place.after_y(y_first[came, :], y_second[came, :]),
        )
        for k in range(3):
            rows = pl.ds(64 + k * pack_rows, pack_rows)
            first[rows, :] = parts[k]
            second[rows, :] = parts[k]


def setup_kernel(
    pack_rows, blocks, pack, y_first, y_second, x_first, x_second, ctab, inv_diag, kap, grp, coarse
):
    place = Place()
    came = pl.ds(64, pack_rows)
    packs = [[None] * 3 for _ in range(3)]
    packs[1][0] = place.before_y(y_first[came, :], y_second[came, :])
    packs[1][1] = pack[...]
    packs[1][2] = place.after_y(y_first[came, :], y_second[came, :])
    for k in range(3):
        rows = pl.ds(64 + k * pack_rows, pack_rows)
        packs[0][k] = place.before_x(x_first[rows, :], x_second[rows, :])
        packs[2][k] = place.after_x(x_first[rows, :], x_second[rows, :])
    for dx in range(3):
        for dy in range(3):
            at = (dx * 3 + dy) * NCD * blocks
            coarse[pl.ds(at, NCD * blocks), :] = packs[dx][dy][8 : 8 + NCD * blocks]
    there_x = [jnp.where(place.prev_x, 1.0, 0.0), 1.0, jnp.where(place.next_x, 1.0, 0.0)]
    there_y = [jnp.where(place.prev_y, 1.0, 0.0), 1.0, jnp.where(place.next_y, 1.0, 0.0)]

    def element_row(base, u, v):
        row = base + (u % 2) * 2 + v % 2
        return packs[u // 2][v // 2][row : row + 1]

    for x in range(4):
        for y in range(4):
            kap[pl.ds(x * 4 + y, 1), :] = element_row(0, x + 1, y + 1)
            grp[pl.ds(x * 4 + y, 1), :] = element_row(4, x + 1, y + 1)
    kappa = [
        [
            place.join_z(jnp.broadcast_to(element_row(0, u, v), TILE)) if True else None
            for v in range(6)
        ]
        for u in range(6)
    ]
    count_z = 1.0 + jnp.where(place.low_z | place.high_z, 1.0, 0.0)
    weight = ctab[T_W]
    line = ctab[T_LINE]

    def pick(values, y):
        low = values[y] + values[y + 1]
        high = values[y + 1] + values[y + 2]
        return jnp.where(place.row == 0, low, jnp.where(place.row == 7, high, values[y + 1]))

    for x in range(4):
        for kind in range(3):
            us = {0: (x, x + 1), 1: (x + 1,), 2: (x + 1, x + 2)}[kind]
            sums, counts = [], []
            for v in range(6):
                acc, num = None, 0.0
                for u in us:
                    acc = kappa[u][v] if acc is None else acc + kappa[u][v]
                    num = num + there_x[u // 2]
                sums.append(acc)
                counts.append(num * there_y[v // 2])
            for y in range(4):
                kappa_sum = pick(sums, y)
                mult = pick(counts, y) * count_z
                present = there_x[(x + 1) // 2] * there_y[(y + 1) // 2] > 0.5
                for a in {0: (0,), 1: range(1, 7), 2: (7,)}[kind]:
                    diag = (float(LINE[a]) + line) * kappa_sum + sigma_p * mult
                    diag = diag * (float(WEIGHTS[a]) * weight)
                    inv_diag[x, a, y] = jnp.where(present, 1.0 / diag, 0.0)


def got_face_sum(place, tile, ch, ex, a, ey, y_first, y_second, x_first, x_second):
    row = pl.ds(ch * 16 + ex * 8 + a, 1)
    got_a, got_b = y_first[row, :], y_second[row, :]
    if ey == 0:
        tile = tile + jnp.where(place.row == 0, place.before_y(got_a, got_b), 0.0)
    else:
        tile = tile + jnp.where(place.row == 7, place.after_y(got_a, got_b), 0.0)
    rows = pl.ds(pl.multiple_of(ch * 16 + ey * 8, 8), 8)
    if ex == 0 and a == 0:
        tile = tile + place.before_x(x_first[rows, :], x_second[rows, :])
    if ex == 1 and a == 7:
        tile = tile + place.after_x(x_first[rows, :], x_second[rows, :])
    return tile


def rhs_kernel(
    summed,
    visc,
    y_first,
    y_second,
    x_first,
    x_second,
    ctab,
    zmat,
    start,
    rhs,
    xf,
    first,
    second,
    grad_z,
    flux_z,
):
    place = Place()
    weight = ctab[T_W]
    inv_mass = [1.0 / (weight * place.mult_tile(ey)) for ey in range(2)]

    def begin(ch, carry):
        for ex in range(2):
            for a in range(8):
                for ey in range(2):
                    tile = got_face_sum(
                        place, summed[ch, ex, a, ey], ch, ex, a, ey,
                        y_first, y_second, x_first, x_second,
                    )
                    scale = place.inv_x(ex, a) * float(1.0 / WEIGHTS[a])
                    start[ch, ex, a, ey] = tile * (inv_mass[ey] * scale)
        return carry

    lax.fori_loop(0, 4, begin, 0)
    grad_z[...] = along_z(start[...].reshape(1024, LANES), zmat[0]).reshape(grad_z.shape)

    def column(index, carry):
        ch, ex, ey = index // 4, index // 2 % 2, index % 2
        coef = jnp.where(ch == 3, 1.0 / prandtl, 1.0)
        field = [start[ch, ex, a, ey] for a in range(8)]
        grad_x = along_x(DERIV, field)
        flux_x, parts = [], []
        for a in range(8):
            grad_y = along_y(ctab, T_D, field[a])
            slope = grad_z[ch, ex, a, ey]
            node = float(WEIGHTS[a]) * weight
            advect = (
                start[0, ex, a, ey] * grad_x[a]
                + start[1, ex, a, ey] * grad_y
                + start[2, ex, a, ey] * slope
            )
            nu = visc[ex, a, ey] * node * coef
            flux_x.append(nu * grad_x[a])
            flux_z[ch, ex, a, ey] = nu * slope
            parts.append(node * advect + along_y(ctab, T_DT, nu * grad_y))
        back = along_x(DERIV.T, flux_x)
        for a in range(8):
            rhs[ch, ex, a, ey] = parts[a] + back[a]
        return carry

    lax.fori_loop(0, 16, column, 0)
    grad_z[...] = along_z(flux_z[...].reshape(1024, LANES), zmat[1]).reshape(grad_z.shape)

    def finish(ch, carry):
        tiles = [
            [
                [
                    place.join_z(-(rhs[ch, ex, a, ey] + grad_z[ch, ex, a, ey]))
                    for ey in range(2)
                ]
                for a in range(8)
            ]
            for ex in range(2)
        ]
        join_own(place, tiles)
        for ex in range(2):
            for a in range(8):
                for ey in range(2):
                    rhs[ch, ex, a, ey] = tiles[ex][a][ey]
        for ey in range(2):
            xf[0, ch, ey] = tiles[0][0][ey]
            xf[1, ch, ey] = tiles[1][7][ey]
        store_y_faces(place, rhs, first, second, (ch,), ch * 16)
        return carry

    lax.fori_loop(0, 4, finish, 0)


def store_own(place, tiles, out, first, second):
    join_own(place, tiles)
    for ex in range(2):
        for a in range(8):
            low, high = tiles[ex][a]
            out[ex, a, 0] = low
            out[ex, a, 1] = high
            first[ex, a] = place.after_y(high, low)
            second[ex, a] = place.after_y(low, high)


def advance_kernel(
    start,
    rhs,
    y_first,
    y_second,
    x_first,
    x_second,
    ctab,
    zmat,
    fields_new,
    out,
    first,
    second,
    grad_z,
):
    place = Place()
    weight = ctab[T_W]
    inv_mass = [dt_step / (weight * place.mult_tile(ey)) for ey in range(2)]

    def step(ch, carry):
        for ex in range(2):
            for a in range(8):
                for ey in range(2):
                    tile = got_face_sum(
                        place, rhs[ch, ex, a, ey], ch, ex, a, ey,
                        y_first, y_second, x_first, x_second,
                    )
                    scale = place.inv_x(ex, a) * float(1.0 / WEIGHTS[a])
                    fields_new[ch, ex, a, ey] = start[ch, ex, a, ey] + tile * (
                        inv_mass[ey] * scale
                    )
        return carry

    lax.fori_loop(0, 4, step, 0)
    grad_z[...] = along_z(fields_new[2].reshape(256, LANES), zmat[0]).reshape(grad_z.shape)
    tiles = [[[None, None] for _ in range(8)] for _ in range(2)]
    for ex in range(2):
        for ey in range(2):
            slope = along_x(DERIV, [fields_new[0, ex, a, ey] for a in range(8)])
            for a in range(8):
                div = slope[a] + along_y(ctab, T_D, fields_new[1, ex, a, ey]) + grad_z[ex, a, ey]
                tiles[ex][a][ey] = place.join_z(div * (float(-WEIGHTS[a]) * weight))
    store_own(place, tiles, out, first, second)


def turn_columns_kernel(own, y_first, y_second, first, second):
    place = Place()

    def line(a, carry):
        for y in range(4):
            sides = []
            for ex in range(2):
                if y in (1, 2):
                    sides.append(own[ex, a, y - 1])
                elif y == 0:
                    sides.append(place.before_y(y_first[ex, a], y_second[ex, a]))
                else:
                    sides.append(place.after_y(y_first[ex, a], y_second[ex, a]))
            first[a, y] = place.after_x(sides[1], sides[0])
            second[a, y] = place.after_x(sides[0], sides[1])
        return carry

    lax.fori_loop(0, 8, line, 0)


def restricted(place, sums, grp):
    values = []
    for c in range(NCD):
        acc = jnp.zeros(TILE, jnp.float32)
        for ex in range(2):
            for ey in range(2):
                group = grp[pl.ds((ex + 1) * 4 + ey + 1, 1), :]
                acc = acc + jnp.where(group == float(c), sums[ex][ey], 0.0)
        values.append(total(acc))
    return values


def message(place, own_values, scalars):
    lane = lax.broadcasted_iota(jnp.int32, (1, LANES), 1)
    spot = (place.ix * place.ny + place.iy) % (LANES // NCD)
    after = (spot + 1) % (LANES // NCD)
    row = jnp.zeros((1, LANES), jnp.float32)
    for c, value in enumerate(own_values):
        row = row + jnp.where(lane == spot * NCD + c, value, 0.0)
    for c, value in enumerate(scalars):
        row = row + jnp.where(lane == after * NCD + c, value, 0.0)
    return row


def smooth_kernel(
    own,
    y_first,
    y_second,
    x_first,
    x_second,
    inv_diag,
    kap,
    grp,
    extra,
    ctab,
    zmat,
    resid,
    smoothed,
    msg,
    ext,
    scaled,
    local,
    edge,
):
    place = Place()
    weight = ctab[T_W]

    def raw(x, a, y):
        if x in (1, 2):
            if y in (1, 2):
                return own[x - 1, a, y - 1]
            if y == 0:
                return place.before_y(y_first[x - 1, a], y_second[x - 1, a])
            return place.after_y(y_first[x - 1, a], y_second[x - 1, a])
        if x == 0:
            return place.before_x(x_first[a, y], x_second[a, y])
        return place.after_x(x_first[a, y], x_second[a, y])

    def put(x, a, tiles):
        low = place.join_y(tiles[0], tiles[1])
        high = place.join_y(tiles[2], tiles[3])
        for y, tile in enumerate(low + high):
            ext[x, a, y] = tile
            scaled[x, a, y] = tile * inv_diag[x, a, y] * float(1.0 / THETA)

    joined = {}
    for x, a, x2, a2 in ((0, 7, 1, 0), (2, 7, 3, 0)):
        both = [raw(x, a, y) + raw(x2, a2, y) for y in range(4)]
        put(x, a, both)
        put(x2, a2, both)
        joined[(x, a)] = joined[(x2, a2)] = True

    for x in range(4):
        first = 1 if (x, 0) in joined else 0
        last = 7 if (x, 7) in joined else 8

        def fill(a, carry, x=x):
            put(x, a, [raw(x, a, y) for y in range(4)])
            return carry

        lax.fori_loop(first, last, fill, 0)

    local[...] = along_z(scaled[pl.ds(1, 2)].reshape(512, LANES), zmat[2]).reshape(local.shape)
    edge[pl.ds(0, 4)] = along_z(scaled[0, 7].reshape(32, LANES), zmat[2]).reshape(4, 8, LANES)
    edge[pl.ds(4, 4)] = along_z(scaled[3, 0].reshape(32, LANES), zmat[2]).reshape(4, 8, LANES)

    def finish_tile(tile, a, slope, x, y):
        kappa = kap[pl.ds(x * 4 + y, 1), :]
        stiff = slope + along_y(ctab, T_K, tile)
        return (kappa * stiff + sigma_p * tile) * (float(WEIGHTS[a]) * weight)

    def column(y, carry):
        for x in (1, 2):
            tiles = [scaled[x, a, y] for a in range(8)]
            slopes = along_x(SCALED, tiles)
            for a in range(8):
                local[x - 1, a, y] = finish_tile(tiles[a], a, slopes[a] + local[x - 1, a, y], x, y)
        for x, a, at in ((0, 7, 0), (3, 0, 4)):
            slope = edge[at + y]
            for k in range(8):
                slope = slope + float(SCALED[a, k]) * scaled[x, k, y]
            edge[at + y] = finish_tile(scaled[x, a, y], a, slope, x, y)
        return carry

    lax.fori_loop(0, 4, column, 0)
    inv_mult = [1.0 / place.mult_tile(ey) for ey in range(2)]
    sums = [[jnp.zeros(TILE, jnp.float32) for _ in range(2)] for _ in range(2)]
    for x in (1, 2):
        for a in range(8):
            if (x, a) == (1, 0):
                tiles = [local[0, 0, y] + edge[y] for y in range(4)]
            elif (x, a) == (2, 7):
                tiles = [local[1, 7, y] + edge[4 + y] for y in range(4)]
            elif (x, a) in ((1, 7), (2, 0)):
                tiles = [local[0, 7, y] + local[1, 0, y] for y in range(4)]
            else:
                tiles = [local[x - 1, a, y] for y in range(4)]
            low = tiles[1] + place.to_low(tiles[0]) + place.to_high(tiles[2])
            high = tiles[2] + place.to_low(tiles[1]) + place.to_high(tiles[3])
            for ey, image in enumerate((low, high)):
                image = place.join_z(image)
                value = ext[x, a, ey + 1]
                update = scaled[x, a, ey + 1]
                defect = (value - image) * inv_diag[x, a, ey + 1]
                resid[x - 1, a, ey] = value
                smoothed[x - 1, a, ey] = (
                    float(1.0 + RHO_NEXT * RHO) * update + float(2.0 * RHO_NEXT / DELTA) * defect
                )
                scale = place.inv_x(x - 1, a)
                sums[x - 1][ey] = sums[x - 1][ey] + value * (inv_mult[ey] * scale)
    row = message(place, restricted(place, sums, grp), []) + extra[...]
    for i in range(msg.shape[0]):
        msg[i] = row


def coarse_part(place, blocks, got, coarse, grp):
    lane = lax.broadcasted_iota(jnp.int32, (1, LANES), 1)
    values = [jnp.zeros((1, LANES), jnp.float32) for _ in range(blocks)]
    per = LANES // NCD
    for i in range(got.shape[0]):
        values[i // per] = jnp.where(lane // NCD == i % per, got[i], values[i // per])

    def solved(dx, dy, c):
        acc = None
        for j in range(blocks):
            term = coarse[pl.ds(((dx * 3 + dy) * NCD + c) * blocks + j, 1), :] * values[j]
            acc = term if acc is None else acc + term
        return jnp.sum(acc, axis=1, keepdims=True)

    device = [[[solved(dx, dy, c) for c in range(NCD)] for dy in range(3)] for dx in range(3)]
    inv_z = jnp.where(place.low_z | place.high_z, 0.5, 1.0)
    rows = []
    for x in range(4):
        line = []
        for y in range(4):
            group = grp[pl.ds(x * 4 + y, 1), :]
            acc = jnp.zeros((1, LANES), jnp.float32)
            for c in range(NCD):
                acc = acc + jnp.where(
                    group == float(c), device[(x + 1) // 2][(y + 1) // 2][c], 0.0
                )
            line.append(place.join_z(jnp.broadcast_to(acc, TILE)) * inv_z)
        rows.append(line)
    low_y = jnp.where(place.prev_y, 0.5, 1.0)
    high_y = jnp.where(place.next_y, 0.5, 1.0)

    def tile(ex, kind, ey):
        if kind == 1:
            vals = [rows[ex + 1][y] for y in range(4)]
        elif kind == 0:
            scale = place.inv_x(ex, 0)
            vals = [(rows[ex][y] + rows[ex + 1][y]) * scale for y in range(4)]
        else:
            scale = place.inv_x(ex, 7)
            vals = [(rows[ex + 1][y] + rows[ex + 2][y]) * scale for y in range(4)]
        mid = vals[ey + 1]
        low = (vals[ey] + mid) * (low_y if ey == 0 else 0.5)
        high = (mid + vals[ey + 2]) * (high_y if ey == 1 else 0.5)
        return jnp.where(place.row == 0, low, jnp.where(place.row == 7, high, mid))

    return tile


def kind_of(a):
    return 0 if a == 0 else (2 if a == 7 else 1)


def own_operator(ctab, kap, field, slope_z, ex, ey):
    weight = ctab[T_W]
    tiles = [field[ex, a, ey] for a in range(8)]
    slopes = along_x(SCALED, tiles)
    kappa = kap[pl.ds((ex + 1) * 4 + ey + 1, 1), :]
    out = []
    for a in range(8):
        stiff = slopes[a] + along_y(ctab, T_K, tiles[a]) + slope_z[ex, a, ey]
        out.append((kappa * stiff + sigma_p * tiles[a]) * (float(WEIGHTS[a]) * weight))
    return tiles, out


def first_direction_kernel(
    blocks, got, coarse, grp, kap, resid, smoothed, ctab, zmat, direction, out, first, second, extra, slope_z
):
    place = Place()
    inv_mult = [1.0 / place.mult_tile(ey) for ey in range(2)]
    part = coarse_part(place, blocks, got, coarse, grp)
    energy = jnp.zeros(TILE, jnp.float32)
    for ex in range(2):
        for ey in range(2):
            kinds = [part(ex, kind, ey) for kind in range(3)]
            for a in range(8):
                value = smoothed[ex, a, ey] + kinds[kind_of(a)]
                direction[ex, a, ey] = value
                scale = place.inv_x(ex, a)
                energy = energy + value * resid[ex, a, ey] * (inv_mult[ey] * scale)
    slope_z[...] = along_z(direction[...].reshape(256, LANES), zmat[2]).reshape(slope_z.shape)
    curvature = jnp.zeros(TILE, jnp.float32)
    tiles = [[[None, None] for _ in range(8)] for _ in range(2)]
    for ex in range(2):
        for ey in range(2):
            values, images = own_operator(ctab, kap, direction, slope_z, ex, ey)
            for a in range(8):
                curvature = curvature + values[a] * images[a]
                tiles[ex][a][ey] = place.join_z(images[a])
    store_own(place, tiles, out, first, second)
    extra[...] = message(place, [], [total(energy), total(curvature)])


def gathered_scalars(got, count):
    lane = lax.broadcasted_iota(jnp.int32, (1, LANES), 1)
    per = LANES // NCD
    sums = []
    for c in range(count):
        acc = jnp.zeros((1, LANES), jnp.float32)
        for i in range(got.shape[0]):
            acc = acc + jnp.where(lane == ((i + 1) % per) * NCD + c, got[i], 0.0)
        sums.append(jnp.sum(acc, axis=1, keepdims=True))
    return sums


def second_direction_kernel(
    blocks,
    got,
    coarse,
    grp,
    kap,
    resid,
    direction,
    image,
    smoothed,
    ctab,
    zmat,
    following,
    known,
    msg,
    slope_z,
):
    place = Place()
    inv_mult = [1.0 / place.mult_tile(ey) for ey in range(2)]
    part = coarse_part(place, blocks, got, coarse, grp)
    energy, curvature = gathered_scalars(got, 2)
    step = energy / curvature
    lane = lax.broadcasted_iota(jnp.int32, (1, LANES), 1)
    known[...] = jnp.where(lane == 0, energy, jnp.where(lane == 1, curvature, 0.0))
    energy_next = jnp.zeros(TILE, jnp.float32)
    cross = jnp.zeros(TILE, jnp.float32)
    for ex in range(2):
        for ey in range(2):
            kinds = [part(ex, kind, ey) for kind in range(3)]
            for a in range(8):
                value = direction[ex, a, ey] - step * (smoothed[ex, a, ey] + kinds[kind_of(a)])
                following[ex, a, ey] = value
                weighed = value * (inv_mult[ey] * place.inv_x(ex, a))
                was = image[ex, a, ey]
                energy_next = energy_next + weighed * (resid[ex, a, ey] - step * was)
                cross = cross + weighed * was
    slope_z[...] = along_z(following[...].reshape(256, LANES), zmat[2]).reshape(slope_z.shape)
    square = jnp.zeros(TILE, jnp.float32)
    for ex in range(2):
        for ey in range(2):
            values, images = own_operator(ctab, kap, following, slope_z, ex, ey)
            for a in range(8):
                square = square + values[a] * images[a]
    row = message(place, [], [total(energy_next), total(square), total(cross)])
    for i in range(msg.shape[0]):
        msg[i] = row


def pressure_kernel(got, known, direction, following, pressure):
    energy = known[:, pl.ds(0, 1)]
    curvature = known[:, pl.ds(1, 1)]
    energy_next, square, cross = gathered_scalars(got, 3)
    ratio = energy_next / energy
    step = energy / curvature
    step_next = energy_next / (square + 2.0 * ratio * cross + ratio * ratio * curvature)
    weight_old = step + step_next * ratio
    for ex in range(2):
        for a in range(8):
            for ey in range(2):
                pressure[ex, a, ey] = (
                    weight_old * direction[ex, a, ey] + step_next * following[ex, a, ey]
                )


def call(body, outs, scratch=()):
    return pl.pallas_call(
        body,
        out_shape=[jax.ShapeDtypeStruct(shape, jnp.float32) for shape in outs],
        scratch_shapes=[pltpu.VMEM(shape, jnp.float32) for shape in scratch],
        compiler_params=pltpu.CompilerParams(vmem_limit_bytes=24 * 1024 * 1024),
    )


def swap(first, second, axis):
    count = lax.axis_size(axis)
    first_pairs = [(i, i ^ 1) for i in range(count) if i ^ 1 < count]
    second_pairs = [(i, ((i + 1) ^ 1) - 1) for i in range(1, count) if ((i + 1) ^ 1) - 1 < count]
    return (
        lax.ppermute(first, axis, first_pairs),
        lax.ppermute(second, axis, second_pairs),
    )


def per_device(fields, viscosity, inv_density, elem_group, coarse_inverse):
    length = fields.shape[5]
    elems_z = length // NODES
    devices = lax.axis_size("gx") * lax.axis_size("gy")
    blocks = coarse_inverse.shape[1] // LANES
    pack_rows = -(-(8 + NCD * blocks) // 8) * 8
    tiles_np, mats_np, spread_np = constant_tables(elems_z)
    ctab, zmat, spread = jnp.asarray(tiles_np), jnp.asarray(mats_np), jnp.asarray(spread_np)
    one = fields.shape[1:]
    four = fields.shape
    xf_shape = (2, 4, 2, 8, LANES)
    faces = (64, LANES)
    ext = (4, 8, 4, 8, LANES)
    column = (2, 8, 8, LANES)
    wide = (8, 4, 8, LANES)
    rows = (devices, 1, LANES)

    def exchange_all(msg):
        return lax.all_to_all(msg, BOTH, 0, 0, tiled=True)

    summed, xf, pack, first, second = call(
        functools.partial(mass_kernel, pack_rows),
        [four, xf_shape, (pack_rows, LANES), (64 + pack_rows, LANES), (64 + pack_rows, LANES)],
    )(
        fields,
        inv_density.reshape(4, elems_z),
        elem_group.reshape(4, elems_z),
        coarse_inverse.reshape(NCD * blocks, LANES),
        ctab,
        spread,
    )
    y_got = swap(first, second, "gy")
    x_shape = (64 + 3 * pack_rows, LANES)
    first, second = call(functools.partial(turn_faces_kernel, pack_rows), [x_shape, x_shape])(
        xf, pack, *y_got
    )
    x_got = swap(first, second, "gx")
    inv_diag, kap, grp, coarse = call(
        functools.partial(setup_kernel, pack_rows, blocks),
        [ext, (16, LANES), (16, LANES), (9 * NCD * blocks, LANES)],
    )(pack, *y_got, *x_got, ctab)
    start, rhs, xf, first, second = call(
        rhs_kernel, [four, four, xf_shape, faces, faces], [four, four]
    )(summed, viscosity, *y_got, *x_got, ctab, zmat)
    y_got = swap(first, second, "gy")
    first, second = call(functools.partial(turn_faces_kernel, 0), [faces, faces])(xf, *y_got)
    x_got = swap(first, second, "gx")
    fields_new, own, first, second = call(
        advance_kernel, [four, one, column, column], [one]
    )(start, rhs, *y_got, *x_got, ctab, zmat)

    def smooth(own, first, second, extra):
        y_got = swap(first, second, "gy")
        first, second = call(turn_columns_kernel, [wide, wide])(own, *y_got)
        x_got = swap(first, second, "gx")
        return call(
            smooth_kernel, [one, one, rows], [ext, ext, (2,) + ext[1:], (8, 8, LANES)]
        )(own, *y_got, *x_got, inv_diag, kap, grp, extra, ctab, zmat)

    resid, smoothed, msg = smooth(own, first, second, jnp.zeros((1, LANES), jnp.float32))
    got = exchange_all(msg)
    direction, own, first, second, extra = call(
        functools.partial(first_direction_kernel, blocks),
        [one, one, column, column, (1, LANES)],
        [one],
    )(got, coarse, grp, kap, resid, smoothed, ctab, zmat)
    image, image_smoothed, msg = smooth(own, first, second, extra)
    got = exchange_all(msg)
    following, known, msg = call(
        functools.partial(second_direction_kernel, blocks), [one, (1, LANES), rows], [one]
    )(got, coarse, grp, kap, resid, direction, image, image_smoothed, ctab, zmat)
    got = exchange_all(msg)
    (pressure,) = call(pressure_kernel, [one])(got, known, direction, following)
    return (fields_new, pressure)


def solution(mesh):
    placed = (
        P(None, "gx", None, "gy", None, None),
        P("gx", None, "gy", None, None),
        P("gx", "gy", None),
        P("gx", "gy", None),
        P(("gx", "gy"), None),
    )
    return jax.shard_map(
        per_device,
        mesh=mesh,
        in_specs=placed,
        out_specs=(P(None, "gx", None, "gy", None, None), P("gx", None, "gy", None, None)),
        check_vma=False,
    )
```

```python
import functools

import jax
import jax.numpy as jnp
import numpy as np
from jax import lax
from jax.experimental import pallas as pl
from jax.experimental.pallas import tpu as pltpu
from jax.sharding import PartitionSpec as P

NCD = 4
NODES = 8
LANES = 128
TILE = (8, 128)
BOTH = ("gx", "gy")

dt_step = 0.01
sigma_p = 4.0
prandtl = 0.7
cheb_ratio = 0.1


def tables():
    points = np.array(
        [
            -1.0,
            -0.8717401485096066,
            -0.5917001814331423,
            -0.2092992179024789,
            0.2092992179024789,
            0.5917001814331423,
            0.8717401485096066,
            1.0,
        ]
    )
    weights = np.array(
        [
            1.0 / 28.0,
            0.2107042271435061,
            0.3411226924835044,
            0.4124587946587038,
            0.4124587946587038,
            0.3411226924835044,
            0.2107042271435061,
            1.0 / 28.0,
        ]
    )
    identity = np.eye(8)
    differ = points[:, None] - points[None, :] + identity
    barycentric = 1.0 / np.prod(differ, axis=1)
    offdiag = barycentric[None, :] / barycentric[:, None] / differ * (1.0 - identity)
    derivative = offdiag - identity * np.sum(offdiag, axis=1)[:, None]
    mass_one = identity * weights[None, :]
    stiff_one = derivative.T @ mass_one @ derivative
    stiff_three = (
        np.kron(np.kron(stiff_one, mass_one), mass_one)
        + np.kron(np.kron(mass_one, stiff_one), mass_one)
        + np.kron(np.kron(mass_one, mass_one), stiff_one)
    )
    three_diag = np.sum(stiff_three * np.eye(512), axis=1)
    spectral_bound = float(np.max(np.sum(np.abs(stiff_three), axis=1) / three_diag))
    return (derivative, weights, stiff_one, spectral_bound)


DERIV, WEIGHTS, STIFF, BOUND = tables()
SCALED = STIFF / WEIGHTS[:, None]
LINE = np.diag(STIFF) / WEIGHTS
THETA = 0.5 * (BOUND + cheb_ratio * BOUND)
DELTA = 0.5 * (BOUND - cheb_ratio * BOUND)
RHO = DELTA / THETA
RHO_NEXT = 1.0 / (2.0 * THETA / DELTA - RHO)


def constant_tables(elems_z):
    def turned(matrix):
        rows = np.arange(8)
        return [np.repeat(matrix[rows, (rows - s) % 8][:, None], LANES, 1) for s in range(8)]

    wz = np.tile(WEIGHTS, elems_z)
    kz = np.tile(LINE, elems_z)
    tiles = turned(DERIV) + turned(DERIV.T) + turned(SCALED)
    tiles += [WEIGHTS[:, None] * wz[None, :], LINE[:, None] + kz[None, :]]
    tiles += [np.repeat(DERIV[7][:, None], LANES, 1), np.repeat(DERIV[0][:, None], LANES, 1)]
    eye = np.eye(elems_z)
    mats = [np.kron(eye, DERIV.T), np.kron(eye, DERIV), np.kron(eye, SCALED.T)]
    return np.stack(tiles).astype(np.float32), np.stack(mats).astype(np.float32)


T_D, T_DT, T_K, T_W, T_LINE, T_TOP, T_BOTTOM = 0, 8, 16, 24, 25, 26, 27


class Place:
    def __init__(self):
        self.ix = lax.axis_index("gx")
        self.iy = lax.axis_index("gy")
        self.nx = lax.axis_size("gx")
        self.ny = lax.axis_size("gy")
        self.even_x = self.ix % 2 == 0
        self.even_y = self.iy % 2 == 0
        self.row = lax.broadcasted_iota(jnp.int32, TILE, 0)
        self.lane = lax.broadcasted_iota(jnp.int32, TILE, 1)
        self.low_z = (self.lane % 8 == 0) & (self.lane > 0)
        self.high_z = (self.lane % 8 == 7) & (self.lane < LANES - 1)
        self.prev_x = self.ix > 0
        self.next_x = self.ix < self.nx - 1
        self.prev_y = self.iy > 0
        self.next_y = self.iy < self.ny - 1

    def mult_tile(self, ey):
        along_z = 1.0 + jnp.where(self.low_z | self.high_z, 1.0, 0.0)
        low = 1.0 if ey == 1 else jnp.where(self.prev_y, 1.0, 0.0)
        high = 1.0 if ey == 0 else jnp.where(self.next_y, 1.0, 0.0)
        along_y = 1.0 + jnp.where(self.row == 0, low, jnp.where(self.row == 7, high, 0.0))
        return along_y * along_z

    def inv_x(self, ex, a):
        if a == 0:
            return 0.5 if ex == 1 else jnp.where(self.prev_x, 0.5, 1.0)
        if a == 7:
            return 0.5 if ex == 0 else jnp.where(self.next_x, 0.5, 1.0)
        return 1.0

    def mult_x(self, ex, a):
        if a == 0:
            return 2.0 if ex == 1 else jnp.where(self.prev_x, 2.0, 1.0)
        if a == 7:
            return 2.0 if ex == 0 else jnp.where(self.next_x, 2.0, 1.0)
        return 1.0

    def share_x(self, ex, a):
        if (ex, a) == (0, 0):
            return jnp.where(self.prev_x, 0.5, 1.0)
        if (ex, a) == (1, 7):
            return jnp.where(self.next_x, 0.5, 1.0)
        return 1.0

    def share_y(self, ey):
        if ey == 0:
            return jnp.where((self.row == 0) & self.prev_y, 0.5, 1.0)
        return jnp.where((self.row == 7) & self.next_y, 0.5, 1.0)

    def inv_y(self, ey):
        low = 0.5 if ey == 1 else jnp.where(self.prev_y, 0.5, 1.0)
        high = 0.5 if ey == 0 else jnp.where(self.next_y, 0.5, 1.0)
        return jnp.where(self.row == 0, low, jnp.where(self.row == 7, high, 1.0))

    def inv_z(self):
        return jnp.where(self.low_z | self.high_z, 0.5, 1.0)

    def join_z(self, t):
        up = pltpu.roll(t, LANES - 1, 1)
        down = pltpu.roll(t, 1, 1)
        return t + jnp.where(self.high_z, up, jnp.where(self.low_z, down, 0.0))

    def to_low(self, below):
        return jnp.where(self.row == 0, pltpu.roll(below, 1, 0), 0.0)

    def to_high(self, above):
        return jnp.where(self.row == 7, pltpu.roll(above, 7, 0), 0.0)

    def join_y(self, below, above):
        return below + self.to_high(above), above + self.to_low(below)

    def before_x(self, first, second):
        return jnp.where(self.even_x, second, first)

    def after_x(self, first, second):
        return jnp.where(self.even_x, first, second)

    def before_y(self, first, second):
        return jnp.where(self.even_y, second, first)

    def after_y(self, first, second):
        return jnp.where(self.even_y, first, second)


def along_x(matrix, tiles):
    out = []
    for i in range(8):
        acc = None
        for a in range(8):
            term = float(matrix[i, a]) * tiles[a]
            acc = term if acc is None else acc + term
        out.append(acc)
    return out


def along_y(ctab, base, tile):
    acc = ctab[base] * tile
    for s in range(1, 8):
        acc = acc + ctab[base + s] * pltpu.roll(tile, s, 0)
    return acc


def along_z(rows, matrix):
    return jnp.dot(
        rows, matrix, precision=lax.Precision.HIGHEST, preferred_element_type=jnp.float32
    )


def total(tile):
    return jnp.sum(jnp.sum(tile, axis=0, keepdims=True), axis=1, keepdims=True)


def store_y_faces(place, field, first_out, second_out, lead, at):
    for ex in range(2):
        for a in range(8):
            low = field[lead + (ex, a, 0, pl.ds(0, 1), slice(None))]
            high = field[lead + (ex, a, 1, pl.ds(7, 1), slice(None))]
            row = at + ex * 8 + a
            first_out[pl.ds(row, 1), :] = place.after_y(high, low)
            second_out[pl.ds(row, 1), :] = place.after_y(low, high)


def join_own(place, tiles):
    for ex in range(2):
        for a in range(8):
            tiles[ex][a] = list(place.join_y(*tiles[ex][a]))
    for ey in range(2):
        both = tiles[0][7][ey] + tiles[1][0][ey]
        tiles[0][7][ey] = both
        tiles[1][0][ey] = both


def weight_of(node):
    edge = jnp.minimum(node, 7 - node)
    value = jnp.where(edge == 2, float(WEIGHTS[2]), float(WEIGHTS[3]))
    return jnp.where(
        edge == 0, float(WEIGHTS[0]), jnp.where(edge == 1, float(WEIGHTS[1]), value)
    )


def mass_kernel(
    pack_rows,
    fields_in,
    kappa_in,
    group_in,
    coarse_in,
    out,
    xf,
    pack,
    first,
    second,
    fields,
    kappa,
    group,
    coarse,
    sems,
):
    copies = [pltpu.make_async_copy(fields_in.at[ch], fields.at[ch], sems.at[ch]) for ch in range(4)]
    copies += [
        pltpu.make_async_copy(kappa_in, kappa, sems.at[4]),
        pltpu.make_async_copy(group_in, group, sems.at[5]),
        pltpu.make_async_copy(coarse_in, coarse, sems.at[6]),
    ]
    for copy in copies:
        copy.start()
    place = Place()
    for copy in copies[4:]:
        copy.wait()
    pack[...] = jnp.zeros(pack.shape, jnp.float32)
    elems = kappa.shape[2]
    spread_to = lax.broadcasted_iota(jnp.int32, (elems, LANES), 1) // NODES
    spread = (spread_to == lax.broadcasted_iota(jnp.int32, (elems, LANES), 0)).astype(jnp.float32)
    blocks = coarse.shape[1] // LANES
    for ex in range(2):
        pack[pl.ds(2 * ex, 2), :] = along_z(kappa[ex], spread)
        pack[pl.ds(4 + 2 * ex, 2), :] = along_z(group[ex].astype(jnp.float32), spread)
    for c in range(NCD):
        for j in range(blocks):
            pack[pl.ds(8 + c * blocks + j, 1), :] = coarse[pl.ds(c, 1), pl.ds(j * LANES, LANES)]
    first[pl.ds(64, pack_rows), :] = pack[...]
    second[pl.ds(64, pack_rows), :] = pack[...]
    weight = weight_of(place.row) * weight_of(place.lane % NODES)
    for ch in range(4):
        copies[ch].wait()
        tiles = [
            [
                [
                    place.join_z(fields[ch, ex, a, ey] * (float(WEIGHTS[a]) * weight))
                    for ey in range(2)
                ]
                for a in range(8)
            ]
            for ex in range(2)
        ]
        join_own(place, tiles)
        for ex in range(2):
            for a in range(8):
                for ey in range(2):
                    out[ch, ex, a, ey] = tiles[ex][a][ey]
        for ey in range(2):
            xf[0, ch, ey] = tiles[0][0][ey]
            xf[1, ch, ey] = tiles[1][7][ey]
        store_y_faces(place, out, first, second, (ch,), ch * 16)


def turn_faces_kernel(pack_rows, xf, pack, y_first, y_second, first, second):
    place = Place()
    for ch in range(4):
        sides = []
        for side in range(2):
            row = pl.ds(ch * 16 + 15 * side, 1)
            got_a, got_b = y_first[row, :], y_second[row, :]
            low = xf[side, ch, 0] + jnp.where(place.row == 0, place.before_y(got_a, got_b), 0.0)
            high = xf[side, ch, 1] + jnp.where(place.row == 7, place.after_y(got_a, got_b), 0.0)
            sides.append((low, high))
        for ey in range(2):
            rows = pl.ds(ch * 16 + ey * 8, 8)
            first[rows, :] = place.after_x(sides[1][ey], sides[0][ey])
            second[rows, :] = place.after_x(sides[0][ey], sides[1][ey])
    came = pl.ds(64, pack_rows)
    parts = (
        place.before_y(y_first[came, :], y_second[came, :]),
        pack[...],
        place.after_y(y_first[came, :], y_second[came, :]),
    )
    for k in range(3):
        rows = pl.ds(64 + k * pack_rows, pack_rows)
        first[rows, :] = parts[k]
        second[rows, :] = parts[k]


def setup_kernel(
    pack_rows, blocks, pack, y_first, y_second, x_first, x_second, ctab, inv_diag, kap, grp, coarse
):
    place = Place()
    came = pl.ds(64, pack_rows)
    packs = [[None] * 3 for _ in range(3)]
    packs[1][0] = place.before_y(y_first[came, :], y_second[came, :])
    packs[1][1] = pack[...]
    packs[1][2] = place.after_y(y_first[came, :], y_second[came, :])
    for k in range(3):
        rows = pl.ds(64 + k * pack_rows, pack_rows)
        packs[0][k] = place.before_x(x_first[rows, :], x_second[rows, :])
        packs[2][k] = place.after_x(x_first[rows, :], x_second[rows, :])
    for dx in range(3):
        for dy in range(3):
            at = (dx * 3 + dy) * NCD * blocks
            coarse[pl.ds(at, NCD * blocks), :] = packs[dx][dy][8 : 8 + NCD * blocks]
    there_x = [jnp.where(place.prev_x, 1.0, 0.0), 1.0, jnp.where(place.next_x, 1.0, 0.0)]
    there_y = [jnp.where(place.prev_y, 1.0, 0.0), 1.0, jnp.where(place.next_y, 1.0, 0.0)]

    def element_row(base, u, v):
        row = base + (u % 2) * 2 + v % 2
        return packs[u // 2][v // 2][row : row + 1]

    for x in range(4):
        for y in range(4):
            kap[pl.ds(x * 4 + y, 1), :] = element_row(0, x + 1, y + 1)
            grp[pl.ds(x * 4 + y, 1), :] = element_row(4, x + 1, y + 1)
    kappa = [
        [
            place.join_z(jnp.broadcast_to(element_row(0, u, v), TILE))
            for v in range(6)
        ]
        for u in range(6)
    ]
    count_z = 1.0 + jnp.where(place.low_z | place.high_z, 1.0, 0.0)
    weight = ctab[T_W]
    line = ctab[T_LINE]

    def pick(values, y):
        low = values[y] + values[y + 1]
        high = values[y + 1] + values[y + 2]
        return jnp.where(place.row == 0, low, jnp.where(place.row == 7, high, values[y + 1]))

    for x in range(4):
        for kind in range(3):
            us = {0: (x, x + 1), 1: (x + 1,), 2: (x + 1, x + 2)}[kind]
            sums, counts = [], []
            for v in range(6):
                acc, num = None, 0.0
                for u in us:
                    acc = kappa[u][v] if acc is None else acc + kappa[u][v]
                    num = num + there_x[u // 2]
                sums.append(acc)
                counts.append(num * there_y[v // 2])
            for y in range(4):
                kappa_sum = pick(sums, y)
                mult = pick(counts, y) * count_z
                present = there_x[(x + 1) // 2] * there_y[(y + 1) // 2] > 0.5
                for a in {0: (0,), 1: range(1, 7), 2: (7,)}[kind]:
                    diag = (float(LINE[a]) + line) * kappa_sum + sigma_p * mult
                    diag = diag * (float(WEIGHTS[a]) * weight)
                    inv_diag[x, a, y] = jnp.where(present, 1.0 / diag, 0.0)


def got_face_sum(place, tile, ch, ex, a, ey, y_first, y_second, x_first, x_second):
    row = pl.ds(ch * 16 + ex * 8 + a, 1)
    got_a, got_b = y_first[row, :], y_second[row, :]
    if ey == 0:
        tile = tile + jnp.where(place.row == 0, place.before_y(got_a, got_b), 0.0)
    else:
        tile = tile + jnp.where(place.row == 7, place.after_y(got_a, got_b), 0.0)
    rows = pl.ds(pl.multiple_of(ch * 16 + ey * 8, 8), 8)
    if ex == 0 and a == 0:
        tile = tile + place.before_x(x_first[rows, :], x_second[rows, :])
    if ex == 1 and a == 7:
        tile = tile + place.after_x(x_first[rows, :], x_second[rows, :])
    return tile


def rhs_kernel(
    summed,
    visc,
    y_first,
    y_second,
    x_first,
    x_second,
    ctab,
    zmat,
    share,
    first,
    second,
    start,
    rhs,
    grad_z,
    flux_z,
):
    place = Place()
    weight = ctab[T_W]
    inv_mass = [1.0 / (weight * place.mult_tile(ey)) for ey in range(2)]

    def begin(ch, carry):
        for ex in range(2):
            for a in range(8):
                for ey in range(2):
                    tile = got_face_sum(
                        place, summed[ch, ex, a, ey], ch, ex, a, ey,
                        y_first, y_second, x_first, x_second,
                    )
                    scale = place.inv_x(ex, a) * float(1.0 / WEIGHTS[a])
                    start[ch, ex, a, ey] = tile * (inv_mass[ey] * scale)
        return carry

    lax.fori_loop(0, 4, begin, 0)
    grad_z[...] = along_z(start[...].reshape(1024, LANES), zmat[0]).reshape(grad_z.shape)

    def column(index, carry):
        ch, ex, ey = index // 4, index // 2 % 2, index % 2
        coef = jnp.where(ch == 3, 1.0 / prandtl, 1.0)
        field = [start[ch, ex, a, ey] for a in range(8)]
        grad_x = along_x(DERIV, field)
        flux_x, parts = [], []
        for a in range(8):
            grad_y = along_y(ctab, T_D, field[a])
            slope = grad_z[ch, ex, a, ey]
            node = float(WEIGHTS[a]) * weight
            advect = (
                start[0, ex, a, ey] * grad_x[a]
                + start[1, ex, a, ey] * grad_y
                + start[2, ex, a, ey] * slope
            )
            nu = visc[ex, a, ey] * node * coef
            flux_x.append(nu * grad_x[a])
            flux_z[ch, ex, a, ey] = nu * slope
            parts.append(node * advect + along_y(ctab, T_DT, nu * grad_y))
        back = along_x(DERIV.T, flux_x)
        for a in range(8):
            rhs[ch, ex, a, ey] = parts[a] + back[a]
        return carry

    lax.fori_loop(0, 16, column, 0)
    grad_z[...] = along_z(flux_z[...].reshape(1024, LANES), zmat[1]).reshape(grad_z.shape)

    def finish(ch, carry):
        tiles = [
            [
                [
                    place.join_z(-(rhs[ch, ex, a, ey] + grad_z[ch, ex, a, ey]))
                    for ey in range(2)
                ]
                for a in range(8)
            ]
            for ex in range(2)
        ]
        join_own(place, tiles)
        for ex in range(2):
            for a in range(8):
                scale = place.inv_x(ex, a) * float(dt_step / WEIGHTS[a])
                for ey in range(2):
                    part = start[ch, ex, a, ey] * (place.share_y(ey) * place.share_x(ex, a))
                    share[ch, ex, a, ey] = part + tiles[ex][a][ey] * (inv_mass[ey] * scale)
        return carry

    lax.fori_loop(0, 4, finish, 0)
    for ex in range(2):
        for a in range(8):
            low, high = share[1, ex, a, 0], share[1, ex, a, 1]
            rows = pl.ds((ex * 8 + a) * 8, 8)
            first[rows, :] = place.after_y(high, low)
            second[rows, :] = place.after_y(low, high)
    for k, ch in enumerate((0, 2, 3)):
        store_y_faces(place, share, first, second, (ch,), 128 + k * 16)


def store_own(place, tiles, out, first, second):
    join_own(place, tiles)
    for ex in range(2):
        for a in range(8):
            low, high = tiles[ex][a]
            out[ex, a, 0] = low
            out[ex, a, 1] = high
            first[ex, a] = place.after_y(high, low)
            second[ex, a] = place.after_y(low, high)


FACE_ROW = {0: 128, 2: 144, 3: 160}
SIDE_ROW = {1: 128, 2: 160, 3: 176}


def with_y(place, share, y_first, y_second, ch, ex, a):
    low, high = share[ch, ex, a, 0], share[ch, ex, a, 1]
    if ch == 1:
        rows = pl.ds((ex * 8 + a) * 8, 8)
        got_a, got_b = y_first[rows, :], y_second[rows, :]
        return (
            low + place.to_low(place.before_y(got_a, got_b)),
            high + place.to_high(place.after_y(got_a, got_b)),
        )
    row = pl.ds(FACE_ROW[ch] + ex * 8 + a, 1)
    got_a, got_b = y_first[row, :], y_second[row, :]
    return (
        low + jnp.where(place.row == 0, place.before_y(got_a, got_b), 0.0),
        high + jnp.where(place.row == 7, place.after_y(got_a, got_b), 0.0),
    )


def turn_step_kernel(share, y_first, y_second, first, second):
    place = Place()

    def put(row, next_side, prev_side):
        rows = pl.ds(row, 8)
        first[rows, :] = place.after_x(next_side, prev_side)
        second[rows, :] = place.after_x(prev_side, next_side)

    for a in range(8):
        prev_side = with_y(place, share, y_first, y_second, 0, 0, a)
        next_side = with_y(place, share, y_first, y_second, 0, 1, a)
        for ey in range(2):
            put(a * 16 + ey * 8, next_side[ey], prev_side[ey])
    for ch in (1, 2, 3):
        prev_side = with_y(place, share, y_first, y_second, ch, 0, 0)
        next_side = with_y(place, share, y_first, y_second, ch, 1, 7)
        if ch == 1:
            sides = []
            for (ex, a), own in (((0, 0), prev_side), ((1, 7), next_side)):
                rows = pl.ds((ex * 8 + a) * 8, 8)
                got_a, got_b = y_first[rows, :], y_second[rows, :]
                sides.append(
                    (place.before_y(got_a, got_b),) + own + (place.after_y(got_a, got_b),)
                )
            prev_side, next_side = sides
        for k, (after, before) in enumerate(zip(next_side, prev_side)):
            put(SIDE_ROW[ch] + k * 8, after, before)


def advance_kernel(
    share,
    y_first,
    y_second,
    x_first,
    x_second,
    inv_diag,
    kap,
    grp,
    ctab,
    zmat,
    fields_new,
    resid,
    own,
    msg,
    grad_z,
    scaled,
):
    place = Place()
    weight = ctab[T_W]

    def before(row):
        rows = pl.ds(row, 8)
        return place.before_x(x_first[rows, :], x_second[rows, :])

    def after(row):
        rows = pl.ds(row, 8)
        return place.after_x(x_first[rows, :], x_second[rows, :])

    for ch in range(4):
        for ex in range(2):
            for a in range(8):
                tiles = list(with_y(place, share, y_first, y_second, ch, ex, a))
                for ey in range(2):
                    at = {0: 0, 1: 136, 2: 160, 3: 176}[ch] + ey * 8
                    if (ex, a) == (0, 0):
                        tiles[ey] = tiles[ey] + before(at + (112 if ch == 0 else 0))
                    if (ex, a) == (1, 7):
                        tiles[ey] = tiles[ey] + after(at)
                    fields_new[ch, ex, a, ey] = tiles[ey]
    grad_z[...] = along_z(fields_new[2].reshape(256, LANES), zmat[0]).reshape(grad_z.shape)
    slope = [[None, None], [None, None]]
    for ey in range(2):
        for ex in range(2):
            slope[ex][ey] = along_x(DERIV, [fields_new[0, ex, a, ey] for a in range(8)])
        low = float(DERIV[7, 7]) * fields_new[0, 0, 0, ey]
        high = float(DERIV[0, 0]) * fields_new[0, 1, 7, ey]
        for k in range(7):
            low = low + float(DERIV[7, k]) * before(k * 16 + ey * 8)
            high = high + float(DERIV[0, k + 1]) * after((k + 1) * 16 + ey * 8)
        mid = 0.5 * (slope[0][ey][7] + slope[1][ey][0])
        slope[0][ey][7] = mid
        slope[1][ey][0] = mid
        own_low, own_high = slope[0][ey][0], slope[1][ey][7]
        slope[0][ey][0] = jnp.where(place.prev_x, 0.5 * (own_low + low), own_low)
        slope[1][ey][7] = jnp.where(place.next_x, 0.5 * (own_high + high), own_high)
    sums = [[jnp.zeros(TILE, jnp.float32) for _ in range(2)] for _ in range(2)]
    inv_mult = [1.0 / place.mult_tile(ey) for ey in range(2)]
    inv_y = [place.inv_y(ey) for ey in range(2)]
    inv_z = place.inv_z()
    mass = [weight * place.mult_tile(ey) for ey in range(2)]
    there_low = jnp.where(place.prev_y, 1.0, 0.0)
    there_high = jnp.where(place.next_y, 1.0, 0.0)
    for ex in range(2):
        for a in range(8):
            flow = [fields_new[1, ex, a, ey] for ey in range(2)]
            rows = pl.ds((ex * 8 + a) * 8, 8)
            got_a, got_b = y_first[rows, :], y_second[rows, :]
            below = place.before_y(got_a, got_b)
            above = place.after_y(got_a, got_b)
            if (ex, a) == (0, 0):
                below = below + before(128)
                above = above + before(152)
            if (ex, a) == (1, 7):
                below = below + after(128)
                above = above + after(152)
            below = jnp.where(place.row == 7, pltpu.roll(flow[0], 7, 0), below)
            above = jnp.where(place.row == 0, pltpu.roll(flow[1], 1, 0), above)
            below = jnp.sum(ctab[T_TOP] * below, axis=0, keepdims=True) * there_low
            above = jnp.sum(ctab[T_BOTTOM] * above, axis=0, keepdims=True) * there_high
            grad_y = list(place.join_y(*[along_y(ctab, T_D, tile) for tile in flow]))
            grad_y[0] = grad_y[0] + jnp.where(place.row == 0, below, 0.0)
            grad_y[1] = grad_y[1] + jnp.where(place.row == 7, above, 0.0)
            for ey in range(2):
                div = (
                    slope[ex][ey][a]
                    + grad_y[ey] * inv_y[ey]
                    + place.join_z(grad_z[ex, a, ey]) * inv_z
                )
                value = div * (mass[ey] * (place.mult_x(ex, a) * float(-WEIGHTS[a])))
                resid[ex, a, ey] = value
                scaled[ex, a, ey] = value * inv_diag[ex + 1, a, ey + 1] * float(1.0 / THETA)
                sums[ex][ey] = sums[ex][ey] + value * (inv_mult[ey] * place.inv_x(ex, a))
    grad_z[...] = along_z(scaled[...].reshape(256, LANES), zmat[2]).reshape(grad_z.shape)
    tiles = [[[None, None] for _ in range(8)] for _ in range(2)]
    for ex in range(2):
        for ey in range(2):
            images = own_operator(ctab, kap, scaled, grad_z, ex, ey)[1]
            for a in range(8):
                tiles[ex][a][ey] = place.join_z(images[a])
    join_own(place, tiles)
    for ex in range(2):
        for a in range(8):
            for ey in range(2):
                own[ex, a, ey] = tiles[ex][a][ey]
    row = message(place, restricted(place, sums, grp), [])
    blank = jnp.where(place.row == 0, jnp.broadcast_to(row, TILE), 0.0)
    zero = jnp.zeros(TILE, jnp.float32)

    def clear(i, carry):
        msg[i, pl.ds(0, 8), :] = zero
        msg[i, pl.ds(8, 8), :] = blank
        return carry

    lax.fori_loop(0, msg.shape[0], clear, 0)
    for dx, dy, there in neighbours(place):

        @pl.when(there)
        def _():
            to = (place.ix + dx) * place.ny + place.iy + dy
            ex, a = (0, 0) if dx < 0 else (1, 7)
            ey, b = (0, 0) if dy < 0 else (1, 7)
            if dy == 0:
                msg[to, pl.ds(0, 8), :] = own[ex, a, 0]
                msg[to, pl.ds(9, 7), :] = own[ex, a, 1, pl.ds(1, 7), :]
            elif dx == 0:
                for r in range(16):
                    if r != 8:
                        msg[to, pl.ds(r, 1), :] = own[r // 8, r % 8, ey, pl.ds(b, 1), :]
            else:
                msg[to, pl.ds(0, 1), :] = own[ex, a, ey, pl.ds(b, 1), :]


def neighbours(place):
    along = ((-1, place.prev_x), (0, None), (1, place.next_x))
    across = ((-1, place.prev_y), (0, None), (1, place.next_y))
    out = []
    for dx, has_x in along:
        for dy, has_y in across:
            if dx == 0 and dy == 0:
                continue
            there = has_y if has_x is None else (has_x if has_y is None else has_x & has_y)
            out.append((dx, dy, there))
    return out


def turn_columns_kernel(own, y_first, y_second, first, second):
    place = Place()

    def line(a, carry):
        for y in range(4):
            sides = []
            for ex in range(2):
                if y in (1, 2):
                    sides.append(own[ex, a, y - 1])
                elif y == 0:
                    sides.append(place.before_y(y_first[ex, a], y_second[ex, a]))
                else:
                    sides.append(place.after_y(y_first[ex, a], y_second[ex, a]))
            first[a, y] = place.after_x(sides[1], sides[0])
            second[a, y] = place.after_x(sides[0], sides[1])
        return carry

    lax.fori_loop(0, 8, line, 0)


def restricted(place, sums, grp):
    values = []
    for c in range(NCD):
        acc = jnp.zeros(TILE, jnp.float32)
        for ex in range(2):
            for ey in range(2):
                group = grp[pl.ds((ex + 1) * 4 + ey + 1, 1), :]
                acc = acc + jnp.where(group == float(c), sums[ex][ey], 0.0)
        values.append(total(acc))
    return values


def message(place, own_values, scalars):
    lane = lax.broadcasted_iota(jnp.int32, (1, LANES), 1)
    spot = (place.ix * place.ny + place.iy) % (LANES // NCD)
    after = (spot + 1) % (LANES // NCD)
    row = jnp.zeros((1, LANES), jnp.float32)
    for c, value in enumerate(own_values):
        row = row + jnp.where(lane == spot * NCD + c, value, 0.0)
    for c, value in enumerate(scalars):
        row = row + jnp.where(lane == after * NCD + c, value, 0.0)
    return row


def send_to_all(msg, row):
    def send(i, carry):
        msg[i] = row
        return carry

    lax.fori_loop(0, msg.shape[0], send, 0, unroll=msg.shape[0] <= 64)


def smooth_kernel(
    own,
    y_first,
    y_second,
    x_first,
    x_second,
    inv_diag,
    kap,
    grp,
    extra,
    ctab,
    zmat,
    resid,
    smoothed,
    msg,
    ext,
    scaled,
    local,
    edge,
):
    place = Place()
    weight = ctab[T_W]

    def raw(x, a, y):
        if x in (1, 2):
            if y in (1, 2):
                return own[x - 1, a, y - 1]
            if y == 0:
                return place.before_y(y_first[x - 1, a], y_second[x - 1, a])
            return place.after_y(y_first[x - 1, a], y_second[x - 1, a])
        if x == 0:
            return place.before_x(x_first[a, y], x_second[a, y])
        return place.after_x(x_first[a, y], x_second[a, y])

    def put(x, a, tiles):
        low = place.join_y(tiles[0], tiles[1])
        high = place.join_y(tiles[2], tiles[3])
        for y, tile in enumerate(low + high):
            ext[x, a, y] = tile
            scaled[x, a, y] = tile * inv_diag[x, a, y] * float(1.0 / THETA)

    joined = {}
    for x, a, x2, a2 in ((0, 7, 1, 0), (2, 7, 3, 0)):
        both = [raw(x, a, y) + raw(x2, a2, y) for y in range(4)]
        put(x, a, both)
        put(x2, a2, both)
        joined[(x, a)] = joined[(x2, a2)] = True

    for x in range(4):
        first = 1 if (x, 0) in joined else 0
        last = 7 if (x, 7) in joined else 8

        def fill(a, carry, x=x):
            put(x, a, [raw(x, a, y) for y in range(4)])
            return carry

        lax.fori_loop(first, last, fill, 0)

    local[...] = along_z(scaled[pl.ds(1, 2)].reshape(512, LANES), zmat[2]).reshape(local.shape)
    edge[pl.ds(0, 4)] = along_z(scaled[0, 7].reshape(32, LANES), zmat[2]).reshape(4, 8, LANES)
    edge[pl.ds(4, 4)] = along_z(scaled[3, 0].reshape(32, LANES), zmat[2]).reshape(4, 8, LANES)

    def finish_tile(tile, a, slope, x, y):
        kappa = kap[pl.ds(x * 4 + y, 1), :]
        stiff = slope + along_y(ctab, T_K, tile)
        return (kappa * stiff + sigma_p * tile) * (float(WEIGHTS[a]) * weight)

    def column(y, carry):
        for x in (1, 2):
            tiles = [scaled[x, a, y] for a in range(8)]
            slopes = along_x(SCALED, tiles)
            for a in range(8):
                local[x - 1, a, y] = finish_tile(tiles[a], a, slopes[a] + local[x - 1, a, y], x, y)
        for x, a, at in ((0, 7, 0), (3, 0, 4)):
            slope = edge[at + y]
            for k in range(8):
                slope = slope + float(SCALED[a, k]) * scaled[x, k, y]
            edge[at + y] = finish_tile(scaled[x, a, y], a, slope, x, y)
        return carry

    lax.fori_loop(0, 4, column, 0)
    inv_mult = [1.0 / place.mult_tile(ey) for ey in range(2)]
    sums = [[jnp.zeros(TILE, jnp.float32) for _ in range(2)] for _ in range(2)]
    for x in (1, 2):
        for a in range(8):
            if (x, a) == (1, 0):
                tiles = [local[0, 0, y] + edge[y] for y in range(4)]
            elif (x, a) == (2, 7):
                tiles = [local[1, 7, y] + edge[4 + y] for y in range(4)]
            elif (x, a) in ((1, 7), (2, 0)):
                tiles = [local[0, 7, y] + local[1, 0, y] for y in range(4)]
            else:
                tiles = [local[x - 1, a, y] for y in range(4)]
            low = tiles[1] + place.to_low(tiles[0]) + place.to_high(tiles[2])
            high = tiles[2] + place.to_low(tiles[1]) + place.to_high(tiles[3])
            for ey, image in enumerate((low, high)):
                image = place.join_z(image)
                value = ext[x, a, ey + 1]
                update = scaled[x, a, ey + 1]
                defect = (value - image) * inv_diag[x, a, ey + 1]
                resid[x - 1, a, ey] = value
                smoothed[x - 1, a, ey] = (
                    float(1.0 + RHO_NEXT * RHO) * update + float(2.0 * RHO_NEXT / DELTA) * defect
                )
                scale = place.inv_x(x - 1, a)
                sums[x - 1][ey] = sums[x - 1][ey] + value * (inv_mult[ey] * scale)
    send_to_all(msg, message(place, restricted(place, sums, grp), []) + extra[...])


def coarse_part(place, blocks, got, coarse, grp, at=0):
    lane = lax.broadcasted_iota(jnp.int32, (1, LANES), 1)
    values = [jnp.zeros((1, LANES), jnp.float32) for _ in range(blocks)]
    per = LANES // NCD
    for j in range(blocks):

        def gather(i, acc, j=j):
            return jnp.where(lane // NCD == i, got[j * per + i, pl.ds(at, 1), :], acc)

        values[j] = lax.fori_loop(0, per, gather, values[j], unroll=blocks == 1)

    def solved(dx, dy, c):
        acc = None
        for j in range(blocks):
            term = coarse[pl.ds(((dx * 3 + dy) * NCD + c) * blocks + j, 1), :] * values[j]
            acc = term if acc is None else acc + term
        return jnp.sum(acc, axis=1, keepdims=True)

    device = [[[solved(dx, dy, c) for c in range(NCD)] for dy in range(3)] for dx in range(3)]
    inv_z = jnp.where(place.low_z | place.high_z, 0.5, 1.0)
    rows = []
    for x in range(4):
        line = []
        for y in range(4):
            group = grp[pl.ds(x * 4 + y, 1), :]
            acc = jnp.zeros((1, LANES), jnp.float32)
            for c in range(NCD):
                acc = acc + jnp.where(
                    group == float(c), device[(x + 1) // 2][(y + 1) // 2][c], 0.0
                )
            line.append(place.join_z(jnp.broadcast_to(acc, TILE)) * inv_z)
        rows.append(line)
    low_y = jnp.where(place.prev_y, 0.5, 1.0)
    high_y = jnp.where(place.next_y, 0.5, 1.0)

    def tile(ex, kind, ey):
        if kind == 1:
            vals = [rows[ex + 1][y] for y in range(4)]
        elif kind == 0:
            scale = place.inv_x(ex, 0)
            vals = [(rows[ex][y] + rows[ex + 1][y]) * scale for y in range(4)]
        else:
            scale = place.inv_x(ex, 7)
            vals = [(rows[ex + 1][y] + rows[ex + 2][y]) * scale for y in range(4)]
        mid = vals[ey + 1]
        low = (vals[ey] + mid) * (low_y if ey == 0 else 0.5)
        high = (mid + vals[ey + 2]) * (high_y if ey == 1 else 0.5)
        return jnp.where(place.row == 0, low, jnp.where(place.row == 7, high, mid))

    return tile


def kind_of(a):
    return 0 if a == 0 else (2 if a == 7 else 1)


def own_operator(ctab, kap, field, slope_z, ex, ey):
    weight = ctab[T_W]
    tiles = [field[ex, a, ey] for a in range(8)]
    slopes = along_x(SCALED, tiles)
    kappa = kap[pl.ds((ex + 1) * 4 + ey + 1, 1), :]
    out = []
    for a in range(8):
        stiff = slopes[a] + along_y(ctab, T_K, tiles[a]) + slope_z[ex, a, ey]
        out.append((kappa * stiff + sigma_p * tiles[a]) * (float(WEIGHTS[a]) * weight))
    return tiles, out


def first_direction_kernel(
    blocks,
    got,
    coarse,
    grp,
    kap,
    inv_diag,
    resid,
    own,
    ctab,
    zmat,
    direction,
    out,
    first,
    second,
    extra,
    slope_z,
    image,
):
    place = Place()
    inv_mult = [1.0 / place.mult_tile(ey) for ey in range(2)]
    part = coarse_part(place, blocks, got, coarse, grp, 8)
    image[...] = own[...]
    for dx, dy, there in neighbours(place):

        @pl.when(there)
        def _():
            frm = (place.ix + dx) * place.ny + place.iy + dy
            ex, a = (0, 0) if dx < 0 else (1, 7)
            ey, b = (0, 0) if dy < 0 else (1, 7)
            edge = place.row == b
            if dy == 0:
                low = got[frm, pl.ds(0, 8), :]
                high = jnp.where(
                    place.row == 0, pltpu.roll(low, 1, 0), got[frm, pl.ds(8, 8), :]
                )
                image[ex, a, 0] = image[ex, a, 0] + low
                image[ex, a, 1] = image[ex, a, 1] + high
            elif dx == 0:
                for r in range(16):
                    line = got[frm, pl.ds(7 if r == 8 else r, 1), :]
                    tile = image[r // 8, r % 8, ey]
                    image[r // 8, r % 8, ey] = tile + jnp.where(edge, line, 0.0)
            else:
                line = got[frm, pl.ds(0, 1), :]
                image[ex, a, ey] = image[ex, a, ey] + jnp.where(edge, line, 0.0)

    energy = jnp.zeros(TILE, jnp.float32)
    for ex in range(2):
        for ey in range(2):
            kinds = [part(ex, kind, ey) for kind in range(3)]
            for a in range(8):
                known = resid[ex, a, ey]
                inverse = inv_diag[ex + 1, a, ey + 1]
                defect = (known - image[ex, a, ey]) * inverse
                value = (
                    float((1.0 + RHO_NEXT * RHO) / THETA) * (known * inverse)
                    + float(2.0 * RHO_NEXT / DELTA) * defect
                    + kinds[kind_of(a)]
                )
                direction[ex, a, ey] = value
                scale = place.inv_x(ex, a)
                energy = energy + value * known * (inv_mult[ey] * scale)
    slope_z[...] = along_z(direction[...].reshape(256, LANES), zmat[2]).reshape(slope_z.shape)
    curvature = jnp.zeros(TILE, jnp.float32)
    tiles = [[[None, None] for _ in range(8)] for _ in range(2)]
    for ex in range(2):
        for ey in range(2):
            values, images = own_operator(ctab, kap, direction, slope_z, ex, ey)
            for a in range(8):
                curvature = curvature + values[a] * images[a]
                tiles[ex][a][ey] = place.join_z(images[a])
    store_own(place, tiles, out, first, second)
    extra[...] = message(place, [], [total(energy), total(curvature)])


def gathered_scalars(got, count):
    lane = lax.broadcasted_iota(jnp.int32, (1, LANES), 1)
    per = LANES // NCD
    sums = []
    for c in range(count):
        acc = jnp.zeros((1, LANES), jnp.float32)

        def gather(i, acc, c=c):
            return acc + jnp.where(lane == ((i + 1) % per) * NCD + c, got[i], 0.0)

        acc = lax.fori_loop(0, got.shape[0], gather, acc, unroll=got.shape[0] <= per)
        sums.append(jnp.sum(acc, axis=1, keepdims=True))
    return sums


def second_direction_kernel(
    blocks,
    got,
    coarse,
    grp,
    kap,
    resid,
    direction,
    image,
    smoothed,
    ctab,
    zmat,
    following,
    known,
    msg,
    slope_z,
):
    place = Place()
    inv_mult = [1.0 / place.mult_tile(ey) for ey in range(2)]
    part = coarse_part(place, blocks, got, coarse, grp)
    energy, curvature = gathered_scalars(got, 2)
    step = energy / curvature
    lane = lax.broadcasted_iota(jnp.int32, (1, LANES), 1)
    known[...] = jnp.where(lane == 0, energy, jnp.where(lane == 1, curvature, 0.0))
    energy_next = jnp.zeros(TILE, jnp.float32)
    cross = jnp.zeros(TILE, jnp.float32)
    for ex in range(2):
        for ey in range(2):
            kinds = [part(ex, kind, ey) for kind in range(3)]
            for a in range(8):
                value = direction[ex, a, ey] - step * (smoothed[ex, a, ey] + kinds[kind_of(a)])
                following[ex, a, ey] = value
                weighed = value * (inv_mult[ey] * place.inv_x(ex, a))
                was = image[ex, a, ey]
                energy_next = energy_next + weighed * (resid[ex, a, ey] - step * was)
                cross = cross + weighed * was
    slope_z[...] = along_z(following[...].reshape(256, LANES), zmat[2]).reshape(slope_z.shape)
    square = jnp.zeros(TILE, jnp.float32)
    for ex in range(2):
        for ey in range(2):
            values, images = own_operator(ctab, kap, following, slope_z, ex, ey)
            for a in range(8):
                square = square + values[a] * images[a]
    send_to_all(msg, message(place, [], [total(energy_next), total(square), total(cross)]))


def pressure_kernel(got, known, direction, following, pressure):
    energy = known[:, pl.ds(0, 1)]
    curvature = known[:, pl.ds(1, 1)]
    energy_next, square, cross = gathered_scalars(got, 3)
    ratio = energy_next / energy
    step = energy / curvature
    step_next = energy_next / (square + 2.0 * ratio * cross + ratio * ratio * curvature)
    weight_old = step + step_next * ratio
    for ex in range(2):
        for a in range(8):
            for ey in range(2):
                pressure[ex, a, ey] = (
                    weight_old * direction[ex, a, ey] + step_next * following[ex, a, ey]
                )


def call(body, outs, scratch=(), **more):
    return pl.pallas_call(
        body,
        out_shape=[jax.ShapeDtypeStruct(shape, jnp.float32) for shape in outs],
        scratch_shapes=[
            pltpu.VMEM(shape, jnp.float32) if isinstance(shape, tuple) else shape
            for shape in scratch
        ],
        **more,
        compiler_params=pltpu.CompilerParams(vmem_limit_bytes=24 * 1024 * 1024),
    )


def swap(first, second, axis):
    count = lax.axis_size(axis)
    first_pairs = [(i, i ^ 1) for i in range(count) if i ^ 1 < count]
    second_pairs = [(i, ((i + 1) ^ 1) - 1) for i in range(1, count) if ((i + 1) ^ 1) - 1 < count]
    second_got = lax.ppermute(second, axis, second_pairs)
    return lax.ppermute(first, axis, first_pairs), second_got


def per_device(fields, viscosity, inv_density, elem_group, coarse_inverse):
    length = fields.shape[5]
    elems_z = length // NODES
    devices = lax.axis_size("gx") * lax.axis_size("gy")
    blocks = coarse_inverse.shape[1] // LANES
    pack_rows = -(-(8 + NCD * blocks) // 8) * 8
    tiles_np, mats_np = constant_tables(elems_z)
    ctab, zmat = jnp.asarray(tiles_np), jnp.asarray(mats_np)
    one = fields.shape[1:]
    four = fields.shape
    ext = (4, 8, 4, 8, LANES)
    column = (2, 8, 8, LANES)
    wide = (8, 4, 8, LANES)
    rows = (devices, 1, LANES)
    y_shape, x_shape = (64 + pack_rows, LANES), (64 + 3 * pack_rows, LANES)

    def exchange_all(msg):
        return lax.all_to_all(msg, BOTH, 0, 0, tiled=True)

    summed, xf, pack, first, second = call(
        functools.partial(mass_kernel, pack_rows),
        [four, (2, 4, 2, 8, LANES), (pack_rows, LANES), y_shape, y_shape],
        [
            four,
            inv_density.shape,
            pltpu.VMEM(elem_group.shape, jnp.int32),
            coarse_inverse.shape,
            pltpu.SemaphoreType.DMA((7,)),
        ],
        in_specs=[pl.BlockSpec(memory_space=pltpu.HBM)] * 4,
    )(fields, inv_density, elem_group, coarse_inverse)
    y_got = swap(first, second, "gy")
    first, second = call(functools.partial(turn_faces_kernel, pack_rows), [x_shape, x_shape])(
        xf, pack, *y_got
    )
    x_got = swap(first, second, "gx")
    inv_diag, kap, grp, coarse = call(
        functools.partial(setup_kernel, pack_rows, blocks),
        [ext, (16, LANES), (16, LANES), (9 * NCD * blocks, LANES)],
    )(pack, *y_got, *x_got, ctab)
    share, first, second = call(
        rhs_kernel, [four, (176, LANES), (176, LANES)], [four, four, four, four]
    )(summed, viscosity, *y_got, *x_got, ctab, zmat)
    y_got = swap(first, second, "gy")
    first, second = call(turn_step_kernel, [(192, LANES), (192, LANES)])(share, *y_got)
    x_got = swap(first, second, "gx")
    fields_new, resid, own, msg = call(
        advance_kernel, [four, one, one, (devices, 16, LANES)], [one, one]
    )(share, *y_got, *x_got, inv_diag, kap, grp, ctab, zmat)
    got = exchange_all(msg)
    direction, own, first, second, extra = call(
        functools.partial(first_direction_kernel, blocks),
        [one, one, column, column, (1, LANES)],
        [one, one],
    )(got, coarse, grp, kap, inv_diag, resid, own, ctab, zmat)
    y_got = swap(first, second, "gy")
    first, second = call(turn_columns_kernel, [wide, wide])(own, *y_got)
    x_got = swap(first, second, "gx")
    image, image_smoothed, msg = call(
        smooth_kernel, [one, one, rows], [ext, ext, (2,) + ext[1:], (8, 8, LANES)]
    )(own, *y_got, *x_got, inv_diag, kap, grp, extra, ctab, zmat)
    got = exchange_all(msg)
    following, known, msg = call(
        functools.partial(second_direction_kernel, blocks), [one, (1, LANES), rows], [one]
    )(got, coarse, grp, kap, resid, direction, image, image_smoothed, ctab, zmat)
    got = exchange_all(msg)
    (pressure,) = call(pressure_kernel, [one])(got, known, direction, following)
    return (fields_new, pressure)


def solution(mesh):
    placed = (
        P(None, "gx", None, "gy", None, None),
        P("gx", None, "gy", None, None),
        P("gx", "gy", None),
        P("gx", "gy", None),
        P(("gx", "gy"), None),
    )
    return jax.shard_map(
        per_device,
        mesh=mesh,
        in_specs=placed,
        out_specs=(P(None, "gx", None, "gy", None, None), P("gx", None, "gy", None, None)),
        check_vma=False,
    )
```

```python
import functools

import jax
import jax.numpy as jnp
import numpy as np
from jax import lax
from jax.experimental import pallas as pl
from jax.experimental.pallas import tpu as pltpu
from jax.sharding import PartitionSpec as P

NCD = 4
NODES = 8
LANES = 128
TILE = (8, 128)
BOTH = ("gx", "gy")

dt_step = 0.01
sigma_p = 4.0
prandtl = 0.7
cheb_ratio = 0.1


def tables():
    points = np.array(
        [
            -1.0,
            -0.8717401485096066,
            -0.5917001814331423,
            -0.2092992179024789,
            0.2092992179024789,
            0.5917001814331423,
            0.8717401485096066,
            1.0,
        ]
    )
    weights = np.array(
        [
            1.0 / 28.0,
            0.2107042271435061,
            0.3411226924835044,
            0.4124587946587038,
            0.4124587946587038,
            0.3411226924835044,
            0.2107042271435061,
            1.0 / 28.0,
        ]
    )
    identity = np.eye(8)
    differ = points[:, None] - points[None, :] + identity
    barycentric = 1.0 / np.prod(differ, axis=1)
    offdiag = barycentric[None, :] / barycentric[:, None] / differ * (1.0 - identity)
    derivative = offdiag - identity * np.sum(offdiag, axis=1)[:, None]
    mass_one = identity * weights[None, :]
    stiff_one = derivative.T @ mass_one @ derivative
    stiff_three = (
        np.kron(np.kron(stiff_one, mass_one), mass_one)
        + np.kron(np.kron(mass_one, stiff_one), mass_one)
        + np.kron(np.kron(mass_one, mass_one), stiff_one)
    )
    three_diag = np.sum(stiff_three * np.eye(512), axis=1)
    spectral_bound = float(np.max(np.sum(np.abs(stiff_three), axis=1) / three_diag))
    return (derivative, weights, stiff_one, spectral_bound)


DERIV, WEIGHTS, STIFF, BOUND = tables()
SCALED = STIFF / WEIGHTS[:, None]
LINE = np.diag(STIFF) / WEIGHTS
THETA = 0.5 * (BOUND + cheb_ratio * BOUND)
DELTA = 0.5 * (BOUND - cheb_ratio * BOUND)
RHO = DELTA / THETA
RHO_NEXT = 1.0 / (2.0 * THETA / DELTA - RHO)


def constant_tables(elems_z):
    def turned(matrix):
        rows = np.arange(8)
        return [np.repeat(matrix[rows, (rows - s) % 8][:, None], LANES, 1) for s in range(8)]

    wz = np.tile(WEIGHTS, elems_z)
    kz = np.tile(LINE, elems_z)
    tiles = turned(DERIV) + turned(DERIV.T) + turned(SCALED)
    tiles += [WEIGHTS[:, None] * wz[None, :], LINE[:, None] + kz[None, :]]
    for matrix in (DERIV, SCALED):
        for node in (7, 0):
            inner = matrix[node] * (np.arange(8) != node)
            tiles.append(np.repeat(inner[:, None], LANES, 1))
    eye = np.eye(elems_z)
    mats = [np.kron(eye, DERIV.T), np.kron(eye, DERIV), np.kron(eye, SCALED.T)]
    return np.stack(tiles).astype(np.float32), np.stack(mats).astype(np.float32)


T_D, T_DT, T_K, T_W, T_LINE = 0, 8, 16, 24, 25
T_TOP, T_BOTTOM, T_KTOP, T_KBOTTOM = 26, 27, 28, 29


class Place:
    def __init__(self):
        self.ix = lax.axis_index("gx")
        self.iy = lax.axis_index("gy")
        self.nx = lax.axis_size("gx")
        self.ny = lax.axis_size("gy")
        self.even_x = self.ix % 2 == 0
        self.even_y = self.iy % 2 == 0
        self.row = lax.broadcasted_iota(jnp.int32, TILE, 0)
        self.lane = lax.broadcasted_iota(jnp.int32, TILE, 1)
        self.low_z = (self.lane % 8 == 0) & (self.lane > 0)
        self.high_z = (self.lane % 8 == 7) & (self.lane < LANES - 1)
        self.prev_x = self.ix > 0
        self.next_x = self.ix < self.nx - 1
        self.prev_y = self.iy > 0
        self.next_y = self.iy < self.ny - 1

    def mult_tile(self, ey):
        along_z = 1.0 + jnp.where(self.low_z | self.high_z, 1.0, 0.0)
        low = 1.0 if ey == 1 else jnp.where(self.prev_y, 1.0, 0.0)
        high = 1.0 if ey == 0 else jnp.where(self.next_y, 1.0, 0.0)
        along_y = 1.0 + jnp.where(self.row == 0, low, jnp.where(self.row == 7, high, 0.0))
        return along_y * along_z

    def inv_x(self, ex, a):
        if a == 0:
            return 0.5 if ex == 1 else jnp.where(self.prev_x, 0.5, 1.0)
        if a == 7:
            return 0.5 if ex == 0 else jnp.where(self.next_x, 0.5, 1.0)
        return 1.0

    def mult_x(self, ex, a):
        if a == 0:
            return 2.0 if ex == 1 else jnp.where(self.prev_x, 2.0, 1.0)
        if a == 7:
            return 2.0 if ex == 0 else jnp.where(self.next_x, 2.0, 1.0)
        return 1.0

    def share_x(self, ex, a):
        if (ex, a) == (0, 0):
            return jnp.where(self.prev_x, 0.5, 1.0)
        if (ex, a) == (1, 7):
            return jnp.where(self.next_x, 0.5, 1.0)
        return 1.0

    def share_y(self, ey):
        if ey == 0:
            return jnp.where((self.row == 0) & self.prev_y, 0.5, 1.0)
        return jnp.where((self.row == 7) & self.next_y, 0.5, 1.0)

    def inv_y(self, ey):
        low = 0.5 if ey == 1 else jnp.where(self.prev_y, 0.5, 1.0)
        high = 0.5 if ey == 0 else jnp.where(self.next_y, 0.5, 1.0)
        return jnp.where(self.row == 0, low, jnp.where(self.row == 7, high, 1.0))

    def inv_z(self):
        return jnp.where(self.low_z | self.high_z, 0.5, 1.0)

    def join_z(self, t):
        up = pltpu.roll(t, LANES - 1, 1)
        down = pltpu.roll(t, 1, 1)
        return t + jnp.where(self.high_z, up, jnp.where(self.low_z, down, 0.0))

    def to_low(self, below):
        return jnp.where(self.row == 0, pltpu.roll(below, 1, 0), 0.0)

    def to_high(self, above):
        return jnp.where(self.row == 7, pltpu.roll(above, 7, 0), 0.0)

    def join_y(self, below, above):
        return below + self.to_high(above), above + self.to_low(below)

    def before_x(self, first, second):
        return jnp.where(self.even_x, second, first)

    def after_x(self, first, second):
        return jnp.where(self.even_x, first, second)

    def before_y(self, first, second):
        return jnp.where(self.even_y, second, first)

    def after_y(self, first, second):
        return jnp.where(self.even_y, first, second)


def along_x(matrix, tiles):
    out = []
    for i in range(8):
        acc = None
        for a in range(8):
            term = float(matrix[i, a]) * tiles[a]
            acc = term if acc is None else acc + term
        out.append(acc)
    return out


def along_y(ctab, base, tile):
    acc = ctab[base] * tile
    for s in range(1, 8):
        acc = acc + ctab[base + s] * pltpu.roll(tile, s, 0)
    return acc


def along_z(rows, matrix):
    return jnp.dot(
        rows, matrix, precision=lax.Precision.HIGHEST, preferred_element_type=jnp.float32
    )


def total(tile):
    return jnp.sum(jnp.sum(tile, axis=0, keepdims=True), axis=1, keepdims=True)


def store_y_faces(place, field, first_out, second_out, lead, at):
    for ex in range(2):
        for a in range(8):
            low = field[lead + (ex, a, 0, pl.ds(0, 1), slice(None))]
            high = field[lead + (ex, a, 1, pl.ds(7, 1), slice(None))]
            row = at + ex * 8 + a
            first_out[pl.ds(row, 1), :] = place.after_y(high, low)
            second_out[pl.ds(row, 1), :] = place.after_y(low, high)


def join_own(place, tiles):
    for ex in range(2):
        for a in range(8):
            tiles[ex][a] = list(place.join_y(*tiles[ex][a]))
    for ey in range(2):
        both = tiles[0][7][ey] + tiles[1][0][ey]
        tiles[0][7][ey] = both
        tiles[1][0][ey] = both


def weight_of(node):
    edge = jnp.minimum(node, 7 - node)
    value = jnp.where(edge == 2, float(WEIGHTS[2]), float(WEIGHTS[3]))
    return jnp.where(
        edge == 0, float(WEIGHTS[0]), jnp.where(edge == 1, float(WEIGHTS[1]), value)
    )


def mass_kernel(fields_in, out, xf, first, second, fields, sems):
    copies = [pltpu.make_async_copy(fields_in.at[ch], fields.at[ch], sems.at[ch]) for ch in range(4)]
    for copy in copies:
        copy.start()
    place = Place()
    weight = weight_of(place.row) * weight_of(place.lane % NODES)
    for ch in range(4):
        copies[ch].wait()
        tiles = [
            [
                [
                    place.join_z(fields[ch, ex, a, ey] * (float(WEIGHTS[a]) * weight))
                    for ey in range(2)
                ]
                for a in range(8)
            ]
            for ex in range(2)
        ]
        join_own(place, tiles)
        for ex in range(2):
            for a in range(8):
                for ey in range(2):
                    out[ch, ex, a, ey] = tiles[ex][a][ey]
        for ey in range(2):
            xf[0, ch, ey] = tiles[0][0][ey]
            xf[1, ch, ey] = tiles[1][7][ey]
        store_y_faces(place, out, first, second, (ch,), ch * 16)


def turn_faces(place, xf, y_first, y_second, first, second):
    for ch in range(4):
        sides = []
        for side in range(2):
            row = pl.ds(ch * 16 + 15 * side, 1)
            got_a, got_b = y_first[row, :], y_second[row, :]
            low = xf[side, ch, 0] + jnp.where(place.row == 0, place.before_y(got_a, got_b), 0.0)
            high = xf[side, ch, 1] + jnp.where(place.row == 7, place.after_y(got_a, got_b), 0.0)
            sides.append((low, high))
        for ey in range(2):
            rows = pl.ds(ch * 16 + ey * 8, 8)
            first[rows, :] = place.after_x(sides[1][ey], sides[0][ey])
            second[rows, :] = place.after_x(sides[0][ey], sides[1][ey])


def turn_faces_kernel(xf, y_first, y_second, first, second):
    turn_faces(Place(), xf, y_first, y_second, first, second)


def turn_edges(place, inner_x, y_first, y_second, first, second, at, edge, inner_y):
    sides = []
    for side in range(2):
        row = pl.ds(edge + side, 1)
        got_a, got_b = y_first[row, :], y_second[row, :]
        low = inner_x[side, 0] + jnp.where(place.row == 0, place.before_y(got_a, got_b), 0.0)
        high = inner_x[side, 1] + jnp.where(place.row == 7, place.after_y(got_a, got_b), 0.0)
        sides.append((low, high))
    for ey in range(2):
        rows = pl.ds(at + ey * 8, 8)
        first[rows, :] = place.after_x(sides[1][ey], sides[0][ey])
        second[rows, :] = place.after_x(sides[0][ey], sides[1][ey])
    for k, pick in enumerate((place.before_y, place.after_y)):
        sides = []
        for side in range(2):
            row = pl.ds(inner_y + 15 * side, 1)
            sides.append(pick(y_first[row, :], y_second[row, :]))
        row = pl.ds(edge + k, 1)
        first[row, :] = place.after_x(sides[1], sides[0])
        second[row, :] = place.after_x(sides[0], sides[1])


STEP_U, STEP_V, STEP_EDGE, STEP_PACK = 64, 64, 80, 88


def turn_step_kernel(pack_rows, xf, inner_x, pack, y_first, y_second, first, second):
    place = Place()
    turn_faces(place, xf, y_first, y_second, first, second)
    first[pl.ds(STEP_EDGE, 8), :] = jnp.zeros(TILE, jnp.float32)
    second[pl.ds(STEP_EDGE, 8), :] = jnp.zeros(TILE, jnp.float32)
    turn_edges(place, inner_x, y_first, y_second, first, second, STEP_U, STEP_EDGE, STEP_V)
    came = pl.ds(STEP_PACK, pack_rows)
    parts = (
        place.before_y(y_first[came, :], y_second[came, :]),
        pack[...],
        place.after_y(y_first[came, :], y_second[came, :]),
    )
    for k in range(3):
        rows = pl.ds(STEP_PACK + k * pack_rows, pack_rows)
        first[rows, :] = parts[k]
        second[rows, :] = parts[k]


def setup_kernel(
    pack_rows, blocks, pack, y_first, y_second, x_first, x_second, ctab, inv_diag, kap, grp, coarse
):
    place = Place()
    came = pl.ds(STEP_PACK, pack_rows)
    packs = [[None] * 3 for _ in range(3)]
    packs[1][0] = place.before_y(y_first[came, :], y_second[came, :])
    packs[1][1] = pack[...]
    packs[1][2] = place.after_y(y_first[came, :], y_second[came, :])
    for k in range(3):
        rows = pl.ds(STEP_PACK + k * pack_rows, pack_rows)
        packs[0][k] = place.before_x(x_first[rows, :], x_second[rows, :])
        packs[2][k] = place.after_x(x_first[rows, :], x_second[rows, :])
    for dx in range(3):
        for dy in range(3):
            at = (dx * 3 + dy) * NCD * blocks
            coarse[pl.ds(at, NCD * blocks), :] = packs[dx][dy][8 : 8 + NCD * blocks]
    there_x = [jnp.where(place.prev_x, 1.0, 0.0), 1.0, jnp.where(place.next_x, 1.0, 0.0)]
    there_y = [jnp.where(place.prev_y, 1.0, 0.0), 1.0, jnp.where(place.next_y, 1.0, 0.0)]

    def element_row(base, u, v):
        row = base + (u % 2) * 2 + v % 2
        return packs[u // 2][v // 2][row : row + 1]

    for x in range(4):
        for y in range(4):
            kap[pl.ds(x * 4 + y, 1), :] = element_row(0, x + 1, y + 1)
            grp[pl.ds(x * 4 + y, 1), :] = element_row(4, x + 1, y + 1)
    kappa = [
        [
            place.join_z(jnp.broadcast_to(element_row(0, u + 1, v + 1), TILE))
            for v in range(4)
        ]
        for u in range(4)
    ]
    count_z = 1.0 + jnp.where(place.low_z | place.high_z, 1.0, 0.0)
    weight = ctab[T_W]
    line = ctab[T_LINE]

    def pick(values, ey):
        low = values[ey] + values[ey + 1]
        high = values[ey + 1] + values[ey + 2]
        return jnp.where(place.row == 0, low, jnp.where(place.row == 7, high, values[ey + 1]))

    for ex in range(2):
        for kind in range(3):
            us = {0: (ex, ex + 1), 1: (ex + 1,), 2: (ex + 1, ex + 2)}[kind]
            sums, counts = [], []
            for v in range(4):
                acc, num = None, 0.0
                for u in us:
                    acc = kappa[u][v] if acc is None else acc + kappa[u][v]
                    num = num + there_x[(u + 1) // 2]
                sums.append(acc)
                counts.append(num * there_y[(v + 1) // 2])
            for ey in range(2):
                kappa_sum = pick(sums, ey)
                mult = pick(counts, ey) * count_z
                for a in {0: (0,), 1: range(1, 7), 2: (7,)}[kind]:
                    diag = (float(LINE[a]) + line) * kappa_sum + sigma_p * mult
                    inv_diag[ex, a, ey] = 1.0 / (diag * (float(WEIGHTS[a]) * weight))


def got_face_sum(place, tile, ch, ex, a, ey, y_first, y_second, x_first, x_second):
    row = pl.ds(ch * 16 + ex * 8 + a, 1)
    got_a, got_b = y_first[row, :], y_second[row, :]
    if ey == 0:
        tile = tile + jnp.where(place.row == 0, place.before_y(got_a, got_b), 0.0)
    else:
        tile = tile + jnp.where(place.row == 7, place.after_y(got_a, got_b), 0.0)
    rows = pl.ds(pl.multiple_of(ch * 16 + ey * 8, 8), 8)
    if ex == 0 and a == 0:
        tile = tile + place.before_x(x_first[rows, :], x_second[rows, :])
    if ex == 1 and a == 7:
        tile = tile + place.after_x(x_first[rows, :], x_second[rows, :])
    return tile


def fill_pack(place, kappa, group, coarse, pack, facts):
    pack[...] = jnp.zeros(pack.shape, jnp.float32)
    facts[...] = jnp.zeros(facts.shape, jnp.float32)
    elems = kappa.shape[2]
    to = lax.broadcasted_iota(jnp.int32, (elems, LANES), 1)
    element = lax.broadcasted_iota(jnp.int32, (elems, LANES), 0)
    spread = (to // NODES == element).astype(jnp.float32)
    blocks = coarse.shape[1] // LANES
    for ex in range(2):
        numbers = group[ex].astype(jnp.float32)
        pack[pl.ds(2 * ex, 2), :] = along_z(kappa[ex], spread)
        pack[pl.ds(4 + 2 * ex, 2), :] = along_z(numbers, spread)
        row = jnp.zeros((1, LANES), jnp.float32)
        for ey in range(2):
            at = (2 * place.iy + ey) * elems
            spot = (to == at + element).astype(jnp.float32)
            after = (to == (at + 2 * elems) % LANES + element).astype(jnp.float32)
            row = row + along_z(kappa[ex, pl.ds(ey, 1), :], spot)
            row = row + along_z(numbers[ey : ey + 1], after)
        facts[pl.ds(2 + ex, 1), :] = row
    for c in range(NCD):
        for j in range(blocks):
            line = coarse[pl.ds(c, 1), pl.ds(j * LANES, LANES)]
            pack[pl.ds(8 + c * blocks + j, 1), :] = line
        facts[pl.ds(4 + c, 1), :] = coarse[pl.ds(c, 1), pl.ds(0, LANES)]


def rhs_kernel(
    pack_rows,
    summed,
    visc,
    kappa,
    group,
    coarse,
    y_first,
    y_second,
    x_first,
    x_second,
    ctab,
    zmat,
    share,
    xf,
    inner_x,
    pack,
    facts,
    first,
    second,
    start,
    rhs,
    grad_z,
    flux_z,
):
    place = Place()
    weight = ctab[T_W]
    inv_mass = [1.0 / (weight * place.mult_tile(ey)) for ey in range(2)]

    def begin(ch, carry):
        for ex in range(2):
            for a in range(8):
                for ey in range(2):
                    tile = got_face_sum(
                        place, summed[ch, ex, a, ey], ch, ex, a, ey,
                        y_first, y_second, x_first, x_second,
                    )
                    scale = place.inv_x(ex, a) * float(1.0 / WEIGHTS[a])
                    start[ch, ex, a, ey] = tile * (inv_mass[ey] * scale)
        return carry

    lax.fori_loop(0, 4, begin, 0)
    grad_z[...] = along_z(start[...].reshape(1024, LANES), zmat[0]).reshape(grad_z.shape)

    def column(index, carry):
        ch, ex, ey = index // 4, index // 2 % 2, index % 2
        coef = jnp.where(ch == 3, 1.0 / prandtl, 1.0)
        field = [start[ch, ex, a, ey] for a in range(8)]
        grad_x = along_x(DERIV, field)
        flux_x, parts = [], []
        for a in range(8):
            grad_y = along_y(ctab, T_D, field[a])
            slope = grad_z[ch, ex, a, ey]
            node = float(WEIGHTS[a]) * weight
            advect = (
                start[0, ex, a, ey] * grad_x[a]
                + start[1, ex, a, ey] * grad_y
                + start[2, ex, a, ey] * slope
            )
            nu = visc[ex, a, ey] * node * coef
            flux_x.append(nu * grad_x[a])
            flux_z[ch, ex, a, ey] = nu * slope
            parts.append(node * advect + along_y(ctab, T_DT, nu * grad_y))
        back = along_x(DERIV.T, flux_x)
        for a in range(8):
            rhs[ch, ex, a, ey] = parts[a] + back[a]
        return carry

    lax.fori_loop(0, 16, column, 0)
    grad_z[...] = along_z(flux_z[...].reshape(1024, LANES), zmat[1]).reshape(grad_z.shape)

    def finish(ch, carry):
        tiles = [
            [
                [
                    place.join_z(-(rhs[ch, ex, a, ey] + grad_z[ch, ex, a, ey]))
                    for ey in range(2)
                ]
                for a in range(8)
            ]
            for ex in range(2)
        ]
        join_own(place, tiles)
        for ex in range(2):
            for a in range(8):
                scale = place.inv_x(ex, a) * float(dt_step / WEIGHTS[a])
                for ey in range(2):
                    part = start[ch, ex, a, ey] * (place.share_y(ey) * place.share_x(ex, a))
                    share[ch, ex, a, ey] = part + tiles[ex][a][ey] * (inv_mass[ey] * scale)
        return carry

    lax.fori_loop(0, 4, finish, 0)
    for ch in range(4):
        store_y_faces(place, share, first, second, (ch,), ch * 16)
        for ey in range(2):
            xf[0, ch, ey] = share[ch, 0, 0, ey]
            xf[1, ch, ey] = share[ch, 1, 7, ey]
    first[pl.ds(STEP_EDGE, 8), :] = jnp.zeros(TILE, jnp.float32)
    second[pl.ds(STEP_EDGE, 8), :] = jnp.zeros(TILE, jnp.float32)

    def column_of(ex, ey):
        return [share[0, ex, a, ey] for a in range(8)]

    def tile_of(ex, a, ey):
        return share[1, ex, a, ey]

    store_inner(
        place, DERIV, ctab[T_BOTTOM], ctab[T_TOP], column_of, tile_of, inner_x, first, second,
        STEP_V, STEP_EDGE,
    )
    fill_pack(place, kappa, group, coarse, pack, facts)
    first[pl.ds(STEP_PACK, pack_rows), :] = pack[...]
    second[pl.ds(STEP_PACK, pack_rows), :] = pack[...]


def store_inner(
    place, matrix, bottom, top, column_of, tile_of, inner_x, first, second, at, edge
):
    for ey in range(2):
        low, high = column_of(0, ey), column_of(1, ey)
        below = float(matrix[0, 1]) * low[1]
        above = float(matrix[7, 0]) * high[0]
        for k in range(2, 8):
            below = below + float(matrix[0, k]) * low[k]
            above = above + float(matrix[7, k - 1]) * high[k - 1]
        inner_x[0, ey] = below
        inner_x[1, ey] = above
    for side in range(2):
        low = inner_x[side, 0, pl.ds(0, 1), :]
        high = inner_x[side, 1, pl.ds(7, 1), :]
        first[pl.ds(edge + side, 1), :] = place.after_y(high, low)
        second[pl.ds(edge + side, 1), :] = place.after_y(low, high)
    for ex in range(2):
        for a in range(8):
            low = jnp.sum(bottom * tile_of(ex, a, 0), axis=0, keepdims=True)
            high = jnp.sum(top * tile_of(ex, a, 1), axis=0, keepdims=True)
            row = pl.ds(at + ex * 8 + a, 1)
            first[row, :] = place.after_y(high, low)
            second[row, :] = place.after_y(low, high)


def advance_kernel(
    share,
    y_first,
    y_second,
    x_first,
    x_second,
    inv_diag,
    kap,
    grp,
    ctab,
    zmat,
    fields_new,
    resid,
    own,
    msg,
    grad_z,
    scaled,
):
    place = Place()
    weight = ctab[T_W]

    def before(row, count=8):
        rows = pl.ds(row, count)
        return place.before_x(x_first[rows, :], x_second[rows, :])

    def after(row, count=8):
        rows = pl.ds(row, count)
        return place.after_x(x_first[rows, :], x_second[rows, :])

    def step(ch, carry):
        for ex in range(2):
            for a in range(8):
                for ey in range(2):
                    fields_new[ch, ex, a, ey] = got_face_sum(
                        place, share[ch, ex, a, ey], ch, ex, a, ey,
                        y_first, y_second, x_first, x_second,
                    )
        return carry

    lax.fori_loop(0, 4, step, 0)
    grad_z[...] = along_z(fields_new[2].reshape(256, LANES), zmat[0]).reshape(grad_z.shape)
    slope = [[None, None], [None, None]]
    for ey in range(2):
        for ex in range(2):
            slope[ex][ey] = along_x(DERIV, [fields_new[0, ex, a, ey] for a in range(8)])
        mid = 0.5 * (slope[0][ey][7] + slope[1][ey][0])
        slope[0][ey][7] = mid
        slope[1][ey][0] = mid
        low, high = slope[0][ey][0], slope[1][ey][7]
        inner_low = low - float(DERIV[0, 0]) * fields_new[0, 0, 0, ey] + before(STEP_U + ey * 8)
        inner_high = high - float(DERIV[7, 7]) * fields_new[0, 1, 7, ey] + after(STEP_U + ey * 8)
        slope[0][ey][0] = jnp.where(place.prev_x, 0.5 * inner_low, low)
        slope[1][ey][7] = jnp.where(place.next_x, 0.5 * inner_high, high)
    sums = [[jnp.zeros(TILE, jnp.float32) for _ in range(2)] for _ in range(2)]
    inv_mult = [1.0 / place.mult_tile(ey) for ey in range(2)]
    inv_y = [place.inv_y(ey) for ey in range(2)]
    inv_z = place.inv_z()
    mass = [weight * place.mult_tile(ey) for ey in range(2)]
    there_low = jnp.where(place.prev_y, 1.0, 0.0)
    there_high = jnp.where(place.next_y, 1.0, 0.0)
    for ex in range(2):
        for a in range(8):
            flow = [fields_new[1, ex, a, ey] for ey in range(2)]
            below, above = inner_along_y(
                place, y_first, y_second, before, after, ex, a, STEP_V, STEP_EDGE
            )
            below = (below - float(DERIV[0, 0]) * flow[0]) * there_low
            above = (above - float(DERIV[7, 7]) * flow[1]) * there_high
            grad_y = list(place.join_y(*[along_y(ctab, T_D, tile) for tile in flow]))
            grad_y[0] = grad_y[0] + jnp.where(place.row == 0, below, 0.0)
            grad_y[1] = grad_y[1] + jnp.where(place.row == 7, above, 0.0)
            for ey in range(2):
                div = (
                    slope[ex][ey][a]
                    + grad_y[ey] * inv_y[ey]
                    + place.join_z(grad_z[ex, a, ey]) * inv_z
                )
                value = div * (mass[ey] * (place.mult_x(ex, a) * float(-WEIGHTS[a])))
                resid[ex, a, ey] = value
                scaled[ex, a, ey] = value * inv_diag[ex, a, ey] * float(1.0 / THETA)
                sums[ex][ey] = sums[ex][ey] + value * (inv_mult[ey] * place.inv_x(ex, a))
    grad_z[...] = along_z(scaled[...].reshape(256, LANES), zmat[2]).reshape(grad_z.shape)
    tiles = [[[None, None] for _ in range(8)] for _ in range(2)]
    for ex in range(2):
        for ey in range(2):
            images = own_operator(ctab, kap, scaled, grad_z, ex, ey)[1]
            for a in range(8):
                tiles[ex][a][ey] = place.join_z(images[a])
    join_own(place, tiles)
    for ex in range(2):
        for a in range(8):
            for ey in range(2):
                own[ex, a, ey] = tiles[ex][a][ey]
    row = message(place, restricted(place, sums, grp), [])
    blank = jnp.where(place.row == 0, jnp.broadcast_to(row, TILE), 0.0)
    zero = jnp.zeros(TILE, jnp.float32)

    def clear(i, carry):
        msg[i, pl.ds(0, 8), :] = zero
        msg[i, pl.ds(8, 8), :] = blank
        return carry

    lax.fori_loop(0, msg.shape[0], clear, 0)
    for dx, dy, there in neighbours(place):

        @pl.when(there)
        def _():
            to = (place.ix + dx) * place.ny + place.iy + dy
            ex, a = (0, 0) if dx < 0 else (1, 7)
            ey, b = (0, 0) if dy < 0 else (1, 7)
            if dy == 0:
                msg[to, pl.ds(0, 8), :] = own[ex, a, 0]
                msg[to, pl.ds(9, 7), :] = own[ex, a, 1, pl.ds(1, 7), :]
            elif dx == 0:
                for r in range(16):
                    if r != 8:
                        msg[to, pl.ds(r, 1), :] = own[r // 8, r % 8, ey, pl.ds(b, 1), :]
            else:
                msg[to, pl.ds(0, 1), :] = own[ex, a, ey, pl.ds(b, 1), :]


def inner_along_y(place, y_first, y_second, before, after, ex, a, at, edge):
    row = pl.ds(at + ex * 8 + a, 1)
    got_a, got_b = y_first[row, :], y_second[row, :]
    below, above = place.before_y(got_a, got_b), place.after_y(got_a, got_b)
    if (ex, a) == (0, 0):
        below = below + before(edge, 1)
        above = above + before(edge + 1, 1)
    if (ex, a) == (1, 7):
        below = below + after(edge, 1)
        above = above + after(edge + 1, 1)
    return below, above


def neighbours(place):
    along = ((-1, place.prev_x), (0, None), (1, place.next_x))
    across = ((-1, place.prev_y), (0, None), (1, place.next_y))
    out = []
    for dx, has_x in along:
        for dy, has_y in across:
            if dx == 0 and dy == 0:
                continue
            there = has_y if has_x is None else (has_x if has_y is None else has_x & has_y)
            out.append((dx, dy, there))
    return out


SMOOTH_X, SMOOTH_Y, SMOOTH_EDGE, SMOOTH_ROWS = 16, 16, 32, 40


def turn_smooth_kernel(own, inner_x, y_first, y_second, first, second):
    place = Place()
    sides = []
    for side, (ex, a) in enumerate(((0, 0), (1, 7))):
        row = pl.ds(15 * side, 1)
        got_a, got_b = y_first[row, :], y_second[row, :]
        low = own[ex, a, 0] + jnp.where(place.row == 0, place.before_y(got_a, got_b), 0.0)
        high = own[ex, a, 1] + jnp.where(place.row == 7, place.after_y(got_a, got_b), 0.0)
        sides.append((low, high))
    for ey in range(2):
        rows = pl.ds(ey * 8, 8)
        first[rows, :] = place.after_x(sides[1][ey], sides[0][ey])
        second[rows, :] = place.after_x(sides[0][ey], sides[1][ey])
    first[pl.ds(SMOOTH_EDGE, 8), :] = jnp.zeros(TILE, jnp.float32)
    second[pl.ds(SMOOTH_EDGE, 8), :] = jnp.zeros(TILE, jnp.float32)
    turn_edges(
        place, inner_x, y_first, y_second, first, second, SMOOTH_X, SMOOTH_EDGE, SMOOTH_Y
    )


def restricted(place, sums, grp):
    values = []
    for c in range(NCD):
        acc = jnp.zeros(TILE, jnp.float32)
        for ex in range(2):
            for ey in range(2):
                group = grp[pl.ds((ex + 1) * 4 + ey + 1, 1), :]
                acc = acc + jnp.where(group == float(c), sums[ex][ey], 0.0)
        values.append(total(acc))
    return values


def message(place, own_values, scalars):
    lane = lax.broadcasted_iota(jnp.int32, (1, LANES), 1)
    spot = (place.ix * place.ny + place.iy) % (LANES // NCD)
    after = (spot + 1) % (LANES // NCD)
    row = jnp.zeros((1, LANES), jnp.float32)
    for c, value in enumerate(own_values):
        row = row + jnp.where(lane == spot * NCD + c, value, 0.0)
    for c, value in enumerate(scalars):
        if value is None:
            continue
        row = row + jnp.where(lane == after * NCD + c, value, 0.0)
    return row


def send_to_all(msg, row):
    def send(i, carry):
        msg[i] = row
        return carry

    lax.fori_loop(0, msg.shape[0], send, 0, unroll=msg.shape[0] <= 64)


def smooth_kernel(
    own,
    y_first,
    y_second,
    x_first,
    x_second,
    inv_diag,
    kap,
    grp,
    extra,
    facts,
    ctab,
    zmat,
    image,
    smoothed,
    msg,
    scaled,
    slope_z,
):
    place = Place()
    weight = ctab[T_W]
    corner = float(SCALED[0, 0])

    def before(row, count=8):
        rows = pl.ds(row, count)
        return place.before_x(x_first[rows, :], x_second[rows, :])

    def after(row, count=8):
        rows = pl.ds(row, count)
        return place.after_x(x_first[rows, :], x_second[rows, :])

    for ex in range(2):
        for a in range(8):
            for ey in range(2):
                tile = got_face_sum(
                    place, own[ex, a, ey], 0, ex, a, ey, y_first, y_second, x_first, x_second
                )
                image[ex, a, ey] = tile
                scaled[ex, a, ey] = tile * inv_diag[ex, a, ey] * float(1.0 / THETA)
    slope_z[...] = along_z(scaled[...].reshape(256, LANES), zmat[2]).reshape(slope_z.shape)
    there_x = (jnp.where(place.prev_x, 1.0, 0.0), jnp.where(place.next_x, 1.0, 0.0))
    there_y = (jnp.where(place.prev_y, 1.0, 0.0), jnp.where(place.next_y, 1.0, 0.0))

    def kappa_of(x, y):
        return kap[pl.ds(x * 4 + y, 1), :]

    tiles = [[[None, None] for _ in range(8)] for _ in range(2)]
    for ex in range(2):
        for ey in range(2):
            values = [scaled[ex, a, ey] for a in range(8)]
            slopes = along_x(SCALED, values)
            y_next = 0 if ey == 0 else 3
            edge_row = place.row == (0 if ey == 0 else 7)
            for a in range(8):
                value = values[a]
                slope_y = along_y(ctab, T_K, value)
                flat = slope_z[ex, a, ey]
                same = slopes[a] + slope_y + flat
                acc = kappa_of(ex + 1, ey + 1) * same + sigma_p * value
                inner = inner_along_y(
                    place, y_first, y_second, before, after, ex, a, SMOOTH_Y, SMOOTH_EDGE
                )[ey]
                turned_y = inner + corner * value
                beyond = kappa_of(ex + 1, y_next) * (slopes[a] + turned_y + flat)
                beyond = (beyond + sigma_p * value) * there_y[ey]
                if (ex, a) in ((0, 0), (1, 7)):
                    x_next = 0 if ex == 0 else 3
                    get = before if ex == 0 else after
                    turned_x = get(SMOOTH_X + ey * 8) + corner * value
                    side = kappa_of(x_next, ey + 1) * (turned_x + slope_y + flat)
                    acc = acc + (side + sigma_p * value) * there_x[ex]
                    far = kappa_of(x_next, y_next) * (turned_x + turned_y + flat)
                    beyond = beyond + (far + sigma_p * value) * (there_x[ex] * there_y[ey])
                acc = acc + jnp.where(edge_row, beyond, 0.0)
                tiles[ex][a][ey] = place.join_z(acc * (float(WEIGHTS[a]) * weight))
    join_own(place, tiles)
    inv_mult = [1.0 / place.mult_tile(ey) for ey in range(2)]
    sums = [[jnp.zeros(TILE, jnp.float32) for _ in range(2)] for _ in range(2)]
    square = jnp.zeros(TILE, jnp.float32)
    for ex in range(2):
        for a in range(8):
            for ey in range(2):
                value = image[ex, a, ey]
                defect = (value - tiles[ex][a][ey]) * inv_diag[ex, a, ey]
                update = scaled[ex, a, ey]
                result = (
                    float(1.0 + RHO_NEXT * RHO) * update + float(2.0 * RHO_NEXT / DELTA) * defect
                )
                smoothed[ex, a, ey] = result
                weighed = value * (inv_mult[ey] * place.inv_x(ex, a))
                sums[ex][ey] = sums[ex][ey] + weighed
                square = square + weighed * result
    own_sums = restricted(place, sums, grp)
    if msg.shape[1] == 1:
        send_to_all(msg, message(place, own_sums, []) + extra[...])
        return
    slope_z[...] = along_z(smoothed[...].reshape(256, LANES), zmat[2]).reshape(slope_z.shape)
    energy = jnp.zeros(TILE, jnp.float32)
    for ex in range(2):
        for ey in range(2):
            values, images = own_operator(ctab, kap, smoothed, slope_z, ex, ey)
            for a in range(8):
                energy = energy + values[a] * images[a]
                tiles[ex][a][ey] = place.join_z(images[a])
    join_own(place, tiles)
    row = message(place, own_sums, [None, None, total(square), total(energy)]) + extra[...]
    dual = restricted_around(place, tiles, inv_mult, grp)
    out = facts[...]
    out = out + jnp.where(place.row == 0, jnp.broadcast_to(row, TILE), 0.0)
    out = out + jnp.where(place.row == 1, jnp.broadcast_to(dual, TILE), 0.0)
    send_to_all(msg, out)


def restricted_around(place, tiles, inv_mult, grp):
    lane = lax.broadcasted_iota(jnp.int32, (1, LANES), 1)
    weighed = [
        [[tiles[ex][a][ey] * (inv_mult[ey] * place.inv_x(ex, a)) for ey in range(2)] for a in range(8)]
        for ex in range(2)
    ]

    def rows_of(tile, y):
        if y == 0:
            return jnp.where(place.row == 0, tile[0], 0.0)
        if y == 3:
            return jnp.where(place.row == 7, tile[1], 0.0)
        return tile[y - 1]

    there_x = (place.prev_x, None, None, place.next_x)
    there_y = (place.prev_y, None, None, place.next_y)
    by_device = [
        [[jnp.zeros(TILE, jnp.float32) for _ in range(NCD)] for _ in range(3)] for _ in range(3)
    ]
    for x in range(4):
        for y in range(4):
            if x == 0:
                acc = rows_of(weighed[0][0], y)
            elif x == 3:
                acc = rows_of(weighed[1][7], y)
            else:
                acc = rows_of(weighed[x - 1][0], y)
                for a in range(1, 8):
                    acc = acc + rows_of(weighed[x - 1][a], y)
            for there in (there_x[x], there_y[y]):
                if there is not None:
                    acc = jnp.where(there, acc, 0.0)
            group = grp[pl.ds(x * 4 + y, 1), :]
            device = by_device[(x + 1) // 2][(y + 1) // 2]
            for c in range(NCD):
                device[c] = device[c] + jnp.where(group == float(c), acc, 0.0)
    row = jnp.zeros((1, LANES), jnp.float32)
    for dx in range(3):
        for dy in range(3):
            at = ((place.ix + dx - 1) * place.ny + place.iy + dy - 1) * NCD
            for c in range(NCD):
                row = row + jnp.where(lane == at + c, total(by_device[dx][dy][c]), 0.0)
    return row


def coarse_part(place, blocks, got, coarse, grp, at=0):
    lane = lax.broadcasted_iota(jnp.int32, (1, LANES), 1)
    values = [jnp.zeros((1, LANES), jnp.float32) for _ in range(blocks)]
    per = LANES // NCD
    for j in range(blocks):

        def gather(i, acc, j=j):
            return jnp.where(lane // NCD == i, got[j * per + i, pl.ds(at, 1), :], acc)

        values[j] = lax.fori_loop(0, per, gather, values[j], unroll=blocks == 1)

    def solved(dx, dy, c):
        acc = None
        for j in range(blocks):
            term = coarse[pl.ds(((dx * 3 + dy) * NCD + c) * blocks + j, 1), :] * values[j]
            acc = term if acc is None else acc + term
        return jnp.sum(acc, axis=1, keepdims=True)

    return prolonged(place, solved, grp)


def prolonged(place, solved, grp):
    device = [[[solved(dx, dy, c) for c in range(NCD)] for dy in range(3)] for dx in range(3)]
    inv_z = jnp.where(place.low_z | place.high_z, 0.5, 1.0)
    rows = []
    for x in range(4):
        line = []
        for y in range(4):
            group = grp[pl.ds(x * 4 + y, 1), :]
            acc = jnp.zeros((1, LANES), jnp.float32)
            for c in range(NCD):
                acc = acc + jnp.where(
                    group == float(c), device[(x + 1) // 2][(y + 1) // 2][c], 0.0
                )
            line.append(place.join_z(jnp.broadcast_to(acc, TILE)) * inv_z)
        rows.append(line)
    low_y = jnp.where(place.prev_y, 0.5, 1.0)
    high_y = jnp.where(place.next_y, 0.5, 1.0)

    def tile(ex, kind, ey):
        if kind == 1:
            vals = [rows[ex + 1][y] for y in range(4)]
        elif kind == 0:
            scale = place.inv_x(ex, 0)
            vals = [(rows[ex][y] + rows[ex + 1][y]) * scale for y in range(4)]
        else:
            scale = place.inv_x(ex, 7)
            vals = [(rows[ex + 1][y] + rows[ex + 2][y]) * scale for y in range(4)]
        mid = vals[ey + 1]
        low = (vals[ey] + mid) * (low_y if ey == 0 else 0.5)
        high = (mid + vals[ey + 2]) * (high_y if ey == 1 else 0.5)
        return jnp.where(place.row == 0, low, jnp.where(place.row == 7, high, mid))

    return tile


def kind_of(a):
    return 0 if a == 0 else (2 if a == 7 else 1)


def own_operator(ctab, kap, field, slope_z, ex, ey):
    weight = ctab[T_W]
    tiles = [field[ex, a, ey] for a in range(8)]
    slopes = along_x(SCALED, tiles)
    kappa = kap[pl.ds((ex + 1) * 4 + ey + 1, 1), :]
    out = []
    for a in range(8):
        stiff = slopes[a] + along_y(ctab, T_K, tiles[a]) + slope_z[ex, a, ey]
        out.append((kappa * stiff + sigma_p * tiles[a]) * (float(WEIGHTS[a]) * weight))
    return tiles, out


def first_direction_kernel(
    blocks,
    got,
    coarse,
    grp,
    kap,
    inv_diag,
    resid,
    own,
    ctab,
    zmat,
    direction,
    out,
    inner_x,
    first,
    second,
    extra,
    slope_z,
    image,
):
    place = Place()
    inv_mult = [1.0 / place.mult_tile(ey) for ey in range(2)]
    part = coarse_part(place, blocks, got, coarse, grp, 8)
    image[...] = own[...]
    for dx, dy, there in neighbours(place):

        @pl.when(there)
        def _():
            frm = (place.ix + dx) * place.ny + place.iy + dy
            ex, a = (0, 0) if dx < 0 else (1, 7)
            ey, b = (0, 0) if dy < 0 else (1, 7)
            edge = place.row == b
            if dy == 0:
                low = got[frm, pl.ds(0, 8), :]
                high = jnp.where(
                    place.row == 0, pltpu.roll(low, 1, 0), got[frm, pl.ds(8, 8), :]
                )
                image[ex, a, 0] = image[ex, a, 0] + low
                image[ex, a, 1] = image[ex, a, 1] + high
            elif dx == 0:
                for r in range(16):
                    line = got[frm, pl.ds(7 if r == 8 else r, 1), :]
                    tile = image[r // 8, r % 8, ey]
                    image[r // 8, r % 8, ey] = tile + jnp.where(edge, line, 0.0)
            else:
                line = got[frm, pl.ds(0, 1), :]
                image[ex, a, ey] = image[ex, a, ey] + jnp.where(edge, line, 0.0)

    energy = jnp.zeros(TILE, jnp.float32)
    for ex in range(2):
        for ey in range(2):
            kinds = [part(ex, kind, ey) for kind in range(3)]
            for a in range(8):
                known = resid[ex, a, ey]
                inverse = inv_diag[ex, a, ey]
                defect = (known - image[ex, a, ey]) * inverse
                value = (
                    float((1.0 + RHO_NEXT * RHO) / THETA) * (known * inverse)
                    + float(2.0 * RHO_NEXT / DELTA) * defect
                    + kinds[kind_of(a)]
                )
                direction[ex, a, ey] = value
                scale = place.inv_x(ex, a)
                energy = energy + value * known * (inv_mult[ey] * scale)
    slope_z[...] = along_z(direction[...].reshape(256, LANES), zmat[2]).reshape(slope_z.shape)
    curvature = jnp.zeros(TILE, jnp.float32)
    tiles = [[[None, None] for _ in range(8)] for _ in range(2)]
    for ex in range(2):
        for ey in range(2):
            values, images = own_operator(ctab, kap, direction, slope_z, ex, ey)
            for a in range(8):
                curvature = curvature + values[a] * images[a]
                tiles[ex][a][ey] = place.join_z(images[a])
    join_own(place, tiles)
    for ex in range(2):
        for a in range(8):
            for ey in range(2):
                out[ex, a, ey] = tiles[ex][a][ey]
    store_y_faces(place, out, first, second, (), 0)
    first[pl.ds(SMOOTH_EDGE, 8), :] = jnp.zeros(TILE, jnp.float32)
    second[pl.ds(SMOOTH_EDGE, 8), :] = jnp.zeros(TILE, jnp.float32)

    def tile_of(ex, a, ey):
        return tiles[ex][a][ey] * inv_diag[ex, a, ey] * float(1.0 / THETA)

    def column_of(ex, ey):
        return [tile_of(ex, a, ey) for a in range(8)]

    store_inner(
        place, SCALED, ctab[T_KBOTTOM], ctab[T_KTOP], column_of, tile_of, inner_x, first, second,
        SMOOTH_Y, SMOOTH_EDGE,
    )
    extra[...] = message(place, [], [total(energy), total(curvature)])


def gathered_scalars(got, count):
    lane = lax.broadcasted_iota(jnp.int32, (1, LANES), 1)
    per = LANES // NCD
    sums = []
    for c in range(count):
        acc = jnp.zeros((1, LANES), jnp.float32)

        def gather(i, acc, c=c):
            return acc + jnp.where(lane == ((i + 1) % per) * NCD + c, got[i], 0.0)

        acc = lax.fori_loop(0, got.shape[0], gather, acc, unroll=got.shape[0] <= per)
        sums.append(jnp.sum(acc, axis=1, keepdims=True))
    return sums


def second_direction_kernel(
    blocks,
    got,
    coarse,
    grp,
    kap,
    resid,
    direction,
    image,
    smoothed,
    ctab,
    zmat,
    following,
    known,
    msg,
    slope_z,
):
    place = Place()
    inv_mult = [1.0 / place.mult_tile(ey) for ey in range(2)]
    part = coarse_part(place, blocks, got, coarse, grp)
    energy, curvature = gathered_scalars(got, 2)
    step = energy / curvature
    lane = lax.broadcasted_iota(jnp.int32, (1, LANES), 1)
    known[...] = jnp.where(lane == 0, energy, jnp.where(lane == 1, curvature, 0.0))
    energy_next = jnp.zeros(TILE, jnp.float32)
    cross = jnp.zeros(TILE, jnp.float32)
    for ex in range(2):
        for ey in range(2):
            kinds = [part(ex, kind, ey) for kind in range(3)]
            for a in range(8):
                value = direction[ex, a, ey] - step * (smoothed[ex, a, ey] + kinds[kind_of(a)])
                following[ex, a, ey] = value
                weighed = value * (inv_mult[ey] * place.inv_x(ex, a))
                was = image[ex, a, ey]
                energy_next = energy_next + weighed * (resid[ex, a, ey] - step * was)
                cross = cross + weighed * was
    slope_z[...] = along_z(following[...].reshape(256, LANES), zmat[2]).reshape(slope_z.shape)
    square = jnp.zeros(TILE, jnp.float32)
    for ex in range(2):
        for ey in range(2):
            values, images = own_operator(ctab, kap, following, slope_z, ex, ey)
            for a in range(8):
                square = square + values[a] * images[a]
    send_to_all(msg, message(place, [], [total(energy_next), total(square), total(cross)]))


def pressure_kernel(got, known, direction, following, pressure):
    energy = known[:, pl.ds(0, 1)]
    curvature = known[:, pl.ds(1, 1)]
    energy_next, square, cross = gathered_scalars(got, 3)
    ratio = energy_next / energy
    step = energy / curvature
    step_next = energy_next / (square + 2.0 * ratio * cross + ratio * ratio * curvature)
    weight_old = step + step_next * ratio
    for ex in range(2):
        for a in range(8):
            for ey in range(2):
                pressure[ex, a, ey] = (
                    weight_old * direction[ex, a, ey] + step_next * following[ex, a, ey]
                )


def coarse_energy(place, got, values, kappa, number):
    lane, row = place.lane, place.row
    for ex in range(2):
        for gx in range(8):
            own = jnp.zeros((1, LANES), jnp.float32)
            group = jnp.zeros((1, LANES), jnp.float32)
            spot = lane[0:1] // 32
            for gy in range(4):
                line = got[gx * 4 + gy, pl.ds(2 + ex, 1), :]
                own = jnp.where(spot == gy, line, own)
                group = jnp.where(spot == (gy + 1) % 4, line, group)
            kappa[ex, pl.ds(gx, 1), :] = own
            number[ex, pl.ds(gx, 1), :] = group
    grid = [jnp.zeros(TILE, jnp.float32) for _ in range(2)]
    numbers = [pltpu.roll(number[ex], 96, 1) for ex in range(2)]
    for q in range(4):
        for c in range(NCD):
            mine = jnp.where(lane == row * 16 + q * 4 + c, values, 0.0)
            mine = jnp.sum(mine, axis=1, keepdims=True)
            for ex in range(2):
                chosen = (lane // 32 == q) & (numbers[ex] == float(c))
                grid[ex] = jnp.where(chosen, mine, grid[ex])

    def ends_y(v):
        low = jnp.where(lane >= 16, 0.5 * (v + pltpu.roll(v, 16, 1)), v)
        return low, v, jnp.where(lane < 112, 0.5 * (v + pltpu.roll(v, 112, 1)), v)

    def ends_z(v):
        low = jnp.where(lane % 16 > 0, 0.5 * (v + pltpu.roll(v, 1, 1)), v)
        return low, v, jnp.where(lane % 16 < 15, 0.5 * (v + pltpu.roll(v, 127, 1)), v)

    low = jnp.where(row > 0, 0.5 * (grid[0] + pltpu.roll(grid[1], 1, 0)), grid[0])
    mid = 0.5 * (grid[0] + grid[1])
    high = jnp.where(row < 7, 0.5 * (grid[1] + pltpu.roll(grid[0], 7, 0)), grid[1])
    mass = [float(WEIGHTS[0]), float(np.sum(WEIGHTS[1:7])), float(WEIGHTS[7])]
    links = (
        (0, 1, -float(np.sum(STIFF[0, 1:7]))),
        (0, 2, -float(STIFF[0, 7])),
        (1, 2, -float(np.sum(STIFF[7, 1:7]))),
    )
    energy = jnp.zeros(TILE, jnp.float32)
    for ex, line in enumerate(((low, grid[0], mid), (mid, grid[1], high))):
        nodes = [[ends_z(v) for v in ends_y(w)] for w in line]
        stiff = jnp.zeros(TILE, jnp.float32)
        square = jnp.zeros(TILE, jnp.float32)
        for i in range(3):
            for j in range(3):
                for k, l, weight in links:
                    factor = weight * mass[i] * mass[j]
                    for first, second in (
                        (nodes[k][i][j], nodes[l][i][j]),
                        (nodes[i][k][j], nodes[i][l][j]),
                        (nodes[i][j][k], nodes[i][j][l]),
                    ):
                        gap = first - second
                        stiff = stiff + (factor * gap) * gap
                for k in range(3):
                    value = nodes[i][j][k]
                    square = square + (mass[i] * mass[j] * mass[k] * value) * value
        energy = energy + kappa[ex] * stiff + sigma_p * square
    return total(energy)


def finish_kernel(
    got, grp, direction, smoothed, pressure, matrix, kappa, number
):
    place = Place()
    per = LANES // NCD
    row_lane = lax.broadcasted_iota(jnp.int32, (1, LANES), 1)
    rest = jnp.zeros((1, LANES), jnp.float32)
    dual = jnp.zeros((1, LANES), jnp.float32)
    sums = [jnp.zeros((1, LANES), jnp.float32) for _ in range(4)]
    for i in range(per):
        line = got[i, pl.ds(0, 1), :]
        rest = jnp.where(row_lane // NCD == i, line, rest)
        dual = dual + got[i, pl.ds(1, 1), :]
        for c in range(4):
            sums[c] = sums[c] + jnp.where(row_lane == ((i + 1) % per) * NCD + c, line, 0.0)
        matrix[pl.ds(i * NCD, NCD), :] = got[i, pl.ds(4, NCD), :]
    energy, curvature, square, self_energy = [
        jnp.sum(value, axis=1, keepdims=True) for value in sums
    ]
    values = lax.dot_general(
        jnp.broadcast_to(rest, TILE),
        matrix[...],
        (((1,), (1,)), ((), ())),
        precision=lax.Precision.HIGHEST,
        preferred_element_type=jnp.float32,
    )
    line = values[0:1]
    cross = square + jnp.sum(line * rest, axis=1, keepdims=True)
    both = self_energy + 2.0 * jnp.sum(line * dual, axis=1, keepdims=True)
    both = both + coarse_energy(place, got, values, kappa, number)
    step = energy / curvature
    energy_next = step * step * cross - energy
    ratio = energy_next / energy
    with_image = curvature - step * cross
    with_itself = curvature - 2.0 * step * cross + step * step * both
    step_next = energy_next / (
        with_itself + 2.0 * ratio * with_image + ratio * ratio * curvature
    )
    old = step + step_next * (1.0 + ratio)
    new = -step_next * step

    def solved(dx, dy, c):
        at = ((place.ix + dx - 1) * place.ny + place.iy + dy - 1) * NCD + c
        return jnp.sum(jnp.where(row_lane == at, line, 0.0), axis=1, keepdims=True)

    part = prolonged(place, masked(place, solved), grp)
    for ex in range(2):
        for ey in range(2):
            kinds = [part(ex, kind, ey) for kind in range(3)]
            for a in range(8):
                pressure[ex, a, ey] = old * direction[ex, a, ey] + new * (
                    smoothed[ex, a, ey] + kinds[kind_of(a)]
                )


def masked(place, solved):
    there_x = (place.prev_x, None, place.next_x)
    there_y = (place.prev_y, None, place.next_y)

    def value(dx, dy, c):
        out = solved(dx, dy, c)
        for there in (there_x[dx], there_y[dy]):
            if there is not None:
                out = jnp.where(there, out, 0.0)
        return out

    return value


def call(body, outs, scratch=(), **more):
    return pl.pallas_call(
        body,
        out_shape=[jax.ShapeDtypeStruct(shape, jnp.float32) for shape in outs],
        scratch_shapes=[
            pltpu.VMEM(shape, jnp.float32) if isinstance(shape, tuple) else shape
            for shape in scratch
        ],
        **more,
        compiler_params=pltpu.CompilerParams(vmem_limit_bytes=24 * 1024 * 1024),
    )


def swap(first, second, axis):
    count = lax.axis_size(axis)
    first_pairs = [(i, i ^ 1) for i in range(count) if i ^ 1 < count]
    second_pairs = [(i, ((i + 1) ^ 1) - 1) for i in range(1, count) if ((i + 1) ^ 1) - 1 < count]
    second_got = lax.ppermute(second, axis, second_pairs)
    return lax.ppermute(first, axis, first_pairs), second_got


def per_device(fields, viscosity, inv_density, elem_group, coarse_inverse):
    length = fields.shape[5]
    elems_z = length // NODES
    devices = lax.axis_size("gx") * lax.axis_size("gy")
    blocks = coarse_inverse.shape[1] // LANES
    pack_rows = -(-(8 + NCD * blocks) // 8) * 8
    tiles_np, mats_np = constant_tables(elems_z)
    ctab, zmat = jnp.asarray(tiles_np), jnp.asarray(mats_np)
    one = fields.shape[1:]
    four = fields.shape
    faces = (64, LANES)
    xf_shape = (2, 4, 2, 8, LANES)
    inner_shape = (2, 2, 8, LANES)
    y_shape, x_shape = (STEP_PACK + pack_rows, LANES), (STEP_PACK + 3 * pack_rows, LANES)
    smooth_shape = (SMOOTH_ROWS, LANES)
    rows = (devices, 1, LANES)
    grid_fits = (
        blocks == 1
        and lax.axis_size("gx") == 8
        and lax.axis_size("gy") * fields.shape[3] * elems_z == LANES
    )

    def exchange_all(msg):
        return lax.all_to_all(msg, BOTH, 0, 0, tiled=True)

    summed, xf, first, second = call(
        mass_kernel,
        [four, xf_shape, faces, faces],
        [four, pltpu.SemaphoreType.DMA((4,))],
        in_specs=[pl.BlockSpec(memory_space=pltpu.HBM)],
    )(fields)
    y_got = swap(first, second, "gy")
    first, second = call(turn_faces_kernel, [faces, faces])(xf, *y_got)
    x_got = swap(first, second, "gx")
    share, xf, inner_x, pack, facts, first, second = call(
        functools.partial(rhs_kernel, pack_rows),
        [four, xf_shape, inner_shape, (pack_rows, LANES), TILE, y_shape, y_shape],
        [four, four, four, four],
    )(
        summed,
        viscosity,
        inv_density,
        elem_group,
        coarse_inverse,
        *y_got,
        *x_got,
        ctab,
        zmat,
    )
    y_got = swap(first, second, "gy")
    first, second = call(functools.partial(turn_step_kernel, pack_rows), [x_shape, x_shape])(
        xf, inner_x, pack, *y_got
    )
    x_got = swap(first, second, "gx")
    inv_diag, kap, grp, coarse = call(
        functools.partial(setup_kernel, pack_rows, blocks),
        [one, (16, LANES), (16, LANES), (9 * NCD * blocks, LANES)],
    )(pack, *y_got, *x_got, ctab)
    fields_new, resid, own, msg = call(
        advance_kernel, [four, one, one, (devices, 16, LANES)], [one, one]
    )(share, *y_got, *x_got, inv_diag, kap, grp, ctab, zmat)
    got = exchange_all(msg)
    direction, own, inner_x, first, second, extra = call(
        functools.partial(first_direction_kernel, blocks),
        [one, one, inner_shape, smooth_shape, smooth_shape, (1, LANES)],
        [one, one],
    )(got, coarse, grp, kap, inv_diag, resid, own, ctab, zmat)
    y_got = swap(first, second, "gy")
    first, second = call(turn_smooth_kernel, [smooth_shape, smooth_shape])(own, inner_x, *y_got)
    x_got = swap(first, second, "gx")
    image, image_smoothed, msg = call(
        smooth_kernel, [one, one, (devices, 8, LANES) if grid_fits else rows], [one, one]
    )(own, *y_got, *x_got, inv_diag, kap, grp, extra, facts, ctab, zmat)
    got = exchange_all(msg)
    if grid_fits:
        (pressure,) = call(
            finish_kernel, [one], [(LANES, LANES), (2,) + TILE, (2,) + TILE]
        )(got, grp, direction, image_smoothed)
        return (fields_new, pressure)
    following, known, msg = call(
        functools.partial(second_direction_kernel, blocks), [one, (1, LANES), rows], [one]
    )(got, coarse, grp, kap, resid, direction, image, image_smoothed, ctab, zmat)
    got = exchange_all(msg)
    (pressure,) = call(pressure_kernel, [one])(got, known, direction, following)
    return (fields_new, pressure)


def solution(mesh):
    placed = (
        P(None, "gx", None, "gy", None, None),
        P("gx", None, "gy", None, None),
        P("gx", "gy", None),
        P("gx", "gy", None),
        P(("gx", "gy"), None),
    )
    return jax.shard_map(
        per_device,
        mesh=mesh,
        in_specs=placed,
        out_specs=(P(None, "gx", None, "gy", None, None), P("gx", None, "gy", None, None)),
        check_vma=False,
    )
```

```python
import functools

import jax
import jax.numpy as jnp
import ml_dtypes
import numpy as np
from jax import lax
from jax.experimental import pallas as pl
from jax.experimental.pallas import tpu as pltpu
from jax.sharding import PartitionSpec as P

NCD = 4
NODES = 8
LANES = 128
TILE = (8, 128)
BOTH = ("gx", "gy")

dt_step = 0.01
sigma_p = 4.0
prandtl = 0.7
cheb_ratio = 0.1


def tables():
    points = np.array(
        [
            -1.0,
            -0.8717401485096066,
            -0.5917001814331423,
            -0.2092992179024789,
            0.2092992179024789,
            0.5917001814331423,
            0.8717401485096066,
            1.0,
        ]
    )
    weights = np.array(
        [
            1.0 / 28.0,
            0.2107042271435061,
            0.3411226924835044,
            0.4124587946587038,
            0.4124587946587038,
            0.3411226924835044,
            0.2107042271435061,
            1.0 / 28.0,
        ]
    )
    identity = np.eye(8)
    differ = points[:, None] - points[None, :] + identity
    barycentric = 1.0 / np.prod(differ, axis=1)
    offdiag = barycentric[None, :] / barycentric[:, None] / differ * (1.0 - identity)
    derivative = offdiag - identity * np.sum(offdiag, axis=1)[:, None]
    mass_one = identity * weights[None, :]
    stiff_one = derivative.T @ mass_one @ derivative
    stiff_three = (
        np.kron(np.kron(stiff_one, mass_one), mass_one)
        + np.kron(np.kron(mass_one, stiff_one), mass_one)
        + np.kron(np.kron(mass_one, mass_one), stiff_one)
    )
    three_diag = np.sum(stiff_three * np.eye(512), axis=1)
    spectral_bound = float(np.max(np.sum(np.abs(stiff_three), axis=1) / three_diag))
    return (derivative, weights, stiff_one, spectral_bound)


DERIV, WEIGHTS, STIFF, BOUND = tables()
SCALED = STIFF / WEIGHTS[:, None]
LINE = np.diag(STIFF) / WEIGHTS
THETA = 0.5 * (BOUND + cheb_ratio * BOUND)
DELTA = 0.5 * (BOUND - cheb_ratio * BOUND)
RHO = DELTA / THETA
RHO_NEXT = 1.0 / (2.0 * THETA / DELTA - RHO)


def constant_tables(elems_z):
    def turned(matrix):
        rows = np.arange(8)
        return [np.repeat(matrix[rows, (rows - s) % 8][:, None], LANES, 1) for s in range(8)]

    wz = np.tile(WEIGHTS, elems_z)
    kz = np.tile(LINE, elems_z)
    tiles = turned(DERIV) + turned(DERIV.T) + turned(SCALED)
    tiles += [WEIGHTS[:, None] * wz[None, :], LINE[:, None] + kz[None, :]]
    for matrix in (DERIV, SCALED):
        for node in (7, 0):
            inner = matrix[node] * (np.arange(8) != node)
            tiles.append(np.repeat(inner[:, None], LANES, 1))
    eye = np.eye(elems_z)
    mats = [np.kron(eye, DERIV.T), np.kron(eye, DERIV), np.kron(eye, SCALED.T)]
    halves = []
    for mat in mats:
        high = mat.astype(ml_dtypes.bfloat16)
        low = (mat - high.astype(np.float64)).astype(ml_dtypes.bfloat16)
        both = np.concatenate([high, low], 1)
        halves.append(np.concatenate([both, both], 0))
    return np.stack(tiles).astype(np.float32), np.stack(halves)


T_D, T_DT, T_K, T_W, T_LINE = 0, 8, 16, 24, 25
T_TOP, T_BOTTOM, T_KTOP, T_KBOTTOM = 26, 27, 28, 29


class Place:
    def __init__(self):
        self.ix = lax.axis_index("gx")
        self.iy = lax.axis_index("gy")
        self.nx = lax.axis_size("gx")
        self.ny = lax.axis_size("gy")
        self.even_x = self.ix % 2 == 0
        self.even_y = self.iy % 2 == 0
        self.row = lax.broadcasted_iota(jnp.int32, TILE, 0)
        self.lane = lax.broadcasted_iota(jnp.int32, TILE, 1)
        self.low_z = (self.lane % 8 == 0) & (self.lane > 0)
        self.high_z = (self.lane % 8 == 7) & (self.lane < LANES - 1)
        self.prev_x = self.ix > 0
        self.next_x = self.ix < self.nx - 1
        self.prev_y = self.iy > 0
        self.next_y = self.iy < self.ny - 1

    def mult_tile(self, ey):
        along_z = 1.0 + jnp.where(self.low_z | self.high_z, 1.0, 0.0)
        low = 1.0 if ey == 1 else jnp.where(self.prev_y, 1.0, 0.0)
        high = 1.0 if ey == 0 else jnp.where(self.next_y, 1.0, 0.0)
        along_y = 1.0 + jnp.where(self.row == 0, low, jnp.where(self.row == 7, high, 0.0))
        return along_y * along_z

    def inv_x(self, ex, a):
        if a == 0:
            return 0.5 if ex == 1 else jnp.where(self.prev_x, 0.5, 1.0)
        if a == 7:
            return 0.5 if ex == 0 else jnp.where(self.next_x, 0.5, 1.0)
        return 1.0

    def mult_x(self, ex, a):
        if a == 0:
            return 2.0 if ex == 1 else jnp.where(self.prev_x, 2.0, 1.0)
        if a == 7:
            return 2.0 if ex == 0 else jnp.where(self.next_x, 2.0, 1.0)
        return 1.0

    def share_x(self, ex, a):
        if (ex, a) == (0, 0):
            return jnp.where(self.prev_x, 0.5, 1.0)
        if (ex, a) == (1, 7):
            return jnp.where(self.next_x, 0.5, 1.0)
        return 1.0

    def share_y(self, ey):
        if ey == 0:
            return jnp.where((self.row == 0) & self.prev_y, 0.5, 1.0)
        return jnp.where((self.row == 7) & self.next_y, 0.5, 1.0)

    def inv_y(self, ey):
        low = 0.5 if ey == 1 else jnp.where(self.prev_y, 0.5, 1.0)
        high = 0.5 if ey == 0 else jnp.where(self.next_y, 0.5, 1.0)
        return jnp.where(self.row == 0, low, jnp.where(self.row == 7, high, 1.0))

    def inv_z(self):
        return jnp.where(self.low_z | self.high_z, 0.5, 1.0)

    def join_z(self, t):
        up = pltpu.roll(t, LANES - 1, 1)
        down = pltpu.roll(t, 1, 1)
        return t + jnp.where(self.high_z, up, jnp.where(self.low_z, down, 0.0))

    def to_low(self, below):
        return jnp.where(self.row == 0, pltpu.roll(below, 1, 0), 0.0)

    def to_high(self, above):
        return jnp.where(self.row == 7, pltpu.roll(above, 7, 0), 0.0)

    def join_y(self, below, above):
        return below + self.to_high(above), above + self.to_low(below)

    def before_x(self, first, second):
        return jnp.where(self.even_x, second, first)

    def after_x(self, first, second):
        return jnp.where(self.even_x, first, second)

    def before_y(self, first, second):
        return jnp.where(self.even_y, second, first)

    def after_y(self, first, second):
        return jnp.where(self.even_y, first, second)


def along_x(matrix, tiles, sign):
    even = [tiles[a] + tiles[7 - a] for a in range(4)]
    odd = [tiles[a] - tiles[7 - a] for a in range(4)]
    out = [None] * 8
    for i in range(4):
        plus, minus = None, None
        for a in range(4):
            p = float(0.5 * (matrix[i, a] + matrix[i, 7 - a])) * even[a]
            m = float(0.5 * (matrix[i, a] - matrix[i, 7 - a])) * odd[a]
            plus = p if plus is None else plus + p
            minus = m if minus is None else minus + m
        out[i] = plus + minus
        out[7 - i] = minus - plus if sign < 0 else plus - minus
    return out


def along_y(ctab, base, tile):
    acc = ctab[base] * tile
    for s in range(1, 8):
        acc = acc + ctab[base + s] * pltpu.roll(tile, s, 0)
    return acc


def exact_dot(rows, matrix):
    return jnp.dot(
        rows, matrix, precision=lax.Precision.HIGHEST, preferred_element_type=jnp.float32
    )


def along_z(rows, matrix):
    high = rows.astype(jnp.bfloat16)
    low = (rows - high.astype(jnp.float32)).astype(jnp.bfloat16)
    both = jnp.dot(
        jnp.concatenate([high, low], axis=1), matrix, preferred_element_type=jnp.float32
    )
    return both[:, :LANES] + both[:, LANES:]


def total(tile):
    return jnp.sum(jnp.sum(tile, axis=0, keepdims=True), axis=1, keepdims=True)


def store_y_faces(place, field, first_out, second_out, lead, at):
    for ex in range(2):
        for a in range(8):
            low = field[lead + (ex, a, 0, pl.ds(0, 1), slice(None))]
            high = field[lead + (ex, a, 1, pl.ds(7, 1), slice(None))]
            row = at + ex * 8 + a
            first_out[pl.ds(row, 1), :] = place.after_y(high, low)
            second_out[pl.ds(row, 1), :] = place.after_y(low, high)


def join_own(place, tiles):
    for ex in range(2):
        for a in range(8):
            tiles[ex][a] = list(place.join_y(*tiles[ex][a]))
    for ey in range(2):
        both = tiles[0][7][ey] + tiles[1][0][ey]
        tiles[0][7][ey] = both
        tiles[1][0][ey] = both


def weight_of(node):
    edge = jnp.minimum(node, 7 - node)
    value = jnp.where(edge == 2, float(WEIGHTS[2]), float(WEIGHTS[3]))
    return jnp.where(
        edge == 0, float(WEIGHTS[0]), jnp.where(edge == 1, float(WEIGHTS[1]), value)
    )


def mass_kernel(fields, out, xf, first, second):
    place = Place()
    weight = weight_of(place.row) * weight_of(place.lane % NODES)
    for ch in range(4):
        tiles = [
            [
                [
                    place.join_z(fields[ch, ex, a, ey] * (float(WEIGHTS[a]) * weight))
                    for ey in range(2)
                ]
                for a in range(8)
            ]
            for ex in range(2)
        ]
        join_own(place, tiles)
        for ex in range(2):
            for a in range(8):
                for ey in range(2):
                    out[ch, ex, a, ey] = tiles[ex][a][ey]
        for ey in range(2):
            xf[0, ch, ey] = tiles[0][0][ey]
            xf[1, ch, ey] = tiles[1][7][ey]
        store_y_faces(place, out, first, second, (ch,), ch * 16)


def turn_faces(place, xf, y_first, y_second, first, second):
    for ch in range(4):
        sides = []
        for side in range(2):
            row = pl.ds(ch * 16 + 15 * side, 1)
            got_a, got_b = y_first[row, :], y_second[row, :]
            low = xf[side, ch, 0] + jnp.where(place.row == 0, place.before_y(got_a, got_b), 0.0)
            high = xf[side, ch, 1] + jnp.where(place.row == 7, place.after_y(got_a, got_b), 0.0)
            sides.append((low, high))
        for ey in range(2):
            rows = pl.ds(ch * 16 + ey * 8, 8)
            first[rows, :] = place.after_x(sides[1][ey], sides[0][ey])
            second[rows, :] = place.after_x(sides[0][ey], sides[1][ey])


def turn_faces_kernel(xf, y_first, y_second, first, second):
    turn_faces(Place(), xf, y_first, y_second, first, second)


def turn_edges(place, inner_x, y_first, y_second, first, second, at, edge, inner_y):
    sides = []
    for side in range(2):
        row = pl.ds(edge + side, 1)
        got_a, got_b = y_first[row, :], y_second[row, :]
        low = inner_x[side, 0] + jnp.where(place.row == 0, place.before_y(got_a, got_b), 0.0)
        high = inner_x[side, 1] + jnp.where(place.row == 7, place.after_y(got_a, got_b), 0.0)
        sides.append((low, high))
    for ey in range(2):
        rows = pl.ds(at + ey * 8, 8)
        first[rows, :] = place.after_x(sides[1][ey], sides[0][ey])
        second[rows, :] = place.after_x(sides[0][ey], sides[1][ey])
    for k, pick in enumerate((place.before_y, place.after_y)):
        sides = []
        for side in range(2):
            row = pl.ds(inner_y + 15 * side, 1)
            sides.append(pick(y_first[row, :], y_second[row, :]))
        row = pl.ds(edge + k, 1)
        first[row, :] = place.after_x(sides[1], sides[0])
        second[row, :] = place.after_x(sides[0], sides[1])


STEP_U, STEP_V, STEP_EDGE, STEP_PACK = 64, 64, 80, 88


def turn_step_kernel(pack_rows, xf, inner_x, pack, y_first, y_second, first, second):
    place = Place()
    turn_faces(place, xf, y_first, y_second, first, second)
    first[pl.ds(STEP_EDGE, 8), :] = jnp.zeros(TILE, jnp.float32)
    second[pl.ds(STEP_EDGE, 8), :] = jnp.zeros(TILE, jnp.float32)
    turn_edges(place, inner_x, y_first, y_second, first, second, STEP_U, STEP_EDGE, STEP_V)
    came = pl.ds(STEP_PACK, pack_rows)
    parts = (
        place.before_y(y_first[came, :], y_second[came, :]),
        pack[...],
        place.after_y(y_first[came, :], y_second[came, :]),
    )
    for k in range(3):
        rows = pl.ds(STEP_PACK + k * pack_rows, pack_rows)
        first[rows, :] = parts[k]
        second[rows, :] = parts[k]


def setup_kernel(
    pack_rows, blocks, pack, y_first, y_second, x_first, x_second, ctab, inv_diag, kap, grp, coarse
):
    place = Place()
    came = pl.ds(STEP_PACK, pack_rows)
    packs = [[None] * 3 for _ in range(3)]
    packs[1][0] = place.before_y(y_first[came, :], y_second[came, :])
    packs[1][1] = pack[...]
    packs[1][2] = place.after_y(y_first[came, :], y_second[came, :])
    for k in range(3):
        rows = pl.ds(STEP_PACK + k * pack_rows, pack_rows)
        packs[0][k] = place.before_x(x_first[rows, :], x_second[rows, :])
        packs[2][k] = place.after_x(x_first[rows, :], x_second[rows, :])
    for dx in range(3):
        for dy in range(3):
            at = (dx * 3 + dy) * NCD * blocks
            coarse[pl.ds(at, NCD * blocks), :] = packs[dx][dy][8 : 8 + NCD * blocks]
    there_x = [jnp.where(place.prev_x, 1.0, 0.0), 1.0, jnp.where(place.next_x, 1.0, 0.0)]
    there_y = [jnp.where(place.prev_y, 1.0, 0.0), 1.0, jnp.where(place.next_y, 1.0, 0.0)]

    def element_row(base, u, v):
        row = base + (u % 2) * 2 + v % 2
        return packs[u // 2][v // 2][row : row + 1]

    for x in range(4):
        for y in range(4):
            kap[pl.ds(x * 4 + y, 1), :] = element_row(0, x + 1, y + 1)
            grp[pl.ds(x * 4 + y, 1), :] = element_row(4, x + 1, y + 1)
    kappa = [
        [
            place.join_z(jnp.broadcast_to(element_row(0, u + 1, v + 1), TILE))
            for v in range(4)
        ]
        for u in range(4)
    ]
    count_z = 1.0 + jnp.where(place.low_z | place.high_z, 1.0, 0.0)
    weight = ctab[T_W]
    line = ctab[T_LINE]

    def pick(values, ey):
        low = values[ey] + values[ey + 1]
        high = values[ey + 1] + values[ey + 2]
        return jnp.where(place.row == 0, low, jnp.where(place.row == 7, high, values[ey + 1]))

    for ex in range(2):
        for kind in range(3):
            us = {0: (ex, ex + 1), 1: (ex + 1,), 2: (ex + 1, ex + 2)}[kind]
            sums, counts = [], []
            for v in range(4):
                acc, num = None, 0.0
                for u in us:
                    acc = kappa[u][v] if acc is None else acc + kappa[u][v]
                    num = num + there_x[(u + 1) // 2]
                sums.append(acc)
                counts.append(num * there_y[(v + 1) // 2])
            for ey in range(2):
                kappa_sum = pick(sums, ey)
                mult = pick(counts, ey) * count_z
                for a in {0: (0,), 1: range(1, 7), 2: (7,)}[kind]:
                    diag = (float(LINE[a]) + line) * kappa_sum + sigma_p * mult
                    inv_diag[ex, a, ey] = 1.0 / (diag * (float(WEIGHTS[a]) * weight))


def got_face_sum(place, tile, ch, ex, a, ey, y_first, y_second, x_first, x_second):
    row = pl.ds(ch * 16 + ex * 8 + a, 1)
    got_a, got_b = y_first[row, :], y_second[row, :]
    if ey == 0:
        tile = tile + jnp.where(place.row == 0, place.before_y(got_a, got_b), 0.0)
    else:
        tile = tile + jnp.where(place.row == 7, place.after_y(got_a, got_b), 0.0)
    rows = pl.ds(pl.multiple_of(ch * 16 + ey * 8, 8), 8)
    if ex == 0 and a == 0:
        tile = tile + place.before_x(x_first[rows, :], x_second[rows, :])
    if ex == 1 and a == 7:
        tile = tile + place.after_x(x_first[rows, :], x_second[rows, :])
    return tile


def pack_kernel(kappa, group, coarse, pack, facts):
    place = Place()
    pack[...] = jnp.zeros(pack.shape, jnp.float32)
    facts[...] = jnp.zeros(facts.shape, jnp.float32)
    elems = kappa.shape[2]
    to = lax.broadcasted_iota(jnp.int32, (elems, LANES), 1)
    element = lax.broadcasted_iota(jnp.int32, (elems, LANES), 0)
    spread = (to // NODES == element).astype(jnp.float32)
    blocks = coarse.shape[1] // LANES
    for ex in range(2):
        numbers = group[ex].astype(jnp.float32)
        pack[pl.ds(2 * ex, 2), :] = exact_dot(kappa[ex], spread)
        pack[pl.ds(4 + 2 * ex, 2), :] = exact_dot(numbers, spread)
        row = jnp.zeros((1, LANES), jnp.float32)
        for ey in range(2):
            at = (2 * place.iy + ey) * elems
            spot = (to == at + element).astype(jnp.float32)
            after = (to == (at + 2 * elems) % LANES + element).astype(jnp.float32)
            row = row + exact_dot(kappa[ex, pl.ds(ey, 1), :], spot)
            row = row + exact_dot(numbers[ey : ey + 1], after)
        facts[pl.ds(2 + ex, 1), :] = row
    for c in range(NCD):
        for j in range(blocks):
            line = coarse[pl.ds(c, 1), pl.ds(j * LANES, LANES)]
            pack[pl.ds(8 + c * blocks + j, 1), :] = line
        facts[pl.ds(4 + c, 1), :] = coarse[pl.ds(c, 1), pl.ds(0, LANES)]


def rhs_kernel(
    pack_rows,
    summed,
    visc,
    pack,
    y_first,
    y_second,
    x_first,
    x_second,
    ctab,
    zmat,
    share,
    xf,
    inner_x,
    first,
    second,
    start,
    rhs,
    grad_z,
    flux_z,
):
    place = Place()
    weight = ctab[T_W]
    inv_mass = [1.0 / (weight * place.mult_tile(ey)) for ey in range(2)]

    def begin(ch, carry):
        for ex in range(2):
            for a in range(8):
                for ey in range(2):
                    tile = got_face_sum(
                        place, summed[ch, ex, a, ey], ch, ex, a, ey,
                        y_first, y_second, x_first, x_second,
                    )
                    scale = place.inv_x(ex, a) * float(1.0 / WEIGHTS[a])
                    start[ch, ex, a, ey] = tile * (inv_mass[ey] * scale)
        return carry

    lax.fori_loop(0, 4, begin, 0)
    grad_z[...] = along_z(start[...].reshape(1024, LANES), zmat[0]).reshape(grad_z.shape)

    def column(index, carry):
        ch, ex, ey = index // 4, index // 2 % 2, index % 2
        coef = jnp.where(ch == 3, 1.0 / prandtl, 1.0)
        field = [start[ch, ex, a, ey] for a in range(8)]
        grad_x = along_x(DERIV, field, -1)
        flux_x, parts = [], []
        for a in range(8):
            grad_y = along_y(ctab, T_D, field[a])
            slope = grad_z[ch, ex, a, ey]
            node = float(WEIGHTS[a]) * weight
            advect = (
                start[0, ex, a, ey] * grad_x[a]
                + start[1, ex, a, ey] * grad_y
                + start[2, ex, a, ey] * slope
            )
            nu = visc[ex, a, ey] * node * coef
            flux_x.append(nu * grad_x[a])
            flux_z[ch, ex, a, ey] = nu * slope
            parts.append(node * advect + along_y(ctab, T_DT, nu * grad_y))
        back = along_x(DERIV.T, flux_x, -1)
        for a in range(8):
            rhs[ch, ex, a, ey] = parts[a] + back[a]
        return carry

    lax.fori_loop(0, 16, column, 0)
    grad_z[...] = along_z(flux_z[...].reshape(1024, LANES), zmat[1]).reshape(grad_z.shape)

    def finish(ch, carry):
        tiles = [
            [
                [
                    place.join_z(-(rhs[ch, ex, a, ey] + grad_z[ch, ex, a, ey]))
                    for ey in range(2)
                ]
                for a in range(8)
            ]
            for ex in range(2)
        ]
        join_own(place, tiles)
        for ex in range(2):
            for a in range(8):
                scale = place.inv_x(ex, a) * float(dt_step / WEIGHTS[a])
                for ey in range(2):
                    part = start[ch, ex, a, ey] * (place.share_y(ey) * place.share_x(ex, a))
                    share[ch, ex, a, ey] = part + tiles[ex][a][ey] * (inv_mass[ey] * scale)
        return carry

    lax.fori_loop(0, 4, finish, 0)
    for ch in range(4):
        store_y_faces(place, share, first, second, (ch,), ch * 16)
        for ey in range(2):
            xf[0, ch, ey] = share[ch, 0, 0, ey]
            xf[1, ch, ey] = share[ch, 1, 7, ey]
    first[pl.ds(STEP_EDGE, 8), :] = jnp.zeros(TILE, jnp.float32)
    second[pl.ds(STEP_EDGE, 8), :] = jnp.zeros(TILE, jnp.float32)

    def column_of(ex, ey):
        return [share[0, ex, a, ey] for a in range(8)]

    def tile_of(ex, a, ey):
        return share[1, ex, a, ey]

    store_inner(
        place, DERIV, ctab[T_BOTTOM], ctab[T_TOP], column_of, tile_of, inner_x, first, second,
        STEP_V, STEP_EDGE,
    )
    first[pl.ds(STEP_PACK, pack_rows), :] = pack[...]
    second[pl.ds(STEP_PACK, pack_rows), :] = pack[...]


def store_inner(
    place, matrix, bottom, top, column_of, tile_of, inner_x, first, second, at, edge
):
    for ey in range(2):
        low, high = column_of(0, ey), column_of(1, ey)
        below = float(matrix[0, 1]) * low[1]
        above = float(matrix[7, 0]) * high[0]
        for k in range(2, 8):
            below = below + float(matrix[0, k]) * low[k]
            above = above + float(matrix[7, k - 1]) * high[k - 1]
        inner_x[0, ey] = below
        inner_x[1, ey] = above
    for side in range(2):
        low = inner_x[side, 0, pl.ds(0, 1), :]
        high = inner_x[side, 1, pl.ds(7, 1), :]
        first[pl.ds(edge + side, 1), :] = place.after_y(high, low)
        second[pl.ds(edge + side, 1), :] = place.after_y(low, high)
    for ex in range(2):
        for a in range(8):
            low = jnp.sum(bottom * tile_of(ex, a, 0), axis=0, keepdims=True)
            high = jnp.sum(top * tile_of(ex, a, 1), axis=0, keepdims=True)
            row = pl.ds(at + ex * 8 + a, 1)
            first[row, :] = place.after_y(high, low)
            second[row, :] = place.after_y(low, high)


def advance_kernel(
    share,
    y_first,
    y_second,
    x_first,
    x_second,
    inv_diag,
    kap,
    grp,
    ctab,
    zmat,
    fields_new,
    resid,
    own,
    msg,
    grad_z,
    scaled,
):
    place = Place()
    weight = ctab[T_W]

    def before(row, count=8):
        rows = pl.ds(row, count)
        return place.before_x(x_first[rows, :], x_second[rows, :])

    def after(row, count=8):
        rows = pl.ds(row, count)
        return place.after_x(x_first[rows, :], x_second[rows, :])

    def step(ch, carry):
        for ex in range(2):
            for a in range(8):
                for ey in range(2):
                    fields_new[ch, ex, a, ey] = got_face_sum(
                        place, share[ch, ex, a, ey], ch, ex, a, ey,
                        y_first, y_second, x_first, x_second,
                    )
        return carry

    lax.fori_loop(0, 4, step, 0)
    grad_z[...] = along_z(fields_new[2].reshape(256, LANES), zmat[0]).reshape(grad_z.shape)
    slope = [[None, None], [None, None]]
    for ey in range(2):
        for ex in range(2):
            slope[ex][ey] = along_x(DERIV, [fields_new[0, ex, a, ey] for a in range(8)], -1)
        mid = 0.5 * (slope[0][ey][7] + slope[1][ey][0])
        slope[0][ey][7] = mid
        slope[1][ey][0] = mid
        low, high = slope[0][ey][0], slope[1][ey][7]
        inner_low = low - float(DERIV[0, 0]) * fields_new[0, 0, 0, ey] + before(STEP_U + ey * 8)
        inner_high = high - float(DERIV[7, 7]) * fields_new[0, 1, 7, ey] + after(STEP_U + ey * 8)
        slope[0][ey][0] = jnp.where(place.prev_x, 0.5 * inner_low, low)
        slope[1][ey][7] = jnp.where(place.next_x, 0.5 * inner_high, high)
    sums = [[jnp.zeros(TILE, jnp.float32) for _ in range(2)] for _ in range(2)]
    inv_mult = [1.0 / place.mult_tile(ey) for ey in range(2)]
    inv_y = [place.inv_y(ey) for ey in range(2)]
    inv_z = place.inv_z()
    mass = [weight * place.mult_tile(ey) for ey in range(2)]
    there_low = jnp.where(place.prev_y, 1.0, 0.0)
    there_high = jnp.where(place.next_y, 1.0, 0.0)
    for ex in range(2):
        for a in range(8):
            flow = [fields_new[1, ex, a, ey] for ey in range(2)]
            below, above = inner_along_y(
                place, y_first, y_second, before, after, ex, a, STEP_V, STEP_EDGE
            )
            below = (below - float(DERIV[0, 0]) * flow[0]) * there_low
            above = (above - float(DERIV[7, 7]) * flow[1]) * there_high
            grad_y = list(place.join_y(*[along_y(ctab, T_D, tile) for tile in flow]))
            grad_y[0] = grad_y[0] + jnp.where(place.row == 0, below, 0.0)
            grad_y[1] = grad_y[1] + jnp.where(place.row == 7, above, 0.0)
            for ey in range(2):
                div = (
                    slope[ex][ey][a]
                    + grad_y[ey] * inv_y[ey]
                    + place.join_z(grad_z[ex, a, ey]) * inv_z
                )
                value = div * (mass[ey] * (place.mult_x(ex, a) * float(-WEIGHTS[a])))
                resid[ex, a, ey] = value
                scaled[ex, a, ey] = value * inv_diag[ex, a, ey] * float(1.0 / THETA)
                sums[ex][ey] = sums[ex][ey] + value * (inv_mult[ey] * place.inv_x(ex, a))
    grad_z[...] = along_z(scaled[...].reshape(256, LANES), zmat[2]).reshape(grad_z.shape)
    tiles = [[[None, None] for _ in range(8)] for _ in range(2)]
    for ex in range(2):
        for ey in range(2):
            images = own_operator(ctab, kap, scaled, grad_z, ex, ey)[1]
            for a in range(8):
                tiles[ex][a][ey] = place.join_z(images[a])
    join_own(place, tiles)
    for ex in range(2):
        for a in range(8):
            for ey in range(2):
                own[ex, a, ey] = tiles[ex][a][ey]
    row = message(place, restricted(place, sums, grp), [])
    blank = jnp.where(place.row == 0, jnp.broadcast_to(row, TILE), 0.0)
    zero = jnp.zeros(TILE, jnp.float32)

    def clear(i, carry):
        msg[i, pl.ds(0, 8), :] = zero
        msg[i, pl.ds(8, 8), :] = blank
        return carry

    lax.fori_loop(0, msg.shape[0], clear, 0)
    for dx, dy, there in neighbours(place):

        @pl.when(there)
        def _():
            to = (place.ix + dx) * place.ny + place.iy + dy
            ex, a = (0, 0) if dx < 0 else (1, 7)
            ey, b = (0, 0) if dy < 0 else (1, 7)
            if dy == 0:
                msg[to, pl.ds(0, 8), :] = own[ex, a, 0]
                msg[to, pl.ds(9, 7), :] = own[ex, a, 1, pl.ds(1, 7), :]
            elif dx == 0:
                for r in range(16):
                    if r != 8:
                        msg[to, pl.ds(r, 1), :] = own[r // 8, r % 8, ey, pl.ds(b, 1), :]
            else:
                msg[to, pl.ds(0, 1), :] = own[ex, a, ey, pl.ds(b, 1), :]


def inner_along_y(place, y_first, y_second, before, after, ex, a, at, edge):
    row = pl.ds(at + ex * 8 + a, 1)
    got_a, got_b = y_first[row, :], y_second[row, :]
    below, above = place.before_y(got_a, got_b), place.after_y(got_a, got_b)
    if (ex, a) == (0, 0):
        below = below + before(edge, 1)
        above = above + before(edge + 1, 1)
    if (ex, a) == (1, 7):
        below = below + after(edge, 1)
        above = above + after(edge + 1, 1)
    return below, above


def neighbours(place):
    along = ((-1, place.prev_x), (0, None), (1, place.next_x))
    across = ((-1, place.prev_y), (0, None), (1, place.next_y))
    out = []
    for dx, has_x in along:
        for dy, has_y in across:
            if dx == 0 and dy == 0:
                continue
            there = has_y if has_x is None else (has_x if has_y is None else has_x & has_y)
            out.append((dx, dy, there))
    return out


SMOOTH_X, SMOOTH_Y, SMOOTH_EDGE, SMOOTH_ROWS = 16, 16, 32, 40


def turn_smooth_kernel(own, inner_x, y_first, y_second, first, second):
    place = Place()
    sides = []
    for side, (ex, a) in enumerate(((0, 0), (1, 7))):
        row = pl.ds(15 * side, 1)
        got_a, got_b = y_first[row, :], y_second[row, :]
        low = own[ex, a, 0] + jnp.where(place.row == 0, place.before_y(got_a, got_b), 0.0)
        high = own[ex, a, 1] + jnp.where(place.row == 7, place.after_y(got_a, got_b), 0.0)
        sides.append((low, high))
    for ey in range(2):
        rows = pl.ds(ey * 8, 8)
        first[rows, :] = place.after_x(sides[1][ey], sides[0][ey])
        second[rows, :] = place.after_x(sides[0][ey], sides[1][ey])
    first[pl.ds(SMOOTH_EDGE, 8), :] = jnp.zeros(TILE, jnp.float32)
    second[pl.ds(SMOOTH_EDGE, 8), :] = jnp.zeros(TILE, jnp.float32)
    turn_edges(
        place, inner_x, y_first, y_second, first, second, SMOOTH_X, SMOOTH_EDGE, SMOOTH_Y
    )


def restricted(place, sums, grp):
    values = []
    for c in range(NCD):
        acc = jnp.zeros(TILE, jnp.float32)
        for ex in range(2):
            for ey in range(2):
                group = grp[pl.ds((ex + 1) * 4 + ey + 1, 1), :]
                acc = acc + jnp.where(group == float(c), sums[ex][ey], 0.0)
        values.append(total(acc))
    return values


def message(place, own_values, scalars):
    lane = lax.broadcasted_iota(jnp.int32, (1, LANES), 1)
    spot = (place.ix * place.ny + place.iy) % (LANES // NCD)
    after = (spot + 1) % (LANES // NCD)
    row = jnp.zeros((1, LANES), jnp.float32)
    for c, value in enumerate(own_values):
        row = row + jnp.where(lane == spot * NCD + c, value, 0.0)
    for c, value in enumerate(scalars):
        if value is None:
            continue
        row = row + jnp.where(lane == after * NCD + c, value, 0.0)
    return row


def send_to_all(msg, row):
    def send(i, carry):
        msg[i] = row
        return carry

    lax.fori_loop(0, msg.shape[0], send, 0, unroll=msg.shape[0] <= 64)


def smooth_kernel(
    own,
    y_first,
    y_second,
    x_first,
    x_second,
    inv_diag,
    kap,
    grp,
    extra,
    facts,
    ctab,
    zmat,
    image,
    smoothed,
    msg,
    scaled,
    slope_z,
):
    place = Place()
    weight = ctab[T_W]
    corner = float(SCALED[0, 0])

    def before(row, count=8):
        rows = pl.ds(row, count)
        return place.before_x(x_first[rows, :], x_second[rows, :])

    def after(row, count=8):
        rows = pl.ds(row, count)
        return place.after_x(x_first[rows, :], x_second[rows, :])

    for ex in range(2):
        for a in range(8):
            for ey in range(2):
                tile = got_face_sum(
                    place, own[ex, a, ey], 0, ex, a, ey, y_first, y_second, x_first, x_second
                )
                image[ex, a, ey] = tile
                scaled[ex, a, ey] = tile * inv_diag[ex, a, ey] * float(1.0 / THETA)
    slope_z[...] = along_z(scaled[...].reshape(256, LANES), zmat[2]).reshape(slope_z.shape)
    there_x = (jnp.where(place.prev_x, 1.0, 0.0), jnp.where(place.next_x, 1.0, 0.0))
    there_y = (jnp.where(place.prev_y, 1.0, 0.0), jnp.where(place.next_y, 1.0, 0.0))

    def kappa_of(x, y):
        return kap[pl.ds(x * 4 + y, 1), :]

    tiles = [[[None, None] for _ in range(8)] for _ in range(2)]
    for ex in range(2):
        for ey in range(2):
            values = [scaled[ex, a, ey] for a in range(8)]
            slopes = along_x(SCALED, values, 1)
            y_next = 0 if ey == 0 else 3
            edge_row = place.row == (0 if ey == 0 else 7)
            for a in range(8):
                value = values[a]
                slope_y = along_y(ctab, T_K, value)
                flat = slope_z[ex, a, ey]
                same = slopes[a] + slope_y + flat
                acc = kappa_of(ex + 1, ey + 1) * same + sigma_p * value
                inner = inner_along_y(
                    place, y_first, y_second, before, after, ex, a, SMOOTH_Y, SMOOTH_EDGE
                )[ey]
                turned_y = inner + corner * value
                beyond = kappa_of(ex + 1, y_next) * (slopes[a] + turned_y + flat)
                beyond = (beyond + sigma_p * value) * there_y[ey]
                if (ex, a) in ((0, 0), (1, 7)):
                    x_next = 0 if ex == 0 else 3
                    get = before if ex == 0 else after
                    turned_x = get(SMOOTH_X + ey * 8) + corner * value
                    side = kappa_of(x_next, ey + 1) * (turned_x + slope_y + flat)
                    acc = acc + (side + sigma_p * value) * there_x[ex]
                    far = kappa_of(x_next, y_next) * (turned_x + turned_y + flat)
                    beyond = beyond + (far + sigma_p * value) * (there_x[ex] * there_y[ey])
                acc = acc + jnp.where(edge_row, beyond, 0.0)
                tiles[ex][a][ey] = place.join_z(acc * (float(WEIGHTS[a]) * weight))
    join_own(place, tiles)
    inv_mult = [1.0 / place.mult_tile(ey) for ey in range(2)]
    sums = [[jnp.zeros(TILE, jnp.float32) for _ in range(2)] for _ in range(2)]
    square = jnp.zeros(TILE, jnp.float32)
    for ex in range(2):
        for a in range(8):
            for ey in range(2):
                value = image[ex, a, ey]
                defect = (value - tiles[ex][a][ey]) * inv_diag[ex, a, ey]
                update = scaled[ex, a, ey]
                result = (
                    float(1.0 + RHO_NEXT * RHO) * update + float(2.0 * RHO_NEXT / DELTA) * defect
                )
                smoothed[ex, a, ey] = result
                weighed = value * (inv_mult[ey] * place.inv_x(ex, a))
                sums[ex][ey] = sums[ex][ey] + weighed
                square = square + weighed * result
    own_sums = restricted(place, sums, grp)
    if msg.shape[1] == 1:
        send_to_all(msg, message(place, own_sums, []) + extra[...])
        return
    slope_z[...] = along_z(smoothed[...].reshape(256, LANES), zmat[2]).reshape(slope_z.shape)
    energy = jnp.zeros(TILE, jnp.float32)
    for ex in range(2):
        for ey in range(2):
            values, images = own_operator(ctab, kap, smoothed, slope_z, ex, ey)
            for a in range(8):
                energy = energy + values[a] * images[a]
                tiles[ex][a][ey] = place.join_z(images[a])
    join_own(place, tiles)
    row = message(place, own_sums, [None, None, total(square), total(energy)]) + extra[...]
    dual = restricted_around(place, tiles, inv_mult, grp)
    out = facts[...]
    out = out + jnp.where(place.row == 0, jnp.broadcast_to(row, TILE), 0.0)
    out = out + jnp.where(place.row == 1, jnp.broadcast_to(dual, TILE), 0.0)
    send_to_all(msg, out)


def restricted_around(place, tiles, inv_mult, grp):
    lane = lax.broadcasted_iota(jnp.int32, (1, LANES), 1)
    weighed = [
        [[tiles[ex][a][ey] * (inv_mult[ey] * place.inv_x(ex, a)) for ey in range(2)] for a in range(8)]
        for ex in range(2)
    ]

    def rows_of(tile, y):
        if y == 0:
            return jnp.where(place.row == 0, tile[0], 0.0)
        if y == 3:
            return jnp.where(place.row == 7, tile[1], 0.0)
        return tile[y - 1]

    there_x = (place.prev_x, None, None, place.next_x)
    there_y = (place.prev_y, None, None, place.next_y)
    by_device = [
        [[jnp.zeros(TILE, jnp.float32) for _ in range(NCD)] for _ in range(3)] for _ in range(3)
    ]
    for x in range(4):
        for y in range(4):
            if x == 0:
                acc = rows_of(weighed[0][0], y)
            elif x == 3:
                acc = rows_of(weighed[1][7], y)
            else:
                acc = rows_of(weighed[x - 1][0], y)
                for a in range(1, 8):
                    acc = acc + rows_of(weighed[x - 1][a], y)
            for there in (there_x[x], there_y[y]):
                if there is not None:
                    acc = jnp.where(there, acc, 0.0)
            group = grp[pl.ds(x * 4 + y, 1), :]
            device = by_device[(x + 1) // 2][(y + 1) // 2]
            for c in range(NCD):
                device[c] = device[c] + jnp.where(group == float(c), acc, 0.0)
    row = jnp.zeros((1, LANES), jnp.float32)
    for dx in range(3):
        for dy in range(3):
            at = ((place.ix + dx - 1) * place.ny + place.iy + dy - 1) * NCD
            for c in range(NCD):
                row = row + jnp.where(lane == at + c, total(by_device[dx][dy][c]), 0.0)
    return row


def coarse_part(place, blocks, got, coarse, grp, at=0):
    lane = lax.broadcasted_iota(jnp.int32, (1, LANES), 1)
    values = [jnp.zeros((1, LANES), jnp.float32) for _ in range(blocks)]
    per = LANES // NCD
    for j in range(blocks):

        def gather(i, acc, j=j):
            return jnp.where(lane // NCD == i, got[j * per + i, pl.ds(at, 1), :], acc)

        values[j] = lax.fori_loop(0, per, gather, values[j], unroll=blocks == 1)

    def solved(dx, dy, c):
        acc = None
        for j in range(blocks):
            term = coarse[pl.ds(((dx * 3 + dy) * NCD + c) * blocks + j, 1), :] * values[j]
            acc = term if acc is None else acc + term
        return jnp.sum(acc, axis=1, keepdims=True)

    return prolonged(place, solved, grp)


def prolonged(place, solved, grp):
    device = [[[solved(dx, dy, c) for c in range(NCD)] for dy in range(3)] for dx in range(3)]
    inv_z = jnp.where(place.low_z | place.high_z, 0.5, 1.0)
    rows = []
    for x in range(4):
        line = []
        for y in range(4):
            group = grp[pl.ds(x * 4 + y, 1), :]
            acc = jnp.zeros((1, LANES), jnp.float32)
            for c in range(NCD):
                acc = acc + jnp.where(
                    group == float(c), device[(x + 1) // 2][(y + 1) // 2][c], 0.0
                )
            line.append(place.join_z(jnp.broadcast_to(acc, TILE)) * inv_z)
        rows.append(line)
    low_y = jnp.where(place.prev_y, 0.5, 1.0)
    high_y = jnp.where(place.next_y, 0.5, 1.0)

    def tile(ex, kind, ey):
        if kind == 1:
            vals = [rows[ex + 1][y] for y in range(4)]
        elif kind == 0:
            scale = place.inv_x(ex, 0)
            vals = [(rows[ex][y] + rows[ex + 1][y]) * scale for y in range(4)]
        else:
            scale = place.inv_x(ex, 7)
            vals = [(rows[ex + 1][y] + rows[ex + 2][y]) * scale for y in range(4)]
        mid = vals[ey + 1]
        low = (vals[ey] + mid) * (low_y if ey == 0 else 0.5)
        high = (mid + vals[ey + 2]) * (high_y if ey == 1 else 0.5)
        return jnp.where(place.row == 0, low, jnp.where(place.row == 7, high, mid))

    return tile


def kind_of(a):
    return 0 if a == 0 else (2 if a == 7 else 1)


def own_operator(ctab, kap, field, slope_z, ex, ey):
    weight = ctab[T_W]
    tiles = [field[ex, a, ey] for a in range(8)]
    slopes = along_x(SCALED, tiles, 1)
    kappa = kap[pl.ds((ex + 1) * 4 + ey + 1, 1), :]
    out = []
    for a in range(8):
        stiff = slopes[a] + along_y(ctab, T_K, tiles[a]) + slope_z[ex, a, ey]
        out.append((kappa * stiff + sigma_p * tiles[a]) * (float(WEIGHTS[a]) * weight))
    return tiles, out


def first_direction_kernel(
    blocks,
    got,
    coarse,
    grp,
    kap,
    inv_diag,
    resid,
    own,
    ctab,
    zmat,
    direction,
    out,
    inner_x,
    first,
    second,
    extra,
    slope_z,
    image,
):
    place = Place()
    inv_mult = [1.0 / place.mult_tile(ey) for ey in range(2)]
    part = coarse_part(place, blocks, got, coarse, grp, 8)
    image[...] = own[...]
    for dx, dy, there in neighbours(place):

        @pl.when(there)
        def _():
            frm = (place.ix + dx) * place.ny + place.iy + dy
            ex, a = (0, 0) if dx < 0 else (1, 7)
            ey, b = (0, 0) if dy < 0 else (1, 7)
            edge = place.row == b
            if dy == 0:
                low = got[frm, pl.ds(0, 8), :]
                high = jnp.where(
                    place.row == 0, pltpu.roll(low, 1, 0), got[frm, pl.ds(8, 8), :]
                )
                image[ex, a, 0] = image[ex, a, 0] + low
                image[ex, a, 1] = image[ex, a, 1] + high
            elif dx == 0:
                for r in range(16):
                    line = got[frm, pl.ds(7 if r == 8 else r, 1), :]
                    tile = image[r // 8, r % 8, ey]
                    image[r // 8, r % 8, ey] = tile + jnp.where(edge, line, 0.0)
            else:
                line = got[frm, pl.ds(0, 1), :]
                image[ex, a, ey] = image[ex, a, ey] + jnp.where(edge, line, 0.0)

    energy = jnp.zeros(TILE, jnp.float32)
    for ex in range(2):
        for ey in range(2):
            kinds = [part(ex, kind, ey) for kind in range(3)]
            for a in range(8):
                known = resid[ex, a, ey]
                inverse = inv_diag[ex, a, ey]
                defect = (known - image[ex, a, ey]) * inverse
                value = (
                    float((1.0 + RHO_NEXT * RHO) / THETA) * (known * inverse)
                    + float(2.0 * RHO_NEXT / DELTA) * defect
                    + kinds[kind_of(a)]
                )
                direction[ex, a, ey] = value
                scale = place.inv_x(ex, a)
                energy = energy + value * known * (inv_mult[ey] * scale)
    slope_z[...] = along_z(direction[...].reshape(256, LANES), zmat[2]).reshape(slope_z.shape)
    curvature = jnp.zeros(TILE, jnp.float32)
    tiles = [[[None, None] for _ in range(8)] for _ in range(2)]
    for ex in range(2):
        for ey in range(2):
            values, images = own_operator(ctab, kap, direction, slope_z, ex, ey)
            for a in range(8):
                curvature = curvature + values[a] * images[a]
                tiles[ex][a][ey] = place.join_z(images[a])
    join_own(place, tiles)
    for ex in range(2):
        for a in range(8):
            for ey in range(2):
                out[ex, a, ey] = tiles[ex][a][ey]
    store_y_faces(place, out, first, second, (), 0)
    first[pl.ds(SMOOTH_EDGE, 8), :] = jnp.zeros(TILE, jnp.float32)
    second[pl.ds(SMOOTH_EDGE, 8), :] = jnp.zeros(TILE, jnp.float32)

    def tile_of(ex, a, ey):
        return tiles[ex][a][ey] * inv_diag[ex, a, ey] * float(1.0 / THETA)

    def column_of(ex, ey):
        return [tile_of(ex, a, ey) for a in range(8)]

    store_inner(
        place, SCALED, ctab[T_KBOTTOM], ctab[T_KTOP], column_of, tile_of, inner_x, first, second,
        SMOOTH_Y, SMOOTH_EDGE,
    )
    extra[...] = message(place, [], [total(energy), total(curvature)])


def gathered_scalars(got, count):
    lane = lax.broadcasted_iota(jnp.int32, (1, LANES), 1)
    per = LANES // NCD
    sums = []
    for c in range(count):
        acc = jnp.zeros((1, LANES), jnp.float32)

        def gather(i, acc, c=c):
            return acc + jnp.where(lane == ((i + 1) % per) * NCD + c, got[i], 0.0)

        acc = lax.fori_loop(0, got.shape[0], gather, acc, unroll=got.shape[0] <= per)
        sums.append(jnp.sum(acc, axis=1, keepdims=True))
    return sums


def second_direction_kernel(
    blocks,
    got,
    coarse,
    grp,
    kap,
    resid,
    direction,
    image,
    smoothed,
    ctab,
    zmat,
    following,
    known,
    msg,
    slope_z,
):
    place = Place()
    inv_mult = [1.0 / place.mult_tile(ey) for ey in range(2)]
    part = coarse_part(place, blocks, got, coarse, grp)
    energy, curvature = gathered_scalars(got, 2)
    step = energy / curvature
    lane = lax.broadcasted_iota(jnp.int32, (1, LANES), 1)
    known[...] = jnp.where(lane == 0, energy, jnp.where(lane == 1, curvature, 0.0))
    energy_next = jnp.zeros(TILE, jnp.float32)
    cross = jnp.zeros(TILE, jnp.float32)
    for ex in range(2):
        for ey in range(2):
            kinds = [part(ex, kind, ey) for kind in range(3)]
            for a in range(8):
                value = direction[ex, a, ey] - step * (smoothed[ex, a, ey] + kinds[kind_of(a)])
                following[ex, a, ey] = value
                weighed = value * (inv_mult[ey] * place.inv_x(ex, a))
                was = image[ex, a, ey]
                energy_next = energy_next + weighed * (resid[ex, a, ey] - step * was)
                cross = cross + weighed * was
    slope_z[...] = along_z(following[...].reshape(256, LANES), zmat[2]).reshape(slope_z.shape)
    square = jnp.zeros(TILE, jnp.float32)
    for ex in range(2):
        for ey in range(2):
            values, images = own_operator(ctab, kap, following, slope_z, ex, ey)
            for a in range(8):
                square = square + values[a] * images[a]
    send_to_all(msg, message(place, [], [total(energy_next), total(square), total(cross)]))


def pressure_kernel(got, known, direction, following, pressure):
    energy = known[:, pl.ds(0, 1)]
    curvature = known[:, pl.ds(1, 1)]
    energy_next, square, cross = gathered_scalars(got, 3)
    ratio = energy_next / energy
    step = energy / curvature
    step_next = energy_next / (square + 2.0 * ratio * cross + ratio * ratio * curvature)
    weight_old = step + step_next * ratio
    for ex in range(2):
        for a in range(8):
            for ey in range(2):
                pressure[ex, a, ey] = (
                    weight_old * direction[ex, a, ey] + step_next * following[ex, a, ey]
                )


def coarse_energy(place, got, values, kappa, number):
    lane, row = place.lane, place.row
    for ex in range(2):
        for gx in range(8):
            own = jnp.zeros((1, LANES), jnp.float32)
            group = jnp.zeros((1, LANES), jnp.float32)
            spot = lane[0:1] // 32
            for gy in range(4):
                line = got[gx * 4 + gy, pl.ds(2 + ex, 1), :]
                own = jnp.where(spot == gy, line, own)
                group = jnp.where(spot == (gy + 1) % 4, line, group)
            kappa[ex, pl.ds(gx, 1), :] = own
            number[ex, pl.ds(gx, 1), :] = group
    grid = [jnp.zeros(TILE, jnp.float32) for _ in range(2)]
    numbers = [pltpu.roll(number[ex], 96, 1) for ex in range(2)]
    for q in range(4):
        for c in range(NCD):
            mine = jnp.where(lane == row * 16 + q * 4 + c, values, 0.0)
            mine = jnp.sum(mine, axis=1, keepdims=True)
            for ex in range(2):
                chosen = (lane // 32 == q) & (numbers[ex] == float(c))
                grid[ex] = jnp.where(chosen, mine, grid[ex])

    def ends_y(v):
        low = jnp.where(lane >= 16, 0.5 * (v + pltpu.roll(v, 16, 1)), v)
        return low, v, jnp.where(lane < 112, 0.5 * (v + pltpu.roll(v, 112, 1)), v)

    def ends_z(v):
        low = jnp.where(lane % 16 > 0, 0.5 * (v + pltpu.roll(v, 1, 1)), v)
        return low, v, jnp.where(lane % 16 < 15, 0.5 * (v + pltpu.roll(v, 127, 1)), v)

    low = jnp.where(row > 0, 0.5 * (grid[0] + pltpu.roll(grid[1], 1, 0)), grid[0])
    mid = 0.5 * (grid[0] + grid[1])
    high = jnp.where(row < 7, 0.5 * (grid[1] + pltpu.roll(grid[0], 7, 0)), grid[1])
    mass = [float(WEIGHTS[0]), float(np.sum(WEIGHTS[1:7])), float(WEIGHTS[7])]
    links = (
        (0, 1, -float(np.sum(STIFF[0, 1:7]))),
        (0, 2, -float(STIFF[0, 7])),
        (1, 2, -float(np.sum(STIFF[7, 1:7]))),
    )
    energy = jnp.zeros(TILE, jnp.float32)
    for ex, line in enumerate(((low, grid[0], mid), (mid, grid[1], high))):
        nodes = [[ends_z(v) for v in ends_y(w)] for w in line]
        stiff = jnp.zeros(TILE, jnp.float32)
        square = jnp.zeros(TILE, jnp.float32)
        for i in range(3):
            for j in range(3):
                for k, l, weight in links:
                    factor = weight * mass[i] * mass[j]
                    for first, second in (
                        (nodes[k][i][j], nodes[l][i][j]),
                        (nodes[i][k][j], nodes[i][l][j]),
                        (nodes[i][j][k], nodes[i][j][l]),
                    ):
                        gap = first - second
                        stiff = stiff + (factor * gap) * gap
                for k in range(3):
                    value = nodes[i][j][k]
                    square = square + (mass[i] * mass[j] * mass[k] * value) * value
        energy = energy + kappa[ex] * stiff + sigma_p * square
    return total(energy)


def finish_kernel(
    got, grp, direction, smoothed, pressure, matrix, kappa, number
):
    place = Place()
    per = LANES // NCD
    row_lane = lax.broadcasted_iota(jnp.int32, (1, LANES), 1)
    rest = jnp.zeros((1, LANES), jnp.float32)
    dual = jnp.zeros((1, LANES), jnp.float32)
    sums = [jnp.zeros((1, LANES), jnp.float32) for _ in range(4)]
    for i in range(per):
        line = got[i, pl.ds(0, 1), :]
        rest = jnp.where(row_lane // NCD == i, line, rest)
        dual = dual + got[i, pl.ds(1, 1), :]
        for c in range(4):
            sums[c] = sums[c] + jnp.where(row_lane == ((i + 1) % per) * NCD + c, line, 0.0)
        matrix[pl.ds(i * NCD, NCD), :] = got[i, pl.ds(4, NCD), :]
    energy, curvature, square, self_energy = [
        jnp.sum(value, axis=1, keepdims=True) for value in sums
    ]
    values = lax.dot_general(
        jnp.broadcast_to(rest, TILE),
        matrix[...],
        (((1,), (1,)), ((), ())),
        precision=lax.Precision.HIGHEST,
        preferred_element_type=jnp.float32,
    )
    line = values[0:1]
    cross = square + jnp.sum(line * rest, axis=1, keepdims=True)
    both = self_energy + 2.0 * jnp.sum(line * dual, axis=1, keepdims=True)
    both = both + coarse_energy(place, got, values, kappa, number)
    step = energy / curvature
    energy_next = step * step * cross - energy
    ratio = energy_next / energy
    with_image = curvature - step * cross
    with_itself = curvature - 2.0 * step * cross + step * step * both
    step_next = energy_next / (
        with_itself + 2.0 * ratio * with_image + ratio * ratio * curvature
    )
    old = step + step_next * (1.0 + ratio)
    new = -step_next * step

    def solved(dx, dy, c):
        at = ((place.ix + dx - 1) * place.ny + place.iy + dy - 1) * NCD + c
        return jnp.sum(jnp.where(row_lane == at, line, 0.0), axis=1, keepdims=True)

    part = prolonged(place, masked(place, solved), grp)
    for ex in range(2):
        for ey in range(2):
            kinds = [part(ex, kind, ey) for kind in range(3)]
            for a in range(8):
                pressure[ex, a, ey] = old * direction[ex, a, ey] + new * (
                    smoothed[ex, a, ey] + kinds[kind_of(a)]
                )


def masked(place, solved):
    there_x = (place.prev_x, None, place.next_x)
    there_y = (place.prev_y, None, place.next_y)

    def value(dx, dy, c):
        out = solved(dx, dy, c)
        for there in (there_x[dx], there_y[dy]):
            if there is not None:
                out = jnp.where(there, out, 0.0)
        return out

    return value


def call(body, outs, scratch=(), **more):
    return pl.pallas_call(
        body,
        out_shape=[jax.ShapeDtypeStruct(shape, jnp.float32) for shape in outs],
        scratch_shapes=[
            pltpu.VMEM(shape, jnp.float32) if isinstance(shape, tuple) else shape
            for shape in scratch
        ],
        **more,
        compiler_params=pltpu.CompilerParams(vmem_limit_bytes=24 * 1024 * 1024),
    )


def swap(first, second, axis):
    count = lax.axis_size(axis)
    first_pairs = [(i, i ^ 1) for i in range(count) if i ^ 1 < count]
    second_pairs = [(i, ((i + 1) ^ 1) - 1) for i in range(1, count) if ((i + 1) ^ 1) - 1 < count]
    second_got = lax.ppermute(second, axis, second_pairs)
    return lax.ppermute(first, axis, first_pairs), second_got


def per_device(fields, viscosity, inv_density, elem_group, coarse_inverse):
    length = fields.shape[5]
    elems_z = length // NODES
    devices = lax.axis_size("gx") * lax.axis_size("gy")
    blocks = coarse_inverse.shape[1] // LANES
    pack_rows = -(-(8 + NCD * blocks) // 8) * 8
    tiles_np, mats_np = constant_tables(elems_z)
    ctab, zmat = jnp.asarray(tiles_np), jnp.asarray(mats_np)
    one = fields.shape[1:]
    four = fields.shape
    faces = (64, LANES)
    xf_shape = (2, 4, 2, 8, LANES)
    inner_shape = (2, 2, 8, LANES)
    y_shape, x_shape = (STEP_PACK + pack_rows, LANES), (STEP_PACK + 3 * pack_rows, LANES)
    smooth_shape = (SMOOTH_ROWS, LANES)
    rows = (devices, 1, LANES)
    grid_fits = (
        blocks == 1
        and lax.axis_size("gx") == 8
        and lax.axis_size("gy") * fields.shape[3] * elems_z == LANES
    )

    def exchange_all(msg):
        return lax.all_to_all(msg, BOTH, 0, 0, tiled=True)

    summed, xf, first, second = call(
        mass_kernel,
        [four, xf_shape, faces, faces],
    )(fields)
    pack, facts = call(
        pack_kernel,
        [(pack_rows, LANES), TILE],
        cost_estimate=pl.CostEstimate(flops=10**6, bytes_accessed=10**5, transcendentals=0),
    )(inv_density, elem_group, coarse_inverse)
    y_got = swap(first, second, "gy")
    first, second = call(turn_faces_kernel, [faces, faces])(xf, *y_got)
    x_got = swap(first, second, "gx")
    share, xf, inner_x, first, second = call(
        functools.partial(rhs_kernel, pack_rows),
        [four, xf_shape, inner_shape, y_shape, y_shape],
        [four, four, four, four],
    )(
        summed,
        viscosity,
        pack,
        *y_got,
        *x_got,
        ctab,
        zmat,
    )
    y_got = swap(first, second, "gy")
    first, second = call(functools.partial(turn_step_kernel, pack_rows), [x_shape, x_shape])(
        xf, inner_x, pack, *y_got
    )
    x_got = swap(first, second, "gx")
    inv_diag, kap, grp, coarse = call(
        functools.partial(setup_kernel, pack_rows, blocks),
        [one, (16, LANES), (16, LANES), (9 * NCD * blocks, LANES)],
    )(pack, *y_got, *x_got, ctab)
    fields_new, resid, own, msg = call(
        advance_kernel, [four, one, one, (devices, 16, LANES)], [one, one]
    )(share, *y_got, *x_got, inv_diag, kap, grp, ctab, zmat)
    got = exchange_all(msg)
    direction, own, inner_x, first, second, extra = call(
        functools.partial(first_direction_kernel, blocks),
        [one, one, inner_shape, smooth_shape, smooth_shape, (1, LANES)],
        [one, one],
    )(got, coarse, grp, kap, inv_diag, resid, own, ctab, zmat)
    y_got = swap(first, second, "gy")
    first, second = call(turn_smooth_kernel, [smooth_shape, smooth_shape])(own, inner_x, *y_got)
    x_got = swap(first, second, "gx")
    image, image_smoothed, msg = call(
        smooth_kernel, [one, one, (devices, 8, LANES) if grid_fits else rows], [one, one]
    )(own, *y_got, *x_got, inv_diag, kap, grp, extra, facts, ctab, zmat)
    got = exchange_all(msg)
    if grid_fits:
        (pressure,) = call(
            finish_kernel, [one], [(LANES, LANES), (2,) + TILE, (2,) + TILE]
        )(got, grp, direction, image_smoothed)
        return (fields_new, pressure)
    following, known, msg = call(
        functools.partial(second_direction_kernel, blocks), [one, (1, LANES), rows], [one]
    )(got, coarse, grp, kap, resid, direction, image, image_smoothed, ctab, zmat)
    got = exchange_all(msg)
    (pressure,) = call(pressure_kernel, [one])(got, known, direction, following)
    return (fields_new, pressure)


def solution(mesh):
    placed = (
        P(None, "gx", None, "gy", None, None),
        P("gx", None, "gy", None, None),
        P("gx", "gy", None),
        P("gx", "gy", None),
        P(("gx", "gy"), None),
    )
    return jax.shard_map(
        per_device,
        mesh=mesh,
        in_specs=placed,
        out_specs=(P(None, "gx", None, "gy", None, None), P("gx", None, "gy", None, None)),
        check_vma=False,
    )
```

```python
import functools

import jax
import jax.numpy as jnp
import ml_dtypes
import numpy as np
from jax import lax
from jax.experimental import pallas as pl
from jax.experimental.pallas import tpu as pltpu
from jax.sharding import PartitionSpec as P

NCD = 4
NODES = 8
LANES = 128
TILE = (8, 128)
BOTH = ("gx", "gy")

dt_step = 0.01
sigma_p = 4.0
prandtl = 0.7
cheb_ratio = 0.1


def tables():
    points = np.array(
        [
            -1.0,
            -0.8717401485096066,
            -0.5917001814331423,
            -0.2092992179024789,
            0.2092992179024789,
            0.5917001814331423,
            0.8717401485096066,
            1.0,
        ]
    )
    weights = np.array(
        [
            1.0 / 28.0,
            0.2107042271435061,
            0.3411226924835044,
            0.4124587946587038,
            0.4124587946587038,
            0.3411226924835044,
            0.2107042271435061,
            1.0 / 28.0,
        ]
    )
    identity = np.eye(8)
    differ = points[:, None] - points[None, :] + identity
    barycentric = 1.0 / np.prod(differ, axis=1)
    offdiag = barycentric[None, :] / barycentric[:, None] / differ * (1.0 - identity)
    derivative = offdiag - identity * np.sum(offdiag, axis=1)[:, None]
    mass_one = identity * weights[None, :]
    stiff_one = derivative.T @ mass_one @ derivative
    stiff_three = (
        np.kron(np.kron(stiff_one, mass_one), mass_one)
        + np.kron(np.kron(mass_one, stiff_one), mass_one)
        + np.kron(np.kron(mass_one, mass_one), stiff_one)
    )
    three_diag = np.sum(stiff_three * np.eye(512), axis=1)
    spectral_bound = float(np.max(np.sum(np.abs(stiff_three), axis=1) / three_diag))
    return (derivative, weights, stiff_one, spectral_bound)


DERIV, WEIGHTS, STIFF, BOUND = tables()
SCALED = STIFF / WEIGHTS[:, None]
LINE = np.diag(STIFF) / WEIGHTS
THETA = 0.5 * (BOUND + cheb_ratio * BOUND)
DELTA = 0.5 * (BOUND - cheb_ratio * BOUND)
RHO = DELTA / THETA
RHO_NEXT = 1.0 / (2.0 * THETA / DELTA - RHO)


def constant_tables(elems_z):
    def turned(matrix):
        rows = np.arange(8)
        return [np.repeat(matrix[rows, (rows - s) % 8][:, None], LANES, 1) for s in range(8)]

    wz = np.tile(WEIGHTS, elems_z)
    kz = np.tile(LINE, elems_z)
    tiles = turned(DERIV) + turned(DERIV.T) + turned(SCALED)
    tiles += [WEIGHTS[:, None] * wz[None, :], LINE[:, None] + kz[None, :]]
    for matrix in (DERIV, SCALED):
        for node in (7, 0):
            inner = matrix[node] * (np.arange(8) != node)
            tiles.append(np.repeat(inner[:, None], LANES, 1))
    eye = np.eye(elems_z)
    mats = [np.kron(eye, DERIV.T), np.kron(eye, DERIV), np.kron(eye, SCALED.T)]
    halves = []
    for mat in mats:
        high = mat.astype(ml_dtypes.bfloat16)
        low = (mat - high.astype(np.float64)).astype(ml_dtypes.bfloat16)
        both = np.concatenate([high, low], 1)
        halves.append(np.concatenate([both, both], 0))
    return np.stack(tiles).astype(np.float32), np.stack(halves)


T_D, T_DT, T_K, T_W, T_LINE = 0, 8, 16, 24, 25
T_TOP, T_BOTTOM, T_KTOP, T_KBOTTOM = 26, 27, 28, 29


class Place:
    def __init__(self):
        self.ix = lax.axis_index("gx")
        self.iy = lax.axis_index("gy")
        self.nx = lax.axis_size("gx")
        self.ny = lax.axis_size("gy")
        self.even_x = self.ix % 2 == 0
        self.even_y = self.iy % 2 == 0
        self.row = lax.broadcasted_iota(jnp.int32, TILE, 0)
        self.lane = lax.broadcasted_iota(jnp.int32, TILE, 1)
        self.low_z = (self.lane % 8 == 0) & (self.lane > 0)
        self.high_z = (self.lane % 8 == 7) & (self.lane < LANES - 1)
        self.prev_x = self.ix > 0
        self.next_x = self.ix < self.nx - 1
        self.prev_y = self.iy > 0
        self.next_y = self.iy < self.ny - 1

    def mult_tile(self, ey):
        along_z = 1.0 + jnp.where(self.low_z | self.high_z, 1.0, 0.0)
        low = 1.0 if ey == 1 else jnp.where(self.prev_y, 1.0, 0.0)
        high = 1.0 if ey == 0 else jnp.where(self.next_y, 1.0, 0.0)
        along_y = 1.0 + jnp.where(self.row == 0, low, jnp.where(self.row == 7, high, 0.0))
        return along_y * along_z

    def inv_x(self, ex, a):
        if a == 0:
            return 0.5 if ex == 1 else jnp.where(self.prev_x, 0.5, 1.0)
        if a == 7:
            return 0.5 if ex == 0 else jnp.where(self.next_x, 0.5, 1.0)
        return 1.0

    def mult_x(self, ex, a):
        if a == 0:
            return 2.0 if ex == 1 else jnp.where(self.prev_x, 2.0, 1.0)
        if a == 7:
            return 2.0 if ex == 0 else jnp.where(self.next_x, 2.0, 1.0)
        return 1.0

    def share_x(self, ex, a):
        if (ex, a) == (0, 0):
            return jnp.where(self.prev_x, 0.5, 1.0)
        if (ex, a) == (1, 7):
            return jnp.where(self.next_x, 0.5, 1.0)
        return 1.0

    def share_y(self, ey):
        if ey == 0:
            return jnp.where((self.row == 0) & self.prev_y, 0.5, 1.0)
        return jnp.where((self.row == 7) & self.next_y, 0.5, 1.0)

    def inv_y(self, ey):
        low = 0.5 if ey == 1 else jnp.where(self.prev_y, 0.5, 1.0)
        high = 0.5 if ey == 0 else jnp.where(self.next_y, 0.5, 1.0)
        return jnp.where(self.row == 0, low, jnp.where(self.row == 7, high, 1.0))

    def inv_z(self):
        return jnp.where(self.low_z | self.high_z, 0.5, 1.0)

    def join_z(self, t):
        up = pltpu.roll(t, LANES - 1, 1)
        down = pltpu.roll(t, 1, 1)
        return t + jnp.where(self.high_z, up, jnp.where(self.low_z, down, 0.0))

    def to_low(self, below):
        return jnp.where(self.row == 0, pltpu.roll(below, 1, 0), 0.0)

    def to_high(self, above):
        return jnp.where(self.row == 7, pltpu.roll(above, 7, 0), 0.0)

    def join_y(self, below, above):
        return below + self.to_high(above), above + self.to_low(below)

    def before_x(self, first, second):
        return jnp.where(self.even_x, second, first)

    def after_x(self, first, second):
        return jnp.where(self.even_x, first, second)

    def before_y(self, first, second):
        return jnp.where(self.even_y, second, first)

    def after_y(self, first, second):
        return jnp.where(self.even_y, first, second)


def along_x(matrix, tiles, sign):
    even = [tiles[a] + tiles[7 - a] for a in range(4)]
    odd = [tiles[a] - tiles[7 - a] for a in range(4)]
    out = [None] * 8
    for i in range(4):
        plus, minus = None, None
        for a in range(4):
            p = float(0.5 * (matrix[i, a] + matrix[i, 7 - a])) * even[a]
            m = float(0.5 * (matrix[i, a] - matrix[i, 7 - a])) * odd[a]
            plus = p if plus is None else plus + p
            minus = m if minus is None else minus + m
        out[i] = plus + minus
        out[7 - i] = minus - plus if sign < 0 else plus - minus
    return out


def along_y(ctab, base, tile):
    acc = ctab[base] * tile
    for s in range(1, 8):
        acc = acc + ctab[base + s] * pltpu.roll(tile, s, 0)
    return acc


def exact_dot(rows, matrix):
    return jnp.dot(
        rows, matrix, precision=lax.Precision.HIGHEST, preferred_element_type=jnp.float32
    )


def along_z(rows, matrix):
    high = rows.astype(jnp.bfloat16)
    low = (rows - high.astype(jnp.float32)).astype(jnp.bfloat16)
    both = jnp.dot(
        jnp.concatenate([high, low], axis=1), matrix, preferred_element_type=jnp.float32
    )
    return both[:, :LANES] + both[:, LANES:]


def total(tile):
    return jnp.sum(jnp.sum(tile, axis=0, keepdims=True), axis=1, keepdims=True)


def store_y_faces(place, field, first_out, second_out, lead, at):
    for ex in range(2):
        for a in range(8):
            low = field[lead + (ex, a, 0, pl.ds(0, 1), slice(None))]
            high = field[lead + (ex, a, 1, pl.ds(7, 1), slice(None))]
            row = at + ex * 8 + a
            first_out[pl.ds(row, 1), :] = place.after_y(high, low)
            second_out[pl.ds(row, 1), :] = place.after_y(low, high)


def join_own(place, tiles):
    for ex in range(2):
        for a in range(8):
            tiles[ex][a] = list(place.join_y(*tiles[ex][a]))
    for ey in range(2):
        both = tiles[0][7][ey] + tiles[1][0][ey]
        tiles[0][7][ey] = both
        tiles[1][0][ey] = both


def weight_of(node):
    edge = jnp.minimum(node, 7 - node)
    value = jnp.where(edge == 2, float(WEIGHTS[2]), float(WEIGHTS[3]))
    return jnp.where(
        edge == 0, float(WEIGHTS[0]), jnp.where(edge == 1, float(WEIGHTS[1]), value)
    )


def mass_kernel(fields, out, xf, first, second):
    place = Place()
    weight = weight_of(place.row) * weight_of(place.lane % NODES)
    for ch in range(4):
        tiles = [
            [
                [
                    place.join_z(fields[ch, ex, a, ey] * (float(WEIGHTS[a]) * weight))
                    for ey in range(2)
                ]
                for a in range(8)
            ]
            for ex in range(2)
        ]
        join_own(place, tiles)
        for ex in range(2):
            for a in range(8):
                for ey in range(2):
                    out[ch, ex, a, ey] = tiles[ex][a][ey]
        for ey in range(2):
            xf[0, ch, ey] = tiles[0][0][ey]
            xf[1, ch, ey] = tiles[1][7][ey]
        store_y_faces(place, out, first, second, (ch,), ch * 16)


def turn_faces(place, xf, y_first, y_second, first, second):
    for ch in range(4):
        sides = []
        for side in range(2):
            row = pl.ds(ch * 16 + 15 * side, 1)
            got_a, got_b = y_first[row, :], y_second[row, :]
            low = xf[side, ch, 0] + jnp.where(place.row == 0, place.before_y(got_a, got_b), 0.0)
            high = xf[side, ch, 1] + jnp.where(place.row == 7, place.after_y(got_a, got_b), 0.0)
            sides.append((low, high))
        for ey in range(2):
            rows = pl.ds(ch * 16 + ey * 8, 8)
            first[rows, :] = place.after_x(sides[1][ey], sides[0][ey])
            second[rows, :] = place.after_x(sides[0][ey], sides[1][ey])


def turn_faces_kernel(xf, y_first, y_second, first, second):
    turn_faces(Place(), xf, y_first, y_second, first, second)


def turn_edges(place, inner_x, y_first, y_second, first, second, at, edge, inner_y):
    sides = []
    for side in range(2):
        row = pl.ds(edge + side, 1)
        got_a, got_b = y_first[row, :], y_second[row, :]
        low = inner_x[side, 0] + jnp.where(place.row == 0, place.before_y(got_a, got_b), 0.0)
        high = inner_x[side, 1] + jnp.where(place.row == 7, place.after_y(got_a, got_b), 0.0)
        sides.append((low, high))
    for ey in range(2):
        rows = pl.ds(at + ey * 8, 8)
        first[rows, :] = place.after_x(sides[1][ey], sides[0][ey])
        second[rows, :] = place.after_x(sides[0][ey], sides[1][ey])
    for k, pick in enumerate((place.before_y, place.after_y)):
        sides = []
        for side in range(2):
            row = pl.ds(inner_y + 15 * side, 1)
            sides.append(pick(y_first[row, :], y_second[row, :]))
        row = pl.ds(edge + k, 1)
        first[row, :] = place.after_x(sides[1], sides[0])
        second[row, :] = place.after_x(sides[0], sides[1])


STEP_U, STEP_V, STEP_EDGE, STEP_PACK = 64, 64, 80, 88


def turn_step_kernel(pack_rows, xf, inner_x, pack, y_first, y_second, first, second):
    place = Place()
    turn_faces(place, xf, y_first, y_second, first, second)
    first[pl.ds(STEP_EDGE, 8), :] = jnp.zeros(TILE, jnp.float32)
    second[pl.ds(STEP_EDGE, 8), :] = jnp.zeros(TILE, jnp.float32)
    turn_edges(place, inner_x, y_first, y_second, first, second, STEP_U, STEP_EDGE, STEP_V)
    came = pl.ds(STEP_PACK, pack_rows)
    parts = (
        place.before_y(y_first[came, :], y_second[came, :]),
        pack[...],
        place.after_y(y_first[came, :], y_second[came, :]),
    )
    for k in range(3):
        rows = pl.ds(STEP_PACK + k * pack_rows, pack_rows)
        first[rows, :] = parts[k]
        second[rows, :] = parts[k]


def setup_kernel(
    pack_rows, blocks, pack, y_first, y_second, x_first, x_second, ctab, inv_diag, kap, grp, coarse
):
    place = Place()
    came = pl.ds(STEP_PACK, pack_rows)
    packs = [[None] * 3 for _ in range(3)]
    packs[1][0] = place.before_y(y_first[came, :], y_second[came, :])
    packs[1][1] = pack[...]
    packs[1][2] = place.after_y(y_first[came, :], y_second[came, :])
    for k in range(3):
        rows = pl.ds(STEP_PACK + k * pack_rows, pack_rows)
        packs[0][k] = place.before_x(x_first[rows, :], x_second[rows, :])
        packs[2][k] = place.after_x(x_first[rows, :], x_second[rows, :])
    for dx in range(3):
        for dy in range(3):
            at = (dx * 3 + dy) * NCD * blocks
            coarse[pl.ds(at, NCD * blocks), :] = packs[dx][dy][8 : 8 + NCD * blocks]
    there_x = [jnp.where(place.prev_x, 1.0, 0.0), 1.0, jnp.where(place.next_x, 1.0, 0.0)]
    there_y = [jnp.where(place.prev_y, 1.0, 0.0), 1.0, jnp.where(place.next_y, 1.0, 0.0)]

    def element_row(base, u, v):
        row = base + (u % 2) * 2 + v % 2
        return packs[u // 2][v // 2][row : row + 1]

    for x in range(4):
        for y in range(4):
            kap[pl.ds(x * 4 + y, 1), :] = element_row(0, x + 1, y + 1)
            grp[pl.ds(x * 4 + y, 1), :] = element_row(4, x + 1, y + 1)
    kappa = [
        [
            place.join_z(jnp.broadcast_to(element_row(0, u + 1, v + 1), TILE))
            for v in range(4)
        ]
        for u in range(4)
    ]
    count_z = 1.0 + jnp.where(place.low_z | place.high_z, 1.0, 0.0)
    weight = ctab[T_W]
    line = ctab[T_LINE]

    def pick(values, ey):
        low = values[ey] + values[ey + 1]
        high = values[ey + 1] + values[ey + 2]
        return jnp.where(place.row == 0, low, jnp.where(place.row == 7, high, values[ey + 1]))

    for ex in range(2):
        for kind in range(3):
            us = {0: (ex, ex + 1), 1: (ex + 1,), 2: (ex + 1, ex + 2)}[kind]
            sums, counts = [], []
            for v in range(4):
                acc, num = None, 0.0
                for u in us:
                    acc = kappa[u][v] if acc is None else acc + kappa[u][v]
                    num = num + there_x[(u + 1) // 2]
                sums.append(acc)
                counts.append(num * there_y[(v + 1) // 2])
            for ey in range(2):
                kappa_sum = pick(sums, ey)
                mult = pick(counts, ey) * count_z
                for a in {0: (0,), 1: range(1, 7), 2: (7,)}[kind]:
                    diag = (float(LINE[a]) + line) * kappa_sum + sigma_p * mult
                    inv_diag[ex, a, ey] = 1.0 / (diag * (float(WEIGHTS[a]) * weight))


OUTER = ((0, 0), (1, 7))


def got_y_sum(place, tile, ch, ex, a, ey, y_first, y_second):
    row = pl.ds(ch * 16 + ex * 8 + a, 1)
    got_a, got_b = y_first[row, :], y_second[row, :]
    if ey == 0:
        tile = tile + jnp.where(place.row == 0, place.before_y(got_a, got_b), 0.0)
    else:
        tile = tile + jnp.where(place.row == 7, place.after_y(got_a, got_b), 0.0)
    return tile


def got_x_sum(place, tile, ch, ex, ey, x_first, x_second):
    rows = pl.ds(ch * 16 + ey * 8, 8)
    pick = place.before_x if ex == 0 else place.after_x
    return tile + pick(x_first[rows, :], x_second[rows, :])


def pack_kernel(kappa, group, coarse, pack, facts):
    place = Place()
    pack[...] = jnp.zeros(pack.shape, jnp.float32)
    facts[...] = jnp.zeros(facts.shape, jnp.float32)
    elems = kappa.shape[2]
    to = lax.broadcasted_iota(jnp.int32, (elems, LANES), 1)
    element = lax.broadcasted_iota(jnp.int32, (elems, LANES), 0)
    spread = (to // NODES == element).astype(jnp.float32)
    blocks = coarse.shape[1] // LANES
    for ex in range(2):
        numbers = group[ex].astype(jnp.float32)
        pack[pl.ds(2 * ex, 2), :] = exact_dot(kappa[ex], spread)
        pack[pl.ds(4 + 2 * ex, 2), :] = exact_dot(numbers, spread)
        row = jnp.zeros((1, LANES), jnp.float32)
        for ey in range(2):
            at = (2 * place.iy + ey) * elems
            spot = (to == at + element).astype(jnp.float32)
            after = (to == (at + 2 * elems) % LANES + element).astype(jnp.float32)
            row = row + exact_dot(kappa[ex, pl.ds(ey, 1), :], spot)
            row = row + exact_dot(numbers[ey : ey + 1], after)
        facts[pl.ds(2 + ex, 1), :] = row
    for c in range(NCD):
        for j in range(blocks):
            line = coarse[pl.ds(c, 1), pl.ds(j * LANES, LANES)]
            pack[pl.ds(8 + c * blocks + j, 1), :] = line
        facts[pl.ds(4 + c, 1), :] = coarse[pl.ds(c, 1), pl.ds(0, LANES)]


def prepare_kernel(
    summed, visc, y_first, y_second, ctab, zmat, start, part, grad_z, flux_z
):
    place = Place()
    weight = ctab[T_W]
    inv_mass = [1.0 / (weight * place.mult_tile(ey)) for ey in range(2)]

    def begin(ch, carry):
        for ex in range(2):
            for a in range(8):
                for ey in range(2):
                    tile = got_y_sum(
                        place, summed[ch, ex, a, ey], ch, ex, a, ey, y_first, y_second
                    )
                    scale = place.inv_x(ex, a) * float(1.0 / WEIGHTS[a])
                    start[ch, ex, a, ey] = tile * (inv_mass[ey] * scale)
        return carry

    lax.fori_loop(0, 4, begin, 0)
    grad_z[...] = along_z(start[...].reshape(1024, LANES), zmat[0]).reshape(grad_z.shape)

    def column(index, carry):
        ch, ey = index // 2, index % 2
        coef = jnp.where(ch == 3, 1.0 / prandtl, 1.0)
        for ex in range(2):
            for a in range(8):
                if (ex, a) in OUTER:
                    continue
                parts = across(
                    ctab, weight, a, coef, start[ch, ex, a, ey], grad_z[ch, ex, a, ey],
                    start[1, ex, a, ey], start[2, ex, a, ey], visc[ex, a, ey],
                )
                part[ch, ex, a, ey], flux_z[ch, ex, a, ey] = parts
        return carry

    lax.fori_loop(0, 8, column, 0)
    for ch in range(4):
        for ex in range(2):
            inner = pl.ds(1 - ex, 7)
            back = along_z(flux_z[ch, ex, inner].reshape(112, LANES), zmat[1])
            part[ch, ex, inner] = part[ch, ex, inner] + back.reshape(7, 2, 8, LANES)


def across(ctab, weight, a, coef, value, grad_z, flow_y, flow_z, visc):
    node = float(WEIGHTS[a]) * weight
    grad_y = along_y(ctab, T_D, value)
    nu = visc * node * coef
    part = node * (flow_y * grad_y + flow_z * grad_z) + along_y(ctab, T_DT, nu * grad_y)
    return part, nu * grad_z


def rhs_kernel(
    pack_rows,
    begun,
    given,
    visc,
    pack,
    x_first,
    x_second,
    ctab,
    zmat,
    share,
    xf,
    inner_x,
    first,
    second,
    rhs,
    edge,
    edge_z,
    edge_part,
):
    place = Place()
    weight = ctab[T_W]
    inv_mass = [1.0 / (weight * place.mult_tile(ey)) for ey in range(2)]
    for ch in range(4):
        for side, (ex, a) in enumerate(OUTER):
            scale = place.inv_x(ex, a) * float(1.0 / WEIGHTS[a])
            for ey in range(2):
                zero = jnp.zeros(TILE, jnp.float32)
                came = got_x_sum(place, zero, ch, ex, ey, x_first, x_second)
                edge[ch, side, ey] = begun[ch, ex, a, ey] + came * (inv_mass[ey] * scale)
    edge_z[...] = along_z(edge[...].reshape(128, LANES), zmat[0]).reshape(edge.shape)
    for ch in range(4):
        coef = 1.0 / prandtl if ch == 3 else 1.0
        for side, (ex, a) in enumerate(OUTER):
            for ey in range(2):
                parts = across(
                    ctab, weight, a, coef, edge[ch, side, ey], edge_z[ch, side, ey],
                    edge[1, side, ey], edge[2, side, ey], visc[ex, a, ey],
                )
                edge_part[ch, side, ey], edge_z[ch, side, ey] = parts
    edge_part[...] = edge_part[...] + along_z(
        edge_z[...].reshape(128, LANES), zmat[1]
    ).reshape(edge.shape)

    def value_of(ch, ex, a, ey):
        if (ex, a) in OUTER:
            return edge[ch, ex, ey]
        return begun[ch, ex, a, ey]

    def column(index, carry):
        ch, ey = index // 2, index % 2
        coef = jnp.where(ch == 3, 1.0 / prandtl, 1.0)
        for ex in range(2):
            field = [value_of(ch, ex, a, ey) for a in range(8)]
            grad_x = along_x(DERIV, field, -1)
            flux_x, parts = [], []
            for a in range(8):
                node = float(WEIGHTS[a]) * weight
                flux_x.append(visc[ex, a, ey] * node * coef * grad_x[a])
                known = edge_part[ch, ex, ey] if (ex, a) in OUTER else given[ch, ex, a, ey]
                parts.append(known + node * (value_of(0, ex, a, ey) * grad_x[a]))
            back = along_x(DERIV.T, flux_x, -1)
            for a in range(8):
                rhs[ch, ex, a, ey] = parts[a] + back[a]
        return carry

    lax.fori_loop(0, 8, column, 0)

    def finish(ch, carry):
        tiles = [
            [
                [
                    place.join_z(-rhs[ch, ex, a, ey])
                    for ey in range(2)
                ]
                for a in range(8)
            ]
            for ex in range(2)
        ]
        join_own(place, tiles)
        for ex in range(2):
            for a in range(8):
                scale = place.inv_x(ex, a) * float(dt_step / WEIGHTS[a])
                for ey in range(2):
                    value = value_of(ch, ex, a, ey)
                    part = value * (place.share_y(ey) * place.share_x(ex, a))
                    share[ch, ex, a, ey] = part + tiles[ex][a][ey] * (inv_mass[ey] * scale)
        return carry

    lax.fori_loop(0, 4, finish, 0)
    for ch in range(4):
        store_y_faces(place, share, first, second, (ch,), ch * 16)
        for ey in range(2):
            xf[0, ch, ey] = share[ch, 0, 0, ey]
            xf[1, ch, ey] = share[ch, 1, 7, ey]
    first[pl.ds(STEP_EDGE, 8), :] = jnp.zeros(TILE, jnp.float32)
    second[pl.ds(STEP_EDGE, 8), :] = jnp.zeros(TILE, jnp.float32)

    def column_of(ex, ey):
        return [share[0, ex, a, ey] for a in range(8)]

    def tile_of(ex, a, ey):
        return share[1, ex, a, ey]

    store_inner(
        place, DERIV, ctab[T_BOTTOM], ctab[T_TOP], column_of, tile_of, inner_x, first, second,
        STEP_V, STEP_EDGE,
    )
    first[pl.ds(STEP_PACK, pack_rows), :] = pack[...]
    second[pl.ds(STEP_PACK, pack_rows), :] = pack[...]


def store_inner(
    place, matrix, bottom, top, column_of, tile_of, inner_x, first, second, at, edge
):
    for ey in range(2):
        low, high = column_of(0, ey), column_of(1, ey)
        below = float(matrix[0, 1]) * low[1]
        above = float(matrix[7, 0]) * high[0]
        for k in range(2, 8):
            below = below + float(matrix[0, k]) * low[k]
            above = above + float(matrix[7, k - 1]) * high[k - 1]
        inner_x[0, ey] = below
        inner_x[1, ey] = above
    for side in range(2):
        low = inner_x[side, 0, pl.ds(0, 1), :]
        high = inner_x[side, 1, pl.ds(7, 1), :]
        first[pl.ds(edge + side, 1), :] = place.after_y(high, low)
        second[pl.ds(edge + side, 1), :] = place.after_y(low, high)
    for ex in range(2):
        for a in range(8):
            low = jnp.sum(bottom * tile_of(ex, a, 0), axis=0, keepdims=True)
            high = jnp.sum(top * tile_of(ex, a, 1), axis=0, keepdims=True)
            row = pl.ds(at + ex * 8 + a, 1)
            first[row, :] = place.after_y(high, low)
            second[row, :] = place.after_y(low, high)


def cross_flow(place, ctab, flow, slopes, rows, inv_y, inv_z):
    below, above = rows
    below = (below - float(DERIV[0, 0]) * flow[0]) * jnp.where(place.prev_y, 1.0, 0.0)
    above = (above - float(DERIV[7, 7]) * flow[1]) * jnp.where(place.next_y, 1.0, 0.0)
    grad_y = list(place.join_y(*[along_y(ctab, T_D, tile) for tile in flow]))
    grad_y[0] = grad_y[0] + jnp.where(place.row == 0, below, 0.0)
    grad_y[1] = grad_y[1] + jnp.where(place.row == 7, above, 0.0)
    return [grad_y[ey] * inv_y[ey] + place.join_z(slopes[ey]) * inv_z for ey in range(2)]


def approach_kernel(share, y_first, y_second, ctab, zmat, fields_new, part, grad_z):
    place = Place()

    def step(ch, carry):
        for ex in range(2):
            for a in range(8):
                for ey in range(2):
                    fields_new[ch, ex, a, ey] = got_y_sum(
                        place, share[ch, ex, a, ey], ch, ex, a, ey, y_first, y_second
                    )
        return carry

    lax.fori_loop(0, 4, step, 0)
    grad_z[...] = along_z(fields_new[2].reshape(256, LANES), zmat[0]).reshape(grad_z.shape)
    inv_y = [place.inv_y(ey) for ey in range(2)]
    inv_z = place.inv_z()
    for ex in range(2):
        for a in range(8):
            if (ex, a) in OUTER:
                continue
            flow = [fields_new[1, ex, a, ey] for ey in range(2)]
            rows = inner_along_y(place, y_first, y_second, None, None, ex, a, STEP_V, STEP_EDGE)
            slopes = [grad_z[ex, a, ey] for ey in range(2)]
            both = cross_flow(place, ctab, flow, slopes, rows, inv_y, inv_z)
            part[ex, a, 0], part[ex, a, 1] = both


def advance_kernel(
    begun,
    given,
    y_first,
    y_second,
    x_first,
    x_second,
    inv_diag,
    kap,
    grp,
    ctab,
    zmat,
    fields_new,
    resid,
    own,
    msg,
    grad_z,
    scaled,
    edge,
    part,
):
    place = Place()
    weight = ctab[T_W]

    def before(row, count=8):
        rows = pl.ds(row, count)
        return place.before_x(x_first[rows, :], x_second[rows, :])

    def after(row, count=8):
        rows = pl.ds(row, count)
        return place.after_x(x_first[rows, :], x_second[rows, :])

    fields_new[...] = begun[...]
    part[...] = given[...]
    for ch in range(4):
        for ex, a in OUTER:
            for ey in range(2):
                fields_new[ch, ex, a, ey] = got_x_sum(
                    place, begun[ch, ex, a, ey], ch, ex, ey, x_first, x_second
                )
    for side, (ex, a) in enumerate(OUTER):
        edge[side] = fields_new[2, ex, a]
    edge[...] = along_z(edge[...].reshape(32, LANES), zmat[0]).reshape(edge.shape)
    inv_y = [place.inv_y(ey) for ey in range(2)]
    inv_z = place.inv_z()
    for side, (ex, a) in enumerate(OUTER):
        flow = [fields_new[1, ex, a, ey] for ey in range(2)]
        rows = inner_along_y(place, y_first, y_second, before, after, ex, a, STEP_V, STEP_EDGE)
        slopes = [edge[side, ey] for ey in range(2)]
        both = cross_flow(place, ctab, flow, slopes, rows, inv_y, inv_z)
        part[ex, a, 0], part[ex, a, 1] = both
    slope = [[None, None], [None, None]]
    for ey in range(2):
        for ex in range(2):
            slope[ex][ey] = along_x(DERIV, [fields_new[0, ex, a, ey] for a in range(8)], -1)
        mid = 0.5 * (slope[0][ey][7] + slope[1][ey][0])
        slope[0][ey][7] = mid
        slope[1][ey][0] = mid
        low, high = slope[0][ey][0], slope[1][ey][7]
        inner_low = low - float(DERIV[0, 0]) * fields_new[0, 0, 0, ey] + before(STEP_U + ey * 8)
        inner_high = high - float(DERIV[7, 7]) * fields_new[0, 1, 7, ey] + after(STEP_U + ey * 8)
        slope[0][ey][0] = jnp.where(place.prev_x, 0.5 * inner_low, low)
        slope[1][ey][7] = jnp.where(place.next_x, 0.5 * inner_high, high)
    sums = [[jnp.zeros(TILE, jnp.float32) for _ in range(2)] for _ in range(2)]
    inv_mult = [1.0 / place.mult_tile(ey) for ey in range(2)]
    mass = [weight * place.mult_tile(ey) for ey in range(2)]
    for ex in range(2):
        for a in range(8):
            for ey in range(2):
                div = slope[ex][ey][a] + part[ex, a, ey]
                value = div * (mass[ey] * (place.mult_x(ex, a) * float(-WEIGHTS[a])))
                resid[ex, a, ey] = value
                scaled[ex, a, ey] = value * inv_diag[ex, a, ey] * float(1.0 / THETA)
                sums[ex][ey] = sums[ex][ey] + value * (inv_mult[ey] * place.inv_x(ex, a))
    grad_z[...] = along_z(scaled[...].reshape(256, LANES), zmat[2]).reshape(grad_z.shape)
    tiles = [[[None, None] for _ in range(8)] for _ in range(2)]
    for ex in range(2):
        for ey in range(2):
            images = own_operator(ctab, kap, scaled, grad_z, ex, ey)[1]
            for a in range(8):
                tiles[ex][a][ey] = place.join_z(images[a])
    join_own(place, tiles)
    for ex in range(2):
        for a in range(8):
            for ey in range(2):
                own[ex, a, ey] = tiles[ex][a][ey]
    row = message(place, restricted(place, sums, grp), [])
    blank = jnp.where(place.row == 0, jnp.broadcast_to(row, TILE), 0.0)
    zero = jnp.zeros(TILE, jnp.float32)

    def clear(i, carry):
        msg[i, pl.ds(0, 8), :] = zero
        msg[i, pl.ds(8, 8), :] = blank
        return carry

    lax.fori_loop(0, msg.shape[0], clear, 0)
    for dx, dy, there in neighbours(place):

        @pl.when(there)
        def _():
            to = (place.ix + dx) * place.ny + place.iy + dy
            ex, a = (0, 0) if dx < 0 else (1, 7)
            ey, b = (0, 0) if dy < 0 else (1, 7)
            if dy == 0:
                msg[to, pl.ds(0, 8), :] = own[ex, a, 0]
                msg[to, pl.ds(9, 7), :] = own[ex, a, 1, pl.ds(1, 7), :]
            elif dx == 0:
                for r in range(16):
                    if r != 8:
                        msg[to, pl.ds(r, 1), :] = own[r // 8, r % 8, ey, pl.ds(b, 1), :]
            else:
                msg[to, pl.ds(0, 1), :] = own[ex, a, ey, pl.ds(b, 1), :]


def inner_along_y(place, y_first, y_second, before, after, ex, a, at, edge):
    row = pl.ds(at + ex * 8 + a, 1)
    got_a, got_b = y_first[row, :], y_second[row, :]
    below, above = place.before_y(got_a, got_b), place.after_y(got_a, got_b)
    if before is None:
        return below, above
    if (ex, a) == (0, 0):
        below = below + before(edge, 1)
        above = above + before(edge + 1, 1)
    if (ex, a) == (1, 7):
        below = below + after(edge, 1)
        above = above + after(edge + 1, 1)
    return below, above


def neighbours(place):
    along = ((-1, place.prev_x), (0, None), (1, place.next_x))
    across = ((-1, place.prev_y), (0, None), (1, place.next_y))
    out = []
    for dx, has_x in along:
        for dy, has_y in across:
            if dx == 0 and dy == 0:
                continue
            there = has_y if has_x is None else (has_x if has_y is None else has_x & has_y)
            out.append((dx, dy, there))
    return out


SMOOTH_X, SMOOTH_Y, SMOOTH_EDGE, SMOOTH_ROWS = 16, 16, 32, 40


def turn_smooth_kernel(own, inner_x, y_first, y_second, first, second):
    place = Place()
    sides = []
    for side, (ex, a) in enumerate(((0, 0), (1, 7))):
        row = pl.ds(15 * side, 1)
        got_a, got_b = y_first[row, :], y_second[row, :]
        low = own[ex, a, 0] + jnp.where(place.row == 0, place.before_y(got_a, got_b), 0.0)
        high = own[ex, a, 1] + jnp.where(place.row == 7, place.after_y(got_a, got_b), 0.0)
        sides.append((low, high))
    for ey in range(2):
        rows = pl.ds(ey * 8, 8)
        first[rows, :] = place.after_x(sides[1][ey], sides[0][ey])
        second[rows, :] = place.after_x(sides[0][ey], sides[1][ey])
    first[pl.ds(SMOOTH_EDGE, 8), :] = jnp.zeros(TILE, jnp.float32)
    second[pl.ds(SMOOTH_EDGE, 8), :] = jnp.zeros(TILE, jnp.float32)
    turn_edges(
        place, inner_x, y_first, y_second, first, second, SMOOTH_X, SMOOTH_EDGE, SMOOTH_Y
    )


def restricted(place, sums, grp):
    values = []
    for c in range(NCD):
        acc = jnp.zeros(TILE, jnp.float32)
        for ex in range(2):
            for ey in range(2):
                group = grp[pl.ds((ex + 1) * 4 + ey + 1, 1), :]
                acc = acc + jnp.where(group == float(c), sums[ex][ey], 0.0)
        values.append(total(acc))
    return values


def message(place, own_values, scalars):
    lane = lax.broadcasted_iota(jnp.int32, (1, LANES), 1)
    spot = (place.ix * place.ny + place.iy) % (LANES // NCD)
    after = (spot + 1) % (LANES // NCD)
    row = jnp.zeros((1, LANES), jnp.float32)
    for c, value in enumerate(own_values):
        row = row + jnp.where(lane == spot * NCD + c, value, 0.0)
    for c, value in enumerate(scalars):
        if value is None:
            continue
        row = row + jnp.where(lane == after * NCD + c, value, 0.0)
    return row


def send_to_all(msg, row):
    def send(i, carry):
        msg[i] = row
        return carry

    lax.fori_loop(0, msg.shape[0], send, 0, unroll=msg.shape[0] <= 64)


def cross_image(place, ctab, kap, value, flat, inner, ex, ey):
    slope_y = along_y(ctab, T_K, value)
    turned_y = inner + float(SCALED[0, 0]) * value
    own = kap[pl.ds((ex + 1) * 4 + ey + 1, 1), :] * (slope_y + flat) + sigma_p * value
    beyond = kap[pl.ds((ex + 1) * 4 + 3 * ey, 1), :] * (turned_y + flat) + sigma_p * value
    return own + jnp.where(beyond_y(place, ey), beyond, 0.0), slope_y, turned_y


def beyond_y(place, ey):
    if ey == 0:
        return (place.row == 0) & place.prev_y
    return (place.row == 7) & place.next_y


def ready_kernel(
    own, y_first, y_second, inv_diag, kap, ctab, zmat, image, scaled, part, slope_z
):
    place = Place()
    for ex in range(2):
        for a in range(8):
            for ey in range(2):
                tile = got_y_sum(place, own[ex, a, ey], 0, ex, a, ey, y_first, y_second)
                image[ex, a, ey] = tile
                scaled[ex, a, ey] = tile * inv_diag[ex, a, ey] * float(1.0 / THETA)
    slope_z[...] = along_z(scaled[...].reshape(256, LANES), zmat[2]).reshape(slope_z.shape)
    for ex in range(2):
        for a in range(8):
            if (ex, a) in OUTER:
                continue
            rows = inner_along_y(
                place, y_first, y_second, None, None, ex, a, SMOOTH_Y, SMOOTH_EDGE
            )
            for ey in range(2):
                part[ex, a, ey] = cross_image(
                    place, ctab, kap, scaled[ex, a, ey], slope_z[ex, a, ey], rows[ey], ex, ey
                )[0]


def smooth_kernel(
    begun,
    begun_scaled,
    given,
    y_first,
    y_second,
    x_first,
    x_second,
    inv_diag,
    kap,
    grp,
    extra,
    facts,
    ctab,
    zmat,
    image,
    smoothed,
    msg,
    scaled,
    slope_z,
    edge,
):
    place = Place()
    weight = ctab[T_W]
    corner = float(SCALED[0, 0])

    def before(row, count=8):
        rows = pl.ds(row, count)
        return place.before_x(x_first[rows, :], x_second[rows, :])

    def after(row, count=8):
        rows = pl.ds(row, count)
        return place.after_x(x_first[rows, :], x_second[rows, :])

    image[...] = begun[...]
    scaled[...] = begun_scaled[...]
    for side, (ex, a) in enumerate(OUTER):
        for ey in range(2):
            tile = got_x_sum(place, begun[ex, a, ey], 0, ex, ey, x_first, x_second)
            image[ex, a, ey] = tile
            scaled[ex, a, ey] = tile * inv_diag[ex, a, ey] * float(1.0 / THETA)
            edge[side, ey] = scaled[ex, a, ey]
    edge[...] = along_z(edge[...].reshape(32, LANES), zmat[2]).reshape(edge.shape)
    there_x = (place.prev_x, place.next_x)
    zero = jnp.zeros(TILE, jnp.float32)
    tiles = [[[None, None] for _ in range(8)] for _ in range(2)]
    for ex in range(2):
        a_out = OUTER[ex][1]
        rows = inner_along_y(
            place, y_first, y_second, before, after, ex, a_out, SMOOTH_Y, SMOOTH_EDGE
        )
        for ey in range(2):
            values = [scaled[ex, a, ey] for a in range(8)]
            slopes = along_x(SCALED, values, 1)
            far_row = beyond_y(place, ey)
            beside = kap[pl.ds((ex + 1) * 4 + 3 * ey, 1), :]
            kappa = kap[pl.ds((ex + 1) * 4 + ey + 1, 1), :] + jnp.where(far_row, beside, 0.0)
            for a in range(8):
                if a != a_out:
                    acc = given[ex, a, ey]
                else:
                    value, flat = values[a], edge[ex, ey]
                    acc, slope_y, turned_y = cross_image(
                        place, ctab, kap, value, flat, rows[ey], ex, ey
                    )
                    x_next = 3 * ex
                    get = before if ex == 0 else after
                    turned_x = get(SMOOTH_X + ey * 8) + corner * value
                    side = kap[pl.ds(x_next * 4 + ey + 1, 1), :] * (turned_x + slope_y + flat)
                    far = kap[pl.ds(x_next * 4 + 3 * ey, 1), :] * (turned_x + turned_y + flat)
                    side = side + sigma_p * value
                    side = side + jnp.where(far_row, far + sigma_p * value, zero)
                    acc = acc + jnp.where(there_x[ex], side, zero)
                acc = acc + kappa * slopes[a]
                tiles[ex][a][ey] = place.join_z(acc * (float(WEIGHTS[a]) * weight))
    join_own(place, tiles)
    inv_mult = [1.0 / place.mult_tile(ey) for ey in range(2)]
    sums = [[jnp.zeros(TILE, jnp.float32) for _ in range(2)] for _ in range(2)]
    square = jnp.zeros(TILE, jnp.float32)
    for ex in range(2):
        for a in range(8):
            for ey in range(2):
                value = image[ex, a, ey]
                defect = (value - tiles[ex][a][ey]) * inv_diag[ex, a, ey]
                update = scaled[ex, a, ey]
                result = (
                    float(1.0 + RHO_NEXT * RHO) * update + float(2.0 * RHO_NEXT / DELTA) * defect
                )
                smoothed[ex, a, ey] = result
                weighed = value * (inv_mult[ey] * place.inv_x(ex, a))
                sums[ex][ey] = sums[ex][ey] + weighed
                square = square + weighed * result
    own_sums = restricted(place, sums, grp)
    if msg.shape[1] == 1:
        send_to_all(msg, message(place, own_sums, []) + extra[...])
        return
    slope_z[...] = along_z(smoothed[...].reshape(256, LANES), zmat[2]).reshape(slope_z.shape)
    energy = jnp.zeros(TILE, jnp.float32)
    for ex in range(2):
        for ey in range(2):
            values, images = own_operator(ctab, kap, smoothed, slope_z, ex, ey)
            for a in range(8):
                energy = energy + values[a] * images[a]
                tiles[ex][a][ey] = place.join_z(images[a])
    join_own(place, tiles)
    row = message(place, own_sums, [None, None, total(square), total(energy)]) + extra[...]
    dual = restricted_around(place, tiles, inv_mult, grp)
    out = facts[...]
    out = out + jnp.where(place.row == 0, jnp.broadcast_to(row, TILE), 0.0)
    out = out + jnp.where(place.row == 1, jnp.broadcast_to(dual, TILE), 0.0)
    send_to_all(msg, out)


def restricted_around(place, tiles, inv_mult, grp):
    lane = lax.broadcasted_iota(jnp.int32, (1, LANES), 1)
    weighed = [
        [[tiles[ex][a][ey] * (inv_mult[ey] * place.inv_x(ex, a)) for ey in range(2)] for a in range(8)]
        for ex in range(2)
    ]

    def rows_of(tile, y):
        if y == 0:
            return jnp.where(place.row == 0, tile[0], 0.0)
        if y == 3:
            return jnp.where(place.row == 7, tile[1], 0.0)
        return tile[y - 1]

    there_x = (place.prev_x, None, None, place.next_x)
    there_y = (place.prev_y, None, None, place.next_y)
    by_device = [
        [[jnp.zeros(TILE, jnp.float32) for _ in range(NCD)] for _ in range(3)] for _ in range(3)
    ]
    for x in range(4):
        for y in range(4):
            if x == 0:
                acc = rows_of(weighed[0][0], y)
            elif x == 3:
                acc = rows_of(weighed[1][7], y)
            else:
                acc = rows_of(weighed[x - 1][0], y)
                for a in range(1, 8):
                    acc = acc + rows_of(weighed[x - 1][a], y)
            for there in (there_x[x], there_y[y]):
                if there is not None:
                    acc = jnp.where(there, acc, 0.0)
            group = grp[pl.ds(x * 4 + y, 1), :]
            device = by_device[(x + 1) // 2][(y + 1) // 2]
            for c in range(NCD):
                device[c] = device[c] + jnp.where(group == float(c), acc, 0.0)
    row = jnp.zeros((1, LANES), jnp.float32)
    for dx in range(3):
        for dy in range(3):
            at = ((place.ix + dx - 1) * place.ny + place.iy + dy - 1) * NCD
            for c in range(NCD):
                row = row + jnp.where(lane == at + c, total(by_device[dx][dy][c]), 0.0)
    return row


def coarse_part(place, blocks, got, coarse, grp, at=0):
    lane = lax.broadcasted_iota(jnp.int32, (1, LANES), 1)
    values = [jnp.zeros((1, LANES), jnp.float32) for _ in range(blocks)]
    per = LANES // NCD
    for j in range(blocks):

        def gather(i, acc, j=j):
            return jnp.where(lane // NCD == i, got[j * per + i, pl.ds(at, 1), :], acc)

        values[j] = lax.fori_loop(0, per, gather, values[j], unroll=blocks == 1)

    def solved(dx, dy, c):
        acc = None
        for j in range(blocks):
            term = coarse[pl.ds(((dx * 3 + dy) * NCD + c) * blocks + j, 1), :] * values[j]
            acc = term if acc is None else acc + term
        return jnp.sum(acc, axis=1, keepdims=True)

    return prolonged(place, solved, grp)


def prolonged(place, solved, grp):
    device = [[[solved(dx, dy, c) for c in range(NCD)] for dy in range(3)] for dx in range(3)]
    inv_z = jnp.where(place.low_z | place.high_z, 0.5, 1.0)
    rows = []
    for x in range(4):
        line = []
        for y in range(4):
            group = grp[pl.ds(x * 4 + y, 1), :]
            acc = jnp.zeros((1, LANES), jnp.float32)
            for c in range(NCD):
                acc = acc + jnp.where(
                    group == float(c), device[(x + 1) // 2][(y + 1) // 2][c], 0.0
                )
            line.append(place.join_z(jnp.broadcast_to(acc, TILE)) * inv_z)
        rows.append(line)
    low_y = jnp.where(place.prev_y, 0.5, 1.0)
    high_y = jnp.where(place.next_y, 0.5, 1.0)

    def tile(ex, kind, ey):
        if kind == 1:
            vals = [rows[ex + 1][y] for y in range(4)]
        elif kind == 0:
            scale = place.inv_x(ex, 0)
            vals = [(rows[ex][y] + rows[ex + 1][y]) * scale for y in range(4)]
        else:
            scale = place.inv_x(ex, 7)
            vals = [(rows[ex + 1][y] + rows[ex + 2][y]) * scale for y in range(4)]
        mid = vals[ey + 1]
        low = (vals[ey] + mid) * (low_y if ey == 0 else 0.5)
        high = (mid + vals[ey + 2]) * (high_y if ey == 1 else 0.5)
        return jnp.where(place.row == 0, low, jnp.where(place.row == 7, high, mid))

    return tile


def kind_of(a):
    return 0 if a == 0 else (2 if a == 7 else 1)


def own_operator(ctab, kap, field, slope_z, ex, ey):
    weight = ctab[T_W]
    tiles = [field[ex, a, ey] for a in range(8)]
    slopes = along_x(SCALED, tiles, 1)
    kappa = kap[pl.ds((ex + 1) * 4 + ey + 1, 1), :]
    out = []
    for a in range(8):
        stiff = slopes[a] + along_y(ctab, T_K, tiles[a]) + slope_z[ex, a, ey]
        out.append((kappa * stiff + sigma_p * tiles[a]) * (float(WEIGHTS[a]) * weight))
    return tiles, out


def first_direction_kernel(
    blocks,
    got,
    coarse,
    grp,
    kap,
    inv_diag,
    resid,
    own,
    ctab,
    zmat,
    direction,
    out,
    inner_x,
    first,
    second,
    extra,
    slope_z,
    image,
):
    place = Place()
    inv_mult = [1.0 / place.mult_tile(ey) for ey in range(2)]
    part = coarse_part(place, blocks, got, coarse, grp, 8)
    image[...] = own[...]
    for dx, dy, there in neighbours(place):

        @pl.when(there)
        def _():
            frm = (place.ix + dx) * place.ny + place.iy + dy
            ex, a = (0, 0) if dx < 0 else (1, 7)
            ey, b = (0, 0) if dy < 0 else (1, 7)
            edge = place.row == b
            if dy == 0:
                low = got[frm, pl.ds(0, 8), :]
                high = jnp.where(
                    place.row == 0, pltpu.roll(low, 1, 0), got[frm, pl.ds(8, 8), :]
                )
                image[ex, a, 0] = image[ex, a, 0] + low
                image[ex, a, 1] = image[ex, a, 1] + high
            elif dx == 0:
                for r in range(16):
                    line = got[frm, pl.ds(7 if r == 8 else r, 1), :]
                    tile = image[r // 8, r % 8, ey]
                    image[r // 8, r % 8, ey] = tile + jnp.where(edge, line, 0.0)
            else:
                line = got[frm, pl.ds(0, 1), :]
                image[ex, a, ey] = image[ex, a, ey] + jnp.where(edge, line, 0.0)

    energy = jnp.zeros(TILE, jnp.float32)
    for ex in range(2):
        for ey in range(2):
            kinds = [part(ex, kind, ey) for kind in range(3)]
            for a in range(8):
                known = resid[ex, a, ey]
                inverse = inv_diag[ex, a, ey]
                defect = (known - image[ex, a, ey]) * inverse
                value = (
                    float((1.0 + RHO_NEXT * RHO) / THETA) * (known * inverse)
                    + float(2.0 * RHO_NEXT / DELTA) * defect
                    + kinds[kind_of(a)]
                )
                direction[ex, a, ey] = value
                scale = place.inv_x(ex, a)
                energy = energy + value * known * (inv_mult[ey] * scale)
    slope_z[...] = along_z(direction[...].reshape(256, LANES), zmat[2]).reshape(slope_z.shape)
    curvature = jnp.zeros(TILE, jnp.float32)
    tiles = [[[None, None] for _ in range(8)] for _ in range(2)]
    for ex in range(2):
        for ey in range(2):
            values, images = own_operator(ctab, kap, direction, slope_z, ex, ey)
            for a in range(8):
                curvature = curvature + values[a] * images[a]
                tiles[ex][a][ey] = place.join_z(images[a])
    join_own(place, tiles)
    for ex in range(2):
        for a in range(8):
            for ey in range(2):
                out[ex, a, ey] = tiles[ex][a][ey]
    store_y_faces(place, out, first, second, (), 0)
    first[pl.ds(SMOOTH_EDGE, 8), :] = jnp.zeros(TILE, jnp.float32)
    second[pl.ds(SMOOTH_EDGE, 8), :] = jnp.zeros(TILE, jnp.float32)

    def tile_of(ex, a, ey):
        return tiles[ex][a][ey] * inv_diag[ex, a, ey] * float(1.0 / THETA)

    def column_of(ex, ey):
        return [tile_of(ex, a, ey) for a in range(8)]

    store_inner(
        place, SCALED, ctab[T_KBOTTOM], ctab[T_KTOP], column_of, tile_of, inner_x, first, second,
        SMOOTH_Y, SMOOTH_EDGE,
    )
    extra[...] = message(place, [], [total(energy), total(curvature)])


def gathered_scalars(got, count):
    lane = lax.broadcasted_iota(jnp.int32, (1, LANES), 1)
    per = LANES // NCD
    sums = []
    for c in range(count):
        acc = jnp.zeros((1, LANES), jnp.float32)

        def gather(i, acc, c=c):
            return acc + jnp.where(lane == ((i + 1) % per) * NCD + c, got[i], 0.0)

        acc = lax.fori_loop(0, got.shape[0], gather, acc, unroll=got.shape[0] <= per)
        sums.append(jnp.sum(acc, axis=1, keepdims=True))
    return sums


def second_direction_kernel(
    blocks,
    got,
    coarse,
    grp,
    kap,
    resid,
    direction,
    image,
    smoothed,
    ctab,
    zmat,
    following,
    known,
    msg,
    slope_z,
):
    place = Place()
    inv_mult = [1.0 / place.mult_tile(ey) for ey in range(2)]
    part = coarse_part(place, blocks, got, coarse, grp)
    energy, curvature = gathered_scalars(got, 2)
    step = energy / curvature
    lane = lax.broadcasted_iota(jnp.int32, (1, LANES), 1)
    known[...] = jnp.where(lane == 0, energy, jnp.where(lane == 1, curvature, 0.0))
    energy_next = jnp.zeros(TILE, jnp.float32)
    cross = jnp.zeros(TILE, jnp.float32)
    for ex in range(2):
        for ey in range(2):
            kinds = [part(ex, kind, ey) for kind in range(3)]
            for a in range(8):
                value = direction[ex, a, ey] - step * (smoothed[ex, a, ey] + kinds[kind_of(a)])
                following[ex, a, ey] = value
                weighed = value * (inv_mult[ey] * place.inv_x(ex, a))
                was = image[ex, a, ey]
                energy_next = energy_next + weighed * (resid[ex, a, ey] - step * was)
                cross = cross + weighed * was
    slope_z[...] = along_z(following[...].reshape(256, LANES), zmat[2]).reshape(slope_z.shape)
    square = jnp.zeros(TILE, jnp.float32)
    for ex in range(2):
        for ey in range(2):
            values, images = own_operator(ctab, kap, following, slope_z, ex, ey)
            for a in range(8):
                square = square + values[a] * images[a]
    send_to_all(msg, message(place, [], [total(energy_next), total(square), total(cross)]))


def pressure_kernel(got, known, direction, following, pressure):
    energy = known[:, pl.ds(0, 1)]
    curvature = known[:, pl.ds(1, 1)]
    energy_next, square, cross = gathered_scalars(got, 3)
    ratio = energy_next / energy
    step = energy / curvature
    step_next = energy_next / (square + 2.0 * ratio * cross + ratio * ratio * curvature)
    weight_old = step + step_next * ratio
    for ex in range(2):
        for a in range(8):
            for ey in range(2):
                pressure[ex, a, ey] = (
                    weight_old * direction[ex, a, ey] + step_next * following[ex, a, ey]
                )


def coarse_energy(place, got, values, kappa, number):
    lane, row = place.lane, place.row
    for ex in range(2):
        for gx in range(8):
            own = jnp.zeros((1, LANES), jnp.float32)
            group = jnp.zeros((1, LANES), jnp.float32)
            spot = lane[0:1] // 32
            for gy in range(4):
                line = got[gx * 4 + gy, pl.ds(2 + ex, 1), :]
                own = jnp.where(spot == gy, line, own)
                group = jnp.where(spot == (gy + 1) % 4, line, group)
            kappa[ex, pl.ds(gx, 1), :] = own
            number[ex, pl.ds(gx, 1), :] = group
    grid = [jnp.zeros(TILE, jnp.float32) for _ in range(2)]
    numbers = [pltpu.roll(number[ex], 96, 1) for ex in range(2)]
    for q in range(4):
        for c in range(NCD):
            mine = jnp.where(lane == row * 16 + q * 4 + c, values, 0.0)
            mine = jnp.sum(mine, axis=1, keepdims=True)
            for ex in range(2):
                chosen = (lane // 32 == q) & (numbers[ex] == float(c))
                grid[ex] = jnp.where(chosen, mine, grid[ex])

    def ends_y(v):
        low = jnp.where(lane >= 16, 0.5 * (v + pltpu.roll(v, 16, 1)), v)
        return low, v, jnp.where(lane < 112, 0.5 * (v + pltpu.roll(v, 112, 1)), v)

    def ends_z(v):
        low = jnp.where(lane % 16 > 0, 0.5 * (v + pltpu.roll(v, 1, 1)), v)
        return low, v, jnp.where(lane % 16 < 15, 0.5 * (v + pltpu.roll(v, 127, 1)), v)

    low = jnp.where(row > 0, 0.5 * (grid[0] + pltpu.roll(grid[1], 1, 0)), grid[0])
    mid = 0.5 * (grid[0] + grid[1])
    high = jnp.where(row < 7, 0.5 * (grid[1] + pltpu.roll(grid[0], 7, 0)), grid[1])
    mass = [float(WEIGHTS[0]), float(np.sum(WEIGHTS[1:7])), float(WEIGHTS[7])]
    links = (
        (0, 1, -float(np.sum(STIFF[0, 1:7]))),
        (0, 2, -float(STIFF[0, 7])),
        (1, 2, -float(np.sum(STIFF[7, 1:7]))),
    )
    energy = jnp.zeros(TILE, jnp.float32)
    for ex, line in enumerate(((low, grid[0], mid), (mid, grid[1], high))):
        nodes = [[ends_z(v) for v in ends_y(w)] for w in line]
        stiff = jnp.zeros(TILE, jnp.float32)
        square = jnp.zeros(TILE, jnp.float32)
        for i in range(3):
            for j in range(3):
                for k, l, weight in links:
                    factor = weight * mass[i] * mass[j]
                    for first, second in (
                        (nodes[k][i][j], nodes[l][i][j]),
                        (nodes[i][k][j], nodes[i][l][j]),
                        (nodes[i][j][k], nodes[i][j][l]),
                    ):
                        gap = first - second
                        stiff = stiff + (factor * gap) * gap
                for k in range(3):
                    value = nodes[i][j][k]
                    square = square + (mass[i] * mass[j] * mass[k] * value) * value
        energy = energy + kappa[ex] * stiff + sigma_p * square
    return total(energy)


def finish_kernel(
    got, grp, direction, smoothed, pressure, matrix, kappa, number
):
    place = Place()
    per = LANES // NCD
    row_lane = lax.broadcasted_iota(jnp.int32, (1, LANES), 1)
    rest = jnp.zeros((1, LANES), jnp.float32)
    dual = jnp.zeros((1, LANES), jnp.float32)
    sums = [jnp.zeros((1, LANES), jnp.float32) for _ in range(4)]
    for i in range(per):
        line = got[i, pl.ds(0, 1), :]
        rest = jnp.where(row_lane // NCD == i, line, rest)
        dual = dual + got[i, pl.ds(1, 1), :]
        for c in range(4):
            sums[c] = sums[c] + jnp.where(row_lane == ((i + 1) % per) * NCD + c, line, 0.0)
        matrix[pl.ds(i * NCD, NCD), :] = got[i, pl.ds(4, NCD), :]
    energy, curvature, square, self_energy = [
        jnp.sum(value, axis=1, keepdims=True) for value in sums
    ]
    values = lax.dot_general(
        jnp.broadcast_to(rest, TILE),
        matrix[...],
        (((1,), (1,)), ((), ())),
        precision=lax.Precision.HIGHEST,
        preferred_element_type=jnp.float32,
    )
    line = values[0:1]
    cross = square + jnp.sum(line * rest, axis=1, keepdims=True)
    both = self_energy + 2.0 * jnp.sum(line * dual, axis=1, keepdims=True)
    both = both + coarse_energy(place, got, values, kappa, number)
    step = energy / curvature
    energy_next = step * step * cross - energy
    ratio = energy_next / energy
    with_image = curvature - step * cross
    with_itself = curvature - 2.0 * step * cross + step * step * both
    step_next = energy_next / (
        with_itself + 2.0 * ratio * with_image + ratio * ratio * curvature
    )
    old = step + step_next * (1.0 + ratio)
    new = -step_next * step

    def solved(dx, dy, c):
        at = ((place.ix + dx - 1) * place.ny + place.iy + dy - 1) * NCD + c
        return jnp.sum(jnp.where(row_lane == at, line, 0.0), axis=1, keepdims=True)

    part = prolonged(place, masked(place, solved), grp)
    for ex in range(2):
        for ey in range(2):
            kinds = [part(ex, kind, ey) for kind in range(3)]
            for a in range(8):
                pressure[ex, a, ey] = old * direction[ex, a, ey] + new * (
                    smoothed[ex, a, ey] + kinds[kind_of(a)]
                )


def masked(place, solved):
    there_x = (place.prev_x, None, place.next_x)
    there_y = (place.prev_y, None, place.next_y)

    def value(dx, dy, c):
        out = solved(dx, dy, c)
        for there in (there_x[dx], there_y[dy]):
            if there is not None:
                out = jnp.where(there, out, 0.0)
        return out

    return value


def call(body, outs, scratch=(), **more):
    return pl.pallas_call(
        body,
        out_shape=[jax.ShapeDtypeStruct(shape, jnp.float32) for shape in outs],
        scratch_shapes=[
            pltpu.VMEM(shape, jnp.float32) if isinstance(shape, tuple) else shape
            for shape in scratch
        ],
        **more,
        compiler_params=pltpu.CompilerParams(vmem_limit_bytes=24 * 1024 * 1024),
    )


def swap(first, second, axis):
    count = lax.axis_size(axis)
    first_pairs = [(i, i ^ 1) for i in range(count) if i ^ 1 < count]
    second_pairs = [(i, ((i + 1) ^ 1) - 1) for i in range(1, count) if ((i + 1) ^ 1) - 1 < count]
    second_got = lax.ppermute(second, axis, second_pairs)
    return lax.ppermute(first, axis, first_pairs), second_got


def per_device(fields, viscosity, inv_density, elem_group, coarse_inverse):
    length = fields.shape[5]
    elems_z = length // NODES
    devices = lax.axis_size("gx") * lax.axis_size("gy")
    blocks = coarse_inverse.shape[1] // LANES
    pack_rows = -(-(8 + NCD * blocks) // 8) * 8
    tiles_np, mats_np = constant_tables(elems_z)
    ctab, zmat = jnp.asarray(tiles_np), jnp.asarray(mats_np)
    one = fields.shape[1:]
    four = fields.shape
    faces = (64, LANES)
    xf_shape = (2, 4, 2, 8, LANES)
    inner_shape = (2, 2, 8, LANES)
    y_shape, x_shape = (STEP_PACK + pack_rows, LANES), (STEP_PACK + 3 * pack_rows, LANES)
    smooth_shape = (SMOOTH_ROWS, LANES)
    rows = (devices, 1, LANES)
    grid_fits = (
        blocks == 1
        and lax.axis_size("gx") == 8
        and lax.axis_size("gy") * fields.shape[3] * elems_z == LANES
    )

    def exchange_all(msg):
        return lax.all_to_all(msg, BOTH, 0, 0, tiled=True)

    beside = pl.CostEstimate(flops=10**7, bytes_accessed=10**6, transcendentals=0)
    summed, xf, first, second = call(
        mass_kernel,
        [four, xf_shape, faces, faces],
    )(fields)
    pack, facts = call(
        pack_kernel,
        [(pack_rows, LANES), TILE],
        cost_estimate=beside,
    )(inv_density, elem_group, coarse_inverse)
    y_got = swap(first, second, "gy")
    first, second = call(turn_faces_kernel, [faces, faces])(xf, *y_got)
    x_got = swap(first, second, "gx")
    begun, given = call(prepare_kernel, [four, four], [four, four], cost_estimate=beside)(
        summed, viscosity, *y_got, ctab, zmat
    )
    edge_shape = (4, 2, 2, 8, LANES)
    share, xf, inner_x, first, second = call(
        functools.partial(rhs_kernel, pack_rows),
        [four, xf_shape, inner_shape, y_shape, y_shape],
        [four, edge_shape, edge_shape, edge_shape],
    )(begun, given, viscosity, pack, *x_got, ctab, zmat)
    y_got = swap(first, second, "gy")
    first, second = call(functools.partial(turn_step_kernel, pack_rows), [x_shape, x_shape])(
        xf, inner_x, pack, *y_got
    )
    x_got = swap(first, second, "gx")
    inv_diag, kap, grp, coarse = call(
        functools.partial(setup_kernel, pack_rows, blocks),
        [one, (16, LANES), (16, LANES), (9 * NCD * blocks, LANES)],
    )(pack, *y_got, *x_got, ctab)
    begun, given = call(approach_kernel, [four, one], [one], cost_estimate=beside)(
        share, *y_got, ctab, zmat
    )
    side_shape = (2, 2, 8, LANES)
    fields_new, resid, own, msg = call(
        advance_kernel,
        [four, one, one, (devices, 16, LANES)],
        [one, one, side_shape, one],
    )(begun, given, *y_got, *x_got, inv_diag, kap, grp, ctab, zmat)
    got = exchange_all(msg)
    direction, own, inner_x, first, second, extra = call(
        functools.partial(first_direction_kernel, blocks),
        [one, one, inner_shape, smooth_shape, smooth_shape, (1, LANES)],
        [one, one],
    )(got, coarse, grp, kap, inv_diag, resid, own, ctab, zmat)
    y_got = swap(first, second, "gy")
    first, second = call(turn_smooth_kernel, [smooth_shape, smooth_shape])(own, inner_x, *y_got)
    x_got = swap(first, second, "gx")
    begun, begun_scaled, given = call(
        ready_kernel, [one, one, one], [one], cost_estimate=beside
    )(own, *y_got, inv_diag, kap, ctab, zmat)
    image, image_smoothed, msg = call(
        smooth_kernel,
        [one, one, (devices, 8, LANES) if grid_fits else rows],
        [one, one, side_shape],
    )(
        begun, begun_scaled, given, *y_got, *x_got, inv_diag, kap, grp, extra, facts, ctab, zmat
    )
    got = exchange_all(msg)
    if grid_fits:
        (pressure,) = call(
            finish_kernel, [one], [(LANES, LANES), (2,) + TILE, (2,) + TILE]
        )(got, grp, direction, image_smoothed)
        return (fields_new, pressure)
    following, known, msg = call(
        functools.partial(second_direction_kernel, blocks), [one, (1, LANES), rows], [one]
    )(got, coarse, grp, kap, resid, direction, image, image_smoothed, ctab, zmat)
    got = exchange_all(msg)
    (pressure,) = call(pressure_kernel, [one])(got, known, direction, following)
    return (fields_new, pressure)


def solution(mesh):
    placed = (
        P(None, "gx", None, "gy", None, None),
        P("gx", None, "gy", None, None),
        P("gx", "gy", None),
        P("gx", "gy", None),
        P(("gx", "gy"), None),
    )
    return jax.shard_map(
        per_device,
        mesh=mesh,
        in_specs=placed,
        out_specs=(P(None, "gx", None, "gy", None, None), P("gx", None, "gy", None, None)),
        check_vma=False,
    )
```

```python
import functools

import jax
import jax.numpy as jnp
import ml_dtypes
import numpy as np
from jax import lax
from jax.experimental import pallas as pl
from jax.experimental.pallas import tpu as pltpu
from jax.sharding import PartitionSpec as P

NCD = 4
NODES = 8
LANES = 128
TILE = (8, 128)
BOTH = ("gx", "gy")

dt_step = 0.01
sigma_p = 4.0
prandtl = 0.7
cheb_ratio = 0.1


def tables():
    points = np.array(
        [
            -1.0,
            -0.8717401485096066,
            -0.5917001814331423,
            -0.2092992179024789,
            0.2092992179024789,
            0.5917001814331423,
            0.8717401485096066,
            1.0,
        ]
    )
    weights = np.array(
        [
            1.0 / 28.0,
            0.2107042271435061,
            0.3411226924835044,
            0.4124587946587038,
            0.4124587946587038,
            0.3411226924835044,
            0.2107042271435061,
            1.0 / 28.0,
        ]
    )
    identity = np.eye(8)
    differ = points[:, None] - points[None, :] + identity
    barycentric = 1.0 / np.prod(differ, axis=1)
    offdiag = barycentric[None, :] / barycentric[:, None] / differ * (1.0 - identity)
    derivative = offdiag - identity * np.sum(offdiag, axis=1)[:, None]
    mass_one = identity * weights[None, :]
    stiff_one = derivative.T @ mass_one @ derivative
    stiff_three = (
        np.kron(np.kron(stiff_one, mass_one), mass_one)
        + np.kron(np.kron(mass_one, stiff_one), mass_one)
        + np.kron(np.kron(mass_one, mass_one), stiff_one)
    )
    three_diag = np.sum(stiff_three * np.eye(512), axis=1)
    spectral_bound = float(np.max(np.sum(np.abs(stiff_three), axis=1) / three_diag))
    return (derivative, weights, stiff_one, spectral_bound)


DERIV, WEIGHTS, STIFF, BOUND = tables()
SCALED = STIFF / WEIGHTS[:, None]
LINE = np.diag(STIFF) / WEIGHTS
THETA = 0.5 * (BOUND + cheb_ratio * BOUND)
DELTA = 0.5 * (BOUND - cheb_ratio * BOUND)
RHO = DELTA / THETA
RHO_NEXT = 1.0 / (2.0 * THETA / DELTA - RHO)


def constant_tables(elems_z):
    def turned(matrix):
        rows = np.arange(8)
        return [np.repeat(matrix[rows, (rows - s) % 8][:, None], LANES, 1) for s in range(8)]

    wz = np.tile(WEIGHTS, elems_z)
    kz = np.tile(LINE, elems_z)
    tiles = turned(DERIV) + turned(DERIV.T) + turned(SCALED)
    tiles += [WEIGHTS[:, None] * wz[None, :], LINE[:, None] + kz[None, :]]
    for matrix in (DERIV, SCALED):
        for node in (7, 0):
            inner = matrix[node] * (np.arange(8) != node)
            tiles.append(np.repeat(inner[:, None], LANES, 1))
    eye = np.eye(elems_z)
    mats = [np.kron(eye, DERIV.T), np.kron(eye, DERIV), np.kron(eye, SCALED.T)]
    halves = []
    for mat in mats:
        high = mat.astype(ml_dtypes.bfloat16)
        low = (mat - high.astype(np.float64)).astype(ml_dtypes.bfloat16)
        both = np.concatenate([high, low], 1)
        halves.append(np.concatenate([both, both], 0))
    return np.stack(tiles).astype(np.float32), np.stack(halves)


T_D, T_DT, T_K, T_W, T_LINE = 0, 8, 16, 24, 25
T_TOP, T_BOTTOM, T_KTOP, T_KBOTTOM = 26, 27, 28, 29


class Place:
    def __init__(self):
        self.ix = lax.axis_index("gx")
        self.iy = lax.axis_index("gy")
        self.nx = lax.axis_size("gx")
        self.ny = lax.axis_size("gy")
        self.even_x = self.ix % 2 == 0
        self.even_y = self.iy % 2 == 0
        self.row = lax.broadcasted_iota(jnp.int32, TILE, 0)
        self.lane = lax.broadcasted_iota(jnp.int32, TILE, 1)
        self.low_z = (self.lane % 8 == 0) & (self.lane > 0)
        self.high_z = (self.lane % 8 == 7) & (self.lane < LANES - 1)
        self.prev_x = self.ix > 0
        self.next_x = self.ix < self.nx - 1
        self.prev_y = self.iy > 0
        self.next_y = self.iy < self.ny - 1

    def mult_tile(self, ey):
        along_z = 1.0 + jnp.where(self.low_z | self.high_z, 1.0, 0.0)
        low = 1.0 if ey == 1 else jnp.where(self.prev_y, 1.0, 0.0)
        high = 1.0 if ey == 0 else jnp.where(self.next_y, 1.0, 0.0)
        along_y = 1.0 + jnp.where(self.row == 0, low, jnp.where(self.row == 7, high, 0.0))
        return along_y * along_z

    def inv_x(self, ex, a):
        if a == 0:
            return 0.5 if ex == 1 else jnp.where(self.prev_x, 0.5, 1.0)
        if a == 7:
            return 0.5 if ex == 0 else jnp.where(self.next_x, 0.5, 1.0)
        return 1.0

    def mult_x(self, ex, a):
        if a == 0:
            return 2.0 if ex == 1 else jnp.where(self.prev_x, 2.0, 1.0)
        if a == 7:
            return 2.0 if ex == 0 else jnp.where(self.next_x, 2.0, 1.0)
        return 1.0

    def share_x(self, ex, a):
        if (ex, a) == (0, 0):
            return jnp.where(self.prev_x, 0.5, 1.0)
        if (ex, a) == (1, 7):
            return jnp.where(self.next_x, 0.5, 1.0)
        return 1.0

    def share_y(self, ey):
        if ey == 0:
            return jnp.where((self.row == 0) & self.prev_y, 0.5, 1.0)
        return jnp.where((self.row == 7) & self.next_y, 0.5, 1.0)

    def inv_y(self, ey):
        low = 0.5 if ey == 1 else jnp.where(self.prev_y, 0.5, 1.0)
        high = 0.5 if ey == 0 else jnp.where(self.next_y, 0.5, 1.0)
        return jnp.where(self.row == 0, low, jnp.where(self.row == 7, high, 1.0))

    def inv_z(self):
        return jnp.where(self.low_z | self.high_z, 0.5, 1.0)

    def join_z(self, t):
        up = pltpu.roll(t, LANES - 1, 1)
        down = pltpu.roll(t, 1, 1)
        return t + jnp.where(self.high_z, up, jnp.where(self.low_z, down, 0.0))

    def to_low(self, below):
        return jnp.where(self.row == 0, pltpu.roll(below, 1, 0), 0.0)

    def to_high(self, above):
        return jnp.where(self.row == 7, pltpu.roll(above, 7, 0), 0.0)

    def join_y(self, below, above):
        return below + self.to_high(above), above + self.to_low(below)

    def before_x(self, first, second):
        return jnp.where(self.even_x, second, first)

    def after_x(self, first, second):
        return jnp.where(self.even_x, first, second)

    def before_y(self, first, second):
        return jnp.where(self.even_y, second, first)

    def after_y(self, first, second):
        return jnp.where(self.even_y, first, second)


def along_x(matrix, tiles, sign):
    even = [tiles[a] + tiles[7 - a] for a in range(4)]
    odd = [tiles[a] - tiles[7 - a] for a in range(4)]
    out = [None] * 8
    for i in range(4):
        plus, minus = None, None
        for a in range(4):
            p = float(0.5 * (matrix[i, a] + matrix[i, 7 - a])) * even[a]
            m = float(0.5 * (matrix[i, a] - matrix[i, 7 - a])) * odd[a]
            plus = p if plus is None else plus + p
            minus = m if minus is None else minus + m
        out[i] = plus + minus
        out[7 - i] = minus - plus if sign < 0 else plus - minus
    return out


def along_y(ctab, base, tile):
    acc = ctab[base] * tile
    for s in range(1, 8):
        acc = acc + ctab[base + s] * pltpu.roll(tile, s, 0)
    return acc


def exact_dot(rows, matrix):
    return jnp.dot(
        rows, matrix, precision=lax.Precision.HIGHEST, preferred_element_type=jnp.float32
    )


def along_z(rows, matrix):
    high = rows.astype(jnp.bfloat16)
    low = (rows - high.astype(jnp.float32)).astype(jnp.bfloat16)
    both = jnp.dot(
        jnp.concatenate([high, low], axis=1), matrix, preferred_element_type=jnp.float32
    )
    return both[:, :LANES] + both[:, LANES:]


def total(tile):
    return jnp.sum(jnp.sum(tile, axis=0, keepdims=True), axis=1, keepdims=True)


def store_y_faces(place, field, first_out, second_out, lead, at):
    for ex in range(2):
        for a in range(8):
            low = field[lead + (ex, a, 0, pl.ds(0, 1), slice(None))]
            high = field[lead + (ex, a, 1, pl.ds(7, 1), slice(None))]
            row = at + ex * 8 + a
            first_out[pl.ds(row, 1), :] = place.after_y(high, low)
            second_out[pl.ds(row, 1), :] = place.after_y(low, high)


def join_own(place, tiles):
    for ex in range(2):
        for a in range(8):
            tiles[ex][a] = list(place.join_y(*tiles[ex][a]))
    for ey in range(2):
        both = tiles[0][7][ey] + tiles[1][0][ey]
        tiles[0][7][ey] = both
        tiles[1][0][ey] = both


def weight_of(node):
    edge = jnp.minimum(node, 7 - node)
    value = jnp.where(edge == 2, float(WEIGHTS[2]), float(WEIGHTS[3]))
    return jnp.where(
        edge == 0, float(WEIGHTS[0]), jnp.where(edge == 1, float(WEIGHTS[1]), value)
    )


def mass_kernel(fields, out, xf, first, second):
    place = Place()
    weight = weight_of(place.row) * weight_of(place.lane % NODES)
    for ch in range(4):
        tiles = [
            [
                [
                    place.join_z(fields[ch, ex, a, ey] * (float(WEIGHTS[a]) * weight))
                    for ey in range(2)
                ]
                for a in range(8)
            ]
            for ex in range(2)
        ]
        join_own(place, tiles)
        for ex in range(2):
            for a in range(8):
                for ey in range(2):
                    out[ch, ex, a, ey] = tiles[ex][a][ey]
        for ey in range(2):
            xf[0, ch, ey] = tiles[0][0][ey]
            xf[1, ch, ey] = tiles[1][7][ey]
        store_y_faces(place, out, first, second, (ch,), ch * 16)


def turn_faces(place, xf, y_first, y_second, first, second):
    for ch in range(4):
        sides = []
        for side in range(2):
            row = pl.ds(ch * 16 + 15 * side, 1)
            got_a, got_b = y_first[row, :], y_second[row, :]
            low = xf[side, ch, 0] + jnp.where(place.row == 0, place.before_y(got_a, got_b), 0.0)
            high = xf[side, ch, 1] + jnp.where(place.row == 7, place.after_y(got_a, got_b), 0.0)
            sides.append((low, high))
        for ey in range(2):
            rows = pl.ds(ch * 16 + ey * 8, 8)
            first[rows, :] = place.after_x(sides[1][ey], sides[0][ey])
            second[rows, :] = place.after_x(sides[0][ey], sides[1][ey])


def turn_faces_kernel(pack_rows, xf, pack, y_first, y_second, first, second):
    turn_faces(Place(), xf, y_first, y_second, first, second)
    first[pl.ds(64, pack_rows), :] = pack[...]
    second[pl.ds(64, pack_rows), :] = pack[...]


def turn_edges(place, inner_x, y_first, y_second, first, second, at, edge, inner_y):
    sides = []
    for side in range(2):
        row = pl.ds(edge + side, 1)
        got_a, got_b = y_first[row, :], y_second[row, :]
        low = inner_x[side, 0] + jnp.where(place.row == 0, place.before_y(got_a, got_b), 0.0)
        high = inner_x[side, 1] + jnp.where(place.row == 7, place.after_y(got_a, got_b), 0.0)
        sides.append((low, high))
    for ey in range(2):
        rows = pl.ds(at + ey * 8, 8)
        first[rows, :] = place.after_x(sides[1][ey], sides[0][ey])
        second[rows, :] = place.after_x(sides[0][ey], sides[1][ey])
    for k, pick in enumerate((place.before_y, place.after_y)):
        sides = []
        for side in range(2):
            row = pl.ds(inner_y + 15 * side, 1)
            sides.append(pick(y_first[row, :], y_second[row, :]))
        row = pl.ds(edge + k, 1)
        first[row, :] = place.after_x(sides[1], sides[0])
        second[row, :] = place.after_x(sides[0], sides[1])


STEP_U, STEP_V, STEP_EDGE, STEP_PACK = 64, 64, 80, 88


def turn_step_kernel(xf, inner_x, y_first, y_second, first, second):
    place = Place()
    turn_faces(place, xf, y_first, y_second, first, second)
    first[pl.ds(STEP_EDGE, 8), :] = jnp.zeros(TILE, jnp.float32)
    second[pl.ds(STEP_EDGE, 8), :] = jnp.zeros(TILE, jnp.float32)
    turn_edges(place, inner_x, y_first, y_second, first, second, STEP_U, STEP_EDGE, STEP_V)


def setup_kernel(
    pack_rows,
    blocks,
    pack,
    x_first,
    x_second,
    y_first,
    y_second,
    ctab,
    inv_diag,
    kap,
    grp,
    coarse,
    compact,
    spread,
):
    place = Place()
    beside = pl.ds(64, pack_rows)
    packs = [[None] * 3 for _ in range(3)]
    packs[0][1] = place.before_x(x_first[beside, :], x_second[beside, :])
    packs[1][1] = pack[...]
    packs[2][1] = place.after_x(x_first[beside, :], x_second[beside, :])
    for dx in range(3):
        rows = pl.ds(STEP_PACK + dx * pack_rows, pack_rows)
        packs[dx][0] = place.before_y(y_first[rows, :], y_second[rows, :])
        packs[dx][2] = place.after_y(y_first[rows, :], y_second[rows, :])
    compact[...] = jnp.zeros(compact.shape, jnp.float32)
    for dx in range(3):
        for dy in range(3):
            at = (dx * 3 + dy) * NCD * blocks
            coarse[pl.ds(at, NCD * blocks), :] = packs[dx][dy][1 : 1 + NCD * blocks]
            compact[pl.ds(dx * 3 + dy, 1), :] = packs[dx][dy][0:1]
    elems = LANES // NODES
    lane = lax.broadcasted_iota(jnp.int32, (LANES, LANES), 1)
    source = lax.broadcasted_iota(jnp.int32, (LANES, LANES), 0)
    for k in range(8):
        spot = (source == k * elems + lane // NODES).astype(jnp.float32)
        spread[k] = exact_dot(compact[...], spot)
    there_x = [jnp.where(place.prev_x, 1.0, 0.0), 1.0, jnp.where(place.next_x, 1.0, 0.0)]
    there_y = [jnp.where(place.prev_y, 1.0, 0.0), 1.0, jnp.where(place.next_y, 1.0, 0.0)]

    def element_row(base, u, v):
        device = (u // 2) * 3 + v // 2
        return spread[base + (u % 2) * 2 + v % 2, pl.ds(device, 1), :]

    for x in range(4):
        for y in range(4):
            kap[pl.ds(x * 4 + y, 1), :] = element_row(0, x + 1, y + 1)
            grp[pl.ds(x * 4 + y, 1), :] = element_row(4, x + 1, y + 1)
    kappa = [
        [
            place.join_z(jnp.broadcast_to(element_row(0, u + 1, v + 1), TILE))
            for v in range(4)
        ]
        for u in range(4)
    ]
    count_z = 1.0 + jnp.where(place.low_z | place.high_z, 1.0, 0.0)
    weight = ctab[T_W]
    line = ctab[T_LINE]

    def pick(values, ey):
        low = values[ey] + values[ey + 1]
        high = values[ey + 1] + values[ey + 2]
        return jnp.where(place.row == 0, low, jnp.where(place.row == 7, high, values[ey + 1]))

    for ex in range(2):
        for kind in range(3):
            us = {0: (ex, ex + 1), 1: (ex + 1,), 2: (ex + 1, ex + 2)}[kind]
            sums, counts = [], []
            for v in range(4):
                acc, num = None, 0.0
                for u in us:
                    acc = kappa[u][v] if acc is None else acc + kappa[u][v]
                    num = num + there_x[(u + 1) // 2]
                sums.append(acc)
                counts.append(num * there_y[(v + 1) // 2])
            for ey in range(2):
                kappa_sum = pick(sums, ey)
                mult = pick(counts, ey) * count_z
                for a in {0: (0,), 1: range(1, 7), 2: (7,)}[kind]:
                    diag = (float(LINE[a]) + line) * kappa_sum + sigma_p * mult
                    inv_diag[ex, a, ey] = 1.0 / (diag * (float(WEIGHTS[a]) * weight))


OUTER = ((0, 0), (1, 7))


def got_y_sum(place, tile, ch, ex, a, ey, y_first, y_second):
    row = pl.ds(ch * 16 + ex * 8 + a, 1)
    got_a, got_b = y_first[row, :], y_second[row, :]
    if ey == 0:
        tile = tile + jnp.where(place.row == 0, place.before_y(got_a, got_b), 0.0)
    else:
        tile = tile + jnp.where(place.row == 7, place.after_y(got_a, got_b), 0.0)
    return tile


def got_x_sum(place, tile, ch, ex, ey, x_first, x_second):
    rows = pl.ds(ch * 16 + ey * 8, 8)
    pick = place.before_x if ex == 0 else place.after_x
    return tile + pick(x_first[rows, :], x_second[rows, :])


def pack_kernel(kappa, group, coarse, pack, facts):
    place = Place()
    pack[...] = jnp.zeros(pack.shape, jnp.float32)
    facts[...] = jnp.zeros(facts.shape, jnp.float32)
    elems = kappa.shape[2]
    to = lax.broadcasted_iota(jnp.int32, (elems, LANES), 1)
    element = lax.broadcasted_iota(jnp.int32, (elems, LANES), 0)
    blocks = coarse.shape[1] // LANES
    packed = jnp.zeros((1, LANES), jnp.float32)
    for ex in range(2):
        numbers = group[ex].astype(jnp.float32)
        row = jnp.zeros((1, LANES), jnp.float32)
        for ey in range(2):
            mine, number = kappa[ex, pl.ds(ey, 1), :], numbers[ey : ey + 1]
            at = (2 * ex + ey) * elems
            packed = packed + exact_dot(mine, (to == at + element).astype(jnp.float32))
            at = at + 4 * elems
            packed = packed + exact_dot(number, (to == at + element).astype(jnp.float32))
            at = (2 * place.iy + ey) * elems
            row = row + exact_dot(mine, (to == at + element).astype(jnp.float32))
            at = (at + 2 * elems) % LANES
            row = row + exact_dot(number, (to == at + element).astype(jnp.float32))
        facts[pl.ds(2 + ex, 1), :] = row
    pack[pl.ds(0, 1), :] = packed
    for c in range(NCD):
        for j in range(blocks):
            line = coarse[pl.ds(c, 1), pl.ds(j * LANES, LANES)]
            pack[pl.ds(1 + c * blocks + j, 1), :] = line
        facts[pl.ds(4 + c, 1), :] = coarse[pl.ds(c, 1), pl.ds(0, LANES)]


def prepare_kernel(
    summed, visc, y_first, y_second, ctab, zmat, start, part, slope, answer, grad_z, flux_z
):
    place = Place()
    weight = ctab[T_W]
    inv_mass = [1.0 / (weight * place.mult_tile(ey)) for ey in range(2)]

    def begin(ch, carry):
        for ex in range(2):
            for a in range(8):
                for ey in range(2):
                    tile = got_y_sum(
                        place, summed[ch, ex, a, ey], ch, ex, a, ey, y_first, y_second
                    )
                    scale = place.inv_x(ex, a) * float(1.0 / WEIGHTS[a])
                    start[ch, ex, a, ey] = tile * (inv_mass[ey] * scale)
        return carry

    lax.fori_loop(0, 4, begin, 0)
    grad_z[...] = along_z(start[...].reshape(1024, LANES), zmat[0]).reshape(grad_z.shape)

    def column(index, carry):
        ch, ey = index // 2, index % 2
        coef = jnp.where(ch == 3, 1.0 / prandtl, 1.0)
        for ex in range(2):
            grad_x = along_x(DERIV, [start[ch, ex, a, ey] for a in range(8)], -1)
            flux_x = [
                visc[ex, a, ey] * (float(WEIGHTS[a]) * weight) * coef * grad_x[a]
                for a in range(8)
            ]
            back = along_x(DERIV.T, flux_x, -1)
            for a in range(8):
                if (ex, a) in OUTER:
                    slope[ch, ex, ey] = grad_x[a]
                    part[ch, ex, a, ey] = back[a]
                    continue
                rest, flux_z[ch, ex, a, ey] = across(
                    ctab, weight, a, coef, start[ch, ex, a, ey], grad_z[ch, ex, a, ey],
                    start[1, ex, a, ey], start[2, ex, a, ey], visc[ex, a, ey],
                )
                flow = float(WEIGHTS[a]) * weight * start[0, ex, a, ey]
                part[ch, ex, a, ey] = rest + flow * grad_x[a] + back[a]
        return carry

    for ex, outer in OUTER:
        for ey in range(2):
            flux_x = [
                visc[ex, a, ey] * (float(WEIGHTS[a] * DERIV[a, outer]) * weight) for a in range(8)
            ]
            back = along_x(DERIV.T, flux_x, -1)
            for a in range(8):
                answer[ex, a, ey] = back[a]
    lax.fori_loop(0, 8, column, 0)
    for ch in range(4):
        for ex in range(2):
            inner = pl.ds(1 - ex, 7)
            back = along_z(flux_z[ch, ex, inner].reshape(112, LANES), zmat[1])
            part[ch, ex, inner] = part[ch, ex, inner] + back.reshape(7, 2, 8, LANES)


def across(ctab, weight, a, coef, value, grad_z, flow_y, flow_z, visc):
    node = float(WEIGHTS[a]) * weight
    grad_y = along_y(ctab, T_D, value)
    nu = visc * node * coef
    part = node * (flow_y * grad_y + flow_z * grad_z) + along_y(ctab, T_DT, nu * grad_y)
    return part, nu * grad_z


def rhs_kernel(
    pack_rows,
    begun,
    given,
    slope,
    answer,
    visc,
    pack,
    x_first,
    x_second,
    ctab,
    zmat,
    share,
    xf,
    inner_x,
    first,
    second,
    edge,
    edge_z,
    edge_part,
    came,
):
    place = Place()
    weight = ctab[T_W]
    inv_mass = [1.0 / (weight * place.mult_tile(ey)) for ey in range(2)]
    for ch in range(4):
        for side, (ex, a) in enumerate(OUTER):
            scale = place.inv_x(ex, a) * float(1.0 / WEIGHTS[a])
            for ey in range(2):
                zero = jnp.zeros(TILE, jnp.float32)
                extra = got_x_sum(place, zero, ch, ex, ey, x_first, x_second)
                extra = extra * (inv_mass[ey] * scale)
                came[ch, side, ey] = extra
                edge[ch, side, ey] = begun[ch, ex, a, ey] + extra
    edge_z[...] = along_z(edge[...].reshape(128, LANES), zmat[0]).reshape(edge.shape)
    for ch in range(4):
        coef = 1.0 / prandtl if ch == 3 else 1.0
        for side, (ex, a) in enumerate(OUTER):
            for ey in range(2):
                parts = across(
                    ctab, weight, a, coef, edge[ch, side, ey], edge_z[ch, side, ey],
                    edge[1, side, ey], edge[2, side, ey], visc[ex, a, ey],
                )
                edge_part[ch, side, ey], edge_z[ch, side, ey] = parts
    edge_part[...] = edge_part[...] + along_z(
        edge_z[...].reshape(128, LANES), zmat[1]
    ).reshape(edge.shape)

    def side_of(ch, ex, a, ey):
        outer = OUTER[ex][1]
        coef = jnp.where(ch == 3, 1.0 / prandtl, 1.0)
        extra = came[ch, ex, ey]
        node = float(WEIGHTS[a]) * weight
        turn = float(DERIV[a, outer])
        if a == outer:
            known = given[ch, ex, a, ey] + edge_part[ch, ex, ey]
            known = known + node * edge[0, ex, ey] * (slope[ch, ex, ey] + turn * extra)
            return known + extra * (coef * answer[ex, a, ey])
        flow = float(WEIGHTS[a] * turn) * weight * begun[0, ex, a, ey]
        return given[ch, ex, a, ey] + extra * (coef * answer[ex, a, ey] + flow)

    def finish(ch, carry):
        tiles = [
            [[place.join_z(-side_of(ch, ex, a, ey)) for ey in range(2)] for a in range(8)]
            for ex in range(2)
        ]
        join_own(place, tiles)
        for ex in range(2):
            for a in range(8):
                scale = place.inv_x(ex, a) * float(dt_step / WEIGHTS[a])
                for ey in range(2):
                    value = edge[ch, ex, ey] if (ex, a) in OUTER else begun[ch, ex, a, ey]
                    part = value * (place.share_y(ey) * place.share_x(ex, a))
                    share[ch, ex, a, ey] = part + tiles[ex][a][ey] * (inv_mass[ey] * scale)
        return carry

    lax.fori_loop(0, 4, finish, 0)
    for ch in range(4):
        store_y_faces(place, share, first, second, (ch,), ch * 16)
        for ey in range(2):
            xf[0, ch, ey] = share[ch, 0, 0, ey]
            xf[1, ch, ey] = share[ch, 1, 7, ey]
    first[pl.ds(STEP_EDGE, 8), :] = jnp.zeros(TILE, jnp.float32)
    second[pl.ds(STEP_EDGE, 8), :] = jnp.zeros(TILE, jnp.float32)

    def column_of(ex, ey):
        return [share[0, ex, a, ey] for a in range(8)]

    def tile_of(ex, a, ey):
        return share[1, ex, a, ey]

    store_inner(
        place, DERIV, ctab[T_BOTTOM], ctab[T_TOP], column_of, tile_of, inner_x, first, second,
        STEP_V, STEP_EDGE,
    )
    beside = pl.ds(64, pack_rows)
    parts = (
        place.before_x(x_first[beside, :], x_second[beside, :]),
        pack[...],
        place.after_x(x_first[beside, :], x_second[beside, :]),
    )
    for k in range(3):
        rows = pl.ds(STEP_PACK + k * pack_rows, pack_rows)
        first[rows, :] = parts[k]
        second[rows, :] = parts[k]


def store_inner(
    place, matrix, bottom, top, column_of, tile_of, inner_x, first, second, at, edge
):
    for ey in range(2):
        low, high = column_of(0, ey), column_of(1, ey)
        below = float(matrix[0, 1]) * low[1]
        above = float(matrix[7, 0]) * high[0]
        for k in range(2, 8):
            below = below + float(matrix[0, k]) * low[k]
            above = above + float(matrix[7, k - 1]) * high[k - 1]
        inner_x[0, ey] = below
        inner_x[1, ey] = above
    for side in range(2):
        low = inner_x[side, 0, pl.ds(0, 1), :]
        high = inner_x[side, 1, pl.ds(7, 1), :]
        first[pl.ds(edge + side, 1), :] = place.after_y(high, low)
        second[pl.ds(edge + side, 1), :] = place.after_y(low, high)
    for ex in range(2):
        for a in range(8):
            low = jnp.sum(bottom * tile_of(ex, a, 0), axis=0, keepdims=True)
            high = jnp.sum(top * tile_of(ex, a, 1), axis=0, keepdims=True)
            row = pl.ds(at + ex * 8 + a, 1)
            first[row, :] = place.after_y(high, low)
            second[row, :] = place.after_y(low, high)


def cross_flow(place, ctab, flow, slopes, rows, inv_y, inv_z):
    below, above = rows
    below = (below - float(DERIV[0, 0]) * flow[0]) * jnp.where(place.prev_y, 1.0, 0.0)
    above = (above - float(DERIV[7, 7]) * flow[1]) * jnp.where(place.next_y, 1.0, 0.0)
    grad_y = list(place.join_y(*[along_y(ctab, T_D, tile) for tile in flow]))
    grad_y[0] = grad_y[0] + jnp.where(place.row == 0, below, 0.0)
    grad_y[1] = grad_y[1] + jnp.where(place.row == 7, above, 0.0)
    return [grad_y[ey] * inv_y[ey] + place.join_z(slopes[ey]) * inv_z for ey in range(2)]


def approach_kernel(share, y_first, y_second, ctab, zmat, fields_new, part, grad_z):
    place = Place()

    def step(ch, carry):
        for ex in range(2):
            for a in range(8):
                for ey in range(2):
                    fields_new[ch, ex, a, ey] = got_y_sum(
                        place, share[ch, ex, a, ey], ch, ex, a, ey, y_first, y_second
                    )
        return carry

    lax.fori_loop(0, 4, step, 0)
    grad_z[...] = along_z(fields_new[2].reshape(256, LANES), zmat[0]).reshape(grad_z.shape)
    inv_y = [place.inv_y(ey) for ey in range(2)]
    inv_z = place.inv_z()
    for ex in range(2):
        for a in range(8):
            if (ex, a) in OUTER:
                continue
            flow = [fields_new[1, ex, a, ey] for ey in range(2)]
            rows = inner_along_y(place, y_first, y_second, None, None, ex, a, STEP_V, STEP_EDGE)
            slopes = [grad_z[ex, a, ey] for ey in range(2)]
            both = cross_flow(place, ctab, flow, slopes, rows, inv_y, inv_z)
            part[ex, a, 0], part[ex, a, 1] = both


def emit_kernel(begun, x_first, x_second, fields_new):
    place = Place()
    fields_new[...] = begun[...]
    for ch in range(4):
        for ex, a in OUTER:
            for ey in range(2):
                fields_new[ch, ex, a, ey] = got_x_sum(
                    place, begun[ch, ex, a, ey], ch, ex, ey, x_first, x_second
                )


def advance_kernel(
    begun,
    given,
    y_first,
    y_second,
    x_first,
    x_second,
    inv_diag,
    kap,
    grp,
    ctab,
    zmat,
    resid,
    own,
    msg,
    grad_z,
    scaled,
    edge,
    part,
    outer,
):
    place = Place()
    weight = ctab[T_W]

    def before(row, count=8):
        rows = pl.ds(row, count)
        return place.before_x(x_first[rows, :], x_second[rows, :])

    def after(row, count=8):
        rows = pl.ds(row, count)
        return place.after_x(x_first[rows, :], x_second[rows, :])

    part[...] = given[...]
    for ch in range(3):
        for side, (ex, a) in enumerate(OUTER):
            for ey in range(2):
                outer[ch, side, ey] = got_x_sum(
                    place, begun[ch, ex, a, ey], ch, ex, ey, x_first, x_second
                )
    edge[...] = along_z(outer[2].reshape(32, LANES), zmat[0]).reshape(edge.shape)
    inv_y = [place.inv_y(ey) for ey in range(2)]
    inv_z = place.inv_z()
    for side, (ex, a) in enumerate(OUTER):
        flow = [outer[1, side, ey] for ey in range(2)]
        rows = inner_along_y(place, y_first, y_second, before, after, ex, a, STEP_V, STEP_EDGE)
        slopes = [edge[side, ey] for ey in range(2)]
        both = cross_flow(place, ctab, flow, slopes, rows, inv_y, inv_z)
        part[ex, a, 0], part[ex, a, 1] = both
    slope = [[None, None], [None, None]]
    for ey in range(2):
        for ex in range(2):
            line = [
                outer[0, ex, ey] if (ex, a) in OUTER else begun[0, ex, a, ey] for a in range(8)
            ]
            slope[ex][ey] = along_x(DERIV, line, -1)
        mid = 0.5 * (slope[0][ey][7] + slope[1][ey][0])
        slope[0][ey][7] = mid
        slope[1][ey][0] = mid
        low, high = slope[0][ey][0], slope[1][ey][7]
        inner_low = low - float(DERIV[0, 0]) * outer[0, 0, ey] + before(STEP_U + ey * 8)
        inner_high = high - float(DERIV[7, 7]) * outer[0, 1, ey] + after(STEP_U + ey * 8)
        slope[0][ey][0] = jnp.where(place.prev_x, 0.5 * inner_low, low)
        slope[1][ey][7] = jnp.where(place.next_x, 0.5 * inner_high, high)
    sums = [[jnp.zeros(TILE, jnp.float32) for _ in range(2)] for _ in range(2)]
    inv_mult = [1.0 / place.mult_tile(ey) for ey in range(2)]
    mass = [weight * place.mult_tile(ey) for ey in range(2)]
    for ex in range(2):
        for a in range(8):
            for ey in range(2):
                div = slope[ex][ey][a] + part[ex, a, ey]
                value = div * (mass[ey] * (place.mult_x(ex, a) * float(-WEIGHTS[a])))
                resid[ex, a, ey] = value
                scaled[ex, a, ey] = value * inv_diag[ex, a, ey] * float(1.0 / THETA)
                sums[ex][ey] = sums[ex][ey] + value * (inv_mult[ey] * place.inv_x(ex, a))
    grad_z[...] = along_z(scaled[...].reshape(256, LANES), zmat[2]).reshape(grad_z.shape)
    tiles = [[[None, None] for _ in range(8)] for _ in range(2)]
    for ex in range(2):
        for ey in range(2):
            images = own_operator(ctab, kap, scaled, grad_z, ex, ey)[1]
            for a in range(8):
                tiles[ex][a][ey] = place.join_z(images[a])
    join_own(place, tiles)
    for ex in range(2):
        for a in range(8):
            for ey in range(2):
                own[ex, a, ey] = tiles[ex][a][ey]
    row = message(place, restricted(place, sums, grp), [])
    blank = jnp.where(place.row == 0, jnp.broadcast_to(row, TILE), 0.0)
    zero = jnp.zeros(TILE, jnp.float32)

    def clear(i, carry):
        msg[i, pl.ds(0, 8), :] = zero
        msg[i, pl.ds(8, 8), :] = blank
        return carry

    lax.fori_loop(0, msg.shape[0], clear, 0)
    for dx, dy, there in neighbours(place):

        @pl.when(there)
        def _():
            to = (place.ix + dx) * place.ny + place.iy + dy
            ex, a = (0, 0) if dx < 0 else (1, 7)
            ey, b = (0, 0) if dy < 0 else (1, 7)
            if dy == 0:
                msg[to, pl.ds(0, 8), :] = own[ex, a, 0]
                msg[to, pl.ds(9, 7), :] = own[ex, a, 1, pl.ds(1, 7), :]
            elif dx == 0:
                for r in range(16):
                    if r != 8:
                        msg[to, pl.ds(r, 1), :] = own[r // 8, r % 8, ey, pl.ds(b, 1), :]
            else:
                msg[to, pl.ds(0, 1), :] = own[ex, a, ey, pl.ds(b, 1), :]


def inner_along_y(place, y_first, y_second, before, after, ex, a, at, edge):
    row = pl.ds(at + ex * 8 + a, 1)
    got_a, got_b = y_first[row, :], y_second[row, :]
    below, above = place.before_y(got_a, got_b), place.after_y(got_a, got_b)
    if before is None:
        return below, above
    if (ex, a) == (0, 0):
        below = below + before(edge, 1)
        above = above + before(edge + 1, 1)
    if (ex, a) == (1, 7):
        below = below + after(edge, 1)
        above = above + after(edge + 1, 1)
    return below, above


def neighbours(place):
    along = ((-1, place.prev_x), (0, None), (1, place.next_x))
    across = ((-1, place.prev_y), (0, None), (1, place.next_y))
    out = []
    for dx, has_x in along:
        for dy, has_y in across:
            if dx == 0 and dy == 0:
                continue
            there = has_y if has_x is None else (has_x if has_y is None else has_x & has_y)
            out.append((dx, dy, there))
    return out


SMOOTH_X, SMOOTH_Y, SMOOTH_EDGE, SMOOTH_ROWS = 16, 16, 32, 40


def turn_smooth_kernel(own, inner_x, y_first, y_second, first, second):
    place = Place()
    sides = []
    for side, (ex, a) in enumerate(((0, 0), (1, 7))):
        row = pl.ds(15 * side, 1)
        got_a, got_b = y_first[row, :], y_second[row, :]
        low = own[ex, a, 0] + jnp.where(place.row == 0, place.before_y(got_a, got_b), 0.0)
        high = own[ex, a, 1] + jnp.where(place.row == 7, place.after_y(got_a, got_b), 0.0)
        sides.append((low, high))
    for ey in range(2):
        rows = pl.ds(ey * 8, 8)
        first[rows, :] = place.after_x(sides[1][ey], sides[0][ey])
        second[rows, :] = place.after_x(sides[0][ey], sides[1][ey])
    first[pl.ds(SMOOTH_EDGE, 8), :] = jnp.zeros(TILE, jnp.float32)
    second[pl.ds(SMOOTH_EDGE, 8), :] = jnp.zeros(TILE, jnp.float32)
    turn_edges(
        place, inner_x, y_first, y_second, first, second, SMOOTH_X, SMOOTH_EDGE, SMOOTH_Y
    )


def restricted(place, sums, grp):
    values = []
    for c in range(NCD):
        acc = jnp.zeros(TILE, jnp.float32)
        for ex in range(2):
            for ey in range(2):
                group = grp[pl.ds((ex + 1) * 4 + ey + 1, 1), :]
                acc = acc + jnp.where(group == float(c), sums[ex][ey], 0.0)
        values.append(total(acc))
    return values


def message(place, own_values, scalars):
    lane = lax.broadcasted_iota(jnp.int32, (1, LANES), 1)
    spot = (place.ix * place.ny + place.iy) % (LANES // NCD)
    after = (spot + 1) % (LANES // NCD)
    row = jnp.zeros((1, LANES), jnp.float32)
    for c, value in enumerate(own_values):
        row = row + jnp.where(lane == spot * NCD + c, value, 0.0)
    for c, value in enumerate(scalars):
        if value is None:
            continue
        row = row + jnp.where(lane == after * NCD + c, value, 0.0)
    return row


def send_to_all(msg, row):
    def send(i, carry):
        msg[i] = row
        return carry

    lax.fori_loop(0, msg.shape[0], send, 0, unroll=msg.shape[0] <= 64)


def cross_image(place, ctab, kap, value, flat, inner, ex, ey):
    slope_y = along_y(ctab, T_K, value)
    turned_y = inner + float(SCALED[0, 0]) * value
    own = kap[pl.ds((ex + 1) * 4 + ey + 1, 1), :] * (slope_y + flat) + sigma_p * value
    beyond = kap[pl.ds((ex + 1) * 4 + 3 * ey, 1), :] * (turned_y + flat) + sigma_p * value
    return own + jnp.where(beyond_y(place, ey), beyond, 0.0), slope_y, turned_y


def beyond_y(place, ey):
    if ey == 0:
        return (place.row == 0) & place.prev_y
    return (place.row == 7) & place.next_y


def ready_kernel(
    own, y_first, y_second, inv_diag, kap, ctab, zmat, image, scaled, part, slope_z
):
    place = Place()
    for ex in range(2):
        for a in range(8):
            for ey in range(2):
                tile = got_y_sum(place, own[ex, a, ey], 0, ex, a, ey, y_first, y_second)
                image[ex, a, ey] = tile
                scaled[ex, a, ey] = tile * inv_diag[ex, a, ey] * float(1.0 / THETA)
    slope_z[...] = along_z(scaled[...].reshape(256, LANES), zmat[2]).reshape(slope_z.shape)
    for ex in range(2):
        for a in range(8):
            if (ex, a) in OUTER:
                continue
            rows = inner_along_y(
                place, y_first, y_second, None, None, ex, a, SMOOTH_Y, SMOOTH_EDGE
            )
            for ey in range(2):
                part[ex, a, ey] = cross_image(
                    place, ctab, kap, scaled[ex, a, ey], slope_z[ex, a, ey], rows[ey], ex, ey
                )[0]


def smooth_kernel(
    begun,
    begun_scaled,
    given,
    y_first,
    y_second,
    x_first,
    x_second,
    inv_diag,
    kap,
    grp,
    extra,
    facts,
    ctab,
    zmat,
    image,
    smoothed,
    msg,
    scaled,
    slope_z,
    edge,
):
    place = Place()
    weight = ctab[T_W]
    corner = float(SCALED[0, 0])

    def before(row, count=8):
        rows = pl.ds(row, count)
        return place.before_x(x_first[rows, :], x_second[rows, :])

    def after(row, count=8):
        rows = pl.ds(row, count)
        return place.after_x(x_first[rows, :], x_second[rows, :])

    image[...] = begun[...]
    scaled[...] = begun_scaled[...]
    for side, (ex, a) in enumerate(OUTER):
        for ey in range(2):
            tile = got_x_sum(place, begun[ex, a, ey], 0, ex, ey, x_first, x_second)
            image[ex, a, ey] = tile
            scaled[ex, a, ey] = tile * inv_diag[ex, a, ey] * float(1.0 / THETA)
            edge[side, ey] = scaled[ex, a, ey]
    edge[...] = along_z(edge[...].reshape(32, LANES), zmat[2]).reshape(edge.shape)
    there_x = (place.prev_x, place.next_x)
    zero = jnp.zeros(TILE, jnp.float32)
    tiles = [[[None, None] for _ in range(8)] for _ in range(2)]
    for ex in range(2):
        a_out = OUTER[ex][1]
        rows = inner_along_y(
            place, y_first, y_second, before, after, ex, a_out, SMOOTH_Y, SMOOTH_EDGE
        )
        for ey in range(2):
            values = [scaled[ex, a, ey] for a in range(8)]
            slopes = along_x(SCALED, values, 1)
            far_row = beyond_y(place, ey)
            beside = kap[pl.ds((ex + 1) * 4 + 3 * ey, 1), :]
            kappa = kap[pl.ds((ex + 1) * 4 + ey + 1, 1), :] + jnp.where(far_row, beside, 0.0)
            for a in range(8):
                if a != a_out:
                    acc = given[ex, a, ey]
                else:
                    value, flat = values[a], edge[ex, ey]
                    acc, slope_y, turned_y = cross_image(
                        place, ctab, kap, value, flat, rows[ey], ex, ey
                    )
                    x_next = 3 * ex
                    get = before if ex == 0 else after
                    turned_x = get(SMOOTH_X + ey * 8) + corner * value
                    side = kap[pl.ds(x_next * 4 + ey + 1, 1), :] * (turned_x + slope_y + flat)
                    far = kap[pl.ds(x_next * 4 + 3 * ey, 1), :] * (turned_x + turned_y + flat)
                    side = side + sigma_p * value
                    side = side + jnp.where(far_row, far + sigma_p * value, zero)
                    acc = acc + jnp.where(there_x[ex], side, zero)
                acc = acc + kappa * slopes[a]
                tiles[ex][a][ey] = place.join_z(acc * (float(WEIGHTS[a]) * weight))
    join_own(place, tiles)
    inv_mult = [1.0 / place.mult_tile(ey) for ey in range(2)]
    sums = [[jnp.zeros(TILE, jnp.float32) for _ in range(2)] for _ in range(2)]
    square = jnp.zeros(TILE, jnp.float32)
    for ex in range(2):
        for a in range(8):
            for ey in range(2):
                value = image[ex, a, ey]
                defect = (value - tiles[ex][a][ey]) * inv_diag[ex, a, ey]
                update = scaled[ex, a, ey]
                result = (
                    float(1.0 + RHO_NEXT * RHO) * update + float(2.0 * RHO_NEXT / DELTA) * defect
                )
                smoothed[ex, a, ey] = result
                weighed = value * (inv_mult[ey] * place.inv_x(ex, a))
                sums[ex][ey] = sums[ex][ey] + weighed
                square = square + weighed * result
    own_sums = restricted(place, sums, grp)
    if msg.shape[1] == 1:
        send_to_all(msg, message(place, own_sums, []) + extra[...])
        return
    slope_z[...] = along_z(smoothed[...].reshape(256, LANES), zmat[2]).reshape(slope_z.shape)
    energy = jnp.zeros(TILE, jnp.float32)
    for ex in range(2):
        for ey in range(2):
            values, images = own_operator(ctab, kap, smoothed, slope_z, ex, ey)
            for a in range(8):
                energy = energy + values[a] * images[a]
                tiles[ex][a][ey] = place.join_z(images[a])
    join_own(place, tiles)
    row = message(place, own_sums, [None, None, total(square), total(energy)]) + extra[...]
    dual = restricted_around(place, tiles, inv_mult, grp)
    out = facts[...]
    out = out + jnp.where(place.row == 0, jnp.broadcast_to(row, TILE), 0.0)
    out = out + jnp.where(place.row == 1, jnp.broadcast_to(dual, TILE), 0.0)
    send_to_all(msg, out)


def restricted_around(place, tiles, inv_mult, grp):
    lane = lax.broadcasted_iota(jnp.int32, (1, LANES), 1)
    weighed = [
        [[tiles[ex][a][ey] * (inv_mult[ey] * place.inv_x(ex, a)) for ey in range(2)] for a in range(8)]
        for ex in range(2)
    ]

    def rows_of(tile, y):
        if y == 0:
            return jnp.where(place.row == 0, tile[0], 0.0)
        if y == 3:
            return jnp.where(place.row == 7, tile[1], 0.0)
        return tile[y - 1]

    there_x = (place.prev_x, None, None, place.next_x)
    there_y = (place.prev_y, None, None, place.next_y)
    by_device = [
        [[jnp.zeros(TILE, jnp.float32) for _ in range(NCD)] for _ in range(3)] for _ in range(3)
    ]
    for x in range(4):
        for y in range(4):
            if x == 0:
                acc = rows_of(weighed[0][0], y)
            elif x == 3:
                acc = rows_of(weighed[1][7], y)
            else:
                acc = rows_of(weighed[x - 1][0], y)
                for a in range(1, 8):
                    acc = acc + rows_of(weighed[x - 1][a], y)
            for there in (there_x[x], there_y[y]):
                if there is not None:
                    acc = jnp.where(there, acc, 0.0)
            group = grp[pl.ds(x * 4 + y, 1), :]
            device = by_device[(x + 1) // 2][(y + 1) // 2]
            for c in range(NCD):
                device[c] = device[c] + jnp.where(group == float(c), acc, 0.0)
    row = jnp.zeros((1, LANES), jnp.float32)
    for dx in range(3):
        for dy in range(3):
            at = ((place.ix + dx - 1) * place.ny + place.iy + dy - 1) * NCD
            for c in range(NCD):
                row = row + jnp.where(lane == at + c, total(by_device[dx][dy][c]), 0.0)
    return row


def coarse_part(place, blocks, got, coarse, grp, at=0):
    lane = lax.broadcasted_iota(jnp.int32, (1, LANES), 1)
    values = [jnp.zeros((1, LANES), jnp.float32) for _ in range(blocks)]
    per = LANES // NCD
    for j in range(blocks):

        def gather(i, acc, j=j):
            return jnp.where(lane // NCD == i, got[j * per + i, pl.ds(at, 1), :], acc)

        values[j] = lax.fori_loop(0, per, gather, values[j], unroll=blocks == 1)

    def solved(dx, dy, c):
        acc = None
        for j in range(blocks):
            term = coarse[pl.ds(((dx * 3 + dy) * NCD + c) * blocks + j, 1), :] * values[j]
            acc = term if acc is None else acc + term
        return jnp.sum(acc, axis=1, keepdims=True)

    return prolonged(place, solved, grp)


def prolonged(place, solved, grp):
    device = [[[solved(dx, dy, c) for c in range(NCD)] for dy in range(3)] for dx in range(3)]
    inv_z = jnp.where(place.low_z | place.high_z, 0.5, 1.0)
    rows = []
    for x in range(4):
        line = []
        for y in range(4):
            group = grp[pl.ds(x * 4 + y, 1), :]
            acc = jnp.zeros((1, LANES), jnp.float32)
            for c in range(NCD):
                acc = acc + jnp.where(
                    group == float(c), device[(x + 1) // 2][(y + 1) // 2][c], 0.0
                )
            line.append(place.join_z(jnp.broadcast_to(acc, TILE)) * inv_z)
        rows.append(line)
    low_y = jnp.where(place.prev_y, 0.5, 1.0)
    high_y = jnp.where(place.next_y, 0.5, 1.0)

    def tile(ex, kind, ey):
        if kind == 1:
            vals = [rows[ex + 1][y] for y in range(4)]
        elif kind == 0:
            scale = place.inv_x(ex, 0)
            vals = [(rows[ex][y] + rows[ex + 1][y]) * scale for y in range(4)]
        else:
            scale = place.inv_x(ex, 7)
            vals = [(rows[ex + 1][y] + rows[ex + 2][y]) * scale for y in range(4)]
        mid = vals[ey + 1]
        low = (vals[ey] + mid) * (low_y if ey == 0 else 0.5)
        high = (mid + vals[ey + 2]) * (high_y if ey == 1 else 0.5)
        return jnp.where(place.row == 0, low, jnp.where(place.row == 7, high, mid))

    return tile


def kind_of(a):
    return 0 if a == 0 else (2 if a == 7 else 1)


def own_operator(ctab, kap, field, slope_z, ex, ey):
    weight = ctab[T_W]
    tiles = [field[ex, a, ey] for a in range(8)]
    slopes = along_x(SCALED, tiles, 1)
    kappa = kap[pl.ds((ex + 1) * 4 + ey + 1, 1), :]
    out = []
    for a in range(8):
        stiff = slopes[a] + along_y(ctab, T_K, tiles[a]) + slope_z[ex, a, ey]
        out.append((kappa * stiff + sigma_p * tiles[a]) * (float(WEIGHTS[a]) * weight))
    return tiles, out


def first_direction_kernel(
    blocks,
    got,
    coarse,
    grp,
    kap,
    inv_diag,
    resid,
    own,
    ctab,
    zmat,
    direction,
    out,
    inner_x,
    first,
    second,
    extra,
    slope_z,
    image,
):
    place = Place()
    inv_mult = [1.0 / place.mult_tile(ey) for ey in range(2)]
    part = coarse_part(place, blocks, got, coarse, grp, 8)
    image[...] = own[...]
    for dx, dy, there in neighbours(place):

        @pl.when(there)
        def _():
            frm = (place.ix + dx) * place.ny + place.iy + dy
            ex, a = (0, 0) if dx < 0 else (1, 7)
            ey, b = (0, 0) if dy < 0 else (1, 7)
            edge = place.row == b
            if dy == 0:
                low = got[frm, pl.ds(0, 8), :]
                high = jnp.where(
                    place.row == 0, pltpu.roll(low, 1, 0), got[frm, pl.ds(8, 8), :]
                )
                image[ex, a, 0] = image[ex, a, 0] + low
                image[ex, a, 1] = image[ex, a, 1] + high
            elif dx == 0:
                for r in range(16):
                    line = got[frm, pl.ds(7 if r == 8 else r, 1), :]
                    tile = image[r // 8, r % 8, ey]
                    image[r // 8, r % 8, ey] = tile + jnp.where(edge, line, 0.0)
            else:
                line = got[frm, pl.ds(0, 1), :]
                image[ex, a, ey] = image[ex, a, ey] + jnp.where(edge, line, 0.0)

    energy = jnp.zeros(TILE, jnp.float32)
    for ex in range(2):
        for ey in range(2):
            kinds = [part(ex, kind, ey) for kind in range(3)]
            for a in range(8):
                known = resid[ex, a, ey]
                inverse = inv_diag[ex, a, ey]
                defect = (known - image[ex, a, ey]) * inverse
                value = (
                    float((1.0 + RHO_NEXT * RHO) / THETA) * (known * inverse)
                    + float(2.0 * RHO_NEXT / DELTA) * defect
                    + kinds[kind_of(a)]
                )
                direction[ex, a, ey] = value
                scale = place.inv_x(ex, a)
                energy = energy + value * known * (inv_mult[ey] * scale)
    slope_z[...] = along_z(direction[...].reshape(256, LANES), zmat[2]).reshape(slope_z.shape)
    curvature = jnp.zeros(TILE, jnp.float32)
    tiles = [[[None, None] for _ in range(8)] for _ in range(2)]
    for ex in range(2):
        for ey in range(2):
            values, images = own_operator(ctab, kap, direction, slope_z, ex, ey)
            for a in range(8):
                curvature = curvature + values[a] * images[a]
                tiles[ex][a][ey] = place.join_z(images[a])
    join_own(place, tiles)
    for ex in range(2):
        for a in range(8):
            for ey in range(2):
                out[ex, a, ey] = tiles[ex][a][ey]
    store_y_faces(place, out, first, second, (), 0)
    first[pl.ds(SMOOTH_EDGE, 8), :] = jnp.zeros(TILE, jnp.float32)
    second[pl.ds(SMOOTH_EDGE, 8), :] = jnp.zeros(TILE, jnp.float32)

    def tile_of(ex, a, ey):
        return tiles[ex][a][ey] * inv_diag[ex, a, ey] * float(1.0 / THETA)

    def column_of(ex, ey):
        return [tile_of(ex, a, ey) for a in range(8)]

    store_inner(
        place, SCALED, ctab[T_KBOTTOM], ctab[T_KTOP], column_of, tile_of, inner_x, first, second,
        SMOOTH_Y, SMOOTH_EDGE,
    )
    extra[...] = message(place, [], [total(energy), total(curvature)])


def gathered_scalars(got, count):
    lane = lax.broadcasted_iota(jnp.int32, (1, LANES), 1)
    per = LANES // NCD
    sums = []
    for c in range(count):
        acc = jnp.zeros((1, LANES), jnp.float32)

        def gather(i, acc, c=c):
            return acc + jnp.where(lane == ((i + 1) % per) * NCD + c, got[i], 0.0)

        acc = lax.fori_loop(0, got.shape[0], gather, acc, unroll=got.shape[0] <= per)
        sums.append(jnp.sum(acc, axis=1, keepdims=True))
    return sums


def second_direction_kernel(
    blocks,
    got,
    coarse,
    grp,
    kap,
    resid,
    direction,
    image,
    smoothed,
    ctab,
    zmat,
    following,
    known,
    msg,
    slope_z,
):
    place = Place()
    inv_mult = [1.0 / place.mult_tile(ey) for ey in range(2)]
    part = coarse_part(place, blocks, got, coarse, grp)
    energy, curvature = gathered_scalars(got, 2)
    step = energy / curvature
    lane = lax.broadcasted_iota(jnp.int32, (1, LANES), 1)
    known[...] = jnp.where(lane == 0, energy, jnp.where(lane == 1, curvature, 0.0))
    energy_next = jnp.zeros(TILE, jnp.float32)
    cross = jnp.zeros(TILE, jnp.float32)
    for ex in range(2):
        for ey in range(2):
            kinds = [part(ex, kind, ey) for kind in range(3)]
            for a in range(8):
                value = direction[ex, a, ey] - step * (smoothed[ex, a, ey] + kinds[kind_of(a)])
                following[ex, a, ey] = value
                weighed = value * (inv_mult[ey] * place.inv_x(ex, a))
                was = image[ex, a, ey]
                energy_next = energy_next + weighed * (resid[ex, a, ey] - step * was)
                cross = cross + weighed * was
    slope_z[...] = along_z(following[...].reshape(256, LANES), zmat[2]).reshape(slope_z.shape)
    square = jnp.zeros(TILE, jnp.float32)
    for ex in range(2):
        for ey in range(2):
            values, images = own_operator(ctab, kap, following, slope_z, ex, ey)
            for a in range(8):
                square = square + values[a] * images[a]
    send_to_all(msg, message(place, [], [total(energy_next), total(square), total(cross)]))


def pressure_kernel(got, known, direction, following, pressure):
    energy = known[:, pl.ds(0, 1)]
    curvature = known[:, pl.ds(1, 1)]
    energy_next, square, cross = gathered_scalars(got, 3)
    ratio = energy_next / energy
    step = energy / curvature
    step_next = energy_next / (square + 2.0 * ratio * cross + ratio * ratio * curvature)
    weight_old = step + step_next * ratio
    for ex in range(2):
        for a in range(8):
            for ey in range(2):
                pressure[ex, a, ey] = (
                    weight_old * direction[ex, a, ey] + step_next * following[ex, a, ey]
                )


def coarse_energy(place, got, values, kappa, number):
    lane, row = place.lane, place.row
    for ex in range(2):
        for gx in range(8):
            own = jnp.zeros((1, LANES), jnp.float32)
            group = jnp.zeros((1, LANES), jnp.float32)
            spot = lane[0:1] // 32
            for gy in range(4):
                line = got[gx * 4 + gy, pl.ds(2 + ex, 1), :]
                own = jnp.where(spot == gy, line, own)
                group = jnp.where(spot == (gy + 1) % 4, line, group)
            kappa[ex, pl.ds(gx, 1), :] = own
            number[ex, pl.ds(gx, 1), :] = group
    grid = [jnp.zeros(TILE, jnp.float32) for _ in range(2)]
    numbers = [pltpu.roll(number[ex], 96, 1) for ex in range(2)]
    for q in range(4):
        for c in range(NCD):
            mine = jnp.where(lane == row * 16 + q * 4 + c, values, 0.0)
            mine = jnp.sum(mine, axis=1, keepdims=True)
            for ex in range(2):
                chosen = (lane // 32 == q) & (numbers[ex] == float(c))
                grid[ex] = jnp.where(chosen, mine, grid[ex])

    def ends_y(v):
        low = jnp.where(lane >= 16, 0.5 * (v + pltpu.roll(v, 16, 1)), v)
        return low, v, jnp.where(lane < 112, 0.5 * (v + pltpu.roll(v, 112, 1)), v)

    def ends_z(v):
        low = jnp.where(lane % 16 > 0, 0.5 * (v + pltpu.roll(v, 1, 1)), v)
        return low, v, jnp.where(lane % 16 < 15, 0.5 * (v + pltpu.roll(v, 127, 1)), v)

    low = jnp.where(row > 0, 0.5 * (grid[0] + pltpu.roll(grid[1], 1, 0)), grid[0])
    mid = 0.5 * (grid[0] + grid[1])
    high = jnp.where(row < 7, 0.5 * (grid[1] + pltpu.roll(grid[0], 7, 0)), grid[1])
    mass = [float(WEIGHTS[0]), float(np.sum(WEIGHTS[1:7])), float(WEIGHTS[7])]
    links = (
        (0, 1, -float(np.sum(STIFF[0, 1:7]))),
        (0, 2, -float(STIFF[0, 7])),
        (1, 2, -float(np.sum(STIFF[7, 1:7]))),
    )
    energy = jnp.zeros(TILE, jnp.float32)
    for ex, line in enumerate(((low, grid[0], mid), (mid, grid[1], high))):
        nodes = [[ends_z(v) for v in ends_y(w)] for w in line]
        stiff = jnp.zeros(TILE, jnp.float32)
        square = jnp.zeros(TILE, jnp.float32)
        for i in range(3):
            for j in range(3):
                for k, l, weight in links:
                    factor = weight * mass[i] * mass[j]
                    for first, second in (
                        (nodes[k][i][j], nodes[l][i][j]),
                        (nodes[i][k][j], nodes[i][l][j]),
                        (nodes[i][j][k], nodes[i][j][l]),
                    ):
                        gap = first - second
                        stiff = stiff + (factor * gap) * gap
                for k in range(3):
                    value = nodes[i][j][k]
                    square = square + (mass[i] * mass[j] * mass[k] * value) * value
        energy = energy + kappa[ex] * stiff + sigma_p * square
    return total(energy)


def finish_kernel(
    got, grp, direction, smoothed, pressure, matrix, kappa, number
):
    place = Place()
    per = LANES // NCD
    row_lane = lax.broadcasted_iota(jnp.int32, (1, LANES), 1)
    rest = jnp.zeros((1, LANES), jnp.float32)
    dual = jnp.zeros((1, LANES), jnp.float32)
    sums = [jnp.zeros((1, LANES), jnp.float32) for _ in range(4)]
    for i in range(per):
        line = got[i, pl.ds(0, 1), :]
        rest = jnp.where(row_lane // NCD == i, line, rest)
        dual = dual + got[i, pl.ds(1, 1), :]
        for c in range(4):
            sums[c] = sums[c] + jnp.where(row_lane == ((i + 1) % per) * NCD + c, line, 0.0)
        matrix[pl.ds(i * NCD, NCD), :] = got[i, pl.ds(4, NCD), :]
    energy, curvature, square, self_energy = [
        jnp.sum(value, axis=1, keepdims=True) for value in sums
    ]
    values = lax.dot_general(
        jnp.broadcast_to(rest, TILE),
        matrix[...],
        (((1,), (1,)), ((), ())),
        precision=lax.Precision.HIGHEST,
        preferred_element_type=jnp.float32,
    )
    line = values[0:1]
    cross = square + jnp.sum(line * rest, axis=1, keepdims=True)
    both = self_energy + 2.0 * jnp.sum(line * dual, axis=1, keepdims=True)
    both = both + coarse_energy(place, got, values, kappa, number)
    step = energy / curvature
    energy_next = step * step * cross - energy
    ratio = energy_next / energy
    with_image = curvature - step * cross
    with_itself = curvature - 2.0 * step * cross + step * step * both
    step_next = energy_next / (
        with_itself + 2.0 * ratio * with_image + ratio * ratio * curvature
    )
    old = step + step_next * (1.0 + ratio)
    new = -step_next * step

    def solved(dx, dy, c):
        at = ((place.ix + dx - 1) * place.ny + place.iy + dy - 1) * NCD + c
        return jnp.sum(jnp.where(row_lane == at, line, 0.0), axis=1, keepdims=True)

    part = prolonged(place, masked(place, solved), grp)
    for ex in range(2):
        for ey in range(2):
            kinds = [part(ex, kind, ey) for kind in range(3)]
            for a in range(8):
                pressure[ex, a, ey] = old * direction[ex, a, ey] + new * (
                    smoothed[ex, a, ey] + kinds[kind_of(a)]
                )


def masked(place, solved):
    there_x = (place.prev_x, None, place.next_x)
    there_y = (place.prev_y, None, place.next_y)

    def value(dx, dy, c):
        out = solved(dx, dy, c)
        for there in (there_x[dx], there_y[dy]):
            if there is not None:
                out = jnp.where(there, out, 0.0)
        return out

    return value


def call(body, outs, scratch=(), **more):
    return pl.pallas_call(
        body,
        out_shape=[jax.ShapeDtypeStruct(shape, jnp.float32) for shape in outs],
        scratch_shapes=[
            pltpu.VMEM(shape, jnp.float32) if isinstance(shape, tuple) else shape
            for shape in scratch
        ],
        **more,
        compiler_params=pltpu.CompilerParams(vmem_limit_bytes=24 * 1024 * 1024),
    )


def swap(first, second, axis):
    count = lax.axis_size(axis)
    first_pairs = [(i, i ^ 1) for i in range(count) if i ^ 1 < count]
    second_pairs = [(i, ((i + 1) ^ 1) - 1) for i in range(1, count) if ((i + 1) ^ 1) - 1 < count]
    second_got = lax.ppermute(second, axis, second_pairs)
    return lax.ppermute(first, axis, first_pairs), second_got


def per_device(fields, viscosity, inv_density, elem_group, coarse_inverse):
    length = fields.shape[5]
    elems_z = length // NODES
    devices = lax.axis_size("gx") * lax.axis_size("gy")
    blocks = coarse_inverse.shape[1] // LANES
    pack_rows = -(-(1 + NCD * blocks) // 8) * 8
    tiles_np, mats_np = constant_tables(elems_z)
    ctab, zmat = jnp.asarray(tiles_np), jnp.asarray(mats_np)
    one = fields.shape[1:]
    four = fields.shape
    faces = (64, LANES)
    xf_shape = (2, 4, 2, 8, LANES)
    inner_shape = (2, 2, 8, LANES)
    y_shape, x_shape = (STEP_PACK + 3 * pack_rows, LANES), (STEP_PACK, LANES)
    turned = (64 + pack_rows, LANES)
    smooth_shape = (SMOOTH_ROWS, LANES)
    rows = (devices, 1, LANES)
    grid_fits = (
        blocks == 1
        and lax.axis_size("gx") == 8
        and lax.axis_size("gy") * fields.shape[3] * elems_z == LANES
    )

    def exchange_all(msg):
        return lax.all_to_all(msg, BOTH, 0, 0, tiled=True)

    beside = pl.CostEstimate(flops=10**7, bytes_accessed=10**6, transcendentals=0)
    summed, xf, first, second = call(
        mass_kernel,
        [four, xf_shape, faces, faces],
    )(fields)
    pack, facts = call(
        pack_kernel,
        [(pack_rows, LANES), TILE],
        cost_estimate=beside,
    )(inv_density, elem_group, coarse_inverse)
    y_got = swap(first, second, "gy")
    first, second = call(functools.partial(turn_faces_kernel, pack_rows), [turned, turned])(
        xf, pack, *y_got
    )
    side_got = x_got = swap(first, second, "gx")
    edge_shape = (4, 2, 2, 8, LANES)
    begun, given, slope, answer = call(
        prepare_kernel, [four, four, edge_shape, one], [four, four], cost_estimate=beside
    )(summed, viscosity, *y_got, ctab, zmat)
    share, xf, inner_x, first, second = call(
        functools.partial(rhs_kernel, pack_rows),
        [four, xf_shape, inner_shape, y_shape, y_shape],
        [edge_shape, edge_shape, edge_shape, edge_shape],
    )(begun, given, slope, answer, viscosity, pack, *x_got, ctab, zmat)
    y_got = swap(first, second, "gy")
    first, second = call(turn_step_kernel, [x_shape, x_shape])(xf, inner_x, *y_got)
    x_got = swap(first, second, "gx")
    inv_diag, kap, grp, coarse = call(
        functools.partial(setup_kernel, pack_rows, blocks),
        [one, (16, LANES), (16, LANES), (9 * NCD * blocks, LANES)],
        [(16, LANES), (8, 16, LANES)],
        cost_estimate=beside,
    )(pack, *side_got, *y_got, ctab)
    begun, given = call(approach_kernel, [four, one], [one], cost_estimate=beside)(
        share, *y_got, ctab, zmat
    )
    side_shape = (2, 2, 8, LANES)
    (fields_new,) = call(emit_kernel, [four], cost_estimate=beside)(begun, *x_got)
    resid, own, msg = call(
        advance_kernel,
        [one, one, (devices, 16, LANES)],
        [one, one, side_shape, one, (3,) + side_shape],
    )(begun, given, *y_got, *x_got, inv_diag, kap, grp, ctab, zmat)
    got = exchange_all(msg)
    direction, own, inner_x, first, second, extra = call(
        functools.partial(first_direction_kernel, blocks),
        [one, one, inner_shape, smooth_shape, smooth_shape, (1, LANES)],
        [one, one],
    )(got, coarse, grp, kap, inv_diag, resid, own, ctab, zmat)
    y_got = swap(first, second, "gy")
    first, second = call(turn_smooth_kernel, [smooth_shape, smooth_shape])(own, inner_x, *y_got)
    x_got = swap(first, second, "gx")
    begun, begun_scaled, given = call(
        ready_kernel, [one, one, one], [one], cost_estimate=beside
    )(own, *y_got, inv_diag, kap, ctab, zmat)
    image, image_smoothed, msg = call(
        smooth_kernel,
        [one, one, (devices, 8, LANES) if grid_fits else rows],
        [one, one, side_shape],
    )(
        begun, begun_scaled, given, *y_got, *x_got, inv_diag, kap, grp, extra, facts, ctab, zmat
    )
    got = exchange_all(msg)
    if grid_fits:
        (pressure,) = call(
            finish_kernel, [one], [(LANES, LANES), (2,) + TILE, (2,) + TILE]
        )(got, grp, direction, image_smoothed)
        return (fields_new, pressure)
    following, known, msg = call(
        functools.partial(second_direction_kernel, blocks), [one, (1, LANES), rows], [one]
    )(got, coarse, grp, kap, resid, direction, image, image_smoothed, ctab, zmat)
    got = exchange_all(msg)
    (pressure,) = call(pressure_kernel, [one])(got, known, direction, following)
    return (fields_new, pressure)


def solution(mesh):
    placed = (
        P(None, "gx", None, "gy", None, None),
        P("gx", None, "gy", None, None),
        P("gx", "gy", None),
        P("gx", "gy", None),
        P(("gx", "gy"), None),
    )
    return jax.shard_map(
        per_device,
        mesh=mesh,
        in_specs=placed,
        out_specs=(P(None, "gx", None, "gy", None, None), P("gx", None, "gy", None, None)),
        check_vma=False,
    )
```

```python
import functools

import jax
import jax.numpy as jnp
import ml_dtypes
import numpy as np
from jax import lax
from jax.experimental import pallas as pl
from jax.experimental.pallas import tpu as pltpu
from jax.sharding import PartitionSpec as P

NCD = 4
NODES = 8
LANES = 128
TILE = (8, 128)
BOTH = ("gx", "gy")

dt_step = 0.01
sigma_p = 4.0
prandtl = 0.7
cheb_ratio = 0.1


def tables():
    points = np.array(
        [
            -1.0,
            -0.8717401485096066,
            -0.5917001814331423,
            -0.2092992179024789,
            0.2092992179024789,
            0.5917001814331423,
            0.8717401485096066,
            1.0,
        ]
    )
    weights = np.array(
        [
            1.0 / 28.0,
            0.2107042271435061,
            0.3411226924835044,
            0.4124587946587038,
            0.4124587946587038,
            0.3411226924835044,
            0.2107042271435061,
            1.0 / 28.0,
        ]
    )
    identity = np.eye(8)
    differ = points[:, None] - points[None, :] + identity
    barycentric = 1.0 / np.prod(differ, axis=1)
    offdiag = barycentric[None, :] / barycentric[:, None] / differ * (1.0 - identity)
    derivative = offdiag - identity * np.sum(offdiag, axis=1)[:, None]
    mass_one = identity * weights[None, :]
    stiff_one = derivative.T @ mass_one @ derivative
    stiff_three = (
        np.kron(np.kron(stiff_one, mass_one), mass_one)
        + np.kron(np.kron(mass_one, stiff_one), mass_one)
        + np.kron(np.kron(mass_one, mass_one), stiff_one)
    )
    three_diag = np.sum(stiff_three * np.eye(512), axis=1)
    spectral_bound = float(np.max(np.sum(np.abs(stiff_three), axis=1) / three_diag))
    return (derivative, weights, stiff_one, spectral_bound)


DERIV, WEIGHTS, STIFF, BOUND = tables()
SCALED = STIFF / WEIGHTS[:, None]
LINE = np.diag(STIFF) / WEIGHTS
THETA = 0.5 * (BOUND + cheb_ratio * BOUND)
DELTA = 0.5 * (BOUND - cheb_ratio * BOUND)
RHO = DELTA / THETA
RHO_NEXT = 1.0 / (2.0 * THETA / DELTA - RHO)


def constant_tables(elems_z):
    def turned(matrix):
        rows = np.arange(8)
        return [np.repeat(matrix[rows, (rows - s) % 8][:, None], LANES, 1) for s in range(8)]

    wz = np.tile(WEIGHTS, elems_z)
    kz = np.tile(LINE, elems_z)
    tiles = turned(DERIV) + turned(DERIV.T) + turned(SCALED)
    tiles += [WEIGHTS[:, None] * wz[None, :], LINE[:, None] + kz[None, :]]
    for matrix in (DERIV, SCALED):
        for node in (7, 0):
            inner = matrix[node] * (np.arange(8) != node)
            tiles.append(np.repeat(inner[:, None], LANES, 1))
    eye = np.eye(elems_z)
    mats = [np.kron(eye, DERIV.T), np.kron(eye, DERIV), np.kron(eye, SCALED.T)]
    halves = []
    for mat in mats:
        high = mat.astype(ml_dtypes.bfloat16)
        low = (mat - high.astype(np.float64)).astype(ml_dtypes.bfloat16)
        both = np.concatenate([high, low], 1)
        halves.append(np.concatenate([both, both], 0))
    return np.stack(tiles).astype(np.float32), np.stack(halves)


T_D, T_DT, T_K, T_W, T_LINE = 0, 8, 16, 24, 25
T_TOP, T_BOTTOM, T_KTOP, T_KBOTTOM = 26, 27, 28, 29


class Place:
    def __init__(self):
        self.ix = lax.axis_index("gx")
        self.iy = lax.axis_index("gy")
        self.nx = lax.axis_size("gx")
        self.ny = lax.axis_size("gy")
        self.even_x = self.ix % 2 == 0
        self.even_y = self.iy % 2 == 0
        self.row = lax.broadcasted_iota(jnp.int32, TILE, 0)
        self.lane = lax.broadcasted_iota(jnp.int32, TILE, 1)
        self.low_z = (self.lane % 8 == 0) & (self.lane > 0)
        self.high_z = (self.lane % 8 == 7) & (self.lane < LANES - 1)
        self.prev_x = self.ix > 0
        self.next_x = self.ix < self.nx - 1
        self.prev_y = self.iy > 0
        self.next_y = self.iy < self.ny - 1

    def mult_tile(self, ey):
        along_z = 1.0 + jnp.where(self.low_z | self.high_z, 1.0, 0.0)
        low = 1.0 if ey == 1 else jnp.where(self.prev_y, 1.0, 0.0)
        high = 1.0 if ey == 0 else jnp.where(self.next_y, 1.0, 0.0)
        along_y = 1.0 + jnp.where(self.row == 0, low, jnp.where(self.row == 7, high, 0.0))
        return along_y * along_z

    def inv_x(self, ex, a):
        if a == 0:
            return 0.5 if ex == 1 else jnp.where(self.prev_x, 0.5, 1.0)
        if a == 7:
            return 0.5 if ex == 0 else jnp.where(self.next_x, 0.5, 1.0)
        return 1.0

    def mult_x(self, ex, a):
        if a == 0:
            return 2.0 if ex == 1 else jnp.where(self.prev_x, 2.0, 1.0)
        if a == 7:
            return 2.0 if ex == 0 else jnp.where(self.next_x, 2.0, 1.0)
        return 1.0

    def share_x(self, ex, a):
        if (ex, a) == (0, 0):
            return jnp.where(self.prev_x, 0.5, 1.0)
        if (ex, a) == (1, 7):
            return jnp.where(self.next_x, 0.5, 1.0)
        return 1.0

    def share_y(self, ey):
        if ey == 0:
            return jnp.where((self.row == 0) & self.prev_y, 0.5, 1.0)
        return jnp.where((self.row == 7) & self.next_y, 0.5, 1.0)

    def inv_y(self, ey):
        low = 0.5 if ey == 1 else jnp.where(self.prev_y, 0.5, 1.0)
        high = 0.5 if ey == 0 else jnp.where(self.next_y, 0.5, 1.0)
        return jnp.where(self.row == 0, low, jnp.where(self.row == 7, high, 1.0))

    def inv_z(self):
        return jnp.where(self.low_z | self.high_z, 0.5, 1.0)

    def join_z(self, t):
        up = pltpu.roll(t, LANES - 1, 1)
        down = pltpu.roll(t, 1, 1)
        return t + jnp.where(self.high_z, up, jnp.where(self.low_z, down, 0.0))

    def to_low(self, below):
        return jnp.where(self.row == 0, pltpu.roll(below, 1, 0), 0.0)

    def to_high(self, above):
        return jnp.where(self.row == 7, pltpu.roll(above, 7, 0), 0.0)

    def join_y(self, below, above):
        return below + self.to_high(above), above + self.to_low(below)

    def before_x(self, first, second):
        return jnp.where(self.even_x, second, first)

    def after_x(self, first, second):
        return jnp.where(self.even_x, first, second)

    def before_y(self, first, second):
        return jnp.where(self.even_y, second, first)

    def after_y(self, first, second):
        return jnp.where(self.even_y, first, second)


def along_x(matrix, tiles, sign):
    even = [tiles[a] + tiles[7 - a] for a in range(4)]
    odd = [tiles[a] - tiles[7 - a] for a in range(4)]
    out = [None] * 8
    for i in range(4):
        plus, minus = None, None
        for a in range(4):
            p = float(0.5 * (matrix[i, a] + matrix[i, 7 - a])) * even[a]
            m = float(0.5 * (matrix[i, a] - matrix[i, 7 - a])) * odd[a]
            plus = p if plus is None else plus + p
            minus = m if minus is None else minus + m
        out[i] = plus + minus
        out[7 - i] = minus - plus if sign < 0 else plus - minus
    return out


def along_y(ctab, base, tile):
    acc = ctab[base] * tile
    for s in range(1, 8):
        acc = acc + ctab[base + s] * pltpu.roll(tile, s, 0)
    return acc


def exact_dot(rows, matrix):
    return jnp.dot(
        rows, matrix, precision=lax.Precision.HIGHEST, preferred_element_type=jnp.float32
    )


def along_z(rows, matrix):
    high = rows.astype(jnp.bfloat16)
    low = (rows - high.astype(jnp.float32)).astype(jnp.bfloat16)
    both = jnp.dot(
        jnp.concatenate([high, low], axis=1), matrix, preferred_element_type=jnp.float32
    )
    return both[:, :LANES] + both[:, LANES:]


def total(tile):
    return jnp.sum(jnp.sum(tile, axis=0, keepdims=True), axis=1, keepdims=True)


def store_y_faces(place, field, first_out, second_out, lead, at):
    for ex in range(2):
        for a in range(8):
            low = field[lead + (ex, a, 0, pl.ds(0, 1), slice(None))]
            high = field[lead + (ex, a, 1, pl.ds(7, 1), slice(None))]
            row = at + ex * 8 + a
            first_out[pl.ds(row, 1), :] = place.after_y(high, low)
            second_out[pl.ds(row, 1), :] = place.after_y(low, high)


def join_own(place, tiles):
    for ex in range(2):
        for a in range(8):
            tiles[ex][a] = list(place.join_y(*tiles[ex][a]))
    for ey in range(2):
        both = tiles[0][7][ey] + tiles[1][0][ey]
        tiles[0][7][ey] = both
        tiles[1][0][ey] = both


def weight_of(node):
    edge = jnp.minimum(node, 7 - node)
    value = jnp.where(edge == 2, float(WEIGHTS[2]), float(WEIGHTS[3]))
    return jnp.where(
        edge == 0, float(WEIGHTS[0]), jnp.where(edge == 1, float(WEIGHTS[1]), value)
    )


def mass_kernel(fields, out, xf, first, second):
    place = Place()
    weight = weight_of(place.row) * weight_of(place.lane % NODES)
    for ch in range(4):
        tiles = [
            [
                [
                    place.join_z(fields[ch, ex, a, ey] * (float(WEIGHTS[a]) * weight))
                    for ey in range(2)
                ]
                for a in range(8)
            ]
            for ex in range(2)
        ]
        join_own(place, tiles)
        for ex in range(2):
            for a in range(8):
                for ey in range(2):
                    out[ch, ex, a, ey] = tiles[ex][a][ey]
        for ey in range(2):
            xf[0, ch, ey] = tiles[0][0][ey]
            xf[1, ch, ey] = tiles[1][7][ey]
        store_y_faces(place, out, first, second, (ch,), ch * 16)


def turn_faces(place, xf, y_first, y_second, first, second):
    for ch in range(4):
        sides = []
        for side in range(2):
            row = pl.ds(ch * 16 + 15 * side, 1)
            got_a, got_b = y_first[row, :], y_second[row, :]
            low = xf[side, ch, 0] + jnp.where(place.row == 0, place.before_y(got_a, got_b), 0.0)
            high = xf[side, ch, 1] + jnp.where(place.row == 7, place.after_y(got_a, got_b), 0.0)
            sides.append((low, high))
        for ey in range(2):
            rows = pl.ds(ch * 16 + ey * 8, 8)
            first[rows, :] = place.after_x(sides[1][ey], sides[0][ey])
            second[rows, :] = place.after_x(sides[0][ey], sides[1][ey])


def turn_faces_kernel(pack_rows, xf, pack, y_first, y_second, first, second):
    turn_faces(Place(), xf, y_first, y_second, first, second)
    first[pl.ds(64, pack_rows), :] = pack[...]
    second[pl.ds(64, pack_rows), :] = pack[...]


def turn_edges(place, inner_x, y_first, y_second, first, second, at, edge, inner_y):
    sides = []
    for side in range(2):
        row = pl.ds(edge + side, 1)
        got_a, got_b = y_first[row, :], y_second[row, :]
        low = inner_x[side, 0] + jnp.where(place.row == 0, place.before_y(got_a, got_b), 0.0)
        high = inner_x[side, 1] + jnp.where(place.row == 7, place.after_y(got_a, got_b), 0.0)
        sides.append((low, high))
    for ey in range(2):
        rows = pl.ds(at + ey * 8, 8)
        first[rows, :] = place.after_x(sides[1][ey], sides[0][ey])
        second[rows, :] = place.after_x(sides[0][ey], sides[1][ey])
    for k, pick in enumerate((place.before_y, place.after_y)):
        sides = []
        for side in range(2):
            row = pl.ds(inner_y + 15 * side, 1)
            sides.append(pick(y_first[row, :], y_second[row, :]))
        row = pl.ds(edge + k, 1)
        first[row, :] = place.after_x(sides[1], sides[0])
        second[row, :] = place.after_x(sides[0], sides[1])


STEP_U, STEP_V, STEP_EDGE, STEP_PACK = 64, 64, 80, 82


def turn_step_kernel(xf, inner_x, y_first, y_second, first, second):
    place = Place()
    turn_faces(place, xf, y_first, y_second, first, second)
    turn_edges(place, inner_x, y_first, y_second, first, second, STEP_U, STEP_EDGE, STEP_V)


def setup_kernel(
    pack_rows,
    blocks,
    pack,
    x_first,
    x_second,
    y_first,
    y_second,
    ctab,
    inv_diag,
    kap,
    grp,
    coarse,
    compact,
    spread,
):
    place = Place()
    beside = pl.ds(64, pack_rows)
    packs = [[None] * 3 for _ in range(3)]
    packs[0][1] = place.before_x(x_first[beside, :], x_second[beside, :])
    packs[1][1] = pack[...]
    packs[2][1] = place.after_x(x_first[beside, :], x_second[beside, :])
    for dx in range(3):
        rows = pl.ds(STEP_PACK + dx * pack_rows, pack_rows)
        packs[dx][0] = place.before_y(y_first[rows, :], y_second[rows, :])
        packs[dx][2] = place.after_y(y_first[rows, :], y_second[rows, :])
    compact[...] = jnp.zeros(compact.shape, jnp.float32)
    for dx in range(3):
        for dy in range(3):
            at = (dx * 3 + dy) * NCD * blocks
            coarse[pl.ds(at, NCD * blocks), :] = packs[dx][dy][1 : 1 + NCD * blocks]
            compact[pl.ds(dx * 3 + dy, 1), :] = packs[dx][dy][0:1]
    elems = LANES // NODES
    lane = lax.broadcasted_iota(jnp.int32, (LANES, LANES), 1)
    source = lax.broadcasted_iota(jnp.int32, (LANES, LANES), 0)
    for k in range(8):
        spot = (source == k * elems + lane // NODES).astype(jnp.float32)
        spread[k] = exact_dot(compact[...], spot)
    there_x = [jnp.where(place.prev_x, 1.0, 0.0), 1.0, jnp.where(place.next_x, 1.0, 0.0)]
    there_y = [jnp.where(place.prev_y, 1.0, 0.0), 1.0, jnp.where(place.next_y, 1.0, 0.0)]

    def element_row(base, u, v):
        device = (u // 2) * 3 + v // 2
        return spread[base + (u % 2) * 2 + v % 2, pl.ds(device, 1), :]

    for x in range(4):
        for y in range(4):
            kap[pl.ds(x * 4 + y, 1), :] = element_row(0, x + 1, y + 1)
            grp[pl.ds(x * 4 + y, 1), :] = element_row(4, x + 1, y + 1)
    kappa = [
        [
            place.join_z(jnp.broadcast_to(element_row(0, u + 1, v + 1), TILE))
            for v in range(4)
        ]
        for u in range(4)
    ]
    count_z = 1.0 + jnp.where(place.low_z | place.high_z, 1.0, 0.0)
    weight = ctab[T_W]
    line = ctab[T_LINE]

    def pick(values, ey):
        low = values[ey] + values[ey + 1]
        high = values[ey + 1] + values[ey + 2]
        return jnp.where(place.row == 0, low, jnp.where(place.row == 7, high, values[ey + 1]))

    for ex in range(2):
        for kind in range(3):
            us = {0: (ex, ex + 1), 1: (ex + 1,), 2: (ex + 1, ex + 2)}[kind]
            sums, counts = [], []
            for v in range(4):
                acc, num = None, 0.0
                for u in us:
                    acc = kappa[u][v] if acc is None else acc + kappa[u][v]
                    num = num + there_x[(u + 1) // 2]
                sums.append(acc)
                counts.append(num * there_y[(v + 1) // 2])
            for ey in range(2):
                kappa_sum = pick(sums, ey)
                mult = pick(counts, ey) * count_z
                for a in {0: (0,), 1: range(1, 7), 2: (7,)}[kind]:
                    diag = (float(LINE[a]) + line) * kappa_sum + sigma_p * mult
                    inv_diag[ex, a, ey] = 1.0 / (diag * (float(WEIGHTS[a]) * weight))


OUTER = ((0, 0), (1, 7))


def got_y_sum(place, tile, ch, ex, a, ey, y_first, y_second):
    row = pl.ds(ch * 16 + ex * 8 + a, 1)
    got_a, got_b = y_first[row, :], y_second[row, :]
    if ey == 0:
        tile = tile + jnp.where(place.row == 0, place.before_y(got_a, got_b), 0.0)
    else:
        tile = tile + jnp.where(place.row == 7, place.after_y(got_a, got_b), 0.0)
    return tile


def got_x_sum(place, tile, ch, ex, ey, x_first, x_second):
    rows = pl.ds(ch * 16 + ey * 8, 8)
    pick = place.before_x if ex == 0 else place.after_x
    return tile + pick(x_first[rows, :], x_second[rows, :])


def pack_kernel(kappa, group, coarse, pack, facts):
    place = Place()
    facts[...] = jnp.zeros(facts.shape, jnp.float32)
    grid = jnp.zeros((1, LANES), jnp.float32)
    elems = kappa.shape[2]
    to = lax.broadcasted_iota(jnp.int32, (elems, LANES), 1)
    element = lax.broadcasted_iota(jnp.int32, (elems, LANES), 0)
    blocks = coarse.shape[1] // LANES
    packed = jnp.zeros((1, LANES), jnp.float32)
    for ex in range(2):
        numbers = group[ex].astype(jnp.float32)
        for ey in range(2):
            mine, number = kappa[ex, pl.ds(ey, 1), :], numbers[ey : ey + 1]
            at = (2 * ex + ey) * elems
            packed = packed + exact_dot(mine, (to == at + element).astype(jnp.float32))
            at = at + 4 * elems
            packed = packed + exact_dot(number, (to == at + element).astype(jnp.float32))
            at = ((2 * place.iy + ey) * elems + 4 * ex * elems) % LANES
            grid = grid + exact_dot(mine, (to == at + element).astype(jnp.float32))
            at = (at + 2 * elems) % LANES
            grid = grid + exact_dot(number, (to == at + element).astype(jnp.float32))
    pack[pl.ds(0, 1), :] = packed
    for c in range(NCD):
        for j in range(blocks):
            line = coarse[pl.ds(c, 1), pl.ds(j * LANES, LANES)]
            pack[pl.ds(1 + c * blocks + j, 1), :] = line
        facts[:, pl.ds((2 + c) * LANES, LANES)] = coarse[pl.ds(c, 1), pl.ds(0, LANES)]
    facts[:, pl.ds(LANES, LANES)] = grid


def prepare_kernel(
    summed, visc, y_first, y_second, ctab, zmat, start, part, slope, answer, grad_z, flux_z
):
    place = Place()
    weight = ctab[T_W]
    inv_mass = [1.0 / (weight * place.mult_tile(ey)) for ey in range(2)]

    def begin(ch, carry):
        for ex in range(2):
            for a in range(8):
                for ey in range(2):
                    tile = got_y_sum(
                        place, summed[ch, ex, a, ey], ch, ex, a, ey, y_first, y_second
                    )
                    scale = place.inv_x(ex, a) * float(1.0 / WEIGHTS[a])
                    start[ch, ex, a, ey] = tile * (inv_mass[ey] * scale)
        return carry

    lax.fori_loop(0, 4, begin, 0)
    grad_z[...] = along_z(start[...].reshape(1024, LANES), zmat[0]).reshape(grad_z.shape)

    def column(index, carry):
        ch, ey = index // 2, index % 2
        coef = jnp.where(ch == 3, 1.0 / prandtl, 1.0)
        for ex in range(2):
            grad_x = along_x(DERIV, [start[ch, ex, a, ey] for a in range(8)], -1)
            flux_x = [
                visc[ex, a, ey] * (float(WEIGHTS[a]) * weight) * coef * grad_x[a]
                for a in range(8)
            ]
            back = along_x(DERIV.T, flux_x, -1)
            for a in range(8):
                if (ex, a) in OUTER:
                    slope[ch, ex, ey] = grad_x[a]
                    part[ch, ex, a, ey] = back[a]
                    continue
                rest, flux_z[ch, ex, a, ey] = across(
                    ctab, weight, a, coef, start[ch, ex, a, ey], grad_z[ch, ex, a, ey],
                    start[1, ex, a, ey], start[2, ex, a, ey], visc[ex, a, ey],
                )
                flow = float(WEIGHTS[a]) * weight * start[0, ex, a, ey]
                part[ch, ex, a, ey] = rest + flow * grad_x[a] + back[a]
        return carry

    for ex, outer in OUTER:
        for ey in range(2):
            flux_x = [
                visc[ex, a, ey] * (float(WEIGHTS[a] * DERIV[a, outer]) * weight) for a in range(8)
            ]
            back = along_x(DERIV.T, flux_x, -1)
            for a in range(8):
                answer[ex, a, ey] = back[a]
    lax.fori_loop(0, 8, column, 0)
    for ch in range(4):
        for ex in range(2):
            inner = pl.ds(1 - ex, 7)
            back = along_z(flux_z[ch, ex, inner].reshape(112, LANES), zmat[1])
            part[ch, ex, inner] = part[ch, ex, inner] + back.reshape(7, 2, 8, LANES)


def across(ctab, weight, a, coef, value, grad_z, flow_y, flow_z, visc):
    node = float(WEIGHTS[a]) * weight
    grad_y = along_y(ctab, T_D, value)
    nu = visc * node * coef
    part = node * (flow_y * grad_y + flow_z * grad_z) + along_y(ctab, T_DT, nu * grad_y)
    return part, nu * grad_z


def rhs_kernel(
    pack_rows,
    begun,
    given,
    slope,
    answer,
    visc,
    pack,
    x_first,
    x_second,
    ctab,
    zmat,
    share,
    xf,
    inner_x,
    first,
    second,
    edge,
    edge_z,
    edge_part,
    came,
):
    place = Place()
    weight = ctab[T_W]
    inv_mass = [1.0 / (weight * place.mult_tile(ey)) for ey in range(2)]
    for ch in range(4):
        for side, (ex, a) in enumerate(OUTER):
            scale = place.inv_x(ex, a) * float(1.0 / WEIGHTS[a])
            for ey in range(2):
                zero = jnp.zeros(TILE, jnp.float32)
                extra = got_x_sum(place, zero, ch, ex, ey, x_first, x_second)
                extra = extra * (inv_mass[ey] * scale)
                came[ch, side, ey] = extra
                edge[ch, side, ey] = begun[ch, ex, a, ey] + extra
    edge_z[...] = along_z(edge[...].reshape(128, LANES), zmat[0]).reshape(edge.shape)
    for ch in range(4):
        coef = 1.0 / prandtl if ch == 3 else 1.0
        for side, (ex, a) in enumerate(OUTER):
            for ey in range(2):
                parts = across(
                    ctab, weight, a, coef, edge[ch, side, ey], edge_z[ch, side, ey],
                    edge[1, side, ey], edge[2, side, ey], visc[ex, a, ey],
                )
                edge_part[ch, side, ey], edge_z[ch, side, ey] = parts
    edge_part[...] = edge_part[...] + along_z(
        edge_z[...].reshape(128, LANES), zmat[1]
    ).reshape(edge.shape)

    def side_of(ch, ex, a, ey):
        outer = OUTER[ex][1]
        coef = jnp.where(ch == 3, 1.0 / prandtl, 1.0)
        extra = came[ch, ex, ey]
        node = float(WEIGHTS[a]) * weight
        turn = float(DERIV[a, outer])
        if a == outer:
            known = given[ch, ex, a, ey] + edge_part[ch, ex, ey]
            known = known + node * edge[0, ex, ey] * (slope[ch, ex, ey] + turn * extra)
            return known + extra * (coef * answer[ex, a, ey])
        flow = float(WEIGHTS[a] * turn) * weight * begun[0, ex, a, ey]
        return given[ch, ex, a, ey] + extra * (coef * answer[ex, a, ey] + flow)

    def finish(ch, carry):
        tiles = [
            [[place.join_z(-side_of(ch, ex, a, ey)) for ey in range(2)] for a in range(8)]
            for ex in range(2)
        ]
        join_own(place, tiles)
        for ex in range(2):
            for a in range(8):
                scale = place.inv_x(ex, a) * float(dt_step / WEIGHTS[a])
                for ey in range(2):
                    value = edge[ch, ex, ey] if (ex, a) in OUTER else begun[ch, ex, a, ey]
                    part = value * (place.share_y(ey) * place.share_x(ex, a))
                    share[ch, ex, a, ey] = part + tiles[ex][a][ey] * (inv_mass[ey] * scale)
        return carry

    lax.fori_loop(0, 4, finish, 0)
    for ch in range(4):
        store_y_faces(place, share, first, second, (ch,), ch * 16)
        for ey in range(2):
            xf[0, ch, ey] = share[ch, 0, 0, ey]
            xf[1, ch, ey] = share[ch, 1, 7, ey]

    def column_of(ex, ey):
        return [share[0, ex, a, ey] for a in range(8)]

    def tile_of(ex, a, ey):
        return share[1, ex, a, ey]

    store_inner(
        place, DERIV, ctab[T_BOTTOM], ctab[T_TOP], column_of, tile_of, inner_x, first, second,
        STEP_V, STEP_EDGE,
    )
    beside = pl.ds(64, pack_rows)
    parts = (
        place.before_x(x_first[beside, :], x_second[beside, :]),
        pack[...],
        place.after_x(x_first[beside, :], x_second[beside, :]),
    )
    for k in range(3):
        rows = pl.ds(STEP_PACK + k * pack_rows, pack_rows)
        first[rows, :] = parts[k]
        second[rows, :] = parts[k]


def store_inner(
    place, matrix, bottom, top, column_of, tile_of, inner_x, first, second, at, edge
):
    for ey in range(2):
        low, high = column_of(0, ey), column_of(1, ey)
        below = float(matrix[0, 1]) * low[1]
        above = float(matrix[7, 0]) * high[0]
        for k in range(2, 8):
            below = below + float(matrix[0, k]) * low[k]
            above = above + float(matrix[7, k - 1]) * high[k - 1]
        inner_x[0, ey] = below
        inner_x[1, ey] = above
    for side in range(2):
        low = inner_x[side, 0, pl.ds(0, 1), :]
        high = inner_x[side, 1, pl.ds(7, 1), :]
        first[pl.ds(edge + side, 1), :] = place.after_y(high, low)
        second[pl.ds(edge + side, 1), :] = place.after_y(low, high)
    for ex in range(2):
        for a in range(8):
            low = jnp.sum(bottom * tile_of(ex, a, 0), axis=0, keepdims=True)
            high = jnp.sum(top * tile_of(ex, a, 1), axis=0, keepdims=True)
            row = pl.ds(at + ex * 8 + a, 1)
            first[row, :] = place.after_y(high, low)
            second[row, :] = place.after_y(low, high)


def cross_flow(place, ctab, flow, slopes, rows, inv_y, inv_z):
    below, above = rows
    below = (below - float(DERIV[0, 0]) * flow[0]) * jnp.where(place.prev_y, 1.0, 0.0)
    above = (above - float(DERIV[7, 7]) * flow[1]) * jnp.where(place.next_y, 1.0, 0.0)
    grad_y = list(place.join_y(*[along_y(ctab, T_D, tile) for tile in flow]))
    grad_y[0] = grad_y[0] + jnp.where(place.row == 0, below, 0.0)
    grad_y[1] = grad_y[1] + jnp.where(place.row == 7, above, 0.0)
    return [grad_y[ey] * inv_y[ey] + place.join_z(slopes[ey]) * inv_z for ey in range(2)]


def approach_kernel(share, y_first, y_second, ctab, zmat, fields_new, part, grad_z):
    place = Place()

    def step(ch, carry):
        for ex in range(2):
            for a in range(8):
                for ey in range(2):
                    fields_new[ch, ex, a, ey] = got_y_sum(
                        place, share[ch, ex, a, ey], ch, ex, a, ey, y_first, y_second
                    )
        return carry

    lax.fori_loop(0, 4, step, 0)
    grad_z[...] = along_z(fields_new[2].reshape(256, LANES), zmat[0]).reshape(grad_z.shape)
    inv_y = [place.inv_y(ey) for ey in range(2)]
    inv_z = place.inv_z()
    for ex in range(2):
        for a in range(8):
            if (ex, a) in OUTER:
                continue
            flow = [fields_new[1, ex, a, ey] for ey in range(2)]
            rows = inner_along_y(place, y_first, y_second, None, None, ex, a, STEP_V, STEP_EDGE)
            slopes = [grad_z[ex, a, ey] for ey in range(2)]
            both = cross_flow(place, ctab, flow, slopes, rows, inv_y, inv_z)
            part[ex, a, 0], part[ex, a, 1] = both


def emit_kernel(begun, x_first, x_second, extra, fields_new, passed):
    place = Place()
    passed[...] = extra[...]
    fields_new[...] = begun[...]
    for ch in range(4):
        for ex, a in OUTER:
            for ey in range(2):
                fields_new[ch, ex, a, ey] = got_x_sum(
                    place, begun[ch, ex, a, ey], ch, ex, ey, x_first, x_second
                )


def advance_kernel(
    begun,
    given,
    y_first,
    y_second,
    x_first,
    x_second,
    inv_diag,
    kap,
    grp,
    ctab,
    zmat,
    resid,
    own,
    msg,
    grad_z,
    scaled,
    edge,
    part,
    outer,
):
    place = Place()
    weight = ctab[T_W]

    def before(row, count=8):
        rows = pl.ds(row, count)
        return place.before_x(x_first[rows, :], x_second[rows, :])

    def after(row, count=8):
        rows = pl.ds(row, count)
        return place.after_x(x_first[rows, :], x_second[rows, :])

    part[...] = given[...]
    for ch in range(3):
        for side, (ex, a) in enumerate(OUTER):
            for ey in range(2):
                outer[ch, side, ey] = got_x_sum(
                    place, begun[ch, ex, a, ey], ch, ex, ey, x_first, x_second
                )
    edge[...] = along_z(outer[2].reshape(32, LANES), zmat[0]).reshape(edge.shape)
    inv_y = [place.inv_y(ey) for ey in range(2)]
    inv_z = place.inv_z()
    for side, (ex, a) in enumerate(OUTER):
        flow = [outer[1, side, ey] for ey in range(2)]
        rows = inner_along_y(place, y_first, y_second, before, after, ex, a, STEP_V, STEP_EDGE)
        slopes = [edge[side, ey] for ey in range(2)]
        both = cross_flow(place, ctab, flow, slopes, rows, inv_y, inv_z)
        part[ex, a, 0], part[ex, a, 1] = both
    slope = [[None, None], [None, None]]
    for ey in range(2):
        for ex in range(2):
            line = [
                outer[0, ex, ey] if (ex, a) in OUTER else begun[0, ex, a, ey] for a in range(8)
            ]
            slope[ex][ey] = along_x(DERIV, line, -1)
        mid = 0.5 * (slope[0][ey][7] + slope[1][ey][0])
        slope[0][ey][7] = mid
        slope[1][ey][0] = mid
        low, high = slope[0][ey][0], slope[1][ey][7]
        inner_low = low - float(DERIV[0, 0]) * outer[0, 0, ey] + before(STEP_U + ey * 8)
        inner_high = high - float(DERIV[7, 7]) * outer[0, 1, ey] + after(STEP_U + ey * 8)
        slope[0][ey][0] = jnp.where(place.prev_x, 0.5 * inner_low, low)
        slope[1][ey][7] = jnp.where(place.next_x, 0.5 * inner_high, high)
    sums = [[jnp.zeros(TILE, jnp.float32) for _ in range(2)] for _ in range(2)]
    inv_mult = [1.0 / place.mult_tile(ey) for ey in range(2)]
    mass = [weight * place.mult_tile(ey) for ey in range(2)]
    for ex in range(2):
        for a in range(8):
            for ey in range(2):
                div = slope[ex][ey][a] + part[ex, a, ey]
                value = div * (mass[ey] * (place.mult_x(ex, a) * float(-WEIGHTS[a])))
                resid[ex, a, ey] = value
                scaled[ex, a, ey] = value * inv_diag[ex, a, ey] * float(1.0 / THETA)
                sums[ex][ey] = sums[ex][ey] + value * (inv_mult[ey] * place.inv_x(ex, a))
    grad_z[...] = along_z(scaled[...].reshape(256, LANES), zmat[2]).reshape(grad_z.shape)
    tiles = [[[None, None] for _ in range(8)] for _ in range(2)]
    for ex in range(2):
        for ey in range(2):
            images = own_operator(ctab, kap, scaled, grad_z, ex, ey)[1]
            for a in range(8):
                tiles[ex][a][ey] = place.join_z(images[a])
    join_own(place, tiles)
    for ex in range(2):
        for a in range(8):
            for ey in range(2):
                own[ex, a, ey] = tiles[ex][a][ey]
    row = message(place, restricted(place, sums, grp), [])
    blank = jnp.where(place.row == 0, jnp.broadcast_to(row, TILE), 0.0)
    zero = jnp.zeros(TILE, jnp.float32)

    def clear(i, carry):
        msg[i, pl.ds(0, 8), :] = zero
        msg[i, pl.ds(8, 8), :] = blank
        return carry

    lax.fori_loop(0, msg.shape[0], clear, 0)
    for dx, dy, there in neighbours(place):

        @pl.when(there)
        def _():
            to = (place.ix + dx) * place.ny + place.iy + dy
            ex, a = (0, 0) if dx < 0 else (1, 7)
            ey, b = (0, 0) if dy < 0 else (1, 7)
            if dy == 0:
                msg[to, pl.ds(0, 8), :] = own[ex, a, 0]
                msg[to, pl.ds(9, 7), :] = own[ex, a, 1, pl.ds(1, 7), :]
            elif dx == 0:
                for r in range(16):
                    if r != 8:
                        msg[to, pl.ds(r, 1), :] = own[r // 8, r % 8, ey, pl.ds(b, 1), :]
            else:
                msg[to, pl.ds(0, 1), :] = own[ex, a, ey, pl.ds(b, 1), :]


def inner_along_y(place, y_first, y_second, before, after, ex, a, at, edge):
    row = pl.ds(at + ex * 8 + a, 1)
    got_a, got_b = y_first[row, :], y_second[row, :]
    below, above = place.before_y(got_a, got_b), place.after_y(got_a, got_b)
    if before is None:
        return below, above
    if (ex, a) == (0, 0):
        below = below + before(edge, 1)
        above = above + before(edge + 1, 1)
    if (ex, a) == (1, 7):
        below = below + after(edge, 1)
        above = above + after(edge + 1, 1)
    return below, above


def neighbours(place):
    along = ((-1, place.prev_x), (0, None), (1, place.next_x))
    across = ((-1, place.prev_y), (0, None), (1, place.next_y))
    out = []
    for dx, has_x in along:
        for dy, has_y in across:
            if dx == 0 and dy == 0:
                continue
            there = has_y if has_x is None else (has_x if has_y is None else has_x & has_y)
            out.append((dx, dy, there))
    return out


SMOOTH_X, SMOOTH_Y, SMOOTH_EDGE, SMOOTH_ROWS = 16, 16, 32, 34


def turn_smooth_kernel(own, inner_x, y_first, y_second, first, second):
    place = Place()
    sides = []
    for side, (ex, a) in enumerate(((0, 0), (1, 7))):
        row = pl.ds(15 * side, 1)
        got_a, got_b = y_first[row, :], y_second[row, :]
        low = own[ex, a, 0] + jnp.where(place.row == 0, place.before_y(got_a, got_b), 0.0)
        high = own[ex, a, 1] + jnp.where(place.row == 7, place.after_y(got_a, got_b), 0.0)
        sides.append((low, high))
    for ey in range(2):
        rows = pl.ds(ey * 8, 8)
        first[rows, :] = place.after_x(sides[1][ey], sides[0][ey])
        second[rows, :] = place.after_x(sides[0][ey], sides[1][ey])
    turn_edges(
        place, inner_x, y_first, y_second, first, second, SMOOTH_X, SMOOTH_EDGE, SMOOTH_Y
    )


def restricted(place, sums, grp):
    values = []
    for c in range(NCD):
        acc = jnp.zeros(TILE, jnp.float32)
        for ex in range(2):
            for ey in range(2):
                group = grp[pl.ds((ex + 1) * 4 + ey + 1, 1), :]
                acc = acc + jnp.where(group == float(c), sums[ex][ey], 0.0)
        values.append(total(acc))
    return values


AWAY = 16
BEYOND = 18


def message(place, own_values, scalars, away=0, beyond=1):
    lane = lax.broadcasted_iota(jnp.int32, (1, LANES), 1)
    spot = (place.ix * place.ny + place.iy) % (LANES // NCD)
    after = (spot + beyond) % (LANES // NCD)
    spot = (spot + away) % (LANES // NCD)
    row = jnp.zeros((1, LANES), jnp.float32)
    for c, value in enumerate(own_values):
        row = row + jnp.where(lane == spot * NCD + c, value, 0.0)
    for c, value in enumerate(scalars):
        if value is None:
            continue
        row = row + jnp.where(lane == after * NCD + c, value, 0.0)
    return row


def send_to_all(msg, row):
    def send(i, carry):
        msg[i] = row
        return carry

    lax.fori_loop(0, msg.shape[0], send, 0, unroll=msg.shape[0] <= 64)


def cross_image(place, ctab, kap, value, flat, inner, ex, ey):
    slope_y = along_y(ctab, T_K, value)
    turned_y = inner + float(SCALED[0, 0]) * value
    own = kap[pl.ds((ex + 1) * 4 + ey + 1, 1), :] * (slope_y + flat) + sigma_p * value
    beyond = kap[pl.ds((ex + 1) * 4 + 3 * ey, 1), :] * (turned_y + flat) + sigma_p * value
    return own + jnp.where(beyond_y(place, ey), beyond, 0.0), slope_y, turned_y


def beyond_y(place, ey):
    if ey == 0:
        return (place.row == 0) & place.prev_y
    return (place.row == 7) & place.next_y


def ready_kernel(
    own, y_first, y_second, inv_diag, kap, ctab, zmat, image, scaled, part, slope_z
):
    place = Place()
    for ex in range(2):
        for a in range(8):
            for ey in range(2):
                tile = got_y_sum(place, own[ex, a, ey], 0, ex, a, ey, y_first, y_second)
                image[ex, a, ey] = tile
                scaled[ex, a, ey] = tile * inv_diag[ex, a, ey] * float(1.0 / THETA)
    slope_z[...] = along_z(scaled[...].reshape(256, LANES), zmat[2]).reshape(slope_z.shape)
    for ex in range(2):
        for a in range(8):
            if (ex, a) in OUTER:
                continue
            rows = inner_along_y(
                place, y_first, y_second, None, None, ex, a, SMOOTH_Y, SMOOTH_EDGE
            )
            for ey in range(2):
                part[ex, a, ey] = cross_image(
                    place, ctab, kap, scaled[ex, a, ey], slope_z[ex, a, ey], rows[ey], ex, ey
                )[0]


def smooth_kernel(
    begun,
    begun_scaled,
    given,
    y_first,
    y_second,
    x_first,
    x_second,
    inv_diag,
    kap,
    grp,
    extra,
    facts,
    ctab,
    zmat,
    image,
    smoothed,
    msg,
    scaled,
    slope_z,
    edge,
):
    place = Place()
    weight = ctab[T_W]
    corner = float(SCALED[0, 0])

    def before(row, count=8):
        rows = pl.ds(row, count)
        return place.before_x(x_first[rows, :], x_second[rows, :])

    def after(row, count=8):
        rows = pl.ds(row, count)
        return place.after_x(x_first[rows, :], x_second[rows, :])

    image[...] = begun[...]
    scaled[...] = begun_scaled[...]
    for side, (ex, a) in enumerate(OUTER):
        for ey in range(2):
            tile = got_x_sum(place, begun[ex, a, ey], 0, ex, ey, x_first, x_second)
            image[ex, a, ey] = tile
            scaled[ex, a, ey] = tile * inv_diag[ex, a, ey] * float(1.0 / THETA)
            edge[side, ey] = scaled[ex, a, ey]
    edge[...] = along_z(edge[...].reshape(32, LANES), zmat[2]).reshape(edge.shape)
    there_x = (place.prev_x, place.next_x)
    zero = jnp.zeros(TILE, jnp.float32)
    tiles = [[[None, None] for _ in range(8)] for _ in range(2)]
    for ex in range(2):
        a_out = OUTER[ex][1]
        rows = inner_along_y(
            place, y_first, y_second, before, after, ex, a_out, SMOOTH_Y, SMOOTH_EDGE
        )
        for ey in range(2):
            values = [scaled[ex, a, ey] for a in range(8)]
            slopes = along_x(SCALED, values, 1)
            far_row = beyond_y(place, ey)
            beside = kap[pl.ds((ex + 1) * 4 + 3 * ey, 1), :]
            kappa = kap[pl.ds((ex + 1) * 4 + ey + 1, 1), :] + jnp.where(far_row, beside, 0.0)
            for a in range(8):
                if a != a_out:
                    acc = given[ex, a, ey]
                else:
                    value, flat = values[a], edge[ex, ey]
                    acc, slope_y, turned_y = cross_image(
                        place, ctab, kap, value, flat, rows[ey], ex, ey
                    )
                    x_next = 3 * ex
                    get = before if ex == 0 else after
                    turned_x = get(SMOOTH_X + ey * 8) + corner * value
                    side = kap[pl.ds(x_next * 4 + ey + 1, 1), :] * (turned_x + slope_y + flat)
                    far = kap[pl.ds(x_next * 4 + 3 * ey, 1), :] * (turned_x + turned_y + flat)
                    side = side + sigma_p * value
                    side = side + jnp.where(far_row, far + sigma_p * value, zero)
                    acc = acc + jnp.where(there_x[ex], side, zero)
                acc = acc + kappa * slopes[a]
                tiles[ex][a][ey] = place.join_z(acc * (float(WEIGHTS[a]) * weight))
    join_own(place, tiles)
    inv_mult = [1.0 / place.mult_tile(ey) for ey in range(2)]
    sums = [[jnp.zeros(TILE, jnp.float32) for _ in range(2)] for _ in range(2)]
    square = jnp.zeros(TILE, jnp.float32)
    for ex in range(2):
        for a in range(8):
            for ey in range(2):
                value = image[ex, a, ey]
                defect = (value - tiles[ex][a][ey]) * inv_diag[ex, a, ey]
                update = scaled[ex, a, ey]
                result = (
                    float(1.0 + RHO_NEXT * RHO) * update + float(2.0 * RHO_NEXT / DELTA) * defect
                )
                smoothed[ex, a, ey] = result
                weighed = value * (inv_mult[ey] * place.inv_x(ex, a))
                sums[ex][ey] = sums[ex][ey] + weighed
                square = square + weighed * result
    own_sums = restricted(place, sums, grp)
    if msg.shape[2] == LANES:
        sums = [extra[:, pl.ds(k, 1)] for k in range(2)]
        send_to_all(msg, message(place, own_sums, sums))
        return
    slope_z[...] = along_z(smoothed[...].reshape(256, LANES), zmat[2]).reshape(slope_z.shape)
    energy = jnp.zeros(TILE, jnp.float32)
    for ex in range(2):
        for ey in range(2):
            values, images = own_operator(ctab, kap, smoothed, slope_z, ex, ey)
            for a in range(8):
                energy = energy + values[a] * images[a]
                tiles[ex][a][ey] = place.join_z(images[a])
    join_own(place, tiles)
    sums = [extra[:, pl.ds(k, 1)] for k in range(2)] + [total(square), total(energy)]
    row = message(place, own_sums, sums, AWAY, BEYOND)
    row = row + restricted_around(place, tiles, inv_mult, grp)
    send_to_all(msg, jnp.concatenate([row, facts[:, LANES:]], axis=1))


def restricted_around(place, tiles, inv_mult, grp):
    lane = lax.broadcasted_iota(jnp.int32, (1, LANES), 1)
    weighed = [
        [[tiles[ex][a][ey] * (inv_mult[ey] * place.inv_x(ex, a)) for ey in range(2)] for a in range(8)]
        for ex in range(2)
    ]

    def rows_of(tile, y):
        if y == 0:
            return jnp.where(place.row == 0, tile[0], 0.0)
        if y == 3:
            return jnp.where(place.row == 7, tile[1], 0.0)
        return tile[y - 1]

    there_x = (place.prev_x, None, None, place.next_x)
    there_y = (place.prev_y, None, None, place.next_y)
    by_device = [
        [[jnp.zeros(TILE, jnp.float32) for _ in range(NCD)] for _ in range(3)] for _ in range(3)
    ]
    for x in range(4):
        for y in range(4):
            if x == 0:
                acc = rows_of(weighed[0][0], y)
            elif x == 3:
                acc = rows_of(weighed[1][7], y)
            else:
                acc = rows_of(weighed[x - 1][0], y)
                for a in range(1, 8):
                    acc = acc + rows_of(weighed[x - 1][a], y)
            for there in (there_x[x], there_y[y]):
                if there is not None:
                    acc = jnp.where(there, acc, 0.0)
            group = grp[pl.ds(x * 4 + y, 1), :]
            device = by_device[(x + 1) // 2][(y + 1) // 2]
            for c in range(NCD):
                device[c] = device[c] + jnp.where(group == float(c), acc, 0.0)
    row = jnp.zeros((1, LANES), jnp.float32)
    for dx in range(3):
        for dy in range(3):
            at = ((place.ix + dx - 1) * place.ny + place.iy + dy - 1) * NCD
            for c in range(NCD):
                row = row + jnp.where(lane == at + c, total(by_device[dx][dy][c]), 0.0)
    return row


def coarse_part(place, blocks, got, coarse, grp, at=0):
    lane = lax.broadcasted_iota(jnp.int32, (1, LANES), 1)
    values = [jnp.zeros((1, LANES), jnp.float32) for _ in range(blocks)]
    per = LANES // NCD
    for j in range(blocks):

        def gather(i, acc, j=j):
            return jnp.where(lane // NCD == i, got[j * per + i, pl.ds(at, 1), :], acc)

        values[j] = lax.fori_loop(0, per, gather, values[j], unroll=blocks == 1)

    def solved(dx, dy, c):
        acc = None
        for j in range(blocks):
            term = coarse[pl.ds(((dx * 3 + dy) * NCD + c) * blocks + j, 1), :] * values[j]
            acc = term if acc is None else acc + term
        return jnp.sum(acc, axis=1, keepdims=True)

    return prolonged(place, solved, grp)


def prolonged(place, solved, grp):
    device = [[[solved(dx, dy, c) for c in range(NCD)] for dy in range(3)] for dx in range(3)]
    inv_z = jnp.where(place.low_z | place.high_z, 0.5, 1.0)
    rows = []
    for x in range(4):
        line = []
        for y in range(4):
            group = grp[pl.ds(x * 4 + y, 1), :]
            acc = jnp.zeros((1, LANES), jnp.float32)
            for c in range(NCD):
                acc = acc + jnp.where(
                    group == float(c), device[(x + 1) // 2][(y + 1) // 2][c], 0.0
                )
            line.append(place.join_z(jnp.broadcast_to(acc, TILE)) * inv_z)
        rows.append(line)
    low_y = jnp.where(place.prev_y, 0.5, 1.0)
    high_y = jnp.where(place.next_y, 0.5, 1.0)

    def tile(ex, kind, ey):
        if kind == 1:
            vals = [rows[ex + 1][y] for y in range(4)]
        elif kind == 0:
            scale = place.inv_x(ex, 0)
            vals = [(rows[ex][y] + rows[ex + 1][y]) * scale for y in range(4)]
        else:
            scale = place.inv_x(ex, 7)
            vals = [(rows[ex + 1][y] + rows[ex + 2][y]) * scale for y in range(4)]
        mid = vals[ey + 1]
        low = (vals[ey] + mid) * (low_y if ey == 0 else 0.5)
        high = (mid + vals[ey + 2]) * (high_y if ey == 1 else 0.5)
        return jnp.where(place.row == 0, low, jnp.where(place.row == 7, high, mid))

    return tile


def kind_of(a):
    return 0 if a == 0 else (2 if a == 7 else 1)


def own_operator(ctab, kap, field, slope_z, ex, ey):
    weight = ctab[T_W]
    tiles = [field[ex, a, ey] for a in range(8)]
    slopes = along_x(SCALED, tiles, 1)
    kappa = kap[pl.ds((ex + 1) * 4 + ey + 1, 1), :]
    out = []
    for a in range(8):
        stiff = slopes[a] + along_y(ctab, T_K, tiles[a]) + slope_z[ex, a, ey]
        out.append((kappa * stiff + sigma_p * tiles[a]) * (float(WEIGHTS[a]) * weight))
    return tiles, out


def first_direction_kernel(
    blocks,
    got,
    coarse,
    grp,
    kap,
    inv_diag,
    resid,
    own,
    ctab,
    zmat,
    direction,
    out,
    inner_x,
    first,
    second,
    extra,
    slope_z,
    image,
):
    place = Place()
    inv_mult = [1.0 / place.mult_tile(ey) for ey in range(2)]
    part = coarse_part(place, blocks, got, coarse, grp, 8)
    image[...] = own[...]
    for dx, dy, there in neighbours(place):

        @pl.when(there)
        def _():
            frm = (place.ix + dx) * place.ny + place.iy + dy
            ex, a = (0, 0) if dx < 0 else (1, 7)
            ey, b = (0, 0) if dy < 0 else (1, 7)
            edge = place.row == b
            if dy == 0:
                low = got[frm, pl.ds(0, 8), :]
                high = jnp.where(
                    place.row == 0, pltpu.roll(low, 1, 0), got[frm, pl.ds(8, 8), :]
                )
                image[ex, a, 0] = image[ex, a, 0] + low
                image[ex, a, 1] = image[ex, a, 1] + high
            elif dx == 0:
                for r in range(16):
                    line = got[frm, pl.ds(7 if r == 8 else r, 1), :]
                    tile = image[r // 8, r % 8, ey]
                    image[r // 8, r % 8, ey] = tile + jnp.where(edge, line, 0.0)
            else:
                line = got[frm, pl.ds(0, 1), :]
                image[ex, a, ey] = image[ex, a, ey] + jnp.where(edge, line, 0.0)

    energy = jnp.zeros(TILE, jnp.float32)
    for ex in range(2):
        for ey in range(2):
            kinds = [part(ex, kind, ey) for kind in range(3)]
            for a in range(8):
                known = resid[ex, a, ey]
                inverse = inv_diag[ex, a, ey]
                defect = (known - image[ex, a, ey]) * inverse
                value = (
                    float((1.0 + RHO_NEXT * RHO) / THETA) * (known * inverse)
                    + float(2.0 * RHO_NEXT / DELTA) * defect
                    + kinds[kind_of(a)]
                )
                direction[ex, a, ey] = value
                scale = place.inv_x(ex, a)
                energy = energy + value * known * (inv_mult[ey] * scale)
    slope_z[...] = along_z(direction[...].reshape(256, LANES), zmat[2]).reshape(slope_z.shape)
    curvature = jnp.zeros(TILE, jnp.float32)
    tiles = [[[None, None] for _ in range(8)] for _ in range(2)]
    for ex in range(2):
        for ey in range(2):
            values, images = own_operator(ctab, kap, direction, slope_z, ex, ey)
            for a in range(8):
                curvature = curvature + values[a] * images[a]
                tiles[ex][a][ey] = place.join_z(images[a])
    join_own(place, tiles)
    for ex in range(2):
        for a in range(8):
            for ey in range(2):
                out[ex, a, ey] = tiles[ex][a][ey]
    store_y_faces(place, out, first, second, (), 0)

    def tile_of(ex, a, ey):
        return tiles[ex][a][ey] * inv_diag[ex, a, ey] * float(1.0 / THETA)

    def column_of(ex, ey):
        return [tile_of(ex, a, ey) for a in range(8)]

    store_inner(
        place, SCALED, ctab[T_KBOTTOM], ctab[T_KTOP], column_of, tile_of, inner_x, first, second,
        SMOOTH_Y, SMOOTH_EDGE,
    )
    lane = lax.broadcasted_iota(jnp.int32, (1, LANES), 1)
    extra[...] = jnp.where(lane == 0, total(energy), total(curvature))


def gathered_scalars(got, count):
    lane = lax.broadcasted_iota(jnp.int32, (1, LANES), 1)
    per = LANES // NCD
    sums = []
    for c in range(count):
        acc = jnp.zeros((1, LANES), jnp.float32)

        def gather(i, acc, c=c):
            return acc + jnp.where(lane == ((i + 1) % per) * NCD + c, got[i], 0.0)

        acc = lax.fori_loop(0, got.shape[0], gather, acc, unroll=got.shape[0] <= per)
        sums.append(jnp.sum(acc, axis=1, keepdims=True))
    return sums


def second_direction_kernel(
    blocks,
    got,
    coarse,
    grp,
    kap,
    resid,
    direction,
    image,
    smoothed,
    ctab,
    zmat,
    following,
    known,
    msg,
    slope_z,
):
    place = Place()
    inv_mult = [1.0 / place.mult_tile(ey) for ey in range(2)]
    part = coarse_part(place, blocks, got, coarse, grp)
    energy, curvature = gathered_scalars(got, 2)
    step = energy / curvature
    lane = lax.broadcasted_iota(jnp.int32, (1, LANES), 1)
    known[...] = jnp.where(lane == 0, energy, jnp.where(lane == 1, curvature, 0.0))
    energy_next = jnp.zeros(TILE, jnp.float32)
    cross = jnp.zeros(TILE, jnp.float32)
    for ex in range(2):
        for ey in range(2):
            kinds = [part(ex, kind, ey) for kind in range(3)]
            for a in range(8):
                value = direction[ex, a, ey] - step * (smoothed[ex, a, ey] + kinds[kind_of(a)])
                following[ex, a, ey] = value
                weighed = value * (inv_mult[ey] * place.inv_x(ex, a))
                was = image[ex, a, ey]
                energy_next = energy_next + weighed * (resid[ex, a, ey] - step * was)
                cross = cross + weighed * was
    slope_z[...] = along_z(following[...].reshape(256, LANES), zmat[2]).reshape(slope_z.shape)
    square = jnp.zeros(TILE, jnp.float32)
    for ex in range(2):
        for ey in range(2):
            values, images = own_operator(ctab, kap, following, slope_z, ex, ey)
            for a in range(8):
                square = square + values[a] * images[a]
    send_to_all(msg, message(place, [], [total(energy_next), total(square), total(cross)]))


def pressure_kernel(got, known, direction, following, pressure):
    energy = known[:, pl.ds(0, 1)]
    curvature = known[:, pl.ds(1, 1)]
    energy_next, square, cross = gathered_scalars(got, 3)
    ratio = energy_next / energy
    step = energy / curvature
    step_next = energy_next / (square + 2.0 * ratio * cross + ratio * ratio * curvature)
    weight_old = step + step_next * ratio
    for ex in range(2):
        for a in range(8):
            for ey in range(2):
                pressure[ex, a, ey] = (
                    weight_old * direction[ex, a, ey] + step_next * following[ex, a, ey]
                )


def coarse_energy(place, got, values, kappa, number):
    lane, row = place.lane, place.row
    for ex in range(2):
        for gx in range(8):
            own = jnp.zeros((1, LANES), jnp.float32)
            group = jnp.zeros((1, LANES), jnp.float32)
            spot = lane[0:1] // 32
            for gy in range(4):
                line = got[gx * 4 + gy, :, pl.ds(LANES, LANES)]
                own = jnp.where(spot == (gy + 2 * ex) % 4, line, own)
                group = jnp.where(spot == (gy + 1 + 2 * ex) % 4, line, group)
            kappa[ex, pl.ds(gx, 1), :] = own
            number[ex, pl.ds(gx, 1), :] = group
    grid = [jnp.zeros(TILE, jnp.float32) for _ in range(2)]
    numbers = [pltpu.roll(number[0], 96, 1), pltpu.roll(number[1], 32, 1)]
    kappa = [kappa[0], pltpu.roll(kappa[1], 64, 1)]
    for q in range(4):
        for c in range(NCD):
            mine = jnp.where(lane == row * 16 + q * 4 + c, values, 0.0)
            mine = jnp.sum(mine, axis=1, keepdims=True)
            for ex in range(2):
                chosen = (lane // 32 == q) & (numbers[ex] == float(c))
                grid[ex] = jnp.where(chosen, mine, grid[ex])

    def ends_y(v):
        low = jnp.where(lane >= 16, 0.5 * (v + pltpu.roll(v, 16, 1)), v)
        return low, v, jnp.where(lane < 112, 0.5 * (v + pltpu.roll(v, 112, 1)), v)

    def ends_z(v):
        low = jnp.where(lane % 16 > 0, 0.5 * (v + pltpu.roll(v, 1, 1)), v)
        return low, v, jnp.where(lane % 16 < 15, 0.5 * (v + pltpu.roll(v, 127, 1)), v)

    low = jnp.where(row > 0, 0.5 * (grid[0] + pltpu.roll(grid[1], 1, 0)), grid[0])
    mid = 0.5 * (grid[0] + grid[1])
    high = jnp.where(row < 7, 0.5 * (grid[1] + pltpu.roll(grid[0], 7, 0)), grid[1])
    mass = [float(WEIGHTS[0]), float(np.sum(WEIGHTS[1:7])), float(WEIGHTS[7])]
    links = (
        (0, 1, -float(np.sum(STIFF[0, 1:7]))),
        (0, 2, -float(STIFF[0, 7])),
        (1, 2, -float(np.sum(STIFF[7, 1:7]))),
    )
    energy = jnp.zeros(TILE, jnp.float32)
    for ex, line in enumerate(((low, grid[0], mid), (mid, grid[1], high))):
        nodes = [[ends_z(v) for v in ends_y(w)] for w in line]
        stiff = jnp.zeros(TILE, jnp.float32)
        square = jnp.zeros(TILE, jnp.float32)
        for i in range(3):
            for j in range(3):
                for k, l, weight in links:
                    factor = weight * mass[i] * mass[j]
                    for first, second in (
                        (nodes[k][i][j], nodes[l][i][j]),
                        (nodes[i][k][j], nodes[i][l][j]),
                        (nodes[i][j][k], nodes[i][j][l]),
                    ):
                        gap = first - second
                        stiff = stiff + (factor * gap) * gap
                for k in range(3):
                    value = nodes[i][j][k]
                    square = square + (mass[i] * mass[j] * mass[k] * value) * value
        energy = energy + kappa[ex] * stiff + sigma_p * square
    return total(energy)


def finish_kernel(
    got, grp, direction, smoothed, pressure, matrix, kappa, number
):
    place = Place()
    per = LANES // NCD
    row_lane = lax.broadcasted_iota(jnp.int32, (1, LANES), 1)
    rest = jnp.zeros((1, LANES), jnp.float32)
    dual = jnp.zeros((1, LANES), jnp.float32)
    sums = [jnp.zeros((1, LANES), jnp.float32) for _ in range(4)]
    for i in range(per):
        line = got[i, :, pl.ds(0, LANES)]
        mine = row_lane // NCD == (i + AWAY) % per
        known = row_lane // NCD == (i + BEYOND) % per
        rest = jnp.where(mine, line, rest)
        dual = dual + jnp.where(mine | known, 0.0, line)
        for c in range(4):
            sums[c] = sums[c] + jnp.where(row_lane == ((i + BEYOND) % per) * NCD + c, line, 0.0)
            block = got[i, :, pl.ds((2 + c) * LANES, LANES)]
            matrix[pl.ds(i * NCD + c, 1), :] = block
    rest = pltpu.roll(rest, (per - AWAY) * NCD, 1)
    energy, curvature, square, self_energy = [
        jnp.sum(value, axis=1, keepdims=True) for value in sums
    ]
    values = lax.dot_general(
        jnp.broadcast_to(rest, TILE),
        matrix[...],
        (((1,), (1,)), ((), ())),
        precision=lax.Precision.HIGHEST,
        preferred_element_type=jnp.float32,
    )
    line = values[0:1]
    cross = square + jnp.sum(line * rest, axis=1, keepdims=True)
    both = self_energy + 2.0 * jnp.sum(line * dual, axis=1, keepdims=True)
    both = both + coarse_energy(place, got, values, kappa, number)
    step = energy / curvature
    energy_next = step * step * cross - energy
    ratio = energy_next / energy
    with_image = curvature - step * cross
    with_itself = curvature - 2.0 * step * cross + step * step * both
    step_next = energy_next / (
        with_itself + 2.0 * ratio * with_image + ratio * ratio * curvature
    )
    old = step + step_next * (1.0 + ratio)
    new = -step_next * step

    def solved(dx, dy, c):
        at = ((place.ix + dx - 1) * place.ny + place.iy + dy - 1) * NCD + c
        return jnp.sum(jnp.where(row_lane == at, line, 0.0), axis=1, keepdims=True)

    part = prolonged(place, masked(place, solved), grp)
    for ex in range(2):
        for ey in range(2):
            kinds = [part(ex, kind, ey) for kind in range(3)]
            for a in range(8):
                pressure[ex, a, ey] = old * direction[ex, a, ey] + new * (
                    smoothed[ex, a, ey] + kinds[kind_of(a)]
                )


def masked(place, solved):
    there_x = (place.prev_x, None, place.next_x)
    there_y = (place.prev_y, None, place.next_y)

    def value(dx, dy, c):
        out = solved(dx, dy, c)
        for there in (there_x[dx], there_y[dy]):
            if there is not None:
                out = jnp.where(there, out, 0.0)
        return out

    return value


def call(body, outs, scratch=(), **more):
    return pl.pallas_call(
        body,
        out_shape=[jax.ShapeDtypeStruct(shape, jnp.float32) for shape in outs],
        scratch_shapes=[
            pltpu.VMEM(shape, jnp.float32) if isinstance(shape, tuple) else shape
            for shape in scratch
        ],
        **more,
        compiler_params=pltpu.CompilerParams(vmem_limit_bytes=24 * 1024 * 1024),
    )


def swap(first, second, axis):
    count = lax.axis_size(axis)
    first_pairs = [(i, i ^ 1) for i in range(count) if i ^ 1 < count]
    second_pairs = [(i, ((i + 1) ^ 1) - 1) for i in range(1, count) if ((i + 1) ^ 1) - 1 < count]
    second_got = lax.ppermute(second, axis, second_pairs)
    return lax.ppermute(first, axis, first_pairs), second_got


def per_device(fields, viscosity, inv_density, elem_group, coarse_inverse):
    length = fields.shape[5]
    elems_z = length // NODES
    devices = lax.axis_size("gx") * lax.axis_size("gy")
    blocks = coarse_inverse.shape[1] // LANES
    pack_rows = 1 + NCD * blocks
    tiles_np, mats_np = constant_tables(elems_z)
    ctab, zmat = jnp.asarray(tiles_np), jnp.asarray(mats_np)
    one = fields.shape[1:]
    four = fields.shape
    faces = (64, LANES)
    xf_shape = (2, 4, 2, 8, LANES)
    inner_shape = (2, 2, 8, LANES)
    y_shape, x_shape = (STEP_PACK + 3 * pack_rows, LANES), (STEP_PACK, LANES)
    turned = (64 + pack_rows, LANES)
    smooth_shape = (SMOOTH_ROWS, LANES)
    rows = (devices, 1, LANES)
    grid_fits = (
        blocks == 1
        and lax.axis_size("gx") == 8
        and lax.axis_size("gy") * fields.shape[3] * elems_z == LANES
    )

    def exchange_all(msg):
        return lax.all_to_all(msg, BOTH, 0, 0, tiled=True)

    beside = pl.CostEstimate(flops=10**7, bytes_accessed=10**6, transcendentals=0)
    summed, xf, first, second = call(
        mass_kernel,
        [four, xf_shape, faces, faces],
    )(fields)
    pack, facts = call(
        pack_kernel,
        [(pack_rows, LANES), (1, 6 * LANES)],
        cost_estimate=beside,
    )(inv_density, elem_group, coarse_inverse)
    y_got = swap(first, second, "gy")
    first, second = call(functools.partial(turn_faces_kernel, pack_rows), [turned, turned])(
        xf, pack, *y_got
    )
    side_got = x_got = swap(first, second, "gx")
    edge_shape = (4, 2, 2, 8, LANES)
    begun, given, slope, answer = call(
        prepare_kernel, [four, four, edge_shape, one], [four, four], cost_estimate=beside
    )(summed, viscosity, *y_got, ctab, zmat)
    share, xf, inner_x, first, second = call(
        functools.partial(rhs_kernel, pack_rows),
        [four, xf_shape, inner_shape, y_shape, y_shape],
        [edge_shape, edge_shape, edge_shape, edge_shape],
    )(begun, given, slope, answer, viscosity, pack, *x_got, ctab, zmat)
    y_got = swap(first, second, "gy")
    first, second = call(turn_step_kernel, [x_shape, x_shape])(xf, inner_x, *y_got)
    x_got = swap(first, second, "gx")
    inv_diag, kap, grp, coarse = call(
        functools.partial(setup_kernel, pack_rows, blocks),
        [one, (16, LANES), (16, LANES), (9 * NCD * blocks, LANES)],
        [(16, LANES), (8, 16, LANES)],
        cost_estimate=beside,
    )(pack, *side_got, *y_got, ctab)
    begun, given = call(approach_kernel, [four, one], [one], cost_estimate=beside)(
        share, *y_got, ctab, zmat
    )
    side_shape = (2, 2, 8, LANES)
    fields_got = x_got
    fields_begun = begun
    resid, own, msg = call(
        advance_kernel,
        [one, one, (devices, 16, LANES)],
        [one, one, side_shape, one, (3,) + side_shape],
    )(begun, given, *y_got, *x_got, inv_diag, kap, grp, ctab, zmat)
    got = exchange_all(msg)
    direction, own, inner_x, first, second, extra = call(
        functools.partial(first_direction_kernel, blocks),
        [one, one, inner_shape, smooth_shape, smooth_shape, (1, LANES)],
        [one, one],
    )(got, coarse, grp, kap, inv_diag, resid, own, ctab, zmat)
    y_got = swap(first, second, "gy")
    first, second = call(turn_smooth_kernel, [smooth_shape, smooth_shape])(own, inner_x, *y_got)
    x_got = swap(first, second, "gx")
    fields_new, extra = call(emit_kernel, [four, (1, LANES)], cost_estimate=beside)(
        fields_begun, *fields_got, extra
    )
    begun, begun_scaled, given = call(
        ready_kernel, [one, one, one], [one], cost_estimate=beside
    )(own, *y_got, inv_diag, kap, ctab, zmat)
    image, image_smoothed, msg = call(
        smooth_kernel,
        [one, one, (devices, 1, 6 * LANES) if grid_fits else rows],
        [one, one, side_shape],
    )(
        begun, begun_scaled, given, *y_got, *x_got, inv_diag, kap, grp, extra, facts, ctab, zmat
    )
    got = exchange_all(msg)
    if grid_fits:
        (pressure,) = call(
            finish_kernel, [one], [(LANES, LANES), (2,) + TILE, (2,) + TILE]
        )(got, grp, direction, image_smoothed)
        return (fields_new, pressure)
    following, known, msg = call(
        functools.partial(second_direction_kernel, blocks), [one, (1, LANES), rows], [one]
    )(got, coarse, grp, kap, resid, direction, image, image_smoothed, ctab, zmat)
    got = exchange_all(msg)
    (pressure,) = call(pressure_kernel, [one])(got, known, direction, following)
    return (fields_new, pressure)


def solution(mesh):
    placed = (
        P(None, "gx", None, "gy", None, None),
        P("gx", None, "gy", None, None),
        P("gx", "gy", None),
        P("gx", "gy", None),
        P(("gx", "gy"), None),
    )
    return jax.shard_map(
        per_device,
        mesh=mesh,
        in_specs=placed,
        out_specs=(P(None, "gx", None, "gy", None, None), P("gx", None, "gy", None, None)),
        check_vma=False,
    )
```

```python
import functools

import jax
import jax.numpy as jnp
import ml_dtypes
import numpy as np
from jax import lax
from jax.experimental import pallas as pl
from jax.experimental.pallas import tpu as pltpu
from jax.sharding import PartitionSpec as P

NCD = 4
NODES = 8
LANES = 128
TILE = (8, 128)
BOTH = ("gx", "gy")

dt_step = 0.01
sigma_p = 4.0
prandtl = 0.7
cheb_ratio = 0.1


def tables():
    points = np.array(
        [
            -1.0,
            -0.8717401485096066,
            -0.5917001814331423,
            -0.2092992179024789,
            0.2092992179024789,
            0.5917001814331423,
            0.8717401485096066,
            1.0,
        ]
    )
    weights = np.array(
        [
            1.0 / 28.0,
            0.2107042271435061,
            0.3411226924835044,
            0.4124587946587038,
            0.4124587946587038,
            0.3411226924835044,
            0.2107042271435061,
            1.0 / 28.0,
        ]
    )
    identity = np.eye(8)
    differ = points[:, None] - points[None, :] + identity
    barycentric = 1.0 / np.prod(differ, axis=1)
    offdiag = barycentric[None, :] / barycentric[:, None] / differ * (1.0 - identity)
    derivative = offdiag - identity * np.sum(offdiag, axis=1)[:, None]
    mass_one = identity * weights[None, :]
    stiff_one = derivative.T @ mass_one @ derivative
    stiff_three = (
        np.kron(np.kron(stiff_one, mass_one), mass_one)
        + np.kron(np.kron(mass_one, stiff_one), mass_one)
        + np.kron(np.kron(mass_one, mass_one), stiff_one)
    )
    three_diag = np.sum(stiff_three * np.eye(512), axis=1)
    spectral_bound = float(np.max(np.sum(np.abs(stiff_three), axis=1) / three_diag))
    return (derivative, weights, stiff_one, spectral_bound)


DERIV, WEIGHTS, STIFF, BOUND = tables()
SCALED = STIFF / WEIGHTS[:, None]
LINE = np.diag(STIFF) / WEIGHTS
THETA = 0.5 * (BOUND + cheb_ratio * BOUND)
DELTA = 0.5 * (BOUND - cheb_ratio * BOUND)
RHO = DELTA / THETA
RHO_NEXT = 1.0 / (2.0 * THETA / DELTA - RHO)


def constant_tables(elems_z):
    def turned(matrix):
        rows = np.arange(8)
        return [np.repeat(matrix[rows, (rows - s) % 8][:, None], LANES, 1) for s in range(8)]

    wz = np.tile(WEIGHTS, elems_z)
    kz = np.tile(LINE, elems_z)
    tiles = turned(DERIV) + turned(DERIV.T) + turned(SCALED)
    tiles += [WEIGHTS[:, None] * wz[None, :], LINE[:, None] + kz[None, :]]
    for matrix in (DERIV, SCALED):
        for node in (7, 0):
            inner = matrix[node] * (np.arange(8) != node)
            tiles.append(np.repeat(inner[:, None], LANES, 1))
    eye = np.eye(elems_z)
    mats = [np.kron(eye, DERIV.T), np.kron(eye, DERIV), np.kron(eye, SCALED.T)]
    halves = []
    for mat in mats:
        high = mat.astype(ml_dtypes.bfloat16)
        low = (mat - high.astype(np.float64)).astype(ml_dtypes.bfloat16)
        both = np.concatenate([high, low], 1)
        halves.append(np.concatenate([both, both], 0))
    return np.stack(tiles).astype(np.float32), np.stack(halves)


T_D, T_DT, T_K, T_W, T_LINE = 0, 8, 16, 24, 25
T_TOP, T_BOTTOM, T_KTOP, T_KBOTTOM = 26, 27, 28, 29


class Place:
    def __init__(self):
        self.ix = lax.axis_index("gx")
        self.iy = lax.axis_index("gy")
        self.nx = lax.axis_size("gx")
        self.ny = lax.axis_size("gy")
        self.even_x = self.ix % 2 == 0
        self.even_y = self.iy % 2 == 0
        self.row = lax.broadcasted_iota(jnp.int32, TILE, 0)
        self.lane = lax.broadcasted_iota(jnp.int32, TILE, 1)
        self.low_z = (self.lane % 8 == 0) & (self.lane > 0)
        self.high_z = (self.lane % 8 == 7) & (self.lane < LANES - 1)
        self.prev_x = self.ix > 0
        self.next_x = self.ix < self.nx - 1
        self.prev_y = self.iy > 0
        self.next_y = self.iy < self.ny - 1

    def mult_tile(self, ey):
        along_z = 1.0 + jnp.where(self.low_z | self.high_z, 1.0, 0.0)
        low = 1.0 if ey == 1 else jnp.where(self.prev_y, 1.0, 0.0)
        high = 1.0 if ey == 0 else jnp.where(self.next_y, 1.0, 0.0)
        along_y = 1.0 + jnp.where(self.row == 0, low, jnp.where(self.row == 7, high, 0.0))
        return along_y * along_z

    def inv_x(self, ex, a):
        if a == 0:
            return 0.5 if ex == 1 else jnp.where(self.prev_x, 0.5, 1.0)
        if a == 7:
            return 0.5 if ex == 0 else jnp.where(self.next_x, 0.5, 1.0)
        return 1.0

    def mult_x(self, ex, a):
        if a == 0:
            return 2.0 if ex == 1 else jnp.where(self.prev_x, 2.0, 1.0)
        if a == 7:
            return 2.0 if ex == 0 else jnp.where(self.next_x, 2.0, 1.0)
        return 1.0

    def share_x(self, ex, a):
        if (ex, a) == (0, 0):
            return jnp.where(self.prev_x, 0.5, 1.0)
        if (ex, a) == (1, 7):
            return jnp.where(self.next_x, 0.5, 1.0)
        return 1.0

    def share_y(self, ey):
        if ey == 0:
            return jnp.where((self.row == 0) & self.prev_y, 0.5, 1.0)
        return jnp.where((self.row == 7) & self.next_y, 0.5, 1.0)

    def inv_y(self, ey):
        low = 0.5 if ey == 1 else jnp.where(self.prev_y, 0.5, 1.0)
        high = 0.5 if ey == 0 else jnp.where(self.next_y, 0.5, 1.0)
        return jnp.where(self.row == 0, low, jnp.where(self.row == 7, high, 1.0))

    def inv_z(self):
        return jnp.where(self.low_z | self.high_z, 0.5, 1.0)

    def join_z(self, t):
        up = pltpu.roll(t, LANES - 1, 1)
        down = pltpu.roll(t, 1, 1)
        return t + jnp.where(self.high_z, up, jnp.where(self.low_z, down, 0.0))

    def to_low(self, below):
        return jnp.where(self.row == 0, pltpu.roll(below, 1, 0), 0.0)

    def to_high(self, above):
        return jnp.where(self.row == 7, pltpu.roll(above, 7, 0), 0.0)

    def join_y(self, below, above):
        return below + self.to_high(above), above + self.to_low(below)

    def before_x(self, first, second):
        return jnp.where(self.even_x, first, second)

    def after_x(self, first, second):
        return jnp.where(self.even_x, second, first)

    def before_y(self, first, second):
        return jnp.where(self.even_y, second, first)

    def after_y(self, first, second):
        return jnp.where(self.even_y, first, second)


def along_x(matrix, tiles, sign):
    even = [tiles[a] + tiles[7 - a] for a in range(4)]
    odd = [tiles[a] - tiles[7 - a] for a in range(4)]
    out = [None] * 8
    for i in range(4):
        plus, minus = None, None
        for a in range(4):
            p = float(0.5 * (matrix[i, a] + matrix[i, 7 - a])) * even[a]
            m = float(0.5 * (matrix[i, a] - matrix[i, 7 - a])) * odd[a]
            plus = p if plus is None else plus + p
            minus = m if minus is None else minus + m
        out[i] = plus + minus
        out[7 - i] = minus - plus if sign < 0 else plus - minus
    return out


def along_y(ctab, base, tile):
    acc = ctab[base] * tile
    for s in range(1, 8):
        acc = acc + ctab[base + s] * pltpu.roll(tile, s, 0)
    return acc


def exact_dot(rows, matrix):
    return jnp.dot(
        rows, matrix, precision=lax.Precision.HIGHEST, preferred_element_type=jnp.float32
    )


def along_z(rows, matrix):
    high = rows.astype(jnp.bfloat16)
    low = (rows - high.astype(jnp.float32)).astype(jnp.bfloat16)
    both = jnp.dot(
        jnp.concatenate([high, low], axis=1), matrix, preferred_element_type=jnp.float32
    )
    return both[:, :LANES] + both[:, LANES:]


def total(tile):
    return jnp.sum(jnp.sum(tile, axis=0, keepdims=True), axis=1, keepdims=True)


def store_y_faces(place, field, first_out, second_out, lead, at):
    for ex in range(2):
        for a in range(8):
            low = field[lead + (ex, a, 0, pl.ds(0, 1), slice(None))]
            high = field[lead + (ex, a, 1, pl.ds(7, 1), slice(None))]
            row = at + ex * 8 + a
            first_out[pl.ds(row, 1), :] = place.after_y(high, low)
            second_out[pl.ds(row, 1), :] = place.after_y(low, high)


def join_own(place, tiles):
    for ex in range(2):
        for a in range(8):
            tiles[ex][a] = list(place.join_y(*tiles[ex][a]))
    for ey in range(2):
        both = tiles[0][7][ey] + tiles[1][0][ey]
        tiles[0][7][ey] = both
        tiles[1][0][ey] = both


def weight_of(node):
    edge = jnp.minimum(node, 7 - node)
    value = jnp.where(edge == 2, float(WEIGHTS[2]), float(WEIGHTS[3]))
    return jnp.where(
        edge == 0, float(WEIGHTS[0]), jnp.where(edge == 1, float(WEIGHTS[1]), value)
    )


def mass_kernel(fields, out, xf, first, second):
    place = Place()
    weight = weight_of(place.row) * weight_of(place.lane % NODES)
    for ch in range(4):
        tiles = [
            [
                [
                    place.join_z(fields[ch, ex, a, ey] * (float(WEIGHTS[a]) * weight))
                    for ey in range(2)
                ]
                for a in range(8)
            ]
            for ex in range(2)
        ]
        join_own(place, tiles)
        for ex in range(2):
            for a in range(8):
                for ey in range(2):
                    out[ch, ex, a, ey] = tiles[ex][a][ey]
        for ey in range(2):
            xf[0, ch, ey] = tiles[0][0][ey]
            xf[1, ch, ey] = tiles[1][7][ey]
        store_y_faces(place, out, first, second, (ch,), ch * 16)


def turn_faces(place, xf, y_first, y_second, first, second):
    for ch in range(4):
        sides = []
        for side in range(2):
            row = pl.ds(ch * 16 + 15 * side, 1)
            got_a, got_b = y_first[row, :], y_second[row, :]
            low = xf[side, ch, 0] + jnp.where(place.row == 0, place.before_y(got_a, got_b), 0.0)
            high = xf[side, ch, 1] + jnp.where(place.row == 7, place.after_y(got_a, got_b), 0.0)
            sides.append((low, high))
        for ey in range(2):
            rows = pl.ds(ch * 16 + ey * 8, 8)
            first[rows, :] = place.after_x(sides[1][ey], sides[0][ey])
            second[rows, :] = place.after_x(sides[0][ey], sides[1][ey])


def turn_faces_kernel(pack_rows, xf, pack, y_first, y_second, first, second):
    turn_faces(Place(), xf, y_first, y_second, first, second)
    first[pl.ds(64, pack_rows), :] = pack[...]
    second[pl.ds(64, pack_rows), :] = pack[...]


def turn_edges(place, inner_x, y_first, y_second, first, second, at, edge, inner_y):
    sides = []
    for side in range(2):
        row = pl.ds(edge + side, 1)
        got_a, got_b = y_first[row, :], y_second[row, :]
        low = inner_x[side, 0] + jnp.where(place.row == 0, place.before_y(got_a, got_b), 0.0)
        high = inner_x[side, 1] + jnp.where(place.row == 7, place.after_y(got_a, got_b), 0.0)
        sides.append((low, high))
    for ey in range(2):
        rows = pl.ds(at + ey * 8, 8)
        first[rows, :] = place.after_x(sides[1][ey], sides[0][ey])
        second[rows, :] = place.after_x(sides[0][ey], sides[1][ey])
    for k, pick in enumerate((place.before_y, place.after_y)):
        sides = []
        for side in range(2):
            row = pl.ds(inner_y + 15 * side, 1)
            sides.append(pick(y_first[row, :], y_second[row, :]))
        row = pl.ds(edge + k, 1)
        first[row, :] = place.after_x(sides[1], sides[0])
        second[row, :] = place.after_x(sides[0], sides[1])


STEP_U, STEP_V, STEP_EDGE, STEP_PACK = 64, 64, 80, 82


def turn_step_kernel(xf, inner_x, y_first, y_second, first, second):
    place = Place()
    turn_faces(place, xf, y_first, y_second, first, second)
    turn_edges(place, inner_x, y_first, y_second, first, second, STEP_U, STEP_EDGE, STEP_V)


def setup_kernel(
    pack_rows,
    blocks,
    pack,
    x_first,
    x_second,
    y_first,
    y_second,
    ctab,
    inv_diag,
    kap,
    grp,
    coarse,
    compact,
    spread,
):
    place = Place()
    beside = pl.ds(64, pack_rows)
    packs = [[None] * 3 for _ in range(3)]
    packs[0][1] = place.before_x(x_first[beside, :], x_second[beside, :])
    packs[1][1] = pack[...]
    packs[2][1] = place.after_x(x_first[beside, :], x_second[beside, :])
    for dx in range(3):
        rows = pl.ds(STEP_PACK + dx * pack_rows, pack_rows)
        packs[dx][0] = place.before_y(y_first[rows, :], y_second[rows, :])
        packs[dx][2] = place.after_y(y_first[rows, :], y_second[rows, :])
    compact[...] = jnp.zeros(compact.shape, jnp.float32)
    for dx in range(3):
        for dy in range(3):
            at = (dx * 3 + dy) * NCD * blocks
            coarse[pl.ds(at, NCD * blocks), :] = packs[dx][dy][1 : 1 + NCD * blocks]
            compact[pl.ds(dx * 3 + dy, 1), :] = packs[dx][dy][0:1]
    elems = LANES // NODES
    lane = lax.broadcasted_iota(jnp.int32, (LANES, LANES), 1)
    source = lax.broadcasted_iota(jnp.int32, (LANES, LANES), 0)
    for k in range(8):
        spot = (source == k * elems + lane // NODES).astype(jnp.float32)
        spread[k] = exact_dot(compact[...], spot)
    there_x = [jnp.where(place.prev_x, 1.0, 0.0), 1.0, jnp.where(place.next_x, 1.0, 0.0)]
    there_y = [jnp.where(place.prev_y, 1.0, 0.0), 1.0, jnp.where(place.next_y, 1.0, 0.0)]

    def element_row(base, u, v):
        device = (u // 2) * 3 + v // 2
        return spread[base + (u % 2) * 2 + v % 2, pl.ds(device, 1), :]

    for x in range(4):
        for y in range(4):
            kap[pl.ds(x * 4 + y, 1), :] = element_row(0, x + 1, y + 1)
            grp[pl.ds(x * 4 + y, 1), :] = element_row(4, x + 1, y + 1)
    kappa = [
        [
            place.join_z(jnp.broadcast_to(element_row(0, u + 1, v + 1), TILE))
            for v in range(4)
        ]
        for u in range(4)
    ]
    count_z = 1.0 + jnp.where(place.low_z | place.high_z, 1.0, 0.0)
    weight = ctab[T_W]
    line = ctab[T_LINE]

    def pick(values, ey):
        low = values[ey] + values[ey + 1]
        high = values[ey + 1] + values[ey + 2]
        return jnp.where(place.row == 0, low, jnp.where(place.row == 7, high, values[ey + 1]))

    for ex in range(2):
        for kind in range(3):
            us = {0: (ex, ex + 1), 1: (ex + 1,), 2: (ex + 1, ex + 2)}[kind]
            sums, counts = [], []
            for v in range(4):
                acc, num = None, 0.0
                for u in us:
                    acc = kappa[u][v] if acc is None else acc + kappa[u][v]
                    num = num + there_x[(u + 1) // 2]
                sums.append(acc)
                counts.append(num * there_y[(v + 1) // 2])
            for ey in range(2):
                kappa_sum = pick(sums, ey)
                mult = pick(counts, ey) * count_z
                for a in {0: (0,), 1: range(1, 7), 2: (7,)}[kind]:
                    diag = (float(LINE[a]) + line) * kappa_sum + sigma_p * mult
                    inv_diag[ex, a, ey] = 1.0 / (diag * (float(WEIGHTS[a]) * weight))


OUTER = ((0, 0), (1, 7))


def got_y_sum(place, tile, ch, ex, a, ey, y_first, y_second):
    row = pl.ds(ch * 16 + ex * 8 + a, 1)
    got_a, got_b = y_first[row, :], y_second[row, :]
    if ey == 0:
        tile = tile + jnp.where(place.row == 0, place.before_y(got_a, got_b), 0.0)
    else:
        tile = tile + jnp.where(place.row == 7, place.after_y(got_a, got_b), 0.0)
    return tile


def got_x_sum(place, tile, ch, ex, ey, x_first, x_second):
    rows = pl.ds(ch * 16 + ey * 8, 8)
    pick = place.before_x if ex == 0 else place.after_x
    return tile + pick(x_first[rows, :], x_second[rows, :])


def pack_kernel(kappa, group, coarse, pack, facts):
    place = Place()
    facts[...] = jnp.zeros(facts.shape, jnp.float32)
    grid = jnp.zeros((1, LANES), jnp.float32)
    elems = kappa.shape[2]
    to = lax.broadcasted_iota(jnp.int32, (elems, LANES), 1)
    element = lax.broadcasted_iota(jnp.int32, (elems, LANES), 0)
    blocks = coarse.shape[1] // LANES
    packed = jnp.zeros((1, LANES), jnp.float32)
    for ex in range(2):
        numbers = group[ex].astype(jnp.float32)
        for ey in range(2):
            mine, number = kappa[ex, pl.ds(ey, 1), :], numbers[ey : ey + 1]
            at = (2 * ex + ey) * elems
            packed = packed + exact_dot(mine, (to == at + element).astype(jnp.float32))
            at = at + 4 * elems
            packed = packed + exact_dot(number, (to == at + element).astype(jnp.float32))
            at = ((2 * place.iy + ey) * elems + 4 * ex * elems) % LANES
            grid = grid + exact_dot(mine, (to == at + element).astype(jnp.float32))
            at = (at + 2 * elems) % LANES
            grid = grid + exact_dot(number, (to == at + element).astype(jnp.float32))
    pack[pl.ds(0, 1), :] = packed
    for c in range(NCD):
        for j in range(blocks):
            line = coarse[pl.ds(c, 1), pl.ds(j * LANES, LANES)]
            pack[pl.ds(1 + c * blocks + j, 1), :] = line
        facts[:, pl.ds((2 + c) * LANES, LANES)] = coarse[pl.ds(c, 1), pl.ds(0, LANES)]
    facts[:, pl.ds(LANES, LANES)] = grid


def prepare_kernel(
    summed, visc, y_first, y_second, ctab, zmat, start, part, slope, answer, grad_z, flux_z
):
    place = Place()
    weight = ctab[T_W]
    inv_mass = [1.0 / (weight * place.mult_tile(ey)) for ey in range(2)]

    def begin(ch, carry):
        for ex in range(2):
            for a in range(8):
                for ey in range(2):
                    tile = got_y_sum(
                        place, summed[ch, ex, a, ey], ch, ex, a, ey, y_first, y_second
                    )
                    scale = place.inv_x(ex, a) * float(1.0 / WEIGHTS[a])
                    start[ch, ex, a, ey] = tile * (inv_mass[ey] * scale)
        return carry

    lax.fori_loop(0, 4, begin, 0)
    grad_z[...] = along_z(start[...].reshape(1024, LANES), zmat[0]).reshape(grad_z.shape)

    def column(index, carry):
        ch, ey = index // 2, index % 2
        coef = jnp.where(ch == 3, 1.0 / prandtl, 1.0)
        for ex in range(2):
            grad_x = along_x(DERIV, [start[ch, ex, a, ey] for a in range(8)], -1)
            flux_x = [
                visc[ex, a, ey] * (float(WEIGHTS[a]) * weight) * coef * grad_x[a]
                for a in range(8)
            ]
            back = along_x(DERIV.T, flux_x, -1)
            for a in range(8):
                if (ex, a) in OUTER:
                    slope[ch, ex, ey] = grad_x[a]
                    part[ch, ex, a, ey] = back[a]
                    continue
                rest, flux_z[ch, ex, a, ey] = across(
                    ctab, weight, a, coef, start[ch, ex, a, ey], grad_z[ch, ex, a, ey],
                    start[1, ex, a, ey], start[2, ex, a, ey], visc[ex, a, ey],
                )
                flow = float(WEIGHTS[a]) * weight * start[0, ex, a, ey]
                part[ch, ex, a, ey] = rest + flow * grad_x[a] + back[a]
        return carry

    for ex, outer in OUTER:
        for ey in range(2):
            flux_x = [
                visc[ex, a, ey] * (float(WEIGHTS[a] * DERIV[a, outer]) * weight) for a in range(8)
            ]
            back = along_x(DERIV.T, flux_x, -1)
            for a in range(8):
                answer[ex, a, ey] = back[a]
    lax.fori_loop(0, 8, column, 0)
    for ch in range(4):
        for ex in range(2):
            inner = pl.ds(1 - ex, 7)
            back = along_z(flux_z[ch, ex, inner].reshape(112, LANES), zmat[1])
            part[ch, ex, inner] = part[ch, ex, inner] + back.reshape(7, 2, 8, LANES)


def across(ctab, weight, a, coef, value, grad_z, flow_y, flow_z, visc):
    node = float(WEIGHTS[a]) * weight
    grad_y = along_y(ctab, T_D, value)
    nu = visc * node * coef
    part = node * (flow_y * grad_y + flow_z * grad_z) + along_y(ctab, T_DT, nu * grad_y)
    return part, nu * grad_z


def rhs_kernel(
    pack_rows,
    begun,
    given,
    slope,
    answer,
    visc,
    pack,
    x_first,
    x_second,
    ctab,
    zmat,
    share,
    xf,
    inner_x,
    first,
    second,
    edge,
    edge_z,
    edge_part,
    came,
):
    place = Place()
    weight = ctab[T_W]
    inv_mass = [1.0 / (weight * place.mult_tile(ey)) for ey in range(2)]
    for ch in range(4):
        for side, (ex, a) in enumerate(OUTER):
            scale = place.inv_x(ex, a) * float(1.0 / WEIGHTS[a])
            for ey in range(2):
                zero = jnp.zeros(TILE, jnp.float32)
                extra = got_x_sum(place, zero, ch, ex, ey, x_first, x_second)
                extra = extra * (inv_mass[ey] * scale)
                came[ch, side, ey] = extra
                edge[ch, side, ey] = begun[ch, ex, a, ey] + extra
    edge_z[...] = along_z(edge[...].reshape(128, LANES), zmat[0]).reshape(edge.shape)
    for ch in range(4):
        coef = 1.0 / prandtl if ch == 3 else 1.0
        for side, (ex, a) in enumerate(OUTER):
            for ey in range(2):
                parts = across(
                    ctab, weight, a, coef, edge[ch, side, ey], edge_z[ch, side, ey],
                    edge[1, side, ey], edge[2, side, ey], visc[ex, a, ey],
                )
                edge_part[ch, side, ey], edge_z[ch, side, ey] = parts
    edge_part[...] = edge_part[...] + along_z(
        edge_z[...].reshape(128, LANES), zmat[1]
    ).reshape(edge.shape)

    def side_of(ch, ex, a, ey):
        outer = OUTER[ex][1]
        coef = jnp.where(ch == 3, 1.0 / prandtl, 1.0)
        extra = came[ch, ex, ey]
        node = float(WEIGHTS[a]) * weight
        turn = float(DERIV[a, outer])
        if a == outer:
            known = given[ch, ex, a, ey] + edge_part[ch, ex, ey]
            known = known + node * edge[0, ex, ey] * (slope[ch, ex, ey] + turn * extra)
            return known + extra * (coef * answer[ex, a, ey])
        flow = float(WEIGHTS[a] * turn) * weight * begun[0, ex, a, ey]
        return given[ch, ex, a, ey] + extra * (coef * answer[ex, a, ey] + flow)

    def finish(ch, carry):
        tiles = [
            [[place.join_z(-side_of(ch, ex, a, ey)) for ey in range(2)] for a in range(8)]
            for ex in range(2)
        ]
        join_own(place, tiles)
        for ex in range(2):
            for a in range(8):
                scale = place.inv_x(ex, a) * float(dt_step / WEIGHTS[a])
                for ey in range(2):
                    value = edge[ch, ex, ey] if (ex, a) in OUTER else begun[ch, ex, a, ey]
                    part = value * (place.share_y(ey) * place.share_x(ex, a))
                    share[ch, ex, a, ey] = part + tiles[ex][a][ey] * (inv_mass[ey] * scale)
        return carry

    lax.fori_loop(0, 4, finish, 0)
    for ch in range(4):
        store_y_faces(place, share, first, second, (ch,), ch * 16)
        for ey in range(2):
            xf[0, ch, ey] = share[ch, 0, 0, ey]
            xf[1, ch, ey] = share[ch, 1, 7, ey]

    def column_of(ex, ey):
        return [share[0, ex, a, ey] for a in range(8)]

    def tile_of(ex, a, ey):
        return share[1, ex, a, ey]

    store_inner(
        place, DERIV, ctab[T_BOTTOM], ctab[T_TOP], column_of, tile_of, inner_x, first, second,
        STEP_V, STEP_EDGE,
    )
    beside = pl.ds(64, pack_rows)
    parts = (
        place.before_x(x_first[beside, :], x_second[beside, :]),
        pack[...],
        place.after_x(x_first[beside, :], x_second[beside, :]),
    )
    for k in range(3):
        rows = pl.ds(STEP_PACK + k * pack_rows, pack_rows)
        first[rows, :] = parts[k]
        second[rows, :] = parts[k]


def store_inner(
    place, matrix, bottom, top, column_of, tile_of, inner_x, first, second, at, edge
):
    for ey in range(2):
        low, high = column_of(0, ey), column_of(1, ey)
        below = float(matrix[0, 1]) * low[1]
        above = float(matrix[7, 0]) * high[0]
        for k in range(2, 8):
            below = below + float(matrix[0, k]) * low[k]
            above = above + float(matrix[7, k - 1]) * high[k - 1]
        inner_x[0, ey] = below
        inner_x[1, ey] = above
    for side in range(2):
        low = inner_x[side, 0, pl.ds(0, 1), :]
        high = inner_x[side, 1, pl.ds(7, 1), :]
        first[pl.ds(edge + side, 1), :] = place.after_y(high, low)
        second[pl.ds(edge + side, 1), :] = place.after_y(low, high)
    for ex in range(2):
        for a in range(8):
            low = jnp.sum(bottom * tile_of(ex, a, 0), axis=0, keepdims=True)
            high = jnp.sum(top * tile_of(ex, a, 1), axis=0, keepdims=True)
            row = pl.ds(at + ex * 8 + a, 1)
            first[row, :] = place.after_y(high, low)
            second[row, :] = place.after_y(low, high)


def cross_flow(place, ctab, flow, slopes, rows, inv_y, inv_z):
    below, above = rows
    below = (below - float(DERIV[0, 0]) * flow[0]) * jnp.where(place.prev_y, 1.0, 0.0)
    above = (above - float(DERIV[7, 7]) * flow[1]) * jnp.where(place.next_y, 1.0, 0.0)
    grad_y = list(place.join_y(*[along_y(ctab, T_D, tile) for tile in flow]))
    grad_y[0] = grad_y[0] + jnp.where(place.row == 0, below, 0.0)
    grad_y[1] = grad_y[1] + jnp.where(place.row == 7, above, 0.0)
    return [grad_y[ey] * inv_y[ey] + place.join_z(slopes[ey]) * inv_z for ey in range(2)]


def approach_kernel(share, y_first, y_second, ctab, zmat, fields_new, part, grad_z):
    place = Place()

    def step(ch, carry):
        for ex in range(2):
            for a in range(8):
                for ey in range(2):
                    fields_new[ch, ex, a, ey] = got_y_sum(
                        place, share[ch, ex, a, ey], ch, ex, a, ey, y_first, y_second
                    )
        return carry

    lax.fori_loop(0, 4, step, 0)
    grad_z[...] = along_z(fields_new[2].reshape(256, LANES), zmat[0]).reshape(grad_z.shape)
    inv_y = [place.inv_y(ey) for ey in range(2)]
    inv_z = place.inv_z()
    for ex in range(2):
        for a in range(8):
            if (ex, a) in OUTER:
                continue
            flow = [fields_new[1, ex, a, ey] for ey in range(2)]
            rows = inner_along_y(place, y_first, y_second, None, None, ex, a, STEP_V, STEP_EDGE)
            slopes = [grad_z[ex, a, ey] for ey in range(2)]
            both = cross_flow(place, ctab, flow, slopes, rows, inv_y, inv_z)
            part[ex, a, 0], part[ex, a, 1] = both


def emit_kernel(begun, x_first, x_second, extra, fields_new, passed):
    place = Place()
    passed[...] = extra[...]
    fields_new[...] = begun[...]
    for ch in range(4):
        for ex, a in OUTER:
            for ey in range(2):
                fields_new[ch, ex, a, ey] = got_x_sum(
                    place, begun[ch, ex, a, ey], ch, ex, ey, x_first, x_second
                )


def advance_kernel(
    begun,
    given,
    y_first,
    y_second,
    x_first,
    x_second,
    inv_diag,
    kap,
    grp,
    ctab,
    zmat,
    resid,
    own,
    msg,
    grad_z,
    scaled,
    edge,
    part,
    outer,
):
    place = Place()
    weight = ctab[T_W]

    def before(row, count=8):
        rows = pl.ds(row, count)
        return place.before_x(x_first[rows, :], x_second[rows, :])

    def after(row, count=8):
        rows = pl.ds(row, count)
        return place.after_x(x_first[rows, :], x_second[rows, :])

    part[...] = given[...]
    for ch in range(3):
        for side, (ex, a) in enumerate(OUTER):
            for ey in range(2):
                outer[ch, side, ey] = got_x_sum(
                    place, begun[ch, ex, a, ey], ch, ex, ey, x_first, x_second
                )
    edge[...] = along_z(outer[2].reshape(32, LANES), zmat[0]).reshape(edge.shape)
    inv_y = [place.inv_y(ey) for ey in range(2)]
    inv_z = place.inv_z()
    for side, (ex, a) in enumerate(OUTER):
        flow = [outer[1, side, ey] for ey in range(2)]
        rows = inner_along_y(place, y_first, y_second, before, after, ex, a, STEP_V, STEP_EDGE)
        slopes = [edge[side, ey] for ey in range(2)]
        both = cross_flow(place, ctab, flow, slopes, rows, inv_y, inv_z)
        part[ex, a, 0], part[ex, a, 1] = both
    slope = [[None, None], [None, None]]
    for ey in range(2):
        for ex in range(2):
            line = [
                outer[0, ex, ey] if (ex, a) in OUTER else begun[0, ex, a, ey] for a in range(8)
            ]
            slope[ex][ey] = along_x(DERIV, line, -1)
        mid = 0.5 * (slope[0][ey][7] + slope[1][ey][0])
        slope[0][ey][7] = mid
        slope[1][ey][0] = mid
        low, high = slope[0][ey][0], slope[1][ey][7]
        inner_low = low - float(DERIV[0, 0]) * outer[0, 0, ey] + before(STEP_U + ey * 8)
        inner_high = high - float(DERIV[7, 7]) * outer[0, 1, ey] + after(STEP_U + ey * 8)
        slope[0][ey][0] = jnp.where(place.prev_x, 0.5 * inner_low, low)
        slope[1][ey][7] = jnp.where(place.next_x, 0.5 * inner_high, high)
    sums = [[jnp.zeros(TILE, jnp.float32) for _ in range(2)] for _ in range(2)]
    inv_mult = [1.0 / place.mult_tile(ey) for ey in range(2)]
    mass = [weight * place.mult_tile(ey) for ey in range(2)]
    for ex in range(2):
        for a in range(8):
            for ey in range(2):
                div = slope[ex][ey][a] + part[ex, a, ey]
                value = div * (mass[ey] * (place.mult_x(ex, a) * float(-WEIGHTS[a])))
                resid[ex, a, ey] = value
                scaled[ex, a, ey] = value * inv_diag[ex, a, ey] * float(1.0 / THETA)
                sums[ex][ey] = sums[ex][ey] + value * (inv_mult[ey] * place.inv_x(ex, a))
    grad_z[...] = along_z(scaled[...].reshape(256, LANES), zmat[2]).reshape(grad_z.shape)
    tiles = [[[None, None] for _ in range(8)] for _ in range(2)]
    for ex in range(2):
        for ey in range(2):
            images = own_operator(ctab, kap, scaled, grad_z, ex, ey)[1]
            for a in range(8):
                tiles[ex][a][ey] = place.join_z(images[a])
    join_own(place, tiles)
    for ex in range(2):
        for a in range(8):
            for ey in range(2):
                own[ex, a, ey] = tiles[ex][a][ey]
    row = message(place, restricted(place, sums, grp), [])
    blank = jnp.where(place.row == 0, jnp.broadcast_to(row, TILE), 0.0)
    zero = jnp.zeros(TILE, jnp.float32)

    def clear(i, carry):
        msg[i, pl.ds(0, 8), :] = zero
        msg[i, pl.ds(8, 8), :] = blank
        return carry

    lax.fori_loop(0, msg.shape[0], clear, 0)
    for dx, dy, there in neighbours(place):

        @pl.when(there)
        def _():
            to = (place.ix + dx) * place.ny + place.iy + dy
            ex, a = (0, 0) if dx < 0 else (1, 7)
            ey, b = (0, 0) if dy < 0 else (1, 7)
            if dy == 0:
                msg[to, pl.ds(0, 8), :] = own[ex, a, 0]
                msg[to, pl.ds(9, 7), :] = own[ex, a, 1, pl.ds(1, 7), :]
            elif dx == 0:
                for r in range(16):
                    if r != 8:
                        msg[to, pl.ds(r, 1), :] = own[r // 8, r % 8, ey, pl.ds(b, 1), :]
            else:
                msg[to, pl.ds(0, 1), :] = own[ex, a, ey, pl.ds(b, 1), :]


def inner_along_y(place, y_first, y_second, before, after, ex, a, at, edge):
    row = pl.ds(at + ex * 8 + a, 1)
    got_a, got_b = y_first[row, :], y_second[row, :]
    below, above = place.before_y(got_a, got_b), place.after_y(got_a, got_b)
    if before is None:
        return below, above
    if (ex, a) == (0, 0):
        below = below + before(edge, 1)
        above = above + before(edge + 1, 1)
    if (ex, a) == (1, 7):
        below = below + after(edge, 1)
        above = above + after(edge + 1, 1)
    return below, above


def neighbours(place):
    along = ((-1, place.prev_x), (0, None), (1, place.next_x))
    across = ((-1, place.prev_y), (0, None), (1, place.next_y))
    out = []
    for dx, has_x in along:
        for dy, has_y in across:
            if dx == 0 and dy == 0:
                continue
            there = has_y if has_x is None else (has_x if has_y is None else has_x & has_y)
            out.append((dx, dy, there))
    return out


SMOOTH_X, SMOOTH_Y, SMOOTH_EDGE, SMOOTH_ROWS = 16, 16, 32, 34


def turn_smooth_kernel(own, inner_x, y_first, y_second, first, second):
    place = Place()
    sides = []
    for side, (ex, a) in enumerate(((0, 0), (1, 7))):
        row = pl.ds(15 * side, 1)
        got_a, got_b = y_first[row, :], y_second[row, :]
        low = own[ex, a, 0] + jnp.where(place.row == 0, place.before_y(got_a, got_b), 0.0)
        high = own[ex, a, 1] + jnp.where(place.row == 7, place.after_y(got_a, got_b), 0.0)
        sides.append((low, high))
    for ey in range(2):
        rows = pl.ds(ey * 8, 8)
        first[rows, :] = place.after_x(sides[1][ey], sides[0][ey])
        second[rows, :] = place.after_x(sides[0][ey], sides[1][ey])
    turn_edges(
        place, inner_x, y_first, y_second, first, second, SMOOTH_X, SMOOTH_EDGE, SMOOTH_Y
    )


def restricted(place, sums, grp):
    values = []
    for c in range(NCD):
        acc = jnp.zeros(TILE, jnp.float32)
        for ex in range(2):
            for ey in range(2):
                group = grp[pl.ds((ex + 1) * 4 + ey + 1, 1), :]
                acc = acc + jnp.where(group == float(c), sums[ex][ey], 0.0)
        values.append(total(acc))
    return values


AWAY = 16
BEYOND = 18


def message(place, own_values, scalars, away=0, beyond=1):
    lane = lax.broadcasted_iota(jnp.int32, (1, LANES), 1)
    spot = (place.ix * place.ny + place.iy) % (LANES // NCD)
    after = (spot + beyond) % (LANES // NCD)
    spot = (spot + away) % (LANES // NCD)
    row = jnp.zeros((1, LANES), jnp.float32)
    for c, value in enumerate(own_values):
        row = row + jnp.where(lane == spot * NCD + c, value, 0.0)
    for c, value in enumerate(scalars):
        if value is None:
            continue
        row = row + jnp.where(lane == after * NCD + c, value, 0.0)
    return row


def send_to_all(msg, row):
    def send(i, carry):
        msg[i] = row
        return carry

    lax.fori_loop(0, msg.shape[0], send, 0, unroll=msg.shape[0] <= 64)


def cross_image(place, ctab, kap, value, flat, inner, ex, ey):
    slope_y = along_y(ctab, T_K, value)
    turned_y = inner + float(SCALED[0, 0]) * value
    own = kap[pl.ds((ex + 1) * 4 + ey + 1, 1), :] * (slope_y + flat) + sigma_p * value
    beyond = kap[pl.ds((ex + 1) * 4 + 3 * ey, 1), :] * (turned_y + flat) + sigma_p * value
    return own + jnp.where(beyond_y(place, ey), beyond, 0.0), slope_y, turned_y


def beyond_y(place, ey):
    if ey == 0:
        return (place.row == 0) & place.prev_y
    return (place.row == 7) & place.next_y


def ready_kernel(
    own, y_first, y_second, inv_diag, kap, ctab, zmat, image, scaled, part, slope_z
):
    place = Place()
    for ex in range(2):
        for a in range(8):
            for ey in range(2):
                tile = got_y_sum(place, own[ex, a, ey], 0, ex, a, ey, y_first, y_second)
                image[ex, a, ey] = tile
                scaled[ex, a, ey] = tile * inv_diag[ex, a, ey] * float(1.0 / THETA)
    slope_z[...] = along_z(scaled[...].reshape(256, LANES), zmat[2]).reshape(slope_z.shape)
    for ex in range(2):
        for a in range(8):
            if (ex, a) in OUTER:
                continue
            rows = inner_along_y(
                place, y_first, y_second, None, None, ex, a, SMOOTH_Y, SMOOTH_EDGE
            )
            for ey in range(2):
                part[ex, a, ey] = cross_image(
                    place, ctab, kap, scaled[ex, a, ey], slope_z[ex, a, ey], rows[ey], ex, ey
                )[0]


def smooth_kernel(
    begun,
    begun_scaled,
    given,
    y_first,
    y_second,
    x_first,
    x_second,
    inv_diag,
    kap,
    grp,
    extra,
    facts,
    ctab,
    zmat,
    image,
    smoothed,
    msg,
    scaled,
    slope_z,
    edge,
):
    place = Place()
    weight = ctab[T_W]
    corner = float(SCALED[0, 0])

    def before(row, count=8):
        rows = pl.ds(row, count)
        return place.before_x(x_first[rows, :], x_second[rows, :])

    def after(row, count=8):
        rows = pl.ds(row, count)
        return place.after_x(x_first[rows, :], x_second[rows, :])

    image[...] = begun[...]
    scaled[...] = begun_scaled[...]
    for side, (ex, a) in enumerate(OUTER):
        for ey in range(2):
            tile = got_x_sum(place, begun[ex, a, ey], 0, ex, ey, x_first, x_second)
            image[ex, a, ey] = tile
            scaled[ex, a, ey] = tile * inv_diag[ex, a, ey] * float(1.0 / THETA)
            edge[side, ey] = scaled[ex, a, ey]
    edge[...] = along_z(edge[...].reshape(32, LANES), zmat[2]).reshape(edge.shape)
    there_x = (place.prev_x, place.next_x)
    zero = jnp.zeros(TILE, jnp.float32)
    tiles = [[[None, None] for _ in range(8)] for _ in range(2)]
    for ex in range(2):
        a_out = OUTER[ex][1]
        rows = inner_along_y(
            place, y_first, y_second, before, after, ex, a_out, SMOOTH_Y, SMOOTH_EDGE
        )
        for ey in range(2):
            values = [scaled[ex, a, ey] for a in range(8)]
            slopes = along_x(SCALED, values, 1)
            far_row = beyond_y(place, ey)
            beside = kap[pl.ds((ex + 1) * 4 + 3 * ey, 1), :]
            kappa = kap[pl.ds((ex + 1) * 4 + ey + 1, 1), :] + jnp.where(far_row, beside, 0.0)
            for a in range(8):
                if a != a_out:
                    acc = given[ex, a, ey]
                else:
                    value, flat = values[a], edge[ex, ey]
                    acc, slope_y, turned_y = cross_image(
                        place, ctab, kap, value, flat, rows[ey], ex, ey
                    )
                    x_next = 3 * ex
                    get = before if ex == 0 else after
                    turned_x = get(SMOOTH_X + ey * 8) + corner * value
                    side = kap[pl.ds(x_next * 4 + ey + 1, 1), :] * (turned_x + slope_y + flat)
                    far = kap[pl.ds(x_next * 4 + 3 * ey, 1), :] * (turned_x + turned_y + flat)
                    side = side + sigma_p * value
                    side = side + jnp.where(far_row, far + sigma_p * value, zero)
                    acc = acc + jnp.where(there_x[ex], side, zero)
                acc = acc + kappa * slopes[a]
                tiles[ex][a][ey] = place.join_z(acc * (float(WEIGHTS[a]) * weight))
    join_own(place, tiles)
    inv_mult = [1.0 / place.mult_tile(ey) for ey in range(2)]
    sums = [[jnp.zeros(TILE, jnp.float32) for _ in range(2)] for _ in range(2)]
    square = jnp.zeros(TILE, jnp.float32)
    for ex in range(2):
        for a in range(8):
            for ey in range(2):
                value = image[ex, a, ey]
                defect = (value - tiles[ex][a][ey]) * inv_diag[ex, a, ey]
                update = scaled[ex, a, ey]
                result = (
                    float(1.0 + RHO_NEXT * RHO) * update + float(2.0 * RHO_NEXT / DELTA) * defect
                )
                smoothed[ex, a, ey] = result
                weighed = value * (inv_mult[ey] * place.inv_x(ex, a))
                sums[ex][ey] = sums[ex][ey] + weighed
                square = square + weighed * result
    own_sums = restricted(place, sums, grp)
    if msg.shape[2] == LANES:
        sums = [extra[:, pl.ds(k, 1)] for k in range(2)]
        send_to_all(msg, message(place, own_sums, sums))
        return
    slope_z[...] = along_z(smoothed[...].reshape(256, LANES), zmat[2]).reshape(slope_z.shape)
    energy = jnp.zeros(TILE, jnp.float32)
    for ex in range(2):
        for ey in range(2):
            values, images = own_operator(ctab, kap, smoothed, slope_z, ex, ey)
            for a in range(8):
                energy = energy + values[a] * images[a]
                tiles[ex][a][ey] = place.join_z(images[a])
    join_own(place, tiles)
    sums = [extra[:, pl.ds(k, 1)] for k in range(2)] + [total(square), total(energy)]
    row = message(place, own_sums, sums, AWAY, BEYOND)
    row = row + restricted_around(place, tiles, inv_mult, grp)
    send_to_all(msg, jnp.concatenate([row, facts[:, LANES:]], axis=1))


def restricted_around(place, tiles, inv_mult, grp):
    lane = lax.broadcasted_iota(jnp.int32, (1, LANES), 1)
    weighed = [
        [[tiles[ex][a][ey] * (inv_mult[ey] * place.inv_x(ex, a)) for ey in range(2)] for a in range(8)]
        for ex in range(2)
    ]

    def rows_of(tile, y):
        if y == 0:
            return jnp.where(place.row == 0, tile[0], 0.0)
        if y == 3:
            return jnp.where(place.row == 7, tile[1], 0.0)
        return tile[y - 1]

    there_x = (place.prev_x, None, None, place.next_x)
    there_y = (place.prev_y, None, None, place.next_y)
    by_device = [
        [[jnp.zeros(TILE, jnp.float32) for _ in range(NCD)] for _ in range(3)] for _ in range(3)
    ]
    for x in range(4):
        for y in range(4):
            if x == 0:
                acc = rows_of(weighed[0][0], y)
            elif x == 3:
                acc = rows_of(weighed[1][7], y)
            else:
                acc = rows_of(weighed[x - 1][0], y)
                for a in range(1, 8):
                    acc = acc + rows_of(weighed[x - 1][a], y)
            for there in (there_x[x], there_y[y]):
                if there is not None:
                    acc = jnp.where(there, acc, 0.0)
            group = grp[pl.ds(x * 4 + y, 1), :]
            device = by_device[(x + 1) // 2][(y + 1) // 2]
            for c in range(NCD):
                device[c] = device[c] + jnp.where(group == float(c), acc, 0.0)
    row = jnp.zeros((1, LANES), jnp.float32)
    for dx in range(3):
        for dy in range(3):
            at = ((place.ix + dx - 1) * place.ny + place.iy + dy - 1) * NCD
            for c in range(NCD):
                row = row + jnp.where(lane == at + c, total(by_device[dx][dy][c]), 0.0)
    return row


def coarse_part(place, blocks, got, coarse, grp, at=0):
    lane = lax.broadcasted_iota(jnp.int32, (1, LANES), 1)
    values = [jnp.zeros((1, LANES), jnp.float32) for _ in range(blocks)]
    per = LANES // NCD
    for j in range(blocks):

        def gather(i, acc, j=j):
            return jnp.where(lane // NCD == i, got[j * per + i, pl.ds(at, 1), :], acc)

        values[j] = lax.fori_loop(0, per, gather, values[j], unroll=blocks == 1)

    def solved(dx, dy, c):
        acc = None
        for j in range(blocks):
            term = coarse[pl.ds(((dx * 3 + dy) * NCD + c) * blocks + j, 1), :] * values[j]
            acc = term if acc is None else acc + term
        return jnp.sum(acc, axis=1, keepdims=True)

    return prolonged(place, solved, grp)


def prolonged(place, solved, grp):
    device = [[[solved(dx, dy, c) for c in range(NCD)] for dy in range(3)] for dx in range(3)]
    inv_z = jnp.where(place.low_z | place.high_z, 0.5, 1.0)
    rows = []
    for x in range(4):
        line = []
        for y in range(4):
            group = grp[pl.ds(x * 4 + y, 1), :]
            acc = jnp.zeros((1, LANES), jnp.float32)
            for c in range(NCD):
                acc = acc + jnp.where(
                    group == float(c), device[(x + 1) // 2][(y + 1) // 2][c], 0.0
                )
            line.append(place.join_z(jnp.broadcast_to(acc, TILE)) * inv_z)
        rows.append(line)
    low_y = jnp.where(place.prev_y, 0.5, 1.0)
    high_y = jnp.where(place.next_y, 0.5, 1.0)

    def tile(ex, kind, ey):
        if kind == 1:
            vals = [rows[ex + 1][y] for y in range(4)]
        elif kind == 0:
            scale = place.inv_x(ex, 0)
            vals = [(rows[ex][y] + rows[ex + 1][y]) * scale for y in range(4)]
        else:
            scale = place.inv_x(ex, 7)
            vals = [(rows[ex + 1][y] + rows[ex + 2][y]) * scale for y in range(4)]
        mid = vals[ey + 1]
        low = (vals[ey] + mid) * (low_y if ey == 0 else 0.5)
        high = (mid + vals[ey + 2]) * (high_y if ey == 1 else 0.5)
        return jnp.where(place.row == 0, low, jnp.where(place.row == 7, high, mid))

    return tile


def kind_of(a):
    return 0 if a == 0 else (2 if a == 7 else 1)


def own_operator(ctab, kap, field, slope_z, ex, ey):
    weight = ctab[T_W]
    tiles = [field[ex, a, ey] for a in range(8)]
    slopes = along_x(SCALED, tiles, 1)
    kappa = kap[pl.ds((ex + 1) * 4 + ey + 1, 1), :]
    out = []
    for a in range(8):
        stiff = slopes[a] + along_y(ctab, T_K, tiles[a]) + slope_z[ex, a, ey]
        out.append((kappa * stiff + sigma_p * tiles[a]) * (float(WEIGHTS[a]) * weight))
    return tiles, out


def first_direction_kernel(
    blocks,
    got,
    coarse,
    grp,
    kap,
    inv_diag,
    resid,
    own,
    ctab,
    zmat,
    direction,
    out,
    inner_x,
    first,
    second,
    extra,
    slope_z,
    image,
):
    place = Place()
    inv_mult = [1.0 / place.mult_tile(ey) for ey in range(2)]
    part = coarse_part(place, blocks, got, coarse, grp, 8)
    image[...] = own[...]
    for dx, dy, there in neighbours(place):

        @pl.when(there)
        def _():
            frm = (place.ix + dx) * place.ny + place.iy + dy
            ex, a = (0, 0) if dx < 0 else (1, 7)
            ey, b = (0, 0) if dy < 0 else (1, 7)
            edge = place.row == b
            if dy == 0:
                low = got[frm, pl.ds(0, 8), :]
                high = jnp.where(
                    place.row == 0, pltpu.roll(low, 1, 0), got[frm, pl.ds(8, 8), :]
                )
                image[ex, a, 0] = image[ex, a, 0] + low
                image[ex, a, 1] = image[ex, a, 1] + high
            elif dx == 0:
                for r in range(16):
                    line = got[frm, pl.ds(7 if r == 8 else r, 1), :]
                    tile = image[r // 8, r % 8, ey]
                    image[r // 8, r % 8, ey] = tile + jnp.where(edge, line, 0.0)
            else:
                line = got[frm, pl.ds(0, 1), :]
                image[ex, a, ey] = image[ex, a, ey] + jnp.where(edge, line, 0.0)

    energy = jnp.zeros(TILE, jnp.float32)
    for ex in range(2):
        for ey in range(2):
            kinds = [part(ex, kind, ey) for kind in range(3)]
            for a in range(8):
                known = resid[ex, a, ey]
                inverse = inv_diag[ex, a, ey]
                defect = (known - image[ex, a, ey]) * inverse
                value = (
                    float((1.0 + RHO_NEXT * RHO) / THETA) * (known * inverse)
                    + float(2.0 * RHO_NEXT / DELTA) * defect
                    + kinds[kind_of(a)]
                )
                direction[ex, a, ey] = value
                scale = place.inv_x(ex, a)
                energy = energy + value * known * (inv_mult[ey] * scale)
    slope_z[...] = along_z(direction[...].reshape(256, LANES), zmat[2]).reshape(slope_z.shape)
    curvature = jnp.zeros(TILE, jnp.float32)
    tiles = [[[None, None] for _ in range(8)] for _ in range(2)]
    for ex in range(2):
        for ey in range(2):
            values, images = own_operator(ctab, kap, direction, slope_z, ex, ey)
            for a in range(8):
                curvature = curvature + values[a] * images[a]
                tiles[ex][a][ey] = place.join_z(images[a])
    join_own(place, tiles)
    for ex in range(2):
        for a in range(8):
            for ey in range(2):
                out[ex, a, ey] = tiles[ex][a][ey]
    store_y_faces(place, out, first, second, (), 0)

    def tile_of(ex, a, ey):
        return tiles[ex][a][ey] * inv_diag[ex, a, ey] * float(1.0 / THETA)

    def column_of(ex, ey):
        return [tile_of(ex, a, ey) for a in range(8)]

    store_inner(
        place, SCALED, ctab[T_KBOTTOM], ctab[T_KTOP], column_of, tile_of, inner_x, first, second,
        SMOOTH_Y, SMOOTH_EDGE,
    )
    lane = lax.broadcasted_iota(jnp.int32, (1, LANES), 1)
    extra[...] = jnp.where(lane == 0, total(energy), total(curvature))


def gathered_scalars(got, count):
    lane = lax.broadcasted_iota(jnp.int32, (1, LANES), 1)
    per = LANES // NCD
    sums = []
    for c in range(count):
        acc = jnp.zeros((1, LANES), jnp.float32)

        def gather(i, acc, c=c):
            return acc + jnp.where(lane == ((i + 1) % per) * NCD + c, got[i], 0.0)

        acc = lax.fori_loop(0, got.shape[0], gather, acc, unroll=got.shape[0] <= per)
        sums.append(jnp.sum(acc, axis=1, keepdims=True))
    return sums


def second_direction_kernel(
    blocks,
    got,
    coarse,
    grp,
    kap,
    resid,
    direction,
    image,
    smoothed,
    ctab,
    zmat,
    following,
    known,
    msg,
    slope_z,
):
    place = Place()
    inv_mult = [1.0 / place.mult_tile(ey) for ey in range(2)]
    part = coarse_part(place, blocks, got, coarse, grp)
    energy, curvature = gathered_scalars(got, 2)
    step = energy / curvature
    lane = lax.broadcasted_iota(jnp.int32, (1, LANES), 1)
    known[...] = jnp.where(lane == 0, energy, jnp.where(lane == 1, curvature, 0.0))
    energy_next = jnp.zeros(TILE, jnp.float32)
    cross = jnp.zeros(TILE, jnp.float32)
    for ex in range(2):
        for ey in range(2):
            kinds = [part(ex, kind, ey) for kind in range(3)]
            for a in range(8):
                value = direction[ex, a, ey] - step * (smoothed[ex, a, ey] + kinds[kind_of(a)])
                following[ex, a, ey] = value
                weighed = value * (inv_mult[ey] * place.inv_x(ex, a))
                was = image[ex, a, ey]
                energy_next = energy_next + weighed * (resid[ex, a, ey] - step * was)
                cross = cross + weighed * was
    slope_z[...] = along_z(following[...].reshape(256, LANES), zmat[2]).reshape(slope_z.shape)
    square = jnp.zeros(TILE, jnp.float32)
    for ex in range(2):
        for ey in range(2):
            values, images = own_operator(ctab, kap, following, slope_z, ex, ey)
            for a in range(8):
                square = square + values[a] * images[a]
    send_to_all(msg, message(place, [], [total(energy_next), total(square), total(cross)]))


def pressure_kernel(got, known, direction, following, pressure):
    energy = known[:, pl.ds(0, 1)]
    curvature = known[:, pl.ds(1, 1)]
    energy_next, square, cross = gathered_scalars(got, 3)
    ratio = energy_next / energy
    step = energy / curvature
    step_next = energy_next / (square + 2.0 * ratio * cross + ratio * ratio * curvature)
    weight_old = step + step_next * ratio
    for ex in range(2):
        for a in range(8):
            for ey in range(2):
                pressure[ex, a, ey] = (
                    weight_old * direction[ex, a, ey] + step_next * following[ex, a, ey]
                )


def coarse_energy(place, got, values, kappa, number):
    lane, row = place.lane, place.row
    for ex in range(2):
        for gx in range(8):
            own = jnp.zeros((1, LANES), jnp.float32)
            group = jnp.zeros((1, LANES), jnp.float32)
            spot = lane[0:1] // 32
            for gy in range(4):
                line = got[gx * 4 + gy, :, pl.ds(LANES, LANES)]
                own = jnp.where(spot == (gy + 2 * ex) % 4, line, own)
                group = jnp.where(spot == (gy + 1 + 2 * ex) % 4, line, group)
            kappa[ex, pl.ds(gx, 1), :] = own
            number[ex, pl.ds(gx, 1), :] = group
    grid = [jnp.zeros(TILE, jnp.float32) for _ in range(2)]
    numbers = [pltpu.roll(number[0], 96, 1), pltpu.roll(number[1], 32, 1)]
    kappa = [kappa[0], pltpu.roll(kappa[1], 64, 1)]
    for q in range(4):
        for c in range(NCD):
            mine = jnp.where(lane == row * 16 + q * 4 + c, values, 0.0)
            mine = jnp.sum(mine, axis=1, keepdims=True)
            for ex in range(2):
                chosen = (lane // 32 == q) & (numbers[ex] == float(c))
                grid[ex] = jnp.where(chosen, mine, grid[ex])

    def ends_y(v):
        low = jnp.where(lane >= 16, 0.5 * (v + pltpu.roll(v, 16, 1)), v)
        return low, v, jnp.where(lane < 112, 0.5 * (v + pltpu.roll(v, 112, 1)), v)

    def ends_z(v):
        low = jnp.where(lane % 16 > 0, 0.5 * (v + pltpu.roll(v, 1, 1)), v)
        return low, v, jnp.where(lane % 16 < 15, 0.5 * (v + pltpu.roll(v, 127, 1)), v)

    low = jnp.where(row > 0, 0.5 * (grid[0] + pltpu.roll(grid[1], 1, 0)), grid[0])
    mid = 0.5 * (grid[0] + grid[1])
    high = jnp.where(row < 7, 0.5 * (grid[1] + pltpu.roll(grid[0], 7, 0)), grid[1])
    mass = [float(WEIGHTS[0]), float(np.sum(WEIGHTS[1:7])), float(WEIGHTS[7])]
    links = (
        (0, 1, -float(np.sum(STIFF[0, 1:7]))),
        (0, 2, -float(STIFF[0, 7])),
        (1, 2, -float(np.sum(STIFF[7, 1:7]))),
    )
    energy = jnp.zeros(TILE, jnp.float32)
    for ex, line in enumerate(((low, grid[0], mid), (mid, grid[1], high))):
        nodes = [[ends_z(v) for v in ends_y(w)] for w in line]
        stiff = jnp.zeros(TILE, jnp.float32)
        square = jnp.zeros(TILE, jnp.float32)
        for i in range(3):
            for j in range(3):
                for k, l, weight in links:
                    factor = weight * mass[i] * mass[j]
                    for first, second in (
                        (nodes[k][i][j], nodes[l][i][j]),
                        (nodes[i][k][j], nodes[i][l][j]),
                        (nodes[i][j][k], nodes[i][j][l]),
                    ):
                        gap = first - second
                        stiff = stiff + (factor * gap) * gap
                for k in range(3):
                    value = nodes[i][j][k]
                    square = square + (mass[i] * mass[j] * mass[k] * value) * value
        energy = energy + kappa[ex] * stiff + sigma_p * square
    return total(energy)


def finish_kernel(
    got, grp, direction, smoothed, pressure, matrix, kappa, number
):
    place = Place()
    per = LANES // NCD
    row_lane = lax.broadcasted_iota(jnp.int32, (1, LANES), 1)
    rest = jnp.zeros((1, LANES), jnp.float32)
    dual = jnp.zeros((1, LANES), jnp.float32)
    sums = [jnp.zeros((1, LANES), jnp.float32) for _ in range(4)]
    for i in range(per):
        line = got[i, :, pl.ds(0, LANES)]
        mine = row_lane // NCD == (i + AWAY) % per
        known = row_lane // NCD == (i + BEYOND) % per
        rest = jnp.where(mine, line, rest)
        dual = dual + jnp.where(mine | known, 0.0, line)
        for c in range(4):
            sums[c] = sums[c] + jnp.where(row_lane == ((i + BEYOND) % per) * NCD + c, line, 0.0)
            block = got[i, :, pl.ds((2 + c) * LANES, LANES)]
            matrix[pl.ds(i * NCD + c, 1), :] = block
    rest = pltpu.roll(rest, (per - AWAY) * NCD, 1)
    energy, curvature, square, self_energy = [
        jnp.sum(value, axis=1, keepdims=True) for value in sums
    ]
    values = lax.dot_general(
        jnp.broadcast_to(rest, TILE),
        matrix[...],
        (((1,), (1,)), ((), ())),
        precision=lax.Precision.HIGHEST,
        preferred_element_type=jnp.float32,
    )
    line = values[0:1]
    cross = square + jnp.sum(line * rest, axis=1, keepdims=True)
    both = self_energy + 2.0 * jnp.sum(line * dual, axis=1, keepdims=True)
    both = both + coarse_energy(place, got, values, kappa, number)
    step = energy / curvature
    energy_next = step * step * cross - energy
    ratio = energy_next / energy
    with_image = curvature - step * cross
    with_itself = curvature - 2.0 * step * cross + step * step * both
    step_next = energy_next / (
        with_itself + 2.0 * ratio * with_image + ratio * ratio * curvature
    )
    old = step + step_next * (1.0 + ratio)
    new = -step_next * step

    def solved(dx, dy, c):
        at = ((place.ix + dx - 1) * place.ny + place.iy + dy - 1) * NCD + c
        return jnp.sum(jnp.where(row_lane == at, line, 0.0), axis=1, keepdims=True)

    part = prolonged(place, masked(place, solved), grp)
    for ex in range(2):
        for ey in range(2):
            kinds = [part(ex, kind, ey) for kind in range(3)]
            for a in range(8):
                pressure[ex, a, ey] = old * direction[ex, a, ey] + new * (
                    smoothed[ex, a, ey] + kinds[kind_of(a)]
                )


def masked(place, solved):
    there_x = (place.prev_x, None, place.next_x)
    there_y = (place.prev_y, None, place.next_y)

    def value(dx, dy, c):
        out = solved(dx, dy, c)
        for there in (there_x[dx], there_y[dy]):
            if there is not None:
                out = jnp.where(there, out, 0.0)
        return out

    return value


def call(body, outs, scratch=(), **more):
    return pl.pallas_call(
        body,
        out_shape=[jax.ShapeDtypeStruct(shape, jnp.float32) for shape in outs],
        scratch_shapes=[
            pltpu.VMEM(shape, jnp.float32) if isinstance(shape, tuple) else shape
            for shape in scratch
        ],
        **more,
        compiler_params=pltpu.CompilerParams(vmem_limit_bytes=24 * 1024 * 1024),
    )


def swap(first, second, axis):
    count = lax.axis_size(axis)
    first_pairs = [(i, i ^ 1) for i in range(count) if i ^ 1 < count]
    second_pairs = [(i, ((i + 1) ^ 1) - 1) for i in range(1, count) if ((i + 1) ^ 1) - 1 < count]
    if axis in ('gx',):
        first_pairs, second_pairs = second_pairs, first_pairs
    first_got = lax.ppermute(first, axis, first_pairs)
    return first_got, lax.ppermute(second, axis, second_pairs)


def per_device(fields, viscosity, inv_density, elem_group, coarse_inverse):
    length = fields.shape[5]
    elems_z = length // NODES
    devices = lax.axis_size("gx") * lax.axis_size("gy")
    blocks = coarse_inverse.shape[1] // LANES
    pack_rows = 1 + NCD * blocks
    tiles_np, mats_np = constant_tables(elems_z)
    ctab, zmat = jnp.asarray(tiles_np), jnp.asarray(mats_np)
    one = fields.shape[1:]
    four = fields.shape
    faces = (64, LANES)
    xf_shape = (2, 4, 2, 8, LANES)
    inner_shape = (2, 2, 8, LANES)
    y_shape, x_shape = (STEP_PACK + 3 * pack_rows, LANES), (STEP_PACK, LANES)
    turned = (64 + pack_rows, LANES)
    smooth_shape = (SMOOTH_ROWS, LANES)
    rows = (devices, 1, LANES)
    grid_fits = (
        blocks == 1
        and lax.axis_size("gx") == 8
        and lax.axis_size("gy") * fields.shape[3] * elems_z == LANES
    )

    def exchange_all(msg):
        return lax.all_to_all(msg, BOTH, 0, 0, tiled=True)

    beside = pl.CostEstimate(flops=10**7, bytes_accessed=10**6, transcendentals=0)
    summed, xf, first, second = call(
        mass_kernel,
        [four, xf_shape, faces, faces],
    )(fields)
    pack, facts = call(
        pack_kernel,
        [(pack_rows, LANES), (1, 6 * LANES)],
        cost_estimate=beside,
    )(inv_density, elem_group, coarse_inverse)
    y_got = swap(first, second, "gy")
    first, second = call(functools.partial(turn_faces_kernel, pack_rows), [turned, turned])(
        xf, pack, *y_got
    )
    side_got = x_got = swap(first, second, "gx")
    edge_shape = (4, 2, 2, 8, LANES)
    begun, given, slope, answer = call(
        prepare_kernel, [four, four, edge_shape, one], [four, four], cost_estimate=beside
    )(summed, viscosity, *y_got, ctab, zmat)
    share, xf, inner_x, first, second = call(
        functools.partial(rhs_kernel, pack_rows),
        [four, xf_shape, inner_shape, y_shape, y_shape],
        [edge_shape, edge_shape, edge_shape, edge_shape],
    )(begun, given, slope, answer, viscosity, pack, *x_got, ctab, zmat)
    y_got = swap(first, second, "gy")
    first, second = call(turn_step_kernel, [x_shape, x_shape])(xf, inner_x, *y_got)
    x_got = swap(first, second, "gx")
    inv_diag, kap, grp, coarse = call(
        functools.partial(setup_kernel, pack_rows, blocks),
        [one, (16, LANES), (16, LANES), (9 * NCD * blocks, LANES)],
        [(16, LANES), (8, 16, LANES)],
        cost_estimate=beside,
    )(pack, *side_got, *y_got, ctab)
    begun, given = call(approach_kernel, [four, one], [one], cost_estimate=beside)(
        share, *y_got, ctab, zmat
    )
    side_shape = (2, 2, 8, LANES)
    fields_got = x_got
    fields_begun = begun
    resid, own, msg = call(
        advance_kernel,
        [one, one, (devices, 16, LANES)],
        [one, one, side_shape, one, (3,) + side_shape],
    )(begun, given, *y_got, *x_got, inv_diag, kap, grp, ctab, zmat)
    got = exchange_all(msg)
    direction, own, inner_x, first, second, extra = call(
        functools.partial(first_direction_kernel, blocks),
        [one, one, inner_shape, smooth_shape, smooth_shape, (1, LANES)],
        [one, one],
    )(got, coarse, grp, kap, inv_diag, resid, own, ctab, zmat)
    y_got = swap(first, second, "gy")
    first, second = call(turn_smooth_kernel, [smooth_shape, smooth_shape])(own, inner_x, *y_got)
    x_got = swap(first, second, "gx")
    fields_new, extra = call(emit_kernel, [four, (1, LANES)], cost_estimate=beside)(
        fields_begun, *fields_got, extra
    )
    begun, begun_scaled, given = call(
        ready_kernel, [one, one, one], [one], cost_estimate=beside
    )(own, *y_got, inv_diag, kap, ctab, zmat)
    image, image_smoothed, msg = call(
        smooth_kernel,
        [one, one, (devices, 1, 6 * LANES) if grid_fits else rows],
        [one, one, side_shape],
    )(
        begun, begun_scaled, given, *y_got, *x_got, inv_diag, kap, grp, extra, facts, ctab, zmat
    )
    got = exchange_all(msg)
    if grid_fits:
        (pressure,) = call(
            finish_kernel, [one], [(LANES, LANES), (2,) + TILE, (2,) + TILE]
        )(got, grp, direction, image_smoothed)
        return (fields_new, pressure)
    following, known, msg = call(
        functools.partial(second_direction_kernel, blocks), [one, (1, LANES), rows], [one]
    )(got, coarse, grp, kap, resid, direction, image, image_smoothed, ctab, zmat)
    got = exchange_all(msg)
    (pressure,) = call(pressure_kernel, [one])(got, known, direction, following)
    return (fields_new, pressure)


def solution(mesh):
    placed = (
        P(None, "gx", None, "gy", None, None),
        P("gx", None, "gy", None, None),
        P("gx", "gy", None),
        P("gx", "gy", None),
        P(("gx", "gy"), None),
    )
    return jax.shard_map(
        per_device,
        mesh=mesh,
        in_specs=placed,
        out_specs=(P(None, "gx", None, "gy", None, None), P("gx", None, "gy", None, None)),
        check_vma=False,
    )
```

```python
import functools

import jax
import jax.numpy as jnp
import ml_dtypes
import numpy as np
from jax import lax
from jax.experimental import pallas as pl
from jax.experimental.pallas import tpu as pltpu
from jax.sharding import PartitionSpec as P

NCD = 4
NODES = 8
LANES = 128
TILE = (8, 128)
BOTH = ("gx", "gy")

dt_step = 0.01
sigma_p = 4.0
prandtl = 0.7
cheb_ratio = 0.1


def tables():
    points = np.array(
        [
            -1.0,
            -0.8717401485096066,
            -0.5917001814331423,
            -0.2092992179024789,
            0.2092992179024789,
            0.5917001814331423,
            0.8717401485096066,
            1.0,
        ]
    )
    weights = np.array(
        [
            1.0 / 28.0,
            0.2107042271435061,
            0.3411226924835044,
            0.4124587946587038,
            0.4124587946587038,
            0.3411226924835044,
            0.2107042271435061,
            1.0 / 28.0,
        ]
    )
    identity = np.eye(8)
    differ = points[:, None] - points[None, :] + identity
    barycentric = 1.0 / np.prod(differ, axis=1)
    offdiag = barycentric[None, :] / barycentric[:, None] / differ * (1.0 - identity)
    derivative = offdiag - identity * np.sum(offdiag, axis=1)[:, None]
    mass_one = identity * weights[None, :]
    stiff_one = derivative.T @ mass_one @ derivative
    stiff_three = (
        np.kron(np.kron(stiff_one, mass_one), mass_one)
        + np.kron(np.kron(mass_one, stiff_one), mass_one)
        + np.kron(np.kron(mass_one, mass_one), stiff_one)
    )
    three_diag = np.sum(stiff_three * np.eye(512), axis=1)
    spectral_bound = float(np.max(np.sum(np.abs(stiff_three), axis=1) / three_diag))
    return (derivative, weights, stiff_one, spectral_bound)


DERIV, WEIGHTS, STIFF, BOUND = tables()
SCALED = STIFF / WEIGHTS[:, None]
LINE = np.diag(STIFF) / WEIGHTS
THETA = 0.5 * (BOUND + cheb_ratio * BOUND)
DELTA = 0.5 * (BOUND - cheb_ratio * BOUND)
RHO = DELTA / THETA
RHO_NEXT = 1.0 / (2.0 * THETA / DELTA - RHO)


def constant_tables(elems_z):
    def turned(matrix):
        rows = np.arange(8)
        return [np.repeat(matrix[rows, (rows - s) % 8][:, None], LANES, 1) for s in range(8)]

    wz = np.tile(WEIGHTS, elems_z)
    kz = np.tile(LINE, elems_z)
    tiles = turned(DERIV) + turned(DERIV.T) + turned(SCALED)
    tiles += [WEIGHTS[:, None] * wz[None, :], LINE[:, None] + kz[None, :]]
    for matrix in (DERIV, SCALED):
        for node in (7, 0):
            inner = matrix[node] * (np.arange(8) != node)
            tiles.append(np.repeat(inner[:, None], LANES, 1))
    eye = np.eye(elems_z)
    mats = [np.kron(eye, DERIV.T), np.kron(eye, DERIV), np.kron(eye, SCALED.T)]
    halves = []
    for mat in mats:
        high = mat.astype(ml_dtypes.bfloat16)
        low = (mat - high.astype(np.float64)).astype(ml_dtypes.bfloat16)
        both = np.concatenate([high, low], 1)
        halves.append(np.concatenate([both, both], 0))
    return np.stack(tiles).astype(np.float32), np.stack(halves)


T_D, T_DT, T_K, T_W, T_LINE = 0, 8, 16, 24, 25
T_TOP, T_BOTTOM, T_KTOP, T_KBOTTOM = 26, 27, 28, 29


class Place:
    def __init__(self):
        self.ix = lax.axis_index("gx")
        self.iy = lax.axis_index("gy")
        self.nx = lax.axis_size("gx")
        self.ny = lax.axis_size("gy")
        self.even_x = self.ix % 2 == 0
        self.even_y = self.iy % 2 == 0
        self.row = lax.broadcasted_iota(jnp.int32, TILE, 0)
        self.lane = lax.broadcasted_iota(jnp.int32, TILE, 1)
        self.low_z = (self.lane % 8 == 0) & (self.lane > 0)
        self.high_z = (self.lane % 8 == 7) & (self.lane < LANES - 1)
        self.prev_x = self.ix > 0
        self.next_x = self.ix < self.nx - 1
        self.prev_y = self.iy > 0
        self.next_y = self.iy < self.ny - 1

    def mult_tile(self, ey):
        along_z = 1.0 + jnp.where(self.low_z | self.high_z, 1.0, 0.0)
        low = 1.0 if ey == 1 else jnp.where(self.prev_y, 1.0, 0.0)
        high = 1.0 if ey == 0 else jnp.where(self.next_y, 1.0, 0.0)
        along_y = 1.0 + jnp.where(self.row == 0, low, jnp.where(self.row == 7, high, 0.0))
        return along_y * along_z

    def inv_x(self, ex, a):
        if a == 0:
            return 0.5 if ex == 1 else jnp.where(self.prev_x, 0.5, 1.0)
        if a == 7:
            return 0.5 if ex == 0 else jnp.where(self.next_x, 0.5, 1.0)
        return 1.0

    def mult_x(self, ex, a):
        if a == 0:
            return 2.0 if ex == 1 else jnp.where(self.prev_x, 2.0, 1.0)
        if a == 7:
            return 2.0 if ex == 0 else jnp.where(self.next_x, 2.0, 1.0)
        return 1.0

    def share_x(self, ex, a):
        if (ex, a) == (0, 0):
            return jnp.where(self.prev_x, 0.5, 1.0)
        if (ex, a) == (1, 7):
            return jnp.where(self.next_x, 0.5, 1.0)
        return 1.0

    def share_y(self, ey):
        if ey == 0:
            return jnp.where((self.row == 0) & self.prev_y, 0.5, 1.0)
        return jnp.where((self.row == 7) & self.next_y, 0.5, 1.0)

    def inv_y(self, ey):
        low = 0.5 if ey == 1 else jnp.where(self.prev_y, 0.5, 1.0)
        high = 0.5 if ey == 0 else jnp.where(self.next_y, 0.5, 1.0)
        return jnp.where(self.row == 0, low, jnp.where(self.row == 7, high, 1.0))

    def inv_z(self):
        return jnp.where(self.low_z | self.high_z, 0.5, 1.0)

    def join_z(self, t):
        up = pltpu.roll(t, LANES - 1, 1)
        down = pltpu.roll(t, 1, 1)
        return t + jnp.where(self.high_z, up, jnp.where(self.low_z, down, 0.0))

    def to_low(self, below):
        return jnp.where(self.row == 0, pltpu.roll(below, 1, 0), 0.0)

    def to_high(self, above):
        return jnp.where(self.row == 7, pltpu.roll(above, 7, 0), 0.0)

    def join_y(self, below, above):
        return below + self.to_high(above), above + self.to_low(below)

    def before_x(self, first, second):
        return jnp.where(self.even_x, first, second)

    def after_x(self, first, second):
        return jnp.where(self.even_x, second, first)

    def before_y(self, first, second):
        return jnp.where(self.even_y, second, first)

    def after_y(self, first, second):
        return jnp.where(self.even_y, first, second)


def along_x(matrix, tiles, sign):
    even = [tiles[a] + tiles[7 - a] for a in range(4)]
    odd = [tiles[a] - tiles[7 - a] for a in range(4)]
    out = [None] * 8
    for i in range(4):
        plus, minus = None, None
        for a in range(4):
            p = float(0.5 * (matrix[i, a] + matrix[i, 7 - a])) * even[a]
            m = float(0.5 * (matrix[i, a] - matrix[i, 7 - a])) * odd[a]
            plus = p if plus is None else plus + p
            minus = m if minus is None else minus + m
        out[i] = plus + minus
        out[7 - i] = minus - plus if sign < 0 else plus - minus
    return out


def along_y(ctab, base, tile):
    acc = ctab[base] * tile
    for s in range(1, 8):
        acc = acc + ctab[base + s] * pltpu.roll(tile, s, 0)
    return acc


def exact_dot(rows, matrix):
    return jnp.dot(
        rows, matrix, precision=lax.Precision.HIGHEST, preferred_element_type=jnp.float32
    )


def along_z(rows, matrix):
    high = rows.astype(jnp.bfloat16)
    low = (rows - high.astype(jnp.float32)).astype(jnp.bfloat16)
    both = jnp.dot(
        jnp.concatenate([high, low], axis=1), matrix, preferred_element_type=jnp.float32
    )
    return both[:, :LANES] + both[:, LANES:]


def total(tile):
    return jnp.sum(jnp.sum(tile, axis=0, keepdims=True), axis=1, keepdims=True)


def store_y_faces(place, field, first_out, second_out, lead, at):
    for ex in range(2):
        for a in range(8):
            low = field[lead + (ex, a, 0, pl.ds(0, 1), slice(None))]
            high = field[lead + (ex, a, 1, pl.ds(7, 1), slice(None))]
            row = at + ex * 8 + a
            first_out[pl.ds(row, 1), :] = place.after_y(high, low)
            second_out[pl.ds(row, 1), :] = place.after_y(low, high)


def join_own(place, tiles):
    for ex in range(2):
        for a in range(8):
            tiles[ex][a] = list(place.join_y(*tiles[ex][a]))
    for ey in range(2):
        both = tiles[0][7][ey] + tiles[1][0][ey]
        tiles[0][7][ey] = both
        tiles[1][0][ey] = both


def weight_of(node):
    edge = jnp.minimum(node, 7 - node)
    value = jnp.where(edge == 2, float(WEIGHTS[2]), float(WEIGHTS[3]))
    return jnp.where(
        edge == 0, float(WEIGHTS[0]), jnp.where(edge == 1, float(WEIGHTS[1]), value)
    )


def mass_kernel(fields, out, xf, first, second):
    place = Place()
    weight = weight_of(place.row) * weight_of(place.lane % NODES)
    for ch in range(4):
        tiles = [
            [
                [
                    place.join_z(fields[ch, ex, a, ey] * (float(WEIGHTS[a]) * weight))
                    for ey in range(2)
                ]
                for a in range(8)
            ]
            for ex in range(2)
        ]
        join_own(place, tiles)
        for ex in range(2):
            for a in range(8):
                for ey in range(2):
                    out[ch, ex, a, ey] = tiles[ex][a][ey]
        for ey in range(2):
            xf[0, ch, ey] = tiles[0][0][ey]
            xf[1, ch, ey] = tiles[1][7][ey]
        store_y_faces(place, out, first, second, (ch,), ch * 16)


def turn_faces(place, xf, y_first, y_second, first, second):
    for ch in range(4):
        sides = []
        for side in range(2):
            row = pl.ds(ch * 16 + 15 * side, 1)
            got_a, got_b = y_first[row, :], y_second[row, :]
            low = xf[side, ch, 0] + jnp.where(place.row == 0, place.before_y(got_a, got_b), 0.0)
            high = xf[side, ch, 1] + jnp.where(place.row == 7, place.after_y(got_a, got_b), 0.0)
            sides.append((low, high))
        for ey in range(2):
            rows = pl.ds(ch * 16 + ey * 8, 8)
            first[rows, :] = place.after_x(sides[1][ey], sides[0][ey])
            second[rows, :] = place.after_x(sides[0][ey], sides[1][ey])


def turn_faces_kernel(pack_rows, xf, pack, y_first, y_second, first, second):
    turn_faces(Place(), xf, y_first, y_second, first, second)
    first[pl.ds(64, pack_rows), :] = pack[...]
    second[pl.ds(64, pack_rows), :] = pack[...]


def turn_edges(place, inner_x, y_first, y_second, first, second, at, edge, inner_y):
    sides = []
    for side in range(2):
        row = pl.ds(edge + side, 1)
        got_a, got_b = y_first[row, :], y_second[row, :]
        low = inner_x[side, 0] + jnp.where(place.row == 0, place.before_y(got_a, got_b), 0.0)
        high = inner_x[side, 1] + jnp.where(place.row == 7, place.after_y(got_a, got_b), 0.0)
        sides.append((low, high))
    for ey in range(2):
        rows = pl.ds(at + ey * 8, 8)
        first[rows, :] = place.after_x(sides[1][ey], sides[0][ey])
        second[rows, :] = place.after_x(sides[0][ey], sides[1][ey])
    for k, pick in enumerate((place.before_y, place.after_y)):
        sides = []
        for side in range(2):
            row = pl.ds(inner_y + 15 * side, 1)
            sides.append(pick(y_first[row, :], y_second[row, :]))
        row = pl.ds(edge + k, 1)
        first[row, :] = place.after_x(sides[1], sides[0])
        second[row, :] = place.after_x(sides[0], sides[1])


STEP_U, STEP_V, STEP_EDGE, STEP_PACK = 64, 64, 80, 82


def turn_step_kernel(xf, inner_x, y_first, y_second, first, second):
    place = Place()
    turn_faces(place, xf, y_first, y_second, first, second)
    turn_edges(place, inner_x, y_first, y_second, first, second, STEP_U, STEP_EDGE, STEP_V)


def setup_kernel(
    pack_rows,
    blocks,
    pack,
    x_first,
    x_second,
    y_first,
    y_second,
    ctab,
    inv_diag,
    kap,
    grp,
    coarse,
    compact,
    spread,
):
    place = Place()
    beside = pl.ds(64, pack_rows)
    packs = [[None] * 3 for _ in range(3)]
    packs[0][1] = place.before_x(x_first[beside, :], x_second[beside, :])
    packs[1][1] = pack[...]
    packs[2][1] = place.after_x(x_first[beside, :], x_second[beside, :])
    for dx in range(3):
        rows = pl.ds(STEP_PACK + dx * pack_rows, pack_rows)
        packs[dx][0] = place.before_y(y_first[rows, :], y_second[rows, :])
        packs[dx][2] = place.after_y(y_first[rows, :], y_second[rows, :])
    compact[...] = jnp.zeros(compact.shape, jnp.float32)
    for dx in range(3):
        for dy in range(3):
            at = (dx * 3 + dy) * NCD * blocks
            coarse[pl.ds(at, NCD * blocks), :] = packs[dx][dy][1 : 1 + NCD * blocks]
            compact[pl.ds(dx * 3 + dy, 1), :] = packs[dx][dy][0:1]
    elems = LANES // NODES
    lane = lax.broadcasted_iota(jnp.int32, (LANES, LANES), 1)
    source = lax.broadcasted_iota(jnp.int32, (LANES, LANES), 0)
    for k in range(8):
        spot = (source == k * elems + lane // NODES).astype(jnp.float32)
        spread[k] = exact_dot(compact[...], spot)
    there_x = [jnp.where(place.prev_x, 1.0, 0.0), 1.0, jnp.where(place.next_x, 1.0, 0.0)]
    there_y = [jnp.where(place.prev_y, 1.0, 0.0), 1.0, jnp.where(place.next_y, 1.0, 0.0)]

    def element_row(base, u, v):
        device = (u // 2) * 3 + v // 2
        return spread[base + (u % 2) * 2 + v % 2, pl.ds(device, 1), :]

    for x in range(4):
        for y in range(4):
            kap[pl.ds(x * 4 + y, 1), :] = element_row(0, x + 1, y + 1)
            grp[pl.ds(x * 4 + y, 1), :] = element_row(4, x + 1, y + 1)
    kappa = [
        [
            place.join_z(jnp.broadcast_to(element_row(0, u + 1, v + 1), TILE))
            for v in range(4)
        ]
        for u in range(4)
    ]
    count_z = 1.0 + jnp.where(place.low_z | place.high_z, 1.0, 0.0)
    weight = ctab[T_W]
    line = ctab[T_LINE]

    def pick(values, ey):
        low = values[ey] + values[ey + 1]
        high = values[ey + 1] + values[ey + 2]
        return jnp.where(place.row == 0, low, jnp.where(place.row == 7, high, values[ey + 1]))

    for ex in range(2):
        for kind in range(3):
            us = {0: (ex, ex + 1), 1: (ex + 1,), 2: (ex + 1, ex + 2)}[kind]
            sums, counts = [], []
            for v in range(4):
                acc, num = None, 0.0
                for u in us:
                    acc = kappa[u][v] if acc is None else acc + kappa[u][v]
                    num = num + there_x[(u + 1) // 2]
                sums.append(acc)
                counts.append(num * there_y[(v + 1) // 2])
            for ey in range(2):
                kappa_sum = pick(sums, ey)
                mult = pick(counts, ey) * count_z
                for a in {0: (0,), 1: range(1, 7), 2: (7,)}[kind]:
                    diag = (float(LINE[a]) + line) * kappa_sum + sigma_p * mult
                    inv_diag[ex, a, ey] = 1.0 / (diag * (float(WEIGHTS[a]) * weight))


OUTER = ((0, 0), (1, 7))


def got_y_sum(place, tile, ch, ex, a, ey, y_first, y_second):
    row = pl.ds(ch * 16 + ex * 8 + a, 1)
    got_a, got_b = y_first[row, :], y_second[row, :]
    if ey == 0:
        tile = tile + jnp.where(place.row == 0, place.before_y(got_a, got_b), 0.0)
    else:
        tile = tile + jnp.where(place.row == 7, place.after_y(got_a, got_b), 0.0)
    return tile


def got_x_sum(place, tile, ch, ex, ey, x_first, x_second):
    rows = pl.ds(ch * 16 + ey * 8, 8)
    pick = place.before_x if ex == 0 else place.after_x
    return tile + pick(x_first[rows, :], x_second[rows, :])


def pack_kernel(kappa, group, coarse, pack, facts):
    place = Place()
    facts[...] = jnp.zeros(facts.shape, jnp.float32)
    grid = jnp.zeros((1, LANES), jnp.float32)
    elems = kappa.shape[2]
    to = lax.broadcasted_iota(jnp.int32, (elems, LANES), 1)
    element = lax.broadcasted_iota(jnp.int32, (elems, LANES), 0)
    blocks = coarse.shape[1] // LANES
    packed = jnp.zeros((1, LANES), jnp.float32)
    for ex in range(2):
        numbers = group[ex].astype(jnp.float32)
        for ey in range(2):
            mine, number = kappa[ex, pl.ds(ey, 1), :], numbers[ey : ey + 1]
            at = (2 * ex + ey) * elems
            packed = packed + exact_dot(mine, (to == at + element).astype(jnp.float32))
            at = at + 4 * elems
            packed = packed + exact_dot(number, (to == at + element).astype(jnp.float32))
            at = ((2 * place.iy + ey) * elems + 4 * ex * elems) % LANES
            grid = grid + exact_dot(mine, (to == at + element).astype(jnp.float32))
            at = (at + 2 * elems) % LANES
            grid = grid + exact_dot(number, (to == at + element).astype(jnp.float32))
    pack[pl.ds(0, 1), :] = packed
    for c in range(NCD):
        for j in range(blocks):
            line = coarse[pl.ds(c, 1), pl.ds(j * LANES, LANES)]
            pack[pl.ds(1 + c * blocks + j, 1), :] = line
        facts[:, pl.ds((2 + c) * LANES, LANES)] = coarse[pl.ds(c, 1), pl.ds(0, LANES)]
    facts[:, pl.ds(LANES, LANES)] = grid


def prepare_kernel(
    summed, visc, y_first, y_second, ctab, zmat, start, part, slope, answer, grad_z, flux_z
):
    place = Place()
    weight = ctab[T_W]
    inv_mass = [1.0 / (weight * place.mult_tile(ey)) for ey in range(2)]

    def begin(ch, carry):
        for ex in range(2):
            for a in range(8):
                for ey in range(2):
                    tile = got_y_sum(
                        place, summed[ch, ex, a, ey], ch, ex, a, ey, y_first, y_second
                    )
                    scale = place.inv_x(ex, a) * float(1.0 / WEIGHTS[a])
                    start[ch, ex, a, ey] = tile * (inv_mass[ey] * scale)
        return carry

    lax.fori_loop(0, 4, begin, 0)
    grad_z[...] = along_z(start[...].reshape(1024, LANES), zmat[0]).reshape(grad_z.shape)

    def column(index, carry):
        ch, ey = index // 2, index % 2
        coef = jnp.where(ch == 3, 1.0 / prandtl, 1.0)
        for ex in range(2):
            grad_x = along_x(DERIV, [start[ch, ex, a, ey] for a in range(8)], -1)
            flux_x = [
                visc[ex, a, ey] * (float(WEIGHTS[a]) * weight) * coef * grad_x[a]
                for a in range(8)
            ]
            back = along_x(DERIV.T, flux_x, -1)
            for a in range(8):
                if (ex, a) in OUTER:
                    slope[ch, ex, ey] = grad_x[a]
                    part[ch, ex, a, ey] = back[a]
                    continue
                rest, flux_z[ch, ex, a, ey] = across(
                    ctab, weight, a, coef, start[ch, ex, a, ey], grad_z[ch, ex, a, ey],
                    start[1, ex, a, ey], start[2, ex, a, ey], visc[ex, a, ey],
                )
                flow = float(WEIGHTS[a]) * weight * start[0, ex, a, ey]
                part[ch, ex, a, ey] = rest + flow * grad_x[a] + back[a]
        return carry

    for ex, outer in OUTER:
        for ey in range(2):
            flux_x = [
                visc[ex, a, ey] * (float(WEIGHTS[a] * DERIV[a, outer]) * weight) for a in range(8)
            ]
            back = along_x(DERIV.T, flux_x, -1)
            for a in range(8):
                answer[ex, a, ey] = back[a]
    lax.fori_loop(0, 8, column, 0)
    for ch in range(4):
        for ex in range(2):
            inner = pl.ds(1 - ex, 7)
            back = along_z(flux_z[ch, ex, inner].reshape(112, LANES), zmat[1])
            part[ch, ex, inner] = part[ch, ex, inner] + back.reshape(7, 2, 8, LANES)


def across(ctab, weight, a, coef, value, grad_z, flow_y, flow_z, visc):
    node = float(WEIGHTS[a]) * weight
    grad_y = along_y(ctab, T_D, value)
    nu = visc * node * coef
    part = node * (flow_y * grad_y + flow_z * grad_z) + along_y(ctab, T_DT, nu * grad_y)
    return part, nu * grad_z


def rhs_kernel(
    pack_rows,
    begun,
    given,
    slope,
    answer,
    visc,
    pack,
    x_first,
    x_second,
    ctab,
    zmat,
    share,
    xf,
    inner_x,
    first,
    second,
    edge,
    edge_z,
    edge_part,
    came,
):
    place = Place()
    weight = ctab[T_W]
    inv_mass = [1.0 / (weight * place.mult_tile(ey)) for ey in range(2)]
    for ch in range(4):
        for side, (ex, a) in enumerate(OUTER):
            scale = place.inv_x(ex, a) * float(1.0 / WEIGHTS[a])
            for ey in range(2):
                zero = jnp.zeros(TILE, jnp.float32)
                extra = got_x_sum(place, zero, ch, ex, ey, x_first, x_second)
                extra = extra * (inv_mass[ey] * scale)
                came[ch, side, ey] = extra
                edge[ch, side, ey] = begun[ch, ex, a, ey] + extra
    edge_z[...] = along_z(edge[...].reshape(128, LANES), zmat[0]).reshape(edge.shape)
    for ch in range(4):
        coef = 1.0 / prandtl if ch == 3 else 1.0
        for side, (ex, a) in enumerate(OUTER):
            for ey in range(2):
                parts = across(
                    ctab, weight, a, coef, edge[ch, side, ey], edge_z[ch, side, ey],
                    edge[1, side, ey], edge[2, side, ey], visc[ex, a, ey],
                )
                edge_part[ch, side, ey], edge_z[ch, side, ey] = parts
    edge_part[...] = edge_part[...] + along_z(
        edge_z[...].reshape(128, LANES), zmat[1]
    ).reshape(edge.shape)

    def side_of(ch, ex, a, ey):
        outer = OUTER[ex][1]
        coef = jnp.where(ch == 3, 1.0 / prandtl, 1.0)
        extra = came[ch, ex, ey]
        node = float(WEIGHTS[a]) * weight
        turn = float(DERIV[a, outer])
        if a == outer:
            known = given[ch, ex, a, ey] + edge_part[ch, ex, ey]
            known = known + node * edge[0, ex, ey] * (slope[ch, ex, ey] + turn * extra)
            return known + extra * (coef * answer[ex, a, ey])
        flow = float(WEIGHTS[a] * turn) * weight * begun[0, ex, a, ey]
        return given[ch, ex, a, ey] + extra * (coef * answer[ex, a, ey] + flow)

    def finish(ch, carry):
        tiles = [
            [[place.join_z(-side_of(ch, ex, a, ey)) for ey in range(2)] for a in range(8)]
            for ex in range(2)
        ]
        join_own(place, tiles)
        for ex in range(2):
            for a in range(8):
                scale = place.inv_x(ex, a) * float(dt_step / WEIGHTS[a])
                for ey in range(2):
                    value = edge[ch, ex, ey] if (ex, a) in OUTER else begun[ch, ex, a, ey]
                    part = value * (place.share_y(ey) * place.share_x(ex, a))
                    share[ch, ex, a, ey] = part + tiles[ex][a][ey] * (inv_mass[ey] * scale)
        return carry

    lax.fori_loop(0, 4, finish, 0)
    for ch in range(4):
        store_y_faces(place, share, first, second, (ch,), ch * 16)
        for ey in range(2):
            xf[0, ch, ey] = share[ch, 0, 0, ey]
            xf[1, ch, ey] = share[ch, 1, 7, ey]

    def column_of(ex, ey):
        return [share[0, ex, a, ey] for a in range(8)]

    def tile_of(ex, a, ey):
        return share[1, ex, a, ey]

    store_inner(
        place, DERIV, ctab[T_BOTTOM], ctab[T_TOP], column_of, tile_of, inner_x, first, second,
        STEP_V, STEP_EDGE,
    )
    beside = pl.ds(64, pack_rows)
    parts = (
        place.before_x(x_first[beside, :], x_second[beside, :]),
        pack[...],
        place.after_x(x_first[beside, :], x_second[beside, :]),
    )
    for k in range(3):
        rows = pl.ds(STEP_PACK + k * pack_rows, pack_rows)
        first[rows, :] = parts[k]
        second[rows, :] = parts[k]


def store_inner(
    place, matrix, bottom, top, column_of, tile_of, inner_x, first, second, at, edge
):
    for ey in range(2):
        low, high = column_of(0, ey), column_of(1, ey)
        below = float(matrix[0, 1]) * low[1]
        above = float(matrix[7, 0]) * high[0]
        for k in range(2, 8):
            below = below + float(matrix[0, k]) * low[k]
            above = above + float(matrix[7, k - 1]) * high[k - 1]
        inner_x[0, ey] = below
        inner_x[1, ey] = above
    for side in range(2):
        low = inner_x[side, 0, pl.ds(0, 1), :]
        high = inner_x[side, 1, pl.ds(7, 1), :]
        first[pl.ds(edge + side, 1), :] = place.after_y(high, low)
        second[pl.ds(edge + side, 1), :] = place.after_y(low, high)
    for ex in range(2):
        for a in range(8):
            low = jnp.sum(bottom * tile_of(ex, a, 0), axis=0, keepdims=True)
            high = jnp.sum(top * tile_of(ex, a, 1), axis=0, keepdims=True)
            row = pl.ds(at + ex * 8 + a, 1)
            first[row, :] = place.after_y(high, low)
            second[row, :] = place.after_y(low, high)


def cross_flow(place, ctab, flow, slopes, rows, inv_y, inv_z):
    below, above = rows
    below = (below - float(DERIV[0, 0]) * flow[0]) * jnp.where(place.prev_y, 1.0, 0.0)
    above = (above - float(DERIV[7, 7]) * flow[1]) * jnp.where(place.next_y, 1.0, 0.0)
    grad_y = list(place.join_y(*[along_y(ctab, T_D, tile) for tile in flow]))
    grad_y[0] = grad_y[0] + jnp.where(place.row == 0, below, 0.0)
    grad_y[1] = grad_y[1] + jnp.where(place.row == 7, above, 0.0)
    return [grad_y[ey] * inv_y[ey] + place.join_z(slopes[ey]) * inv_z for ey in range(2)]


def approach_kernel(share, y_first, y_second, ctab, zmat, fields_new, part, grad_z):
    place = Place()

    def step(ch, carry):
        for ex in range(2):
            for a in range(8):
                for ey in range(2):
                    fields_new[ch, ex, a, ey] = got_y_sum(
                        place, share[ch, ex, a, ey], ch, ex, a, ey, y_first, y_second
                    )
        return carry

    lax.fori_loop(0, 4, step, 0)
    grad_z[...] = along_z(fields_new[2].reshape(256, LANES), zmat[0]).reshape(grad_z.shape)
    inv_y = [place.inv_y(ey) for ey in range(2)]
    inv_z = place.inv_z()
    for ex in range(2):
        for a in range(8):
            if (ex, a) in OUTER:
                continue
            flow = [fields_new[1, ex, a, ey] for ey in range(2)]
            rows = inner_along_y(place, y_first, y_second, None, None, ex, a, STEP_V, STEP_EDGE)
            slopes = [grad_z[ex, a, ey] for ey in range(2)]
            both = cross_flow(place, ctab, flow, slopes, rows, inv_y, inv_z)
            part[ex, a, 0], part[ex, a, 1] = both


def emit_kernel(begun, x_first, x_second, extra, fields_new, passed):
    place = Place()
    passed[...] = extra[...]
    fields_new[...] = begun[...]
    for ch in range(4):
        for ex, a in OUTER:
            for ey in range(2):
                fields_new[ch, ex, a, ey] = got_x_sum(
                    place, begun[ch, ex, a, ey], ch, ex, ey, x_first, x_second
                )


def advance_kernel(
    begun,
    given,
    y_first,
    y_second,
    x_first,
    x_second,
    inv_diag,
    kap,
    grp,
    ctab,
    zmat,
    resid,
    own,
    msg,
    grad_z,
    scaled,
    edge,
    part,
    outer,
):
    place = Place()
    weight = ctab[T_W]

    def before(row, count=8):
        rows = pl.ds(row, count)
        return place.before_x(x_first[rows, :], x_second[rows, :])

    def after(row, count=8):
        rows = pl.ds(row, count)
        return place.after_x(x_first[rows, :], x_second[rows, :])

    part[...] = given[...]
    for ch in range(3):
        for side, (ex, a) in enumerate(OUTER):
            for ey in range(2):
                outer[ch, side, ey] = got_x_sum(
                    place, begun[ch, ex, a, ey], ch, ex, ey, x_first, x_second
                )
    edge[...] = along_z(outer[2].reshape(32, LANES), zmat[0]).reshape(edge.shape)
    inv_y = [place.inv_y(ey) for ey in range(2)]
    inv_z = place.inv_z()
    for side, (ex, a) in enumerate(OUTER):
        flow = [outer[1, side, ey] for ey in range(2)]
        rows = inner_along_y(place, y_first, y_second, before, after, ex, a, STEP_V, STEP_EDGE)
        slopes = [edge[side, ey] for ey in range(2)]
        both = cross_flow(place, ctab, flow, slopes, rows, inv_y, inv_z)
        part[ex, a, 0], part[ex, a, 1] = both
    slope = [[None, None], [None, None]]
    for ey in range(2):
        for ex in range(2):
            line = [
                outer[0, ex, ey] if (ex, a) in OUTER else begun[0, ex, a, ey] for a in range(8)
            ]
            slope[ex][ey] = along_x(DERIV, line, -1)
        mid = 0.5 * (slope[0][ey][7] + slope[1][ey][0])
        slope[0][ey][7] = mid
        slope[1][ey][0] = mid
        low, high = slope[0][ey][0], slope[1][ey][7]
        inner_low = low - float(DERIV[0, 0]) * outer[0, 0, ey] + before(STEP_U + ey * 8)
        inner_high = high - float(DERIV[7, 7]) * outer[0, 1, ey] + after(STEP_U + ey * 8)
        slope[0][ey][0] = jnp.where(place.prev_x, 0.5 * inner_low, low)
        slope[1][ey][7] = jnp.where(place.next_x, 0.5 * inner_high, high)
    sums = [[jnp.zeros(TILE, jnp.float32) for _ in range(2)] for _ in range(2)]
    inv_mult = [1.0 / place.mult_tile(ey) for ey in range(2)]
    mass = [weight * place.mult_tile(ey) for ey in range(2)]
    for ex in range(2):
        for a in range(8):
            for ey in range(2):
                div = slope[ex][ey][a] + part[ex, a, ey]
                value = div * (mass[ey] * (place.mult_x(ex, a) * float(-WEIGHTS[a])))
                resid[ex, a, ey] = value
                scaled[ex, a, ey] = value * inv_diag[ex, a, ey] * float(1.0 / THETA)
                sums[ex][ey] = sums[ex][ey] + value * (inv_mult[ey] * place.inv_x(ex, a))
    grad_z[...] = along_z(scaled[...].reshape(256, LANES), zmat[2]).reshape(grad_z.shape)
    tiles = [[[None, None] for _ in range(8)] for _ in range(2)]
    for ex in range(2):
        for ey in range(2):
            images = own_operator(ctab, kap, scaled, grad_z, ex, ey)[1]
            for a in range(8):
                tiles[ex][a][ey] = place.join_z(images[a])
    join_own(place, tiles)
    for ex in range(2):
        for a in range(8):
            for ey in range(2):
                own[ex, a, ey] = tiles[ex][a][ey]
    row = message(place, restricted(place, sums, grp), [])
    blank = jnp.where(place.row == 0, jnp.broadcast_to(row, TILE), 0.0)

    def clear(i, carry):
        msg[i] = blank
        return carry

    lax.fori_loop(0, msg.shape[0], clear, 0, unroll=msg.shape[0] <= 64)
    across = Pairing(place)
    for side, (ex, a) in enumerate(OUTER):
        there, ix = across.beside(side)

        @pl.when(there)
        def _():
            msg[ix * place.ny + place.iy] = own[ex, a, 0]
            msg[ix * place.ny + across.twin, pl.ds(1, 7), :] = own[ex, a, 1, pl.ds(1, 7), :]

        @pl.when(there & across.has_far)
        def _():
            msg[ix * place.ny + across.far, pl.ds(1, 1), :] = across.far_row(own, ex, a)

    @pl.when(across.has_far)
    def _():
        for a in range(8):
            msg[place.ix * place.ny + across.far, pl.ds(a, 1), :] = across.far_row(own, 0, a)
            if a > 0:
                to = place.ix * place.ny + across.beyond
                msg[to, pl.ds(a, 1), :] = across.far_row(own, 1, a)


def inner_along_y(place, y_first, y_second, before, after, ex, a, at, edge):
    row = pl.ds(at + ex * 8 + a, 1)
    got_a, got_b = y_first[row, :], y_second[row, :]
    below, above = place.before_y(got_a, got_b), place.after_y(got_a, got_b)
    if before is None:
        return below, above
    if (ex, a) == (0, 0):
        below = below + before(edge, 1)
        above = above + before(edge + 1, 1)
    if (ex, a) == (1, 7):
        below = below + after(edge, 1)
        above = above + after(edge + 1, 1)
    return below, above


class Pairing:
    def __init__(self, place):
        self.place = place
        even = place.even_y
        self.even = even
        self.twin = jnp.where(even, place.iy + 1, place.iy - 1)
        self.far = jnp.where(even, place.iy - 1, place.iy + 1)
        self.has_far = jnp.where(even, place.iy - 1, place.ny - 2 - place.iy) >= 0
        self.beyond = jnp.where(even, place.iy - 2, place.iy + 2)
        self.twin_far = jnp.where(even, place.iy + 2, place.iy - 2)
        self.twin_has_far = jnp.where(even, place.ny - 3 - place.iy, place.iy - 2) >= 0

    def beside(self, side):
        place = self.place
        if side == 0:
            return place.prev_x, place.ix - 1
        return place.next_x, place.ix + 1

    def far_row(self, field, ex, a):
        low = field[ex, a, 0, pl.ds(0, 1), :]
        return jnp.where(self.even, low, field[ex, a, 1, pl.ds(7, 1), :])

    def twin_row(self, field, ex, a):
        low = field[ex, a, 0, pl.ds(0, 1), :]
        return jnp.where(self.even, field[ex, a, 1, pl.ds(7, 1), :], low)


RELAY_FACE, RELAY_EDGE, RELAY_ROWS = 24, 40, 42


def relay_kernel(got, own, out):
    place = Place()
    across = Pairing(place)
    out[...] = jnp.zeros(out.shape, jnp.float32)
    for side in range(2):
        there, ix = across.beside(side)

        @pl.when(there)
        def _():
            out[pl.ds(side * 8, 8), :] = got[ix * place.ny + across.twin]
            corner = got[ix * place.ny + place.iy, pl.ds(0, 1), :]
            out[pl.ds(RELAY_EDGE + side, 1), :] = corner

    @pl.when(across.twin_has_far)
    def _():
        out[pl.ds(16, 8), :] = got[place.ix * place.ny + across.twin_far]

    for ex in range(2):
        for a in range(8):
            out[pl.ds(RELAY_FACE + ex * 8 + a, 1), :] = across.twin_row(own, ex, a)


SMOOTH_X, SMOOTH_Y, SMOOTH_EDGE, SMOOTH_ROWS = 16, 16, 32, 34


def turn_smooth_kernel(own, inner_x, y_first, y_second, first, second):
    place = Place()
    sides = []
    for side, (ex, a) in enumerate(((0, 0), (1, 7))):
        row = pl.ds(15 * side, 1)
        got_a, got_b = y_first[row, :], y_second[row, :]
        low = own[ex, a, 0] + jnp.where(place.row == 0, place.before_y(got_a, got_b), 0.0)
        high = own[ex, a, 1] + jnp.where(place.row == 7, place.after_y(got_a, got_b), 0.0)
        sides.append((low, high))
    for ey in range(2):
        rows = pl.ds(ey * 8, 8)
        first[rows, :] = place.after_x(sides[1][ey], sides[0][ey])
        second[rows, :] = place.after_x(sides[0][ey], sides[1][ey])
    turn_edges(
        place, inner_x, y_first, y_second, first, second, SMOOTH_X, SMOOTH_EDGE, SMOOTH_Y
    )


def restricted(place, sums, grp):
    values = []
    for c in range(NCD):
        acc = jnp.zeros(TILE, jnp.float32)
        for ex in range(2):
            for ey in range(2):
                group = grp[pl.ds((ex + 1) * 4 + ey + 1, 1), :]
                acc = acc + jnp.where(group == float(c), sums[ex][ey], 0.0)
        values.append(total(acc))
    return values


AWAY = 16
BEYOND = 18


def message(place, own_values, scalars, away=0, beyond=1):
    lane = lax.broadcasted_iota(jnp.int32, (1, LANES), 1)
    spot = (place.ix * place.ny + place.iy) % (LANES // NCD)
    after = (spot + beyond) % (LANES // NCD)
    spot = (spot + away) % (LANES // NCD)
    row = jnp.zeros((1, LANES), jnp.float32)
    for c, value in enumerate(own_values):
        row = row + jnp.where(lane == spot * NCD + c, value, 0.0)
    for c, value in enumerate(scalars):
        if value is None:
            continue
        row = row + jnp.where(lane == after * NCD + c, value, 0.0)
    return row


def send_to_all(msg, row):
    def send(i, carry):
        msg[i] = row
        return carry

    lax.fori_loop(0, msg.shape[0], send, 0, unroll=msg.shape[0] <= 64)


def cross_image(place, ctab, kap, value, flat, inner, ex, ey):
    slope_y = along_y(ctab, T_K, value)
    turned_y = inner + float(SCALED[0, 0]) * value
    own = kap[pl.ds((ex + 1) * 4 + ey + 1, 1), :] * (slope_y + flat) + sigma_p * value
    beyond = kap[pl.ds((ex + 1) * 4 + 3 * ey, 1), :] * (turned_y + flat) + sigma_p * value
    return own + jnp.where(beyond_y(place, ey), beyond, 0.0), slope_y, turned_y


def beyond_y(place, ey):
    if ey == 0:
        return (place.row == 0) & place.prev_y
    return (place.row == 7) & place.next_y


def ready_kernel(
    own, y_first, y_second, inv_diag, kap, ctab, zmat, image, scaled, part, slope_z
):
    place = Place()
    for ex in range(2):
        for a in range(8):
            for ey in range(2):
                tile = got_y_sum(place, own[ex, a, ey], 0, ex, a, ey, y_first, y_second)
                image[ex, a, ey] = tile
                scaled[ex, a, ey] = tile * inv_diag[ex, a, ey] * float(1.0 / THETA)
    slope_z[...] = along_z(scaled[...].reshape(256, LANES), zmat[2]).reshape(slope_z.shape)
    for ex in range(2):
        for a in range(8):
            if (ex, a) in OUTER:
                continue
            rows = inner_along_y(
                place, y_first, y_second, None, None, ex, a, SMOOTH_Y, SMOOTH_EDGE
            )
            for ey in range(2):
                part[ex, a, ey] = cross_image(
                    place, ctab, kap, scaled[ex, a, ey], slope_z[ex, a, ey], rows[ey], ex, ey
                )[0]


def smooth_kernel(
    begun,
    begun_scaled,
    given,
    y_first,
    y_second,
    x_first,
    x_second,
    inv_diag,
    kap,
    grp,
    extra,
    facts,
    ctab,
    zmat,
    image,
    smoothed,
    msg,
    scaled,
    slope_z,
    edge,
):
    place = Place()
    weight = ctab[T_W]
    corner = float(SCALED[0, 0])

    def before(row, count=8):
        rows = pl.ds(row, count)
        return place.before_x(x_first[rows, :], x_second[rows, :])

    def after(row, count=8):
        rows = pl.ds(row, count)
        return place.after_x(x_first[rows, :], x_second[rows, :])

    image[...] = begun[...]
    scaled[...] = begun_scaled[...]
    for side, (ex, a) in enumerate(OUTER):
        for ey in range(2):
            tile = got_x_sum(place, begun[ex, a, ey], 0, ex, ey, x_first, x_second)
            image[ex, a, ey] = tile
            scaled[ex, a, ey] = tile * inv_diag[ex, a, ey] * float(1.0 / THETA)
            edge[side, ey] = scaled[ex, a, ey]
    edge[...] = along_z(edge[...].reshape(32, LANES), zmat[2]).reshape(edge.shape)
    there_x = (place.prev_x, place.next_x)
    zero = jnp.zeros(TILE, jnp.float32)
    tiles = [[[None, None] for _ in range(8)] for _ in range(2)]
    for ex in range(2):
        a_out = OUTER[ex][1]
        rows = inner_along_y(
            place, y_first, y_second, before, after, ex, a_out, SMOOTH_Y, SMOOTH_EDGE
        )
        for ey in range(2):
            values = [scaled[ex, a, ey] for a in range(8)]
            slopes = along_x(SCALED, values, 1)
            far_row = beyond_y(place, ey)
            beside = kap[pl.ds((ex + 1) * 4 + 3 * ey, 1), :]
            kappa = kap[pl.ds((ex + 1) * 4 + ey + 1, 1), :] + jnp.where(far_row, beside, 0.0)
            for a in range(8):
                if a != a_out:
                    acc = given[ex, a, ey]
                else:
                    value, flat = values[a], edge[ex, ey]
                    acc, slope_y, turned_y = cross_image(
                        place, ctab, kap, value, flat, rows[ey], ex, ey
                    )
                    x_next = 3 * ex
                    get = before if ex == 0 else after
                    turned_x = get(SMOOTH_X + ey * 8) + corner * value
                    side = kap[pl.ds(x_next * 4 + ey + 1, 1), :] * (turned_x + slope_y + flat)
                    far = kap[pl.ds(x_next * 4 + 3 * ey, 1), :] * (turned_x + turned_y + flat)
                    side = side + sigma_p * value
                    side = side + jnp.where(far_row, far + sigma_p * value, zero)
                    acc = acc + jnp.where(there_x[ex], side, zero)
                acc = acc + kappa * slopes[a]
                tiles[ex][a][ey] = place.join_z(acc * (float(WEIGHTS[a]) * weight))
    join_own(place, tiles)
    inv_mult = [1.0 / place.mult_tile(ey) for ey in range(2)]
    sums = [[jnp.zeros(TILE, jnp.float32) for _ in range(2)] for _ in range(2)]
    square = jnp.zeros(TILE, jnp.float32)
    for ex in range(2):
        for a in range(8):
            for ey in range(2):
                value = image[ex, a, ey]
                defect = (value - tiles[ex][a][ey]) * inv_diag[ex, a, ey]
                update = scaled[ex, a, ey]
                result = (
                    float(1.0 + RHO_NEXT * RHO) * update + float(2.0 * RHO_NEXT / DELTA) * defect
                )
                smoothed[ex, a, ey] = result
                weighed = value * (inv_mult[ey] * place.inv_x(ex, a))
                sums[ex][ey] = sums[ex][ey] + weighed
                square = square + weighed * result
    own_sums = restricted(place, sums, grp)
    if msg.shape[2] == LANES:
        sums = [extra[:, pl.ds(k, 1)] for k in range(2)]
        send_to_all(msg, message(place, own_sums, sums))
        return
    slope_z[...] = along_z(smoothed[...].reshape(256, LANES), zmat[2]).reshape(slope_z.shape)
    energy = jnp.zeros(TILE, jnp.float32)
    for ex in range(2):
        for ey in range(2):
            values, images = own_operator(ctab, kap, smoothed, slope_z, ex, ey)
            for a in range(8):
                energy = energy + values[a] * images[a]
                tiles[ex][a][ey] = place.join_z(images[a])
    join_own(place, tiles)
    sums = [extra[:, pl.ds(k, 1)] for k in range(2)] + [total(square), total(energy)]
    row = message(place, own_sums, sums, AWAY, BEYOND)
    row = row + restricted_around(place, tiles, inv_mult, grp)
    send_to_all(msg, jnp.concatenate([row, facts[:, LANES:]], axis=1))


def restricted_around(place, tiles, inv_mult, grp):
    lane = lax.broadcasted_iota(jnp.int32, (1, LANES), 1)
    weighed = [
        [[tiles[ex][a][ey] * (inv_mult[ey] * place.inv_x(ex, a)) for ey in range(2)] for a in range(8)]
        for ex in range(2)
    ]

    def rows_of(tile, y):
        if y == 0:
            return jnp.where(place.row == 0, tile[0], 0.0)
        if y == 3:
            return jnp.where(place.row == 7, tile[1], 0.0)
        return tile[y - 1]

    there_x = (place.prev_x, None, None, place.next_x)
    there_y = (place.prev_y, None, None, place.next_y)
    by_device = [
        [[jnp.zeros(TILE, jnp.float32) for _ in range(NCD)] for _ in range(3)] for _ in range(3)
    ]
    for x in range(4):
        for y in range(4):
            if x == 0:
                acc = rows_of(weighed[0][0], y)
            elif x == 3:
                acc = rows_of(weighed[1][7], y)
            else:
                acc = rows_of(weighed[x - 1][0], y)
                for a in range(1, 8):
                    acc = acc + rows_of(weighed[x - 1][a], y)
            for there in (there_x[x], there_y[y]):
                if there is not None:
                    acc = jnp.where(there, acc, 0.0)
            group = grp[pl.ds(x * 4 + y, 1), :]
            device = by_device[(x + 1) // 2][(y + 1) // 2]
            for c in range(NCD):
                device[c] = device[c] + jnp.where(group == float(c), acc, 0.0)
    row = jnp.zeros((1, LANES), jnp.float32)
    for dx in range(3):
        for dy in range(3):
            at = ((place.ix + dx - 1) * place.ny + place.iy + dy - 1) * NCD
            for c in range(NCD):
                row = row + jnp.where(lane == at + c, total(by_device[dx][dy][c]), 0.0)
    return row


def coarse_part(place, blocks, got, coarse, grp, others=()):
    lane = lax.broadcasted_iota(jnp.int32, (1, LANES), 1)
    values = [jnp.zeros((1, LANES), jnp.float32) for _ in range(blocks)]
    per = LANES // NCD
    for j in range(blocks):

        def gather(i, acc, j=j):
            return jnp.where(lane // NCD == i, got[j * per + i, pl.ds(0, 1), :], acc)

        values[j] = lax.fori_loop(0, per, gather, values[j], unroll=blocks == 1)
        for there, device, row in others:
            spot = (lane // NCD == device % per) & (device // per == j) & there
            values[j] = jnp.where(spot, row, values[j])

    def solved(dx, dy, c):
        acc = None
        for j in range(blocks):
            term = coarse[pl.ds(((dx * 3 + dy) * NCD + c) * blocks + j, 1), :] * values[j]
            acc = term if acc is None else acc + term
        return jnp.sum(acc, axis=1, keepdims=True)

    return prolonged(place, solved, grp)


def prolonged(place, solved, grp):
    device = [[[solved(dx, dy, c) for c in range(NCD)] for dy in range(3)] for dx in range(3)]
    inv_z = jnp.where(place.low_z | place.high_z, 0.5, 1.0)
    rows = []
    for x in range(4):
        line = []
        for y in range(4):
            group = grp[pl.ds(x * 4 + y, 1), :]
            acc = jnp.zeros((1, LANES), jnp.float32)
            for c in range(NCD):
                acc = acc + jnp.where(
                    group == float(c), device[(x + 1) // 2][(y + 1) // 2][c], 0.0
                )
            line.append(place.join_z(jnp.broadcast_to(acc, TILE)) * inv_z)
        rows.append(line)
    low_y = jnp.where(place.prev_y, 0.5, 1.0)
    high_y = jnp.where(place.next_y, 0.5, 1.0)

    def tile(ex, kind, ey):
        if kind == 1:
            vals = [rows[ex + 1][y] for y in range(4)]
        elif kind == 0:
            scale = place.inv_x(ex, 0)
            vals = [(rows[ex][y] + rows[ex + 1][y]) * scale for y in range(4)]
        else:
            scale = place.inv_x(ex, 7)
            vals = [(rows[ex + 1][y] + rows[ex + 2][y]) * scale for y in range(4)]
        mid = vals[ey + 1]
        low = (vals[ey] + mid) * (low_y if ey == 0 else 0.5)
        high = (mid + vals[ey + 2]) * (high_y if ey == 1 else 0.5)
        return jnp.where(place.row == 0, low, jnp.where(place.row == 7, high, mid))

    return tile


def kind_of(a):
    return 0 if a == 0 else (2 if a == 7 else 1)


def own_operator(ctab, kap, field, slope_z, ex, ey):
    weight = ctab[T_W]
    tiles = [field[ex, a, ey] for a in range(8)]
    slopes = along_x(SCALED, tiles, 1)
    kappa = kap[pl.ds((ex + 1) * 4 + ey + 1, 1), :]
    out = []
    for a in range(8):
        stiff = slopes[a] + along_y(ctab, T_K, tiles[a]) + slope_z[ex, a, ey]
        out.append((kappa * stiff + sigma_p * tiles[a]) * (float(WEIGHTS[a]) * weight))
    return tiles, out


def first_direction_kernel(
    blocks,
    got,
    relayed,
    coarse,
    grp,
    kap,
    inv_diag,
    resid,
    own,
    ctab,
    zmat,
    direction,
    out,
    inner_x,
    first,
    second,
    extra,
    slope_z,
    image,
):
    place = Place()
    inv_mult = [1.0 / place.mult_tile(ey) for ey in range(2)]
    across = Pairing(place)
    others = []
    for side in range(2):
        there, ix = across.beside(side)
        others.append((there, ix * place.ny + place.iy, relayed[pl.ds(side * 8, 1), :]))
    others.append(
        (across.has_far, place.ix * place.ny + across.far, relayed[pl.ds(16, 1), :])
    )
    part = coarse_part(place, blocks, got, coarse, grp, others)
    image[...] = own[...]
    far_edge = jnp.where(across.even, 0, 7)

    def add_row(ex, a, row, edge, low):
        extra = jnp.where(place.row == edge, row, 0.0)
        image[ex, a, 0] = image[ex, a, 0] + jnp.where(low, extra, 0.0)
        image[ex, a, 1] = image[ex, a, 1] + jnp.where(low, 0.0, extra)

    for ex in range(2):
        for a in range(8):
            row = relayed[pl.ds(RELAY_FACE + ex * 8 + a, 1), :]
            add_row(ex, a, row, 7 - far_edge, ~across.even)

    @pl.when(across.has_far)
    def _():
        for a in range(8):
            row = got[place.ix * place.ny + across.far, pl.ds(a, 1), :]
            add_row(0, a, row, far_edge, across.even)
            if a == 7:
                add_row(1, 0, row, far_edge, across.even)
            if a > 0:
                add_row(1, a, relayed[pl.ds(16 + a, 1), :], far_edge, across.even)

    for side, (ex, a) in enumerate(OUTER):
        there, ix = across.beside(side)

        @pl.when(there)
        def _():
            low = got[ix * place.ny + place.iy]
            high = jnp.where(
                place.row == 0, pltpu.roll(low, 1, 0), relayed[pl.ds(side * 8, 8), :]
            )
            image[ex, a, 0] = image[ex, a, 0] + low
            image[ex, a, 1] = image[ex, a, 1] + high
            corner = jnp.where(
                across.even,
                relayed[pl.ds(RELAY_EDGE + side, 1), :],
                got[ix * place.ny + across.twin, pl.ds(7, 1), :],
            )
            add_row(ex, a, corner, 7 - far_edge, ~across.even)

        @pl.when(there & across.has_far)
        def _():
            corner = got[ix * place.ny + across.far, pl.ds(1, 1), :]
            add_row(ex, a, corner, far_edge, across.even)

    energy = jnp.zeros(TILE, jnp.float32)
    for ex in range(2):
        for ey in range(2):
            kinds = [part(ex, kind, ey) for kind in range(3)]
            for a in range(8):
                known = resid[ex, a, ey]
                inverse = inv_diag[ex, a, ey]
                defect = (known - image[ex, a, ey]) * inverse
                value = (
                    float((1.0 + RHO_NEXT * RHO) / THETA) * (known * inverse)
                    + float(2.0 * RHO_NEXT / DELTA) * defect
                    + kinds[kind_of(a)]
                )
                direction[ex, a, ey] = value
                scale = place.inv_x(ex, a)
                energy = energy + value * known * (inv_mult[ey] * scale)
    slope_z[...] = along_z(direction[...].reshape(256, LANES), zmat[2]).reshape(slope_z.shape)
    curvature = jnp.zeros(TILE, jnp.float32)
    tiles = [[[None, None] for _ in range(8)] for _ in range(2)]
    for ex in range(2):
        for ey in range(2):
            values, images = own_operator(ctab, kap, direction, slope_z, ex, ey)
            for a in range(8):
                curvature = curvature + values[a] * images[a]
                tiles[ex][a][ey] = place.join_z(images[a])
    join_own(place, tiles)
    for ex in range(2):
        for a in range(8):
            for ey in range(2):
                out[ex, a, ey] = tiles[ex][a][ey]
    store_y_faces(place, out, first, second, (), 0)

    def tile_of(ex, a, ey):
        return tiles[ex][a][ey] * inv_diag[ex, a, ey] * float(1.0 / THETA)

    def column_of(ex, ey):
        return [tile_of(ex, a, ey) for a in range(8)]

    store_inner(
        place, SCALED, ctab[T_KBOTTOM], ctab[T_KTOP], column_of, tile_of, inner_x, first, second,
        SMOOTH_Y, SMOOTH_EDGE,
    )
    lane = lax.broadcasted_iota(jnp.int32, (1, LANES), 1)
    extra[...] = jnp.where(lane == 0, total(energy), total(curvature))


def gathered_scalars(got, count):
    lane = lax.broadcasted_iota(jnp.int32, (1, LANES), 1)
    per = LANES // NCD
    sums = []
    for c in range(count):
        acc = jnp.zeros((1, LANES), jnp.float32)

        def gather(i, acc, c=c):
            return acc + jnp.where(lane == ((i + 1) % per) * NCD + c, got[i], 0.0)

        acc = lax.fori_loop(0, got.shape[0], gather, acc, unroll=got.shape[0] <= per)
        sums.append(jnp.sum(acc, axis=1, keepdims=True))
    return sums


def second_direction_kernel(
    blocks,
    got,
    coarse,
    grp,
    kap,
    resid,
    direction,
    image,
    smoothed,
    ctab,
    zmat,
    following,
    known,
    msg,
    slope_z,
):
    place = Place()
    inv_mult = [1.0 / place.mult_tile(ey) for ey in range(2)]
    part = coarse_part(place, blocks, got, coarse, grp)
    energy, curvature = gathered_scalars(got, 2)
    step = energy / curvature
    lane = lax.broadcasted_iota(jnp.int32, (1, LANES), 1)
    known[...] = jnp.where(lane == 0, energy, jnp.where(lane == 1, curvature, 0.0))
    energy_next = jnp.zeros(TILE, jnp.float32)
    cross = jnp.zeros(TILE, jnp.float32)
    for ex in range(2):
        for ey in range(2):
            kinds = [part(ex, kind, ey) for kind in range(3)]
            for a in range(8):
                value = direction[ex, a, ey] - step * (smoothed[ex, a, ey] + kinds[kind_of(a)])
                following[ex, a, ey] = value
                weighed = value * (inv_mult[ey] * place.inv_x(ex, a))
                was = image[ex, a, ey]
                energy_next = energy_next + weighed * (resid[ex, a, ey] - step * was)
                cross = cross + weighed * was
    slope_z[...] = along_z(following[...].reshape(256, LANES), zmat[2]).reshape(slope_z.shape)
    square = jnp.zeros(TILE, jnp.float32)
    for ex in range(2):
        for ey in range(2):
            values, images = own_operator(ctab, kap, following, slope_z, ex, ey)
            for a in range(8):
                square = square + values[a] * images[a]
    send_to_all(msg, message(place, [], [total(energy_next), total(square), total(cross)]))


def pressure_kernel(got, known, direction, following, pressure):
    energy = known[:, pl.ds(0, 1)]
    curvature = known[:, pl.ds(1, 1)]
    energy_next, square, cross = gathered_scalars(got, 3)
    ratio = energy_next / energy
    step = energy / curvature
    step_next = energy_next / (square + 2.0 * ratio * cross + ratio * ratio * curvature)
    weight_old = step + step_next * ratio
    for ex in range(2):
        for a in range(8):
            for ey in range(2):
                pressure[ex, a, ey] = (
                    weight_old * direction[ex, a, ey] + step_next * following[ex, a, ey]
                )


def coarse_energy(place, got, values, kappa, number):
    lane, row = place.lane, place.row
    for ex in range(2):
        for gx in range(8):
            own = jnp.zeros((1, LANES), jnp.float32)
            group = jnp.zeros((1, LANES), jnp.float32)
            spot = lane[0:1] // 32
            for gy in range(4):
                line = got[gx * 4 + gy, :, pl.ds(LANES, LANES)]
                own = jnp.where(spot == (gy + 2 * ex) % 4, line, own)
                group = jnp.where(spot == (gy + 1 + 2 * ex) % 4, line, group)
            kappa[ex, pl.ds(gx, 1), :] = own
            number[ex, pl.ds(gx, 1), :] = group
    grid = [jnp.zeros(TILE, jnp.float32) for _ in range(2)]
    numbers = [pltpu.roll(number[0], 96, 1), pltpu.roll(number[1], 32, 1)]
    kappa = [kappa[0], pltpu.roll(kappa[1], 64, 1)]
    for q in range(4):
        for c in range(NCD):
            mine = jnp.where(lane == row * 16 + q * 4 + c, values, 0.0)
            mine = jnp.sum(mine, axis=1, keepdims=True)
            for ex in range(2):
                chosen = (lane // 32 == q) & (numbers[ex] == float(c))
                grid[ex] = jnp.where(chosen, mine, grid[ex])

    def ends_y(v):
        low = jnp.where(lane >= 16, 0.5 * (v + pltpu.roll(v, 16, 1)), v)
        return low, v, jnp.where(lane < 112, 0.5 * (v + pltpu.roll(v, 112, 1)), v)

    def ends_z(v):
        low = jnp.where(lane % 16 > 0, 0.5 * (v + pltpu.roll(v, 1, 1)), v)
        return low, v, jnp.where(lane % 16 < 15, 0.5 * (v + pltpu.roll(v, 127, 1)), v)

    low = jnp.where(row > 0, 0.5 * (grid[0] + pltpu.roll(grid[1], 1, 0)), grid[0])
    mid = 0.5 * (grid[0] + grid[1])
    high = jnp.where(row < 7, 0.5 * (grid[1] + pltpu.roll(grid[0], 7, 0)), grid[1])
    mass = [float(WEIGHTS[0]), float(np.sum(WEIGHTS[1:7])), float(WEIGHTS[7])]
    links = (
        (0, 1, -float(np.sum(STIFF[0, 1:7]))),
        (0, 2, -float(STIFF[0, 7])),
        (1, 2, -float(np.sum(STIFF[7, 1:7]))),
    )
    energy = jnp.zeros(TILE, jnp.float32)
    for ex, line in enumerate(((low, grid[0], mid), (mid, grid[1], high))):
        nodes = [[ends_z(v) for v in ends_y(w)] for w in line]
        stiff = jnp.zeros(TILE, jnp.float32)
        square = jnp.zeros(TILE, jnp.float32)
        for i in range(3):
            for j in range(3):
                for k, l, weight in links:
                    factor = weight * mass[i] * mass[j]
                    for first, second in (
                        (nodes[k][i][j], nodes[l][i][j]),
                        (nodes[i][k][j], nodes[i][l][j]),
                        (nodes[i][j][k], nodes[i][j][l]),
                    ):
                        gap = first - second
                        stiff = stiff + (factor * gap) * gap
                for k in range(3):
                    value = nodes[i][j][k]
                    square = square + (mass[i] * mass[j] * mass[k] * value) * value
        energy = energy + kappa[ex] * stiff + sigma_p * square
    return total(energy)


def finish_kernel(
    got, grp, direction, smoothed, pressure, matrix, kappa, number
):
    place = Place()
    per = LANES // NCD
    row_lane = lax.broadcasted_iota(jnp.int32, (1, LANES), 1)
    rest = jnp.zeros((1, LANES), jnp.float32)
    dual = jnp.zeros((1, LANES), jnp.float32)
    sums = [jnp.zeros((1, LANES), jnp.float32) for _ in range(4)]
    for i in range(per):
        line = got[i, :, pl.ds(0, LANES)]
        mine = row_lane // NCD == (i + AWAY) % per
        known = row_lane // NCD == (i + BEYOND) % per
        rest = jnp.where(mine, line, rest)
        dual = dual + jnp.where(mine | known, 0.0, line)
        for c in range(4):
            sums[c] = sums[c] + jnp.where(row_lane == ((i + BEYOND) % per) * NCD + c, line, 0.0)
            block = got[i, :, pl.ds((2 + c) * LANES, LANES)]
            matrix[pl.ds(i * NCD + c, 1), :] = block
    rest = pltpu.roll(rest, (per - AWAY) * NCD, 1)
    energy, curvature, square, self_energy = [
        jnp.sum(value, axis=1, keepdims=True) for value in sums
    ]
    values = lax.dot_general(
        jnp.broadcast_to(rest, TILE),
        matrix[...],
        (((1,), (1,)), ((), ())),
        precision=lax.Precision.HIGHEST,
        preferred_element_type=jnp.float32,
    )
    line = values[0:1]
    cross = square + jnp.sum(line * rest, axis=1, keepdims=True)
    both = self_energy + 2.0 * jnp.sum(line * dual, axis=1, keepdims=True)
    both = both + coarse_energy(place, got, values, kappa, number)
    step = energy / curvature
    energy_next = step * step * cross - energy
    ratio = energy_next / energy
    with_image = curvature - step * cross
    with_itself = curvature - 2.0 * step * cross + step * step * both
    step_next = energy_next / (
        with_itself + 2.0 * ratio * with_image + ratio * ratio * curvature
    )
    old = step + step_next * (1.0 + ratio)
    new = -step_next * step

    def solved(dx, dy, c):
        at = ((place.ix + dx - 1) * place.ny + place.iy + dy - 1) * NCD + c
        return jnp.sum(jnp.where(row_lane == at, line, 0.0), axis=1, keepdims=True)

    part = prolonged(place, masked(place, solved), grp)
    for ex in range(2):
        for ey in range(2):
            kinds = [part(ex, kind, ey) for kind in range(3)]
            for a in range(8):
                pressure[ex, a, ey] = old * direction[ex, a, ey] + new * (
                    smoothed[ex, a, ey] + kinds[kind_of(a)]
                )


def masked(place, solved):
    there_x = (place.prev_x, None, place.next_x)
    there_y = (place.prev_y, None, place.next_y)

    def value(dx, dy, c):
        out = solved(dx, dy, c)
        for there in (there_x[dx], there_y[dy]):
            if there is not None:
                out = jnp.where(there, out, 0.0)
        return out

    return value


def call(body, outs, scratch=(), **more):
    return pl.pallas_call(
        body,
        out_shape=[jax.ShapeDtypeStruct(shape, jnp.float32) for shape in outs],
        scratch_shapes=[
            pltpu.VMEM(shape, jnp.float32) if isinstance(shape, tuple) else shape
            for shape in scratch
        ],
        **more,
        compiler_params=pltpu.CompilerParams(vmem_limit_bytes=24 * 1024 * 1024),
    )


def swap(first, second, axis):
    count = lax.axis_size(axis)
    first_pairs = [(i, i ^ 1) for i in range(count) if i ^ 1 < count]
    second_pairs = [(i, ((i + 1) ^ 1) - 1) for i in range(1, count) if ((i + 1) ^ 1) - 1 < count]
    if axis in ('gx',):
        first_pairs, second_pairs = second_pairs, first_pairs
    first_got = lax.ppermute(first, axis, first_pairs)
    return first_got, lax.ppermute(second, axis, second_pairs)


def per_device(fields, viscosity, inv_density, elem_group, coarse_inverse):
    length = fields.shape[5]
    elems_z = length // NODES
    devices = lax.axis_size("gx") * lax.axis_size("gy")
    blocks = coarse_inverse.shape[1] // LANES
    pack_rows = 1 + NCD * blocks
    tiles_np, mats_np = constant_tables(elems_z)
    ctab, zmat = jnp.asarray(tiles_np), jnp.asarray(mats_np)
    one = fields.shape[1:]
    four = fields.shape
    faces = (64, LANES)
    xf_shape = (2, 4, 2, 8, LANES)
    inner_shape = (2, 2, 8, LANES)
    y_shape, x_shape = (STEP_PACK + 3 * pack_rows, LANES), (STEP_PACK, LANES)
    turned = (64 + pack_rows, LANES)
    smooth_shape = (SMOOTH_ROWS, LANES)
    rows = (devices, 1, LANES)
    grid_fits = (
        blocks == 1
        and lax.axis_size("gx") == 8
        and lax.axis_size("gy") * fields.shape[3] * elems_z == LANES
    )

    def exchange_all(msg):
        return lax.all_to_all(msg, BOTH, 0, 0, tiled=True)

    beside = pl.CostEstimate(flops=10**7, bytes_accessed=10**6, transcendentals=0)
    summed, xf, first, second = call(
        mass_kernel,
        [four, xf_shape, faces, faces],
    )(fields)
    pack, facts = call(
        pack_kernel,
        [(pack_rows, LANES), (1, 6 * LANES)],
        cost_estimate=beside,
    )(inv_density, elem_group, coarse_inverse)
    y_got = swap(first, second, "gy")
    first, second = call(functools.partial(turn_faces_kernel, pack_rows), [turned, turned])(
        xf, pack, *y_got
    )
    side_got = x_got = swap(first, second, "gx")
    edge_shape = (4, 2, 2, 8, LANES)
    begun, given, slope, answer = call(
        prepare_kernel, [four, four, edge_shape, one], [four, four], cost_estimate=beside
    )(summed, viscosity, *y_got, ctab, zmat)
    share, xf, inner_x, first, second = call(
        functools.partial(rhs_kernel, pack_rows),
        [four, xf_shape, inner_shape, y_shape, y_shape],
        [edge_shape, edge_shape, edge_shape, edge_shape],
    )(begun, given, slope, answer, viscosity, pack, *x_got, ctab, zmat)
    y_got = swap(first, second, "gy")
    first, second = call(turn_step_kernel, [x_shape, x_shape])(xf, inner_x, *y_got)
    x_got = swap(first, second, "gx")
    inv_diag, kap, grp, coarse = call(
        functools.partial(setup_kernel, pack_rows, blocks),
        [one, (16, LANES), (16, LANES), (9 * NCD * blocks, LANES)],
        [(16, LANES), (8, 16, LANES)],
        cost_estimate=beside,
    )(pack, *side_got, *y_got, ctab)
    begun, given = call(approach_kernel, [four, one], [one], cost_estimate=beside)(
        share, *y_got, ctab, zmat
    )
    side_shape = (2, 2, 8, LANES)
    fields_got = x_got
    fields_begun = begun
    resid, own, msg = call(
        advance_kernel,
        [one, one, (devices, 8, LANES)],
        [one, one, side_shape, one, (3,) + side_shape],
    )(begun, given, *y_got, *x_got, inv_diag, kap, grp, ctab, zmat)
    got = exchange_all(msg)
    (relayed,) = call(relay_kernel, [(RELAY_ROWS, LANES)])(got, own)
    relayed = lax.ppermute(
        relayed, "gy", [(i, i ^ 1) for i in range(lax.axis_size("gy")) if i ^ 1 < lax.axis_size("gy")]
    )
    direction, own, inner_x, first, second, extra = call(
        functools.partial(first_direction_kernel, blocks),
        [one, one, inner_shape, smooth_shape, smooth_shape, (1, LANES)],
        [one, one],
    )(got, relayed, coarse, grp, kap, inv_diag, resid, own, ctab, zmat)
    y_got = swap(first, second, "gy")
    first, second = call(turn_smooth_kernel, [smooth_shape, smooth_shape])(own, inner_x, *y_got)
    x_got = swap(first, second, "gx")
    fields_new, extra = call(emit_kernel, [four, (1, LANES)], cost_estimate=beside)(
        fields_begun, *fields_got, extra
    )
    begun, begun_scaled, given = call(
        ready_kernel, [one, one, one], [one], cost_estimate=beside
    )(own, *y_got, inv_diag, kap, ctab, zmat)
    image, image_smoothed, msg = call(
        smooth_kernel,
        [one, one, (devices, 1, 6 * LANES) if grid_fits else rows],
        [one, one, side_shape],
    )(
        begun, begun_scaled, given, *y_got, *x_got, inv_diag, kap, grp, extra, facts, ctab, zmat
    )
    got = exchange_all(msg)
    if grid_fits:
        (pressure,) = call(
            finish_kernel, [one], [(LANES, LANES), (2,) + TILE, (2,) + TILE]
        )(got, grp, direction, image_smoothed)
        return (fields_new, pressure)
    following, known, msg = call(
        functools.partial(second_direction_kernel, blocks), [one, (1, LANES), rows], [one]
    )(got, coarse, grp, kap, resid, direction, image, image_smoothed, ctab, zmat)
    got = exchange_all(msg)
    (pressure,) = call(pressure_kernel, [one])(got, known, direction, following)
    return (fields_new, pressure)


def solution(mesh):
    placed = (
        P(None, "gx", None, "gy", None, None),
        P("gx", None, "gy", None, None),
        P("gx", "gy", None),
        P("gx", "gy", None),
        P(("gx", "gy"), None),
    )
    return jax.shard_map(
        per_device,
        mesh=mesh,
        in_specs=placed,
        out_specs=(P(None, "gx", None, "gy", None, None), P("gx", None, "gy", None, None)),
        check_vma=False,
    )
```

```python
import functools

import jax
import jax.numpy as jnp
import ml_dtypes
import numpy as np
from jax import lax
from jax.experimental import pallas as pl
from jax.experimental.pallas import tpu as pltpu
from jax.sharding import PartitionSpec as P

NCD = 4
NODES = 8
LANES = 128
TILE = (8, 128)
BOTH = ("gx", "gy")

dt_step = 0.01
sigma_p = 4.0
prandtl = 0.7
cheb_ratio = 0.1


def tables():
    points = np.array(
        [
            -1.0,
            -0.8717401485096066,
            -0.5917001814331423,
            -0.2092992179024789,
            0.2092992179024789,
            0.5917001814331423,
            0.8717401485096066,
            1.0,
        ]
    )
    weights = np.array(
        [
            1.0 / 28.0,
            0.2107042271435061,
            0.3411226924835044,
            0.4124587946587038,
            0.4124587946587038,
            0.3411226924835044,
            0.2107042271435061,
            1.0 / 28.0,
        ]
    )
    identity = np.eye(8)
    differ = points[:, None] - points[None, :] + identity
    barycentric = 1.0 / np.prod(differ, axis=1)
    offdiag = barycentric[None, :] / barycentric[:, None] / differ * (1.0 - identity)
    derivative = offdiag - identity * np.sum(offdiag, axis=1)[:, None]
    mass_one = identity * weights[None, :]
    stiff_one = derivative.T @ mass_one @ derivative
    stiff_three = (
        np.kron(np.kron(stiff_one, mass_one), mass_one)
        + np.kron(np.kron(mass_one, stiff_one), mass_one)
        + np.kron(np.kron(mass_one, mass_one), stiff_one)
    )
    three_diag = np.sum(stiff_three * np.eye(512), axis=1)
    spectral_bound = float(np.max(np.sum(np.abs(stiff_three), axis=1) / three_diag))
    return (derivative, weights, stiff_one, spectral_bound)


DERIV, WEIGHTS, STIFF, BOUND = tables()
SCALED = STIFF / WEIGHTS[:, None]
LINE = np.diag(STIFF) / WEIGHTS
THETA = 0.5 * (BOUND + cheb_ratio * BOUND)
DELTA = 0.5 * (BOUND - cheb_ratio * BOUND)
RHO = DELTA / THETA
RHO_NEXT = 1.0 / (2.0 * THETA / DELTA - RHO)


def constant_tables(elems_z):
    def turned(matrix):
        rows = np.arange(8)
        return [np.repeat(matrix[rows, (rows - s) % 8][:, None], LANES, 1) for s in range(8)]

    wz = np.tile(WEIGHTS, elems_z)
    kz = np.tile(LINE, elems_z)
    tiles = turned(DERIV) + turned(DERIV.T) + turned(SCALED)
    tiles += [WEIGHTS[:, None] * wz[None, :], LINE[:, None] + kz[None, :]]
    for matrix in (DERIV, SCALED):
        for node in (7, 0):
            inner = matrix[node] * (np.arange(8) != node)
            tiles.append(np.repeat(inner[:, None], LANES, 1))
    eye = np.eye(elems_z)
    mats = [np.kron(eye, DERIV.T), np.kron(eye, DERIV), np.kron(eye, SCALED.T)]
    halves = []
    for mat in mats:
        high = mat.astype(ml_dtypes.bfloat16)
        low = (mat - high.astype(np.float64)).astype(ml_dtypes.bfloat16)
        both = np.concatenate([high, low], 1)
        halves.append(np.concatenate([both, both], 0))
    return np.stack(tiles).astype(np.float32), np.stack(halves)


T_D, T_DT, T_K, T_W, T_LINE = 0, 8, 16, 24, 25
T_TOP, T_BOTTOM, T_KTOP, T_KBOTTOM = 26, 27, 28, 29


class Place:
    def __init__(self):
        self.ix = lax.axis_index("gx")
        self.iy = lax.axis_index("gy")
        self.nx = lax.axis_size("gx")
        self.ny = lax.axis_size("gy")
        self.even_x = self.ix % 2 == 0
        self.even_y = self.iy % 2 == 0
        self.row = lax.broadcasted_iota(jnp.int32, TILE, 0)
        self.lane = lax.broadcasted_iota(jnp.int32, TILE, 1)
        self.low_z = (self.lane % 8 == 0) & (self.lane > 0)
        self.high_z = (self.lane % 8 == 7) & (self.lane < LANES - 1)
        self.prev_x = self.ix > 0
        self.next_x = self.ix < self.nx - 1
        self.prev_y = self.iy > 0
        self.next_y = self.iy < self.ny - 1

    def mult_tile(self, ey):
        along_z = 1.0 + jnp.where(self.low_z | self.high_z, 1.0, 0.0)
        low = 1.0 if ey == 1 else jnp.where(self.prev_y, 1.0, 0.0)
        high = 1.0 if ey == 0 else jnp.where(self.next_y, 1.0, 0.0)
        along_y = 1.0 + jnp.where(self.row == 0, low, jnp.where(self.row == 7, high, 0.0))
        return along_y * along_z

    def inv_x(self, ex, a):
        if a == 0:
            return 0.5 if ex == 1 else jnp.where(self.prev_x, 0.5, 1.0)
        if a == 7:
            return 0.5 if ex == 0 else jnp.where(self.next_x, 0.5, 1.0)
        return 1.0

    def mult_x(self, ex, a):
        if a == 0:
            return 2.0 if ex == 1 else jnp.where(self.prev_x, 2.0, 1.0)
        if a == 7:
            return 2.0 if ex == 0 else jnp.where(self.next_x, 2.0, 1.0)
        return 1.0

    def share_x(self, ex, a):
        if (ex, a) == (0, 0):
            return jnp.where(self.prev_x, 0.5, 1.0)
        if (ex, a) == (1, 7):
            return jnp.where(self.next_x, 0.5, 1.0)
        return 1.0

    def share_y(self, ey):
        if ey == 0:
            return jnp.where((self.row == 0) & self.prev_y, 0.5, 1.0)
        return jnp.where((self.row == 7) & self.next_y, 0.5, 1.0)

    def inv_y(self, ey):
        low = 0.5 if ey == 1 else jnp.where(self.prev_y, 0.5, 1.0)
        high = 0.5 if ey == 0 else jnp.where(self.next_y, 0.5, 1.0)
        return jnp.where(self.row == 0, low, jnp.where(self.row == 7, high, 1.0))

    def inv_z(self):
        return jnp.where(self.low_z | self.high_z, 0.5, 1.0)

    def join_z(self, t):
        up = pltpu.roll(t, LANES - 1, 1)
        down = pltpu.roll(t, 1, 1)
        return t + jnp.where(self.high_z, up, jnp.where(self.low_z, down, 0.0))

    def to_low(self, below):
        return jnp.where(self.row == 0, pltpu.roll(below, 1, 0), 0.0)

    def to_high(self, above):
        return jnp.where(self.row == 7, pltpu.roll(above, 7, 0), 0.0)

    def join_y(self, below, above):
        return below + self.to_high(above), above + self.to_low(below)

    def before_x(self, first, second):
        return jnp.where(self.prev_x, jnp.where(self.even_x, first, second), 0.0)

    def after_x(self, first, second):
        return jnp.where(self.next_x, jnp.where(self.even_x, second, first), 0.0)

    def send_x(self, first, second):
        return jnp.where(self.even_x, second, first)

    def before_y(self, first, second):
        return jnp.where(self.prev_y, jnp.where(self.even_y, second, first), 0.0)

    def after_y(self, first, second):
        return jnp.where(self.next_y, jnp.where(self.even_y, first, second), 0.0)

    def send_y(self, first, second):
        return jnp.where(self.even_y, first, second)


def along_x(matrix, tiles, sign):
    even = [tiles[a] + tiles[7 - a] for a in range(4)]
    odd = [tiles[a] - tiles[7 - a] for a in range(4)]
    out = [None] * 8
    for i in range(4):
        plus, minus = None, None
        for a in range(4):
            p = float(0.5 * (matrix[i, a] + matrix[i, 7 - a])) * even[a]
            m = float(0.5 * (matrix[i, a] - matrix[i, 7 - a])) * odd[a]
            plus = p if plus is None else plus + p
            minus = m if minus is None else minus + m
        out[i] = plus + minus
        out[7 - i] = minus - plus if sign < 0 else plus - minus
    return out


def along_y(ctab, base, tile):
    acc = ctab[base] * tile
    for s in range(1, 8):
        acc = acc + ctab[base + s] * pltpu.roll(tile, s, 0)
    return acc


def exact_dot(rows, matrix):
    return jnp.dot(
        rows, matrix, precision=lax.Precision.HIGHEST, preferred_element_type=jnp.float32
    )


def along_z(rows, matrix):
    high = rows.astype(jnp.bfloat16)
    low = (rows - high.astype(jnp.float32)).astype(jnp.bfloat16)
    both = jnp.dot(
        jnp.concatenate([high, low], axis=1), matrix, preferred_element_type=jnp.float32
    )
    return both[:, :LANES] + both[:, LANES:]


def total(tile):
    return jnp.sum(jnp.sum(tile, axis=0, keepdims=True), axis=1, keepdims=True)


def store_y_faces(place, field, first_out, second_out, lead, at):
    for ex in range(2):
        for a in range(8):
            low = field[lead + (ex, a, 0, pl.ds(0, 1), slice(None))]
            high = field[lead + (ex, a, 1, pl.ds(7, 1), slice(None))]
            row = at + ex * 8 + a
            first_out[pl.ds(row, 1), :] = place.send_y(high, low)
            second_out[pl.ds(row, 1), :] = place.send_y(low, high)


def join_own(place, tiles):
    for ex in range(2):
        for a in range(8):
            tiles[ex][a] = list(place.join_y(*tiles[ex][a]))
    for ey in range(2):
        both = tiles[0][7][ey] + tiles[1][0][ey]
        tiles[0][7][ey] = both
        tiles[1][0][ey] = both


def weight_of(node):
    edge = jnp.minimum(node, 7 - node)
    value = jnp.where(edge == 2, float(WEIGHTS[2]), float(WEIGHTS[3]))
    return jnp.where(
        edge == 0, float(WEIGHTS[0]), jnp.where(edge == 1, float(WEIGHTS[1]), value)
    )


def mass_kernel(fields, out, xf, first, second):
    place = Place()
    weight = weight_of(place.row) * weight_of(place.lane % NODES)
    for ch in range(4):
        tiles = [
            [
                [
                    place.join_z(fields[ch, ex, a, ey] * (float(WEIGHTS[a]) * weight))
                    for ey in range(2)
                ]
                for a in range(8)
            ]
            for ex in range(2)
        ]
        join_own(place, tiles)
        for ex in range(2):
            for a in range(8):
                for ey in range(2):
                    out[ch, ex, a, ey] = tiles[ex][a][ey]
        for ey in range(2):
            xf[0, ch, ey] = tiles[0][0][ey]
            xf[1, ch, ey] = tiles[1][7][ey]
        store_y_faces(place, out, first, second, (ch,), ch * 16)


def turn_faces(place, xf, y_first, y_second, first, second):
    for ch in range(4):
        sides = []
        for side in range(2):
            row = pl.ds(ch * 16 + 15 * side, 1)
            got_a, got_b = y_first[row, :], y_second[row, :]
            low = xf[side, ch, 0] + jnp.where(place.row == 0, place.before_y(got_a, got_b), 0.0)
            high = xf[side, ch, 1] + jnp.where(place.row == 7, place.after_y(got_a, got_b), 0.0)
            sides.append((low, high))
        for ey in range(2):
            rows = pl.ds(ch * 16 + ey * 8, 8)
            first[rows, :] = place.send_x(sides[1][ey], sides[0][ey])
            second[rows, :] = place.send_x(sides[0][ey], sides[1][ey])


def turn_faces_kernel(pack_rows, xf, pack, y_first, y_second, first, second):
    turn_faces(Place(), xf, y_first, y_second, first, second)
    first[pl.ds(64, pack_rows), :] = pack[...]
    second[pl.ds(64, pack_rows), :] = pack[...]


def turn_edges(place, inner_x, y_first, y_second, first, second, at, edge, inner_y):
    sides = []
    for side in range(2):
        row = pl.ds(edge + side, 1)
        got_a, got_b = y_first[row, :], y_second[row, :]
        low = inner_x[side, 0] + jnp.where(place.row == 0, place.before_y(got_a, got_b), 0.0)
        high = inner_x[side, 1] + jnp.where(place.row == 7, place.after_y(got_a, got_b), 0.0)
        sides.append((low, high))
    for ey in range(2):
        rows = pl.ds(at + ey * 8, 8)
        first[rows, :] = place.send_x(sides[1][ey], sides[0][ey])
        second[rows, :] = place.send_x(sides[0][ey], sides[1][ey])
    for k, pick in enumerate((place.before_y, place.after_y)):
        sides = []
        for side in range(2):
            row = pl.ds(inner_y + 15 * side, 1)
            sides.append(pick(y_first[row, :], y_second[row, :]))
        row = pl.ds(edge + k, 1)
        first[row, :] = place.send_x(sides[1], sides[0])
        second[row, :] = place.send_x(sides[0], sides[1])


STEP_U, STEP_V, STEP_EDGE, STEP_PACK = 64, 64, 80, 82


def turn_step_kernel(xf, inner_x, y_first, y_second, first, second):
    place = Place()
    turn_faces(place, xf, y_first, y_second, first, second)
    turn_edges(place, inner_x, y_first, y_second, first, second, STEP_U, STEP_EDGE, STEP_V)


def setup_kernel(
    pack_rows,
    blocks,
    pack,
    x_first,
    x_second,
    y_first,
    y_second,
    ctab,
    inv_diag,
    kap,
    grp,
    coarse,
    compact,
    spread,
):
    place = Place()
    beside = pl.ds(64, pack_rows)
    packs = [[None] * 3 for _ in range(3)]
    packs[0][1] = place.before_x(x_first[beside, :], x_second[beside, :])
    packs[1][1] = pack[...]
    packs[2][1] = place.after_x(x_first[beside, :], x_second[beside, :])
    for dx in range(3):
        rows = pl.ds(STEP_PACK + dx * pack_rows, pack_rows)
        packs[dx][0] = place.before_y(y_first[rows, :], y_second[rows, :])
        packs[dx][2] = place.after_y(y_first[rows, :], y_second[rows, :])
    compact[...] = jnp.zeros(compact.shape, jnp.float32)
    for dx in range(3):
        for dy in range(3):
            at = (dx * 3 + dy) * NCD * blocks
            coarse[pl.ds(at, NCD * blocks), :] = packs[dx][dy][1 : 1 + NCD * blocks]
            compact[pl.ds(dx * 3 + dy, 1), :] = packs[dx][dy][0:1]
    elems = LANES // NODES
    lane = lax.broadcasted_iota(jnp.int32, (LANES, LANES), 1)
    source = lax.broadcasted_iota(jnp.int32, (LANES, LANES), 0)
    for k in range(8):
        spot = (source == k * elems + lane // NODES).astype(jnp.float32)
        spread[k] = exact_dot(compact[...], spot)
    there_x = [jnp.where(place.prev_x, 1.0, 0.0), 1.0, jnp.where(place.next_x, 1.0, 0.0)]
    there_y = [jnp.where(place.prev_y, 1.0, 0.0), 1.0, jnp.where(place.next_y, 1.0, 0.0)]

    def element_row(base, u, v):
        device = (u // 2) * 3 + v // 2
        return spread[base + (u % 2) * 2 + v % 2, pl.ds(device, 1), :]

    for x in range(4):
        for y in range(4):
            kap[pl.ds(x * 4 + y, 1), :] = element_row(0, x + 1, y + 1)
            grp[pl.ds(x * 4 + y, 1), :] = element_row(4, x + 1, y + 1)
    kappa = [
        [
            place.join_z(jnp.broadcast_to(element_row(0, u + 1, v + 1), TILE))
            for v in range(4)
        ]
        for u in range(4)
    ]
    count_z = 1.0 + jnp.where(place.low_z | place.high_z, 1.0, 0.0)
    weight = ctab[T_W]
    line = ctab[T_LINE]

    def pick(values, ey):
        low = values[ey] + values[ey + 1]
        high = values[ey + 1] + values[ey + 2]
        return jnp.where(place.row == 0, low, jnp.where(place.row == 7, high, values[ey + 1]))

    for ex in range(2):
        for kind in range(3):
            us = {0: (ex, ex + 1), 1: (ex + 1,), 2: (ex + 1, ex + 2)}[kind]
            sums, counts = [], []
            for v in range(4):
                acc, num = None, 0.0
                for u in us:
                    acc = kappa[u][v] if acc is None else acc + kappa[u][v]
                    num = num + there_x[(u + 1) // 2]
                sums.append(acc)
                counts.append(num * there_y[(v + 1) // 2])
            for ey in range(2):
                kappa_sum = pick(sums, ey)
                mult = pick(counts, ey) * count_z
                for a in {0: (0,), 1: range(1, 7), 2: (7,)}[kind]:
                    diag = (float(LINE[a]) + line) * kappa_sum + sigma_p * mult
                    inv_diag[ex, a, ey] = 1.0 / (diag * (float(WEIGHTS[a]) * weight))


OUTER = ((0, 0), (1, 7))


def got_y_sum(place, tile, ch, ex, a, ey, y_first, y_second):
    row = pl.ds(ch * 16 + ex * 8 + a, 1)
    got_a, got_b = y_first[row, :], y_second[row, :]
    if ey == 0:
        tile = tile + jnp.where(place.row == 0, place.before_y(got_a, got_b), 0.0)
    else:
        tile = tile + jnp.where(place.row == 7, place.after_y(got_a, got_b), 0.0)
    return tile


def got_x_sum(place, tile, ch, ex, ey, x_first, x_second):
    rows = pl.ds(ch * 16 + ey * 8, 8)
    pick = place.before_x if ex == 0 else place.after_x
    return tile + pick(x_first[rows, :], x_second[rows, :])


def pack_kernel(kappa, group, coarse, pack, facts):
    place = Place()
    facts[...] = jnp.zeros(facts.shape, jnp.float32)
    grid = jnp.zeros((1, LANES), jnp.float32)
    elems = kappa.shape[2]
    to = lax.broadcasted_iota(jnp.int32, (elems, LANES), 1)
    element = lax.broadcasted_iota(jnp.int32, (elems, LANES), 0)
    blocks = coarse.shape[1] // LANES
    packed = jnp.zeros((1, LANES), jnp.float32)
    for ex in range(2):
        numbers = group[ex].astype(jnp.float32)
        for ey in range(2):
            mine, number = kappa[ex, pl.ds(ey, 1), :], numbers[ey : ey + 1]
            at = (2 * ex + ey) * elems
            packed = packed + exact_dot(mine, (to == at + element).astype(jnp.float32))
            at = at + 4 * elems
            packed = packed + exact_dot(number, (to == at + element).astype(jnp.float32))
            at = ((2 * place.iy + ey) * elems + 4 * ex * elems) % LANES
            grid = grid + exact_dot(mine, (to == at + element).astype(jnp.float32))
            at = (at + 2 * elems) % LANES
            grid = grid + exact_dot(number, (to == at + element).astype(jnp.float32))
    pack[pl.ds(0, 1), :] = packed
    for c in range(NCD):
        for j in range(blocks):
            line = coarse[pl.ds(c, 1), pl.ds(j * LANES, LANES)]
            pack[pl.ds(1 + c * blocks + j, 1), :] = line
        facts[:, pl.ds((2 + c) * LANES, LANES)] = coarse[pl.ds(c, 1), pl.ds(0, LANES)]
    facts[:, pl.ds(LANES, LANES)] = grid


def prepare_kernel(
    summed, visc, y_first, y_second, ctab, zmat, start, part, slope, answer, grad_z, flux_z
):
    place = Place()
    weight = ctab[T_W]
    inv_mass = [1.0 / (weight * place.mult_tile(ey)) for ey in range(2)]

    def begin(ch, carry):
        for ex in range(2):
            for a in range(8):
                for ey in range(2):
                    tile = got_y_sum(
                        place, summed[ch, ex, a, ey], ch, ex, a, ey, y_first, y_second
                    )
                    scale = place.inv_x(ex, a) * float(1.0 / WEIGHTS[a])
                    start[ch, ex, a, ey] = tile * (inv_mass[ey] * scale)
        return carry

    lax.fori_loop(0, 4, begin, 0)
    grad_z[...] = along_z(start[...].reshape(1024, LANES), zmat[0]).reshape(grad_z.shape)

    def column(index, carry):
        ch, ey = index // 2, index % 2
        coef = jnp.where(ch == 3, 1.0 / prandtl, 1.0)
        for ex in range(2):
            grad_x = along_x(DERIV, [start[ch, ex, a, ey] for a in range(8)], -1)
            flux_x = [
                visc[ex, a, ey] * (float(WEIGHTS[a]) * weight) * coef * grad_x[a]
                for a in range(8)
            ]
            back = along_x(DERIV.T, flux_x, -1)
            for a in range(8):
                if (ex, a) in OUTER:
                    slope[ch, ex, ey] = grad_x[a]
                    part[ch, ex, a, ey] = back[a]
                    continue
                rest, flux_z[ch, ex, a, ey] = across(
                    ctab, weight, a, coef, start[ch, ex, a, ey], grad_z[ch, ex, a, ey],
                    start[1, ex, a, ey], start[2, ex, a, ey], visc[ex, a, ey],
                )
                flow = float(WEIGHTS[a]) * weight * start[0, ex, a, ey]
                part[ch, ex, a, ey] = rest + flow * grad_x[a] + back[a]
        return carry

    for ex, outer in OUTER:
        for ey in range(2):
            flux_x = [
                visc[ex, a, ey] * (float(WEIGHTS[a] * DERIV[a, outer]) * weight) for a in range(8)
            ]
            back = along_x(DERIV.T, flux_x, -1)
            for a in range(8):
                answer[ex, a, ey] = back[a]
    lax.fori_loop(0, 8, column, 0)
    for ch in range(4):
        for ex in range(2):
            inner = pl.ds(1 - ex, 7)
            back = along_z(flux_z[ch, ex, inner].reshape(112, LANES), zmat[1])
            part[ch, ex, inner] = part[ch, ex, inner] + back.reshape(7, 2, 8, LANES)


def across(ctab, weight, a, coef, value, grad_z, flow_y, flow_z, visc):
    node = float(WEIGHTS[a]) * weight
    grad_y = along_y(ctab, T_D, value)
    nu = visc * node * coef
    part = node * (flow_y * grad_y + flow_z * grad_z) + along_y(ctab, T_DT, nu * grad_y)
    return part, nu * grad_z


def rhs_kernel(
    pack_rows,
    begun,
    given,
    slope,
    answer,
    visc,
    pack,
    x_first,
    x_second,
    ctab,
    zmat,
    share,
    xf,
    inner_x,
    first,
    second,
    edge,
    edge_z,
    edge_part,
    came,
):
    place = Place()
    weight = ctab[T_W]
    inv_mass = [1.0 / (weight * place.mult_tile(ey)) for ey in range(2)]
    for ch in range(4):
        for side, (ex, a) in enumerate(OUTER):
            scale = place.inv_x(ex, a) * float(1.0 / WEIGHTS[a])
            for ey in range(2):
                zero = jnp.zeros(TILE, jnp.float32)
                extra = got_x_sum(place, zero, ch, ex, ey, x_first, x_second)
                extra = extra * (inv_mass[ey] * scale)
                came[ch, side, ey] = extra
                edge[ch, side, ey] = begun[ch, ex, a, ey] + extra
    edge_z[...] = along_z(edge[...].reshape(128, LANES), zmat[0]).reshape(edge.shape)
    for ch in range(4):
        coef = 1.0 / prandtl if ch == 3 else 1.0
        for side, (ex, a) in enumerate(OUTER):
            for ey in range(2):
                parts = across(
                    ctab, weight, a, coef, edge[ch, side, ey], edge_z[ch, side, ey],
                    edge[1, side, ey], edge[2, side, ey], visc[ex, a, ey],
                )
                edge_part[ch, side, ey], edge_z[ch, side, ey] = parts
    edge_part[...] = edge_part[...] + along_z(
        edge_z[...].reshape(128, LANES), zmat[1]
    ).reshape(edge.shape)

    def side_of(ch, ex, a, ey):
        outer = OUTER[ex][1]
        coef = jnp.where(ch == 3, 1.0 / prandtl, 1.0)
        extra = came[ch, ex, ey]
        node = float(WEIGHTS[a]) * weight
        turn = float(DERIV[a, outer])
        if a == outer:
            known = given[ch, ex, a, ey] + edge_part[ch, ex, ey]
            known = known + node * edge[0, ex, ey] * (slope[ch, ex, ey] + turn * extra)
            return known + extra * (coef * answer[ex, a, ey])
        flow = float(WEIGHTS[a] * turn) * weight * begun[0, ex, a, ey]
        return given[ch, ex, a, ey] + extra * (coef * answer[ex, a, ey] + flow)

    def finish(ch, carry):
        tiles = [
            [[place.join_z(-side_of(ch, ex, a, ey)) for ey in range(2)] for a in range(8)]
            for ex in range(2)
        ]
        join_own(place, tiles)
        for ex in range(2):
            for a in range(8):
                scale = place.inv_x(ex, a) * float(dt_step / WEIGHTS[a])
                for ey in range(2):
                    value = edge[ch, ex, ey] if (ex, a) in OUTER else begun[ch, ex, a, ey]
                    part = value * (place.share_y(ey) * place.share_x(ex, a))
                    share[ch, ex, a, ey] = part + tiles[ex][a][ey] * (inv_mass[ey] * scale)
        return carry

    lax.fori_loop(0, 4, finish, 0)
    for ch in range(4):
        store_y_faces(place, share, first, second, (ch,), ch * 16)
        for ey in range(2):
            xf[0, ch, ey] = share[ch, 0, 0, ey]
            xf[1, ch, ey] = share[ch, 1, 7, ey]

    def column_of(ex, ey):
        return [share[0, ex, a, ey] for a in range(8)]

    def tile_of(ex, a, ey):
        return share[1, ex, a, ey]

    store_inner(
        place, DERIV, ctab[T_BOTTOM], ctab[T_TOP], column_of, tile_of, inner_x, first, second,
        STEP_V, STEP_EDGE,
    )
    beside = pl.ds(64, pack_rows)
    parts = (
        place.before_x(x_first[beside, :], x_second[beside, :]),
        pack[...],
        place.after_x(x_first[beside, :], x_second[beside, :]),
    )
    for k in range(3):
        rows = pl.ds(STEP_PACK + k * pack_rows, pack_rows)
        first[rows, :] = parts[k]
        second[rows, :] = parts[k]


def store_inner(
    place, matrix, bottom, top, column_of, tile_of, inner_x, first, second, at, edge
):
    for ey in range(2):
        low, high = column_of(0, ey), column_of(1, ey)
        below = float(matrix[0, 1]) * low[1]
        above = float(matrix[7, 0]) * high[0]
        for k in range(2, 8):
            below = below + float(matrix[0, k]) * low[k]
            above = above + float(matrix[7, k - 1]) * high[k - 1]
        inner_x[0, ey] = below
        inner_x[1, ey] = above
    for side in range(2):
        low = inner_x[side, 0, pl.ds(0, 1), :]
        high = inner_x[side, 1, pl.ds(7, 1), :]
        first[pl.ds(edge + side, 1), :] = place.send_y(high, low)
        second[pl.ds(edge + side, 1), :] = place.send_y(low, high)
    for ex in range(2):
        for a in range(8):
            low = jnp.sum(bottom * tile_of(ex, a, 0), axis=0, keepdims=True)
            high = jnp.sum(top * tile_of(ex, a, 1), axis=0, keepdims=True)
            row = pl.ds(at + ex * 8 + a, 1)
            first[row, :] = place.send_y(high, low)
            second[row, :] = place.send_y(low, high)


def cross_flow(place, ctab, flow, slopes, rows, inv_y, inv_z):
    below, above = rows
    below = (below - float(DERIV[0, 0]) * flow[0]) * jnp.where(place.prev_y, 1.0, 0.0)
    above = (above - float(DERIV[7, 7]) * flow[1]) * jnp.where(place.next_y, 1.0, 0.0)
    grad_y = list(place.join_y(*[along_y(ctab, T_D, tile) for tile in flow]))
    grad_y[0] = grad_y[0] + jnp.where(place.row == 0, below, 0.0)
    grad_y[1] = grad_y[1] + jnp.where(place.row == 7, above, 0.0)
    return [grad_y[ey] * inv_y[ey] + place.join_z(slopes[ey]) * inv_z for ey in range(2)]


def approach_kernel(share, y_first, y_second, ctab, zmat, fields_new, part, grad_z):
    place = Place()

    def step(ch, carry):
        for ex in range(2):
            for a in range(8):
                for ey in range(2):
                    fields_new[ch, ex, a, ey] = got_y_sum(
                        place, share[ch, ex, a, ey], ch, ex, a, ey, y_first, y_second
                    )
        return carry

    lax.fori_loop(0, 4, step, 0)
    grad_z[...] = along_z(fields_new[2].reshape(256, LANES), zmat[0]).reshape(grad_z.shape)
    inv_y = [place.inv_y(ey) for ey in range(2)]
    inv_z = place.inv_z()
    for ex in range(2):
        for a in range(8):
            if (ex, a) in OUTER:
                continue
            flow = [fields_new[1, ex, a, ey] for ey in range(2)]
            rows = inner_along_y(place, y_first, y_second, None, None, ex, a, STEP_V, STEP_EDGE)
            slopes = [grad_z[ex, a, ey] for ey in range(2)]
            both = cross_flow(place, ctab, flow, slopes, rows, inv_y, inv_z)
            part[ex, a, 0], part[ex, a, 1] = both


def emit_kernel(begun, x_first, x_second, extra, fields_new, passed):
    place = Place()
    passed[...] = extra[...]
    fields_new[...] = begun[...]
    for ch in range(4):
        for ex, a in OUTER:
            for ey in range(2):
                fields_new[ch, ex, a, ey] = got_x_sum(
                    place, begun[ch, ex, a, ey], ch, ex, ey, x_first, x_second
                )


def advance_kernel(
    begun,
    given,
    y_first,
    y_second,
    x_first,
    x_second,
    inv_diag,
    kap,
    grp,
    ctab,
    zmat,
    resid,
    own,
    msg,
    grad_z,
    scaled,
    edge,
    part,
    outer,
):
    place = Place()
    weight = ctab[T_W]

    def before(row, count=8):
        rows = pl.ds(row, count)
        return place.before_x(x_first[rows, :], x_second[rows, :])

    def after(row, count=8):
        rows = pl.ds(row, count)
        return place.after_x(x_first[rows, :], x_second[rows, :])

    part[...] = given[...]
    for ch in range(3):
        for side, (ex, a) in enumerate(OUTER):
            for ey in range(2):
                outer[ch, side, ey] = got_x_sum(
                    place, begun[ch, ex, a, ey], ch, ex, ey, x_first, x_second
                )
    edge[...] = along_z(outer[2].reshape(32, LANES), zmat[0]).reshape(edge.shape)
    inv_y = [place.inv_y(ey) for ey in range(2)]
    inv_z = place.inv_z()
    for side, (ex, a) in enumerate(OUTER):
        flow = [outer[1, side, ey] for ey in range(2)]
        rows = inner_along_y(place, y_first, y_second, before, after, ex, a, STEP_V, STEP_EDGE)
        slopes = [edge[side, ey] for ey in range(2)]
        both = cross_flow(place, ctab, flow, slopes, rows, inv_y, inv_z)
        part[ex, a, 0], part[ex, a, 1] = both
    slope = [[None, None], [None, None]]
    for ey in range(2):
        for ex in range(2):
            line = [
                outer[0, ex, ey] if (ex, a) in OUTER else begun[0, ex, a, ey] for a in range(8)
            ]
            slope[ex][ey] = along_x(DERIV, line, -1)
        mid = 0.5 * (slope[0][ey][7] + slope[1][ey][0])
        slope[0][ey][7] = mid
        slope[1][ey][0] = mid
        low, high = slope[0][ey][0], slope[1][ey][7]
        inner_low = low - float(DERIV[0, 0]) * outer[0, 0, ey] + before(STEP_U + ey * 8)
        inner_high = high - float(DERIV[7, 7]) * outer[0, 1, ey] + after(STEP_U + ey * 8)
        slope[0][ey][0] = jnp.where(place.prev_x, 0.5 * inner_low, low)
        slope[1][ey][7] = jnp.where(place.next_x, 0.5 * inner_high, high)
    sums = [[jnp.zeros(TILE, jnp.float32) for _ in range(2)] for _ in range(2)]
    inv_mult = [1.0 / place.mult_tile(ey) for ey in range(2)]
    mass = [weight * place.mult_tile(ey) for ey in range(2)]
    for ex in range(2):
        for a in range(8):
            for ey in range(2):
                div = slope[ex][ey][a] + part[ex, a, ey]
                value = div * (mass[ey] * (place.mult_x(ex, a) * float(-WEIGHTS[a])))
                resid[ex, a, ey] = value
                scaled[ex, a, ey] = value * inv_diag[ex, a, ey] * float(1.0 / THETA)
                sums[ex][ey] = sums[ex][ey] + value * (inv_mult[ey] * place.inv_x(ex, a))
    grad_z[...] = along_z(scaled[...].reshape(256, LANES), zmat[2]).reshape(grad_z.shape)
    tiles = [[[None, None] for _ in range(8)] for _ in range(2)]
    for ex in range(2):
        for ey in range(2):
            images = own_operator(ctab, kap, scaled, grad_z, ex, ey)[1]
            for a in range(8):
                tiles[ex][a][ey] = place.join_z(images[a])
    join_own(place, tiles)
    for ex in range(2):
        for a in range(8):
            for ey in range(2):
                own[ex, a, ey] = tiles[ex][a][ey]
    row = message(place, restricted(place, sums, grp), [])
    blank = jnp.where(place.row == 0, jnp.broadcast_to(row, TILE), 0.0)

    def clear(i, carry):
        msg[i] = blank
        return carry

    lax.fori_loop(0, msg.shape[0], clear, 0, unroll=msg.shape[0] <= 64)
    across = Pairing(place)
    for side, (ex, a) in enumerate(OUTER):
        there, ix = across.beside(side)

        @pl.when(there)
        def _():
            msg[ix * place.ny + place.iy] = own[ex, a, 0]
            msg[ix * place.ny + across.twin, pl.ds(1, 7), :] = own[ex, a, 1, pl.ds(1, 7), :]

        @pl.when(there & across.has_far)
        def _():
            msg[ix * place.ny + across.far, pl.ds(1, 1), :] = across.far_row(own, ex, a)

    @pl.when(across.has_far)
    def _():
        for a in range(8):
            msg[place.ix * place.ny + across.far, pl.ds(a, 1), :] = across.far_row(own, 0, a)
            if a > 0:
                to = place.ix * place.ny + across.beyond
                msg[to, pl.ds(a, 1), :] = across.far_row(own, 1, a)


def inner_along_y(place, y_first, y_second, before, after, ex, a, at, edge):
    row = pl.ds(at + ex * 8 + a, 1)
    got_a, got_b = y_first[row, :], y_second[row, :]
    below, above = place.before_y(got_a, got_b), place.after_y(got_a, got_b)
    if before is None:
        return below, above
    if (ex, a) == (0, 0):
        below = below + before(edge, 1)
        above = above + before(edge + 1, 1)
    if (ex, a) == (1, 7):
        below = below + after(edge, 1)
        above = above + after(edge + 1, 1)
    return below, above


class Pairing:
    def __init__(self, place):
        self.place = place
        even = place.even_y
        self.even = even
        self.twin = jnp.where(even, place.iy + 1, place.iy - 1)
        self.far = jnp.where(even, place.iy - 1, place.iy + 1)
        self.has_far = jnp.where(even, place.iy - 1, place.ny - 2 - place.iy) >= 0
        self.beyond = jnp.where(even, place.iy - 2, place.iy + 2)
        self.twin_far = jnp.where(even, place.iy + 2, place.iy - 2)
        self.twin_has_far = jnp.where(even, place.ny - 3 - place.iy, place.iy - 2) >= 0

    def beside(self, side):
        place = self.place
        if side == 0:
            return place.prev_x, place.ix - 1
        return place.next_x, place.ix + 1

    def far_row(self, field, ex, a):
        low = field[ex, a, 0, pl.ds(0, 1), :]
        return jnp.where(self.even, low, field[ex, a, 1, pl.ds(7, 1), :])

    def twin_row(self, field, ex, a):
        low = field[ex, a, 0, pl.ds(0, 1), :]
        return jnp.where(self.even, field[ex, a, 1, pl.ds(7, 1), :], low)


RELAY_FACE, RELAY_EDGE, RELAY_ROWS = 24, 40, 42


def relay_kernel(got, own, out):
    place = Place()
    across = Pairing(place)
    out[...] = jnp.zeros(out.shape, jnp.float32)
    for side in range(2):
        there, ix = across.beside(side)

        @pl.when(there)
        def _():
            out[pl.ds(side * 8, 8), :] = got[ix * place.ny + across.twin]
            corner = got[ix * place.ny + place.iy, pl.ds(0, 1), :]
            out[pl.ds(RELAY_EDGE + side, 1), :] = corner

    @pl.when(across.twin_has_far)
    def _():
        out[pl.ds(16, 8), :] = got[place.ix * place.ny + across.twin_far]

    for ex in range(2):
        for a in range(8):
            out[pl.ds(RELAY_FACE + ex * 8 + a, 1), :] = across.twin_row(own, ex, a)


SMOOTH_X, SMOOTH_Y, SMOOTH_EDGE, SMOOTH_ROWS = 16, 16, 32, 34


def turn_smooth_kernel(own, inner_x, y_first, y_second, first, second):
    place = Place()
    sides = []
    for side, (ex, a) in enumerate(((0, 0), (1, 7))):
        row = pl.ds(15 * side, 1)
        got_a, got_b = y_first[row, :], y_second[row, :]
        low = own[ex, a, 0] + jnp.where(place.row == 0, place.before_y(got_a, got_b), 0.0)
        high = own[ex, a, 1] + jnp.where(place.row == 7, place.after_y(got_a, got_b), 0.0)
        sides.append((low, high))
    for ey in range(2):
        rows = pl.ds(ey * 8, 8)
        first[rows, :] = place.send_x(sides[1][ey], sides[0][ey])
        second[rows, :] = place.send_x(sides[0][ey], sides[1][ey])
    turn_edges(
        place, inner_x, y_first, y_second, first, second, SMOOTH_X, SMOOTH_EDGE, SMOOTH_Y
    )


def restricted(place, sums, grp):
    values = []
    for c in range(NCD):
        acc = jnp.zeros(TILE, jnp.float32)
        for ex in range(2):
            for ey in range(2):
                group = grp[pl.ds((ex + 1) * 4 + ey + 1, 1), :]
                acc = acc + jnp.where(group == float(c), sums[ex][ey], 0.0)
        values.append(total(acc))
    return values


AWAY = 16
BEYOND = 18


def message(place, own_values, scalars, away=0, beyond=1):
    lane = lax.broadcasted_iota(jnp.int32, (1, LANES), 1)
    spot = (place.ix * place.ny + place.iy) % (LANES // NCD)
    after = (spot + beyond) % (LANES // NCD)
    spot = (spot + away) % (LANES // NCD)
    row = jnp.zeros((1, LANES), jnp.float32)
    for c, value in enumerate(own_values):
        row = row + jnp.where(lane == spot * NCD + c, value, 0.0)
    for c, value in enumerate(scalars):
        if value is None:
            continue
        row = row + jnp.where(lane == after * NCD + c, value, 0.0)
    return row


def send_to_all(msg, row):
    def send(i, carry):
        msg[i] = row
        return carry

    lax.fori_loop(0, msg.shape[0], send, 0, unroll=msg.shape[0] <= 64)


def cross_image(place, ctab, kap, value, flat, inner, ex, ey):
    slope_y = along_y(ctab, T_K, value)
    turned_y = inner + float(SCALED[0, 0]) * value
    own = kap[pl.ds((ex + 1) * 4 + ey + 1, 1), :] * (slope_y + flat) + sigma_p * value
    beyond = kap[pl.ds((ex + 1) * 4 + 3 * ey, 1), :] * (turned_y + flat) + sigma_p * value
    return own + jnp.where(beyond_y(place, ey), beyond, 0.0), slope_y, turned_y


def beyond_y(place, ey):
    if ey == 0:
        return (place.row == 0) & place.prev_y
    return (place.row == 7) & place.next_y


def ready_kernel(
    own, y_first, y_second, inv_diag, kap, ctab, zmat, image, scaled, part, slope_z
):
    place = Place()
    for ex in range(2):
        for a in range(8):
            for ey in range(2):
                tile = got_y_sum(place, own[ex, a, ey], 0, ex, a, ey, y_first, y_second)
                image[ex, a, ey] = tile
                scaled[ex, a, ey] = tile * inv_diag[ex, a, ey] * float(1.0 / THETA)
    slope_z[...] = along_z(scaled[...].reshape(256, LANES), zmat[2]).reshape(slope_z.shape)
    for ex in range(2):
        for a in range(8):
            if (ex, a) in OUTER:
                continue
            rows = inner_along_y(
                place, y_first, y_second, None, None, ex, a, SMOOTH_Y, SMOOTH_EDGE
            )
            for ey in range(2):
                part[ex, a, ey] = cross_image(
                    place, ctab, kap, scaled[ex, a, ey], slope_z[ex, a, ey], rows[ey], ex, ey
                )[0]


def smooth_kernel(
    begun,
    begun_scaled,
    given,
    y_first,
    y_second,
    x_first,
    x_second,
    inv_diag,
    kap,
    grp,
    extra,
    facts,
    ctab,
    zmat,
    image,
    smoothed,
    msg,
    scaled,
    slope_z,
    edge,
):
    place = Place()
    weight = ctab[T_W]
    corner = float(SCALED[0, 0])

    def before(row, count=8):
        rows = pl.ds(row, count)
        return place.before_x(x_first[rows, :], x_second[rows, :])

    def after(row, count=8):
        rows = pl.ds(row, count)
        return place.after_x(x_first[rows, :], x_second[rows, :])

    image[...] = begun[...]
    scaled[...] = begun_scaled[...]
    for side, (ex, a) in enumerate(OUTER):
        for ey in range(2):
            tile = got_x_sum(place, begun[ex, a, ey], 0, ex, ey, x_first, x_second)
            image[ex, a, ey] = tile
            scaled[ex, a, ey] = tile * inv_diag[ex, a, ey] * float(1.0 / THETA)
            edge[side, ey] = scaled[ex, a, ey]
    edge[...] = along_z(edge[...].reshape(32, LANES), zmat[2]).reshape(edge.shape)
    there_x = (place.prev_x, place.next_x)
    zero = jnp.zeros(TILE, jnp.float32)
    tiles = [[[None, None] for _ in range(8)] for _ in range(2)]
    for ex in range(2):
        a_out = OUTER[ex][1]
        rows = inner_along_y(
            place, y_first, y_second, before, after, ex, a_out, SMOOTH_Y, SMOOTH_EDGE
        )
        for ey in range(2):
            values = [scaled[ex, a, ey] for a in range(8)]
            slopes = along_x(SCALED, values, 1)
            far_row = beyond_y(place, ey)
            beside = kap[pl.ds((ex + 1) * 4 + 3 * ey, 1), :]
            kappa = kap[pl.ds((ex + 1) * 4 + ey + 1, 1), :] + jnp.where(far_row, beside, 0.0)
            for a in range(8):
                if a != a_out:
                    acc = given[ex, a, ey]
                else:
                    value, flat = values[a], edge[ex, ey]
                    acc, slope_y, turned_y = cross_image(
                        place, ctab, kap, value, flat, rows[ey], ex, ey
                    )
                    x_next = 3 * ex
                    get = before if ex == 0 else after
                    turned_x = get(SMOOTH_X + ey * 8) + corner * value
                    side = kap[pl.ds(x_next * 4 + ey + 1, 1), :] * (turned_x + slope_y + flat)
                    far = kap[pl.ds(x_next * 4 + 3 * ey, 1), :] * (turned_x + turned_y + flat)
                    side = side + sigma_p * value
                    side = side + jnp.where(far_row, far + sigma_p * value, zero)
                    acc = acc + jnp.where(there_x[ex], side, zero)
                acc = acc + kappa * slopes[a]
                tiles[ex][a][ey] = place.join_z(acc * (float(WEIGHTS[a]) * weight))
    join_own(place, tiles)
    inv_mult = [1.0 / place.mult_tile(ey) for ey in range(2)]
    sums = [[jnp.zeros(TILE, jnp.float32) for _ in range(2)] for _ in range(2)]
    square = jnp.zeros(TILE, jnp.float32)
    for ex in range(2):
        for a in range(8):
            for ey in range(2):
                value = image[ex, a, ey]
                defect = (value - tiles[ex][a][ey]) * inv_diag[ex, a, ey]
                update = scaled[ex, a, ey]
                result = (
                    float(1.0 + RHO_NEXT * RHO) * update + float(2.0 * RHO_NEXT / DELTA) * defect
                )
                smoothed[ex, a, ey] = result
                weighed = value * (inv_mult[ey] * place.inv_x(ex, a))
                sums[ex][ey] = sums[ex][ey] + weighed
                square = square + weighed * result
    own_sums = restricted(place, sums, grp)
    if msg.shape[2] == LANES:
        sums = [extra[:, pl.ds(k, 1)] for k in range(2)]
        send_to_all(msg, message(place, own_sums, sums))
        return
    slope_z[...] = along_z(smoothed[...].reshape(256, LANES), zmat[2]).reshape(slope_z.shape)
    energy = jnp.zeros(TILE, jnp.float32)
    for ex in range(2):
        for ey in range(2):
            values, images = own_operator(ctab, kap, smoothed, slope_z, ex, ey)
            for a in range(8):
                energy = energy + values[a] * images[a]
                tiles[ex][a][ey] = place.join_z(images[a])
    join_own(place, tiles)
    sums = [extra[:, pl.ds(k, 1)] for k in range(2)] + [total(square), total(energy)]
    row = message(place, own_sums, sums, AWAY, BEYOND)
    row = row + restricted_around(place, tiles, inv_mult, grp)
    send_to_all(msg, jnp.concatenate([row, facts[:, LANES:]], axis=1))


def restricted_around(place, tiles, inv_mult, grp):
    lane = lax.broadcasted_iota(jnp.int32, (1, LANES), 1)
    weighed = [
        [[tiles[ex][a][ey] * (inv_mult[ey] * place.inv_x(ex, a)) for ey in range(2)] for a in range(8)]
        for ex in range(2)
    ]

    def rows_of(tile, y):
        if y == 0:
            return jnp.where(place.row == 0, tile[0], 0.0)
        if y == 3:
            return jnp.where(place.row == 7, tile[1], 0.0)
        return tile[y - 1]

    there_x = (place.prev_x, None, None, place.next_x)
    there_y = (place.prev_y, None, None, place.next_y)
    by_device = [
        [[jnp.zeros(TILE, jnp.float32) for _ in range(NCD)] for _ in range(3)] for _ in range(3)
    ]
    for x in range(4):
        for y in range(4):
            if x == 0:
                acc = rows_of(weighed[0][0], y)
            elif x == 3:
                acc = rows_of(weighed[1][7], y)
            else:
                acc = rows_of(weighed[x - 1][0], y)
                for a in range(1, 8):
                    acc = acc + rows_of(weighed[x - 1][a], y)
            for there in (there_x[x], there_y[y]):
                if there is not None:
                    acc = jnp.where(there, acc, 0.0)
            group = grp[pl.ds(x * 4 + y, 1), :]
            device = by_device[(x + 1) // 2][(y + 1) // 2]
            for c in range(NCD):
                device[c] = device[c] + jnp.where(group == float(c), acc, 0.0)
    row = jnp.zeros((1, LANES), jnp.float32)
    for dx in range(3):
        for dy in range(3):
            at = ((place.ix + dx - 1) * place.ny + place.iy + dy - 1) * NCD
            for c in range(NCD):
                row = row + jnp.where(lane == at + c, total(by_device[dx][dy][c]), 0.0)
    return row


def coarse_part(place, blocks, got, coarse, grp, others=()):
    lane = lax.broadcasted_iota(jnp.int32, (1, LANES), 1)
    values = [jnp.zeros((1, LANES), jnp.float32) for _ in range(blocks)]
    per = LANES // NCD
    for j in range(blocks):

        def gather(i, acc, j=j):
            return jnp.where(lane // NCD == i, got[j * per + i, pl.ds(0, 1), :], acc)

        values[j] = lax.fori_loop(0, per, gather, values[j], unroll=blocks == 1)
        for there, device, row in others:
            spot = (lane // NCD == device % per) & (device // per == j) & there
            values[j] = jnp.where(spot, row, values[j])

    def solved(dx, dy, c):
        acc = None
        for j in range(blocks):
            term = coarse[pl.ds(((dx * 3 + dy) * NCD + c) * blocks + j, 1), :] * values[j]
            acc = term if acc is None else acc + term
        return jnp.sum(acc, axis=1, keepdims=True)

    return prolonged(place, solved, grp)


def prolonged(place, solved, grp):
    device = [[[solved(dx, dy, c) for c in range(NCD)] for dy in range(3)] for dx in range(3)]
    inv_z = jnp.where(place.low_z | place.high_z, 0.5, 1.0)
    rows = []
    for x in range(4):
        line = []
        for y in range(4):
            group = grp[pl.ds(x * 4 + y, 1), :]
            acc = jnp.zeros((1, LANES), jnp.float32)
            for c in range(NCD):
                acc = acc + jnp.where(
                    group == float(c), device[(x + 1) // 2][(y + 1) // 2][c], 0.0
                )
            line.append(place.join_z(jnp.broadcast_to(acc, TILE)) * inv_z)
        rows.append(line)
    low_y = jnp.where(place.prev_y, 0.5, 1.0)
    high_y = jnp.where(place.next_y, 0.5, 1.0)

    def tile(ex, kind, ey):
        if kind == 1:
            vals = [rows[ex + 1][y] for y in range(4)]
        elif kind == 0:
            scale = place.inv_x(ex, 0)
            vals = [(rows[ex][y] + rows[ex + 1][y]) * scale for y in range(4)]
        else:
            scale = place.inv_x(ex, 7)
            vals = [(rows[ex + 1][y] + rows[ex + 2][y]) * scale for y in range(4)]
        mid = vals[ey + 1]
        low = (vals[ey] + mid) * (low_y if ey == 0 else 0.5)
        high = (mid + vals[ey + 2]) * (high_y if ey == 1 else 0.5)
        return jnp.where(place.row == 0, low, jnp.where(place.row == 7, high, mid))

    return tile


def kind_of(a):
    return 0 if a == 0 else (2 if a == 7 else 1)


def own_operator(ctab, kap, field, slope_z, ex, ey):
    weight = ctab[T_W]
    tiles = [field[ex, a, ey] for a in range(8)]
    slopes = along_x(SCALED, tiles, 1)
    kappa = kap[pl.ds((ex + 1) * 4 + ey + 1, 1), :]
    out = []
    for a in range(8):
        stiff = slopes[a] + along_y(ctab, T_K, tiles[a]) + slope_z[ex, a, ey]
        out.append((kappa * stiff + sigma_p * tiles[a]) * (float(WEIGHTS[a]) * weight))
    return tiles, out


def first_direction_kernel(
    blocks,
    got,
    relayed,
    coarse,
    grp,
    kap,
    inv_diag,
    resid,
    own,
    ctab,
    zmat,
    direction,
    out,
    inner_x,
    first,
    second,
    extra,
    slope_z,
    image,
):
    place = Place()
    inv_mult = [1.0 / place.mult_tile(ey) for ey in range(2)]
    across = Pairing(place)
    others = []
    for side in range(2):
        there, ix = across.beside(side)
        others.append((there, ix * place.ny + place.iy, relayed[pl.ds(side * 8, 1), :]))
    others.append(
        (across.has_far, place.ix * place.ny + across.far, relayed[pl.ds(16, 1), :])
    )
    part = coarse_part(place, blocks, got, coarse, grp, others)
    image[...] = own[...]
    far_edge = jnp.where(across.even, 0, 7)

    def add_row(ex, a, row, edge, low):
        extra = jnp.where(place.row == edge, row, 0.0)
        image[ex, a, 0] = image[ex, a, 0] + jnp.where(low, extra, 0.0)
        image[ex, a, 1] = image[ex, a, 1] + jnp.where(low, 0.0, extra)

    for ex in range(2):
        for a in range(8):
            row = relayed[pl.ds(RELAY_FACE + ex * 8 + a, 1), :]
            add_row(ex, a, row, 7 - far_edge, ~across.even)

    @pl.when(across.has_far)
    def _():
        for a in range(8):
            row = got[place.ix * place.ny + across.far, pl.ds(a, 1), :]
            add_row(0, a, row, far_edge, across.even)
            if a == 7:
                add_row(1, 0, row, far_edge, across.even)
            if a > 0:
                add_row(1, a, relayed[pl.ds(16 + a, 1), :], far_edge, across.even)

    for side, (ex, a) in enumerate(OUTER):
        there, ix = across.beside(side)

        @pl.when(there)
        def _():
            low = got[ix * place.ny + place.iy]
            high = jnp.where(
                place.row == 0, pltpu.roll(low, 1, 0), relayed[pl.ds(side * 8, 8), :]
            )
            image[ex, a, 0] = image[ex, a, 0] + low
            image[ex, a, 1] = image[ex, a, 1] + high
            corner = jnp.where(
                across.even,
                relayed[pl.ds(RELAY_EDGE + side, 1), :],
                got[ix * place.ny + across.twin, pl.ds(7, 1), :],
            )
            add_row(ex, a, corner, 7 - far_edge, ~across.even)

        @pl.when(there & across.has_far)
        def _():
            corner = got[ix * place.ny + across.far, pl.ds(1, 1), :]
            add_row(ex, a, corner, far_edge, across.even)

    energy = jnp.zeros(TILE, jnp.float32)
    for ex in range(2):
        for ey in range(2):
            kinds = [part(ex, kind, ey) for kind in range(3)]
            for a in range(8):
                known = resid[ex, a, ey]
                inverse = inv_diag[ex, a, ey]
                defect = (known - image[ex, a, ey]) * inverse
                value = (
                    float((1.0 + RHO_NEXT * RHO) / THETA) * (known * inverse)
                    + float(2.0 * RHO_NEXT / DELTA) * defect
                    + kinds[kind_of(a)]
                )
                direction[ex, a, ey] = value
                scale = place.inv_x(ex, a)
                energy = energy + value * known * (inv_mult[ey] * scale)
    slope_z[...] = along_z(direction[...].reshape(256, LANES), zmat[2]).reshape(slope_z.shape)
    curvature = jnp.zeros(TILE, jnp.float32)
    tiles = [[[None, None] for _ in range(8)] for _ in range(2)]
    for ex in range(2):
        for ey in range(2):
            values, images = own_operator(ctab, kap, direction, slope_z, ex, ey)
            for a in range(8):
                curvature = curvature + values[a] * images[a]
                tiles[ex][a][ey] = place.join_z(images[a])
    join_own(place, tiles)
    for ex in range(2):
        for a in range(8):
            for ey in range(2):
                out[ex, a, ey] = tiles[ex][a][ey]
    store_y_faces(place, out, first, second, (), 0)

    def tile_of(ex, a, ey):
        return tiles[ex][a][ey] * inv_diag[ex, a, ey] * float(1.0 / THETA)

    def column_of(ex, ey):
        return [tile_of(ex, a, ey) for a in range(8)]

    store_inner(
        place, SCALED, ctab[T_KBOTTOM], ctab[T_KTOP], column_of, tile_of, inner_x, first, second,
        SMOOTH_Y, SMOOTH_EDGE,
    )
    lane = lax.broadcasted_iota(jnp.int32, (1, LANES), 1)
    extra[...] = jnp.where(lane == 0, total(energy), total(curvature))


def gathered_scalars(got, count):
    lane = lax.broadcasted_iota(jnp.int32, (1, LANES), 1)
    per = LANES // NCD
    sums = []
    for c in range(count):
        acc = jnp.zeros((1, LANES), jnp.float32)

        def gather(i, acc, c=c):
            return acc + jnp.where(lane == ((i + 1) % per) * NCD + c, got[i], 0.0)

        acc = lax.fori_loop(0, got.shape[0], gather, acc, unroll=got.shape[0] <= per)
        sums.append(jnp.sum(acc, axis=1, keepdims=True))
    return sums


def second_direction_kernel(
    blocks,
    got,
    coarse,
    grp,
    kap,
    resid,
    direction,
    image,
    smoothed,
    ctab,
    zmat,
    following,
    known,
    msg,
    slope_z,
):
    place = Place()
    inv_mult = [1.0 / place.mult_tile(ey) for ey in range(2)]
    part = coarse_part(place, blocks, got, coarse, grp)
    energy, curvature = gathered_scalars(got, 2)
    step = energy / curvature
    lane = lax.broadcasted_iota(jnp.int32, (1, LANES), 1)
    known[...] = jnp.where(lane == 0, energy, jnp.where(lane == 1, curvature, 0.0))
    energy_next = jnp.zeros(TILE, jnp.float32)
    cross = jnp.zeros(TILE, jnp.float32)
    for ex in range(2):
        for ey in range(2):
            kinds = [part(ex, kind, ey) for kind in range(3)]
            for a in range(8):
                value = direction[ex, a, ey] - step * (smoothed[ex, a, ey] + kinds[kind_of(a)])
                following[ex, a, ey] = value
                weighed = value * (inv_mult[ey] * place.inv_x(ex, a))
                was = image[ex, a, ey]
                energy_next = energy_next + weighed * (resid[ex, a, ey] - step * was)
                cross = cross + weighed * was
    slope_z[...] = along_z(following[...].reshape(256, LANES), zmat[2]).reshape(slope_z.shape)
    square = jnp.zeros(TILE, jnp.float32)
    for ex in range(2):
        for ey in range(2):
            values, images = own_operator(ctab, kap, following, slope_z, ex, ey)
            for a in range(8):
                square = square + values[a] * images[a]
    send_to_all(msg, message(place, [], [total(energy_next), total(square), total(cross)]))


def pressure_kernel(got, known, direction, following, pressure):
    energy = known[:, pl.ds(0, 1)]
    curvature = known[:, pl.ds(1, 1)]
    energy_next, square, cross = gathered_scalars(got, 3)
    ratio = energy_next / energy
    step = energy / curvature
    step_next = energy_next / (square + 2.0 * ratio * cross + ratio * ratio * curvature)
    weight_old = step + step_next * ratio
    for ex in range(2):
        for a in range(8):
            for ey in range(2):
                pressure[ex, a, ey] = (
                    weight_old * direction[ex, a, ey] + step_next * following[ex, a, ey]
                )


def coarse_energy(place, got, values, kappa, number):
    lane, row = place.lane, place.row
    for ex in range(2):
        for gx in range(8):
            own = jnp.zeros((1, LANES), jnp.float32)
            group = jnp.zeros((1, LANES), jnp.float32)
            spot = lane[0:1] // 32
            for gy in range(4):
                line = got[gx * 4 + gy, :, pl.ds(LANES, LANES)]
                own = jnp.where(spot == (gy + 2 * ex) % 4, line, own)
                group = jnp.where(spot == (gy + 1 + 2 * ex) % 4, line, group)
            kappa[ex, pl.ds(gx, 1), :] = own
            number[ex, pl.ds(gx, 1), :] = group
    grid = [jnp.zeros(TILE, jnp.float32) for _ in range(2)]
    numbers = [pltpu.roll(number[0], 96, 1), pltpu.roll(number[1], 32, 1)]
    kappa = [kappa[0], pltpu.roll(kappa[1], 64, 1)]
    for q in range(4):
        for c in range(NCD):
            mine = jnp.where(lane == row * 16 + q * 4 + c, values, 0.0)
            mine = jnp.sum(mine, axis=1, keepdims=True)
            for ex in range(2):
                chosen = (lane // 32 == q) & (numbers[ex] == float(c))
                grid[ex] = jnp.where(chosen, mine, grid[ex])

    def ends_y(v):
        low = jnp.where(lane >= 16, 0.5 * (v + pltpu.roll(v, 16, 1)), v)
        return low, v, jnp.where(lane < 112, 0.5 * (v + pltpu.roll(v, 112, 1)), v)

    def ends_z(v):
        low = jnp.where(lane % 16 > 0, 0.5 * (v + pltpu.roll(v, 1, 1)), v)
        return low, v, jnp.where(lane % 16 < 15, 0.5 * (v + pltpu.roll(v, 127, 1)), v)

    low = jnp.where(row > 0, 0.5 * (grid[0] + pltpu.roll(grid[1], 1, 0)), grid[0])
    mid = 0.5 * (grid[0] + grid[1])
    high = jnp.where(row < 7, 0.5 * (grid[1] + pltpu.roll(grid[0], 7, 0)), grid[1])
    mass = [float(WEIGHTS[0]), float(np.sum(WEIGHTS[1:7])), float(WEIGHTS[7])]
    links = (
        (0, 1, -float(np.sum(STIFF[0, 1:7]))),
        (0, 2, -float(STIFF[0, 7])),
        (1, 2, -float(np.sum(STIFF[7, 1:7]))),
    )
    energy = jnp.zeros(TILE, jnp.float32)
    for ex, line in enumerate(((low, grid[0], mid), (mid, grid[1], high))):
        nodes = [[ends_z(v) for v in ends_y(w)] for w in line]
        stiff = jnp.zeros(TILE, jnp.float32)
        square = jnp.zeros(TILE, jnp.float32)
        for i in range(3):
            for j in range(3):
                for k, l, weight in links:
                    factor = weight * mass[i] * mass[j]
                    for first, second in (
                        (nodes[k][i][j], nodes[l][i][j]),
                        (nodes[i][k][j], nodes[i][l][j]),
                        (nodes[i][j][k], nodes[i][j][l]),
                    ):
                        gap = first - second
                        stiff = stiff + (factor * gap) * gap
                for k in range(3):
                    value = nodes[i][j][k]
                    square = square + (mass[i] * mass[j] * mass[k] * value) * value
        energy = energy + kappa[ex] * stiff + sigma_p * square
    return total(energy)


def finish_kernel(
    got, grp, direction, smoothed, pressure, matrix, kappa, number
):
    place = Place()
    per = LANES // NCD
    row_lane = lax.broadcasted_iota(jnp.int32, (1, LANES), 1)
    rest = jnp.zeros((1, LANES), jnp.float32)
    dual = jnp.zeros((1, LANES), jnp.float32)
    sums = [jnp.zeros((1, LANES), jnp.float32) for _ in range(4)]
    for i in range(per):
        line = got[i, :, pl.ds(0, LANES)]
        mine = row_lane // NCD == (i + AWAY) % per
        known = row_lane // NCD == (i + BEYOND) % per
        rest = jnp.where(mine, line, rest)
        dual = dual + jnp.where(mine | known, 0.0, line)
        for c in range(4):
            sums[c] = sums[c] + jnp.where(row_lane == ((i + BEYOND) % per) * NCD + c, line, 0.0)
            block = got[i, :, pl.ds((2 + c) * LANES, LANES)]
            matrix[pl.ds(i * NCD + c, 1), :] = block
    rest = pltpu.roll(rest, (per - AWAY) * NCD, 1)
    energy, curvature, square, self_energy = [
        jnp.sum(value, axis=1, keepdims=True) for value in sums
    ]
    values = exact_dot(jnp.broadcast_to(rest, TILE), matrix[...])
    line = values[0:1]
    cross = square + jnp.sum(line * rest, axis=1, keepdims=True)
    both = self_energy + 2.0 * jnp.sum(line * dual, axis=1, keepdims=True)
    both = both + coarse_energy(place, got, values, kappa, number)
    step = energy / curvature
    energy_next = step * step * cross - energy
    ratio = energy_next / energy
    with_image = curvature - step * cross
    with_itself = curvature - 2.0 * step * cross + step * step * both
    step_next = energy_next / (
        with_itself + 2.0 * ratio * with_image + ratio * ratio * curvature
    )
    old = step + step_next * (1.0 + ratio)
    new = -step_next * step

    def solved(dx, dy, c):
        at = ((place.ix + dx - 1) * place.ny + place.iy + dy - 1) * NCD + c
        return jnp.sum(jnp.where(row_lane == at, line, 0.0), axis=1, keepdims=True)

    part = prolonged(place, masked(place, solved), grp)
    for ex in range(2):
        for ey in range(2):
            kinds = [part(ex, kind, ey) for kind in range(3)]
            for a in range(8):
                pressure[ex, a, ey] = old * direction[ex, a, ey] + new * (
                    smoothed[ex, a, ey] + kinds[kind_of(a)]
                )


def masked(place, solved):
    there_x = (place.prev_x, None, place.next_x)
    there_y = (place.prev_y, None, place.next_y)

    def value(dx, dy, c):
        out = solved(dx, dy, c)
        for there in (there_x[dx], there_y[dy]):
            if there is not None:
                out = jnp.where(there, out, 0.0)
        return out

    return value


def call(body, outs, scratch=(), **more):
    return pl.pallas_call(
        body,
        out_shape=[jax.ShapeDtypeStruct(shape, jnp.float32) for shape in outs],
        scratch_shapes=[
            pltpu.VMEM(shape, jnp.float32) if isinstance(shape, tuple) else shape
            for shape in scratch
        ],
        **more,
        compiler_params=pltpu.CompilerParams(vmem_limit_bytes=24 * 1024 * 1024),
    )


def swap(first, second, axis):
    count = lax.axis_size(axis)
    first_pairs = [(i, i ^ 1) for i in range(count)]
    second_pairs = [(i, (((i + 1) ^ 1) - 1) % count) for i in range(count)]
    if axis == "gx":
        first_pairs, second_pairs = second_pairs, first_pairs
    first_got = lax.ppermute(first, axis, first_pairs)
    return first_got, lax.ppermute(second, axis, second_pairs)


def per_device(fields, viscosity, inv_density, elem_group, coarse_inverse):
    length = fields.shape[5]
    elems_z = length // NODES
    devices = lax.axis_size("gx") * lax.axis_size("gy")
    blocks = coarse_inverse.shape[1] // LANES
    pack_rows = 1 + NCD * blocks
    tiles_np, mats_np = constant_tables(elems_z)
    ctab, zmat = jnp.asarray(tiles_np), jnp.asarray(mats_np)
    one = fields.shape[1:]
    four = fields.shape
    faces = (64, LANES)
    xf_shape = (2, 4, 2, 8, LANES)
    inner_shape = (2, 2, 8, LANES)
    y_shape, x_shape = (STEP_PACK + 3 * pack_rows, LANES), (STEP_PACK, LANES)
    turned = (64 + pack_rows, LANES)
    smooth_shape = (SMOOTH_ROWS, LANES)
    rows = (devices, 1, LANES)
    grid_fits = (
        blocks == 1
        and lax.axis_size("gx") == 8
        and lax.axis_size("gy") * fields.shape[3] * elems_z == LANES
    )

    def exchange_all(msg):
        return lax.all_to_all(msg, BOTH, 0, 0, tiled=True)

    beside = pl.CostEstimate(flops=10**7, bytes_accessed=10**6, transcendentals=0)
    summed, xf, first, second = call(
        mass_kernel,
        [four, xf_shape, faces, faces],
    )(fields)
    pack, facts = call(
        pack_kernel,
        [(pack_rows, LANES), (1, 6 * LANES)],
        cost_estimate=beside,
    )(inv_density, elem_group, coarse_inverse)
    y_got = swap(first, second, "gy")
    first, second = call(functools.partial(turn_faces_kernel, pack_rows), [turned, turned])(
        xf, pack, *y_got
    )
    side_got = x_got = swap(first, second, "gx")
    edge_shape = (4, 2, 2, 8, LANES)
    begun, given, slope, answer = call(
        prepare_kernel, [four, four, edge_shape, one], [four, four], cost_estimate=beside
    )(summed, viscosity, *y_got, ctab, zmat)
    share, xf, inner_x, first, second = call(
        functools.partial(rhs_kernel, pack_rows),
        [four, xf_shape, inner_shape, y_shape, y_shape],
        [edge_shape, edge_shape, edge_shape, edge_shape],
    )(begun, given, slope, answer, viscosity, pack, *x_got, ctab, zmat)
    y_got = swap(first, second, "gy")
    first, second = call(turn_step_kernel, [x_shape, x_shape])(xf, inner_x, *y_got)
    x_got = swap(first, second, "gx")
    inv_diag, kap, grp, coarse = call(
        functools.partial(setup_kernel, pack_rows, blocks),
        [one, (16, LANES), (16, LANES), (9 * NCD * blocks, LANES)],
        [(16, LANES), (8, 16, LANES)],
        cost_estimate=beside,
    )(pack, *side_got, *y_got, ctab)
    begun, given = call(approach_kernel, [four, one], [one], cost_estimate=beside)(
        share, *y_got, ctab, zmat
    )
    side_shape = (2, 2, 8, LANES)
    fields_got = x_got
    fields_begun = begun
    resid, own, msg = call(
        advance_kernel,
        [one, one, (devices, 8, LANES)],
        [one, one, side_shape, one, (3,) + side_shape],
    )(begun, given, *y_got, *x_got, inv_diag, kap, grp, ctab, zmat)
    got = exchange_all(msg)
    (relayed,) = call(relay_kernel, [(RELAY_ROWS, LANES)])(got, own)
    relayed = lax.ppermute(
        relayed, "gy", [(i, i ^ 1) for i in range(lax.axis_size("gy")) if i ^ 1 < lax.axis_size("gy")]
    )
    direction, own, inner_x, first, second, extra = call(
        functools.partial(first_direction_kernel, blocks),
        [one, one, inner_shape, smooth_shape, smooth_shape, (1, LANES)],
        [one, one],
    )(got, relayed, coarse, grp, kap, inv_diag, resid, own, ctab, zmat)
    y_got = swap(first, second, "gy")
    first, second = call(turn_smooth_kernel, [smooth_shape, smooth_shape])(own, inner_x, *y_got)
    x_got = swap(first, second, "gx")
    fields_new, extra = call(emit_kernel, [four, (1, LANES)], cost_estimate=beside)(
        fields_begun, *fields_got, extra
    )
    begun, begun_scaled, given = call(
        ready_kernel, [one, one, one], [one], cost_estimate=beside
    )(own, *y_got, inv_diag, kap, ctab, zmat)
    image, image_smoothed, msg = call(
        smooth_kernel,
        [one, one, (devices, 1, 6 * LANES) if grid_fits else rows],
        [one, one, side_shape],
    )(
        begun, begun_scaled, given, *y_got, *x_got, inv_diag, kap, grp, extra, facts, ctab, zmat
    )
    got = exchange_all(msg)
    if grid_fits:
        (pressure,) = call(
            finish_kernel, [one], [(LANES, LANES), (2,) + TILE, (2,) + TILE]
        )(got, grp, direction, image_smoothed)
        return (fields_new, pressure)
    following, known, msg = call(
        functools.partial(second_direction_kernel, blocks), [one, (1, LANES), rows], [one]
    )(got, coarse, grp, kap, resid, direction, image, image_smoothed, ctab, zmat)
    got = exchange_all(msg)
    (pressure,) = call(pressure_kernel, [one])(got, known, direction, following)
    return (fields_new, pressure)


def solution(mesh):
    placed = (
        P(None, "gx", None, "gy", None, None),
        P("gx", None, "gy", None, None),
        P("gx", "gy", None),
        P("gx", "gy", None),
        P(("gx", "gy"), None),
    )
    return jax.shard_map(
        per_device,
        mesh=mesh,
        in_specs=placed,
        out_specs=(P(None, "gx", None, "gy", None, None), P("gx", None, "gy", None, None)),
        check_vma=False,
    )
```

```python
import functools

import jax
import jax.numpy as jnp
import ml_dtypes
import numpy as np
from jax import lax
from jax.experimental import pallas as pl
from jax.experimental.pallas import tpu as pltpu
from jax.sharding import PartitionSpec as P

NCD = 4
NODES = 8
LANES = 128
TILE = (8, 128)
BOTH = ("gx", "gy")

dt_step = 0.01
sigma_p = 4.0
prandtl = 0.7
cheb_ratio = 0.1


def tables():
    points = np.array(
        [
            -1.0,
            -0.8717401485096066,
            -0.5917001814331423,
            -0.2092992179024789,
            0.2092992179024789,
            0.5917001814331423,
            0.8717401485096066,
            1.0,
        ]
    )
    weights = np.array(
        [
            1.0 / 28.0,
            0.2107042271435061,
            0.3411226924835044,
            0.4124587946587038,
            0.4124587946587038,
            0.3411226924835044,
            0.2107042271435061,
            1.0 / 28.0,
        ]
    )
    identity = np.eye(8)
    differ = points[:, None] - points[None, :] + identity
    barycentric = 1.0 / np.prod(differ, axis=1)
    offdiag = barycentric[None, :] / barycentric[:, None] / differ * (1.0 - identity)
    derivative = offdiag - identity * np.sum(offdiag, axis=1)[:, None]
    mass_one = identity * weights[None, :]
    stiff_one = derivative.T @ mass_one @ derivative
    stiff_three = (
        np.kron(np.kron(stiff_one, mass_one), mass_one)
        + np.kron(np.kron(mass_one, stiff_one), mass_one)
        + np.kron(np.kron(mass_one, mass_one), stiff_one)
    )
    three_diag = np.sum(stiff_three * np.eye(512), axis=1)
    spectral_bound = float(np.max(np.sum(np.abs(stiff_three), axis=1) / three_diag))
    return (derivative, weights, stiff_one, spectral_bound)


DERIV, WEIGHTS, STIFF, BOUND = tables()
SCALED = STIFF / WEIGHTS[:, None]
LINE = np.diag(STIFF) / WEIGHTS
THETA = 0.5 * (BOUND + cheb_ratio * BOUND)
DELTA = 0.5 * (BOUND - cheb_ratio * BOUND)
RHO = DELTA / THETA
RHO_NEXT = 1.0 / (2.0 * THETA / DELTA - RHO)


def constant_tables(elems_z):
    def turned(matrix):
        rows = np.arange(8)
        return [np.repeat(matrix[rows, (rows - s) % 8][:, None], LANES, 1) for s in range(8)]

    wz = np.tile(WEIGHTS, elems_z)
    kz = np.tile(LINE, elems_z)
    tiles = turned(DERIV) + turned(DERIV.T) + turned(SCALED)
    tiles += [WEIGHTS[:, None] * wz[None, :], LINE[:, None] + kz[None, :]]
    for matrix in (DERIV, SCALED):
        for node in (7, 0):
            inner = matrix[node] * (np.arange(8) != node)
            tiles.append(np.repeat(inner[:, None], LANES, 1))
    eye = np.eye(elems_z)
    mats = [np.kron(eye, DERIV.T), np.kron(eye, DERIV), np.kron(eye, SCALED.T)]
    halves = []
    for mat in mats:
        high = mat.astype(ml_dtypes.bfloat16)
        low = (mat - high.astype(np.float64)).astype(ml_dtypes.bfloat16)
        both = np.concatenate([high, low], 1)
        halves.append(np.concatenate([both, both], 0))
    return np.stack(tiles).astype(np.float32), np.stack(halves)


T_D, T_DT, T_K, T_W, T_LINE = 0, 8, 16, 24, 25
T_TOP, T_BOTTOM, T_KTOP, T_KBOTTOM = 26, 27, 28, 29


class Place:
    def __init__(self):
        self.ix = lax.axis_index("gx")
        self.iy = lax.axis_index("gy")
        self.nx = lax.axis_size("gx")
        self.ny = lax.axis_size("gy")
        self.even_x = self.ix % 2 == 0
        self.even_y = self.iy % 2 == 0
        self.row = lax.broadcasted_iota(jnp.int32, TILE, 0)
        self.lane = lax.broadcasted_iota(jnp.int32, TILE, 1)
        self.low_z = (self.lane % 8 == 0) & (self.lane > 0)
        self.high_z = (self.lane % 8 == 7) & (self.lane < LANES - 1)
        self.prev_x = self.ix > 0
        self.next_x = self.ix < self.nx - 1
        self.prev_y = self.iy > 0
        self.next_y = self.iy < self.ny - 1

    def mult_tile(self, ey):
        along_z = 1.0 + jnp.where(self.low_z | self.high_z, 1.0, 0.0)
        low = 1.0 if ey == 1 else jnp.where(self.prev_y, 1.0, 0.0)
        high = 1.0 if ey == 0 else jnp.where(self.next_y, 1.0, 0.0)
        along_y = 1.0 + jnp.where(self.row == 0, low, jnp.where(self.row == 7, high, 0.0))
        return along_y * along_z

    def inv_x(self, ex, a):
        if a == 0:
            return 0.5 if ex == 1 else jnp.where(self.prev_x, 0.5, 1.0)
        if a == 7:
            return 0.5 if ex == 0 else jnp.where(self.next_x, 0.5, 1.0)
        return 1.0

    def mult_x(self, ex, a):
        if a == 0:
            return 2.0 if ex == 1 else jnp.where(self.prev_x, 2.0, 1.0)
        if a == 7:
            return 2.0 if ex == 0 else jnp.where(self.next_x, 2.0, 1.0)
        return 1.0

    def share_x(self, ex, a):
        if (ex, a) == (0, 0):
            return jnp.where(self.prev_x, 0.5, 1.0)
        if (ex, a) == (1, 7):
            return jnp.where(self.next_x, 0.5, 1.0)
        return 1.0

    def share_y(self, ey):
        if ey == 0:
            return jnp.where((self.row == 0) & self.prev_y, 0.5, 1.0)
        return jnp.where((self.row == 7) & self.next_y, 0.5, 1.0)

    def inv_y(self, ey):
        low = 0.5 if ey == 1 else jnp.where(self.prev_y, 0.5, 1.0)
        high = 0.5 if ey == 0 else jnp.where(self.next_y, 0.5, 1.0)
        return jnp.where(self.row == 0, low, jnp.where(self.row == 7, high, 1.0))

    def inv_z(self):
        return jnp.where(self.low_z | self.high_z, 0.5, 1.0)

    def join_z(self, t):
        up = pltpu.roll(t, LANES - 1, 1)
        down = pltpu.roll(t, 1, 1)
        return t + jnp.where(self.high_z, up, jnp.where(self.low_z, down, 0.0))

    def to_low(self, below):
        return jnp.where(self.row == 0, pltpu.roll(below, 1, 0), 0.0)

    def to_high(self, above):
        return jnp.where(self.row == 7, pltpu.roll(above, 7, 0), 0.0)

    def join_y(self, below, above):
        return below + self.to_high(above), above + self.to_low(below)

    def before_x(self, first, second):
        return jnp.where(self.prev_x, jnp.where(self.even_x, first, second), 0.0)

    def after_x(self, first, second):
        return jnp.where(self.next_x, jnp.where(self.even_x, second, first), 0.0)

    def send_x(self, first, second):
        return jnp.where(self.even_x, second, first)

    def before_y(self, first, second):
        return jnp.where(self.prev_y, jnp.where(self.even_y, second, first), 0.0)

    def after_y(self, first, second):
        return jnp.where(self.next_y, jnp.where(self.even_y, first, second), 0.0)

    def send_y(self, first, second):
        return jnp.where(self.even_y, first, second)


def along_x(matrix, tiles, sign):
    even = [tiles[a] + tiles[7 - a] for a in range(4)]
    odd = [tiles[a] - tiles[7 - a] for a in range(4)]
    out = [None] * 8
    for i in range(4):
        plus, minus = None, None
        for a in range(4):
            p = float(0.5 * (matrix[i, a] + matrix[i, 7 - a])) * even[a]
            m = float(0.5 * (matrix[i, a] - matrix[i, 7 - a])) * odd[a]
            plus = p if plus is None else plus + p
            minus = m if minus is None else minus + m
        out[i] = plus + minus
        out[7 - i] = minus - plus if sign < 0 else plus - minus
    return out


def along_y(ctab, base, tile):
    acc = ctab[base] * tile
    for s in range(1, 8):
        acc = acc + ctab[base + s] * pltpu.roll(tile, s, 0)
    return acc


def exact_dot(rows, matrix):
    return jnp.dot(
        rows, matrix, precision=lax.Precision.HIGHEST, preferred_element_type=jnp.float32
    )


def along_z(rows, matrix):
    high = rows.astype(jnp.bfloat16)
    low = (rows - high.astype(jnp.float32)).astype(jnp.bfloat16)
    both = jnp.dot(
        jnp.concatenate([high, low], axis=1), matrix, preferred_element_type=jnp.float32
    )
    return both[:, :LANES] + both[:, LANES:]


def total(tile):
    return jnp.sum(jnp.sum(tile, axis=0, keepdims=True), axis=1, keepdims=True)


def store_y_faces(place, field, first_out, second_out, lead, at):
    for ex in range(2):
        for a in range(8):
            low = field[lead + (ex, a, 0, pl.ds(0, 1), slice(None))]
            high = field[lead + (ex, a, 1, pl.ds(7, 1), slice(None))]
            row = at + ex * 8 + a
            first_out[pl.ds(row, 1), :] = place.send_y(high, low)
            second_out[pl.ds(row, 1), :] = place.send_y(low, high)


def join_own(place, tiles):
    for ex in range(2):
        for a in range(8):
            tiles[ex][a] = list(place.join_y(*tiles[ex][a]))
    for ey in range(2):
        both = tiles[0][7][ey] + tiles[1][0][ey]
        tiles[0][7][ey] = both
        tiles[1][0][ey] = both


def weight_of(node):
    edge = jnp.minimum(node, 7 - node)
    value = jnp.where(edge == 2, float(WEIGHTS[2]), float(WEIGHTS[3]))
    return jnp.where(
        edge == 0, float(WEIGHTS[0]), jnp.where(edge == 1, float(WEIGHTS[1]), value)
    )


def mass_kernel(fields, out, xf, first, second):
    place = Place()
    weight = weight_of(place.row) * weight_of(place.lane % NODES)
    for ch in range(4):
        tiles = [
            [
                [
                    place.join_z(fields[ch, ex, a, ey] * (float(WEIGHTS[a]) * weight))
                    for ey in range(2)
                ]
                for a in range(8)
            ]
            for ex in range(2)
        ]
        join_own(place, tiles)
        for ex in range(2):
            for a in range(8):
                for ey in range(2):
                    out[ch, ex, a, ey] = tiles[ex][a][ey]
        for ey in range(2):
            xf[0, ch, ey] = tiles[0][0][ey]
            xf[1, ch, ey] = tiles[1][7][ey]
        store_y_faces(place, out, first, second, (ch,), ch * 16)


def turn_faces(place, xf, y_first, y_second, first, second):
    for ch in range(4):
        sides = []
        for side in range(2):
            row = pl.ds(ch * 16 + 15 * side, 1)
            got_a, got_b = y_first[row, :], y_second[row, :]
            low = xf[side, ch, 0] + jnp.where(place.row == 0, place.before_y(got_a, got_b), 0.0)
            high = xf[side, ch, 1] + jnp.where(place.row == 7, place.after_y(got_a, got_b), 0.0)
            sides.append((low, high))
        for ey in range(2):
            rows = pl.ds(ch * 16 + ey * 8, 8)
            first[rows, :] = place.send_x(sides[1][ey], sides[0][ey])
            second[rows, :] = place.send_x(sides[0][ey], sides[1][ey])


def turn_faces_kernel(pack_rows, xf, pack, y_first, y_second, first, second):
    turn_faces(Place(), xf, y_first, y_second, first, second)
    first[pl.ds(64, pack_rows), :] = pack[...]
    second[pl.ds(64, pack_rows), :] = pack[...]


def turn_edges(place, inner_x, y_first, y_second, first, second, at, edge, inner_y):
    sides = []
    for side in range(2):
        row = pl.ds(edge + side, 1)
        got_a, got_b = y_first[row, :], y_second[row, :]
        low = inner_x[side, 0] + jnp.where(place.row == 0, place.before_y(got_a, got_b), 0.0)
        high = inner_x[side, 1] + jnp.where(place.row == 7, place.after_y(got_a, got_b), 0.0)
        sides.append((low, high))
    for ey in range(2):
        rows = pl.ds(at + ey * 8, 8)
        first[rows, :] = place.send_x(sides[1][ey], sides[0][ey])
        second[rows, :] = place.send_x(sides[0][ey], sides[1][ey])
    for k, pick in enumerate((place.before_y, place.after_y)):
        sides = []
        for side in range(2):
            row = pl.ds(inner_y + 15 * side, 1)
            sides.append(pick(y_first[row, :], y_second[row, :]))
        row = pl.ds(edge + k, 1)
        first[row, :] = place.send_x(sides[1], sides[0])
        second[row, :] = place.send_x(sides[0], sides[1])


STEP_U, STEP_V, STEP_EDGE, STEP_PACK = 64, 64, 80, 82


def turn_step_kernel(xf, inner_x, y_first, y_second, first, second):
    place = Place()
    turn_faces(place, xf, y_first, y_second, first, second)
    turn_edges(place, inner_x, y_first, y_second, first, second, STEP_U, STEP_EDGE, STEP_V)


def setup_kernel(
    pack_rows,
    blocks,
    pack,
    x_first,
    x_second,
    y_first,
    y_second,
    ctab,
    inv_diag,
    kap,
    grp,
    coarse,
    compact,
    spread,
):
    place = Place()
    beside = pl.ds(64, pack_rows)
    packs = [[None] * 3 for _ in range(3)]
    packs[0][1] = place.before_x(x_first[beside, :], x_second[beside, :])
    packs[1][1] = pack[...]
    packs[2][1] = place.after_x(x_first[beside, :], x_second[beside, :])
    for dx in range(3):
        rows = pl.ds(STEP_PACK + dx * pack_rows, pack_rows)
        packs[dx][0] = place.before_y(y_first[rows, :], y_second[rows, :])
        packs[dx][2] = place.after_y(y_first[rows, :], y_second[rows, :])
    compact[...] = jnp.zeros(compact.shape, jnp.float32)
    for dx in range(3):
        for dy in range(3):
            at = (dx * 3 + dy) * NCD * blocks
            coarse[pl.ds(at, NCD * blocks), :] = packs[dx][dy][1 : 1 + NCD * blocks]
            compact[pl.ds(dx * 3 + dy, 1), :] = packs[dx][dy][0:1]
    elems = LANES // NODES
    lane = lax.broadcasted_iota(jnp.int32, (LANES, LANES), 1)
    source = lax.broadcasted_iota(jnp.int32, (LANES, LANES), 0)
    for k in range(8):
        spot = (source == k * elems + lane // NODES).astype(jnp.float32)
        spread[k] = exact_dot(compact[...], spot)
    there_x = [jnp.where(place.prev_x, 1.0, 0.0), 1.0, jnp.where(place.next_x, 1.0, 0.0)]
    there_y = [jnp.where(place.prev_y, 1.0, 0.0), 1.0, jnp.where(place.next_y, 1.0, 0.0)]

    def element_row(base, u, v):
        device = (u // 2) * 3 + v // 2
        return spread[base + (u % 2) * 2 + v % 2, pl.ds(device, 1), :]

    for x in range(4):
        for y in range(4):
            kap[pl.ds(x * 4 + y, 1), :] = element_row(0, x + 1, y + 1)
            grp[pl.ds(x * 4 + y, 1), :] = element_row(4, x + 1, y + 1)
    kappa = [
        [
            place.join_z(jnp.broadcast_to(element_row(0, u + 1, v + 1), TILE))
            for v in range(4)
        ]
        for u in range(4)
    ]
    count_z = 1.0 + jnp.where(place.low_z | place.high_z, 1.0, 0.0)
    weight = ctab[T_W]
    line = ctab[T_LINE]

    def pick(values, ey):
        low = values[ey] + values[ey + 1]
        high = values[ey + 1] + values[ey + 2]
        return jnp.where(place.row == 0, low, jnp.where(place.row == 7, high, values[ey + 1]))

    for ex in range(2):
        for kind in range(3):
            us = {0: (ex, ex + 1), 1: (ex + 1,), 2: (ex + 1, ex + 2)}[kind]
            sums, counts = [], []
            for v in range(4):
                acc, num = None, 0.0
                for u in us:
                    acc = kappa[u][v] if acc is None else acc + kappa[u][v]
                    num = num + there_x[(u + 1) // 2]
                sums.append(acc)
                counts.append(num * there_y[(v + 1) // 2])
            for ey in range(2):
                kappa_sum = pick(sums, ey)
                mult = pick(counts, ey) * count_z
                for a in {0: (0,), 1: range(1, 7), 2: (7,)}[kind]:
                    diag = (float(LINE[a]) + line) * kappa_sum + sigma_p * mult
                    inv_diag[ex, a, ey] = 1.0 / (diag * (float(WEIGHTS[a]) * weight))


OUTER = ((0, 0), (1, 7))


def got_y_sum(place, tile, ch, ex, a, ey, y_first, y_second):
    row = pl.ds(ch * 16 + ex * 8 + a, 1)
    got_a, got_b = y_first[row, :], y_second[row, :]
    if ey == 0:
        tile = tile + jnp.where(place.row == 0, place.before_y(got_a, got_b), 0.0)
    else:
        tile = tile + jnp.where(place.row == 7, place.after_y(got_a, got_b), 0.0)
    return tile


def got_x_sum(place, tile, ch, ex, ey, x_first, x_second):
    rows = pl.ds(ch * 16 + ey * 8, 8)
    pick = place.before_x if ex == 0 else place.after_x
    return tile + pick(x_first[rows, :], x_second[rows, :])


def pack_kernel(kappa, group, coarse, pack, facts):
    place = Place()
    facts[...] = jnp.zeros(facts.shape, jnp.float32)
    grid = jnp.zeros((1, LANES), jnp.float32)
    elems = kappa.shape[2]
    to = lax.broadcasted_iota(jnp.int32, (elems, LANES), 1)
    element = lax.broadcasted_iota(jnp.int32, (elems, LANES), 0)
    blocks = coarse.shape[1] // LANES
    packed = jnp.zeros((1, LANES), jnp.float32)
    for ex in range(2):
        numbers = group[ex].astype(jnp.float32)
        for ey in range(2):
            mine, number = kappa[ex, pl.ds(ey, 1), :], numbers[ey : ey + 1]
            at = (2 * ex + ey) * elems
            packed = packed + exact_dot(mine, (to == at + element).astype(jnp.float32))
            at = at + 4 * elems
            packed = packed + exact_dot(number, (to == at + element).astype(jnp.float32))
            at = ((2 * place.iy + ey) * elems + 4 * ex * elems) % LANES
            grid = grid + exact_dot(mine, (to == at + element).astype(jnp.float32))
            at = (at + 2 * elems) % LANES
            grid = grid + exact_dot(number, (to == at + element).astype(jnp.float32))
    pack[pl.ds(0, 1), :] = packed
    for c in range(NCD):
        for j in range(blocks):
            line = coarse[pl.ds(c, 1), pl.ds(j * LANES, LANES)]
            pack[pl.ds(1 + c * blocks + j, 1), :] = line
        facts[:, pl.ds((2 + c) * LANES, LANES)] = coarse[pl.ds(c, 1), pl.ds(0, LANES)]
    facts[:, pl.ds(LANES, LANES)] = grid


def prepare_kernel(
    summed, visc, y_first, y_second, ctab, zmat, start, part, slope, answer, grad_z, flux_z
):
    place = Place()
    weight = ctab[T_W]
    inv_mass = [1.0 / (weight * place.mult_tile(ey)) for ey in range(2)]

    def begin(ch, carry):
        for ex in range(2):
            for a in range(8):
                for ey in range(2):
                    tile = got_y_sum(
                        place, summed[ch, ex, a, ey], ch, ex, a, ey, y_first, y_second
                    )
                    scale = place.inv_x(ex, a) * float(1.0 / WEIGHTS[a])
                    start[ch, ex, a, ey] = tile * (inv_mass[ey] * scale)
        return carry

    lax.fori_loop(0, 4, begin, 0)
    grad_z[...] = along_z(start[...].reshape(1024, LANES), zmat[0]).reshape(grad_z.shape)

    def column(index, carry):
        ch, ey = index // 2, index % 2
        coef = jnp.where(ch == 3, 1.0 / prandtl, 1.0)
        for ex in range(2):
            grad_x = along_x(DERIV, [start[ch, ex, a, ey] for a in range(8)], -1)
            flux_x = [
                visc[ex, a, ey] * (float(WEIGHTS[a]) * weight) * coef * grad_x[a]
                for a in range(8)
            ]
            back = along_x(DERIV.T, flux_x, -1)
            for a in range(8):
                if (ex, a) in OUTER:
                    slope[ch, ex, ey] = grad_x[a]
                    part[ch, ex, a, ey] = back[a]
                    continue
                rest, flux_z[ch, ex, a, ey] = across(
                    ctab, weight, a, coef, start[ch, ex, a, ey], grad_z[ch, ex, a, ey],
                    start[1, ex, a, ey], start[2, ex, a, ey], visc[ex, a, ey],
                )
                flow = float(WEIGHTS[a]) * weight * start[0, ex, a, ey]
                part[ch, ex, a, ey] = rest + flow * grad_x[a] + back[a]
        return carry

    for ex, outer in OUTER:
        for ey in range(2):
            flux_x = [
                visc[ex, a, ey] * (float(WEIGHTS[a] * DERIV[a, outer]) * weight) for a in range(8)
            ]
            back = along_x(DERIV.T, flux_x, -1)
            for a in range(8):
                answer[ex, a, ey] = back[a]
    lax.fori_loop(0, 8, column, 0)
    for ch in range(4):
        for ex in range(2):
            inner = pl.ds(1 - ex, 7)
            back = along_z(flux_z[ch, ex, inner].reshape(112, LANES), zmat[1])
            part[ch, ex, inner] = part[ch, ex, inner] + back.reshape(7, 2, 8, LANES)


def across(ctab, weight, a, coef, value, grad_z, flow_y, flow_z, visc):
    node = float(WEIGHTS[a]) * weight
    grad_y = along_y(ctab, T_D, value)
    nu = visc * node * coef
    part = node * (flow_y * grad_y + flow_z * grad_z) + along_y(ctab, T_DT, nu * grad_y)
    return part, nu * grad_z


def rhs_kernel(
    pack_rows,
    begun,
    given,
    slope,
    answer,
    visc,
    pack,
    x_first,
    x_second,
    ctab,
    zmat,
    share,
    xf,
    inner_x,
    first,
    second,
    edge,
    edge_z,
    edge_part,
    came,
):
    place = Place()
    weight = ctab[T_W]
    inv_mass = [1.0 / (weight * place.mult_tile(ey)) for ey in range(2)]
    for ch in range(4):
        for side, (ex, a) in enumerate(OUTER):
            scale = place.inv_x(ex, a) * float(1.0 / WEIGHTS[a])
            for ey in range(2):
                zero = jnp.zeros(TILE, jnp.float32)
                extra = got_x_sum(place, zero, ch, ex, ey, x_first, x_second)
                extra = extra * (inv_mass[ey] * scale)
                came[ch, side, ey] = extra
                edge[ch, side, ey] = begun[ch, ex, a, ey] + extra
    edge_z[...] = along_z(edge[...].reshape(128, LANES), zmat[0]).reshape(edge.shape)
    for ch in range(4):
        coef = 1.0 / prandtl if ch == 3 else 1.0
        for side, (ex, a) in enumerate(OUTER):
            for ey in range(2):
                parts = across(
                    ctab, weight, a, coef, edge[ch, side, ey], edge_z[ch, side, ey],
                    edge[1, side, ey], edge[2, side, ey], visc[ex, a, ey],
                )
                edge_part[ch, side, ey], edge_z[ch, side, ey] = parts
    edge_part[...] = edge_part[...] + along_z(
        edge_z[...].reshape(128, LANES), zmat[1]
    ).reshape(edge.shape)

    def side_of(ch, ex, a, ey):
        outer = OUTER[ex][1]
        coef = jnp.where(ch == 3, 1.0 / prandtl, 1.0)
        extra = came[ch, ex, ey]
        node = float(WEIGHTS[a]) * weight
        turn = float(DERIV[a, outer])
        if a == outer:
            known = given[ch, ex, a, ey] + edge_part[ch, ex, ey]
            known = known + node * edge[0, ex, ey] * (slope[ch, ex, ey] + turn * extra)
            return known + extra * (coef * answer[ex, a, ey])
        flow = float(WEIGHTS[a] * turn) * weight * begun[0, ex, a, ey]
        return given[ch, ex, a, ey] + extra * (coef * answer[ex, a, ey] + flow)

    def finish(ch, carry):
        tiles = [
            [[place.join_z(-side_of(ch, ex, a, ey)) for ey in range(2)] for a in range(8)]
            for ex in range(2)
        ]
        join_own(place, tiles)
        for ex in range(2):
            for a in range(8):
                scale = place.inv_x(ex, a) * float(dt_step / WEIGHTS[a])
                for ey in range(2):
                    value = edge[ch, ex, ey] if (ex, a) in OUTER else begun[ch, ex, a, ey]
                    part = value * (place.share_y(ey) * place.share_x(ex, a))
                    share[ch, ex, a, ey] = part + tiles[ex][a][ey] * (inv_mass[ey] * scale)
        return carry

    lax.fori_loop(0, 4, finish, 0)
    for ch in range(4):
        store_y_faces(place, share, first, second, (ch,), ch * 16)
        for ey in range(2):
            xf[0, ch, ey] = share[ch, 0, 0, ey]
            xf[1, ch, ey] = share[ch, 1, 7, ey]

    def column_of(ex, ey):
        return [share[0, ex, a, ey] for a in range(8)]

    def tile_of(ex, a, ey):
        return share[1, ex, a, ey]

    store_inner(
        place, DERIV, ctab[T_BOTTOM], ctab[T_TOP], column_of, tile_of, inner_x, first, second,
        STEP_V, STEP_EDGE,
    )
    beside = pl.ds(64, pack_rows)
    parts = (
        place.before_x(x_first[beside, :], x_second[beside, :]),
        pack[...],
        place.after_x(x_first[beside, :], x_second[beside, :]),
    )
    for k in range(3):
        rows = pl.ds(STEP_PACK + k * pack_rows, pack_rows)
        first[rows, :] = parts[k]
        second[rows, :] = parts[k]


def store_inner(
    place, matrix, bottom, top, column_of, tile_of, inner_x, first, second, at, edge
):
    for ey in range(2):
        low, high = column_of(0, ey), column_of(1, ey)
        below = float(matrix[0, 1]) * low[1]
        above = float(matrix[7, 0]) * high[0]
        for k in range(2, 8):
            below = below + float(matrix[0, k]) * low[k]
            above = above + float(matrix[7, k - 1]) * high[k - 1]
        inner_x[0, ey] = below
        inner_x[1, ey] = above
    for side in range(2):
        low = inner_x[side, 0, pl.ds(0, 1), :]
        high = inner_x[side, 1, pl.ds(7, 1), :]
        first[pl.ds(edge + side, 1), :] = place.send_y(high, low)
        second[pl.ds(edge + side, 1), :] = place.send_y(low, high)
    for ex in range(2):
        for a in range(8):
            low = jnp.sum(bottom * tile_of(ex, a, 0), axis=0, keepdims=True)
            high = jnp.sum(top * tile_of(ex, a, 1), axis=0, keepdims=True)
            row = pl.ds(at + ex * 8 + a, 1)
            first[row, :] = place.send_y(high, low)
            second[row, :] = place.send_y(low, high)


def cross_flow(place, ctab, flow, slopes, rows, inv_y, inv_z):
    below, above = rows
    below = (below - float(DERIV[0, 0]) * flow[0]) * jnp.where(place.prev_y, 1.0, 0.0)
    above = (above - float(DERIV[7, 7]) * flow[1]) * jnp.where(place.next_y, 1.0, 0.0)
    grad_y = list(place.join_y(*[along_y(ctab, T_D, tile) for tile in flow]))
    grad_y[0] = grad_y[0] + jnp.where(place.row == 0, below, 0.0)
    grad_y[1] = grad_y[1] + jnp.where(place.row == 7, above, 0.0)
    return [grad_y[ey] * inv_y[ey] + place.join_z(slopes[ey]) * inv_z for ey in range(2)]


def approach_kernel(share, y_first, y_second, ctab, zmat, fields_new, part, grad_z):
    place = Place()

    def step(ch, carry):
        for ex in range(2):
            for a in range(8):
                for ey in range(2):
                    fields_new[ch, ex, a, ey] = got_y_sum(
                        place, share[ch, ex, a, ey], ch, ex, a, ey, y_first, y_second
                    )
        return carry

    lax.fori_loop(0, 4, step, 0)
    grad_z[...] = along_z(fields_new[2].reshape(256, LANES), zmat[0]).reshape(grad_z.shape)
    inv_y = [place.inv_y(ey) for ey in range(2)]
    inv_z = place.inv_z()
    for ex in range(2):
        for a in range(8):
            if (ex, a) in OUTER:
                continue
            flow = [fields_new[1, ex, a, ey] for ey in range(2)]
            rows = inner_along_y(place, y_first, y_second, None, None, ex, a, STEP_V, STEP_EDGE)
            slopes = [grad_z[ex, a, ey] for ey in range(2)]
            both = cross_flow(place, ctab, flow, slopes, rows, inv_y, inv_z)
            part[ex, a, 0], part[ex, a, 1] = both


def emit_kernel(begun, x_first, x_second, extra, fields_new, passed):
    place = Place()
    passed[...] = extra[...]
    fields_new[...] = begun[...]
    for ch in range(4):
        for ex, a in OUTER:
            for ey in range(2):
                fields_new[ch, ex, a, ey] = got_x_sum(
                    place, begun[ch, ex, a, ey], ch, ex, ey, x_first, x_second
                )


def advance_kernel(
    begun,
    given,
    y_first,
    y_second,
    x_first,
    x_second,
    inv_diag,
    kap,
    grp,
    ctab,
    zmat,
    resid,
    own,
    msg,
    grad_z,
    scaled,
    edge,
    part,
    outer,
):
    place = Place()
    weight = ctab[T_W]

    def before(row, count=8):
        rows = pl.ds(row, count)
        return place.before_x(x_first[rows, :], x_second[rows, :])

    def after(row, count=8):
        rows = pl.ds(row, count)
        return place.after_x(x_first[rows, :], x_second[rows, :])

    part[...] = given[...]
    for ch in range(3):
        for side, (ex, a) in enumerate(OUTER):
            for ey in range(2):
                outer[ch, side, ey] = got_x_sum(
                    place, begun[ch, ex, a, ey], ch, ex, ey, x_first, x_second
                )
    edge[...] = along_z(outer[2].reshape(32, LANES), zmat[0]).reshape(edge.shape)
    inv_y = [place.inv_y(ey) for ey in range(2)]
    inv_z = place.inv_z()
    for side, (ex, a) in enumerate(OUTER):
        flow = [outer[1, side, ey] for ey in range(2)]
        rows = inner_along_y(place, y_first, y_second, before, after, ex, a, STEP_V, STEP_EDGE)
        slopes = [edge[side, ey] for ey in range(2)]
        both = cross_flow(place, ctab, flow, slopes, rows, inv_y, inv_z)
        part[ex, a, 0], part[ex, a, 1] = both
    slope = [[None, None], [None, None]]
    for ey in range(2):
        for ex in range(2):
            line = [
                outer[0, ex, ey] if (ex, a) in OUTER else begun[0, ex, a, ey] for a in range(8)
            ]
            slope[ex][ey] = along_x(DERIV, line, -1)
        mid = 0.5 * (slope[0][ey][7] + slope[1][ey][0])
        slope[0][ey][7] = mid
        slope[1][ey][0] = mid
        low, high = slope[0][ey][0], slope[1][ey][7]
        inner_low = low - float(DERIV[0, 0]) * outer[0, 0, ey] + before(STEP_U + ey * 8)
        inner_high = high - float(DERIV[7, 7]) * outer[0, 1, ey] + after(STEP_U + ey * 8)
        slope[0][ey][0] = jnp.where(place.prev_x, 0.5 * inner_low, low)
        slope[1][ey][7] = jnp.where(place.next_x, 0.5 * inner_high, high)
    sums = [[jnp.zeros(TILE, jnp.float32) for _ in range(2)] for _ in range(2)]
    inv_mult = [1.0 / place.mult_tile(ey) for ey in range(2)]
    mass = [weight * place.mult_tile(ey) for ey in range(2)]
    for ex in range(2):
        for a in range(8):
            for ey in range(2):
                div = slope[ex][ey][a] + part[ex, a, ey]
                value = div * (mass[ey] * (place.mult_x(ex, a) * float(-WEIGHTS[a])))
                resid[ex, a, ey] = value
                scaled[ex, a, ey] = value * inv_diag[ex, a, ey] * float(1.0 / THETA)
                sums[ex][ey] = sums[ex][ey] + value * (inv_mult[ey] * place.inv_x(ex, a))
    grad_z[...] = along_z(scaled[...].reshape(256, LANES), zmat[2]).reshape(grad_z.shape)
    tiles = [[[None, None] for _ in range(8)] for _ in range(2)]
    for ex in range(2):
        for ey in range(2):
            images = own_operator(ctab, kap, scaled, grad_z, ex, ey)[1]
            for a in range(8):
                tiles[ex][a][ey] = place.join_z(images[a])
    join_own(place, tiles)
    for ex in range(2):
        for a in range(8):
            for ey in range(2):
                own[ex, a, ey] = tiles[ex][a][ey]
    row = message(place, restricted(place, sums, grp), [])
    blank = jnp.where(place.row == 0, jnp.broadcast_to(row, TILE), 0.0)

    def clear(i, carry):
        msg[i] = blank
        return carry

    lax.fori_loop(0, msg.shape[0], clear, 0, unroll=msg.shape[0] <= 64)
    across = Pairing(place)
    for side, (ex, a) in enumerate(OUTER):
        there, ix = across.beside(side)

        @pl.when(there)
        def _():
            msg[ix * place.ny + place.iy] = own[ex, a, 0]
            msg[ix * place.ny + across.twin, pl.ds(1, 7), :] = own[ex, a, 1, pl.ds(1, 7), :]

        @pl.when(there & across.has_far)
        def _():
            msg[ix * place.ny + across.far, pl.ds(1, 1), :] = across.far_row(own, ex, a)

    @pl.when(across.has_far)
    def _():
        for a in range(8):
            msg[place.ix * place.ny + across.far, pl.ds(a, 1), :] = across.far_row(own, 0, a)
            if a > 0:
                to = place.ix * place.ny + across.beyond
                msg[to, pl.ds(a, 1), :] = across.far_row(own, 1, a)


def inner_along_y(place, y_first, y_second, before, after, ex, a, at, edge):
    row = pl.ds(at + ex * 8 + a, 1)
    got_a, got_b = y_first[row, :], y_second[row, :]
    below, above = place.before_y(got_a, got_b), place.after_y(got_a, got_b)
    if before is None:
        return below, above
    if (ex, a) == (0, 0):
        below = below + before(edge, 1)
        above = above + before(edge + 1, 1)
    if (ex, a) == (1, 7):
        below = below + after(edge, 1)
        above = above + after(edge + 1, 1)
    return below, above


class Pairing:
    def __init__(self, place):
        self.place = place
        even = place.even_y
        self.even = even
        self.twin = jnp.where(even, place.iy + 1, place.iy - 1)
        self.far = jnp.where(even, place.iy - 1, place.iy + 1)
        self.has_far = jnp.where(even, place.iy - 1, place.ny - 2 - place.iy) >= 0
        self.beyond = jnp.where(even, place.iy - 2, place.iy + 2)
        self.twin_far = jnp.where(even, place.iy + 2, place.iy - 2)
        self.twin_has_far = jnp.where(even, place.ny - 3 - place.iy, place.iy - 2) >= 0

    def beside(self, side):
        place = self.place
        if side == 0:
            return place.prev_x, place.ix - 1
        return place.next_x, place.ix + 1

    def far_row(self, field, ex, a):
        low = field[ex, a, 0, pl.ds(0, 1), :]
        return jnp.where(self.even, low, field[ex, a, 1, pl.ds(7, 1), :])

    def twin_row(self, field, ex, a):
        low = field[ex, a, 0, pl.ds(0, 1), :]
        return jnp.where(self.even, field[ex, a, 1, pl.ds(7, 1), :], low)


RELAY_FACE, RELAY_EDGE, RELAY_ROWS = 24, 40, 42


def relay_kernel(got, own, out):
    place = Place()
    across = Pairing(place)
    out[...] = jnp.zeros(out.shape, jnp.float32)
    for side in range(2):
        there, ix = across.beside(side)

        @pl.when(there)
        def _():
            out[pl.ds(side * 8, 8), :] = got[ix * place.ny + across.twin]
            corner = got[ix * place.ny + place.iy, pl.ds(0, 1), :]
            out[pl.ds(RELAY_EDGE + side, 1), :] = corner

    @pl.when(across.twin_has_far)
    def _():
        out[pl.ds(16, 8), :] = got[place.ix * place.ny + across.twin_far]

    for ex in range(2):
        for a in range(8):
            out[pl.ds(RELAY_FACE + ex * 8 + a, 1), :] = across.twin_row(own, ex, a)


SMOOTH_X, SMOOTH_Y, SMOOTH_EDGE, SMOOTH_ROWS = 16, 16, 32, 34


def turn_smooth_kernel(own, inner_x, y_first, y_second, first, second):
    place = Place()
    sides = []
    for side, (ex, a) in enumerate(((0, 0), (1, 7))):
        row = pl.ds(15 * side, 1)
        got_a, got_b = y_first[row, :], y_second[row, :]
        low = own[ex, a, 0] + jnp.where(place.row == 0, place.before_y(got_a, got_b), 0.0)
        high = own[ex, a, 1] + jnp.where(place.row == 7, place.after_y(got_a, got_b), 0.0)
        sides.append((low, high))
    for ey in range(2):
        rows = pl.ds(ey * 8, 8)
        first[rows, :] = place.send_x(sides[1][ey], sides[0][ey])
        second[rows, :] = place.send_x(sides[0][ey], sides[1][ey])
    turn_edges(
        place, inner_x, y_first, y_second, first, second, SMOOTH_X, SMOOTH_EDGE, SMOOTH_Y
    )


def restricted(place, sums, grp):
    values = []
    for c in range(NCD):
        acc = jnp.zeros(TILE, jnp.float32)
        for ex in range(2):
            for ey in range(2):
                group = grp[pl.ds((ex + 1) * 4 + ey + 1, 1), :]
                acc = acc + jnp.where(group == float(c), sums[ex][ey], 0.0)
        values.append(total(acc))
    return values


AWAY = 16
BEYOND = 18


def message(place, own_values, scalars, away=0, beyond=1):
    lane = lax.broadcasted_iota(jnp.int32, (1, LANES), 1)
    spot = (place.ix * place.ny + place.iy) % (LANES // NCD)
    after = (spot + beyond) % (LANES // NCD)
    spot = (spot + away) % (LANES // NCD)
    row = jnp.zeros((1, LANES), jnp.float32)
    for c, value in enumerate(own_values):
        row = row + jnp.where(lane == spot * NCD + c, value, 0.0)
    for c, value in enumerate(scalars):
        if value is None:
            continue
        row = row + jnp.where(lane == after * NCD + c, value, 0.0)
    return row


def send_to_all(msg, row):
    def send(i, carry):
        msg[i] = row
        return carry

    lax.fori_loop(0, msg.shape[0], send, 0, unroll=msg.shape[0] <= 64)


def cross_image(place, ctab, kap, value, flat, inner, ex, ey):
    slope_y = along_y(ctab, T_K, value)
    turned_y = inner + float(SCALED[0, 0]) * value
    own = kap[pl.ds((ex + 1) * 4 + ey + 1, 1), :] * (slope_y + flat) + sigma_p * value
    beyond = kap[pl.ds((ex + 1) * 4 + 3 * ey, 1), :] * (turned_y + flat) + sigma_p * value
    return own + jnp.where(beyond_y(place, ey), beyond, 0.0), slope_y, turned_y


def beyond_y(place, ey):
    if ey == 0:
        return (place.row == 0) & place.prev_y
    return (place.row == 7) & place.next_y


def ready_kernel(
    own, y_first, y_second, inv_diag, kap, ctab, zmat, image, scaled, part, slope_z
):
    place = Place()
    for ex in range(2):
        for a in range(8):
            for ey in range(2):
                tile = got_y_sum(place, own[ex, a, ey], 0, ex, a, ey, y_first, y_second)
                image[ex, a, ey] = tile
                scaled[ex, a, ey] = tile * inv_diag[ex, a, ey] * float(1.0 / THETA)
    slope_z[...] = along_z(scaled[...].reshape(256, LANES), zmat[2]).reshape(slope_z.shape)
    for ex in range(2):
        for a in range(8):
            if (ex, a) in OUTER:
                continue
            rows = inner_along_y(
                place, y_first, y_second, None, None, ex, a, SMOOTH_Y, SMOOTH_EDGE
            )
            for ey in range(2):
                part[ex, a, ey] = cross_image(
                    place, ctab, kap, scaled[ex, a, ey], slope_z[ex, a, ey], rows[ey], ex, ey
                )[0]


def smooth_kernel(
    begun,
    begun_scaled,
    given,
    y_first,
    y_second,
    x_first,
    x_second,
    inv_diag,
    kap,
    grp,
    extra,
    facts,
    ctab,
    zmat,
    image,
    smoothed,
    msg,
    scaled,
    slope_z,
    edge,
):
    place = Place()
    weight = ctab[T_W]
    corner = float(SCALED[0, 0])

    def before(row, count=8):
        rows = pl.ds(row, count)
        return place.before_x(x_first[rows, :], x_second[rows, :])

    def after(row, count=8):
        rows = pl.ds(row, count)
        return place.after_x(x_first[rows, :], x_second[rows, :])

    image[...] = begun[...]
    scaled[...] = begun_scaled[...]
    for side, (ex, a) in enumerate(OUTER):
        for ey in range(2):
            tile = got_x_sum(place, begun[ex, a, ey], 0, ex, ey, x_first, x_second)
            image[ex, a, ey] = tile
            scaled[ex, a, ey] = tile * inv_diag[ex, a, ey] * float(1.0 / THETA)
            edge[side, ey] = scaled[ex, a, ey]
    edge[...] = along_z(edge[...].reshape(32, LANES), zmat[2]).reshape(edge.shape)
    there_x = (place.prev_x, place.next_x)
    zero = jnp.zeros(TILE, jnp.float32)
    tiles = [[[None, None] for _ in range(8)] for _ in range(2)]
    for ex in range(2):
        a_out = OUTER[ex][1]
        rows = inner_along_y(
            place, y_first, y_second, before, after, ex, a_out, SMOOTH_Y, SMOOTH_EDGE
        )
        for ey in range(2):
            values = [scaled[ex, a, ey] for a in range(8)]
            slopes = along_x(SCALED, values, 1)
            far_row = beyond_y(place, ey)
            beside = kap[pl.ds((ex + 1) * 4 + 3 * ey, 1), :]
            kappa = kap[pl.ds((ex + 1) * 4 + ey + 1, 1), :] + jnp.where(far_row, beside, 0.0)
            for a in range(8):
                if a != a_out:
                    acc = given[ex, a, ey]
                else:
                    value, flat = values[a], edge[ex, ey]
                    acc, slope_y, turned_y = cross_image(
                        place, ctab, kap, value, flat, rows[ey], ex, ey
                    )
                    x_next = 3 * ex
                    get = before if ex == 0 else after
                    turned_x = get(SMOOTH_X + ey * 8) + corner * value
                    side = kap[pl.ds(x_next * 4 + ey + 1, 1), :] * (turned_x + slope_y + flat)
                    far = kap[pl.ds(x_next * 4 + 3 * ey, 1), :] * (turned_x + turned_y + flat)
                    side = side + sigma_p * value
                    side = side + jnp.where(far_row, far + sigma_p * value, zero)
                    acc = acc + jnp.where(there_x[ex], side, zero)
                acc = acc + kappa * slopes[a]
                tiles[ex][a][ey] = place.join_z(acc * (float(WEIGHTS[a]) * weight))
    join_own(place, tiles)
    inv_mult = [1.0 / place.mult_tile(ey) for ey in range(2)]
    sums = [[jnp.zeros(TILE, jnp.float32) for _ in range(2)] for _ in range(2)]
    square = jnp.zeros(TILE, jnp.float32)
    for ex in range(2):
        for a in range(8):
            for ey in range(2):
                value = image[ex, a, ey]
                defect = (value - tiles[ex][a][ey]) * inv_diag[ex, a, ey]
                update = scaled[ex, a, ey]
                result = (
                    float(1.0 + RHO_NEXT * RHO) * update + float(2.0 * RHO_NEXT / DELTA) * defect
                )
                smoothed[ex, a, ey] = result
                weighed = value * (inv_mult[ey] * place.inv_x(ex, a))
                sums[ex][ey] = sums[ex][ey] + weighed
                square = square + weighed * result
    own_sums = restricted(place, sums, grp)
    if msg.shape[2] == LANES:
        sums = [extra[:, pl.ds(k, 1)] for k in range(2)]
        send_to_all(msg, message(place, own_sums, sums))
        return
    slope_z[...] = along_z(smoothed[...].reshape(256, LANES), zmat[2]).reshape(slope_z.shape)
    energy = jnp.zeros(TILE, jnp.float32)
    for ex in range(2):
        for ey in range(2):
            values, images = own_operator(ctab, kap, smoothed, slope_z, ex, ey)
            for a in range(8):
                energy = energy + values[a] * images[a]
                tiles[ex][a][ey] = place.join_z(images[a])
    join_own(place, tiles)
    sums = [extra[:, pl.ds(k, 1)] for k in range(2)] + [total(square), total(energy)]
    row = message(place, own_sums, sums, AWAY, BEYOND)
    row = row + restricted_around(place, tiles, inv_mult, grp)
    send_to_all(msg, jnp.concatenate([row, facts[:, LANES:]], axis=1))


def restricted_around(place, tiles, inv_mult, grp):
    lane = lax.broadcasted_iota(jnp.int32, (1, LANES), 1)
    weighed = [
        [[tiles[ex][a][ey] * (inv_mult[ey] * place.inv_x(ex, a)) for ey in range(2)] for a in range(8)]
        for ex in range(2)
    ]

    def rows_of(tile, y):
        if y == 0:
            return jnp.where(place.row == 0, tile[0], 0.0)
        if y == 3:
            return jnp.where(place.row == 7, tile[1], 0.0)
        return tile[y - 1]

    there_x = (place.prev_x, None, None, place.next_x)
    there_y = (place.prev_y, None, None, place.next_y)
    by_device = [
        [[jnp.zeros(TILE, jnp.float32) for _ in range(NCD)] for _ in range(3)] for _ in range(3)
    ]
    for x in range(4):
        for y in range(4):
            if x == 0:
                acc = rows_of(weighed[0][0], y)
            elif x == 3:
                acc = rows_of(weighed[1][7], y)
            else:
                acc = rows_of(weighed[x - 1][0], y)
                for a in range(1, 8):
                    acc = acc + rows_of(weighed[x - 1][a], y)
            for there in (there_x[x], there_y[y]):
                if there is not None:
                    acc = jnp.where(there, acc, 0.0)
            group = grp[pl.ds(x * 4 + y, 1), :]
            device = by_device[(x + 1) // 2][(y + 1) // 2]
            for c in range(NCD):
                device[c] = device[c] + jnp.where(group == float(c), acc, 0.0)
    row = jnp.zeros((1, LANES), jnp.float32)
    for dx in range(3):
        for dy in range(3):
            at = ((place.ix + dx - 1) * place.ny + place.iy + dy - 1) * NCD
            for c in range(NCD):
                row = row + jnp.where(lane == at + c, total(by_device[dx][dy][c]), 0.0)
    return row


def coarse_part(place, blocks, got, coarse, grp, others=()):
    lane = lax.broadcasted_iota(jnp.int32, (1, LANES), 1)
    values = [jnp.zeros((1, LANES), jnp.float32) for _ in range(blocks)]
    per = LANES // NCD
    for j in range(blocks):

        def gather(i, acc, j=j):
            return jnp.where(lane // NCD == i, got[j * per + i, pl.ds(0, 1), :], acc)

        values[j] = lax.fori_loop(0, per, gather, values[j], unroll=blocks == 1)
        for there, device, row in others:
            spot = (lane // NCD == device % per) & (device // per == j) & there
            values[j] = jnp.where(spot, row, values[j])

    def solved(dx, dy, c):
        acc = None
        for j in range(blocks):
            term = coarse[pl.ds(((dx * 3 + dy) * NCD + c) * blocks + j, 1), :] * values[j]
            acc = term if acc is None else acc + term
        return jnp.sum(acc, axis=1, keepdims=True)

    return prolonged(place, solved, grp)


def prolonged(place, solved, grp):
    device = [[[solved(dx, dy, c) for c in range(NCD)] for dy in range(3)] for dx in range(3)]
    inv_z = jnp.where(place.low_z | place.high_z, 0.5, 1.0)
    rows = []
    for x in range(4):
        line = []
        for y in range(4):
            group = grp[pl.ds(x * 4 + y, 1), :]
            acc = jnp.zeros((1, LANES), jnp.float32)
            for c in range(NCD):
                acc = acc + jnp.where(
                    group == float(c), device[(x + 1) // 2][(y + 1) // 2][c], 0.0
                )
            line.append(place.join_z(jnp.broadcast_to(acc, TILE)) * inv_z)
        rows.append(line)
    low_y = jnp.where(place.prev_y, 0.5, 1.0)
    high_y = jnp.where(place.next_y, 0.5, 1.0)

    def tile(ex, kind, ey):
        if kind == 1:
            vals = [rows[ex + 1][y] for y in range(4)]
        elif kind == 0:
            scale = place.inv_x(ex, 0)
            vals = [(rows[ex][y] + rows[ex + 1][y]) * scale for y in range(4)]
        else:
            scale = place.inv_x(ex, 7)
            vals = [(rows[ex + 1][y] + rows[ex + 2][y]) * scale for y in range(4)]
        mid = vals[ey + 1]
        low = (vals[ey] + mid) * (low_y if ey == 0 else 0.5)
        high = (mid + vals[ey + 2]) * (high_y if ey == 1 else 0.5)
        return jnp.where(place.row == 0, low, jnp.where(place.row == 7, high, mid))

    return tile


def kind_of(a):
    return 0 if a == 0 else (2 if a == 7 else 1)


def own_operator(ctab, kap, field, slope_z, ex, ey):
    weight = ctab[T_W]
    tiles = [field[ex, a, ey] for a in range(8)]
    slopes = along_x(SCALED, tiles, 1)
    kappa = kap[pl.ds((ex + 1) * 4 + ey + 1, 1), :]
    out = []
    for a in range(8):
        stiff = slopes[a] + along_y(ctab, T_K, tiles[a]) + slope_z[ex, a, ey]
        out.append((kappa * stiff + sigma_p * tiles[a]) * (float(WEIGHTS[a]) * weight))
    return tiles, out


def first_direction_kernel(
    blocks,
    got,
    relayed,
    coarse,
    grp,
    kap,
    inv_diag,
    resid,
    own,
    ctab,
    zmat,
    direction,
    out,
    inner_x,
    first,
    second,
    extra,
    slope_z,
    image,
):
    place = Place()
    inv_mult = [1.0 / place.mult_tile(ey) for ey in range(2)]
    across = Pairing(place)
    others = []
    for side in range(2):
        there, ix = across.beside(side)
        others.append((there, ix * place.ny + place.iy, relayed[pl.ds(side * 8, 1), :]))
    others.append(
        (across.has_far, place.ix * place.ny + across.far, relayed[pl.ds(16, 1), :])
    )
    part = coarse_part(place, blocks, got, coarse, grp, others)
    image[...] = own[...]
    far_edge = jnp.where(across.even, 0, 7)

    def add_row(ex, a, row, edge, low):
        extra = jnp.where(place.row == edge, row, 0.0)
        image[ex, a, 0] = image[ex, a, 0] + jnp.where(low, extra, 0.0)
        image[ex, a, 1] = image[ex, a, 1] + jnp.where(low, 0.0, extra)

    for ex in range(2):
        for a in range(8):
            row = relayed[pl.ds(RELAY_FACE + ex * 8 + a, 1), :]
            add_row(ex, a, row, 7 - far_edge, ~across.even)

    @pl.when(across.has_far)
    def _():
        for a in range(8):
            row = got[place.ix * place.ny + across.far, pl.ds(a, 1), :]
            add_row(0, a, row, far_edge, across.even)
            if a == 7:
                add_row(1, 0, row, far_edge, across.even)
            if a > 0:
                add_row(1, a, relayed[pl.ds(16 + a, 1), :], far_edge, across.even)

    for side, (ex, a) in enumerate(OUTER):
        there, ix = across.beside(side)

        @pl.when(there)
        def _():
            low = got[ix * place.ny + place.iy]
            high = jnp.where(
                place.row == 0, pltpu.roll(low, 1, 0), relayed[pl.ds(side * 8, 8), :]
            )
            image[ex, a, 0] = image[ex, a, 0] + low
            image[ex, a, 1] = image[ex, a, 1] + high
            corner = jnp.where(
                across.even,
                relayed[pl.ds(RELAY_EDGE + side, 1), :],
                got[ix * place.ny + across.twin, pl.ds(7, 1), :],
            )
            add_row(ex, a, corner, 7 - far_edge, ~across.even)

        @pl.when(there & across.has_far)
        def _():
            corner = got[ix * place.ny + across.far, pl.ds(1, 1), :]
            add_row(ex, a, corner, far_edge, across.even)

    energy = jnp.zeros(TILE, jnp.float32)
    for ex in range(2):
        for ey in range(2):
            kinds = [part(ex, kind, ey) for kind in range(3)]
            for a in range(8):
                known = resid[ex, a, ey]
                inverse = inv_diag[ex, a, ey]
                defect = (known - image[ex, a, ey]) * inverse
                value = (
                    float((1.0 + RHO_NEXT * RHO) / THETA) * (known * inverse)
                    + float(2.0 * RHO_NEXT / DELTA) * defect
                    + kinds[kind_of(a)]
                )
                direction[ex, a, ey] = value
                scale = place.inv_x(ex, a)
                energy = energy + value * known * (inv_mult[ey] * scale)
    slope_z[...] = along_z(direction[...].reshape(256, LANES), zmat[2]).reshape(slope_z.shape)
    curvature = jnp.zeros(TILE, jnp.float32)
    tiles = [[[None, None] for _ in range(8)] for _ in range(2)]
    for ex in range(2):
        for ey in range(2):
            values, images = own_operator(ctab, kap, direction, slope_z, ex, ey)
            for a in range(8):
                curvature = curvature + values[a] * images[a]
                tiles[ex][a][ey] = place.join_z(images[a])
    join_own(place, tiles)
    for ex in range(2):
        for a in range(8):
            for ey in range(2):
                out[ex, a, ey] = tiles[ex][a][ey]
    store_y_faces(place, out, first, second, (), 0)

    def tile_of(ex, a, ey):
        return tiles[ex][a][ey] * inv_diag[ex, a, ey] * float(1.0 / THETA)

    def column_of(ex, ey):
        return [tile_of(ex, a, ey) for a in range(8)]

    store_inner(
        place, SCALED, ctab[T_KBOTTOM], ctab[T_KTOP], column_of, tile_of, inner_x, first, second,
        SMOOTH_Y, SMOOTH_EDGE,
    )
    lane = lax.broadcasted_iota(jnp.int32, (1, LANES), 1)
    extra[...] = jnp.where(lane == 0, total(energy), total(curvature))


def gathered_scalars(got, count):
    lane = lax.broadcasted_iota(jnp.int32, (1, LANES), 1)
    per = LANES // NCD
    sums = []
    for c in range(count):
        acc = jnp.zeros((1, LANES), jnp.float32)

        def gather(i, acc, c=c):
            return acc + jnp.where(lane == ((i + 1) % per) * NCD + c, got[i], 0.0)

        acc = lax.fori_loop(0, got.shape[0], gather, acc, unroll=got.shape[0] <= per)
        sums.append(jnp.sum(acc, axis=1, keepdims=True))
    return sums


def second_direction_kernel(
    blocks,
    got,
    coarse,
    grp,
    kap,
    resid,
    direction,
    image,
    smoothed,
    ctab,
    zmat,
    following,
    known,
    msg,
    slope_z,
):
    place = Place()
    inv_mult = [1.0 / place.mult_tile(ey) for ey in range(2)]
    part = coarse_part(place, blocks, got, coarse, grp)
    energy, curvature = gathered_scalars(got, 2)
    step = energy / curvature
    lane = lax.broadcasted_iota(jnp.int32, (1, LANES), 1)
    known[...] = jnp.where(lane == 0, energy, jnp.where(lane == 1, curvature, 0.0))
    energy_next = jnp.zeros(TILE, jnp.float32)
    cross = jnp.zeros(TILE, jnp.float32)
    for ex in range(2):
        for ey in range(2):
            kinds = [part(ex, kind, ey) for kind in range(3)]
            for a in range(8):
                value = direction[ex, a, ey] - step * (smoothed[ex, a, ey] + kinds[kind_of(a)])
                following[ex, a, ey] = value
                weighed = value * (inv_mult[ey] * place.inv_x(ex, a))
                was = image[ex, a, ey]
                energy_next = energy_next + weighed * (resid[ex, a, ey] - step * was)
                cross = cross + weighed * was
    slope_z[...] = along_z(following[...].reshape(256, LANES), zmat[2]).reshape(slope_z.shape)
    square = jnp.zeros(TILE, jnp.float32)
    for ex in range(2):
        for ey in range(2):
            values, images = own_operator(ctab, kap, following, slope_z, ex, ey)
            for a in range(8):
                square = square + values[a] * images[a]
    send_to_all(msg, message(place, [], [total(energy_next), total(square), total(cross)]))


def pressure_kernel(got, known, direction, following, pressure):
    energy = known[:, pl.ds(0, 1)]
    curvature = known[:, pl.ds(1, 1)]
    energy_next, square, cross = gathered_scalars(got, 3)
    ratio = energy_next / energy
    step = energy / curvature
    step_next = energy_next / (square + 2.0 * ratio * cross + ratio * ratio * curvature)
    weight_old = step + step_next * ratio
    for ex in range(2):
        for a in range(8):
            for ey in range(2):
                pressure[ex, a, ey] = (
                    weight_old * direction[ex, a, ey] + step_next * following[ex, a, ey]
                )


def coarse_energy(place, got, values, kappa, number):
    lane, row = place.lane, place.row
    for ex in range(2):
        for gx in range(8):
            own = jnp.zeros((1, LANES), jnp.float32)
            group = jnp.zeros((1, LANES), jnp.float32)
            spot = lane[0:1] // 32
            for gy in range(4):
                line = got[gx * 4 + gy, :, pl.ds(LANES, LANES)]
                own = jnp.where(spot == (gy + 2 * ex) % 4, line, own)
                group = jnp.where(spot == (gy + 1 + 2 * ex) % 4, line, group)
            kappa[ex, pl.ds(gx, 1), :] = own
            number[ex, pl.ds(gx, 1), :] = group
    grid = [jnp.zeros(TILE, jnp.float32) for _ in range(2)]
    numbers = [pltpu.roll(number[0], 96, 1), pltpu.roll(number[1], 32, 1)]
    kappa = [kappa[0], pltpu.roll(kappa[1], 64, 1)]
    for q in range(4):
        for c in range(NCD):
            mine = jnp.where(lane == row * 16 + q * 4 + c, values, 0.0)
            mine = jnp.sum(mine, axis=1, keepdims=True)
            for ex in range(2):
                chosen = (lane // 32 == q) & (numbers[ex] == float(c))
                grid[ex] = jnp.where(chosen, mine, grid[ex])

    def ends_y(v):
        low = jnp.where(lane >= 16, 0.5 * (v + pltpu.roll(v, 16, 1)), v)
        return low, v, jnp.where(lane < 112, 0.5 * (v + pltpu.roll(v, 112, 1)), v)

    def ends_z(v):
        low = jnp.where(lane % 16 > 0, 0.5 * (v + pltpu.roll(v, 1, 1)), v)
        return low, v, jnp.where(lane % 16 < 15, 0.5 * (v + pltpu.roll(v, 127, 1)), v)

    low = jnp.where(row > 0, 0.5 * (grid[0] + pltpu.roll(grid[1], 1, 0)), grid[0])
    mid = 0.5 * (grid[0] + grid[1])
    high = jnp.where(row < 7, 0.5 * (grid[1] + pltpu.roll(grid[0], 7, 0)), grid[1])
    mass = [float(WEIGHTS[0]), float(np.sum(WEIGHTS[1:7])), float(WEIGHTS[7])]
    links = (
        (0, 1, -float(np.sum(STIFF[0, 1:7]))),
        (0, 2, -float(STIFF[0, 7])),
        (1, 2, -float(np.sum(STIFF[7, 1:7]))),
    )
    energy = jnp.zeros(TILE, jnp.float32)
    for ex, line in enumerate(((low, grid[0], mid), (mid, grid[1], high))):
        nodes = [[ends_z(v) for v in ends_y(w)] for w in line]
        stiff = jnp.zeros(TILE, jnp.float32)
        square = jnp.zeros(TILE, jnp.float32)
        for i in range(3):
            for j in range(3):
                for k, l, weight in links:
                    factor = weight * mass[i] * mass[j]
                    for first, second in (
                        (nodes[k][i][j], nodes[l][i][j]),
                        (nodes[i][k][j], nodes[i][l][j]),
                        (nodes[i][j][k], nodes[i][j][l]),
                    ):
                        gap = first - second
                        stiff = stiff + (factor * gap) * gap
                for k in range(3):
                    value = nodes[i][j][k]
                    square = square + (mass[i] * mass[j] * mass[k] * value) * value
        energy = energy + kappa[ex] * stiff + sigma_p * square
    return total(energy)


def finish_kernel(
    got, grp, direction, smoothed, pressure, matrix, kappa, number
):
    place = Place()
    per = LANES // NCD
    row_lane = lax.broadcasted_iota(jnp.int32, (1, LANES), 1)
    rest = jnp.zeros((1, LANES), jnp.float32)
    dual = jnp.zeros((1, LANES), jnp.float32)
    sums = [jnp.zeros((1, LANES), jnp.float32) for _ in range(4)]
    for i in range(per):
        line = got[i, :, pl.ds(0, LANES)]
        mine = row_lane // NCD == (i + AWAY) % per
        known = row_lane // NCD == (i + BEYOND) % per
        rest = jnp.where(mine, line, rest)
        dual = dual + jnp.where(mine | known, 0.0, line)
        for c in range(4):
            sums[c] = sums[c] + jnp.where(row_lane == ((i + BEYOND) % per) * NCD + c, line, 0.0)
            block = got[i, :, pl.ds((2 + c) * LANES, LANES)]
            matrix[pl.ds(i * NCD + c, 1), :] = block
    rest = pltpu.roll(rest, (per - AWAY) * NCD, 1)
    energy, curvature, square, self_energy = [
        jnp.sum(value, axis=1, keepdims=True) for value in sums
    ]
    values = exact_dot(jnp.broadcast_to(rest, TILE), matrix[...])
    line = values[0:1]
    cross = square + jnp.sum(line * rest, axis=1, keepdims=True)
    both = self_energy + 2.0 * jnp.sum(line * dual, axis=1, keepdims=True)
    both = both + coarse_energy(place, got, values, kappa, number)
    step = energy / curvature
    energy_next = step * step * cross - energy
    ratio = energy_next / energy
    with_image = curvature - step * cross
    with_itself = curvature - 2.0 * step * cross + step * step * both
    step_next = energy_next / (
        with_itself + 2.0 * ratio * with_image + ratio * ratio * curvature
    )
    old = step + step_next * (1.0 + ratio)
    new = -step_next * step

    def solved(dx, dy, c):
        at = ((place.ix + dx - 1) * place.ny + place.iy + dy - 1) * NCD + c
        return jnp.sum(jnp.where(row_lane == at, line, 0.0), axis=1, keepdims=True)

    part = prolonged(place, masked(place, solved), grp)
    for ex in range(2):
        for ey in range(2):
            kinds = [part(ex, kind, ey) for kind in range(3)]
            for a in range(8):
                pressure[ex, a, ey] = old * direction[ex, a, ey] + new * (
                    smoothed[ex, a, ey] + kinds[kind_of(a)]
                )


def masked(place, solved):
    there_x = (place.prev_x, None, place.next_x)
    there_y = (place.prev_y, None, place.next_y)

    def value(dx, dy, c):
        out = solved(dx, dy, c)
        for there in (there_x[dx], there_y[dy]):
            if there is not None:
                out = jnp.where(there, out, 0.0)
        return out

    return value


def call(body, outs, scratch=(), **more):
    return pl.pallas_call(
        body,
        out_shape=[jax.ShapeDtypeStruct(shape, jnp.float32) for shape in outs],
        scratch_shapes=[
            pltpu.VMEM(shape, jnp.float32) if isinstance(shape, tuple) else shape
            for shape in scratch
        ],
        **more,
        compiler_params=pltpu.CompilerParams(vmem_limit_bytes=24 * 1024 * 1024),
    )


def swap(first, second, axis):
    along, across = lax.axis_size("gx"), lax.axis_size("gy")

    def number(ix, iy):
        return ix * across + iy

    pairs = ([], [])
    for ix in range(along):
        for iy in range(across):
            at, count = (ix, along) if axis == "gx" else (iy, across)
            for k, to in enumerate((at ^ 1, ((at + 1) ^ 1) - 1)):
                if 0 <= to < count:
                    there = (to, iy) if axis == "gx" else (ix, to)
                else:
                    there = (ix, iy ^ 1) if axis == "gx" else (ix, across - 1 - iy)
                pairs[k].append((number(ix, iy), number(*there)))
    if axis == "gx":
        pairs = pairs[::-1]
    first_got = lax.ppermute(first, BOTH, pairs[0])
    return first_got, lax.ppermute(second, BOTH, pairs[1])


def per_device(fields, viscosity, inv_density, elem_group, coarse_inverse):
    length = fields.shape[5]
    elems_z = length // NODES
    devices = lax.axis_size("gx") * lax.axis_size("gy")
    blocks = coarse_inverse.shape[1] // LANES
    pack_rows = 1 + NCD * blocks
    tiles_np, mats_np = constant_tables(elems_z)
    ctab, zmat = jnp.asarray(tiles_np), jnp.asarray(mats_np)
    one = fields.shape[1:]
    four = fields.shape
    faces = (64, LANES)
    xf_shape = (2, 4, 2, 8, LANES)
    inner_shape = (2, 2, 8, LANES)
    y_shape, x_shape = (STEP_PACK + 3 * pack_rows, LANES), (STEP_PACK, LANES)
    turned = (64 + pack_rows, LANES)
    smooth_shape = (SMOOTH_ROWS, LANES)
    rows = (devices, 1, LANES)
    grid_fits = (
        blocks == 1
        and lax.axis_size("gx") == 8
        and lax.axis_size("gy") * fields.shape[3] * elems_z == LANES
    )

    def exchange_all(msg):
        return lax.all_to_all(msg, BOTH, 0, 0, tiled=True)

    beside = pl.CostEstimate(flops=10**7, bytes_accessed=10**6, transcendentals=0)
    summed, xf, first, second = call(
        mass_kernel,
        [four, xf_shape, faces, faces],
    )(fields)
    pack, facts = call(
        pack_kernel,
        [(pack_rows, LANES), (1, 6 * LANES)],
        cost_estimate=beside,
    )(inv_density, elem_group, coarse_inverse)
    y_got = swap(first, second, "gy")
    first, second = call(functools.partial(turn_faces_kernel, pack_rows), [turned, turned])(
        xf, pack, *y_got
    )
    side_got = x_got = swap(first, second, "gx")
    edge_shape = (4, 2, 2, 8, LANES)
    begun, given, slope, answer = call(
        prepare_kernel, [four, four, edge_shape, one], [four, four], cost_estimate=beside
    )(summed, viscosity, *y_got, ctab, zmat)
    share, xf, inner_x, first, second = call(
        functools.partial(rhs_kernel, pack_rows),
        [four, xf_shape, inner_shape, y_shape, y_shape],
        [edge_shape, edge_shape, edge_shape, edge_shape],
    )(begun, given, slope, answer, viscosity, pack, *x_got, ctab, zmat)
    y_got = swap(first, second, "gy")
    first, second = call(turn_step_kernel, [x_shape, x_shape])(xf, inner_x, *y_got)
    x_got = swap(first, second, "gx")
    inv_diag, kap, grp, coarse = call(
        functools.partial(setup_kernel, pack_rows, blocks),
        [one, (16, LANES), (16, LANES), (9 * NCD * blocks, LANES)],
        [(16, LANES), (8, 16, LANES)],
        cost_estimate=beside,
    )(pack, *side_got, *y_got, ctab)
    begun, given = call(approach_kernel, [four, one], [one], cost_estimate=beside)(
        share, *y_got, ctab, zmat
    )
    side_shape = (2, 2, 8, LANES)
    fields_got = x_got
    fields_begun = begun
    resid, own, msg = call(
        advance_kernel,
        [one, one, (devices, 8, LANES)],
        [one, one, side_shape, one, (3,) + side_shape],
    )(begun, given, *y_got, *x_got, inv_diag, kap, grp, ctab, zmat)
    got = exchange_all(msg)
    (relayed,) = call(relay_kernel, [(RELAY_ROWS, LANES)])(got, own)
    relayed = lax.ppermute(
        relayed, "gy", [(i, i ^ 1) for i in range(lax.axis_size("gy")) if i ^ 1 < lax.axis_size("gy")]
    )
    direction, own, inner_x, first, second, extra = call(
        functools.partial(first_direction_kernel, blocks),
        [one, one, inner_shape, smooth_shape, smooth_shape, (1, LANES)],
        [one, one],
    )(got, relayed, coarse, grp, kap, inv_diag, resid, own, ctab, zmat)
    y_got = swap(first, second, "gy")
    first, second = call(turn_smooth_kernel, [smooth_shape, smooth_shape])(own, inner_x, *y_got)
    x_got = swap(first, second, "gx")
    fields_new, extra = call(emit_kernel, [four, (1, LANES)], cost_estimate=beside)(
        fields_begun, *fields_got, extra
    )
    begun, begun_scaled, given = call(
        ready_kernel, [one, one, one], [one], cost_estimate=beside
    )(own, *y_got, inv_diag, kap, ctab, zmat)
    image, image_smoothed, msg = call(
        smooth_kernel,
        [one, one, (devices, 1, 6 * LANES) if grid_fits else rows],
        [one, one, side_shape],
    )(
        begun, begun_scaled, given, *y_got, *x_got, inv_diag, kap, grp, extra, facts, ctab, zmat
    )
    got = exchange_all(msg)
    if grid_fits:
        (pressure,) = call(
            finish_kernel, [one], [(LANES, LANES), (2,) + TILE, (2,) + TILE]
        )(got, grp, direction, image_smoothed)
        return (fields_new, pressure)
    following, known, msg = call(
        functools.partial(second_direction_kernel, blocks), [one, (1, LANES), rows], [one]
    )(got, coarse, grp, kap, resid, direction, image, image_smoothed, ctab, zmat)
    got = exchange_all(msg)
    (pressure,) = call(pressure_kernel, [one])(got, known, direction, following)
    return (fields_new, pressure)


def solution(mesh):
    placed = (
        P(None, "gx", None, "gy", None, None),
        P("gx", None, "gy", None, None),
        P("gx", "gy", None),
        P("gx", "gy", None),
        P(("gx", "gy"), None),
    )
    return jax.shard_map(
        per_device,
        mesh=mesh,
        in_specs=placed,
        out_specs=(P(None, "gx", None, "gy", None, None), P("gx", None, "gy", None, None)),
        check_vma=False,
    )
```

```python
import functools

import jax
import jax.numpy as jnp
import ml_dtypes
import numpy as np
from jax import lax
from jax.experimental import pallas as pl
from jax.experimental.pallas import tpu as pltpu
from jax.sharding import PartitionSpec as P

NCD = 4
NODES = 8
LANES = 128
TILE = (8, 128)
BOTH = ("gx", "gy")

dt_step = 0.01
sigma_p = 4.0
prandtl = 0.7
cheb_ratio = 0.1


def tables():
    points = np.array(
        [
            -1.0,
            -0.8717401485096066,
            -0.5917001814331423,
            -0.2092992179024789,
            0.2092992179024789,
            0.5917001814331423,
            0.8717401485096066,
            1.0,
        ]
    )
    weights = np.array(
        [
            1.0 / 28.0,
            0.2107042271435061,
            0.3411226924835044,
            0.4124587946587038,
            0.4124587946587038,
            0.3411226924835044,
            0.2107042271435061,
            1.0 / 28.0,
        ]
    )
    identity = np.eye(8)
    differ = points[:, None] - points[None, :] + identity
    barycentric = 1.0 / np.prod(differ, axis=1)
    offdiag = barycentric[None, :] / barycentric[:, None] / differ * (1.0 - identity)
    derivative = offdiag - identity * np.sum(offdiag, axis=1)[:, None]
    mass_one = identity * weights[None, :]
    stiff_one = derivative.T @ mass_one @ derivative
    stiff_three = (
        np.kron(np.kron(stiff_one, mass_one), mass_one)
        + np.kron(np.kron(mass_one, stiff_one), mass_one)
        + np.kron(np.kron(mass_one, mass_one), stiff_one)
    )
    three_diag = np.sum(stiff_three * np.eye(512), axis=1)
    spectral_bound = float(np.max(np.sum(np.abs(stiff_three), axis=1) / three_diag))
    return (derivative, weights, stiff_one, spectral_bound)


DERIV, WEIGHTS, STIFF, BOUND = tables()
SCALED = STIFF / WEIGHTS[:, None]
LINE = np.diag(STIFF) / WEIGHTS
THETA = 0.5 * (BOUND + cheb_ratio * BOUND)
DELTA = 0.5 * (BOUND - cheb_ratio * BOUND)
RHO = DELTA / THETA
RHO_NEXT = 1.0 / (2.0 * THETA / DELTA - RHO)


def constant_tables(elems_z):
    def turned(matrix):
        rows = np.arange(8)
        return [np.repeat(matrix[rows, (rows - s) % 8][:, None], LANES, 1) for s in range(8)]

    wz = np.tile(WEIGHTS, elems_z)
    kz = np.tile(LINE, elems_z)
    tiles = turned(DERIV) + turned(DERIV.T) + turned(SCALED)
    tiles += [WEIGHTS[:, None] * wz[None, :], LINE[:, None] + kz[None, :]]
    for matrix in (DERIV, SCALED):
        for node in (7, 0):
            inner = matrix[node] * (np.arange(8) != node)
            tiles.append(np.repeat(inner[:, None], LANES, 1))
    eye = np.eye(elems_z)
    mats = [np.kron(eye, DERIV.T), np.kron(eye, DERIV), np.kron(eye, SCALED.T)]
    halves = []
    for mat in mats:
        high = mat.astype(ml_dtypes.bfloat16)
        low = (mat - high.astype(np.float64)).astype(ml_dtypes.bfloat16)
        both = np.concatenate([high, low], 1)
        halves.append(np.concatenate([both, both], 0))
    return np.stack(tiles).astype(np.float32), np.stack(halves)


T_D, T_DT, T_K, T_W, T_LINE = 0, 8, 16, 24, 25
T_TOP, T_BOTTOM, T_KTOP, T_KBOTTOM = 26, 27, 28, 29


class Place:
    def __init__(self):
        self.ix = lax.axis_index("gx")
        self.iy = lax.axis_index("gy")
        self.nx = lax.axis_size("gx")
        self.ny = lax.axis_size("gy")
        self.even_x = self.ix % 2 == 0
        self.even_y = self.iy % 2 == 0
        self.row = lax.broadcasted_iota(jnp.int32, TILE, 0)
        self.lane = lax.broadcasted_iota(jnp.int32, TILE, 1)
        self.low_z = (self.lane % 8 == 0) & (self.lane > 0)
        self.high_z = (self.lane % 8 == 7) & (self.lane < LANES - 1)
        self.prev_x = self.ix > 0
        self.next_x = self.ix < self.nx - 1
        self.prev_y = self.iy > 0
        self.next_y = self.iy < self.ny - 1

    def mult_tile(self, ey):
        along_z = 1.0 + jnp.where(self.low_z | self.high_z, 1.0, 0.0)
        low = 1.0 if ey == 1 else jnp.where(self.prev_y, 1.0, 0.0)
        high = 1.0 if ey == 0 else jnp.where(self.next_y, 1.0, 0.0)
        along_y = 1.0 + jnp.where(self.row == 0, low, jnp.where(self.row == 7, high, 0.0))
        return along_y * along_z

    def inv_x(self, ex, a):
        if a == 0:
            return 0.5 if ex == 1 else jnp.where(self.prev_x, 0.5, 1.0)
        if a == 7:
            return 0.5 if ex == 0 else jnp.where(self.next_x, 0.5, 1.0)
        return 1.0

    def mult_x(self, ex, a):
        if a == 0:
            return 2.0 if ex == 1 else jnp.where(self.prev_x, 2.0, 1.0)
        if a == 7:
            return 2.0 if ex == 0 else jnp.where(self.next_x, 2.0, 1.0)
        return 1.0

    def share_x(self, ex, a):
        if (ex, a) == (0, 0):
            return jnp.where(self.prev_x, 0.5, 1.0)
        if (ex, a) == (1, 7):
            return jnp.where(self.next_x, 0.5, 1.0)
        return 1.0

    def share_y(self, ey):
        if ey == 0:
            return jnp.where((self.row == 0) & self.prev_y, 0.5, 1.0)
        return jnp.where((self.row == 7) & self.next_y, 0.5, 1.0)

    def inv_y(self, ey):
        low = 0.5 if ey == 1 else jnp.where(self.prev_y, 0.5, 1.0)
        high = 0.5 if ey == 0 else jnp.where(self.next_y, 0.5, 1.0)
        return jnp.where(self.row == 0, low, jnp.where(self.row == 7, high, 1.0))

    def inv_z(self):
        return jnp.where(self.low_z | self.high_z, 0.5, 1.0)

    def join_z(self, t):
        up = pltpu.roll(t, LANES - 1, 1)
        down = pltpu.roll(t, 1, 1)
        return t + jnp.where(self.high_z, up, jnp.where(self.low_z, down, 0.0))

    def to_low(self, below):
        return jnp.where(self.row == 0, pltpu.roll(below, 1, 0), 0.0)

    def to_high(self, above):
        return jnp.where(self.row == 7, pltpu.roll(above, 7, 0), 0.0)

    def join_y(self, below, above):
        return below + self.to_high(above), above + self.to_low(below)

    def before_x(self, first, second):
        return jnp.where(self.prev_x, jnp.where(self.even_x, first, second), 0.0)

    def after_x(self, first, second):
        return jnp.where(self.next_x, jnp.where(self.even_x, second, first), 0.0)

    def send_x(self, first, second):
        return jnp.where(self.even_x, second, first)

    def before_y(self, first, second):
        return jnp.where(self.prev_y, jnp.where(self.even_y, first, second), 0.0)

    def after_y(self, first, second):
        return jnp.where(self.next_y, jnp.where(self.even_y, second, first), 0.0)

    def send_y(self, first, second):
        return jnp.where(self.even_y, second, first)


def along_x(matrix, tiles, sign):
    even = [tiles[a] + tiles[7 - a] for a in range(4)]
    odd = [tiles[a] - tiles[7 - a] for a in range(4)]
    out = [None] * 8
    for i in range(4):
        plus, minus = None, None
        for a in range(4):
            p = float(0.5 * (matrix[i, a] + matrix[i, 7 - a])) * even[a]
            m = float(0.5 * (matrix[i, a] - matrix[i, 7 - a])) * odd[a]
            plus = p if plus is None else plus + p
            minus = m if minus is None else minus + m
        out[i] = plus + minus
        out[7 - i] = minus - plus if sign < 0 else plus - minus
    return out


def along_y(ctab, base, tile):
    acc = ctab[base] * tile
    for s in range(1, 8):
        acc = acc + ctab[base + s] * pltpu.roll(tile, s, 0)
    return acc


def exact_dot(rows, matrix):
    return jnp.dot(
        rows, matrix, precision=lax.Precision.HIGHEST, preferred_element_type=jnp.float32
    )


def along_z(rows, matrix):
    high = rows.astype(jnp.bfloat16)
    low = (rows - high.astype(jnp.float32)).astype(jnp.bfloat16)
    both = jnp.dot(
        jnp.concatenate([high, low], axis=1), matrix, preferred_element_type=jnp.float32
    )
    return both[:, :LANES] + both[:, LANES:]


def total(tile):
    return jnp.sum(jnp.sum(tile, axis=0, keepdims=True), axis=1, keepdims=True)


def store_y_faces(place, field, first_out, second_out, lead, at):
    for ex in range(2):
        for a in range(8):
            low = field[lead + (ex, a, 0, pl.ds(0, 1), slice(None))]
            high = field[lead + (ex, a, 1, pl.ds(7, 1), slice(None))]
            row = at + ex * 8 + a
            first_out[pl.ds(row, 1), :] = place.send_y(high, low)
            second_out[pl.ds(row, 1), :] = place.send_y(low, high)


def join_own(place, tiles):
    for ex in range(2):
        for a in range(8):
            tiles[ex][a] = list(place.join_y(*tiles[ex][a]))
    for ey in range(2):
        both = tiles[0][7][ey] + tiles[1][0][ey]
        tiles[0][7][ey] = both
        tiles[1][0][ey] = both


def weight_of(node):
    edge = jnp.minimum(node, 7 - node)
    value = jnp.where(edge == 2, float(WEIGHTS[2]), float(WEIGHTS[3]))
    return jnp.where(
        edge == 0, float(WEIGHTS[0]), jnp.where(edge == 1, float(WEIGHTS[1]), value)
    )


def faces_kernel(fields, first, second, edges):
    place = Place()
    weight = weight_of(place.row) * weight_of(place.lane % NODES) * float(WEIGHTS[0])
    for ch in range(4):
        for ex in range(2):
            for a in range(8):
                edges[0, ch, ex, pl.ds(a, 1), :] = fields[ch, ex, a, 0, pl.ds(0, 1), :]
                edges[1, ch, ex, pl.ds(a, 1), :] = fields[ch, ex, a, 1, pl.ds(7, 1), :]
    for ch in range(4):
        sides = [
            place.join_y(*[place.join_z(edges[side, ch, ex] * weight) for ex in range(2)])
            for side in range(2)
        ]
        for ex in range(2):
            rows = pl.ds(ch * 16 + ex * 8, 8)
            first[rows, :] = place.send_y(sides[1][ex], sides[0][ex])
            second[rows, :] = place.send_y(sides[0][ex], sides[1][ex])


def mass_kernel(fields, out, xf):
    place = Place()
    weight = weight_of(place.row) * weight_of(place.lane % NODES)
    for ch in range(4):
        tiles = [
            [
                [
                    place.join_z(fields[ch, ex, a, ey] * (float(WEIGHTS[a]) * weight))
                    for ey in range(2)
                ]
                for a in range(8)
            ]
            for ex in range(2)
        ]
        join_own(place, tiles)
        for ex in range(2):
            for a in range(8):
                for ey in range(2):
                    out[ch, ex, a, ey] = tiles[ex][a][ey]
        for ey in range(2):
            xf[0, ch, ey] = tiles[0][0][ey]
            xf[1, ch, ey] = tiles[1][7][ey]


def turn_faces(place, xf, y_first, y_second, first, second):
    for ch in range(4):
        sides = []
        for side in range(2):
            row = pl.ds(ch * 16 + 15 * side, 1)
            got_a, got_b = y_first[row, :], y_second[row, :]
            low = xf[side, ch, 0] + jnp.where(place.row == 0, place.before_y(got_a, got_b), 0.0)
            high = xf[side, ch, 1] + jnp.where(place.row == 7, place.after_y(got_a, got_b), 0.0)
            sides.append((low, high))
        for ey in range(2):
            rows = pl.ds(ch * 16 + ey * 8, 8)
            first[rows, :] = place.send_x(sides[1][ey], sides[0][ey])
            second[rows, :] = place.send_x(sides[0][ey], sides[1][ey])


def turn_faces_kernel(pack_rows, xf, pack, y_first, y_second, first, second):
    turn_faces(Place(), xf, y_first, y_second, first, second)
    first[pl.ds(64, pack_rows), :] = pack[...]
    second[pl.ds(64, pack_rows), :] = pack[...]


def turn_edges(place, inner_x, y_first, y_second, first, second, at, edge, inner_y):
    sides = []
    for side in range(2):
        row = pl.ds(edge + side, 1)
        got_a, got_b = y_first[row, :], y_second[row, :]
        low = inner_x[side, 0] + jnp.where(place.row == 0, place.before_y(got_a, got_b), 0.0)
        high = inner_x[side, 1] + jnp.where(place.row == 7, place.after_y(got_a, got_b), 0.0)
        sides.append((low, high))
    for ey in range(2):
        rows = pl.ds(at + ey * 8, 8)
        first[rows, :] = place.send_x(sides[1][ey], sides[0][ey])
        second[rows, :] = place.send_x(sides[0][ey], sides[1][ey])
    for k, pick in enumerate((place.before_y, place.after_y)):
        sides = []
        for side in range(2):
            row = pl.ds(inner_y + 15 * side, 1)
            sides.append(pick(y_first[row, :], y_second[row, :]))
        row = pl.ds(edge + k, 1)
        first[row, :] = place.send_x(sides[1], sides[0])
        second[row, :] = place.send_x(sides[0], sides[1])


STEP_U, STEP_V, STEP_EDGE, STEP_PACK = 64, 64, 80, 82


def turn_step_kernel(xf, inner_x, y_first, y_second, first, second):
    place = Place()
    turn_faces(place, xf, y_first, y_second, first, second)
    turn_edges(place, inner_x, y_first, y_second, first, second, STEP_U, STEP_EDGE, STEP_V)


def setup_kernel(
    pack_rows,
    blocks,
    pack,
    x_first,
    x_second,
    y_first,
    y_second,
    ctab,
    inv_diag,
    kap,
    grp,
    coarse,
    compact,
    spread,
):
    place = Place()
    beside = pl.ds(64, pack_rows)
    packs = [[None] * 3 for _ in range(3)]
    packs[0][1] = place.before_x(x_first[beside, :], x_second[beside, :])
    packs[1][1] = pack[...]
    packs[2][1] = place.after_x(x_first[beside, :], x_second[beside, :])
    for dx in range(3):
        rows = pl.ds(STEP_PACK + dx * pack_rows, pack_rows)
        packs[dx][0] = place.before_y(y_first[rows, :], y_second[rows, :])
        packs[dx][2] = place.after_y(y_first[rows, :], y_second[rows, :])
    compact[...] = jnp.zeros(compact.shape, jnp.float32)
    for dx in range(3):
        for dy in range(3):
            at = (dx * 3 + dy) * NCD * blocks
            coarse[pl.ds(at, NCD * blocks), :] = packs[dx][dy][1 : 1 + NCD * blocks]
            compact[pl.ds(dx * 3 + dy, 1), :] = packs[dx][dy][0:1]
    elems = LANES // NODES
    lane = lax.broadcasted_iota(jnp.int32, (LANES, LANES), 1)
    source = lax.broadcasted_iota(jnp.int32, (LANES, LANES), 0)
    for k in range(8):
        at = (k % 4 // 2) * 4 * elems + (k // 4) * 2 * elems + (k % 2) * elems
        spot = (source == at + lane // NODES).astype(jnp.float32)
        spread[k] = exact_dot(compact[...], spot)
    there_x = [jnp.where(place.prev_x, 1.0, 0.0), 1.0, jnp.where(place.next_x, 1.0, 0.0)]
    there_y = [jnp.where(place.prev_y, 1.0, 0.0), 1.0, jnp.where(place.next_y, 1.0, 0.0)]

    def element_row(base, u, v):
        device = (u // 2) * 3 + v // 2
        return spread[base + (u % 2) * 2 + v % 2, pl.ds(device, 1), :]

    for x in range(4):
        for y in range(4):
            kap[pl.ds(x * 4 + y, 1), :] = element_row(0, x + 1, y + 1)
            grp[pl.ds(x * 4 + y, 1), :] = element_row(4, x + 1, y + 1)
    kappa = [
        [
            place.join_z(jnp.broadcast_to(element_row(0, u + 1, v + 1), TILE))
            for v in range(4)
        ]
        for u in range(4)
    ]
    count_z = 1.0 + jnp.where(place.low_z | place.high_z, 1.0, 0.0)
    weight = ctab[T_W]
    line = ctab[T_LINE]

    def pick(values, ey):
        low = values[ey] + values[ey + 1]
        high = values[ey + 1] + values[ey + 2]
        return jnp.where(place.row == 0, low, jnp.where(place.row == 7, high, values[ey + 1]))

    for ex in range(2):
        for kind in range(3):
            us = {0: (ex, ex + 1), 1: (ex + 1,), 2: (ex + 1, ex + 2)}[kind]
            sums, counts = [], []
            for v in range(4):
                acc, num = None, 0.0
                for u in us:
                    acc = kappa[u][v] if acc is None else acc + kappa[u][v]
                    num = num + there_x[(u + 1) // 2]
                sums.append(acc)
                counts.append(num * there_y[(v + 1) // 2])
            for ey in range(2):
                kappa_sum = pick(sums, ey)
                mult = pick(counts, ey) * count_z
                for a in {0: (0,), 1: range(1, 7), 2: (7,)}[kind]:
                    diag = (float(LINE[a]) + line) * kappa_sum + sigma_p * mult
                    inv_diag[ex, a, ey] = 1.0 / (diag * (float(WEIGHTS[a]) * weight))


OUTER = ((0, 0), (1, 7))


def got_y_sum(place, tile, ch, ex, a, ey, y_first, y_second):
    row = pl.ds(ch * 16 + ex * 8 + a, 1)
    got_a, got_b = y_first[row, :], y_second[row, :]
    if ey == 0:
        tile = tile + jnp.where(place.row == 0, place.before_y(got_a, got_b), 0.0)
    else:
        tile = tile + jnp.where(place.row == 7, place.after_y(got_a, got_b), 0.0)
    return tile


def got_x_sum(place, tile, ch, ex, ey, x_first, x_second):
    rows = pl.ds(ch * 16 + ey * 8, 8)
    pick = place.before_x if ex == 0 else place.after_x
    return tile + pick(x_first[rows, :], x_second[rows, :])


def facts_kernel(pack, facts):
    place = Place()
    grid = pltpu.roll(pack[pl.ds(0, 1), :], (place.iy % 4) * (LANES // 4), 1)
    facts[:, pl.ds(0, LANES)] = jnp.zeros((1, LANES), jnp.float32)
    facts[:, pl.ds(LANES, LANES)] = grid
    for c in range(NCD):
        facts[:, pl.ds((2 + c) * LANES, LANES)] = pack[pl.ds(1 + c, 1), :]


def prepare_kernel(
    summed, visc, y_first, y_second, ctab, zmat, start, part, slope, answer, grad_z, flux_z
):
    place = Place()
    weight = ctab[T_W]
    inv_mass = [1.0 / (weight * place.mult_tile(ey)) for ey in range(2)]

    def begin(ch, carry):
        for ex in range(2):
            for a in range(8):
                for ey in range(2):
                    tile = got_y_sum(
                        place, summed[ch, ex, a, ey], ch, ex, a, ey, y_first, y_second
                    )
                    scale = place.inv_x(ex, a) * float(1.0 / WEIGHTS[a])
                    start[ch, ex, a, ey] = tile * (inv_mass[ey] * scale)
        return carry

    lax.fori_loop(0, 4, begin, 0)
    grad_z[...] = along_z(start[...].reshape(1024, LANES), zmat[0]).reshape(grad_z.shape)

    def column(index, carry):
        ch, ey = index // 2, index % 2
        coef = jnp.where(ch == 3, 1.0 / prandtl, 1.0)
        for ex in range(2):
            grad_x = along_x(DERIV, [start[ch, ex, a, ey] for a in range(8)], -1)
            flux_x = [
                visc[ex, a, ey] * (float(WEIGHTS[a]) * weight) * coef * grad_x[a]
                for a in range(8)
            ]
            back = along_x(DERIV.T, flux_x, -1)
            for a in range(8):
                if (ex, a) in OUTER:
                    slope[ch, ex, ey] = grad_x[a]
                    part[ch, ex, a, ey] = back[a]
                    continue
                rest, flux_z[ch, ex, a, ey] = across(
                    ctab, weight, a, coef, start[ch, ex, a, ey], grad_z[ch, ex, a, ey],
                    start[1, ex, a, ey], start[2, ex, a, ey], visc[ex, a, ey],
                )
                flow = float(WEIGHTS[a]) * weight * start[0, ex, a, ey]
                part[ch, ex, a, ey] = rest + flow * grad_x[a] + back[a]
        return carry

    for ex, outer in OUTER:
        for ey in range(2):
            flux_x = [
                visc[ex, a, ey] * (float(WEIGHTS[a] * DERIV[a, outer]) * weight) for a in range(8)
            ]
            back = along_x(DERIV.T, flux_x, -1)
            for a in range(8):
                answer[ex, a, ey] = back[a]
    lax.fori_loop(0, 8, column, 0)
    for ch in range(4):
        for ex in range(2):
            inner = pl.ds(1 - ex, 7)
            back = along_z(flux_z[ch, ex, inner].reshape(112, LANES), zmat[1])
            part[ch, ex, inner] = part[ch, ex, inner] + back.reshape(7, 2, 8, LANES)


def across(ctab, weight, a, coef, value, grad_z, flow_y, flow_z, visc):
    node = float(WEIGHTS[a]) * weight
    grad_y = along_y(ctab, T_D, value)
    nu = visc * node * coef
    part = node * (flow_y * grad_y + flow_z * grad_z) + along_y(ctab, T_DT, nu * grad_y)
    return part, nu * grad_z


def rhs_kernel(
    pack_rows,
    begun,
    given,
    slope,
    answer,
    visc,
    pack,
    x_first,
    x_second,
    ctab,
    zmat,
    share,
    xf,
    inner_x,
    first,
    second,
    edge,
    edge_z,
    edge_part,
    came,
):
    place = Place()
    weight = ctab[T_W]
    inv_mass = [1.0 / (weight * place.mult_tile(ey)) for ey in range(2)]
    for ch in range(4):
        for side, (ex, a) in enumerate(OUTER):
            scale = place.inv_x(ex, a) * float(1.0 / WEIGHTS[a])
            for ey in range(2):
                zero = jnp.zeros(TILE, jnp.float32)
                extra = got_x_sum(place, zero, ch, ex, ey, x_first, x_second)
                extra = extra * (inv_mass[ey] * scale)
                came[ch, side, ey] = extra
                edge[ch, side, ey] = begun[ch, ex, a, ey] + extra
    edge_z[...] = along_z(edge[...].reshape(128, LANES), zmat[0]).reshape(edge.shape)
    for ch in range(4):
        coef = 1.0 / prandtl if ch == 3 else 1.0
        for side, (ex, a) in enumerate(OUTER):
            for ey in range(2):
                parts = across(
                    ctab, weight, a, coef, edge[ch, side, ey], edge_z[ch, side, ey],
                    edge[1, side, ey], edge[2, side, ey], visc[ex, a, ey],
                )
                edge_part[ch, side, ey], edge_z[ch, side, ey] = parts
    edge_part[...] = edge_part[...] + along_z(
        edge_z[...].reshape(128, LANES), zmat[1]
    ).reshape(edge.shape)

    def side_of(ch, ex, a, ey):
        outer = OUTER[ex][1]
        coef = jnp.where(ch == 3, 1.0 / prandtl, 1.0)
        extra = came[ch, ex, ey]
        node = float(WEIGHTS[a]) * weight
        turn = float(DERIV[a, outer])
        if a == outer:
            known = given[ch, ex, a, ey] + edge_part[ch, ex, ey]
            known = known + node * edge[0, ex, ey] * (slope[ch, ex, ey] + turn * extra)
            return known + extra * (coef * answer[ex, a, ey])
        flow = float(WEIGHTS[a] * turn) * weight * begun[0, ex, a, ey]
        return given[ch, ex, a, ey] + extra * (coef * answer[ex, a, ey] + flow)

    def finish(ch, carry):
        tiles = [
            [[place.join_z(-side_of(ch, ex, a, ey)) for ey in range(2)] for a in range(8)]
            for ex in range(2)
        ]
        join_own(place, tiles)
        for ex in range(2):
            for a in range(8):
                scale = place.inv_x(ex, a) * float(dt_step / WEIGHTS[a])
                for ey in range(2):
                    value = edge[ch, ex, ey] if (ex, a) in OUTER else begun[ch, ex, a, ey]
                    part = value * (place.share_y(ey) * place.share_x(ex, a))
                    share[ch, ex, a, ey] = part + tiles[ex][a][ey] * (inv_mass[ey] * scale)
        return carry

    lax.fori_loop(0, 4, finish, 0)
    for ch in range(4):
        store_y_faces(place, share, first, second, (ch,), ch * 16)
        for ey in range(2):
            xf[0, ch, ey] = share[ch, 0, 0, ey]
            xf[1, ch, ey] = share[ch, 1, 7, ey]

    def column_of(ex, ey):
        return [share[0, ex, a, ey] for a in range(8)]

    def tile_of(ex, a, ey):
        return share[1, ex, a, ey]

    store_inner(
        place, DERIV, ctab[T_BOTTOM], ctab[T_TOP], column_of, tile_of, inner_x, first, second,
        STEP_V, STEP_EDGE,
    )
    beside = pl.ds(64, pack_rows)
    parts = (
        place.before_x(x_first[beside, :], x_second[beside, :]),
        pack[...],
        place.after_x(x_first[beside, :], x_second[beside, :]),
    )
    for k in range(3):
        rows = pl.ds(STEP_PACK + k * pack_rows, pack_rows)
        first[rows, :] = parts[k]
        second[rows, :] = parts[k]


def store_inner(
    place, matrix, bottom, top, column_of, tile_of, inner_x, first, second, at, edge
):
    for ey in range(2):
        low, high = column_of(0, ey), column_of(1, ey)
        below = float(matrix[0, 1]) * low[1]
        above = float(matrix[7, 0]) * high[0]
        for k in range(2, 8):
            below = below + float(matrix[0, k]) * low[k]
            above = above + float(matrix[7, k - 1]) * high[k - 1]
        inner_x[0, ey] = below
        inner_x[1, ey] = above
    for side in range(2):
        low = inner_x[side, 0, pl.ds(0, 1), :]
        high = inner_x[side, 1, pl.ds(7, 1), :]
        first[pl.ds(edge + side, 1), :] = place.send_y(high, low)
        second[pl.ds(edge + side, 1), :] = place.send_y(low, high)
    for ex in range(2):
        for a in range(8):
            low = jnp.sum(bottom * tile_of(ex, a, 0), axis=0, keepdims=True)
            high = jnp.sum(top * tile_of(ex, a, 1), axis=0, keepdims=True)
            row = pl.ds(at + ex * 8 + a, 1)
            first[row, :] = place.send_y(high, low)
            second[row, :] = place.send_y(low, high)


def cross_flow(place, ctab, flow, slopes, rows, inv_y, inv_z):
    below, above = rows
    below = (below - float(DERIV[0, 0]) * flow[0]) * jnp.where(place.prev_y, 1.0, 0.0)
    above = (above - float(DERIV[7, 7]) * flow[1]) * jnp.where(place.next_y, 1.0, 0.0)
    grad_y = list(place.join_y(*[along_y(ctab, T_D, tile) for tile in flow]))
    grad_y[0] = grad_y[0] + jnp.where(place.row == 0, below, 0.0)
    grad_y[1] = grad_y[1] + jnp.where(place.row == 7, above, 0.0)
    return [grad_y[ey] * inv_y[ey] + place.join_z(slopes[ey]) * inv_z for ey in range(2)]


def approach_kernel(share, y_first, y_second, ctab, zmat, fields_new, part, grad_z):
    place = Place()

    def step(ch, carry):
        for ex in range(2):
            for a in range(8):
                for ey in range(2):
                    fields_new[ch, ex, a, ey] = got_y_sum(
                        place, share[ch, ex, a, ey], ch, ex, a, ey, y_first, y_second
                    )
        return carry

    lax.fori_loop(0, 4, step, 0)
    grad_z[...] = along_z(fields_new[2].reshape(256, LANES), zmat[0]).reshape(grad_z.shape)
    inv_y = [place.inv_y(ey) for ey in range(2)]
    inv_z = place.inv_z()
    for ex in range(2):
        for a in range(8):
            if (ex, a) in OUTER:
                continue
            flow = [fields_new[1, ex, a, ey] for ey in range(2)]
            rows = inner_along_y(place, y_first, y_second, None, None, ex, a, STEP_V, STEP_EDGE)
            slopes = [grad_z[ex, a, ey] for ey in range(2)]
            both = cross_flow(place, ctab, flow, slopes, rows, inv_y, inv_z)
            part[ex, a, 0], part[ex, a, 1] = both


def emit_kernel(begun, x_first, x_second, extra, fields_new, passed):
    place = Place()
    passed[...] = extra[...]
    fields_new[...] = begun[...]
    for ch in range(4):
        for ex, a in OUTER:
            for ey in range(2):
                fields_new[ch, ex, a, ey] = got_x_sum(
                    place, begun[ch, ex, a, ey], ch, ex, ey, x_first, x_second
                )


def advance_kernel(
    begun,
    given,
    y_first,
    y_second,
    x_first,
    x_second,
    inv_diag,
    kap,
    grp,
    ctab,
    zmat,
    resid,
    own,
    msg,
    grad_z,
    scaled,
    edge,
    part,
    outer,
):
    place = Place()
    weight = ctab[T_W]

    def before(row, count=8):
        rows = pl.ds(row, count)
        return place.before_x(x_first[rows, :], x_second[rows, :])

    def after(row, count=8):
        rows = pl.ds(row, count)
        return place.after_x(x_first[rows, :], x_second[rows, :])

    part[...] = given[...]
    for ch in range(3):
        for side, (ex, a) in enumerate(OUTER):
            for ey in range(2):
                outer[ch, side, ey] = got_x_sum(
                    place, begun[ch, ex, a, ey], ch, ex, ey, x_first, x_second
                )
    edge[...] = along_z(outer[2].reshape(32, LANES), zmat[0]).reshape(edge.shape)
    inv_y = [place.inv_y(ey) for ey in range(2)]
    inv_z = place.inv_z()
    for side, (ex, a) in enumerate(OUTER):
        flow = [outer[1, side, ey] for ey in range(2)]
        rows = inner_along_y(place, y_first, y_second, before, after, ex, a, STEP_V, STEP_EDGE)
        slopes = [edge[side, ey] for ey in range(2)]
        both = cross_flow(place, ctab, flow, slopes, rows, inv_y, inv_z)
        part[ex, a, 0], part[ex, a, 1] = both
    slope = [[None, None], [None, None]]
    for ey in range(2):
        for ex in range(2):
            line = [
                outer[0, ex, ey] if (ex, a) in OUTER else begun[0, ex, a, ey] for a in range(8)
            ]
            slope[ex][ey] = along_x(DERIV, line, -1)
        mid = 0.5 * (slope[0][ey][7] + slope[1][ey][0])
        slope[0][ey][7] = mid
        slope[1][ey][0] = mid
        low, high = slope[0][ey][0], slope[1][ey][7]
        inner_low = low - float(DERIV[0, 0]) * outer[0, 0, ey] + before(STEP_U + ey * 8)
        inner_high = high - float(DERIV[7, 7]) * outer[0, 1, ey] + after(STEP_U + ey * 8)
        slope[0][ey][0] = jnp.where(place.prev_x, 0.5 * inner_low, low)
        slope[1][ey][7] = jnp.where(place.next_x, 0.5 * inner_high, high)
    sums = [[jnp.zeros(TILE, jnp.float32) for _ in range(2)] for _ in range(2)]
    inv_mult = [1.0 / place.mult_tile(ey) for ey in range(2)]
    mass = [weight * place.mult_tile(ey) for ey in range(2)]
    for ex in range(2):
        for a in range(8):
            for ey in range(2):
                div = slope[ex][ey][a] + part[ex, a, ey]
                value = div * (mass[ey] * (place.mult_x(ex, a) * float(-WEIGHTS[a])))
                resid[ex, a, ey] = value
                scaled[ex, a, ey] = value * inv_diag[ex, a, ey] * float(1.0 / THETA)
                sums[ex][ey] = sums[ex][ey] + value * (inv_mult[ey] * place.inv_x(ex, a))
    grad_z[...] = along_z(scaled[...].reshape(256, LANES), zmat[2]).reshape(grad_z.shape)
    tiles = [[[None, None] for _ in range(8)] for _ in range(2)]
    for ex in range(2):
        for ey in range(2):
            images = own_operator(ctab, kap, scaled, grad_z, ex, ey)[1]
            for a in range(8):
                tiles[ex][a][ey] = place.join_z(images[a])
    join_own(place, tiles)
    for ex in range(2):
        for a in range(8):
            for ey in range(2):
                own[ex, a, ey] = tiles[ex][a][ey]
    row = message(place, restricted(place, sums, grp), [])
    blank = jnp.where(place.row == 0, jnp.broadcast_to(row, TILE), 0.0)

    def clear(i, carry):
        msg[i] = blank
        return carry

    lax.fori_loop(0, msg.shape[0], clear, 0, unroll=msg.shape[0] <= 64)
    across = Pairing(place)
    for side, (ex, a) in enumerate(OUTER):
        there, ix = across.beside(side)

        @pl.when(there)
        def _():
            msg[ix * place.ny + place.iy] = own[ex, a, 0]
            msg[ix * place.ny + across.twin, pl.ds(1, 7), :] = own[ex, a, 1, pl.ds(1, 7), :]

        @pl.when(there & across.has_far)
        def _():
            msg[ix * place.ny + across.far, pl.ds(1, 1), :] = across.far_row(own, ex, a)

    @pl.when(across.has_far)
    def _():
        for a in range(8):
            msg[place.ix * place.ny + across.far, pl.ds(a, 1), :] = across.far_row(own, 0, a)
            if a > 0:
                to = place.ix * place.ny + across.beyond
                msg[to, pl.ds(a, 1), :] = across.far_row(own, 1, a)


def inner_along_y(place, y_first, y_second, before, after, ex, a, at, edge):
    row = pl.ds(at + ex * 8 + a, 1)
    got_a, got_b = y_first[row, :], y_second[row, :]
    below, above = place.before_y(got_a, got_b), place.after_y(got_a, got_b)
    if before is None:
        return below, above
    if (ex, a) == (0, 0):
        below = below + before(edge, 1)
        above = above + before(edge + 1, 1)
    if (ex, a) == (1, 7):
        below = below + after(edge, 1)
        above = above + after(edge + 1, 1)
    return below, above


class Pairing:
    def __init__(self, place):
        self.place = place
        even = place.even_y
        self.even = even
        self.twin = jnp.where(even, place.iy + 1, place.iy - 1)
        self.far = jnp.where(even, place.iy - 1, place.iy + 1)
        self.has_far = jnp.where(even, place.iy - 1, place.ny - 2 - place.iy) >= 0
        self.beyond = jnp.where(even, place.iy - 2, place.iy + 2)
        self.twin_far = jnp.where(even, place.iy + 2, place.iy - 2)
        self.twin_has_far = jnp.where(even, place.ny - 3 - place.iy, place.iy - 2) >= 0

    def beside(self, side):
        place = self.place
        if side == 0:
            return place.prev_x, place.ix - 1
        return place.next_x, place.ix + 1

    def far_row(self, field, ex, a):
        low = field[ex, a, 0, pl.ds(0, 1), :]
        return jnp.where(self.even, low, field[ex, a, 1, pl.ds(7, 1), :])

    def twin_row(self, field, ex, a):
        low = field[ex, a, 0, pl.ds(0, 1), :]
        return jnp.where(self.even, field[ex, a, 1, pl.ds(7, 1), :], low)


RELAY_FACE, RELAY_EDGE, RELAY_ROWS = 24, 40, 42


def relay_kernel(got, own, out):
    place = Place()
    across = Pairing(place)
    out[...] = jnp.zeros(out.shape, jnp.float32)
    for side in range(2):
        there, ix = across.beside(side)

        @pl.when(there)
        def _():
            out[pl.ds(side * 8, 8), :] = got[ix * place.ny + across.twin]
            corner = got[ix * place.ny + place.iy, pl.ds(0, 1), :]
            out[pl.ds(RELAY_EDGE + side, 1), :] = corner

    @pl.when(across.twin_has_far)
    def _():
        out[pl.ds(16, 8), :] = got[place.ix * place.ny + across.twin_far]

    for ex in range(2):
        for a in range(8):
            out[pl.ds(RELAY_FACE + ex * 8 + a, 1), :] = across.twin_row(own, ex, a)


SMOOTH_X, SMOOTH_Y, SMOOTH_EDGE, SMOOTH_ROWS = 16, 16, 32, 34


def turn_smooth_kernel(own, inner_x, y_first, y_second, first, second):
    place = Place()
    sides = []
    for side, (ex, a) in enumerate(((0, 0), (1, 7))):
        row = pl.ds(15 * side, 1)
        got_a, got_b = y_first[row, :], y_second[row, :]
        low = own[ex, a, 0] + jnp.where(place.row == 0, place.before_y(got_a, got_b), 0.0)
        high = own[ex, a, 1] + jnp.where(place.row == 7, place.after_y(got_a, got_b), 0.0)
        sides.append((low, high))
    for ey in range(2):
        rows = pl.ds(ey * 8, 8)
        first[rows, :] = place.send_x(sides[1][ey], sides[0][ey])
        second[rows, :] = place.send_x(sides[0][ey], sides[1][ey])
    turn_edges(
        place, inner_x, y_first, y_second, first, second, SMOOTH_X, SMOOTH_EDGE, SMOOTH_Y
    )


def restricted(place, sums, grp):
    values = []
    for c in range(NCD):
        acc = jnp.zeros(TILE, jnp.float32)
        for ex in range(2):
            for ey in range(2):
                group = grp[pl.ds((ex + 1) * 4 + ey + 1, 1), :]
                acc = acc + jnp.where(group == float(c), sums[ex][ey], 0.0)
        values.append(total(acc))
    return values


AWAY = 16
BEYOND = 18


def message(place, own_values, scalars, away=0, beyond=1):
    lane = lax.broadcasted_iota(jnp.int32, (1, LANES), 1)
    spot = (place.ix * place.ny + place.iy) % (LANES // NCD)
    after = (spot + beyond) % (LANES // NCD)
    spot = (spot + away) % (LANES // NCD)
    row = jnp.zeros((1, LANES), jnp.float32)
    for c, value in enumerate(own_values):
        row = row + jnp.where(lane == spot * NCD + c, value, 0.0)
    for c, value in enumerate(scalars):
        if value is None:
            continue
        row = row + jnp.where(lane == after * NCD + c, value, 0.0)
    return row


def send_to_all(msg, row):
    def send(i, carry):
        msg[i] = row
        return carry

    lax.fori_loop(0, msg.shape[0], send, 0, unroll=msg.shape[0] <= 64)


def cross_image(place, ctab, kap, value, flat, inner, ex, ey):
    slope_y = along_y(ctab, T_K, value)
    turned_y = inner + float(SCALED[0, 0]) * value
    own = kap[pl.ds((ex + 1) * 4 + ey + 1, 1), :] * (slope_y + flat) + sigma_p * value
    beyond = kap[pl.ds((ex + 1) * 4 + 3 * ey, 1), :] * (turned_y + flat) + sigma_p * value
    return own + jnp.where(beyond_y(place, ey), beyond, 0.0), slope_y, turned_y


def beyond_y(place, ey):
    if ey == 0:
        return (place.row == 0) & place.prev_y
    return (place.row == 7) & place.next_y


def ready_kernel(
    own, y_first, y_second, inv_diag, kap, ctab, zmat, image, scaled, part, slope_z
):
    place = Place()
    for ex in range(2):
        for a in range(8):
            for ey in range(2):
                tile = got_y_sum(place, own[ex, a, ey], 0, ex, a, ey, y_first, y_second)
                image[ex, a, ey] = tile
                scaled[ex, a, ey] = tile * inv_diag[ex, a, ey] * float(1.0 / THETA)
    slope_z[...] = along_z(scaled[...].reshape(256, LANES), zmat[2]).reshape(slope_z.shape)
    for ex in range(2):
        for a in range(8):
            if (ex, a) in OUTER:
                continue
            rows = inner_along_y(
                place, y_first, y_second, None, None, ex, a, SMOOTH_Y, SMOOTH_EDGE
            )
            for ey in range(2):
                part[ex, a, ey] = cross_image(
                    place, ctab, kap, scaled[ex, a, ey], slope_z[ex, a, ey], rows[ey], ex, ey
                )[0]


def smooth_kernel(
    begun,
    begun_scaled,
    given,
    y_first,
    y_second,
    x_first,
    x_second,
    inv_diag,
    kap,
    grp,
    extra,
    facts,
    ctab,
    zmat,
    image,
    smoothed,
    msg,
    scaled,
    slope_z,
    edge,
):
    place = Place()
    weight = ctab[T_W]
    corner = float(SCALED[0, 0])

    def before(row, count=8):
        rows = pl.ds(row, count)
        return place.before_x(x_first[rows, :], x_second[rows, :])

    def after(row, count=8):
        rows = pl.ds(row, count)
        return place.after_x(x_first[rows, :], x_second[rows, :])

    image[...] = begun[...]
    scaled[...] = begun_scaled[...]
    for side, (ex, a) in enumerate(OUTER):
        for ey in range(2):
            tile = got_x_sum(place, begun[ex, a, ey], 0, ex, ey, x_first, x_second)
            image[ex, a, ey] = tile
            scaled[ex, a, ey] = tile * inv_diag[ex, a, ey] * float(1.0 / THETA)
            edge[side, ey] = scaled[ex, a, ey]
    edge[...] = along_z(edge[...].reshape(32, LANES), zmat[2]).reshape(edge.shape)
    there_x = (place.prev_x, place.next_x)
    zero = jnp.zeros(TILE, jnp.float32)
    tiles = [[[None, None] for _ in range(8)] for _ in range(2)]
    for ex in range(2):
        a_out = OUTER[ex][1]
        rows = inner_along_y(
            place, y_first, y_second, before, after, ex, a_out, SMOOTH_Y, SMOOTH_EDGE
        )
        for ey in range(2):
            values = [scaled[ex, a, ey] for a in range(8)]
            slopes = along_x(SCALED, values, 1)
            far_row = beyond_y(place, ey)
            beside = kap[pl.ds((ex + 1) * 4 + 3 * ey, 1), :]
            kappa = kap[pl.ds((ex + 1) * 4 + ey + 1, 1), :] + jnp.where(far_row, beside, 0.0)
            for a in range(8):
                if a != a_out:
                    acc = given[ex, a, ey]
                else:
                    value, flat = values[a], edge[ex, ey]
                    acc, slope_y, turned_y = cross_image(
                        place, ctab, kap, value, flat, rows[ey], ex, ey
                    )
                    x_next = 3 * ex
                    get = before if ex == 0 else after
                    turned_x = get(SMOOTH_X + ey * 8) + corner * value
                    side = kap[pl.ds(x_next * 4 + ey + 1, 1), :] * (turned_x + slope_y + flat)
                    far = kap[pl.ds(x_next * 4 + 3 * ey, 1), :] * (turned_x + turned_y + flat)
                    side = side + sigma_p * value
                    side = side + jnp.where(far_row, far + sigma_p * value, zero)
                    acc = acc + jnp.where(there_x[ex], side, zero)
                acc = acc + kappa * slopes[a]
                tiles[ex][a][ey] = place.join_z(acc * (float(WEIGHTS[a]) * weight))
    join_own(place, tiles)
    inv_mult = [1.0 / place.mult_tile(ey) for ey in range(2)]
    sums = [[jnp.zeros(TILE, jnp.float32) for _ in range(2)] for _ in range(2)]
    square = jnp.zeros(TILE, jnp.float32)
    for ex in range(2):
        for a in range(8):
            for ey in range(2):
                value = image[ex, a, ey]
                defect = (value - tiles[ex][a][ey]) * inv_diag[ex, a, ey]
                update = scaled[ex, a, ey]
                result = (
                    float(1.0 + RHO_NEXT * RHO) * update + float(2.0 * RHO_NEXT / DELTA) * defect
                )
                smoothed[ex, a, ey] = result
                weighed = value * (inv_mult[ey] * place.inv_x(ex, a))
                sums[ex][ey] = sums[ex][ey] + weighed
                square = square + weighed * result
    own_sums = restricted(place, sums, grp)
    if msg.shape[2] == LANES:
        sums = [extra[:, pl.ds(k, 1)] for k in range(2)]
        send_to_all(msg, message(place, own_sums, sums))
        return
    slope_z[...] = along_z(smoothed[...].reshape(256, LANES), zmat[2]).reshape(slope_z.shape)
    energy = jnp.zeros(TILE, jnp.float32)
    for ex in range(2):
        for ey in range(2):
            values, images = own_operator(ctab, kap, smoothed, slope_z, ex, ey)
            for a in range(8):
                energy = energy + values[a] * images[a]
                tiles[ex][a][ey] = place.join_z(images[a])
    join_own(place, tiles)
    sums = [extra[:, pl.ds(k, 1)] for k in range(2)] + [total(square), total(energy)]
    row = message(place, own_sums, sums, AWAY, BEYOND)
    row = row + restricted_around(place, tiles, inv_mult, grp)
    send_to_all(msg, jnp.concatenate([row, facts[:, LANES:]], axis=1))


def restricted_around(place, tiles, inv_mult, grp):
    lane = lax.broadcasted_iota(jnp.int32, (1, LANES), 1)
    weighed = [
        [[tiles[ex][a][ey] * (inv_mult[ey] * place.inv_x(ex, a)) for ey in range(2)] for a in range(8)]
        for ex in range(2)
    ]

    def rows_of(tile, y):
        if y == 0:
            return jnp.where(place.row == 0, tile[0], 0.0)
        if y == 3:
            return jnp.where(place.row == 7, tile[1], 0.0)
        return tile[y - 1]

    there_x = (place.prev_x, None, None, place.next_x)
    there_y = (place.prev_y, None, None, place.next_y)
    by_device = [
        [[jnp.zeros(TILE, jnp.float32) for _ in range(NCD)] for _ in range(3)] for _ in range(3)
    ]
    for x in range(4):
        for y in range(4):
            if x == 0:
                acc = rows_of(weighed[0][0], y)
            elif x == 3:
                acc = rows_of(weighed[1][7], y)
            else:
                acc = rows_of(weighed[x - 1][0], y)
                for a in range(1, 8):
                    acc = acc + rows_of(weighed[x - 1][a], y)
            for there in (there_x[x], there_y[y]):
                if there is not None:
                    acc = jnp.where(there, acc, 0.0)
            group = grp[pl.ds(x * 4 + y, 1), :]
            device = by_device[(x + 1) // 2][(y + 1) // 2]
            for c in range(NCD):
                device[c] = device[c] + jnp.where(group == float(c), acc, 0.0)
    row = jnp.zeros((1, LANES), jnp.float32)
    for dx in range(3):
        for dy in range(3):
            at = ((place.ix + dx - 1) * place.ny + place.iy + dy - 1) * NCD
            for c in range(NCD):
                row = row + jnp.where(lane == at + c, total(by_device[dx][dy][c]), 0.0)
    return row


def coarse_part(place, blocks, got, coarse, grp, others=()):
    lane = lax.broadcasted_iota(jnp.int32, (1, LANES), 1)
    values = [jnp.zeros((1, LANES), jnp.float32) for _ in range(blocks)]
    per = LANES // NCD
    for j in range(blocks):

        def gather(i, acc, j=j):
            return jnp.where(lane // NCD == i, got[j * per + i, pl.ds(0, 1), :], acc)

        values[j] = lax.fori_loop(0, per, gather, values[j], unroll=blocks == 1)
        for there, device, row in others:
            spot = (lane // NCD == device % per) & (device // per == j) & there
            values[j] = jnp.where(spot, row, values[j])

    def solved(dx, dy, c):
        acc = None
        for j in range(blocks):
            term = coarse[pl.ds(((dx * 3 + dy) * NCD + c) * blocks + j, 1), :] * values[j]
            acc = term if acc is None else acc + term
        return jnp.sum(acc, axis=1, keepdims=True)

    return prolonged(place, solved, grp)


def prolonged(place, solved, grp):
    device = [[[solved(dx, dy, c) for c in range(NCD)] for dy in range(3)] for dx in range(3)]
    inv_z = jnp.where(place.low_z | place.high_z, 0.5, 1.0)
    rows = []
    for x in range(4):
        line = []
        for y in range(4):
            group = grp[pl.ds(x * 4 + y, 1), :]
            acc = jnp.zeros((1, LANES), jnp.float32)
            for c in range(NCD):
                acc = acc + jnp.where(
                    group == float(c), device[(x + 1) // 2][(y + 1) // 2][c], 0.0
                )
            line.append(place.join_z(jnp.broadcast_to(acc, TILE)) * inv_z)
        rows.append(line)
    low_y = jnp.where(place.prev_y, 0.5, 1.0)
    high_y = jnp.where(place.next_y, 0.5, 1.0)

    def tile(ex, kind, ey):
        if kind == 1:
            vals = [rows[ex + 1][y] for y in range(4)]
        elif kind == 0:
            scale = place.inv_x(ex, 0)
            vals = [(rows[ex][y] + rows[ex + 1][y]) * scale for y in range(4)]
        else:
            scale = place.inv_x(ex, 7)
            vals = [(rows[ex + 1][y] + rows[ex + 2][y]) * scale for y in range(4)]
        mid = vals[ey + 1]
        low = (vals[ey] + mid) * (low_y if ey == 0 else 0.5)
        high = (mid + vals[ey + 2]) * (high_y if ey == 1 else 0.5)
        return jnp.where(place.row == 0, low, jnp.where(place.row == 7, high, mid))

    return tile


def kind_of(a):
    return 0 if a == 0 else (2 if a == 7 else 1)


def own_operator(ctab, kap, field, slope_z, ex, ey):
    weight = ctab[T_W]
    tiles = [field[ex, a, ey] for a in range(8)]
    slopes = along_x(SCALED, tiles, 1)
    kappa = kap[pl.ds((ex + 1) * 4 + ey + 1, 1), :]
    out = []
    for a in range(8):
        stiff = slopes[a] + along_y(ctab, T_K, tiles[a]) + slope_z[ex, a, ey]
        out.append((kappa * stiff + sigma_p * tiles[a]) * (float(WEIGHTS[a]) * weight))
    return tiles, out


def first_direction_kernel(
    blocks,
    got,
    relayed,
    coarse,
    grp,
    kap,
    inv_diag,
    resid,
    own,
    ctab,
    zmat,
    direction,
    out,
    inner_x,
    first,
    second,
    extra,
    slope_z,
    image,
):
    place = Place()
    inv_mult = [1.0 / place.mult_tile(ey) for ey in range(2)]
    across = Pairing(place)
    others = []
    for side in range(2):
        there, ix = across.beside(side)
        others.append((there, ix * place.ny + place.iy, relayed[pl.ds(side * 8, 1), :]))
    others.append(
        (across.has_far, place.ix * place.ny + across.far, relayed[pl.ds(16, 1), :])
    )
    part = coarse_part(place, blocks, got, coarse, grp, others)
    image[...] = own[...]
    far_edge = jnp.where(across.even, 0, 7)

    def add_row(ex, a, row, edge, low):
        extra = jnp.where(place.row == edge, row, 0.0)
        image[ex, a, 0] = image[ex, a, 0] + jnp.where(low, extra, 0.0)
        image[ex, a, 1] = image[ex, a, 1] + jnp.where(low, 0.0, extra)

    for ex in range(2):
        for a in range(8):
            row = relayed[pl.ds(RELAY_FACE + ex * 8 + a, 1), :]
            add_row(ex, a, row, 7 - far_edge, ~across.even)

    @pl.when(across.has_far)
    def _():
        for a in range(8):
            row = got[place.ix * place.ny + across.far, pl.ds(a, 1), :]
            add_row(0, a, row, far_edge, across.even)
            if a == 7:
                add_row(1, 0, row, far_edge, across.even)
            if a > 0:
                add_row(1, a, relayed[pl.ds(16 + a, 1), :], far_edge, across.even)

    for side, (ex, a) in enumerate(OUTER):
        there, ix = across.beside(side)

        @pl.when(there)
        def _():
            low = got[ix * place.ny + place.iy]
            high = jnp.where(
                place.row == 0, pltpu.roll(low, 1, 0), relayed[pl.ds(side * 8, 8), :]
            )
            image[ex, a, 0] = image[ex, a, 0] + low
            image[ex, a, 1] = image[ex, a, 1] + high
            corner = jnp.where(
                across.even,
                relayed[pl.ds(RELAY_EDGE + side, 1), :],
                got[ix * place.ny + across.twin, pl.ds(7, 1), :],
            )
            add_row(ex, a, corner, 7 - far_edge, ~across.even)

        @pl.when(there & across.has_far)
        def _():
            corner = got[ix * place.ny + across.far, pl.ds(1, 1), :]
            add_row(ex, a, corner, far_edge, across.even)

    energy = jnp.zeros(TILE, jnp.float32)
    for ex in range(2):
        for ey in range(2):
            kinds = [part(ex, kind, ey) for kind in range(3)]
            for a in range(8):
                known = resid[ex, a, ey]
                inverse = inv_diag[ex, a, ey]
                defect = (known - image[ex, a, ey]) * inverse
                value = (
                    float((1.0 + RHO_NEXT * RHO) / THETA) * (known * inverse)
                    + float(2.0 * RHO_NEXT / DELTA) * defect
                    + kinds[kind_of(a)]
                )
                direction[ex, a, ey] = value
                scale = place.inv_x(ex, a)
                energy = energy + value * known * (inv_mult[ey] * scale)
    slope_z[...] = along_z(direction[...].reshape(256, LANES), zmat[2]).reshape(slope_z.shape)
    curvature = jnp.zeros(TILE, jnp.float32)
    tiles = [[[None, None] for _ in range(8)] for _ in range(2)]
    for ex in range(2):
        for ey in range(2):
            values, images = own_operator(ctab, kap, direction, slope_z, ex, ey)
            for a in range(8):
                curvature = curvature + values[a] * images[a]
                tiles[ex][a][ey] = place.join_z(images[a])
    join_own(place, tiles)
    for ex in range(2):
        for a in range(8):
            for ey in range(2):
                out[ex, a, ey] = tiles[ex][a][ey]
    store_y_faces(place, out, first, second, (), 0)

    def tile_of(ex, a, ey):
        return tiles[ex][a][ey] * inv_diag[ex, a, ey] * float(1.0 / THETA)

    def column_of(ex, ey):
        return [tile_of(ex, a, ey) for a in range(8)]

    store_inner(
        place, SCALED, ctab[T_KBOTTOM], ctab[T_KTOP], column_of, tile_of, inner_x, first, second,
        SMOOTH_Y, SMOOTH_EDGE,
    )
    lane = lax.broadcasted_iota(jnp.int32, (1, LANES), 1)
    extra[...] = jnp.where(lane == 0, total(energy), total(curvature))


def gathered_scalars(got, count):
    lane = lax.broadcasted_iota(jnp.int32, (1, LANES), 1)
    per = LANES // NCD
    sums = []
    for c in range(count):
        acc = jnp.zeros((1, LANES), jnp.float32)

        def gather(i, acc, c=c):
            return acc + jnp.where(lane == ((i + 1) % per) * NCD + c, got[i], 0.0)

        acc = lax.fori_loop(0, got.shape[0], gather, acc, unroll=got.shape[0] <= per)
        sums.append(jnp.sum(acc, axis=1, keepdims=True))
    return sums


def second_direction_kernel(
    blocks,
    got,
    coarse,
    grp,
    kap,
    resid,
    direction,
    image,
    smoothed,
    ctab,
    zmat,
    following,
    known,
    msg,
    slope_z,
):
    place = Place()
    inv_mult = [1.0 / place.mult_tile(ey) for ey in range(2)]
    part = coarse_part(place, blocks, got, coarse, grp)
    energy, curvature = gathered_scalars(got, 2)
    step = energy / curvature
    lane = lax.broadcasted_iota(jnp.int32, (1, LANES), 1)
    known[...] = jnp.where(lane == 0, energy, jnp.where(lane == 1, curvature, 0.0))
    energy_next = jnp.zeros(TILE, jnp.float32)
    cross = jnp.zeros(TILE, jnp.float32)
    for ex in range(2):
        for ey in range(2):
            kinds = [part(ex, kind, ey) for kind in range(3)]
            for a in range(8):
                value = direction[ex, a, ey] - step * (smoothed[ex, a, ey] + kinds[kind_of(a)])
                following[ex, a, ey] = value
                weighed = value * (inv_mult[ey] * place.inv_x(ex, a))
                was = image[ex, a, ey]
                energy_next = energy_next + weighed * (resid[ex, a, ey] - step * was)
                cross = cross + weighed * was
    slope_z[...] = along_z(following[...].reshape(256, LANES), zmat[2]).reshape(slope_z.shape)
    square = jnp.zeros(TILE, jnp.float32)
    for ex in range(2):
        for ey in range(2):
            values, images = own_operator(ctab, kap, following, slope_z, ex, ey)
            for a in range(8):
                square = square + values[a] * images[a]
    send_to_all(msg, message(place, [], [total(energy_next), total(square), total(cross)]))


def pressure_kernel(got, known, direction, following, pressure):
    energy = known[:, pl.ds(0, 1)]
    curvature = known[:, pl.ds(1, 1)]
    energy_next, square, cross = gathered_scalars(got, 3)
    ratio = energy_next / energy
    step = energy / curvature
    step_next = energy_next / (square + 2.0 * ratio * cross + ratio * ratio * curvature)
    weight_old = step + step_next * ratio
    for ex in range(2):
        for a in range(8):
            for ey in range(2):
                pressure[ex, a, ey] = (
                    weight_old * direction[ex, a, ey] + step_next * following[ex, a, ey]
                )


def coarse_energy(place, got, values, kappa, number):
    lane, row = place.lane, place.row
    for ex in range(2):
        for gx in range(8):
            own = jnp.zeros((1, LANES), jnp.float32)
            group = jnp.zeros((1, LANES), jnp.float32)
            spot = lane[0:1] // 32
            for gy in range(4):
                line = got[gx * 4 + gy, :, pl.ds(LANES, LANES)]
                own = jnp.where(spot == (gy + 2 * ex) % 4, line, own)
                group = jnp.where(spot == (gy + 1 + 2 * ex) % 4, line, group)
            kappa[ex, pl.ds(gx, 1), :] = own
            number[ex, pl.ds(gx, 1), :] = group
    grid = [jnp.zeros(TILE, jnp.float32) for _ in range(2)]
    numbers = [pltpu.roll(number[0], 96, 1), pltpu.roll(number[1], 32, 1)]
    kappa = [kappa[0], pltpu.roll(kappa[1], 64, 1)]
    for q in range(4):
        for c in range(NCD):
            mine = jnp.where(lane == row * 16 + q * 4 + c, values, 0.0)
            mine = jnp.sum(mine, axis=1, keepdims=True)
            for ex in range(2):
                chosen = (lane // 32 == q) & (numbers[ex] == float(c))
                grid[ex] = jnp.where(chosen, mine, grid[ex])

    def ends_y(v):
        low = jnp.where(lane >= 16, 0.5 * (v + pltpu.roll(v, 16, 1)), v)
        return low, v, jnp.where(lane < 112, 0.5 * (v + pltpu.roll(v, 112, 1)), v)

    def ends_z(v):
        low = jnp.where(lane % 16 > 0, 0.5 * (v + pltpu.roll(v, 1, 1)), v)
        return low, v, jnp.where(lane % 16 < 15, 0.5 * (v + pltpu.roll(v, 127, 1)), v)

    low = jnp.where(row > 0, 0.5 * (grid[0] + pltpu.roll(grid[1], 1, 0)), grid[0])
    mid = 0.5 * (grid[0] + grid[1])
    high = jnp.where(row < 7, 0.5 * (grid[1] + pltpu.roll(grid[0], 7, 0)), grid[1])
    mass = [float(WEIGHTS[0]), float(np.sum(WEIGHTS[1:7])), float(WEIGHTS[7])]
    links = (
        (0, 1, -float(np.sum(STIFF[0, 1:7]))),
        (0, 2, -float(STIFF[0, 7])),
        (1, 2, -float(np.sum(STIFF[7, 1:7]))),
    )
    energy = jnp.zeros(TILE, jnp.float32)
    for ex, line in enumerate(((low, grid[0], mid), (mid, grid[1], high))):
        nodes = [[ends_z(v) for v in ends_y(w)] for w in line]
        stiff = jnp.zeros(TILE, jnp.float32)
        square = jnp.zeros(TILE, jnp.float32)
        for i in range(3):
            for j in range(3):
                for k, l, weight in links:
                    factor = weight * mass[i] * mass[j]
                    for first, second in (
                        (nodes[k][i][j], nodes[l][i][j]),
                        (nodes[i][k][j], nodes[i][l][j]),
                        (nodes[i][j][k], nodes[i][j][l]),
                    ):
                        gap = first - second
                        stiff = stiff + (factor * gap) * gap
                for k in range(3):
                    value = nodes[i][j][k]
                    square = square + (mass[i] * mass[j] * mass[k] * value) * value
        energy = energy + kappa[ex] * stiff + sigma_p * square
    return total(energy)


def finish_kernel(
    got, grp, direction, smoothed, pressure, matrix, kappa, number
):
    place = Place()
    per = LANES // NCD
    row_lane = lax.broadcasted_iota(jnp.int32, (1, LANES), 1)
    rest = jnp.zeros((1, LANES), jnp.float32)
    dual = jnp.zeros((1, LANES), jnp.float32)
    sums = [jnp.zeros((1, LANES), jnp.float32) for _ in range(4)]
    for i in range(per):
        line = got[i, :, pl.ds(0, LANES)]
        mine = row_lane // NCD == (i + AWAY) % per
        known = row_lane // NCD == (i + BEYOND) % per
        rest = jnp.where(mine, line, rest)
        dual = dual + jnp.where(mine | known, 0.0, line)
        for c in range(4):
            sums[c] = sums[c] + jnp.where(row_lane == ((i + BEYOND) % per) * NCD + c, line, 0.0)
            block = got[i, :, pl.ds((2 + c) * LANES, LANES)]
            matrix[pl.ds(i * NCD + c, 1), :] = block
    rest = pltpu.roll(rest, (per - AWAY) * NCD, 1)
    energy, curvature, square, self_energy = [
        jnp.sum(value, axis=1, keepdims=True) for value in sums
    ]
    values = exact_dot(jnp.broadcast_to(rest, TILE), matrix[...])
    line = values[0:1]
    cross = square + jnp.sum(line * rest, axis=1, keepdims=True)
    both = self_energy + 2.0 * jnp.sum(line * dual, axis=1, keepdims=True)
    both = both + coarse_energy(place, got, values, kappa, number)
    step = energy / curvature
    energy_next = step * step * cross - energy
    ratio = energy_next / energy
    with_image = curvature - step * cross
    with_itself = curvature - 2.0 * step * cross + step * step * both
    step_next = energy_next / (
        with_itself + 2.0 * ratio * with_image + ratio * ratio * curvature
    )
    old = step + step_next * (1.0 + ratio)
    new = -step_next * step

    def solved(dx, dy, c):
        at = ((place.ix + dx - 1) * place.ny + place.iy + dy - 1) * NCD + c
        return jnp.sum(jnp.where(row_lane == at, line, 0.0), axis=1, keepdims=True)

    part = prolonged(place, masked(place, solved), grp)
    for ex in range(2):
        for ey in range(2):
            kinds = [part(ex, kind, ey) for kind in range(3)]
            for a in range(8):
                pressure[ex, a, ey] = old * direction[ex, a, ey] + new * (
                    smoothed[ex, a, ey] + kinds[kind_of(a)]
                )


def masked(place, solved):
    there_x = (place.prev_x, None, place.next_x)
    there_y = (place.prev_y, None, place.next_y)

    def value(dx, dy, c):
        out = solved(dx, dy, c)
        for there in (there_x[dx], there_y[dy]):
            if there is not None:
                out = jnp.where(there, out, 0.0)
        return out

    return value


def call(body, outs, scratch=(), **more):
    return pl.pallas_call(
        body,
        out_shape=[jax.ShapeDtypeStruct(shape, jnp.float32) for shape in outs],
        scratch_shapes=[
            pltpu.VMEM(shape, jnp.float32) if isinstance(shape, tuple) else shape
            for shape in scratch
        ],
        **more,
        compiler_params=pltpu.CompilerParams(vmem_limit_bytes=24 * 1024 * 1024),
    )


def swap(first, second, axis):
    along, across = lax.axis_size("gx"), lax.axis_size("gy")

    def number(ix, iy):
        return ix * across + iy

    pairs = ([], [])
    for ix in range(along):
        for iy in range(across):
            at, count = (ix, along) if axis == "gx" else (iy, across)
            for k, to in enumerate((at ^ 1, ((at + 1) ^ 1) - 1)):
                if 0 <= to < count:
                    there = (to, iy) if axis == "gx" else (ix, to)
                else:
                    there = (ix, iy ^ 1) if axis == "gx" else (ix, across - 1 - iy)
                pairs[k].append((number(ix, iy), number(*there)))
    pairs = pairs[::-1]
    first_got = lax.ppermute(first, BOTH, pairs[0])
    return first_got, lax.ppermute(second, BOTH, pairs[1])


def per_device(fields, viscosity, inv_density, elem_group, coarse_inverse):
    length = fields.shape[5]
    elems_z = length // NODES
    devices = lax.axis_size("gx") * lax.axis_size("gy")
    blocks = coarse_inverse.shape[1] // LANES
    pack_rows = 1 + NCD * blocks
    tiles_np, mats_np = constant_tables(elems_z)
    ctab, zmat = jnp.asarray(tiles_np), jnp.asarray(mats_np)
    one = fields.shape[1:]
    four = fields.shape
    faces = (64, LANES)
    xf_shape = (2, 4, 2, 8, LANES)
    inner_shape = (2, 2, 8, LANES)
    y_shape, x_shape = (STEP_PACK + 3 * pack_rows, LANES), (STEP_PACK, LANES)
    turned = (64 + pack_rows, LANES)
    smooth_shape = (SMOOTH_ROWS, LANES)
    rows = (devices, 1, LANES)
    grid_fits = (
        blocks == 1
        and lax.axis_size("gx") == 8
        and lax.axis_size("gy") * fields.shape[3] * elems_z == LANES
    )

    def exchange_all(msg):
        return lax.all_to_all(msg, BOTH, 0, 0, tiled=True)

    beside = pl.CostEstimate(flops=10**7, bytes_accessed=10**6, transcendentals=0)
    first, second = call(faces_kernel, [faces, faces], [xf_shape])(fields)
    numbers = elem_group.astype(jnp.float32)
    row = jnp.stack([inv_density, numbers], 1).reshape(1, LANES)
    pack = jnp.concatenate([row, coarse_inverse.reshape(NCD * blocks, LANES)], 0)
    (facts,) = call(facts_kernel, [(1, 6 * LANES)], cost_estimate=beside)(pack)
    summed, xf = call(mass_kernel, [four, xf_shape], cost_estimate=beside)(fields)
    y_got = swap(first, second, "gy")
    first, second = call(functools.partial(turn_faces_kernel, pack_rows), [turned, turned])(
        xf, pack, *y_got
    )
    side_got = x_got = swap(first, second, "gx")
    edge_shape = (4, 2, 2, 8, LANES)
    begun, given, slope, answer = call(
        prepare_kernel, [four, four, edge_shape, one], [four, four], cost_estimate=beside
    )(summed, viscosity, *y_got, ctab, zmat)
    share, xf, inner_x, first, second = call(
        functools.partial(rhs_kernel, pack_rows),
        [four, xf_shape, inner_shape, y_shape, y_shape],
        [edge_shape, edge_shape, edge_shape, edge_shape],
    )(begun, given, slope, answer, viscosity, pack, *x_got, ctab, zmat)
    y_got = swap(first, second, "gy")
    first, second = call(turn_step_kernel, [x_shape, x_shape])(xf, inner_x, *y_got)
    x_got = swap(first, second, "gx")
    inv_diag, kap, grp, coarse = call(
        functools.partial(setup_kernel, pack_rows, blocks),
        [one, (16, LANES), (16, LANES), (9 * NCD * blocks, LANES)],
        [(16, LANES), (8, 16, LANES)],
        cost_estimate=beside,
    )(pack, *side_got, *y_got, ctab)
    begun, given = call(approach_kernel, [four, one], [one], cost_estimate=beside)(
        share, *y_got, ctab, zmat
    )
    side_shape = (2, 2, 8, LANES)
    fields_got = x_got
    fields_begun = begun
    resid, own, msg = call(
        advance_kernel,
        [one, one, (devices, 8, LANES)],
        [one, one, side_shape, one, (3,) + side_shape],
    )(begun, given, *y_got, *x_got, inv_diag, kap, grp, ctab, zmat)
    got = exchange_all(msg)
    (relayed,) = call(relay_kernel, [(RELAY_ROWS, LANES)])(got, own)
    relayed = lax.ppermute(
        relayed, "gy", [(i, i ^ 1) for i in range(lax.axis_size("gy")) if i ^ 1 < lax.axis_size("gy")]
    )
    direction, own, inner_x, first, second, extra = call(
        functools.partial(first_direction_kernel, blocks),
        [one, one, inner_shape, smooth_shape, smooth_shape, (1, LANES)],
        [one, one],
    )(got, relayed, coarse, grp, kap, inv_diag, resid, own, ctab, zmat)
    y_got = swap(first, second, "gy")
    first, second = call(turn_smooth_kernel, [smooth_shape, smooth_shape])(own, inner_x, *y_got)
    x_got = swap(first, second, "gx")
    fields_new, extra = call(emit_kernel, [four, (1, LANES)], cost_estimate=beside)(
        fields_begun, *fields_got, extra
    )
    begun, begun_scaled, given = call(
        ready_kernel, [one, one, one], [one], cost_estimate=beside
    )(own, *y_got, inv_diag, kap, ctab, zmat)
    image, image_smoothed, msg = call(
        smooth_kernel,
        [one, one, (devices, 1, 6 * LANES) if grid_fits else rows],
        [one, one, side_shape],
    )(
        begun, begun_scaled, given, *y_got, *x_got, inv_diag, kap, grp, extra, facts, ctab, zmat
    )
    got = exchange_all(msg)
    if grid_fits:
        (pressure,) = call(
            finish_kernel, [one], [(LANES, LANES), (2,) + TILE, (2,) + TILE]
        )(got, grp, direction, image_smoothed)
        return (fields_new, pressure)
    following, known, msg = call(
        functools.partial(second_direction_kernel, blocks), [one, (1, LANES), rows], [one]
    )(got, coarse, grp, kap, resid, direction, image, image_smoothed, ctab, zmat)
    got = exchange_all(msg)
    (pressure,) = call(pressure_kernel, [one])(got, known, direction, following)
    return (fields_new, pressure)


def solution(mesh):
    placed = (
        P(None, "gx", None, "gy", None, None),
        P("gx", None, "gy", None, None),
        P("gx", "gy", None),
        P("gx", "gy", None),
        P(("gx", "gy"), None),
    )
    return jax.shard_map(
        per_device,
        mesh=mesh,
        in_specs=placed,
        out_specs=(P(None, "gx", None, "gy", None, None), P("gx", None, "gy", None, None)),
        check_vma=False,
    )
```

```python
import functools

import jax
import jax.numpy as jnp
import ml_dtypes
import numpy as np
from jax import lax
from jax.experimental import pallas as pl
from jax.experimental.pallas import tpu as pltpu
from jax.sharding import PartitionSpec as P

NCD = 4
NODES = 8
LANES = 128
TILE = (8, 128)
BOTH = ("gx", "gy")

dt_step = 0.01
sigma_p = 4.0
prandtl = 0.7
cheb_ratio = 0.1


def tables():
    points = np.array(
        [
            -1.0,
            -0.8717401485096066,
            -0.5917001814331423,
            -0.2092992179024789,
            0.2092992179024789,
            0.5917001814331423,
            0.8717401485096066,
            1.0,
        ]
    )
    weights = np.array(
        [
            1.0 / 28.0,
            0.2107042271435061,
            0.3411226924835044,
            0.4124587946587038,
            0.4124587946587038,
            0.3411226924835044,
            0.2107042271435061,
            1.0 / 28.0,
        ]
    )
    identity = np.eye(8)
    differ = points[:, None] - points[None, :] + identity
    barycentric = 1.0 / np.prod(differ, axis=1)
    offdiag = barycentric[None, :] / barycentric[:, None] / differ * (1.0 - identity)
    derivative = offdiag - identity * np.sum(offdiag, axis=1)[:, None]
    mass_one = identity * weights[None, :]
    stiff_one = derivative.T @ mass_one @ derivative
    stiff_three = (
        np.kron(np.kron(stiff_one, mass_one), mass_one)
        + np.kron(np.kron(mass_one, stiff_one), mass_one)
        + np.kron(np.kron(mass_one, mass_one), stiff_one)
    )
    three_diag = np.sum(stiff_three * np.eye(512), axis=1)
    spectral_bound = float(np.max(np.sum(np.abs(stiff_three), axis=1) / three_diag))
    return (derivative, weights, stiff_one, spectral_bound)


DERIV, WEIGHTS, STIFF, BOUND = tables()
SCALED = STIFF / WEIGHTS[:, None]
LINE = np.diag(STIFF) / WEIGHTS
THETA = 0.5 * (BOUND + cheb_ratio * BOUND)
DELTA = 0.5 * (BOUND - cheb_ratio * BOUND)
RHO = DELTA / THETA
RHO_NEXT = 1.0 / (2.0 * THETA / DELTA - RHO)


def constant_tables(elems_z):
    def turned(matrix):
        rows = np.arange(8)
        return [np.repeat(matrix[rows, (rows - s) % 8][:, None], LANES, 1) for s in range(8)]

    wz = np.tile(WEIGHTS, elems_z)
    kz = np.tile(LINE, elems_z)
    tiles = turned(DERIV) + turned(DERIV.T) + turned(SCALED)
    tiles += [WEIGHTS[:, None] * wz[None, :], LINE[:, None] + kz[None, :]]
    for matrix in (DERIV, SCALED):
        for node in (7, 0):
            inner = matrix[node] * (np.arange(8) != node)
            tiles.append(np.repeat(inner[:, None], LANES, 1))
    eye = np.eye(elems_z)
    mats = [np.kron(eye, DERIV.T), np.kron(eye, DERIV), np.kron(eye, SCALED.T)]
    halves = []
    for mat in mats:
        high = mat.astype(ml_dtypes.bfloat16)
        low = (mat - high.astype(np.float64)).astype(ml_dtypes.bfloat16)
        both = np.concatenate([high, low], 1)
        halves.append(np.concatenate([both, both], 0))
    return np.stack(tiles).astype(np.float32), np.stack(halves)


T_D, T_DT, T_K, T_W, T_LINE = 0, 8, 16, 24, 25
T_TOP, T_BOTTOM, T_KTOP, T_KBOTTOM = 26, 27, 28, 29


class Place:
    def __init__(self):
        self.ix = lax.axis_index("gx")
        self.iy = lax.axis_index("gy")
        self.nx = lax.axis_size("gx")
        self.ny = lax.axis_size("gy")
        self.even_x = self.ix % 2 == 0
        self.even_y = self.iy % 2 == 0
        self.row = lax.broadcasted_iota(jnp.int32, TILE, 0)
        self.lane = lax.broadcasted_iota(jnp.int32, TILE, 1)
        self.low_z = (self.lane % 8 == 0) & (self.lane > 0)
        self.high_z = (self.lane % 8 == 7) & (self.lane < LANES - 1)
        self.prev_x = self.ix > 0
        self.next_x = self.ix < self.nx - 1
        self.prev_y = self.iy > 0
        self.next_y = self.iy < self.ny - 1

    def mult_tile(self, ey):
        along_z = 1.0 + jnp.where(self.low_z | self.high_z, 1.0, 0.0)
        low = 1.0 if ey == 1 else jnp.where(self.prev_y, 1.0, 0.0)
        high = 1.0 if ey == 0 else jnp.where(self.next_y, 1.0, 0.0)
        along_y = 1.0 + jnp.where(self.row == 0, low, jnp.where(self.row == 7, high, 0.0))
        return along_y * along_z

    def inv_x(self, ex, a):
        if a == 0:
            return 0.5 if ex == 1 else jnp.where(self.prev_x, 0.5, 1.0)
        if a == 7:
            return 0.5 if ex == 0 else jnp.where(self.next_x, 0.5, 1.0)
        return 1.0

    def mult_x(self, ex, a):
        if a == 0:
            return 2.0 if ex == 1 else jnp.where(self.prev_x, 2.0, 1.0)
        if a == 7:
            return 2.0 if ex == 0 else jnp.where(self.next_x, 2.0, 1.0)
        return 1.0

    def share_x(self, ex, a):
        if (ex, a) == (0, 0):
            return jnp.where(self.prev_x, 0.5, 1.0)
        if (ex, a) == (1, 7):
            return jnp.where(self.next_x, 0.5, 1.0)
        return 1.0

    def share_y(self, ey):
        if ey == 0:
            return jnp.where((self.row == 0) & self.prev_y, 0.5, 1.0)
        return jnp.where((self.row == 7) & self.next_y, 0.5, 1.0)

    def inv_y(self, ey):
        low = 0.5 if ey == 1 else jnp.where(self.prev_y, 0.5, 1.0)
        high = 0.5 if ey == 0 else jnp.where(self.next_y, 0.5, 1.0)
        return jnp.where(self.row == 0, low, jnp.where(self.row == 7, high, 1.0))

    def inv_z(self):
        return jnp.where(self.low_z | self.high_z, 0.5, 1.0)

    def join_z(self, t):
        up = pltpu.roll(t, LANES - 1, 1)
        down = pltpu.roll(t, 1, 1)
        return t + jnp.where(self.high_z, up, jnp.where(self.low_z, down, 0.0))

    def to_low(self, below):
        return jnp.where(self.row == 0, pltpu.roll(below, 1, 0), 0.0)

    def to_high(self, above):
        return jnp.where(self.row == 7, pltpu.roll(above, 7, 0), 0.0)

    def join_y(self, below, above):
        return below + self.to_high(above), above + self.to_low(below)

    def before_x(self, first, second):
        return jnp.where(self.prev_x, jnp.where(self.even_x, first, second), 0.0)

    def after_x(self, first, second):
        return jnp.where(self.next_x, jnp.where(self.even_x, second, first), 0.0)

    def send_x(self, first, second):
        return jnp.where(self.even_x, second, first)

    def before_y(self, first, second):
        return jnp.where(self.prev_y, jnp.where(self.even_y, first, second), 0.0)

    def after_y(self, first, second):
        return jnp.where(self.next_y, jnp.where(self.even_y, second, first), 0.0)

    def send_y(self, first, second):
        return jnp.where(self.even_y, second, first)


def along_x(matrix, tiles, sign):
    even = [tiles[a] + tiles[7 - a] for a in range(4)]
    odd = [tiles[a] - tiles[7 - a] for a in range(4)]
    out = [None] * 8
    for i in range(4):
        plus, minus = None, None
        for a in range(4):
            p = float(0.5 * (matrix[i, a] + matrix[i, 7 - a])) * even[a]
            m = float(0.5 * (matrix[i, a] - matrix[i, 7 - a])) * odd[a]
            plus = p if plus is None else plus + p
            minus = m if minus is None else minus + m
        out[i] = plus + minus
        out[7 - i] = minus - plus if sign < 0 else plus - minus
    return out


def along_y(ctab, base, tile):
    acc = ctab[base] * tile
    for s in range(1, 8):
        acc = acc + ctab[base + s] * pltpu.roll(tile, s, 0)
    return acc


def exact_dot(rows, matrix):
    return jnp.dot(
        rows, matrix, precision=lax.Precision.HIGHEST, preferred_element_type=jnp.float32
    )


def along_z(rows, matrix):
    high = rows.astype(jnp.bfloat16)
    low = (rows - high.astype(jnp.float32)).astype(jnp.bfloat16)
    both = jnp.dot(
        jnp.concatenate([high, low], axis=1), matrix, preferred_element_type=jnp.float32
    )
    return both[:, :LANES] + both[:, LANES:]


def total(tile):
    return jnp.sum(jnp.sum(tile, axis=0, keepdims=True), axis=1, keepdims=True)


def store_y_faces(place, field, first_out, second_out, lead, at):
    for ex in range(2):
        for a in range(8):
            low = field[lead + (ex, a, 0, pl.ds(0, 1), slice(None))]
            high = field[lead + (ex, a, 1, pl.ds(7, 1), slice(None))]
            row = at + ex * 8 + a
            first_out[pl.ds(row, 1), :] = place.send_y(high, low)
            second_out[pl.ds(row, 1), :] = place.send_y(low, high)


def join_own(place, tiles):
    for ex in range(2):
        for a in range(8):
            tiles[ex][a] = list(place.join_y(*tiles[ex][a]))
    for ey in range(2):
        both = tiles[0][7][ey] + tiles[1][0][ey]
        tiles[0][7][ey] = both
        tiles[1][0][ey] = both


def weight_of(node):
    edge = jnp.minimum(node, 7 - node)
    value = jnp.where(edge == 2, float(WEIGHTS[2]), float(WEIGHTS[3]))
    return jnp.where(
        edge == 0, float(WEIGHTS[0]), jnp.where(edge == 1, float(WEIGHTS[1]), value)
    )


def faces_kernel(fields, first, second, edges):
    place = Place()
    weight = weight_of(place.row) * weight_of(place.lane % NODES) * float(WEIGHTS[0])
    for ch in range(4):
        for ex in range(2):
            for a in range(8):
                edges[0, ch, ex, pl.ds(a, 1), :] = fields[ch, ex, a, 0, pl.ds(0, 1), :]
                edges[1, ch, ex, pl.ds(a, 1), :] = fields[ch, ex, a, 1, pl.ds(7, 1), :]
    for ch in range(4):
        sides = [
            place.join_y(*[place.join_z(edges[side, ch, ex] * weight) for ex in range(2)])
            for side in range(2)
        ]
        for ex in range(2):
            rows = pl.ds(ch * 16 + ex * 8, 8)
            first[rows, :] = place.send_y(sides[1][ex], sides[0][ex])
            second[rows, :] = place.send_y(sides[0][ex], sides[1][ex])


def mass_kernel(fields, out, xf):
    place = Place()
    weight = weight_of(place.row) * weight_of(place.lane % NODES)
    for ch in range(4):
        tiles = [
            [
                [
                    place.join_z(fields[ch, ex, a, ey] * (float(WEIGHTS[a]) * weight))
                    for ey in range(2)
                ]
                for a in range(8)
            ]
            for ex in range(2)
        ]
        join_own(place, tiles)
        for ex in range(2):
            for a in range(8):
                for ey in range(2):
                    out[ch, ex, a, ey] = tiles[ex][a][ey]
        for ey in range(2):
            xf[0, ch, ey] = tiles[0][0][ey]
            xf[1, ch, ey] = tiles[1][7][ey]


def turn_faces(place, xf, y_first, y_second, first, second):
    for ch in range(4):
        sides = []
        for side in range(2):
            row = pl.ds(ch * 16 + 15 * side, 1)
            got_a, got_b = y_first[row, :], y_second[row, :]
            low = xf[side, ch, 0] + jnp.where(place.row == 0, place.before_y(got_a, got_b), 0.0)
            high = xf[side, ch, 1] + jnp.where(place.row == 7, place.after_y(got_a, got_b), 0.0)
            sides.append((low, high))
        for ey in range(2):
            rows = pl.ds(ch * 16 + ey * 8, 8)
            first[rows, :] = place.send_x(sides[1][ey], sides[0][ey])
            second[rows, :] = place.send_x(sides[0][ey], sides[1][ey])


def turn_faces_kernel(pack_rows, xf, pack, y_first, y_second, first, second):
    turn_faces(Place(), xf, y_first, y_second, first, second)
    first[pl.ds(64, pack_rows), :] = pack[...]
    second[pl.ds(64, pack_rows), :] = pack[...]


def turn_edges(place, inner_x, y_first, y_second, first, second, at, edge, inner_y):
    sides = []
    for side in range(2):
        row = pl.ds(edge + side, 1)
        got_a, got_b = y_first[row, :], y_second[row, :]
        low = inner_x[side, 0] + jnp.where(place.row == 0, place.before_y(got_a, got_b), 0.0)
        high = inner_x[side, 1] + jnp.where(place.row == 7, place.after_y(got_a, got_b), 0.0)
        sides.append((low, high))
    for ey in range(2):
        rows = pl.ds(at + ey * 8, 8)
        first[rows, :] = place.send_x(sides[1][ey], sides[0][ey])
        second[rows, :] = place.send_x(sides[0][ey], sides[1][ey])
    for k, pick in enumerate((place.before_y, place.after_y)):
        sides = []
        for side in range(2):
            row = pl.ds(inner_y + 15 * side, 1)
            sides.append(pick(y_first[row, :], y_second[row, :]))
        row = pl.ds(edge + k, 1)
        first[row, :] = place.send_x(sides[1], sides[0])
        second[row, :] = place.send_x(sides[0], sides[1])


STEP_U, STEP_V, STEP_EDGE, STEP_PACK = 64, 64, 80, 82


def turn_step_kernel(xf, inner_x, y_first, y_second, first, second):
    place = Place()
    turn_faces(place, xf, y_first, y_second, first, second)
    turn_edges(place, inner_x, y_first, y_second, first, second, STEP_U, STEP_EDGE, STEP_V)


def setup_kernel(
    pack_rows,
    blocks,
    pack,
    x_first,
    x_second,
    y_first,
    y_second,
    ctab,
    inv_diag,
    kap,
    grp,
    coarse,
    compact,
    spread,
):
    place = Place()
    beside = pl.ds(64, pack_rows)
    packs = [[None] * 3 for _ in range(3)]
    packs[0][1] = place.before_x(x_first[beside, :], x_second[beside, :])
    packs[1][1] = pack[...]
    packs[2][1] = place.after_x(x_first[beside, :], x_second[beside, :])
    for dx in range(3):
        rows = pl.ds(STEP_PACK + dx * pack_rows, pack_rows)
        packs[dx][0] = place.before_y(y_first[rows, :], y_second[rows, :])
        packs[dx][2] = place.after_y(y_first[rows, :], y_second[rows, :])
    compact[...] = jnp.zeros(compact.shape, jnp.float32)
    for dx in range(3):
        for dy in range(3):
            at = (dx * 3 + dy) * NCD * blocks
            coarse[pl.ds(at, NCD * blocks), :] = packs[dx][dy][1 : 1 + NCD * blocks]
            compact[pl.ds(dx * 3 + dy, 1), :] = packs[dx][dy][0:1]
    elems = LANES // NODES
    lane = lax.broadcasted_iota(jnp.int32, (LANES, LANES), 1)
    source = lax.broadcasted_iota(jnp.int32, (LANES, LANES), 0)
    for k in range(8):
        at = (k % 4 // 2) * 4 * elems + (k // 4) * 2 * elems + (k % 2) * elems
        spot = (source == at + lane // NODES).astype(jnp.float32)
        spread[k] = exact_dot(compact[...], spot)
    there_x = [jnp.where(place.prev_x, 1.0, 0.0), 1.0, jnp.where(place.next_x, 1.0, 0.0)]
    there_y = [jnp.where(place.prev_y, 1.0, 0.0), 1.0, jnp.where(place.next_y, 1.0, 0.0)]

    def element_row(base, u, v):
        device = (u // 2) * 3 + v // 2
        return spread[base + (u % 2) * 2 + v % 2, pl.ds(device, 1), :]

    for x in range(4):
        for y in range(4):
            kap[pl.ds(x * 4 + y, 1), :] = element_row(0, x + 1, y + 1)
            grp[pl.ds(x * 4 + y, 1), :] = element_row(4, x + 1, y + 1)
    kappa = [
        [
            place.join_z(jnp.broadcast_to(element_row(0, u + 1, v + 1), TILE))
            for v in range(4)
        ]
        for u in range(4)
    ]
    count_z = 1.0 + jnp.where(place.low_z | place.high_z, 1.0, 0.0)
    weight = ctab[T_W]
    line = ctab[T_LINE]

    def pick(values, ey):
        low = values[ey] + values[ey + 1]
        high = values[ey + 1] + values[ey + 2]
        return jnp.where(place.row == 0, low, jnp.where(place.row == 7, high, values[ey + 1]))

    for ex in range(2):
        for kind in range(3):
            us = {0: (ex, ex + 1), 1: (ex + 1,), 2: (ex + 1, ex + 2)}[kind]
            sums, counts = [], []
            for v in range(4):
                acc, num = None, 0.0
                for u in us:
                    acc = kappa[u][v] if acc is None else acc + kappa[u][v]
                    num = num + there_x[(u + 1) // 2]
                sums.append(acc)
                counts.append(num * there_y[(v + 1) // 2])
            for ey in range(2):
                kappa_sum = pick(sums, ey)
                mult = pick(counts, ey) * count_z
                for a in {0: (0,), 1: range(1, 7), 2: (7,)}[kind]:
                    diag = (float(LINE[a]) + line) * kappa_sum + sigma_p * mult
                    inv_diag[ex, a, ey] = 1.0 / (diag * (float(WEIGHTS[a]) * weight))


OUTER = ((0, 0), (1, 7))


def got_y_sum(place, tile, ch, ex, a, ey, y_first, y_second):
    row = pl.ds(ch * 16 + ex * 8 + a, 1)
    got_a, got_b = y_first[row, :], y_second[row, :]
    if ey == 0:
        tile = tile + jnp.where(place.row == 0, place.before_y(got_a, got_b), 0.0)
    else:
        tile = tile + jnp.where(place.row == 7, place.after_y(got_a, got_b), 0.0)
    return tile


def got_x_sum(place, tile, ch, ex, ey, x_first, x_second):
    rows = pl.ds(ch * 16 + ey * 8, 8)
    pick = place.before_x if ex == 0 else place.after_x
    return tile + pick(x_first[rows, :], x_second[rows, :])


def facts_kernel(pack, facts):
    place = Place()
    grid = pltpu.roll(pack[pl.ds(0, 1), :], (place.iy % 4) * (LANES // 4), 1)
    facts[:, pl.ds(0, LANES)] = jnp.zeros((1, LANES), jnp.float32)
    facts[:, pl.ds(LANES, LANES)] = grid
    for c in range(NCD):
        facts[:, pl.ds((2 + c) * LANES, LANES)] = pack[pl.ds(1 + c, 1), :]


def prepare_kernel(
    summed, visc, y_first, y_second, ctab, zmat, start, part, slope, answer, grad_z, flux_z
):
    place = Place()
    weight = ctab[T_W]
    inv_mass = [1.0 / (weight * place.mult_tile(ey)) for ey in range(2)]

    def begin(ch, carry):
        for ex in range(2):
            for a in range(8):
                for ey in range(2):
                    tile = got_y_sum(
                        place, summed[ch, ex, a, ey], ch, ex, a, ey, y_first, y_second
                    )
                    scale = place.inv_x(ex, a) * float(1.0 / WEIGHTS[a])
                    start[ch, ex, a, ey] = tile * (inv_mass[ey] * scale)
        return carry

    lax.fori_loop(0, 4, begin, 0)
    grad_z[...] = along_z(start[...].reshape(1024, LANES), zmat[0]).reshape(grad_z.shape)

    def column(index, carry):
        ch, ey = index // 2, index % 2
        coef = 1.0 / prandtl if ch == 3 else 1.0
        for ex in range(2):
            grad_x = along_x(DERIV, [start[ch, ex, a, ey] for a in range(8)], -1)
            flux_x = [
                visc[ex, a, ey] * (float(WEIGHTS[a]) * weight) * coef * grad_x[a]
                for a in range(8)
            ]
            back = along_x(DERIV.T, flux_x, -1)
            for a in range(8):
                if (ex, a) in OUTER:
                    slope[ch, ex, ey] = grad_x[a]
                    part[ch, ex, a, ey] = back[a]
                    continue
                rest, flux_z[ch, ex, a, ey] = across(
                    ctab, weight, a, coef, start[ch, ex, a, ey], grad_z[ch, ex, a, ey],
                    start[1, ex, a, ey], start[2, ex, a, ey], visc[ex, a, ey],
                )
                flow = float(WEIGHTS[a]) * weight * start[0, ex, a, ey]
                part[ch, ex, a, ey] = rest + flow * grad_x[a] + back[a]
        return carry

    for ex, outer in OUTER:
        for ey in range(2):
            flux_x = [
                visc[ex, a, ey] * (float(WEIGHTS[a] * DERIV[a, outer]) * weight) for a in range(8)
            ]
            back = along_x(DERIV.T, flux_x, -1)
            for a in range(8):
                answer[ex, a, ey] = back[a]
    for index in range(8):
        column(index, 0)
    for ch in range(4):
        for ex in range(2):
            inner = pl.ds(1 - ex, 7)
            back = along_z(flux_z[ch, ex, inner].reshape(112, LANES), zmat[1])
            part[ch, ex, inner] = part[ch, ex, inner] + back.reshape(7, 2, 8, LANES)


def across(ctab, weight, a, coef, value, grad_z, flow_y, flow_z, visc):
    node = float(WEIGHTS[a]) * weight
    grad_y = along_y(ctab, T_D, value)
    nu = visc * node * coef
    part = node * (flow_y * grad_y + flow_z * grad_z) + along_y(ctab, T_DT, nu * grad_y)
    return part, nu * grad_z


def rhs_kernel(
    pack_rows,
    begun,
    given,
    slope,
    answer,
    visc,
    pack,
    x_first,
    x_second,
    ctab,
    zmat,
    share,
    xf,
    inner_x,
    first,
    second,
    edge,
    edge_z,
    edge_part,
    came,
):
    place = Place()
    weight = ctab[T_W]
    inv_mass = [1.0 / (weight * place.mult_tile(ey)) for ey in range(2)]
    for ch in range(4):
        for side, (ex, a) in enumerate(OUTER):
            scale = place.inv_x(ex, a) * float(1.0 / WEIGHTS[a])
            for ey in range(2):
                zero = jnp.zeros(TILE, jnp.float32)
                extra = got_x_sum(place, zero, ch, ex, ey, x_first, x_second)
                extra = extra * (inv_mass[ey] * scale)
                came[ch, side, ey] = extra
                edge[ch, side, ey] = begun[ch, ex, a, ey] + extra
    edge_z[...] = along_z(edge[...].reshape(128, LANES), zmat[0]).reshape(edge.shape)
    for ch in range(4):
        coef = 1.0 / prandtl if ch == 3 else 1.0
        for side, (ex, a) in enumerate(OUTER):
            for ey in range(2):
                parts = across(
                    ctab, weight, a, coef, edge[ch, side, ey], edge_z[ch, side, ey],
                    edge[1, side, ey], edge[2, side, ey], visc[ex, a, ey],
                )
                edge_part[ch, side, ey], edge_z[ch, side, ey] = parts
    edge_part[...] = edge_part[...] + along_z(
        edge_z[...].reshape(128, LANES), zmat[1]
    ).reshape(edge.shape)

    def side_of(ch, ex, a, ey):
        outer = OUTER[ex][1]
        coef = 1.0 / prandtl if ch == 3 else 1.0
        extra = came[ch, ex, ey]
        node = float(WEIGHTS[a]) * weight
        turn = float(DERIV[a, outer])
        if a == outer:
            known = given[ch, ex, a, ey] + edge_part[ch, ex, ey]
            known = known + node * edge[0, ex, ey] * (slope[ch, ex, ey] + turn * extra)
            return known + extra * (coef * answer[ex, a, ey])
        flow = float(WEIGHTS[a] * turn) * weight * begun[0, ex, a, ey]
        return given[ch, ex, a, ey] + extra * (coef * answer[ex, a, ey] + flow)

    def finish(ch, carry):
        tiles = [
            [[place.join_z(-side_of(ch, ex, a, ey)) for ey in range(2)] for a in range(8)]
            for ex in range(2)
        ]
        join_own(place, tiles)
        for ex in range(2):
            for a in range(8):
                scale = place.inv_x(ex, a) * float(dt_step / WEIGHTS[a])
                for ey in range(2):
                    value = edge[ch, ex, ey] if (ex, a) in OUTER else begun[ch, ex, a, ey]
                    part = value * (place.share_y(ey) * place.share_x(ex, a))
                    share[ch, ex, a, ey] = part + tiles[ex][a][ey] * (inv_mass[ey] * scale)
        return carry

    for ch in range(4):
        finish(ch, 0)
    for ch in range(4):
        store_y_faces(place, share, first, second, (ch,), ch * 16)
        for ey in range(2):
            xf[0, ch, ey] = share[ch, 0, 0, ey]
            xf[1, ch, ey] = share[ch, 1, 7, ey]

    def column_of(ex, ey):
        return [share[0, ex, a, ey] for a in range(8)]

    def tile_of(ex, a, ey):
        return share[1, ex, a, ey]

    store_inner(
        place, DERIV, ctab[T_BOTTOM], ctab[T_TOP], column_of, tile_of, inner_x, first, second,
        STEP_V, STEP_EDGE,
    )
    beside = pl.ds(64, pack_rows)
    parts = (
        place.before_x(x_first[beside, :], x_second[beside, :]),
        pack[...],
        place.after_x(x_first[beside, :], x_second[beside, :]),
    )
    for k in range(3):
        rows = pl.ds(STEP_PACK + k * pack_rows, pack_rows)
        first[rows, :] = parts[k]
        second[rows, :] = parts[k]


def store_inner(
    place, matrix, bottom, top, column_of, tile_of, inner_x, first, second, at, edge
):
    for ey in range(2):
        low, high = column_of(0, ey), column_of(1, ey)
        below = float(matrix[0, 1]) * low[1]
        above = float(matrix[7, 0]) * high[0]
        for k in range(2, 8):
            below = below + float(matrix[0, k]) * low[k]
            above = above + float(matrix[7, k - 1]) * high[k - 1]
        inner_x[0, ey] = below
        inner_x[1, ey] = above
    for side in range(2):
        low = inner_x[side, 0, pl.ds(0, 1), :]
        high = inner_x[side, 1, pl.ds(7, 1), :]
        first[pl.ds(edge + side, 1), :] = place.send_y(high, low)
        second[pl.ds(edge + side, 1), :] = place.send_y(low, high)
    for ex in range(2):
        for a in range(8):
            low = jnp.sum(bottom * tile_of(ex, a, 0), axis=0, keepdims=True)
            high = jnp.sum(top * tile_of(ex, a, 1), axis=0, keepdims=True)
            row = pl.ds(at + ex * 8 + a, 1)
            first[row, :] = place.send_y(high, low)
            second[row, :] = place.send_y(low, high)


def cross_flow(place, ctab, flow, slopes, rows, inv_y, inv_z):
    below, above = rows
    below = (below - float(DERIV[0, 0]) * flow[0]) * jnp.where(place.prev_y, 1.0, 0.0)
    above = (above - float(DERIV[7, 7]) * flow[1]) * jnp.where(place.next_y, 1.0, 0.0)
    grad_y = list(place.join_y(*[along_y(ctab, T_D, tile) for tile in flow]))
    grad_y[0] = grad_y[0] + jnp.where(place.row == 0, below, 0.0)
    grad_y[1] = grad_y[1] + jnp.where(place.row == 7, above, 0.0)
    return [grad_y[ey] * inv_y[ey] + place.join_z(slopes[ey]) * inv_z for ey in range(2)]


def approach_kernel(share, y_first, y_second, ctab, zmat, fields_new, part, grad_z):
    place = Place()

    def step(ch, carry):
        for ex in range(2):
            for a in range(8):
                for ey in range(2):
                    fields_new[ch, ex, a, ey] = got_y_sum(
                        place, share[ch, ex, a, ey], ch, ex, a, ey, y_first, y_second
                    )
        return carry

    lax.fori_loop(0, 4, step, 0)
    grad_z[...] = along_z(fields_new[2].reshape(256, LANES), zmat[0]).reshape(grad_z.shape)
    inv_y = [place.inv_y(ey) for ey in range(2)]
    inv_z = place.inv_z()
    for ex in range(2):
        for a in range(8):
            if (ex, a) in OUTER:
                continue
            flow = [fields_new[1, ex, a, ey] for ey in range(2)]
            rows = inner_along_y(place, y_first, y_second, None, None, ex, a, STEP_V, STEP_EDGE)
            slopes = [grad_z[ex, a, ey] for ey in range(2)]
            both = cross_flow(place, ctab, flow, slopes, rows, inv_y, inv_z)
            part[ex, a, 0], part[ex, a, 1] = both


def emit_kernel(begun, x_first, x_second, extra, fields_new, passed):
    place = Place()
    passed[...] = extra[...]
    fields_new[...] = begun[...]
    for ch in range(4):
        for ex, a in OUTER:
            for ey in range(2):
                fields_new[ch, ex, a, ey] = got_x_sum(
                    place, begun[ch, ex, a, ey], ch, ex, ey, x_first, x_second
                )


def advance_kernel(
    begun,
    given,
    y_first,
    y_second,
    x_first,
    x_second,
    inv_diag,
    kap,
    grp,
    ctab,
    zmat,
    resid,
    own,
    msg,
    grad_z,
    scaled,
    edge,
    part,
    outer,
):
    place = Place()
    weight = ctab[T_W]

    def before(row, count=8):
        rows = pl.ds(row, count)
        return place.before_x(x_first[rows, :], x_second[rows, :])

    def after(row, count=8):
        rows = pl.ds(row, count)
        return place.after_x(x_first[rows, :], x_second[rows, :])

    part[...] = given[...]
    for ch in range(3):
        for side, (ex, a) in enumerate(OUTER):
            for ey in range(2):
                outer[ch, side, ey] = got_x_sum(
                    place, begun[ch, ex, a, ey], ch, ex, ey, x_first, x_second
                )
    edge[...] = along_z(outer[2].reshape(32, LANES), zmat[0]).reshape(edge.shape)
    inv_y = [place.inv_y(ey) for ey in range(2)]
    inv_z = place.inv_z()
    for side, (ex, a) in enumerate(OUTER):
        flow = [outer[1, side, ey] for ey in range(2)]
        rows = inner_along_y(place, y_first, y_second, before, after, ex, a, STEP_V, STEP_EDGE)
        slopes = [edge[side, ey] for ey in range(2)]
        both = cross_flow(place, ctab, flow, slopes, rows, inv_y, inv_z)
        part[ex, a, 0], part[ex, a, 1] = both
    slope = [[None, None], [None, None]]
    for ey in range(2):
        for ex in range(2):
            line = [
                outer[0, ex, ey] if (ex, a) in OUTER else begun[0, ex, a, ey] for a in range(8)
            ]
            slope[ex][ey] = along_x(DERIV, line, -1)
        mid = 0.5 * (slope[0][ey][7] + slope[1][ey][0])
        slope[0][ey][7] = mid
        slope[1][ey][0] = mid
        low, high = slope[0][ey][0], slope[1][ey][7]
        inner_low = low - float(DERIV[0, 0]) * outer[0, 0, ey] + before(STEP_U + ey * 8)
        inner_high = high - float(DERIV[7, 7]) * outer[0, 1, ey] + after(STEP_U + ey * 8)
        slope[0][ey][0] = jnp.where(place.prev_x, 0.5 * inner_low, low)
        slope[1][ey][7] = jnp.where(place.next_x, 0.5 * inner_high, high)
    sums = [[jnp.zeros(TILE, jnp.float32) for _ in range(2)] for _ in range(2)]
    inv_mult = [1.0 / place.mult_tile(ey) for ey in range(2)]
    mass = [weight * place.mult_tile(ey) for ey in range(2)]
    for ex in range(2):
        for a in range(8):
            for ey in range(2):
                div = slope[ex][ey][a] + part[ex, a, ey]
                value = div * (mass[ey] * (place.mult_x(ex, a) * float(-WEIGHTS[a])))
                resid[ex, a, ey] = value
                scaled[ex, a, ey] = value * inv_diag[ex, a, ey] * float(1.0 / THETA)
                sums[ex][ey] = sums[ex][ey] + value * (inv_mult[ey] * place.inv_x(ex, a))
    grad_z[...] = along_z(scaled[...].reshape(256, LANES), zmat[2]).reshape(grad_z.shape)
    tiles = [[[None, None] for _ in range(8)] for _ in range(2)]
    for ex in range(2):
        for ey in range(2):
            images = own_operator(ctab, kap, scaled, grad_z, ex, ey)[1]
            for a in range(8):
                tiles[ex][a][ey] = place.join_z(images[a])
    join_own(place, tiles)
    for ex in range(2):
        for a in range(8):
            for ey in range(2):
                own[ex, a, ey] = tiles[ex][a][ey]
    row = message(place, restricted(place, sums, grp), [])
    blank = jnp.where(place.row == 0, jnp.broadcast_to(row, TILE), 0.0)

    def clear(i, carry):
        msg[i] = blank
        return carry

    lax.fori_loop(0, msg.shape[0], clear, 0, unroll=msg.shape[0] <= 64)
    across = Pairing(place)
    for side, (ex, a) in enumerate(OUTER):
        there, ix = across.beside(side)

        @pl.when(there)
        def _():
            msg[ix * place.ny + place.iy] = own[ex, a, 0]
            msg[ix * place.ny + across.twin, pl.ds(1, 7), :] = own[ex, a, 1, pl.ds(1, 7), :]

        @pl.when(there & across.has_far)
        def _():
            msg[ix * place.ny + across.far, pl.ds(1, 1), :] = across.far_row(own, ex, a)

    @pl.when(across.has_far)
    def _():
        for a in range(8):
            msg[place.ix * place.ny + across.far, pl.ds(a, 1), :] = across.far_row(own, 0, a)
            if a > 0:
                to = place.ix * place.ny + across.beyond
                msg[to, pl.ds(a, 1), :] = across.far_row(own, 1, a)


def inner_along_y(place, y_first, y_second, before, after, ex, a, at, edge):
    row = pl.ds(at + ex * 8 + a, 1)
    got_a, got_b = y_first[row, :], y_second[row, :]
    below, above = place.before_y(got_a, got_b), place.after_y(got_a, got_b)
    if before is None:
        return below, above
    if (ex, a) == (0, 0):
        below = below + before(edge, 1)
        above = above + before(edge + 1, 1)
    if (ex, a) == (1, 7):
        below = below + after(edge, 1)
        above = above + after(edge + 1, 1)
    return below, above


class Pairing:
    def __init__(self, place):
        self.place = place
        even = place.even_y
        self.even = even
        self.twin = jnp.where(even, place.iy + 1, place.iy - 1)
        self.far = jnp.where(even, place.iy - 1, place.iy + 1)
        self.has_far = jnp.where(even, place.iy - 1, place.ny - 2 - place.iy) >= 0
        self.beyond = jnp.where(even, place.iy - 2, place.iy + 2)
        self.twin_far = jnp.where(even, place.iy + 2, place.iy - 2)
        self.twin_has_far = jnp.where(even, place.ny - 3 - place.iy, place.iy - 2) >= 0

    def beside(self, side):
        place = self.place
        if side == 0:
            return place.prev_x, place.ix - 1
        return place.next_x, place.ix + 1

    def far_row(self, field, ex, a):
        low = field[ex, a, 0, pl.ds(0, 1), :]
        return jnp.where(self.even, low, field[ex, a, 1, pl.ds(7, 1), :])

    def twin_row(self, field, ex, a):
        low = field[ex, a, 0, pl.ds(0, 1), :]
        return jnp.where(self.even, field[ex, a, 1, pl.ds(7, 1), :], low)


RELAY_FACE, RELAY_EDGE, RELAY_ROWS = 24, 40, 42


def relay_kernel(got, own, out):
    place = Place()
    across = Pairing(place)
    out[...] = jnp.zeros(out.shape, jnp.float32)
    for side in range(2):
        there, ix = across.beside(side)

        @pl.when(there)
        def _():
            out[pl.ds(side * 8, 8), :] = got[ix * place.ny + across.twin]
            corner = got[ix * place.ny + place.iy, pl.ds(0, 1), :]
            out[pl.ds(RELAY_EDGE + side, 1), :] = corner

    @pl.when(across.twin_has_far)
    def _():
        out[pl.ds(16, 8), :] = got[place.ix * place.ny + across.twin_far]

    for ex in range(2):
        for a in range(8):
            out[pl.ds(RELAY_FACE + ex * 8 + a, 1), :] = across.twin_row(own, ex, a)


SMOOTH_X, SMOOTH_Y, SMOOTH_EDGE, SMOOTH_ROWS = 16, 16, 32, 34


def turn_smooth_kernel(own, inner_x, y_first, y_second, first, second):
    place = Place()
    sides = []
    for side, (ex, a) in enumerate(((0, 0), (1, 7))):
        row = pl.ds(15 * side, 1)
        got_a, got_b = y_first[row, :], y_second[row, :]
        low = own[ex, a, 0] + jnp.where(place.row == 0, place.before_y(got_a, got_b), 0.0)
        high = own[ex, a, 1] + jnp.where(place.row == 7, place.after_y(got_a, got_b), 0.0)
        sides.append((low, high))
    for ey in range(2):
        rows = pl.ds(ey * 8, 8)
        first[rows, :] = place.send_x(sides[1][ey], sides[0][ey])
        second[rows, :] = place.send_x(sides[0][ey], sides[1][ey])
    turn_edges(
        place, inner_x, y_first, y_second, first, second, SMOOTH_X, SMOOTH_EDGE, SMOOTH_Y
    )


def restricted(place, sums, grp):
    values = []
    for c in range(NCD):
        acc = jnp.zeros(TILE, jnp.float32)
        for ex in range(2):
            for ey in range(2):
                group = grp[pl.ds((ex + 1) * 4 + ey + 1, 1), :]
                acc = acc + jnp.where(group == float(c), sums[ex][ey], 0.0)
        values.append(total(acc))
    return values


AWAY = 16
BEYOND = 18


def message(place, own_values, scalars, away=0, beyond=1):
    lane = lax.broadcasted_iota(jnp.int32, (1, LANES), 1)
    spot = (place.ix * place.ny + place.iy) % (LANES // NCD)
    after = (spot + beyond) % (LANES // NCD)
    spot = (spot + away) % (LANES // NCD)
    row = jnp.zeros((1, LANES), jnp.float32)
    for c, value in enumerate(own_values):
        row = row + jnp.where(lane == spot * NCD + c, value, 0.0)
    for c, value in enumerate(scalars):
        if value is None:
            continue
        row = row + jnp.where(lane == after * NCD + c, value, 0.0)
    return row


def send_to_all(msg, row):
    def send(i, carry):
        msg[i] = row
        return carry

    lax.fori_loop(0, msg.shape[0], send, 0, unroll=msg.shape[0] <= 64)


def cross_image(place, ctab, kap, value, flat, inner, ex, ey):
    slope_y = along_y(ctab, T_K, value)
    turned_y = inner + float(SCALED[0, 0]) * value
    own = kap[pl.ds((ex + 1) * 4 + ey + 1, 1), :] * (slope_y + flat) + sigma_p * value
    beyond = kap[pl.ds((ex + 1) * 4 + 3 * ey, 1), :] * (turned_y + flat) + sigma_p * value
    return own + jnp.where(beyond_y(place, ey), beyond, 0.0), slope_y, turned_y


def beyond_y(place, ey):
    if ey == 0:
        return (place.row == 0) & place.prev_y
    return (place.row == 7) & place.next_y


def ready_kernel(
    own, y_first, y_second, inv_diag, kap, ctab, zmat, image, scaled, part, slope_z
):
    place = Place()
    for ex in range(2):
        for a in range(8):
            for ey in range(2):
                tile = got_y_sum(place, own[ex, a, ey], 0, ex, a, ey, y_first, y_second)
                image[ex, a, ey] = tile
                scaled[ex, a, ey] = tile * inv_diag[ex, a, ey] * float(1.0 / THETA)
    slope_z[...] = along_z(scaled[...].reshape(256, LANES), zmat[2]).reshape(slope_z.shape)
    for ex in range(2):
        for a in range(8):
            if (ex, a) in OUTER:
                continue
            rows = inner_along_y(
                place, y_first, y_second, None, None, ex, a, SMOOTH_Y, SMOOTH_EDGE
            )
            for ey in range(2):
                part[ex, a, ey] = cross_image(
                    place, ctab, kap, scaled[ex, a, ey], slope_z[ex, a, ey], rows[ey], ex, ey
                )[0]


def smooth_kernel(
    begun,
    begun_scaled,
    given,
    y_first,
    y_second,
    x_first,
    x_second,
    inv_diag,
    kap,
    grp,
    extra,
    facts,
    ctab,
    zmat,
    image,
    smoothed,
    msg,
    scaled,
    slope_z,
    edge,
):
    place = Place()
    weight = ctab[T_W]
    corner = float(SCALED[0, 0])

    def before(row, count=8):
        rows = pl.ds(row, count)
        return place.before_x(x_first[rows, :], x_second[rows, :])

    def after(row, count=8):
        rows = pl.ds(row, count)
        return place.after_x(x_first[rows, :], x_second[rows, :])

    image[...] = begun[...]
    scaled[...] = begun_scaled[...]
    for side, (ex, a) in enumerate(OUTER):
        for ey in range(2):
            tile = got_x_sum(place, begun[ex, a, ey], 0, ex, ey, x_first, x_second)
            image[ex, a, ey] = tile
            scaled[ex, a, ey] = tile * inv_diag[ex, a, ey] * float(1.0 / THETA)
            edge[side, ey] = scaled[ex, a, ey]
    edge[...] = along_z(edge[...].reshape(32, LANES), zmat[2]).reshape(edge.shape)
    there_x = (place.prev_x, place.next_x)
    zero = jnp.zeros(TILE, jnp.float32)
    tiles = [[[None, None] for _ in range(8)] for _ in range(2)]
    for ex in range(2):
        a_out = OUTER[ex][1]
        rows = inner_along_y(
            place, y_first, y_second, before, after, ex, a_out, SMOOTH_Y, SMOOTH_EDGE
        )
        for ey in range(2):
            values = [scaled[ex, a, ey] for a in range(8)]
            slopes = along_x(SCALED, values, 1)
            far_row = beyond_y(place, ey)
            beside = kap[pl.ds((ex + 1) * 4 + 3 * ey, 1), :]
            kappa = kap[pl.ds((ex + 1) * 4 + ey + 1, 1), :] + jnp.where(far_row, beside, 0.0)
            for a in range(8):
                if a != a_out:
                    acc = given[ex, a, ey]
                else:
                    value, flat = values[a], edge[ex, ey]
                    acc, slope_y, turned_y = cross_image(
                        place, ctab, kap, value, flat, rows[ey], ex, ey
                    )
                    x_next = 3 * ex
                    get = before if ex == 0 else after
                    turned_x = get(SMOOTH_X + ey * 8) + corner * value
                    side = kap[pl.ds(x_next * 4 + ey + 1, 1), :] * (turned_x + slope_y + flat)
                    far = kap[pl.ds(x_next * 4 + 3 * ey, 1), :] * (turned_x + turned_y + flat)
                    side = side + sigma_p * value
                    side = side + jnp.where(far_row, far + sigma_p * value, zero)
                    acc = acc + jnp.where(there_x[ex], side, zero)
                acc = acc + kappa * slopes[a]
                tiles[ex][a][ey] = place.join_z(acc * (float(WEIGHTS[a]) * weight))
    join_own(place, tiles)
    inv_mult = [1.0 / place.mult_tile(ey) for ey in range(2)]
    sums = [[jnp.zeros(TILE, jnp.float32) for _ in range(2)] for _ in range(2)]
    square = jnp.zeros(TILE, jnp.float32)
    for ex in range(2):
        for a in range(8):
            for ey in range(2):
                value = image[ex, a, ey]
                defect = (value - tiles[ex][a][ey]) * inv_diag[ex, a, ey]
                update = scaled[ex, a, ey]
                result = (
                    float(1.0 + RHO_NEXT * RHO) * update + float(2.0 * RHO_NEXT / DELTA) * defect
                )
                smoothed[ex, a, ey] = result
                weighed = value * (inv_mult[ey] * place.inv_x(ex, a))
                sums[ex][ey] = sums[ex][ey] + weighed
                square = square + weighed * result
    own_sums = restricted(place, sums, grp)
    if msg.shape[2] == LANES:
        sums = [extra[:, pl.ds(k, 1)] for k in range(2)]
        send_to_all(msg, message(place, own_sums, sums))
        return
    slope_z[...] = along_z(smoothed[...].reshape(256, LANES), zmat[2]).reshape(slope_z.shape)
    energy = jnp.zeros(TILE, jnp.float32)
    for ex in range(2):
        for ey in range(2):
            values, images = own_operator(ctab, kap, smoothed, slope_z, ex, ey)
            for a in range(8):
                energy = energy + values[a] * images[a]
                tiles[ex][a][ey] = place.join_z(images[a])
    join_own(place, tiles)
    sums = [extra[:, pl.ds(k, 1)] for k in range(2)] + [total(square), total(energy)]
    row = message(place, own_sums, sums, AWAY, BEYOND)
    row = row + restricted_around(place, tiles, inv_mult, grp)
    send_to_all(msg, jnp.concatenate([row, facts[:, LANES:]], axis=1))


def restricted_around(place, tiles, inv_mult, grp):
    lane = lax.broadcasted_iota(jnp.int32, (1, LANES), 1)
    weighed = [
        [[tiles[ex][a][ey] * (inv_mult[ey] * place.inv_x(ex, a)) for ey in range(2)] for a in range(8)]
        for ex in range(2)
    ]

    def rows_of(tile, y):
        if y == 0:
            return jnp.where(place.row == 0, tile[0], 0.0)
        if y == 3:
            return jnp.where(place.row == 7, tile[1], 0.0)
        return tile[y - 1]

    there_x = (place.prev_x, None, None, place.next_x)
    there_y = (place.prev_y, None, None, place.next_y)
    by_device = [
        [[jnp.zeros(TILE, jnp.float32) for _ in range(NCD)] for _ in range(3)] for _ in range(3)
    ]
    for x in range(4):
        for y in range(4):
            if x == 0:
                acc = rows_of(weighed[0][0], y)
            elif x == 3:
                acc = rows_of(weighed[1][7], y)
            else:
                acc = rows_of(weighed[x - 1][0], y)
                for a in range(1, 8):
                    acc = acc + rows_of(weighed[x - 1][a], y)
            for there in (there_x[x], there_y[y]):
                if there is not None:
                    acc = jnp.where(there, acc, 0.0)
            group = grp[pl.ds(x * 4 + y, 1), :]
            device = by_device[(x + 1) // 2][(y + 1) // 2]
            for c in range(NCD):
                device[c] = device[c] + jnp.where(group == float(c), acc, 0.0)
    row = jnp.zeros((1, LANES), jnp.float32)
    for dx in range(3):
        for dy in range(3):
            at = ((place.ix + dx - 1) * place.ny + place.iy + dy - 1) * NCD
            for c in range(NCD):
                row = row + jnp.where(lane == at + c, total(by_device[dx][dy][c]), 0.0)
    return row


def coarse_part(place, blocks, got, coarse, grp, others=()):
    lane = lax.broadcasted_iota(jnp.int32, (1, LANES), 1)
    values = [jnp.zeros((1, LANES), jnp.float32) for _ in range(blocks)]
    per = LANES // NCD
    for j in range(blocks):

        def gather(i, acc, j=j):
            return jnp.where(lane // NCD == i, got[j * per + i, pl.ds(0, 1), :], acc)

        values[j] = lax.fori_loop(0, per, gather, values[j], unroll=blocks == 1)
        for there, device, row in others:
            spot = (lane // NCD == device % per) & (device // per == j) & there
            values[j] = jnp.where(spot, row, values[j])

    def solved(dx, dy, c):
        acc = None
        for j in range(blocks):
            term = coarse[pl.ds(((dx * 3 + dy) * NCD + c) * blocks + j, 1), :] * values[j]
            acc = term if acc is None else acc + term
        return jnp.sum(acc, axis=1, keepdims=True)

    return prolonged(place, solved, grp)


def prolonged(place, solved, grp):
    device = [[[solved(dx, dy, c) for c in range(NCD)] for dy in range(3)] for dx in range(3)]
    inv_z = jnp.where(place.low_z | place.high_z, 0.5, 1.0)
    rows = []
    for x in range(4):
        line = []
        for y in range(4):
            group = grp[pl.ds(x * 4 + y, 1), :]
            acc = jnp.zeros((1, LANES), jnp.float32)
            for c in range(NCD):
                acc = acc + jnp.where(
                    group == float(c), device[(x + 1) // 2][(y + 1) // 2][c], 0.0
                )
            line.append(place.join_z(jnp.broadcast_to(acc, TILE)) * inv_z)
        rows.append(line)
    low_y = jnp.where(place.prev_y, 0.5, 1.0)
    high_y = jnp.where(place.next_y, 0.5, 1.0)

    def tile(ex, kind, ey):
        if kind == 1:
            vals = [rows[ex + 1][y] for y in range(4)]
        elif kind == 0:
            scale = place.inv_x(ex, 0)
            vals = [(rows[ex][y] + rows[ex + 1][y]) * scale for y in range(4)]
        else:
            scale = place.inv_x(ex, 7)
            vals = [(rows[ex + 1][y] + rows[ex + 2][y]) * scale for y in range(4)]
        mid = vals[ey + 1]
        low = (vals[ey] + mid) * (low_y if ey == 0 else 0.5)
        high = (mid + vals[ey + 2]) * (high_y if ey == 1 else 0.5)
        return jnp.where(place.row == 0, low, jnp.where(place.row == 7, high, mid))

    return tile


def kind_of(a):
    return 0 if a == 0 else (2 if a == 7 else 1)


def own_operator(ctab, kap, field, slope_z, ex, ey):
    weight = ctab[T_W]
    tiles = [field[ex, a, ey] for a in range(8)]
    slopes = along_x(SCALED, tiles, 1)
    kappa = kap[pl.ds((ex + 1) * 4 + ey + 1, 1), :]
    out = []
    for a in range(8):
        stiff = slopes[a] + along_y(ctab, T_K, tiles[a]) + slope_z[ex, a, ey]
        out.append((kappa * stiff + sigma_p * tiles[a]) * (float(WEIGHTS[a]) * weight))
    return tiles, out


def first_direction_kernel(
    blocks,
    got,
    relayed,
    coarse,
    grp,
    kap,
    inv_diag,
    resid,
    own,
    ctab,
    zmat,
    direction,
    out,
    inner_x,
    first,
    second,
    extra,
    slope_z,
    image,
):
    place = Place()
    inv_mult = [1.0 / place.mult_tile(ey) for ey in range(2)]
    across = Pairing(place)
    others = []
    for side in range(2):
        there, ix = across.beside(side)
        others.append((there, ix * place.ny + place.iy, relayed[pl.ds(side * 8, 1), :]))
    others.append(
        (across.has_far, place.ix * place.ny + across.far, relayed[pl.ds(16, 1), :])
    )
    part = coarse_part(place, blocks, got, coarse, grp, others)
    image[...] = own[...]
    far_edge = jnp.where(across.even, 0, 7)

    def add_row(ex, a, row, edge, low):
        extra = jnp.where(place.row == edge, row, 0.0)
        image[ex, a, 0] = image[ex, a, 0] + jnp.where(low, extra, 0.0)
        image[ex, a, 1] = image[ex, a, 1] + jnp.where(low, 0.0, extra)

    for ex in range(2):
        for a in range(8):
            row = relayed[pl.ds(RELAY_FACE + ex * 8 + a, 1), :]
            add_row(ex, a, row, 7 - far_edge, ~across.even)

    @pl.when(across.has_far)
    def _():
        for a in range(8):
            row = got[place.ix * place.ny + across.far, pl.ds(a, 1), :]
            add_row(0, a, row, far_edge, across.even)
            if a == 7:
                add_row(1, 0, row, far_edge, across.even)
            if a > 0:
                add_row(1, a, relayed[pl.ds(16 + a, 1), :], far_edge, across.even)

    for side, (ex, a) in enumerate(OUTER):
        there, ix = across.beside(side)

        @pl.when(there)
        def _():
            low = got[ix * place.ny + place.iy]
            high = jnp.where(
                place.row == 0, pltpu.roll(low, 1, 0), relayed[pl.ds(side * 8, 8), :]
            )
            image[ex, a, 0] = image[ex, a, 0] + low
            image[ex, a, 1] = image[ex, a, 1] + high
            corner = jnp.where(
                across.even,
                relayed[pl.ds(RELAY_EDGE + side, 1), :],
                got[ix * place.ny + across.twin, pl.ds(7, 1), :],
            )
            add_row(ex, a, corner, 7 - far_edge, ~across.even)

        @pl.when(there & across.has_far)
        def _():
            corner = got[ix * place.ny + across.far, pl.ds(1, 1), :]
            add_row(ex, a, corner, far_edge, across.even)

    energy = jnp.zeros(TILE, jnp.float32)
    for ex in range(2):
        for ey in range(2):
            kinds = [part(ex, kind, ey) for kind in range(3)]
            for a in range(8):
                known = resid[ex, a, ey]
                inverse = inv_diag[ex, a, ey]
                defect = (known - image[ex, a, ey]) * inverse
                value = (
                    float((1.0 + RHO_NEXT * RHO) / THETA) * (known * inverse)
                    + float(2.0 * RHO_NEXT / DELTA) * defect
                    + kinds[kind_of(a)]
                )
                direction[ex, a, ey] = value
                scale = place.inv_x(ex, a)
                energy = energy + value * known * (inv_mult[ey] * scale)
    slope_z[...] = along_z(direction[...].reshape(256, LANES), zmat[2]).reshape(slope_z.shape)
    curvature = jnp.zeros(TILE, jnp.float32)
    tiles = [[[None, None] for _ in range(8)] for _ in range(2)]
    for ex in range(2):
        for ey in range(2):
            values, images = own_operator(ctab, kap, direction, slope_z, ex, ey)
            for a in range(8):
                curvature = curvature + values[a] * images[a]
                tiles[ex][a][ey] = place.join_z(images[a])
    join_own(place, tiles)
    for ex in range(2):
        for a in range(8):
            for ey in range(2):
                out[ex, a, ey] = tiles[ex][a][ey]
    store_y_faces(place, out, first, second, (), 0)

    def tile_of(ex, a, ey):
        return tiles[ex][a][ey] * inv_diag[ex, a, ey] * float(1.0 / THETA)

    def column_of(ex, ey):
        return [tile_of(ex, a, ey) for a in range(8)]

    store_inner(
        place, SCALED, ctab[T_KBOTTOM], ctab[T_KTOP], column_of, tile_of, inner_x, first, second,
        SMOOTH_Y, SMOOTH_EDGE,
    )
    lane = lax.broadcasted_iota(jnp.int32, (1, LANES), 1)
    extra[...] = jnp.where(lane == 0, total(energy), total(curvature))


def gathered_scalars(got, count):
    lane = lax.broadcasted_iota(jnp.int32, (1, LANES), 1)
    per = LANES // NCD
    sums = []
    for c in range(count):
        acc = jnp.zeros((1, LANES), jnp.float32)

        def gather(i, acc, c=c):
            return acc + jnp.where(lane == ((i + 1) % per) * NCD + c, got[i], 0.0)

        acc = lax.fori_loop(0, got.shape[0], gather, acc, unroll=got.shape[0] <= per)
        sums.append(jnp.sum(acc, axis=1, keepdims=True))
    return sums


def second_direction_kernel(
    blocks,
    got,
    coarse,
    grp,
    kap,
    resid,
    direction,
    image,
    smoothed,
    ctab,
    zmat,
    following,
    known,
    msg,
    slope_z,
):
    place = Place()
    inv_mult = [1.0 / place.mult_tile(ey) for ey in range(2)]
    part = coarse_part(place, blocks, got, coarse, grp)
    energy, curvature = gathered_scalars(got, 2)
    step = energy / curvature
    lane = lax.broadcasted_iota(jnp.int32, (1, LANES), 1)
    known[...] = jnp.where(lane == 0, energy, jnp.where(lane == 1, curvature, 0.0))
    energy_next = jnp.zeros(TILE, jnp.float32)
    cross = jnp.zeros(TILE, jnp.float32)
    for ex in range(2):
        for ey in range(2):
            kinds = [part(ex, kind, ey) for kind in range(3)]
            for a in range(8):
                value = direction[ex, a, ey] - step * (smoothed[ex, a, ey] + kinds[kind_of(a)])
                following[ex, a, ey] = value
                weighed = value * (inv_mult[ey] * place.inv_x(ex, a))
                was = image[ex, a, ey]
                energy_next = energy_next + weighed * (resid[ex, a, ey] - step * was)
                cross = cross + weighed * was
    slope_z[...] = along_z(following[...].reshape(256, LANES), zmat[2]).reshape(slope_z.shape)
    square = jnp.zeros(TILE, jnp.float32)
    for ex in range(2):
        for ey in range(2):
            values, images = own_operator(ctab, kap, following, slope_z, ex, ey)
            for a in range(8):
                square = square + values[a] * images[a]
    send_to_all(msg, message(place, [], [total(energy_next), total(square), total(cross)]))


def pressure_kernel(got, known, direction, following, pressure):
    energy = known[:, pl.ds(0, 1)]
    curvature = known[:, pl.ds(1, 1)]
    energy_next, square, cross = gathered_scalars(got, 3)
    ratio = energy_next / energy
    step = energy / curvature
    step_next = energy_next / (square + 2.0 * ratio * cross + ratio * ratio * curvature)
    weight_old = step + step_next * ratio
    for ex in range(2):
        for a in range(8):
            for ey in range(2):
                pressure[ex, a, ey] = (
                    weight_old * direction[ex, a, ey] + step_next * following[ex, a, ey]
                )


def coarse_energy(place, got, values, kappa, number):
    lane, row = place.lane, place.row
    for ex in range(2):
        for gx in range(8):
            own = jnp.zeros((1, LANES), jnp.float32)
            group = jnp.zeros((1, LANES), jnp.float32)
            spot = lane[0:1] // 32
            for gy in range(4):
                line = got[gx * 4 + gy, :, pl.ds(LANES, LANES)]
                own = jnp.where(spot == (gy + 2 * ex) % 4, line, own)
                group = jnp.where(spot == (gy + 1 + 2 * ex) % 4, line, group)
            kappa[ex, pl.ds(gx, 1), :] = own
            number[ex, pl.ds(gx, 1), :] = group
    grid = [jnp.zeros(TILE, jnp.float32) for _ in range(2)]
    numbers = [pltpu.roll(number[0], 96, 1), pltpu.roll(number[1], 32, 1)]
    kappa = [kappa[0], pltpu.roll(kappa[1], 64, 1)]
    for q in range(4):
        for c in range(NCD):
            mine = jnp.where(lane == row * 16 + q * 4 + c, values, 0.0)
            mine = jnp.sum(mine, axis=1, keepdims=True)
            for ex in range(2):
                chosen = (lane // 32 == q) & (numbers[ex] == float(c))
                grid[ex] = jnp.where(chosen, mine, grid[ex])

    def ends_y(v):
        low = jnp.where(lane >= 16, 0.5 * (v + pltpu.roll(v, 16, 1)), v)
        return low, v, jnp.where(lane < 112, 0.5 * (v + pltpu.roll(v, 112, 1)), v)

    def ends_z(v):
        low = jnp.where(lane % 16 > 0, 0.5 * (v + pltpu.roll(v, 1, 1)), v)
        return low, v, jnp.where(lane % 16 < 15, 0.5 * (v + pltpu.roll(v, 127, 1)), v)

    low = jnp.where(row > 0, 0.5 * (grid[0] + pltpu.roll(grid[1], 1, 0)), grid[0])
    mid = 0.5 * (grid[0] + grid[1])
    high = jnp.where(row < 7, 0.5 * (grid[1] + pltpu.roll(grid[0], 7, 0)), grid[1])
    mass = [float(WEIGHTS[0]), float(np.sum(WEIGHTS[1:7])), float(WEIGHTS[7])]
    links = (
        (0, 1, -float(np.sum(STIFF[0, 1:7]))),
        (0, 2, -float(STIFF[0, 7])),
        (1, 2, -float(np.sum(STIFF[7, 1:7]))),
    )
    energy = jnp.zeros(TILE, jnp.float32)
    for ex, line in enumerate(((low, grid[0], mid), (mid, grid[1], high))):
        nodes = [[ends_z(v) for v in ends_y(w)] for w in line]
        stiff = jnp.zeros(TILE, jnp.float32)
        square = jnp.zeros(TILE, jnp.float32)
        for i in range(3):
            for j in range(3):
                for k, l, weight in links:
                    factor = weight * mass[i] * mass[j]
                    for first, second in (
                        (nodes[k][i][j], nodes[l][i][j]),
                        (nodes[i][k][j], nodes[i][l][j]),
                        (nodes[i][j][k], nodes[i][j][l]),
                    ):
                        gap = first - second
                        stiff = stiff + (factor * gap) * gap
                for k in range(3):
                    value = nodes[i][j][k]
                    square = square + (mass[i] * mass[j] * mass[k] * value) * value
        energy = energy + kappa[ex] * stiff + sigma_p * square
    return total(energy)


def finish_kernel(
    got, grp, direction, smoothed, pressure, matrix, kappa, number
):
    place = Place()
    per = LANES // NCD
    row_lane = lax.broadcasted_iota(jnp.int32, (1, LANES), 1)
    rest = jnp.zeros((1, LANES), jnp.float32)
    dual = jnp.zeros((1, LANES), jnp.float32)
    scalars = jnp.zeros((1, LANES), jnp.float32)
    for i in range(per):
        line = got[i, :, pl.ds(0, LANES)]
        mine = row_lane // NCD == (i + AWAY) % per
        known = row_lane // NCD == (i + BEYOND) % per
        rest = jnp.where(mine, line, rest)
        dual = dual + jnp.where(mine | known, 0.0, line)
        scalars = jnp.where(known, line, scalars)
        for c in range(NCD):
            block = got[i, :, pl.ds((2 + c) * LANES, LANES)]
            matrix[pl.ds(i * NCD + c, 1), :] = block
    rest = pltpu.roll(rest, (per - AWAY) * NCD, 1)
    energy, curvature, square, self_energy = [
        jnp.sum(jnp.where(row_lane % NCD == c, scalars, 0.0), axis=1, keepdims=True)
        for c in range(4)
    ]
    values = exact_dot(jnp.broadcast_to(rest, TILE), matrix[...])
    line = values[0:1]
    cross = square + jnp.sum(line * rest, axis=1, keepdims=True)
    both = self_energy + 2.0 * jnp.sum(line * dual, axis=1, keepdims=True)
    both = both + coarse_energy(place, got, values, kappa, number)
    step = energy / curvature
    energy_next = step * step * cross - energy
    ratio = energy_next / energy
    with_image = curvature - step * cross
    with_itself = curvature - 2.0 * step * cross + step * step * both
    step_next = energy_next / (
        with_itself + 2.0 * ratio * with_image + ratio * ratio * curvature
    )
    old = step + step_next * (1.0 + ratio)
    new = -step_next * step

    def solved(dx, dy, c):
        at = ((place.ix + dx - 1) * place.ny + place.iy + dy - 1) * NCD + c
        return jnp.sum(jnp.where(row_lane == at, line, 0.0), axis=1, keepdims=True)

    part = prolonged(place, masked(place, solved), grp)
    for ex in range(2):
        for ey in range(2):
            kinds = [part(ex, kind, ey) for kind in range(3)]
            for a in range(8):
                pressure[ex, a, ey] = old * direction[ex, a, ey] + new * (
                    smoothed[ex, a, ey] + kinds[kind_of(a)]
                )


def masked(place, solved):
    there_x = (place.prev_x, None, place.next_x)
    there_y = (place.prev_y, None, place.next_y)

    def value(dx, dy, c):
        out = solved(dx, dy, c)
        for there in (there_x[dx], there_y[dy]):
            if there is not None:
                out = jnp.where(there, out, 0.0)
        return out

    return value


def call(body, outs, scratch=(), **more):
    return pl.pallas_call(
        body,
        out_shape=[jax.ShapeDtypeStruct(shape, jnp.float32) for shape in outs],
        scratch_shapes=[
            pltpu.VMEM(shape, jnp.float32) if isinstance(shape, tuple) else shape
            for shape in scratch
        ],
        **more,
        compiler_params=pltpu.CompilerParams(vmem_limit_bytes=24 * 1024 * 1024),
    )


def swap(first, second, axis):
    along, across = lax.axis_size("gx"), lax.axis_size("gy")

    def number(ix, iy):
        return ix * across + iy

    pairs = ([], [])
    for ix in range(along):
        for iy in range(across):
            at, count = (ix, along) if axis == "gx" else (iy, across)
            for k, to in enumerate((at ^ 1, ((at + 1) ^ 1) - 1)):
                if 0 <= to < count:
                    there = (to, iy) if axis == "gx" else (ix, to)
                else:
                    there = (ix, iy ^ 1) if axis == "gx" else (ix, across - 1 - iy)
                pairs[k].append((number(ix, iy), number(*there)))
    pairs = pairs[::-1]
    first_got = lax.ppermute(first, BOTH, pairs[0])
    return first_got, lax.ppermute(second, BOTH, pairs[1])


def per_device(fields, viscosity, inv_density, elem_group, coarse_inverse):
    length = fields.shape[5]
    elems_z = length // NODES
    devices = lax.axis_size("gx") * lax.axis_size("gy")
    blocks = coarse_inverse.shape[1] // LANES
    pack_rows = 1 + NCD * blocks
    tiles_np, mats_np = constant_tables(elems_z)
    ctab, zmat = jnp.asarray(tiles_np), jnp.asarray(mats_np)
    one = fields.shape[1:]
    four = fields.shape
    faces = (64, LANES)
    xf_shape = (2, 4, 2, 8, LANES)
    inner_shape = (2, 2, 8, LANES)
    y_shape, x_shape = (STEP_PACK + 3 * pack_rows, LANES), (STEP_PACK, LANES)
    turned = (64 + pack_rows, LANES)
    smooth_shape = (SMOOTH_ROWS, LANES)
    rows = (devices, 1, LANES)
    grid_fits = (
        blocks == 1
        and lax.axis_size("gx") == 8
        and lax.axis_size("gy") * fields.shape[3] * elems_z == LANES
    )

    def exchange_all(msg):
        return lax.all_to_all(msg, BOTH, 0, 0, tiled=True)

    beside = pl.CostEstimate(flops=10**7, bytes_accessed=10**6, transcendentals=0)
    first, second = call(faces_kernel, [faces, faces], [xf_shape])(fields)
    numbers = elem_group.astype(jnp.float32)
    row = jnp.stack([inv_density, numbers], 1).reshape(1, LANES)
    pack = jnp.concatenate([row, coarse_inverse.reshape(NCD * blocks, LANES)], 0)
    (facts,) = call(facts_kernel, [(1, 6 * LANES)], cost_estimate=beside)(pack)
    summed, xf = call(mass_kernel, [four, xf_shape], cost_estimate=beside)(fields)
    y_got = swap(first, second, "gy")
    first, second = call(functools.partial(turn_faces_kernel, pack_rows), [turned, turned])(
        xf, pack, *y_got
    )
    side_got = x_got = swap(first, second, "gx")
    edge_shape = (4, 2, 2, 8, LANES)
    begun, given, slope, answer = call(
        prepare_kernel, [four, four, edge_shape, one], [four, four], cost_estimate=beside
    )(summed, viscosity, *y_got, ctab, zmat)
    share, xf, inner_x, first, second = call(
        functools.partial(rhs_kernel, pack_rows),
        [four, xf_shape, inner_shape, y_shape, y_shape],
        [edge_shape, edge_shape, edge_shape, edge_shape],
    )(begun, given, slope, answer, viscosity, pack, *x_got, ctab, zmat)
    y_got = swap(first, second, "gy")
    first, second = call(turn_step_kernel, [x_shape, x_shape])(xf, inner_x, *y_got)
    x_got = swap(first, second, "gx")
    inv_diag, kap, grp, coarse = call(
        functools.partial(setup_kernel, pack_rows, blocks),
        [one, (16, LANES), (16, LANES), (9 * NCD * blocks, LANES)],
        [(16, LANES), (8, 16, LANES)],
        cost_estimate=beside,
    )(pack, *side_got, *y_got, ctab)
    begun, given = call(approach_kernel, [four, one], [one], cost_estimate=beside)(
        share, *y_got, ctab, zmat
    )
    side_shape = (2, 2, 8, LANES)
    fields_got = x_got
    fields_begun = begun
    resid, own, msg = call(
        advance_kernel,
        [one, one, (devices, 8, LANES)],
        [one, one, side_shape, one, (3,) + side_shape],
    )(begun, given, *y_got, *x_got, inv_diag, kap, grp, ctab, zmat)
    got = exchange_all(msg)
    (relayed,) = call(relay_kernel, [(RELAY_ROWS, LANES)])(got, own)
    relayed = lax.ppermute(
        relayed, "gy", [(i, i ^ 1) for i in range(lax.axis_size("gy")) if i ^ 1 < lax.axis_size("gy")]
    )
    direction, own, inner_x, first, second, extra = call(
        functools.partial(first_direction_kernel, blocks),
        [one, one, inner_shape, smooth_shape, smooth_shape, (1, LANES)],
        [one, one],
    )(got, relayed, coarse, grp, kap, inv_diag, resid, own, ctab, zmat)
    y_got = swap(first, second, "gy")
    first, second = call(turn_smooth_kernel, [smooth_shape, smooth_shape])(own, inner_x, *y_got)
    x_got = swap(first, second, "gx")
    fields_new, extra = call(emit_kernel, [four, (1, LANES)], cost_estimate=beside)(
        fields_begun, *fields_got, extra
    )
    begun, begun_scaled, given = call(
        ready_kernel, [one, one, one], [one], cost_estimate=beside
    )(own, *y_got, inv_diag, kap, ctab, zmat)
    image, image_smoothed, msg = call(
        smooth_kernel,
        [one, one, (devices, 1, 6 * LANES) if grid_fits else rows],
        [one, one, side_shape],
    )(
        begun, begun_scaled, given, *y_got, *x_got, inv_diag, kap, grp, extra, facts, ctab, zmat
    )
    got = exchange_all(msg)
    if grid_fits:
        (pressure,) = call(
            finish_kernel, [one], [(LANES, LANES), (2,) + TILE, (2,) + TILE]
        )(got, grp, direction, image_smoothed)
        return (fields_new, pressure)
    following, known, msg = call(
        functools.partial(second_direction_kernel, blocks), [one, (1, LANES), rows], [one]
    )(got, coarse, grp, kap, resid, direction, image, image_smoothed, ctab, zmat)
    got = exchange_all(msg)
    (pressure,) = call(pressure_kernel, [one])(got, known, direction, following)
    return (fields_new, pressure)


def solution(mesh):
    placed = (
        P(None, "gx", None, "gy", None, None),
        P("gx", None, "gy", None, None),
        P("gx", "gy", None),
        P("gx", "gy", None),
        P(("gx", "gy"), None),
    )
    return jax.shard_map(
        per_device,
        mesh=mesh,
        in_specs=placed,
        out_specs=(P(None, "gx", None, "gy", None, None), P("gx", None, "gy", None, None)),
        check_vma=False,
    )
```

```python
import functools

import jax
import jax.numpy as jnp
import ml_dtypes
import numpy as np
from jax import lax
from jax.experimental import pallas as pl
from jax.experimental.pallas import tpu as pltpu
from jax.sharding import PartitionSpec as P

NCD = 4
NODES = 8
LANES = 128
TILE = (8, 128)
BOTH = ("gx", "gy")

dt_step = 0.01
sigma_p = 4.0
prandtl = 0.7
cheb_ratio = 0.1


def tables():
    points = np.array(
        [
            -1.0,
            -0.8717401485096066,
            -0.5917001814331423,
            -0.2092992179024789,
            0.2092992179024789,
            0.5917001814331423,
            0.8717401485096066,
            1.0,
        ]
    )
    weights = np.array(
        [
            1.0 / 28.0,
            0.2107042271435061,
            0.3411226924835044,
            0.4124587946587038,
            0.4124587946587038,
            0.3411226924835044,
            0.2107042271435061,
            1.0 / 28.0,
        ]
    )
    identity = np.eye(8)
    differ = points[:, None] - points[None, :] + identity
    barycentric = 1.0 / np.prod(differ, axis=1)
    offdiag = barycentric[None, :] / barycentric[:, None] / differ * (1.0 - identity)
    derivative = offdiag - identity * np.sum(offdiag, axis=1)[:, None]
    mass_one = identity * weights[None, :]
    stiff_one = derivative.T @ mass_one @ derivative
    stiff_three = (
        np.kron(np.kron(stiff_one, mass_one), mass_one)
        + np.kron(np.kron(mass_one, stiff_one), mass_one)
        + np.kron(np.kron(mass_one, mass_one), stiff_one)
    )
    three_diag = np.sum(stiff_three * np.eye(512), axis=1)
    spectral_bound = float(np.max(np.sum(np.abs(stiff_three), axis=1) / three_diag))
    return (derivative, weights, stiff_one, spectral_bound)


DERIV, WEIGHTS, STIFF, BOUND = tables()
SCALED = STIFF / WEIGHTS[:, None]
LINE = np.diag(STIFF) / WEIGHTS
THETA = 0.5 * (BOUND + cheb_ratio * BOUND)
DELTA = 0.5 * (BOUND - cheb_ratio * BOUND)
RHO = DELTA / THETA
RHO_NEXT = 1.0 / (2.0 * THETA / DELTA - RHO)


def constant_tables(elems_z):
    def turned(matrix):
        rows = np.arange(8)
        return [np.repeat(matrix[rows, (rows - s) % 8][:, None], LANES, 1) for s in range(8)]

    wz = np.tile(WEIGHTS, elems_z)
    kz = np.tile(LINE, elems_z)
    tiles = turned(DERIV) + turned(DERIV.T) + turned(SCALED)
    tiles += [WEIGHTS[:, None] * wz[None, :], LINE[:, None] + kz[None, :]]
    for matrix in (DERIV, SCALED):
        for node in (7, 0):
            inner = matrix[node] * (np.arange(8) != node)
            tiles.append(np.repeat(inner[:, None], LANES, 1))
    eye = np.eye(elems_z)
    mats = [np.kron(eye, DERIV.T), np.kron(eye, DERIV), np.kron(eye, SCALED.T)]
    halves = []
    for mat in mats:
        high = mat.astype(ml_dtypes.bfloat16)
        low = (mat - high.astype(np.float64)).astype(ml_dtypes.bfloat16)
        both = np.concatenate([high, low], 1)
        halves.append(np.concatenate([both, both], 0))
    return np.stack(tiles).astype(np.float32), np.stack(halves)


T_D, T_DT, T_K, T_W, T_LINE = 0, 8, 16, 24, 25
T_TOP, T_BOTTOM, T_KTOP, T_KBOTTOM = 26, 27, 28, 29


class Place:
    def __init__(self):
        self.ix = lax.axis_index("gx")
        self.iy = lax.axis_index("gy")
        self.nx = lax.axis_size("gx")
        self.ny = lax.axis_size("gy")
        self.even_x = self.ix % 2 == 0
        self.even_y = self.iy % 2 == 0
        self.row = lax.broadcasted_iota(jnp.int32, TILE, 0)
        self.lane = lax.broadcasted_iota(jnp.int32, TILE, 1)
        self.low_z = (self.lane % 8 == 0) & (self.lane > 0)
        self.high_z = (self.lane % 8 == 7) & (self.lane < LANES - 1)
        self.prev_x = self.ix > 0
        self.next_x = self.ix < self.nx - 1
        self.prev_y = self.iy > 0
        self.next_y = self.iy < self.ny - 1

    def mult_tile(self, ey):
        along_z = 1.0 + jnp.where(self.low_z | self.high_z, 1.0, 0.0)
        low = 1.0 if ey == 1 else jnp.where(self.prev_y, 1.0, 0.0)
        high = 1.0 if ey == 0 else jnp.where(self.next_y, 1.0, 0.0)
        along_y = 1.0 + jnp.where(self.row == 0, low, jnp.where(self.row == 7, high, 0.0))
        return along_y * along_z

    def inv_x(self, ex, a):
        if a == 0:
            return 0.5 if ex == 1 else jnp.where(self.prev_x, 0.5, 1.0)
        if a == 7:
            return 0.5 if ex == 0 else jnp.where(self.next_x, 0.5, 1.0)
        return 1.0

    def mult_x(self, ex, a):
        if a == 0:
            return 2.0 if ex == 1 else jnp.where(self.prev_x, 2.0, 1.0)
        if a == 7:
            return 2.0 if ex == 0 else jnp.where(self.next_x, 2.0, 1.0)
        return 1.0

    def share_x(self, ex, a):
        if (ex, a) == (0, 0):
            return jnp.where(self.prev_x, 0.5, 1.0)
        if (ex, a) == (1, 7):
            return jnp.where(self.next_x, 0.5, 1.0)
        return 1.0

    def share_y(self, ey):
        if ey == 0:
            return jnp.where((self.row == 0) & self.prev_y, 0.5, 1.0)
        return jnp.where((self.row == 7) & self.next_y, 0.5, 1.0)

    def inv_y(self, ey):
        low = 0.5 if ey == 1 else jnp.where(self.prev_y, 0.5, 1.0)
        high = 0.5 if ey == 0 else jnp.where(self.next_y, 0.5, 1.0)
        return jnp.where(self.row == 0, low, jnp.where(self.row == 7, high, 1.0))

    def inv_z(self):
        return jnp.where(self.low_z | self.high_z, 0.5, 1.0)

    def join_z(self, t):
        up = pltpu.roll(t, LANES - 1, 1)
        down = pltpu.roll(t, 1, 1)
        return t + jnp.where(self.high_z, up, jnp.where(self.low_z, down, 0.0))

    def to_low(self, below):
        return jnp.where(self.row == 0, pltpu.roll(below, 1, 0), 0.0)

    def to_high(self, above):
        return jnp.where(self.row == 7, pltpu.roll(above, 7, 0), 0.0)

    def join_y(self, below, above):
        return below + self.to_high(above), above + self.to_low(below)

    def before_x(self, first, second):
        return jnp.where(self.prev_x, jnp.where(self.even_x, first, second), 0.0)

    def after_x(self, first, second):
        return jnp.where(self.next_x, jnp.where(self.even_x, second, first), 0.0)

    def send_x(self, first, second):
        return jnp.where(self.even_x, second, first)

    def before_y(self, first, second):
        return jnp.where(self.prev_y, jnp.where(self.even_y, first, second), 0.0)

    def after_y(self, first, second):
        return jnp.where(self.next_y, jnp.where(self.even_y, second, first), 0.0)

    def send_y(self, first, second):
        return jnp.where(self.even_y, second, first)


def along_x(matrix, tiles, sign):
    even = [tiles[a] + tiles[7 - a] for a in range(4)]
    odd = [tiles[a] - tiles[7 - a] for a in range(4)]
    out = [None] * 8
    for i in range(4):
        plus, minus = None, None
        for a in range(4):
            p = float(0.5 * (matrix[i, a] + matrix[i, 7 - a])) * even[a]
            m = float(0.5 * (matrix[i, a] - matrix[i, 7 - a])) * odd[a]
            plus = p if plus is None else plus + p
            minus = m if minus is None else minus + m
        out[i] = plus + minus
        out[7 - i] = minus - plus if sign < 0 else plus - minus
    return out


def along_y(ctab, base, tile):
    acc = ctab[base] * tile
    for s in range(1, 8):
        acc = acc + ctab[base + s] * pltpu.roll(tile, s, 0)
    return acc


def exact_dot(rows, matrix):
    return jnp.dot(
        rows, matrix, precision=lax.Precision.HIGHEST, preferred_element_type=jnp.float32
    )


def along_z(rows, matrix):
    high = rows.astype(jnp.bfloat16)
    low = (rows - high.astype(jnp.float32)).astype(jnp.bfloat16)
    both = jnp.dot(
        jnp.concatenate([high, low], axis=1), matrix, preferred_element_type=jnp.float32
    )
    return both[:, :LANES] + both[:, LANES:]


def total(tile):
    return jnp.sum(jnp.sum(tile, axis=0, keepdims=True), axis=1, keepdims=True)


def store_y_faces(place, field, first_out, second_out, lead, at):
    for ex in range(2):
        for a in range(8):
            low = field[lead + (ex, a, 0, pl.ds(0, 1), slice(None))]
            high = field[lead + (ex, a, 1, pl.ds(7, 1), slice(None))]
            row = at + ex * 8 + a
            first_out[pl.ds(row, 1), :] = place.send_y(high, low)
            second_out[pl.ds(row, 1), :] = place.send_y(low, high)


def join_own(place, tiles):
    for ex in range(2):
        for a in range(8):
            tiles[ex][a] = list(place.join_y(*tiles[ex][a]))
    for ey in range(2):
        both = tiles[0][7][ey] + tiles[1][0][ey]
        tiles[0][7][ey] = both
        tiles[1][0][ey] = both


def weight_of(node):
    edge = jnp.minimum(node, 7 - node)
    value = jnp.where(edge == 2, float(WEIGHTS[2]), float(WEIGHTS[3]))
    return jnp.where(
        edge == 0, float(WEIGHTS[0]), jnp.where(edge == 1, float(WEIGHTS[1]), value)
    )


def faces_kernel(fields, first, second, edges):
    place = Place()
    weight = weight_of(place.row) * weight_of(place.lane % NODES) * float(WEIGHTS[0])
    for ch in range(4):
        for ex in range(2):
            for a in range(8):
                edges[0, ch, ex, pl.ds(a, 1), :] = fields[ch, ex, a, 0, pl.ds(0, 1), :]
                edges[1, ch, ex, pl.ds(a, 1), :] = fields[ch, ex, a, 1, pl.ds(7, 1), :]
    for ch in range(4):
        sides = [
            place.join_y(*[place.join_z(edges[side, ch, ex] * weight) for ex in range(2)])
            for side in range(2)
        ]
        for ex in range(2):
            rows = pl.ds(ch * 16 + ex * 8, 8)
            first[rows, :] = place.send_y(sides[1][ex], sides[0][ex])
            second[rows, :] = place.send_y(sides[0][ex], sides[1][ex])


def mass_kernel(fields, out, xf):
    place = Place()
    weight = weight_of(place.row) * weight_of(place.lane % NODES)
    for ch in range(4):
        tiles = [
            [
                [
                    place.join_z(fields[ch, ex, a, ey] * (float(WEIGHTS[a]) * weight))
                    for ey in range(2)
                ]
                for a in range(8)
            ]
            for ex in range(2)
        ]
        join_own(place, tiles)
        for ex in range(2):
            for a in range(8):
                for ey in range(2):
                    out[ch, ex, a, ey] = tiles[ex][a][ey]
        for ey in range(2):
            xf[0, ch, ey] = tiles[0][0][ey]
            xf[1, ch, ey] = tiles[1][7][ey]


def turn_faces(place, xf, y_first, y_second, first, second):
    for ch in range(4):
        sides = []
        for side in range(2):
            row = pl.ds(ch * 16 + 15 * side, 1)
            got_a, got_b = y_first[row, :], y_second[row, :]
            low = xf[side, ch, 0] + jnp.where(place.row == 0, place.before_y(got_a, got_b), 0.0)
            high = xf[side, ch, 1] + jnp.where(place.row == 7, place.after_y(got_a, got_b), 0.0)
            sides.append((low, high))
        for ey in range(2):
            rows = pl.ds(ch * 16 + ey * 8, 8)
            first[rows, :] = place.send_x(sides[1][ey], sides[0][ey])
            second[rows, :] = place.send_x(sides[0][ey], sides[1][ey])


def turn_faces_kernel(pack_rows, xf, pack, y_first, y_second, first, second):
    turn_faces(Place(), xf, y_first, y_second, first, second)
    first[pl.ds(64, pack_rows), :] = pack[...]
    second[pl.ds(64, pack_rows), :] = pack[...]


def turn_edges(place, inner_x, y_first, y_second, first, second, at, edge, inner_y):
    sides = []
    for side in range(2):
        row = pl.ds(edge + side, 1)
        got_a, got_b = y_first[row, :], y_second[row, :]
        low = inner_x[side, 0] + jnp.where(place.row == 0, place.before_y(got_a, got_b), 0.0)
        high = inner_x[side, 1] + jnp.where(place.row == 7, place.after_y(got_a, got_b), 0.0)
        sides.append((low, high))
    for ey in range(2):
        rows = pl.ds(at + ey * 8, 8)
        first[rows, :] = place.send_x(sides[1][ey], sides[0][ey])
        second[rows, :] = place.send_x(sides[0][ey], sides[1][ey])
    for k, pick in enumerate((place.before_y, place.after_y)):
        sides = []
        for side in range(2):
            row = pl.ds(inner_y + 15 * side, 1)
            sides.append(pick(y_first[row, :], y_second[row, :]))
        row = pl.ds(edge + k, 1)
        first[row, :] = place.send_x(sides[1], sides[0])
        second[row, :] = place.send_x(sides[0], sides[1])


STEP_U, STEP_V, STEP_EDGE, STEP_PACK = 64, 64, 80, 82


def turn_step_kernel(xf, inner_x, y_first, y_second, first, second):
    place = Place()
    turn_faces(place, xf, y_first, y_second, first, second)
    turn_edges(place, inner_x, y_first, y_second, first, second, STEP_U, STEP_EDGE, STEP_V)


def setup_kernel(
    pack_rows,
    blocks,
    pack,
    x_first,
    x_second,
    y_first,
    y_second,
    ctab,
    inv_diag,
    kap,
    grp,
    coarse,
    compact,
    spread,
):
    place = Place()
    beside = pl.ds(64, pack_rows)
    packs = [[None] * 3 for _ in range(3)]
    packs[0][1] = place.before_x(x_first[beside, :], x_second[beside, :])
    packs[1][1] = pack[...]
    packs[2][1] = place.after_x(x_first[beside, :], x_second[beside, :])
    for dx in range(3):
        rows = pl.ds(STEP_PACK + dx * pack_rows, pack_rows)
        packs[dx][0] = place.before_y(y_first[rows, :], y_second[rows, :])
        packs[dx][2] = place.after_y(y_first[rows, :], y_second[rows, :])
    compact[...] = jnp.zeros(compact.shape, jnp.float32)
    for dx in range(3):
        for dy in range(3):
            at = (dx * 3 + dy) * NCD * blocks
            coarse[pl.ds(at, NCD * blocks), :] = packs[dx][dy][1 : 1 + NCD * blocks]
            compact[pl.ds(dx * 3 + dy, 1), :] = packs[dx][dy][0:1]
    elems = LANES // NODES
    lane = lax.broadcasted_iota(jnp.int32, (LANES, LANES), 1)
    source = lax.broadcasted_iota(jnp.int32, (LANES, LANES), 0)
    for k in range(8):
        at = (k % 4 // 2) * 4 * elems + (k // 4) * 2 * elems + (k % 2) * elems
        spot = (source == at + lane // NODES).astype(jnp.float32)
        spread[k] = exact_dot(compact[...], spot)
    there_x = [jnp.where(place.prev_x, 1.0, 0.0), 1.0, jnp.where(place.next_x, 1.0, 0.0)]
    there_y = [jnp.where(place.prev_y, 1.0, 0.0), 1.0, jnp.where(place.next_y, 1.0, 0.0)]

    def element_row(base, u, v):
        device = (u // 2) * 3 + v // 2
        return spread[base + (u % 2) * 2 + v % 2, pl.ds(device, 1), :]

    for x in range(4):
        for y in range(4):
            kap[pl.ds(x * 4 + y, 1), :] = element_row(0, x + 1, y + 1)
            grp[pl.ds(x * 4 + y, 1), :] = element_row(4, x + 1, y + 1)
    kappa = [
        [
            place.join_z(jnp.broadcast_to(element_row(0, u + 1, v + 1), TILE))
            for v in range(4)
        ]
        for u in range(4)
    ]
    count_z = 1.0 + jnp.where(place.low_z | place.high_z, 1.0, 0.0)
    weight = ctab[T_W]
    line = ctab[T_LINE]

    def pick(values, ey):
        low = values[ey] + values[ey + 1]
        high = values[ey + 1] + values[ey + 2]
        return jnp.where(place.row == 0, low, jnp.where(place.row == 7, high, values[ey + 1]))

    for ex in range(2):
        for kind in range(3):
            us = {0: (ex, ex + 1), 1: (ex + 1,), 2: (ex + 1, ex + 2)}[kind]
            sums, counts = [], []
            for v in range(4):
                acc, num = None, 0.0
                for u in us:
                    acc = kappa[u][v] if acc is None else acc + kappa[u][v]
                    num = num + there_x[(u + 1) // 2]
                sums.append(acc)
                counts.append(num * there_y[(v + 1) // 2])
            for ey in range(2):
                kappa_sum = pick(sums, ey)
                mult = pick(counts, ey) * count_z
                for a in {0: (0,), 1: range(1, 7), 2: (7,)}[kind]:
                    diag = (float(LINE[a]) + line) * kappa_sum + sigma_p * mult
                    inv_diag[ex, a, ey] = 1.0 / (diag * (float(WEIGHTS[a]) * weight))


OUTER = ((0, 0), (1, 7))


def got_y_sum(place, tile, ch, ex, a, ey, y_first, y_second):
    row = pl.ds(ch * 16 + ex * 8 + a, 1)
    got_a, got_b = y_first[row, :], y_second[row, :]
    if ey == 0:
        tile = tile + jnp.where(place.row == 0, place.before_y(got_a, got_b), 0.0)
    else:
        tile = tile + jnp.where(place.row == 7, place.after_y(got_a, got_b), 0.0)
    return tile


def got_x_sum(place, tile, ch, ex, ey, x_first, x_second):
    rows = pl.ds(ch * 16 + ey * 8, 8)
    pick = place.before_x if ex == 0 else place.after_x
    return tile + pick(x_first[rows, :], x_second[rows, :])


def facts_kernel(pack, facts):
    place = Place()
    grid = pltpu.roll(pack[pl.ds(0, 1), :], (place.iy % 4) * (LANES // 4), 1)
    facts[:, pl.ds(0, LANES)] = jnp.zeros((1, LANES), jnp.float32)
    facts[:, pl.ds(LANES, LANES)] = grid
    for c in range(NCD):
        facts[:, pl.ds((2 + c) * LANES, LANES)] = pack[pl.ds(1 + c, 1), :]


def prepare_kernel(
    summed, visc, y_first, y_second, ctab, zmat, start, part, slope, answer, grad_z, flux_z
):
    place = Place()
    weight = ctab[T_W]
    inv_mass = [1.0 / (weight * place.mult_tile(ey)) for ey in range(2)]

    def begin(ch, carry):
        for ex in range(2):
            for a in range(8):
                for ey in range(2):
                    tile = got_y_sum(
                        place, summed[ch, ex, a, ey], ch, ex, a, ey, y_first, y_second
                    )
                    scale = place.inv_x(ex, a) * float(1.0 / WEIGHTS[a])
                    start[ch, ex, a, ey] = tile * (inv_mass[ey] * scale)
        return carry

    lax.fori_loop(0, 4, begin, 0)
    grad_z[...] = along_z(start[...].reshape(1024, LANES), zmat[0]).reshape(grad_z.shape)

    def column(index, carry):
        ch, ey = index // 2, index % 2
        coef = 1.0 / prandtl if ch == 3 else 1.0
        for ex in range(2):
            grad_x = along_x(DERIV, [start[ch, ex, a, ey] for a in range(8)], -1)
            flux_x = [
                visc[ex, a, ey] * (float(WEIGHTS[a]) * weight) * coef * grad_x[a]
                for a in range(8)
            ]
            back = along_x(DERIV.T, flux_x, -1)
            for a in range(8):
                if (ex, a) in OUTER:
                    slope[ch, ex, ey] = grad_x[a]
                    part[ch, ex, a, ey] = back[a]
                    continue
                rest, flux_z[ch, ex, a, ey] = across(
                    ctab, weight, a, coef, start[ch, ex, a, ey], grad_z[ch, ex, a, ey],
                    start[1, ex, a, ey], start[2, ex, a, ey], visc[ex, a, ey],
                )
                flow = float(WEIGHTS[a]) * weight * start[0, ex, a, ey]
                part[ch, ex, a, ey] = rest + flow * grad_x[a] + back[a]
        return carry

    for ex, outer in OUTER:
        for ey in range(2):
            flux_x = [
                visc[ex, a, ey] * (float(WEIGHTS[a] * DERIV[a, outer]) * weight) for a in range(8)
            ]
            back = along_x(DERIV.T, flux_x, -1)
            for a in range(8):
                answer[ex, a, ey] = back[a]
    for index in range(8):
        column(index, 0)
    for ch in range(4):
        for ex in range(2):
            inner = pl.ds(1 - ex, 7)
            back = along_z(flux_z[ch, ex, inner].reshape(112, LANES), zmat[1])
            part[ch, ex, inner] = part[ch, ex, inner] + back.reshape(7, 2, 8, LANES)


def across(ctab, weight, a, coef, value, grad_z, flow_y, flow_z, visc):
    node = float(WEIGHTS[a]) * weight
    grad_y = along_y(ctab, T_D, value)
    nu = visc * node * coef
    part = node * (flow_y * grad_y + flow_z * grad_z) + along_y(ctab, T_DT, nu * grad_y)
    return part, nu * grad_z


def rhs_kernel(
    pack_rows,
    begun,
    given,
    slope,
    answer,
    visc,
    pack,
    x_first,
    x_second,
    ctab,
    zmat,
    share,
    xf,
    inner_x,
    first,
    second,
    edge,
    edge_z,
    edge_part,
    came,
):
    place = Place()
    weight = ctab[T_W]
    inv_mass = [1.0 / (weight * place.mult_tile(ey)) for ey in range(2)]
    for ch in range(4):
        for side, (ex, a) in enumerate(OUTER):
            scale = place.inv_x(ex, a) * float(1.0 / WEIGHTS[a])
            for ey in range(2):
                zero = jnp.zeros(TILE, jnp.float32)
                extra = got_x_sum(place, zero, ch, ex, ey, x_first, x_second)
                extra = extra * (inv_mass[ey] * scale)
                came[ch, side, ey] = extra
                edge[ch, side, ey] = begun[ch, ex, a, ey] + extra
    edge_z[...] = along_z(edge[...].reshape(128, LANES), zmat[0]).reshape(edge.shape)
    for ch in range(4):
        coef = 1.0 / prandtl if ch == 3 else 1.0
        for side, (ex, a) in enumerate(OUTER):
            for ey in range(2):
                parts = across(
                    ctab, weight, a, coef, edge[ch, side, ey], edge_z[ch, side, ey],
                    edge[1, side, ey], edge[2, side, ey], visc[ex, a, ey],
                )
                edge_part[ch, side, ey], edge_z[ch, side, ey] = parts
    edge_part[...] = edge_part[...] + along_z(
        edge_z[...].reshape(128, LANES), zmat[1]
    ).reshape(edge.shape)

    def side_of(ch, ex, a, ey):
        outer = OUTER[ex][1]
        coef = 1.0 / prandtl if ch == 3 else 1.0
        extra = came[ch, ex, ey]
        node = float(WEIGHTS[a]) * weight
        turn = float(DERIV[a, outer])
        if a == outer:
            known = given[ch, ex, a, ey] + edge_part[ch, ex, ey]
            known = known + node * edge[0, ex, ey] * (slope[ch, ex, ey] + turn * extra)
            return known + extra * (coef * answer[ex, a, ey])
        flow = float(WEIGHTS[a] * turn) * weight * begun[0, ex, a, ey]
        return given[ch, ex, a, ey] + extra * (coef * answer[ex, a, ey] + flow)

    def finish(ch, carry):
        tiles = [
            [[place.join_z(-side_of(ch, ex, a, ey)) for ey in range(2)] for a in range(8)]
            for ex in range(2)
        ]
        join_own(place, tiles)
        for ex in range(2):
            for a in range(8):
                scale = place.inv_x(ex, a) * float(dt_step / WEIGHTS[a])
                for ey in range(2):
                    value = edge[ch, ex, ey] if (ex, a) in OUTER else begun[ch, ex, a, ey]
                    part = value * (place.share_y(ey) * place.share_x(ex, a))
                    share[ch, ex, a, ey] = part + tiles[ex][a][ey] * (inv_mass[ey] * scale)
        return carry

    for ch in range(4):
        finish(ch, 0)
    for ch in range(4):
        store_y_faces(place, share, first, second, (ch,), ch * 16)
        for ey in range(2):
            xf[0, ch, ey] = share[ch, 0, 0, ey]
            xf[1, ch, ey] = share[ch, 1, 7, ey]

    def column_of(ex, ey):
        return [share[0, ex, a, ey] for a in range(8)]

    def tile_of(ex, a, ey):
        return share[1, ex, a, ey]

    store_inner(
        place, DERIV, ctab[T_BOTTOM], ctab[T_TOP], column_of, tile_of, inner_x, first, second,
        STEP_V, STEP_EDGE,
    )
    beside = pl.ds(64, pack_rows)
    parts = (
        place.before_x(x_first[beside, :], x_second[beside, :]),
        pack[...],
        place.after_x(x_first[beside, :], x_second[beside, :]),
    )
    for k in range(3):
        rows = pl.ds(STEP_PACK + k * pack_rows, pack_rows)
        first[rows, :] = parts[k]
        second[rows, :] = parts[k]


def store_inner(
    place, matrix, bottom, top, column_of, tile_of, inner_x, first, second, at, edge
):
    for ey in range(2):
        low, high = column_of(0, ey), column_of(1, ey)
        below = float(matrix[0, 1]) * low[1]
        above = float(matrix[7, 0]) * high[0]
        for k in range(2, 8):
            below = below + float(matrix[0, k]) * low[k]
            above = above + float(matrix[7, k - 1]) * high[k - 1]
        inner_x[0, ey] = below
        inner_x[1, ey] = above
    for side in range(2):
        low = inner_x[side, 0, pl.ds(0, 1), :]
        high = inner_x[side, 1, pl.ds(7, 1), :]
        first[pl.ds(edge + side, 1), :] = place.send_y(high, low)
        second[pl.ds(edge + side, 1), :] = place.send_y(low, high)
    for ex in range(2):
        for a in range(8):
            low = jnp.sum(bottom * tile_of(ex, a, 0), axis=0, keepdims=True)
            high = jnp.sum(top * tile_of(ex, a, 1), axis=0, keepdims=True)
            row = pl.ds(at + ex * 8 + a, 1)
            first[row, :] = place.send_y(high, low)
            second[row, :] = place.send_y(low, high)


def cross_flow(place, ctab, flow, slopes, rows, inv_y, inv_z):
    below, above = rows
    below = (below - float(DERIV[0, 0]) * flow[0]) * jnp.where(place.prev_y, 1.0, 0.0)
    above = (above - float(DERIV[7, 7]) * flow[1]) * jnp.where(place.next_y, 1.0, 0.0)
    grad_y = list(place.join_y(*[along_y(ctab, T_D, tile) for tile in flow]))
    grad_y[0] = grad_y[0] + jnp.where(place.row == 0, below, 0.0)
    grad_y[1] = grad_y[1] + jnp.where(place.row == 7, above, 0.0)
    return [grad_y[ey] * inv_y[ey] + place.join_z(slopes[ey]) * inv_z for ey in range(2)]


def approach_kernel(share, y_first, y_second, ctab, zmat, fields_new, part, grad_z):
    place = Place()

    def step(ch, carry):
        for ex in range(2):
            for a in range(8):
                for ey in range(2):
                    fields_new[ch, ex, a, ey] = got_y_sum(
                        place, share[ch, ex, a, ey], ch, ex, a, ey, y_first, y_second
                    )
        return carry

    lax.fori_loop(0, 4, step, 0)
    grad_z[...] = along_z(fields_new[2].reshape(256, LANES), zmat[0]).reshape(grad_z.shape)
    inv_y = [place.inv_y(ey) for ey in range(2)]
    inv_z = place.inv_z()
    for ex in range(2):
        for a in range(8):
            if (ex, a) in OUTER:
                continue
            flow = [fields_new[1, ex, a, ey] for ey in range(2)]
            rows = inner_along_y(place, y_first, y_second, None, None, ex, a, STEP_V, STEP_EDGE)
            slopes = [grad_z[ex, a, ey] for ey in range(2)]
            both = cross_flow(place, ctab, flow, slopes, rows, inv_y, inv_z)
            part[ex, a, 0], part[ex, a, 1] = both


def emit_kernel(begun, x_first, x_second, extra, fields_new, passed):
    place = Place()
    passed[...] = extra[...]
    fields_new[...] = begun[...]
    for ch in range(4):
        for ex, a in OUTER:
            for ey in range(2):
                fields_new[ch, ex, a, ey] = got_x_sum(
                    place, begun[ch, ex, a, ey], ch, ex, ey, x_first, x_second
                )


def advance_kernel(
    begun,
    given,
    y_first,
    y_second,
    x_first,
    x_second,
    inv_diag,
    kap,
    grp,
    ctab,
    zmat,
    resid,
    own,
    msg,
    grad_z,
    scaled,
    edge,
    part,
    outer,
):
    place = Place()
    weight = ctab[T_W]

    def before(row, count=8):
        rows = pl.ds(row, count)
        return place.before_x(x_first[rows, :], x_second[rows, :])

    def after(row, count=8):
        rows = pl.ds(row, count)
        return place.after_x(x_first[rows, :], x_second[rows, :])

    for ch in range(3):
        for side, (ex, a) in enumerate(OUTER):
            for ey in range(2):
                outer[ch, side, ey] = got_x_sum(
                    place, begun[ch, ex, a, ey], ch, ex, ey, x_first, x_second
                )
    edge[...] = along_z(outer[2].reshape(32, LANES), zmat[0]).reshape(edge.shape)
    inv_y = [place.inv_y(ey) for ey in range(2)]
    inv_z = place.inv_z()
    for side, (ex, a) in enumerate(OUTER):
        flow = [outer[1, side, ey] for ey in range(2)]
        rows = inner_along_y(place, y_first, y_second, before, after, ex, a, STEP_V, STEP_EDGE)
        slopes = [edge[side, ey] for ey in range(2)]
        both = cross_flow(place, ctab, flow, slopes, rows, inv_y, inv_z)
        part[ex, a, 0], part[ex, a, 1] = both
    slope = [[None, None], [None, None]]
    for ey in range(2):
        for ex in range(2):
            line = [
                outer[0, ex, ey] if (ex, a) in OUTER else begun[0, ex, a, ey] for a in range(8)
            ]
            slope[ex][ey] = along_x(DERIV, line, -1)
        mid = 0.5 * (slope[0][ey][7] + slope[1][ey][0])
        slope[0][ey][7] = mid
        slope[1][ey][0] = mid
        low, high = slope[0][ey][0], slope[1][ey][7]
        inner_low = low - float(DERIV[0, 0]) * outer[0, 0, ey] + before(STEP_U + ey * 8)
        inner_high = high - float(DERIV[7, 7]) * outer[0, 1, ey] + after(STEP_U + ey * 8)
        slope[0][ey][0] = jnp.where(place.prev_x, 0.5 * inner_low, low)
        slope[1][ey][7] = jnp.where(place.next_x, 0.5 * inner_high, high)
    sums = [[jnp.zeros(TILE, jnp.float32) for _ in range(2)] for _ in range(2)]
    inv_mult = [1.0 / place.mult_tile(ey) for ey in range(2)]
    mass = [weight * place.mult_tile(ey) for ey in range(2)]
    for ex in range(2):
        for a in range(8):
            for ey in range(2):
                rest = part if (ex, a) in OUTER else given
                div = slope[ex][ey][a] + rest[ex, a, ey]
                value = div * (mass[ey] * (place.mult_x(ex, a) * float(-WEIGHTS[a])))
                resid[ex, a, ey] = value
                scaled[ex, a, ey] = value * inv_diag[ex, a, ey] * float(1.0 / THETA)
                sums[ex][ey] = sums[ex][ey] + value * (inv_mult[ey] * place.inv_x(ex, a))
    grad_z[...] = along_z(scaled[...].reshape(256, LANES), zmat[2]).reshape(grad_z.shape)
    tiles = [[[None, None] for _ in range(8)] for _ in range(2)]
    for ex in range(2):
        for ey in range(2):
            images = own_operator(ctab, kap, scaled, grad_z, ex, ey)[1]
            for a in range(8):
                tiles[ex][a][ey] = place.join_z(images[a])
    join_own(place, tiles)
    for ex in range(2):
        for a in range(8):
            for ey in range(2):
                own[ex, a, ey] = tiles[ex][a][ey]
    row = message(place, restricted(place, sums, grp), [])
    blank = jnp.where(place.row == 0, jnp.broadcast_to(row, TILE), 0.0)

    def clear(i, carry):
        msg[i] = blank
        return carry

    lax.fori_loop(0, msg.shape[0], clear, 0, unroll=msg.shape[0] <= 64)
    across = Pairing(place)
    for side, (ex, a) in enumerate(OUTER):
        there, ix = across.beside(side)

        @pl.when(there)
        def _():
            msg[ix * place.ny + place.iy] = own[ex, a, 0]
            msg[ix * place.ny + across.twin, pl.ds(1, 7), :] = own[ex, a, 1, pl.ds(1, 7), :]

        @pl.when(there & across.has_far)
        def _():
            msg[ix * place.ny + across.far, pl.ds(1, 1), :] = across.far_row(own, ex, a)

    @pl.when(across.has_far)
    def _():
        for a in range(8):
            msg[place.ix * place.ny + across.far, pl.ds(a, 1), :] = across.far_row(own, 0, a)
            if a > 0:
                to = place.ix * place.ny + across.beyond
                msg[to, pl.ds(a, 1), :] = across.far_row(own, 1, a)


def inner_along_y(place, y_first, y_second, before, after, ex, a, at, edge):
    row = pl.ds(at + ex * 8 + a, 1)
    got_a, got_b = y_first[row, :], y_second[row, :]
    below, above = place.before_y(got_a, got_b), place.after_y(got_a, got_b)
    if before is None:
        return below, above
    if (ex, a) == (0, 0):
        below = below + before(edge, 1)
        above = above + before(edge + 1, 1)
    if (ex, a) == (1, 7):
        below = below + after(edge, 1)
        above = above + after(edge + 1, 1)
    return below, above


class Pairing:
    def __init__(self, place):
        self.place = place
        even = place.even_y
        self.even = even
        self.twin = jnp.where(even, place.iy + 1, place.iy - 1)
        self.far = jnp.where(even, place.iy - 1, place.iy + 1)
        self.has_far = jnp.where(even, place.iy - 1, place.ny - 2 - place.iy) >= 0
        self.beyond = jnp.where(even, place.iy - 2, place.iy + 2)
        self.twin_far = jnp.where(even, place.iy + 2, place.iy - 2)
        self.twin_has_far = jnp.where(even, place.ny - 3 - place.iy, place.iy - 2) >= 0

    def beside(self, side):
        place = self.place
        if side == 0:
            return place.prev_x, place.ix - 1
        return place.next_x, place.ix + 1

    def far_row(self, field, ex, a):
        low = field[ex, a, 0, pl.ds(0, 1), :]
        return jnp.where(self.even, low, field[ex, a, 1, pl.ds(7, 1), :])

    def twin_row(self, field, ex, a):
        low = field[ex, a, 0, pl.ds(0, 1), :]
        return jnp.where(self.even, field[ex, a, 1, pl.ds(7, 1), :], low)


RELAY_FACE, RELAY_EDGE, RELAY_ROWS = 24, 40, 42


def relay_kernel(got, own, out):
    place = Place()
    across = Pairing(place)
    out[...] = jnp.zeros(out.shape, jnp.float32)
    for side in range(2):
        there, ix = across.beside(side)

        @pl.when(there)
        def _():
            out[pl.ds(side * 8, 8), :] = got[ix * place.ny + across.twin]
            corner = got[ix * place.ny + place.iy, pl.ds(0, 1), :]
            out[pl.ds(RELAY_EDGE + side, 1), :] = corner

    @pl.when(across.twin_has_far)
    def _():
        out[pl.ds(16, 8), :] = got[place.ix * place.ny + across.twin_far]

    for ex in range(2):
        for a in range(8):
            out[pl.ds(RELAY_FACE + ex * 8 + a, 1), :] = across.twin_row(own, ex, a)


SMOOTH_X, SMOOTH_Y, SMOOTH_EDGE, SMOOTH_ROWS = 16, 16, 32, 34


def turn_smooth_kernel(own, inner_x, y_first, y_second, first, second):
    place = Place()
    sides = []
    for side, (ex, a) in enumerate(((0, 0), (1, 7))):
        row = pl.ds(15 * side, 1)
        got_a, got_b = y_first[row, :], y_second[row, :]
        low = own[ex, a, 0] + jnp.where(place.row == 0, place.before_y(got_a, got_b), 0.0)
        high = own[ex, a, 1] + jnp.where(place.row == 7, place.after_y(got_a, got_b), 0.0)
        sides.append((low, high))
    for ey in range(2):
        rows = pl.ds(ey * 8, 8)
        first[rows, :] = place.send_x(sides[1][ey], sides[0][ey])
        second[rows, :] = place.send_x(sides[0][ey], sides[1][ey])
    turn_edges(
        place, inner_x, y_first, y_second, first, second, SMOOTH_X, SMOOTH_EDGE, SMOOTH_Y
    )


def restricted(place, sums, grp):
    values = []
    for c in range(NCD):
        acc = jnp.zeros(TILE, jnp.float32)
        for ex in range(2):
            for ey in range(2):
                group = grp[pl.ds((ex + 1) * 4 + ey + 1, 1), :]
                acc = acc + jnp.where(group == float(c), sums[ex][ey], 0.0)
        values.append(total(acc))
    return values


AWAY = 16
BEYOND = 18


def message(place, own_values, scalars, away=0, beyond=1):
    lane = lax.broadcasted_iota(jnp.int32, (1, LANES), 1)
    spot = (place.ix * place.ny + place.iy) % (LANES // NCD)
    after = (spot + beyond) % (LANES // NCD)
    spot = (spot + away) % (LANES // NCD)
    row = jnp.zeros((1, LANES), jnp.float32)
    for c, value in enumerate(own_values):
        row = row + jnp.where(lane == spot * NCD + c, value, 0.0)
    for c, value in enumerate(scalars):
        if value is None:
            continue
        row = row + jnp.where(lane == after * NCD + c, value, 0.0)
    return row


def send_to_all(msg, row):
    def send(i, carry):
        msg[i] = row
        return carry

    lax.fori_loop(0, msg.shape[0], send, 0, unroll=msg.shape[0] <= 64)


def cross_image(place, ctab, kap, value, flat, inner, ex, ey):
    slope_y = along_y(ctab, T_K, value)
    turned_y = inner + float(SCALED[0, 0]) * value
    own = kap[pl.ds((ex + 1) * 4 + ey + 1, 1), :] * (slope_y + flat) + sigma_p * value
    beyond = kap[pl.ds((ex + 1) * 4 + 3 * ey, 1), :] * (turned_y + flat) + sigma_p * value
    return own + jnp.where(beyond_y(place, ey), beyond, 0.0), slope_y, turned_y


def beyond_y(place, ey):
    if ey == 0:
        return (place.row == 0) & place.prev_y
    return (place.row == 7) & place.next_y


def ready_kernel(
    own, y_first, y_second, inv_diag, kap, ctab, zmat, image, scaled, part, slope_z
):
    place = Place()
    for ex in range(2):
        for a in range(8):
            for ey in range(2):
                tile = got_y_sum(place, own[ex, a, ey], 0, ex, a, ey, y_first, y_second)
                image[ex, a, ey] = tile
                scaled[ex, a, ey] = tile * inv_diag[ex, a, ey] * float(1.0 / THETA)
    slope_z[...] = along_z(scaled[...].reshape(256, LANES), zmat[2]).reshape(slope_z.shape)
    for ex in range(2):
        for a in range(8):
            if (ex, a) in OUTER:
                continue
            rows = inner_along_y(
                place, y_first, y_second, None, None, ex, a, SMOOTH_Y, SMOOTH_EDGE
            )
            for ey in range(2):
                part[ex, a, ey] = cross_image(
                    place, ctab, kap, scaled[ex, a, ey], slope_z[ex, a, ey], rows[ey], ex, ey
                )[0]


def smooth_kernel(
    begun,
    begun_scaled,
    given,
    y_first,
    y_second,
    x_first,
    x_second,
    inv_diag,
    kap,
    grp,
    extra,
    facts,
    ctab,
    zmat,
    image,
    smoothed,
    msg,
    scaled,
    slope_z,
    edge,
):
    place = Place()
    weight = ctab[T_W]
    corner = float(SCALED[0, 0])

    def before(row, count=8):
        rows = pl.ds(row, count)
        return place.before_x(x_first[rows, :], x_second[rows, :])

    def after(row, count=8):
        rows = pl.ds(row, count)
        return place.after_x(x_first[rows, :], x_second[rows, :])

    if msg.shape[2] == LANES:
        image[...] = begun[...]
    for side, (ex, a) in enumerate(OUTER):
        for ey in range(2):
            tile = got_x_sum(place, begun[ex, a, ey], 0, ex, ey, x_first, x_second)
            image[ex, a, ey] = tile
            scaled[ex, a, ey] = tile * inv_diag[ex, a, ey] * float(1.0 / THETA)
            edge[side, ey] = scaled[ex, a, ey]
    edge[...] = along_z(edge[...].reshape(32, LANES), zmat[2]).reshape(edge.shape)
    there_x = (place.prev_x, place.next_x)
    zero = jnp.zeros(TILE, jnp.float32)
    tiles = [[[None, None] for _ in range(8)] for _ in range(2)]
    for ex in range(2):
        a_out = OUTER[ex][1]
        rows = inner_along_y(
            place, y_first, y_second, before, after, ex, a_out, SMOOTH_Y, SMOOTH_EDGE
        )
        for ey in range(2):
            values = [(scaled if a == a_out else begun_scaled)[ex, a, ey] for a in range(8)]
            slopes = along_x(SCALED, values, 1)
            far_row = beyond_y(place, ey)
            beside = kap[pl.ds((ex + 1) * 4 + 3 * ey, 1), :]
            kappa = kap[pl.ds((ex + 1) * 4 + ey + 1, 1), :] + jnp.where(far_row, beside, 0.0)
            for a in range(8):
                if a != a_out:
                    acc = given[ex, a, ey]
                else:
                    value, flat = values[a], edge[ex, ey]
                    acc, slope_y, turned_y = cross_image(
                        place, ctab, kap, value, flat, rows[ey], ex, ey
                    )
                    x_next = 3 * ex
                    get = before if ex == 0 else after
                    turned_x = get(SMOOTH_X + ey * 8) + corner * value
                    side = kap[pl.ds(x_next * 4 + ey + 1, 1), :] * (turned_x + slope_y + flat)
                    far = kap[pl.ds(x_next * 4 + 3 * ey, 1), :] * (turned_x + turned_y + flat)
                    side = side + sigma_p * value
                    side = side + jnp.where(far_row, far + sigma_p * value, zero)
                    acc = acc + jnp.where(there_x[ex], side, zero)
                acc = acc + kappa * slopes[a]
                tiles[ex][a][ey] = place.join_z(acc * (float(WEIGHTS[a]) * weight))
    join_own(place, tiles)
    inv_mult = [1.0 / place.mult_tile(ey) for ey in range(2)]
    sums = [[jnp.zeros(TILE, jnp.float32) for _ in range(2)] for _ in range(2)]
    square = jnp.zeros(TILE, jnp.float32)
    for ex in range(2):
        for a in range(8):
            for ey in range(2):
                outer = (ex, a) in OUTER
                value = (image if outer else begun)[ex, a, ey]
                defect = (value - tiles[ex][a][ey]) * inv_diag[ex, a, ey]
                update = (scaled if outer else begun_scaled)[ex, a, ey]
                result = (
                    float(1.0 + RHO_NEXT * RHO) * update + float(2.0 * RHO_NEXT / DELTA) * defect
                )
                smoothed[ex, a, ey] = result
                weighed = value * (inv_mult[ey] * place.inv_x(ex, a))
                sums[ex][ey] = sums[ex][ey] + weighed
                square = square + weighed * result
    own_sums = restricted(place, sums, grp)
    if msg.shape[2] == LANES:
        sums = [extra[:, pl.ds(k, 1)] for k in range(2)]
        send_to_all(msg, message(place, own_sums, sums))
        return
    slope_z[...] = along_z(smoothed[...].reshape(256, LANES), zmat[2]).reshape(slope_z.shape)
    energy = jnp.zeros(TILE, jnp.float32)
    for ex in range(2):
        for ey in range(2):
            values, images = own_operator(ctab, kap, smoothed, slope_z, ex, ey)
            for a in range(8):
                energy = energy + values[a] * images[a]
                tiles[ex][a][ey] = place.join_z(images[a])
    join_own(place, tiles)
    sums = [extra[:, pl.ds(k, 1)] for k in range(2)] + [total(square), total(energy)]
    row = message(place, own_sums, sums, AWAY, BEYOND)
    row = row + restricted_around(place, tiles, inv_mult, grp)
    send_to_all(msg, jnp.concatenate([row, facts[:, LANES:]], axis=1))


def restricted_around(place, tiles, inv_mult, grp):
    lane = lax.broadcasted_iota(jnp.int32, (1, LANES), 1)
    weighed = [
        [[tiles[ex][a][ey] * (inv_mult[ey] * place.inv_x(ex, a)) for ey in range(2)] for a in range(8)]
        for ex in range(2)
    ]

    def rows_of(tile, y):
        if y == 0:
            return jnp.where(place.row == 0, tile[0], 0.0)
        if y == 3:
            return jnp.where(place.row == 7, tile[1], 0.0)
        return tile[y - 1]

    there_x = (place.prev_x, None, None, place.next_x)
    there_y = (place.prev_y, None, None, place.next_y)
    by_device = [
        [[jnp.zeros(TILE, jnp.float32) for _ in range(NCD)] for _ in range(3)] for _ in range(3)
    ]
    for x in range(4):
        for y in range(4):
            if x == 0:
                acc = rows_of(weighed[0][0], y)
            elif x == 3:
                acc = rows_of(weighed[1][7], y)
            else:
                acc = rows_of(weighed[x - 1][0], y)
                for a in range(1, 8):
                    acc = acc + rows_of(weighed[x - 1][a], y)
            for there in (there_x[x], there_y[y]):
                if there is not None:
                    acc = jnp.where(there, acc, 0.0)
            group = grp[pl.ds(x * 4 + y, 1), :]
            device = by_device[(x + 1) // 2][(y + 1) // 2]
            for c in range(NCD):
                device[c] = device[c] + jnp.where(group == float(c), acc, 0.0)
    row = jnp.zeros((1, LANES), jnp.float32)
    for dx in range(3):
        for dy in range(3):
            at = ((place.ix + dx - 1) * place.ny + place.iy + dy - 1) * NCD
            for c in range(NCD):
                row = row + jnp.where(lane == at + c, total(by_device[dx][dy][c]), 0.0)
    return row


def coarse_part(place, blocks, got, coarse, grp, others=()):
    lane = lax.broadcasted_iota(jnp.int32, (1, LANES), 1)
    values = [jnp.zeros((1, LANES), jnp.float32) for _ in range(blocks)]
    per = LANES // NCD
    for j in range(blocks):

        def gather(i, acc, j=j):
            return jnp.where(lane // NCD == i, got[j * per + i, pl.ds(0, 1), :], acc)

        values[j] = lax.fori_loop(0, per, gather, values[j], unroll=blocks == 1)
        for there, device, row in others:
            spot = (lane // NCD == device % per) & (device // per == j) & there
            values[j] = jnp.where(spot, row, values[j])

    def solved(dx, dy, c):
        acc = None
        for j in range(blocks):
            term = coarse[pl.ds(((dx * 3 + dy) * NCD + c) * blocks + j, 1), :] * values[j]
            acc = term if acc is None else acc + term
        return jnp.sum(acc, axis=1, keepdims=True)

    return prolonged(place, solved, grp)


def prolonged(place, solved, grp):
    device = [[[solved(dx, dy, c) for c in range(NCD)] for dy in range(3)] for dx in range(3)]
    inv_z = jnp.where(place.low_z | place.high_z, 0.5, 1.0)
    rows = []
    for x in range(4):
        line = []
        for y in range(4):
            group = grp[pl.ds(x * 4 + y, 1), :]
            acc = jnp.zeros((1, LANES), jnp.float32)
            for c in range(NCD):
                acc = acc + jnp.where(
                    group == float(c), device[(x + 1) // 2][(y + 1) // 2][c], 0.0
                )
            line.append(place.join_z(jnp.broadcast_to(acc, TILE)) * inv_z)
        rows.append(line)
    low_y = jnp.where(place.prev_y, 0.5, 1.0)
    high_y = jnp.where(place.next_y, 0.5, 1.0)

    def tile(ex, kind, ey):
        if kind == 1:
            vals = [rows[ex + 1][y] for y in range(4)]
        elif kind == 0:
            scale = place.inv_x(ex, 0)
            vals = [(rows[ex][y] + rows[ex + 1][y]) * scale for y in range(4)]
        else:
            scale = place.inv_x(ex, 7)
            vals = [(rows[ex + 1][y] + rows[ex + 2][y]) * scale for y in range(4)]
        mid = vals[ey + 1]
        low = (vals[ey] + mid) * (low_y if ey == 0 else 0.5)
        high = (mid + vals[ey + 2]) * (high_y if ey == 1 else 0.5)
        return jnp.where(place.row == 0, low, jnp.where(place.row == 7, high, mid))

    return tile


def kind_of(a):
    return 0 if a == 0 else (2 if a == 7 else 1)


def own_operator(ctab, kap, field, slope_z, ex, ey):
    weight = ctab[T_W]
    tiles = [field[ex, a, ey] for a in range(8)]
    slopes = along_x(SCALED, tiles, 1)
    kappa = kap[pl.ds((ex + 1) * 4 + ey + 1, 1), :]
    out = []
    for a in range(8):
        stiff = slopes[a] + along_y(ctab, T_K, tiles[a]) + slope_z[ex, a, ey]
        out.append((kappa * stiff + sigma_p * tiles[a]) * (float(WEIGHTS[a]) * weight))
    return tiles, out


def first_direction_kernel(
    blocks,
    got,
    relayed,
    coarse,
    grp,
    kap,
    inv_diag,
    resid,
    own,
    ctab,
    zmat,
    direction,
    out,
    inner_x,
    first,
    second,
    extra,
    slope_z,
    image,
):
    place = Place()
    inv_mult = [1.0 / place.mult_tile(ey) for ey in range(2)]
    across = Pairing(place)
    others = []
    for side in range(2):
        there, ix = across.beside(side)
        others.append((there, ix * place.ny + place.iy, relayed[pl.ds(side * 8, 1), :]))
    others.append(
        (across.has_far, place.ix * place.ny + across.far, relayed[pl.ds(16, 1), :])
    )
    part = coarse_part(place, blocks, got, coarse, grp, others)
    image[...] = own[...]
    far_edge = jnp.where(across.even, 0, 7)

    def add_row(ex, a, row, edge, low):
        extra = jnp.where(place.row == edge, row, 0.0)
        image[ex, a, 0] = image[ex, a, 0] + jnp.where(low, extra, 0.0)
        image[ex, a, 1] = image[ex, a, 1] + jnp.where(low, 0.0, extra)

    for ex in range(2):
        for a in range(8):
            row = relayed[pl.ds(RELAY_FACE + ex * 8 + a, 1), :]
            add_row(ex, a, row, 7 - far_edge, ~across.even)

    @pl.when(across.has_far)
    def _():
        for a in range(8):
            row = got[place.ix * place.ny + across.far, pl.ds(a, 1), :]
            add_row(0, a, row, far_edge, across.even)
            if a == 7:
                add_row(1, 0, row, far_edge, across.even)
            if a > 0:
                add_row(1, a, relayed[pl.ds(16 + a, 1), :], far_edge, across.even)

    for side, (ex, a) in enumerate(OUTER):
        there, ix = across.beside(side)

        @pl.when(there)
        def _():
            low = got[ix * place.ny + place.iy]
            high = jnp.where(
                place.row == 0, pltpu.roll(low, 1, 0), relayed[pl.ds(side * 8, 8), :]
            )
            image[ex, a, 0] = image[ex, a, 0] + low
            image[ex, a, 1] = image[ex, a, 1] + high
            corner = jnp.where(
                across.even,
                relayed[pl.ds(RELAY_EDGE + side, 1), :],
                got[ix * place.ny + across.twin, pl.ds(7, 1), :],
            )
            add_row(ex, a, corner, 7 - far_edge, ~across.even)

        @pl.when(there & across.has_far)
        def _():
            corner = got[ix * place.ny + across.far, pl.ds(1, 1), :]
            add_row(ex, a, corner, far_edge, across.even)

    energy = jnp.zeros(TILE, jnp.float32)
    for ex in range(2):
        for ey in range(2):
            kinds = [part(ex, kind, ey) for kind in range(3)]
            for a in range(8):
                known = resid[ex, a, ey]
                inverse = inv_diag[ex, a, ey]
                defect = (known - image[ex, a, ey]) * inverse
                value = (
                    float((1.0 + RHO_NEXT * RHO) / THETA) * (known * inverse)
                    + float(2.0 * RHO_NEXT / DELTA) * defect
                    + kinds[kind_of(a)]
                )
                direction[ex, a, ey] = value
                scale = place.inv_x(ex, a)
                energy = energy + value * known * (inv_mult[ey] * scale)
    slope_z[...] = along_z(direction[...].reshape(256, LANES), zmat[2]).reshape(slope_z.shape)
    curvature = jnp.zeros(TILE, jnp.float32)
    tiles = [[[None, None] for _ in range(8)] for _ in range(2)]
    for ex in range(2):
        for ey in range(2):
            values, images = own_operator(ctab, kap, direction, slope_z, ex, ey)
            for a in range(8):
                curvature = curvature + values[a] * images[a]
                tiles[ex][a][ey] = place.join_z(images[a])
    join_own(place, tiles)
    for ex in range(2):
        for a in range(8):
            for ey in range(2):
                out[ex, a, ey] = tiles[ex][a][ey]
    store_y_faces(place, out, first, second, (), 0)

    def tile_of(ex, a, ey):
        return tiles[ex][a][ey] * inv_diag[ex, a, ey] * float(1.0 / THETA)

    def column_of(ex, ey):
        return [tile_of(ex, a, ey) for a in range(8)]

    store_inner(
        place, SCALED, ctab[T_KBOTTOM], ctab[T_KTOP], column_of, tile_of, inner_x, first, second,
        SMOOTH_Y, SMOOTH_EDGE,
    )
    lane = lax.broadcasted_iota(jnp.int32, (1, LANES), 1)
    extra[...] = jnp.where(lane == 0, total(energy), total(curvature))


def gathered_scalars(got, count):
    lane = lax.broadcasted_iota(jnp.int32, (1, LANES), 1)
    per = LANES // NCD
    sums = []
    for c in range(count):
        acc = jnp.zeros((1, LANES), jnp.float32)

        def gather(i, acc, c=c):
            return acc + jnp.where(lane == ((i + 1) % per) * NCD + c, got[i], 0.0)

        acc = lax.fori_loop(0, got.shape[0], gather, acc, unroll=got.shape[0] <= per)
        sums.append(jnp.sum(acc, axis=1, keepdims=True))
    return sums


def second_direction_kernel(
    blocks,
    got,
    coarse,
    grp,
    kap,
    resid,
    direction,
    image,
    smoothed,
    ctab,
    zmat,
    following,
    known,
    msg,
    slope_z,
):
    place = Place()
    inv_mult = [1.0 / place.mult_tile(ey) for ey in range(2)]
    part = coarse_part(place, blocks, got, coarse, grp)
    energy, curvature = gathered_scalars(got, 2)
    step = energy / curvature
    lane = lax.broadcasted_iota(jnp.int32, (1, LANES), 1)
    known[...] = jnp.where(lane == 0, energy, jnp.where(lane == 1, curvature, 0.0))
    energy_next = jnp.zeros(TILE, jnp.float32)
    cross = jnp.zeros(TILE, jnp.float32)
    for ex in range(2):
        for ey in range(2):
            kinds = [part(ex, kind, ey) for kind in range(3)]
            for a in range(8):
                value = direction[ex, a, ey] - step * (smoothed[ex, a, ey] + kinds[kind_of(a)])
                following[ex, a, ey] = value
                weighed = value * (inv_mult[ey] * place.inv_x(ex, a))
                was = image[ex, a, ey]
                energy_next = energy_next + weighed * (resid[ex, a, ey] - step * was)
                cross = cross + weighed * was
    slope_z[...] = along_z(following[...].reshape(256, LANES), zmat[2]).reshape(slope_z.shape)
    square = jnp.zeros(TILE, jnp.float32)
    for ex in range(2):
        for ey in range(2):
            values, images = own_operator(ctab, kap, following, slope_z, ex, ey)
            for a in range(8):
                square = square + values[a] * images[a]
    send_to_all(msg, message(place, [], [total(energy_next), total(square), total(cross)]))


def pressure_kernel(got, known, direction, following, pressure):
    energy = known[:, pl.ds(0, 1)]
    curvature = known[:, pl.ds(1, 1)]
    energy_next, square, cross = gathered_scalars(got, 3)
    ratio = energy_next / energy
    step = energy / curvature
    step_next = energy_next / (square + 2.0 * ratio * cross + ratio * ratio * curvature)
    weight_old = step + step_next * ratio
    for ex in range(2):
        for a in range(8):
            for ey in range(2):
                pressure[ex, a, ey] = (
                    weight_old * direction[ex, a, ey] + step_next * following[ex, a, ey]
                )


def coarse_energy(place, got, values, kappa, number):
    lane, row = place.lane, place.row
    for ex in range(2):
        for gx in range(8):
            own = jnp.zeros((1, LANES), jnp.float32)
            group = jnp.zeros((1, LANES), jnp.float32)
            spot = lane[0:1] // 32
            for gy in range(4):
                line = got[gx * 4 + gy, :, pl.ds(LANES, LANES)]
                own = jnp.where(spot == (gy + 2 * ex) % 4, line, own)
                group = jnp.where(spot == (gy + 1 + 2 * ex) % 4, line, group)
            kappa[ex, pl.ds(gx, 1), :] = own
            number[ex, pl.ds(gx, 1), :] = group
    grid = [jnp.zeros(TILE, jnp.float32) for _ in range(2)]
    numbers = [pltpu.roll(number[0], 96, 1), pltpu.roll(number[1], 32, 1)]
    kappa = [kappa[0], pltpu.roll(kappa[1], 64, 1)]
    for q in range(4):
        for c in range(NCD):
            mine = jnp.where(lane == row * 16 + q * 4 + c, values, 0.0)
            mine = jnp.sum(mine, axis=1, keepdims=True)
            for ex in range(2):
                chosen = (lane // 32 == q) & (numbers[ex] == float(c))
                grid[ex] = jnp.where(chosen, mine, grid[ex])

    def ends_y(v):
        low = jnp.where(lane >= 16, 0.5 * (v + pltpu.roll(v, 16, 1)), v)
        return low, v, jnp.where(lane < 112, 0.5 * (v + pltpu.roll(v, 112, 1)), v)

    def ends_z(v):
        low = jnp.where(lane % 16 > 0, 0.5 * (v + pltpu.roll(v, 1, 1)), v)
        return low, v, jnp.where(lane % 16 < 15, 0.5 * (v + pltpu.roll(v, 127, 1)), v)

    low = jnp.where(row > 0, 0.5 * (grid[0] + pltpu.roll(grid[1], 1, 0)), grid[0])
    mid = 0.5 * (grid[0] + grid[1])
    high = jnp.where(row < 7, 0.5 * (grid[1] + pltpu.roll(grid[0], 7, 0)), grid[1])
    mass = [float(WEIGHTS[0]), float(np.sum(WEIGHTS[1:7])), float(WEIGHTS[7])]
    links = (
        (0, 1, -float(np.sum(STIFF[0, 1:7]))),
        (0, 2, -float(STIFF[0, 7])),
        (1, 2, -float(np.sum(STIFF[7, 1:7]))),
    )
    energy = jnp.zeros(TILE, jnp.float32)
    for ex, line in enumerate(((low, grid[0], mid), (mid, grid[1], high))):
        nodes = [[ends_z(v) for v in ends_y(w)] for w in line]
        stiff = jnp.zeros(TILE, jnp.float32)
        square = jnp.zeros(TILE, jnp.float32)
        for i in range(3):
            for j in range(3):
                for k, l, weight in links:
                    factor = weight * mass[i] * mass[j]
                    for first, second in (
                        (nodes[k][i][j], nodes[l][i][j]),
                        (nodes[i][k][j], nodes[i][l][j]),
                        (nodes[i][j][k], nodes[i][j][l]),
                    ):
                        gap = first - second
                        stiff = stiff + (factor * gap) * gap
                for k in range(3):
                    value = nodes[i][j][k]
                    square = square + (mass[i] * mass[j] * mass[k] * value) * value
        energy = energy + kappa[ex] * stiff + sigma_p * square
    return total(energy)


def finish_kernel(
    got, grp, direction, smoothed, pressure, matrix, kappa, number
):
    place = Place()
    per = LANES // NCD
    row_lane = lax.broadcasted_iota(jnp.int32, (1, LANES), 1)
    rest = jnp.zeros((1, LANES), jnp.float32)
    dual = jnp.zeros((1, LANES), jnp.float32)
    scalars = jnp.zeros((1, LANES), jnp.float32)
    for i in range(per):
        line = got[i, :, pl.ds(0, LANES)]
        mine = row_lane // NCD == (i + AWAY) % per
        known = row_lane // NCD == (i + BEYOND) % per
        rest = jnp.where(mine, line, rest)
        dual = dual + jnp.where(mine | known, 0.0, line)
        scalars = jnp.where(known, line, scalars)
        for c in range(NCD):
            block = got[i, :, pl.ds((2 + c) * LANES, LANES)]
            matrix[pl.ds(i * NCD + c, 1), :] = block
    rest = pltpu.roll(rest, (per - AWAY) * NCD, 1)
    energy, curvature, square, self_energy = [
        jnp.sum(jnp.where(row_lane % NCD == c, scalars, 0.0), axis=1, keepdims=True)
        for c in range(4)
    ]
    values = exact_dot(jnp.broadcast_to(rest, TILE), matrix[...])
    line = values[0:1]
    cross = square + jnp.sum(line * rest, axis=1, keepdims=True)
    both = self_energy + 2.0 * jnp.sum(line * dual, axis=1, keepdims=True)
    both = both + coarse_energy(place, got, values, kappa, number)
    step = energy / curvature
    energy_next = step * step * cross - energy
    ratio = energy_next / energy
    with_image = curvature - step * cross
    with_itself = curvature - 2.0 * step * cross + step * step * both
    step_next = energy_next / (
        with_itself + 2.0 * ratio * with_image + ratio * ratio * curvature
    )
    old = step + step_next * (1.0 + ratio)
    new = -step_next * step

    def solved(dx, dy, c):
        at = ((place.ix + dx - 1) * place.ny + place.iy + dy - 1) * NCD + c
        return jnp.sum(jnp.where(row_lane == at, line, 0.0), axis=1, keepdims=True)

    part = prolonged(place, masked(place, solved), grp)
    for ex in range(2):
        for ey in range(2):
            kinds = [part(ex, kind, ey) for kind in range(3)]
            for a in range(8):
                pressure[ex, a, ey] = old * direction[ex, a, ey] + new * (
                    smoothed[ex, a, ey] + kinds[kind_of(a)]
                )


def masked(place, solved):
    there_x = (place.prev_x, None, place.next_x)
    there_y = (place.prev_y, None, place.next_y)

    def value(dx, dy, c):
        out = solved(dx, dy, c)
        for there in (there_x[dx], there_y[dy]):
            if there is not None:
                out = jnp.where(there, out, 0.0)
        return out

    return value


def call(body, outs, scratch=(), **more):
    return pl.pallas_call(
        body,
        out_shape=[jax.ShapeDtypeStruct(shape, jnp.float32) for shape in outs],
        scratch_shapes=[
            pltpu.VMEM(shape, jnp.float32) if isinstance(shape, tuple) else shape
            for shape in scratch
        ],
        **more,
        compiler_params=pltpu.CompilerParams(vmem_limit_bytes=24 * 1024 * 1024),
    )


def swap(first, second, axis):
    along, across = lax.axis_size("gx"), lax.axis_size("gy")

    def number(ix, iy):
        return ix * across + iy

    pairs = ([], [])
    for ix in range(along):
        for iy in range(across):
            at, count = (ix, along) if axis == "gx" else (iy, across)
            for k, to in enumerate((at ^ 1, ((at + 1) ^ 1) - 1)):
                if 0 <= to < count:
                    there = (to, iy) if axis == "gx" else (ix, to)
                else:
                    there = (ix, iy ^ 1) if axis == "gx" else (ix, across - 1 - iy)
                pairs[k].append((number(ix, iy), number(*there)))
    pairs = pairs[::-1]
    first_got = lax.ppermute(first, BOTH, pairs[0])
    return first_got, lax.ppermute(second, BOTH, pairs[1])


def per_device(fields, viscosity, inv_density, elem_group, coarse_inverse):
    length = fields.shape[5]
    elems_z = length // NODES
    devices = lax.axis_size("gx") * lax.axis_size("gy")
    blocks = coarse_inverse.shape[1] // LANES
    pack_rows = 1 + NCD * blocks
    tiles_np, mats_np = constant_tables(elems_z)
    ctab, zmat = jnp.asarray(tiles_np), jnp.asarray(mats_np)
    one = fields.shape[1:]
    four = fields.shape
    faces = (64, LANES)
    xf_shape = (2, 4, 2, 8, LANES)
    inner_shape = (2, 2, 8, LANES)
    y_shape, x_shape = (STEP_PACK + 3 * pack_rows, LANES), (STEP_PACK, LANES)
    turned = (64 + pack_rows, LANES)
    smooth_shape = (SMOOTH_ROWS, LANES)
    rows = (devices, 1, LANES)
    grid_fits = (
        blocks == 1
        and lax.axis_size("gx") == 8
        and lax.axis_size("gy") * fields.shape[3] * elems_z == LANES
    )

    def exchange_all(msg):
        return lax.all_to_all(msg, BOTH, 0, 0, tiled=True)

    beside = pl.CostEstimate(flops=10**7, bytes_accessed=10**6, transcendentals=0)
    first, second = call(faces_kernel, [faces, faces], [xf_shape])(fields)
    numbers = elem_group.astype(jnp.float32)
    row = jnp.stack([inv_density, numbers], 1).reshape(1, LANES)
    pack = jnp.concatenate([row, coarse_inverse.reshape(NCD * blocks, LANES)], 0)
    (facts,) = call(facts_kernel, [(1, 6 * LANES)], cost_estimate=beside)(pack)
    summed, xf = call(mass_kernel, [four, xf_shape], cost_estimate=beside)(fields)
    y_got = swap(first, second, "gy")
    first, second = call(functools.partial(turn_faces_kernel, pack_rows), [turned, turned])(
        xf, pack, *y_got
    )
    side_got = x_got = swap(first, second, "gx")
    edge_shape = (4, 2, 2, 8, LANES)
    begun, given, slope, answer = call(
        prepare_kernel, [four, four, edge_shape, one], [four, four], cost_estimate=beside
    )(summed, viscosity, *y_got, ctab, zmat)
    share, xf, inner_x, first, second = call(
        functools.partial(rhs_kernel, pack_rows),
        [four, xf_shape, inner_shape, y_shape, y_shape],
        [edge_shape, edge_shape, edge_shape, edge_shape],
    )(begun, given, slope, answer, viscosity, pack, *x_got, ctab, zmat)
    y_got = swap(first, second, "gy")
    first, second = call(turn_step_kernel, [x_shape, x_shape])(xf, inner_x, *y_got)
    x_got = swap(first, second, "gx")
    inv_diag, kap, grp, coarse = call(
        functools.partial(setup_kernel, pack_rows, blocks),
        [one, (16, LANES), (16, LANES), (9 * NCD * blocks, LANES)],
        [(16, LANES), (8, 16, LANES)],
        cost_estimate=beside,
    )(pack, *side_got, *y_got, ctab)
    begun, given = call(approach_kernel, [four, one], [one], cost_estimate=beside)(
        share, *y_got, ctab, zmat
    )
    side_shape = (2, 2, 8, LANES)
    fields_got = x_got
    fields_begun = begun
    resid, own, msg = call(
        advance_kernel,
        [one, one, (devices, 8, LANES)],
        [one, one, side_shape, one, (3,) + side_shape],
    )(begun, given, *y_got, *x_got, inv_diag, kap, grp, ctab, zmat)
    got = exchange_all(msg)
    (relayed,) = call(relay_kernel, [(RELAY_ROWS, LANES)])(got, own)
    relayed = lax.ppermute(
        relayed, "gy", [(i, i ^ 1) for i in range(lax.axis_size("gy")) if i ^ 1 < lax.axis_size("gy")]
    )
    direction, own, inner_x, first, second, extra = call(
        functools.partial(first_direction_kernel, blocks),
        [one, one, inner_shape, smooth_shape, smooth_shape, (1, LANES)],
        [one, one],
    )(got, relayed, coarse, grp, kap, inv_diag, resid, own, ctab, zmat)
    y_got = swap(first, second, "gy")
    first, second = call(turn_smooth_kernel, [smooth_shape, smooth_shape])(own, inner_x, *y_got)
    x_got = swap(first, second, "gx")
    fields_new, extra = call(emit_kernel, [four, (1, LANES)], cost_estimate=beside)(
        fields_begun, *fields_got, extra
    )
    begun, begun_scaled, given = call(
        ready_kernel, [one, one, one], [one], cost_estimate=beside
    )(own, *y_got, inv_diag, kap, ctab, zmat)
    image, image_smoothed, msg = call(
        smooth_kernel,
        [one, one, (devices, 1, 6 * LANES) if grid_fits else rows],
        [one, one, side_shape],
    )(
        begun, begun_scaled, given, *y_got, *x_got, inv_diag, kap, grp, extra, facts, ctab, zmat
    )
    got = exchange_all(msg)
    if grid_fits:
        (pressure,) = call(
            finish_kernel, [one], [(LANES, LANES), (2,) + TILE, (2,) + TILE]
        )(got, grp, direction, image_smoothed)
        return (fields_new, pressure)
    following, known, msg = call(
        functools.partial(second_direction_kernel, blocks), [one, (1, LANES), rows], [one]
    )(got, coarse, grp, kap, resid, direction, image, image_smoothed, ctab, zmat)
    got = exchange_all(msg)
    (pressure,) = call(pressure_kernel, [one])(got, known, direction, following)
    return (fields_new, pressure)


def solution(mesh):
    placed = (
        P(None, "gx", None, "gy", None, None),
        P("gx", None, "gy", None, None),
        P("gx", "gy", None),
        P("gx", "gy", None),
        P(("gx", "gy"), None),
    )
    return jax.shard_map(
        per_device,
        mesh=mesh,
        in_specs=placed,
        out_specs=(P(None, "gx", None, "gy", None, None), P("gx", None, "gy", None, None)),
        check_vma=False,
    )
```
